32 devices in a mesh: groups: 2 (over y), adapter: 16 (over z, x, core).
Axes of the slice: x: 2, y: 2, z: 4, core: 2. Of those that a mesh axis runs over, the one named last changes fastest.
Arguments:
- tokens: bfloat16 [1024, 8, 3200], P(('groups', 'adapter')), parts along dimension 0, may hold values from -40 to 40
- request_block_adapter: int32 [1024], P(('groups', 'adapter')), parts along dimension 0, may hold values from 0 to 127, as said below
- request_block_rows: int32 [1024], P(('groups', 'adapter')), parts along dimension 0, may hold values from 1 to 8
- adapter_down_weight: bfloat16 [128, 3200, 64], P('adapter'), may hold values from -0.109375 to 0.109375
- adapter_up_weight: bfloat16 [128, 64, 3200], P('adapter'), may hold values from -0.75 to 0.75
Outputs:
- mixed: bfloat16 [1024, 8, 3200], P(('groups', 'adapter')), parts along dimension 0
The draws below stay inside these ranges and needn't reach their ends.
There are 2 independent parts, one for each index of `groups`. The reference program is written for one: setup_inputs(seed, part) draws one part's arguments, and reference() takes and returns one part's arrays. A program takes and returns all parts, laid end to end along the dimension named above; an argument that names none is the same for every part. Nothing has to cross between parts.
Inputs may be any that keep to these rules, and one draw needn't show every extreme that they name: `request_block_adapter`: adapter a is held by the device of index a // 8. The 32 blocks of one device go to at most 8 blocks for each holding device; in every draw some devices receive exactly 8 blocks from every device.
All inputs are finite; a program needn't handle non-finite values.
Results may differ from the reference program's by a relative error of at most 0.0031.
Values may be sent and summed in bfloat16 or wider, within the bound.
No kernel may reach another device: no remote copies, remote signals or barrier semaphores. Data moves between devices by JAX's collectives and lax.ppermute only.
A program may use at most 64 MiB of HBM per device.

```python
import math
import jax
import jax.numpy as jnp
from jax import lax

MODEL_WIDTH = 3200
ADAPTER_RANK = 64
RB = 8
ADP_DEV = 8
NB_DEV = 32
ADAPTER_TOTAL = 128
BLOCKS = 512
N_ADAPTER = 16


def draw_tokens(key, part):
    key = jax.random.fold_in(key, 5)
    k_rows, k_cols, k_base = jax.random.split(key, 3)
    input_shape = (BLOCKS, RB, MODEL_WIDTH)
    rows_scale = jnp.exp((jax.random.uniform(k_rows, (BLOCKS, RB, 1)) - 0.5) * math.log(10.0))
    cols_scale = jnp.exp((jax.random.uniform(k_cols, (MODEL_WIDTH,)) - 0.5) * math.log(10.0))
    base = jax.random.normal(k_base, input_shape)
    base = jnp.clip(base, -4.0, 4.0)
    return (base * rows_scale * cols_scale).astype(jnp.bfloat16)


def draw_request_block_adapter(key, part):
    key = jax.random.fold_in(key, 11)
    k_hot, k_score, k_order, k_within = jax.random.split(key, 4)
    slots = max(1, 4 * NB_DEV // N_ADAPTER)
    hot_count = max(1, min(N_ADAPTER // 8, NB_DEV // (2 * slots)))
    total_slots = N_ADAPTER * slots
    hot_devices = jax.random.permutation(k_hot, N_ADAPTER)[:hot_count]
    is_hot = jnp.zeros((N_ADAPTER,), jnp.int32).at[hot_devices].set(1)
    slot_owner = jnp.arange(total_slots, dtype=jnp.int32) // slots
    slot_hot = is_hot[slot_owner]
    scores = jax.random.randint(k_score, (N_ADAPTER, total_slots), 0, 2 ** 20)
    scores = (scores + slot_hot[None, :] * 2 ** 20) * total_slots + jnp.arange(total_slots, dtype=jnp.int32)[None, :]
    chosen = lax.top_k(scores, NB_DEV)[1]
    owners = chosen // slots
    shuffle = jax.random.randint(k_order, (N_ADAPTER, NB_DEV), 0, 2 ** 20) * NB_DEV + jnp.arange(NB_DEV, dtype=jnp.int32)[None, :]
    order = jnp.argsort(shuffle, axis=1, stable=True)
    owners = jnp.take_along_axis(owners, order, axis=1)
    within = jax.random.randint(k_within, (N_ADAPTER, NB_DEV), 0, ADP_DEV)
    return (owners * ADP_DEV + within).reshape(-1).astype(jnp.int32)


def with_ends(result, rng, low, high):
    index_at = [jax.random.randint(jax.random.fold_in(rng, axis), (), 0, length) for axis, length in enumerate(result.shape)]
    widest = result.shape.index(max(result.shape))
    beside = index_at[:widest] + [(index_at[widest] + 1) % result.shape[widest]] + index_at[widest + 1:]
    return result.at[tuple(index_at)].set(low).at[tuple(beside)].set(high)


def block_levels(key, extent, shards, least, high):
    level = 1.0
    for axis_at, blocks in shards:
        heights = jax.random.uniform(jax.random.fold_in(jax.random.fold_in(key, 6), axis_at), (blocks,), jnp.float32, least / len(shards), high / len(shards))
        level = level * jnp.repeat(jnp.exp(heights), extent[axis_at] // blocks).reshape((-1,) + (1,) * (len(extent) - 1 - axis_at))
    return level


def scatter_about(rng, dims, width, reach, pieces=(), kind=jnp.bfloat16):
    level = block_levels(rng, dims, pieces, -0.22, 0.18) if pieces else 1.0
    drawn = jax.random.normal(rng, dims, jnp.float32) * width * level
    return jnp.minimum(jnp.maximum(drawn, -reach), reach).astype(kind)


def setup_inputs(seed: int = 0, part: int = 0) -> dict:
    seeds = jax.random.split(jax.random.key(seed), 6)
    part_keys = jax.random.split(jax.random.fold_in(seeds[5], part), 6)
    tokens = draw_tokens(jax.random.fold_in(jax.random.fold_in(seeds[5], part), 71), part)
    request_block_adapter = draw_request_block_adapter(jax.random.fold_in(jax.random.fold_in(seeds[5], part), 71), part)
    request_block_rows = with_ends(jax.random.randint(part_keys[2], (BLOCKS,), 1, RB + 1), jax.random.fold_in(part_keys[2], 1), 1, RB).astype(jnp.int32)
    adapter_down_weight = scatter_about(seeds[3], (ADAPTER_TOTAL, MODEL_WIDTH, ADAPTER_RANK), MODEL_WIDTH ** -0.5, 0.109375, ((0, 16),))
    adapter_up_weight = scatter_about(seeds[4], (ADAPTER_TOTAL, ADAPTER_RANK, MODEL_WIDTH), ADAPTER_RANK ** -0.5, 0.75, ((0, 16),))
    return dict(tokens=tokens, request_block_adapter=request_block_adapter, request_block_rows=request_block_rows, adapter_down_weight=adapter_down_weight, adapter_up_weight=adapter_up_weight)


def reference(tokens, request_block_adapter, request_block_rows, adapter_down_weight, adapter_up_weight):
    values = tokens.astype(jnp.float32)
    mean_sq = lax.optimization_barrier(jnp.mean(values * values, axis=-1, keepdims=True))
    normed = (values * lax.rsqrt(mean_sq + 1e-06)).astype(jnp.bfloat16)
    grouped = normed.reshape(N_ADAPTER, NB_DEV, RB, MODEL_WIDTH)
    tenants = request_block_adapter.reshape(N_ADAPTER, NB_DEV).astype(jnp.int32)

    def one_group(pair):
        hidden_state, selected_adapter = pair
        projected_rows = adapter_down_weight[selected_adapter].astype(jnp.float32)
        down_matrix = jnp.einsum('brd,bdk->brk', hidden_state.astype(jnp.float32), projected_rows).astype(jnp.bfloat16)
        expanded_rows = adapter_up_weight[selected_adapter].astype(jnp.float32)
        lowrank_update = jnp.einsum('lwp,lpu->lwu', down_matrix.astype(jnp.float32), expanded_rows)
        return lowrank_update.astype(jnp.bfloat16)
    lowrank_update = lax.map(one_group, (grouped, tenants)).reshape(BLOCKS, RB, MODEL_WIDTH)
    live = jnp.arange(RB, dtype=jnp.int32)[None, :] < request_block_rows[:, None]
    mixed = values + jnp.where(live[:, :, None], lowrank_update.astype(jnp.float32), jnp.float32(0.0))
    return mixed.astype(jnp.bfloat16)
```

```python
import functools

import jax
import jax.numpy as jnp
from jax import lax
from jax.experimental import pallas as pl
from jax.experimental.pallas import tpu as pltpu
from jax.sharding import PartitionSpec as P

LANES = 128
HALF = 64
EIGHT = 8
VMEM = pl.BlockSpec(memory_space=pltpu.VMEM)
SMEM = pl.BlockSpec(memory_space=pltpu.SMEM)


def normalise(tokens):
    values = tokens.astype(jnp.float32)
    mean_sq = jnp.mean(values * values, axis=-1, keepdims=True)
    return (values, (values * lax.rsqrt(mean_sq + 1e-06)).astype(jnp.bfloat16))


def resident_update(hidden_state, block_labels, adapter_down_weight, adapter_up_weight):
    feature_width = hidden_state.shape[-1]
    leading = hidden_state.shape[:-1]
    resident_rows, unused_value, inner_rank = adapter_down_weight.shape
    flattened_tokens = hidden_state.reshape(-1, feature_width)
    down_matrix = jnp.einsum(
        "tq,iqg->tig", flattened_tokens, adapter_down_weight, preferred_element_type=jnp.float32
    )
    down_matrix = down_matrix.astype(jnp.bfloat16).reshape(
        flattened_tokens.shape[0], resident_rows * inner_rank
    )
    column_owner = jnp.arange(resident_rows * inner_rank, dtype=jnp.int32) // inner_rank
    picked = block_labels.reshape(-1, 1) == column_owner[None, :]
    down_matrix = jnp.where(picked, down_matrix, jnp.zeros_like(down_matrix))
    lowrank_update = jnp.dot(
        down_matrix,
        adapter_up_weight.reshape(resident_rows * inner_rank, feature_width),
        preferred_element_type=jnp.float32,
    )
    return lowrank_update.astype(jnp.bfloat16).reshape(leading + (feature_width,))


def rows_to_holders(
    tokens, request_block_adapter, request_block_rows, adapter_down_weight, adapter_up_weight
):
    blocks, rows, feature_width = tokens.shape
    devices = lax.axis_size("adapter")
    resident_rows = adapter_down_weight.shape[0]
    slots = max(1, 4 * blocks // devices)
    values, normed = normalise(tokens)
    owner = request_block_adapter // resident_rows
    within = request_block_adapter - owner * resident_rows
    serial = jnp.arange(blocks, dtype=jnp.int32)
    earlier = (owner[:, None] == owner[None, :]) & (serial[None, :] < serial[:, None])
    position = owner * slots + jnp.sum(earlier, axis=1)
    outgoing = (
        jnp.zeros((devices * slots, rows, feature_width), jnp.bfloat16).at[position].set(normed)
    )
    outgoing = outgoing.reshape(devices, slots, rows, feature_width)
    block_labels = jnp.full((devices * slots,), -1, jnp.int32).at[position].set(within)
    block_labels = jnp.broadcast_to(block_labels[:, None], (devices * slots, rows)).reshape(
        devices, slots, rows
    )
    arriving_rows, row_markers = (
        lax.all_to_all(outgoing, "adapter", split_axis=0, concat_axis=0, tiled=True),
        lax.all_to_all(block_labels, "adapter", split_axis=0, concat_axis=0, tiled=True),
    )
    lowrank_update = resident_update(
        arriving_rows, row_markers, adapter_down_weight, adapter_up_weight
    )
    returned = lax.all_to_all(lowrank_update, "adapter", split_axis=0, concat_axis=0, tiled=True)
    mine = returned.reshape(devices * slots, rows, feature_width)[position]
    live = jnp.arange(rows, dtype=jnp.int32)[None, :] < request_block_rows[:, None]
    mixed = values + jnp.where(live[:, :, None], mine.astype(jnp.float32), jnp.float32(0.0))
    return mixed.astype(jnp.bfloat16)


def lanes_of(rows):
    return lax.broadcasted_iota(jnp.int32, (rows, LANES), 1)


def pack_all(read, out_ref, devices, total):
    half, part = total // 2, total // devices
    low = lanes_of(half) < HALF
    for j in range(devices):
        out_ref[j, 0:total, :] = read(0, total, j).astype(jnp.bfloat16)
    for i in range(devices // 2):
        upper = read(0, half, devices + i).astype(jnp.float32)
        lower = read(half, half, devices + i).astype(jnp.float32)
        even = jnp.where(low, upper, pltpu.roll(lower, HALF, 1))
        odd = jnp.where(low, pltpu.roll(upper, HALF, 1), lower)
        out_ref[2 * i, total : total + half, :] = even.astype(jnp.bfloat16)
        out_ref[2 * i + 1, total : total + half, :] = odd.astype(jnp.bfloat16)
    last = devices + devices // 2
    group = lanes_of(part) // EIGHT
    pieces = [read(m * part, part, last).astype(jnp.float32) for m in range(devices)]
    for j in range(devices):
        merged = pieces[j]
        for m in range(devices):
            if m != j:
                shifted = pltpu.roll(pieces[m], (EIGHT * (m - j)) % LANES, 1)
                merged = jnp.where(group == m, shifted, merged)
        out_ref[j, total + half : total + half + part, :] = merged.astype(jnp.bfloat16)


def unpack_second(share, devices, total):
    half, part = total // 2, total // devices
    first = share[total : total + half, :].astype(jnp.float32)
    rest = share[total + half : total + half + part, :].astype(jnp.float32)
    halves = jnp.concatenate([first, pltpu.roll(first, HALF, 1)], axis=0)
    eights = jnp.concatenate(
        [pltpu.roll(rest, (HALF - EIGHT * m) % LANES, 1) for m in range(devices)], axis=0
    )
    return jnp.where(lanes_of(total) < HALF, halves, eights)


def weight_pack_kernel(devices, total, which_ref, weight_ref, out_ref):
    start = pl.multiple_of(which_ref[0] * total, total)

    def read(row, count, tile):
        return weight_ref[pl.ds(start + row, count), tile * LANES : (tile + 1) * LANES]

    pack_all(read, out_ref, devices, total)


def token_pack_kernel(devices, total, position_ref, tokens_ref, out_ref, sorted_ref):
    blocks, rows, width = tokens_ref.shape

    def one(b, carry):
        values = tokens_ref[b].astype(jnp.float32)
        mean_sq = jnp.mean(values * values, axis=-1, keepdims=True)
        start = pl.multiple_of(position_ref[b] * rows, rows)
        sorted_ref[pl.ds(start, rows), :] = values * lax.rsqrt(mean_sq + 1e-06)
        return carry

    lax.fori_loop(0, blocks, one, 0, unroll=4)

    def read(row, count, tile):
        return sorted_ref[row : row + count, tile * LANES : (tile + 1) * LANES]

    pack_all(read, out_ref, devices, total)


def fill_labels(devices, blocks, rows, labels_ref, label_rows_ref):
    def one(b, carry):
        for s in range(devices):
            start = pl.multiple_of(b * rows, rows)
            label_rows_ref[s, pl.ds(start, rows), :] = jnp.full(
                (rows, LANES), labels_ref[s * blocks + b], jnp.int32
            )
        return carry

    lax.fori_loop(0, blocks, one, 0)
    total = blocks * rows
    spare = label_rows_ref.shape[1] - total
    for s in range(devices):
        label_rows_ref[s, total : total + spare, :] = jnp.full((spare, LANES), -1, jnp.int32)


def down_kernel(
    devices,
    blocks,
    rows,
    window,
    resident,
    labels_ref,
    starts_ref,
    group_ref,
    rows_ref,
    own_ref,
    twin_ref,
    out_ref,
    spread_ref,
    sum_ref,
    label_rows_ref,
):
    total = blocks * rows
    weight_rows = resident // 2 * HALF
    fill_labels(devices, blocks, rows, labels_ref, label_rows_ref)
    inside = lanes_of(total) < HALF + EIGHT

    def spread(s, carry):
        spread_ref[s, 0:total, 0:LANES] = rows_ref[s, 0:total, :].astype(jnp.float32)
        second = unpack_second(rows_ref.at[s], devices, total)
        spread_ref[s, 0:total, LANES:] = jnp.where(inside, second, 0.0)
        spread_ref[s, total : total + window, :] = jnp.zeros((window, 2 * LANES), jnp.float32)
        return carry

    lax.fori_loop(0, devices, spread, 0)
    group = group_ref[0]
    own_at = group * (resident // 2)
    twin_at = (1 - group) * (resident // 2)
    upper = (lanes_of(window) >= HALF).astype(jnp.int32)

    def weight_of(ref, h):
        second = unpack_second(ref.at[h], devices, weight_rows).astype(jnp.bfloat16)
        return jnp.concatenate([ref[h, 0:weight_rows, :], second], axis=1)

    def holder(h, carry):
        own = weight_of(own_ref, h)
        twin = weight_of(twin_ref, h)
        for s in range(devices):
            start = pl.multiple_of(starts_ref[s * devices + h] * rows, rows)
            part = spread_ref[s, pl.ds(start, window), :].astype(jnp.bfloat16)
            label = label_rows_ref[s, pl.ds(start, window), :] - h * resident - upper
            dims = (((1,), (1,)), ((), ()))
            mine = lax.dot_general(part, own, dims, preferred_element_type=jnp.float32)
            other = lax.dot_general(part, twin, dims, preferred_element_type=jnp.float32)
            picked = jnp.zeros((window, LANES), jnp.float32)
            for t in range(resident // 4):
                columns = slice(t * LANES, (t + 1) * LANES)
                picked = jnp.where(label == own_at + 2 * t, mine[:, columns], picked)
                picked = jnp.where(label == twin_at + 2 * t, other[:, columns], picked)
            sum_ref[s, pl.ds(start, window), :] = picked + pltpu.roll(picked, HALF, 1)
        return carry

    lax.fori_loop(0, devices, holder, 0)
    low = lanes_of(total // 2) < HALF

    def leave(s, carry):
        out_ref[s] = jnp.where(
            low, sum_ref[s, 0 : total // 2, :], sum_ref[s, total // 2 : total, :]
        ).astype(out_ref.dtype)
        return carry

    lax.fori_loop(0, devices, leave, 0)


def up_kernel(
    devices,
    blocks,
    rows,
    window,
    resident,
    labels_ref,
    starts_ref,
    group_ref,
    down_ref,
    own_ref,
    twin_ref,
    out_ref,
    twice_ref,
    delta_ref,
    label_rows_ref,
):
    total = blocks * rows
    half, share = total // 2, total // devices
    weight_rows = resident // 2 * HALF
    fill_labels(devices, blocks, rows, labels_ref, label_rows_ref)
    low = lanes_of(half) < HALF

    def spread(s, carry):
        packed = down_ref[s].astype(jnp.bfloat16).astype(jnp.float32)
        turned = pltpu.roll(packed, HALF, 1)
        twice_ref[s, 0:half, :] = jnp.where(low, packed, turned)
        twice_ref[s, half:total, :] = jnp.where(low, turned, packed)
        twice_ref[s, total : total + window, :] = jnp.zeros((window, LANES), jnp.float32)
        return carry

    lax.fori_loop(0, devices, spread, 0)
    group = group_ref[0]
    own_at = group * (resident // 2)
    twin_at = (1 - group) * (resident // 2)
    upper = (lanes_of(window) >= HALF).astype(jnp.int32)

    def weight_of(ref, h):
        second = unpack_second(ref.at[h], devices, weight_rows).astype(jnp.bfloat16)
        return jnp.concatenate([ref[h, 0:weight_rows, :], second], axis=1)

    def holder(h, carry):
        own = weight_of(own_ref, h)
        twin = weight_of(twin_ref, h)
        for s in range(devices):
            start = pl.multiple_of(starts_ref[s * devices + h] * rows, rows)
            part = twice_ref[s, pl.ds(start, window), :]
            label = label_rows_ref[s, pl.ds(start, window), :] - h * resident - upper
            sides = []
            for at in (own_at, twin_at):
                placed = [
                    jnp.where(label == at + 2 * t, part, 0.0) for t in range(resident // 4)
                ]
                sides.append(jnp.concatenate(placed, axis=1).astype(jnp.bfloat16))
            delta_ref[s, pl.ds(start, window), :] = jnp.dot(
                sides[0], own, preferred_element_type=jnp.float32
            ) + jnp.dot(sides[1], twin, preferred_element_type=jnp.float32)
        return carry

    lax.fori_loop(0, devices, holder, 0)
    eighth = lanes_of(share) // EIGHT

    def leave(s, carry):
        out_ref[s, 0:total, :] = delta_ref[s, 0:total, 0:LANES].astype(jnp.bfloat16)
        second = delta_ref[s, 0:total, LANES:]
        halves = jnp.where(low, second[0:half], pltpu.roll(second[half:total], HALF, 1))
        out_ref[s, total : total + half, :] = halves.astype(jnp.bfloat16)
        merged = jnp.zeros((share, LANES), jnp.float32)
        for m in range(devices):
            piece = second[m * share : (m + 1) * share]
            shifted = pltpu.roll(piece, (EIGHT * m - HALF) % LANES, 1)
            merged = jnp.where(eighth == m, shifted, merged)
        out_ref[s, total + half : total + half + share, :] = merged.astype(jnp.bfloat16)
        return carry

    lax.fori_loop(0, devices, leave, 0)


def mix_kernel(devices, position_ref, used_ref, tokens_ref, returned_ref, out_ref, delta_ref):
    blocks, rows, width = tokens_ref.shape
    total = blocks * rows
    half, share = total // 2, total // devices
    low = lanes_of(half) < HALF
    for j in range(devices):
        delta_ref[:, j * LANES : (j + 1) * LANES] = returned_ref[j, 0:total, :].astype(jnp.float32)
    for i in range(devices // 2):
        even = returned_ref[2 * i, total : total + half, :].astype(jnp.float32)
        odd = returned_ref[2 * i + 1, total : total + half, :].astype(jnp.float32)
        columns = slice((devices + i) * LANES, (devices + i + 1) * LANES)
        delta_ref[0:half, columns] = jnp.where(low, even, pltpu.roll(odd, HALF, 1))
        delta_ref[half:total, columns] = jnp.where(low, pltpu.roll(even, HALF, 1), odd)
    last = devices + devices // 2
    eighth = lanes_of(share) // EIGHT
    pieces = [
        returned_ref[j, total + half : total + half + share, :].astype(jnp.float32)
        for j in range(devices)
    ]
    for m in range(devices):
        merged = pieces[m]
        for j in range(devices):
            if j != m:
                shifted = pltpu.roll(pieces[j], (EIGHT * (j - m)) % LANES, 1)
                merged = jnp.where(eighth == j, shifted, merged)
        delta_ref[m * share : (m + 1) * share, last * LANES : (last + 1) * LANES] = merged
    row = lax.broadcasted_iota(jnp.int32, (rows, width), 0)

    def one(b, carry):
        start = pl.multiple_of(position_ref[b] * rows, rows)
        delta = jnp.where(row < used_ref[b], delta_ref[pl.ds(start, rows), :], 0.0)
        out_ref[b] = (tokens_ref[b].astype(jnp.float32) + delta).astype(jnp.bfloat16)
        return carry

    lax.fori_loop(0, blocks, one, 0, unroll=4)


def call(kernel, out_shape, in_specs, scratch, flops, moved):
    return pl.pallas_call(
        kernel,
        out_shape=out_shape,
        in_specs=in_specs,
        out_specs=VMEM,
        scratch_shapes=scratch,
        compiler_params=pltpu.CompilerParams(vmem_limit_bytes=48 * 2**20),
        cost_estimate=pl.CostEstimate(flops=flops, bytes_accessed=moved, transcendentals=0),
    )


def exchange(value):
    return lax.all_to_all(value, "adapter", split_axis=0, concat_axis=0, tiled=True)


def features_to_devices(
    tokens, request_block_adapter, request_block_rows, adapter_down_weight, adapter_up_weight
):
    blocks, rows, width = tokens.shape
    devices = lax.axis_size("adapter")
    resident, unused_width, rank = adapter_down_weight.shape
    slots = max(1, 4 * blocks // devices)
    window = slots * rows
    total = blocks * rows
    weight_rows = resident // 2 * rank
    bf16, f32, i32 = jnp.bfloat16, jnp.float32, jnp.int32

    serial = jnp.arange(blocks, dtype=i32)
    key = request_block_adapter * blocks + serial
    position = jnp.sum(key[None, :] < key[:, None], axis=1).astype(i32)
    ordered = jnp.sum(
        jnp.where(position[:, None] == serial[None, :], request_block_adapter[:, None], 0), axis=0
    ).astype(i32)
    labels = lax.all_gather(ordered, "adapter")
    holders = jnp.arange(devices, dtype=i32) * resident
    starts = jnp.sum(labels[:, None, :] < holders[None, :, None], axis=2).astype(i32).reshape(-1)
    labels = labels.reshape(-1)
    group = lax.axis_index("groups").astype(i32).reshape(1)

    def packed(count):
        return jax.ShapeDtypeStruct((devices, count + count // 2 + count // devices, LANES), bf16)

    size = devices * packed(total).shape[1] * LANES * 2
    pack_weight = call(
        functools.partial(weight_pack_kernel, devices, weight_rows),
        packed(weight_rows),
        [SMEM, VMEM],
        [],
        0,
        3 * size,
    )
    down_share = exchange(
        pack_weight(group, adapter_down_weight.transpose(0, 2, 1).reshape(resident * rank, width))
    )
    down_twin = lax.ppermute(down_share, "groups", [(0, 1), (1, 0)])
    up_share = exchange(pack_weight(group, adapter_up_weight.reshape(resident * rank, width)))
    up_twin = lax.ppermute(up_share, "groups", [(0, 1), (1, 0)])
    outgoing = call(
        functools.partial(token_pack_kernel, devices, total),
        packed(total),
        [SMEM, VMEM],
        [pltpu.VMEM((total, width), f32)],
        0,
        2 * size,
    )(position, tokens)
    arrived = exchange(outgoing)

    longest = total + window
    flops = 2 * devices * devices * window * 2 * weight_rows * 2 * LANES
    partial = call(
        functools.partial(down_kernel, devices, blocks, rows, window, resident),
        jax.ShapeDtypeStruct((devices, total // 2, LANES), f32),
        [SMEM, SMEM, SMEM, VMEM, VMEM, VMEM],
        [
            pltpu.VMEM((devices, longest, 2 * LANES), f32),
            pltpu.VMEM((devices, longest, LANES), f32),
            pltpu.VMEM((devices, longest, LANES), i32),
        ],
        flops,
        3 * size,
    )(labels, starts, group, arrived, down_share, down_twin)
    down = lax.psum(partial, "adapter")
    leaving = call(
        functools.partial(up_kernel, devices, blocks, rows, window, resident),
        packed(total),
        [SMEM, SMEM, SMEM, VMEM, VMEM, VMEM],
        [
            pltpu.VMEM((devices, longest, LANES), f32),
            pltpu.VMEM((devices, longest, 2 * LANES), f32),
            pltpu.VMEM((devices, longest, LANES), i32),
        ],
        flops,
        3 * size,
    )(labels, starts, group, down, up_share, up_twin)
    returned = exchange(leaving)
    return call(
        functools.partial(mix_kernel, devices),
        jax.ShapeDtypeStruct(tokens.shape, bf16),
        [SMEM, SMEM, VMEM, VMEM],
        [pltpu.VMEM((total, width), f32)],
        0,
        3 * size,
    )(position, request_block_rows, tokens, returned)


def solution(mesh):
    placed = (
        P(("groups", "adapter"), None, None),
        P(("groups", "adapter")),
        P(("groups", "adapter")),
        P("adapter", None, None),
        P("adapter", None, None),
    )

    def per_device(tokens, request_block_adapter, request_block_rows, down_weight, up_weight):
        devices = mesh.shape["adapter"]
        even_deal = devices * EIGHT == LANES and tokens.shape[2] == devices * (
            LANES + HALF + EIGHT
        )
        even_deal = even_deal and mesh.shape["groups"] == 2 and down_weight.shape[2] == HALF
        plan = features_to_devices if even_deal else rows_to_holders
        return plan(tokens, request_block_adapter, request_block_rows, down_weight, up_weight)

    return jax.shard_map(
        per_device,
        mesh=mesh,
        in_specs=placed,
        out_specs=P(("groups", "adapter"), None, None),
        check_vma=False,
    )
```

```python
import functools

import jax
import jax.numpy as jnp
from jax import lax
from jax.experimental import pallas as pl
from jax.experimental.pallas import tpu as pltpu
from jax.sharding import PartitionSpec as P

LANES = 128
HALF = 64
EIGHT = 8
VMEM = pl.BlockSpec(memory_space=pltpu.VMEM)
SMEM = pl.BlockSpec(memory_space=pltpu.SMEM)


def normalise(tokens):
    values = tokens.astype(jnp.float32)
    mean_sq = jnp.mean(values * values, axis=-1, keepdims=True)
    return (values, (values * lax.rsqrt(mean_sq + 1e-06)).astype(jnp.bfloat16))


def resident_update(hidden_state, block_labels, adapter_down_weight, adapter_up_weight):
    feature_width = hidden_state.shape[-1]
    leading = hidden_state.shape[:-1]
    resident_rows, unused_value, inner_rank = adapter_down_weight.shape
    flattened_tokens = hidden_state.reshape(-1, feature_width)
    down_matrix = jnp.einsum(
        "tq,iqg->tig", flattened_tokens, adapter_down_weight, preferred_element_type=jnp.float32
    )
    down_matrix = down_matrix.astype(jnp.bfloat16).reshape(
        flattened_tokens.shape[0], resident_rows * inner_rank
    )
    column_owner = jnp.arange(resident_rows * inner_rank, dtype=jnp.int32) // inner_rank
    picked = block_labels.reshape(-1, 1) == column_owner[None, :]
    down_matrix = jnp.where(picked, down_matrix, jnp.zeros_like(down_matrix))
    lowrank_update = jnp.dot(
        down_matrix,
        adapter_up_weight.reshape(resident_rows * inner_rank, feature_width),
        preferred_element_type=jnp.float32,
    )
    return lowrank_update.astype(jnp.bfloat16).reshape(leading + (feature_width,))


def rows_to_holders(
    tokens, request_block_adapter, request_block_rows, adapter_down_weight, adapter_up_weight
):
    blocks, rows, feature_width = tokens.shape
    devices = lax.axis_size("adapter")
    resident_rows = adapter_down_weight.shape[0]
    slots = max(1, 4 * blocks // devices)
    values, normed = normalise(tokens)
    owner = request_block_adapter // resident_rows
    within = request_block_adapter - owner * resident_rows
    serial = jnp.arange(blocks, dtype=jnp.int32)
    earlier = (owner[:, None] == owner[None, :]) & (serial[None, :] < serial[:, None])
    position = owner * slots + jnp.sum(earlier, axis=1)
    outgoing = (
        jnp.zeros((devices * slots, rows, feature_width), jnp.bfloat16).at[position].set(normed)
    )
    outgoing = outgoing.reshape(devices, slots, rows, feature_width)
    block_labels = jnp.full((devices * slots,), -1, jnp.int32).at[position].set(within)
    block_labels = jnp.broadcast_to(block_labels[:, None], (devices * slots, rows)).reshape(
        devices, slots, rows
    )
    arriving_rows, row_markers = (
        lax.all_to_all(outgoing, "adapter", split_axis=0, concat_axis=0, tiled=True),
        lax.all_to_all(block_labels, "adapter", split_axis=0, concat_axis=0, tiled=True),
    )
    lowrank_update = resident_update(
        arriving_rows, row_markers, adapter_down_weight, adapter_up_weight
    )
    returned = lax.all_to_all(lowrank_update, "adapter", split_axis=0, concat_axis=0, tiled=True)
    mine = returned.reshape(devices * slots, rows, feature_width)[position]
    live = jnp.arange(rows, dtype=jnp.int32)[None, :] < request_block_rows[:, None]
    mixed = values + jnp.where(live[:, :, None], mine.astype(jnp.float32), jnp.float32(0.0))
    return mixed.astype(jnp.bfloat16)


def lanes_of(rows):
    return lax.broadcasted_iota(jnp.int32, (rows, LANES), 1)


def share_rows(total, devices):
    return total + total // 2 + total // devices


def pack_all(read, out_ref, devices, total, base):
    half, part = total // 2, total // devices
    low = lanes_of(half) < HALF
    at_half, at_part = base + total, base + total + half
    for j in range(devices):
        out_ref[j, base : base + total, :] = read(0, total, j).astype(jnp.bfloat16)
    for i in range(devices // 2):
        upper = read(0, half, devices + i).astype(jnp.float32)
        lower = read(half, half, devices + i).astype(jnp.float32)
        even = jnp.where(low, upper, pltpu.roll(lower, HALF, 1))
        odd = jnp.where(low, pltpu.roll(upper, HALF, 1), lower)
        out_ref[2 * i, at_half : at_half + half, :] = even.astype(jnp.bfloat16)
        out_ref[2 * i + 1, at_half : at_half + half, :] = odd.astype(jnp.bfloat16)
    last = devices + devices // 2
    group = lanes_of(part) // EIGHT
    pieces = [read(m * part, part, last).astype(jnp.float32) for m in range(devices)]
    for j in range(devices):
        merged = pieces[j]
        for m in range(devices):
            if m != j:
                shifted = pltpu.roll(pieces[m], (EIGHT * (m - j)) % LANES, 1)
                merged = jnp.where(group == m, shifted, merged)
        out_ref[j, at_part : at_part + part, :] = merged.astype(jnp.bfloat16)


def unpack_second(share, devices, total, base=0):
    half, part = total // 2, total // devices
    at_half, at_part = base + total, base + total + half
    first = share[at_half : at_half + half, :].astype(jnp.float32)
    rest = share[at_part : at_part + part, :].astype(jnp.float32)
    halves = jnp.concatenate([first, pltpu.roll(first, HALF, 1)], axis=0)
    eights = jnp.concatenate(
        [pltpu.roll(rest, (HALF - EIGHT * m) % LANES, 1) for m in range(devices)], axis=0
    )
    return jnp.where(lanes_of(total) < HALF, halves, eights)


def weight_of(ref, h, devices, weight_rows, base=0):
    second = unpack_second(ref.at[h], devices, weight_rows, base).astype(jnp.bfloat16)
    return jnp.concatenate([ref[h, base : base + weight_rows, :], second], axis=1)


def weight_pack_kernel(devices, total, which_ref, weight_ref, out_ref):
    start = pl.multiple_of(which_ref[0] * total, total)

    def read(row, count, tile):
        return weight_ref[pl.ds(start + row, count), tile * LANES : (tile + 1) * LANES]

    pack_all(read, out_ref, devices, total, 0)


def first_pack_kernel(
    devices, total, weight_rows, which_ref, position_ref, tokens_ref, weight_ref, out_ref, sorted_ref
):
    blocks, rows, width = tokens_ref.shape

    def one(b, carry):
        values = tokens_ref[b].astype(jnp.float32)
        mean_sq = jnp.mean(values * values, axis=-1, keepdims=True)
        start = pl.multiple_of(position_ref[b] * rows, rows)
        sorted_ref[pl.ds(start, rows), :] = values * lax.rsqrt(mean_sq + 1e-06)
        return carry

    lax.fori_loop(0, blocks, one, 0, unroll=4)

    def read_rows(row, count, tile):
        return sorted_ref[row : row + count, tile * LANES : (tile + 1) * LANES]

    pack_all(read_rows, out_ref, devices, total, 0)
    start = pl.multiple_of(which_ref[0] * weight_rows, weight_rows)

    def read_weight(row, count, tile):
        return weight_ref[pl.ds(start + row, count), tile * LANES : (tile + 1) * LANES]

    pack_all(read_weight, out_ref, devices, weight_rows, share_rows(total, devices))


def fill_labels(devices, blocks, rows, labels_ref, label_rows_ref):
    def one(b, carry):
        for s in range(devices):
            start = pl.multiple_of(b * rows, rows)
            label_rows_ref[s, pl.ds(start, rows), :] = jnp.full(
                (rows, LANES), labels_ref[s * blocks + b], jnp.int32
            )
        return carry

    lax.fori_loop(0, blocks, one, 0)
    total = blocks * rows
    spare = label_rows_ref.shape[1] - total
    for s in range(devices):
        label_rows_ref[s, total : total + spare, :] = jnp.full((spare, LANES), -1, jnp.int32)


def down_kernel(
    devices,
    blocks,
    rows,
    window,
    resident,
    labels_ref,
    starts_ref,
    group_ref,
    first_ref,
    twin_ref,
    out_ref,
    spread_ref,
    sum_ref,
    label_rows_ref,
    batch_ref,
    product_ref,
):
    total = blocks * rows
    weight_rows = resident // 2 * HALF
    batch = total // window
    fill_labels(devices, blocks, rows, labels_ref, label_rows_ref)
    inside = lanes_of(total) < HALF + EIGHT

    def spread(s, carry):
        spread_ref[s, 0:total, 0:LANES] = first_ref[s, 0:total, :].astype(jnp.float32)
        second = unpack_second(first_ref.at[s], devices, total)
        spread_ref[s, 0:total, LANES:] = jnp.where(inside, second, 0.0)
        spread_ref[s, total : total + window, :] = jnp.zeros((window, 2 * LANES), jnp.float32)
        return carry

    lax.fori_loop(0, devices, spread, 0)
    group = group_ref[0]
    own_at = group * (resident // 2)
    twin_at = (1 - group) * (resident // 2)
    upper = (lanes_of(window) >= HALF).astype(jnp.int32)
    dims = (((1,), (1,)), ((), ()))

    def holder(h, carry):
        own = weight_of(first_ref, h, devices, weight_rows, share_rows(total, devices))
        twin = weight_of(twin_ref, h, devices, weight_rows)
        both = jnp.concatenate([own, twin], axis=0)

        def start_of(s):
            return pl.multiple_of(starts_ref[s * devices + h] * rows, rows)

        for s in range(devices):
            batch_ref[s * window : (s + 1) * window, :] = spread_ref[
                s, pl.ds(start_of(s), window), :
            ].astype(jnp.bfloat16)
        for c in range(devices // batch):
            piece = slice(c * total, (c + 1) * total)
            product_ref[piece, :] = lax.dot_general(
                batch_ref[piece, :], both, dims, preferred_element_type=jnp.float32
            )
        for s in range(devices):
            start = start_of(s)
            label = label_rows_ref[s, pl.ds(start, window), :] - h * resident - upper
            picked = jnp.zeros((window, LANES), jnp.float32)
            for t in range(resident // 2):
                at = own_at + 2 * t if t < resident // 4 else twin_at + 2 * t - resident // 2
                product = product_ref[
                    s * window : (s + 1) * window, t * LANES : (t + 1) * LANES
                ]
                picked = jnp.where(label == at, product, picked)
            sum_ref[s, pl.ds(start, window), :] = picked + pltpu.roll(picked, HALF, 1)
        return carry

    lax.fori_loop(0, devices, holder, 0)
    low = lanes_of(total // 2) < HALF

    def leave(s, carry):
        out_ref[s] = jnp.where(
            low, sum_ref[s, 0 : total // 2, :], sum_ref[s, total // 2 : total, :]
        ).astype(out_ref.dtype)
        return carry

    lax.fori_loop(0, devices, leave, 0)


def add_kernel(devices, parts_ref, out_ref):
    total = parts_ref[0].astype(jnp.float32)
    for j in range(1, devices):
        total = total + parts_ref[j].astype(jnp.float32)
    rounded = total.astype(jnp.bfloat16)
    for j in range(devices):
        out_ref[j] = rounded


def up_kernel(
    devices,
    blocks,
    rows,
    window,
    resident,
    labels_ref,
    starts_ref,
    group_ref,
    down_ref,
    own_ref,
    twin_ref,
    out_ref,
    twice_ref,
    delta_ref,
    label_rows_ref,
    batch_ref,
):
    total = blocks * rows
    half, share = total // 2, total // devices
    weight_rows = resident // 2 * HALF
    batch = total // window
    fill_labels(devices, blocks, rows, labels_ref, label_rows_ref)
    low = lanes_of(half) < HALF

    def spread(s, carry):
        packed = down_ref[s].astype(jnp.float32)
        turned = pltpu.roll(packed, HALF, 1)
        twice_ref[s, 0:half, :] = jnp.where(low, packed, turned)
        twice_ref[s, half:total, :] = jnp.where(low, turned, packed)
        twice_ref[s, total : total + window, :] = jnp.zeros((window, LANES), jnp.float32)
        return carry

    lax.fori_loop(0, devices, spread, 0)
    group = group_ref[0]
    own_at = group * (resident // 2)
    twin_at = (1 - group) * (resident // 2)
    upper = (lanes_of(window) >= HALF).astype(jnp.int32)

    def holder(h, carry):
        own = weight_of(own_ref, h, devices, weight_rows)
        twin = weight_of(twin_ref, h, devices, weight_rows)
        both = jnp.concatenate([own, twin], axis=0)

        def start_of(s):
            return pl.multiple_of(starts_ref[s * devices + h] * rows, rows)

        for s in range(devices):
            start = start_of(s)
            part = twice_ref[s, pl.ds(start, window), :]
            label = label_rows_ref[s, pl.ds(start, window), :] - h * resident - upper
            for t in range(resident // 2):
                at = own_at + 2 * t if t < resident // 4 else twin_at + 2 * t - resident // 2
                batch_ref[s * window : (s + 1) * window, t * LANES : (t + 1) * LANES] = jnp.where(
                    label == at, part, 0.0
                ).astype(jnp.bfloat16)
        for c in range(devices // batch):
            product = jnp.dot(
                batch_ref[c * total : (c + 1) * total, :], both, preferred_element_type=jnp.float32
            )
            for i in range(batch):
                s = c * batch + i
                delta_ref[s, pl.ds(start_of(s), window), :] = product[
                    i * window : (i + 1) * window
                ]
        return carry

    lax.fori_loop(0, devices, holder, 0)
    eighth = lanes_of(share) // EIGHT

    def leave(s, carry):
        out_ref[s, 0:total, :] = delta_ref[s, 0:total, 0:LANES].astype(jnp.bfloat16)
        second = delta_ref[s, 0:total, LANES:]
        halves = jnp.where(low, second[0:half], pltpu.roll(second[half:total], HALF, 1))
        out_ref[s, total : total + half, :] = halves.astype(jnp.bfloat16)
        merged = jnp.zeros((share, LANES), jnp.float32)
        for m in range(devices):
            piece = second[m * share : (m + 1) * share]
            shifted = pltpu.roll(piece, (EIGHT * m - HALF) % LANES, 1)
            merged = jnp.where(eighth == m, shifted, merged)
        out_ref[s, total + half : total + half + share, :] = merged.astype(jnp.bfloat16)
        return carry

    lax.fori_loop(0, devices, leave, 0)


def mix_kernel(devices, position_ref, used_ref, tokens_ref, returned_ref, out_ref, delta_ref):
    blocks, rows, width = tokens_ref.shape
    total = blocks * rows
    half, share = total // 2, total // devices
    low = lanes_of(half) < HALF
    for j in range(devices):
        delta_ref[:, j * LANES : (j + 1) * LANES] = returned_ref[j, 0:total, :].astype(jnp.float32)
    for i in range(devices // 2):
        even = returned_ref[2 * i, total : total + half, :].astype(jnp.float32)
        odd = returned_ref[2 * i + 1, total : total + half, :].astype(jnp.float32)
        columns = slice((devices + i) * LANES, (devices + i + 1) * LANES)
        delta_ref[0:half, columns] = jnp.where(low, even, pltpu.roll(odd, HALF, 1))
        delta_ref[half:total, columns] = jnp.where(low, pltpu.roll(even, HALF, 1), odd)
    last = devices + devices // 2
    eighth = lanes_of(share) // EIGHT
    pieces = [
        returned_ref[j, total + half : total + half + share, :].astype(jnp.float32)
        for j in range(devices)
    ]
    for m in range(devices):
        merged = pieces[m]
        for j in range(devices):
            if j != m:
                shifted = pltpu.roll(pieces[j], (EIGHT * (j - m)) % LANES, 1)
                merged = jnp.where(eighth == j, shifted, merged)
        delta_ref[m * share : (m + 1) * share, last * LANES : (last + 1) * LANES] = merged
    row = lax.broadcasted_iota(jnp.int32, (rows, width), 0)

    def one(b, carry):
        start = pl.multiple_of(position_ref[b] * rows, rows)
        delta = jnp.where(row < used_ref[b], delta_ref[pl.ds(start, rows), :], 0.0)
        out_ref[b] = (tokens_ref[b].astype(jnp.float32) + delta).astype(jnp.bfloat16)
        return carry

    lax.fori_loop(0, blocks, one, 0, unroll=4)


def call(kernel, out_shape, in_specs, scratch, flops, moved):
    return pl.pallas_call(
        kernel,
        out_shape=out_shape,
        in_specs=in_specs,
        out_specs=VMEM,
        scratch_shapes=scratch,
        compiler_params=pltpu.CompilerParams(vmem_limit_bytes=48 * 2**20),
        cost_estimate=pl.CostEstimate(flops=flops, bytes_accessed=moved, transcendentals=0),
    )


def exchange(value):
    return lax.all_to_all(value, "adapter", split_axis=0, concat_axis=0, tiled=True)


def gather_labels(ordered, devices):
    held = ordered[None]
    step = 1
    while step < devices:
        pairs = [(i, i ^ step) for i in range(devices)]
        held = jnp.concatenate([held, lax.ppermute(held, "adapter", pairs)], axis=0)
        step *= 2
    serial = jnp.arange(devices, dtype=jnp.int32)
    source = jnp.bitwise_xor(lax.axis_index("adapter").astype(jnp.int32), serial)
    chosen = source[:, None] == serial[None, :]
    return jnp.sum(jnp.where(chosen[:, :, None], held[None], 0), axis=1)


def features_to_devices(
    tokens, request_block_adapter, request_block_rows, adapter_down_weight, adapter_up_weight
):
    blocks, rows, width = tokens.shape
    devices = lax.axis_size("adapter")
    resident, unused_width, rank = adapter_down_weight.shape
    slots = max(1, 4 * blocks // devices)
    window = slots * rows
    total = blocks * rows
    weight_rows = resident // 2 * rank
    bf16, f32, i32 = jnp.bfloat16, jnp.float32, jnp.int32

    serial = jnp.arange(blocks, dtype=i32)
    key = request_block_adapter * blocks + serial
    position = jnp.sum(key[None, :] < key[:, None], axis=1).astype(i32)
    ordered = jnp.sum(
        jnp.where(position[:, None] == serial[None, :], request_block_adapter[:, None], 0), axis=0
    ).astype(i32)
    labels = gather_labels(ordered, devices)
    holders = jnp.arange(devices, dtype=i32) * resident
    starts = jnp.sum(labels[:, None, :] < holders[None, :, None], axis=2).astype(i32).reshape(-1)
    labels = labels.reshape(-1)
    group = lax.axis_index("groups").astype(i32).reshape(1)

    def shares(count):
        return jax.ShapeDtypeStruct((devices, count, LANES), bf16)

    row_share, weight_share = share_rows(total, devices), share_rows(weight_rows, devices)
    size = devices * row_share * LANES * 2
    outgoing = call(
        functools.partial(first_pack_kernel, devices, total, weight_rows),
        shares(row_share + weight_share),
        [SMEM, SMEM, VMEM, VMEM],
        [pltpu.VMEM((total, width), f32)],
        0,
        4 * size,
    )(group, position, tokens, adapter_down_weight.transpose(0, 2, 1).reshape(-1, width))
    first = exchange(outgoing)
    swap = [(0, 1), (1, 0)]
    down_twin = lax.ppermute(first[:, row_share:, :], "groups", swap)
    up_packed = call(
        functools.partial(weight_pack_kernel, devices, weight_rows),
        shares(weight_share),
        [SMEM, VMEM],
        [],
        0,
        3 * size,
    )(group, adapter_up_weight.reshape(-1, width))
    up_packed, first = lax.optimization_barrier((up_packed, first))
    up_share = exchange(up_packed)
    up_twin = lax.ppermute(up_share, "groups", swap)

    longest = total + window
    columns = resident * rank
    flops = 2 * devices * devices * window * columns * 2 * LANES
    label_rows = pltpu.VMEM((devices, longest, LANES), i32)
    partial = call(
        functools.partial(down_kernel, devices, blocks, rows, window, resident),
        shares(total // 2),
        [SMEM, SMEM, SMEM, VMEM, VMEM],
        [
            pltpu.VMEM((devices, longest, 2 * LANES), f32),
            pltpu.VMEM((devices, longest, LANES), f32),
            label_rows,
            pltpu.VMEM((devices * window, 2 * LANES), bf16),
            pltpu.VMEM((devices * window, columns), f32),
        ],
        flops,
        3 * size,
    )(labels, starts, group, first, down_twin)
    summed = call(
        functools.partial(add_kernel, devices), shares(total // 2), [VMEM], [], 0, size
    )(exchange(partial))
    down = exchange(summed)
    leaving = call(
        functools.partial(up_kernel, devices, blocks, rows, window, resident),
        shares(row_share),
        [SMEM, SMEM, SMEM, VMEM, VMEM, VMEM],
        [
            pltpu.VMEM((devices, longest, LANES), f32),
            pltpu.VMEM((devices, longest, 2 * LANES), f32),
            label_rows,
            pltpu.VMEM((devices * window, columns), bf16),
        ],
        flops,
        3 * size,
    )(labels, starts, group, down, up_share, up_twin)
    returned = exchange(leaving)
    return call(
        functools.partial(mix_kernel, devices),
        jax.ShapeDtypeStruct(tokens.shape, bf16),
        [SMEM, SMEM, VMEM, VMEM],
        [pltpu.VMEM((total, width), f32)],
        0,
        3 * size,
    )(position, request_block_rows, tokens, returned)


def solution(mesh):
    placed = (
        P(("groups", "adapter"), None, None),
        P(("groups", "adapter")),
        P(("groups", "adapter")),
        P("adapter", None, None),
        P("adapter", None, None),
    )

    def per_device(tokens, request_block_adapter, request_block_rows, down_weight, up_weight):
        devices = mesh.shape["adapter"]
        even_deal = devices * EIGHT == LANES and tokens.shape[2] == devices * (
            LANES + HALF + EIGHT
        )
        even_deal = even_deal and mesh.shape["groups"] == 2 and down_weight.shape[2] == HALF
        plan = features_to_devices if even_deal else rows_to_holders
        return plan(tokens, request_block_adapter, request_block_rows, down_weight, up_weight)

    return jax.shard_map(
        per_device,
        mesh=mesh,
        in_specs=placed,
        out_specs=P(("groups", "adapter"), None, None),
        check_vma=False,
    )
```

```python
import functools

import jax
import jax.numpy as jnp
from jax import lax
from jax.experimental import pallas as pl
from jax.experimental.pallas import tpu as pltpu
from jax.sharding import PartitionSpec as P

LANES = 128
HALF = 64
QUAD = 4
VMEM = pl.BlockSpec(memory_space=pltpu.VMEM)
SMEM = pl.BlockSpec(memory_space=pltpu.SMEM)


def normalise(tokens):
    values = tokens.astype(jnp.float32)
    mean_sq = jnp.mean(values * values, axis=-1, keepdims=True)
    return (values, (values * lax.rsqrt(mean_sq + 1e-06)).astype(jnp.bfloat16))


def resident_update(hidden_state, block_labels, adapter_down_weight, adapter_up_weight):
    feature_width = hidden_state.shape[-1]
    leading = hidden_state.shape[:-1]
    resident_rows, unused_value, inner_rank = adapter_down_weight.shape
    flattened_tokens = hidden_state.reshape(-1, feature_width)
    down_matrix = jnp.einsum(
        "tq,iqg->tig", flattened_tokens, adapter_down_weight, preferred_element_type=jnp.float32
    )
    down_matrix = down_matrix.astype(jnp.bfloat16).reshape(
        flattened_tokens.shape[0], resident_rows * inner_rank
    )
    column_owner = jnp.arange(resident_rows * inner_rank, dtype=jnp.int32) // inner_rank
    picked = block_labels.reshape(-1, 1) == column_owner[None, :]
    down_matrix = jnp.where(picked, down_matrix, jnp.zeros_like(down_matrix))
    lowrank_update = jnp.dot(
        down_matrix,
        adapter_up_weight.reshape(resident_rows * inner_rank, feature_width),
        preferred_element_type=jnp.float32,
    )
    return lowrank_update.astype(jnp.bfloat16).reshape(leading + (feature_width,))


def rows_to_holders(
    tokens, request_block_adapter, request_block_rows, adapter_down_weight, adapter_up_weight
):
    blocks, rows, feature_width = tokens.shape
    devices = lax.axis_size("adapter")
    resident_rows = adapter_down_weight.shape[0]
    slots = max(1, 4 * blocks // devices)
    values, normed = normalise(tokens)
    owner = request_block_adapter // resident_rows
    within = request_block_adapter - owner * resident_rows
    serial = jnp.arange(blocks, dtype=jnp.int32)
    earlier = (owner[:, None] == owner[None, :]) & (serial[None, :] < serial[:, None])
    position = owner * slots + jnp.sum(earlier, axis=1)
    outgoing = (
        jnp.zeros((devices * slots, rows, feature_width), jnp.bfloat16).at[position].set(normed)
    )
    outgoing = outgoing.reshape(devices, slots, rows, feature_width)
    block_labels = jnp.full((devices * slots,), -1, jnp.int32).at[position].set(within)
    block_labels = jnp.broadcast_to(block_labels[:, None], (devices * slots, rows)).reshape(
        devices, slots, rows
    )
    arriving_rows, row_markers = (
        lax.all_to_all(outgoing, "adapter", split_axis=0, concat_axis=0, tiled=True),
        lax.all_to_all(block_labels, "adapter", split_axis=0, concat_axis=0, tiled=True),
    )
    lowrank_update = resident_update(
        arriving_rows, row_markers, adapter_down_weight, adapter_up_weight
    )
    returned = lax.all_to_all(lowrank_update, "adapter", split_axis=0, concat_axis=0, tiled=True)
    mine = returned.reshape(devices * slots, rows, feature_width)[position]
    live = jnp.arange(rows, dtype=jnp.int32)[None, :] < request_block_rows[:, None]
    mixed = values + jnp.where(live[:, :, None], mine.astype(jnp.float32), jnp.float32(0.0))
    return mixed.astype(jnp.bfloat16)


def lanes_of(rows):
    return lax.broadcasted_iota(jnp.int32, (rows, LANES), 1)


def normalise_kernel(tokens_ref, out_ref):
    values = tokens_ref[...].astype(jnp.float32)
    mean_sq = jnp.mean(values * values, axis=-1, keepdims=True)
    out_ref[...] = (values * lax.rsqrt(mean_sq + 1e-06)).astype(jnp.bfloat16)


def weight_kernel(whole, part_ref, weight_ref, *out_refs):
    quarter = LANES // QUAD
    last = weight_ref[:, QUAD * whole :].astype(jnp.float32)
    inside = lanes_of(last.shape[0]) < quarter
    for k, out_ref in enumerate(out_refs):
        j = part_ref[k]
        out_ref[:, 0:whole] = weight_ref[:, pl.ds(pl.multiple_of(j * whole, LANES), whole)]
        turned = pltpu.roll(last, lax.rem(LANES - quarter * j, LANES), 1)
        out_ref[:, whole:] = jnp.where(inside, turned, 0.0).astype(jnp.bfloat16)


def pack_kernel(whole, cap, target_ref, label_ref, rows_ref, out_ref):
    total = rows_ref.shape[0]
    quads = out_ref.shape[0] // QUAD
    quarter = LANES // QUAD
    lane = lanes_of(total)
    last = rows_ref[:, QUAD * whole :].astype(jnp.float32)
    label = jnp.where(lane == quarter, label_ref[...], 0.0)
    ends = []
    for j in range(QUAD):
        turned = pltpu.roll(last, (LANES - quarter * j) % LANES, 1) if j else last
        ends.append(jnp.where(lane < quarter, turned, label).astype(jnp.bfloat16))
    for q in range(quads):
        place = lax.broadcasted_iota(jnp.int32, (cap, total), 0) + q * cap
        chosen = jnp.where(target_ref[...] == place, 1.0, 0.0).astype(jnp.bfloat16)
        for j in range(QUAD):
            columns = slice(j * whole, (j + 1) * whole)
            out_ref[q * QUAD + j, :, 0:whole] = jnp.dot(
                chosen, rows_ref[:, columns], preferred_element_type=jnp.float32
            ).astype(jnp.bfloat16)
            out_ref[q * QUAD + j, :, whole:] = jnp.dot(
                chosen, ends[j], preferred_element_type=jnp.float32
            ).astype(jnp.bfloat16)


def label_of(last_tile, resident):
    rows = last_tile.shape[0]
    quarter = LANES // QUAD
    label = last_tile[:, quarter : quarter + 1].astype(jnp.float32) - 1.0
    return label - jnp.where(lanes_of(rows) < HALF, 0.0, 1.0)


def down_kernel(chunk, resident, part_ref, rows_ref, *refs):
    weight_refs, out_ref = refs[:QUAD], refs[QUAD]
    width = rows_ref.shape[1]
    dims = (((1,), (1,)), ((), ()))
    low = lanes_of(chunk // 2) < HALF

    def one(c, carry):
        at = pl.ds(pl.multiple_of(c * chunk, chunk), chunk)
        label = label_of(rows_ref[at, width - LANES :], resident)
        picked = jnp.zeros((chunk, LANES), jnp.float32)
        for k in range(QUAD):
            product = lax.dot_general(
                rows_ref[at, :], weight_refs[k][...], dims, preferred_element_type=jnp.float32
            )
            first = (part_ref[k] * resident).astype(jnp.float32)
            for t in range(resident // 2):
                columns = slice(t * LANES, (t + 1) * LANES)
                picked = jnp.where(label == first + 2.0 * t, product[:, columns], picked)
        picked = picked + pltpu.roll(picked, HALF, 1)
        half = pl.ds(pl.multiple_of(c * (chunk // 2), chunk // 2), chunk // 2)
        out_ref[half, :] = jnp.where(
            low, picked[0 : chunk // 2], picked[chunk // 2 : chunk]
        ).astype(jnp.bfloat16)
        return carry

    lax.fori_loop(0, rows_ref.shape[0] // chunk, one, 0)


def up_kernel(chunk, resident, part_ref, ends_ref, *refs):
    sum_refs, weight_refs, out_ref = refs[:QUAD], refs[QUAD : 2 * QUAD], refs[2 * QUAD]
    width = ends_ref.shape[1]
    low = lanes_of(chunk // 2) < HALF

    def one(c, carry):
        at = pl.ds(pl.multiple_of(c * chunk, chunk), chunk)
        half = pl.ds(pl.multiple_of(c * (chunk // 2), chunk // 2), chunk // 2)
        label = label_of(ends_ref[at, width - LANES :], resident)
        down = sum_refs[0][half, :].astype(jnp.float32)
        for ref in sum_refs[1:]:
            down = down + ref[half, :].astype(jnp.float32)
        down = down.astype(jnp.bfloat16).astype(jnp.float32)
        turned = pltpu.roll(down, HALF, 1)
        twice = jnp.concatenate(
            [jnp.where(low, down, turned), jnp.where(low, turned, down)], axis=0
        )
        delta = jnp.zeros((chunk, out_ref.shape[1]), jnp.float32)
        for k in range(QUAD):
            first = (part_ref[k] * resident).astype(jnp.float32)
            placed = [
                jnp.where(label == first + 2.0 * t, twice, 0.0) for t in range(resident // 2)
            ]
            placed = jnp.concatenate(placed, axis=1).astype(jnp.bfloat16)
            delta = delta + jnp.dot(
                placed, weight_refs[k][...], preferred_element_type=jnp.float32
            )
        out_ref[at, :] = delta.astype(jnp.bfloat16)
        return carry

    lax.fori_loop(0, ends_ref.shape[0] // chunk, one, 0)


def mix_kernel(whole, cap, target_ref, tokens_ref, returned_ref, out_ref):
    total = tokens_ref.shape[0]
    quads = returned_ref.shape[0] // QUAD
    quarter = LANES // QUAD
    lane = lanes_of(total)
    place = lax.broadcasted_iota(jnp.int32, (total, quads * cap), 1)
    chosen = jnp.where(target_ref[...] == place, 1.0, 0.0).astype(jnp.bfloat16)
    end = jnp.zeros((total, LANES), jnp.float32)
    for j in range(QUAD):
        share = jnp.concatenate([returned_ref[q * QUAD + j] for q in range(quads)], axis=0)
        delta = jnp.dot(chosen, share, preferred_element_type=jnp.float32)
        columns = slice(j * whole, (j + 1) * whole)
        out_ref[:, columns] = (
            tokens_ref[:, columns].astype(jnp.float32) + delta[:, 0:whole]
        ).astype(jnp.bfloat16)
        last = delta[:, whole:]
        turned = pltpu.roll(last, quarter * j, 1) if j else last
        end = jnp.where((lane >= quarter * j) & (lane < quarter * (j + 1)), turned, end)
    out_ref[:, QUAD * whole :] = (
        tokens_ref[:, QUAD * whole :].astype(jnp.float32) + end
    ).astype(jnp.bfloat16)


def call(kernel, out_shape, in_specs, flops, moved):
    many = isinstance(out_shape, list)
    return pl.pallas_call(
        kernel,
        out_shape=out_shape,
        in_specs=in_specs,
        out_specs=[VMEM] * len(out_shape) if many else VMEM,
        compiler_params=pltpu.CompilerParams(vmem_limit_bytes=48 * 2**20),
        cost_estimate=pl.CostEstimate(flops=flops, bytes_accessed=moved, transcendentals=0),
    )


def exchange(value):
    return lax.all_to_all(value, "adapter", split_axis=0, concat_axis=0, tiled=True)


def neighbours(values, devices):
    arrived = [values[0]]
    for k in range(1, QUAD):
        pairs = [(i, i ^ k) for i in range(devices)]
        arrived.append(lax.ppermute(values[k], "adapter", pairs))
    return arrived


def quad_branch(
    cap, tokens, normed, quad, place, label, parts, adapter_down_weight, adapter_up_weight
):
    total, width = tokens.shape
    devices = lax.axis_size("adapter")
    resident, rank, unused_width = adapter_up_weight.shape
    whole = width // LANES // QUAD * LANES
    share = whole + LANES
    bf16, i32 = jnp.bfloat16, jnp.int32
    target = jnp.where(place >= 0, quad * cap + place, -1).astype(i32)
    arriving = devices * cap
    chunk = total
    columns = resident * rank
    flops = 2 * arriving * QUAD * columns * share

    outgoing = call(
        functools.partial(pack_kernel, whole, cap),
        jax.ShapeDtypeStruct((devices, cap, share), bf16),
        [VMEM, VMEM, VMEM],
        2 * devices // QUAD * cap * total * QUAD * share,
        2 * (total * width + arriving * share),
    )(target.reshape(1, total), label.reshape(total, 1), normed)
    arrived = exchange(outgoing).reshape(arriving, share)

    def dealt(weight):
        shares = [jax.ShapeDtypeStruct((columns, share), bf16)] * QUAD
        values = call(
            functools.partial(weight_kernel, whole), shares, [SMEM, VMEM], 0, 4 * columns * width
        )(parts, weight)
        return neighbours(values, devices)

    down_weights = dealt(adapter_down_weight.transpose(0, 2, 1).reshape(columns, width))
    up_weights = dealt(adapter_up_weight.reshape(columns, width))
    partial = call(
        functools.partial(down_kernel, chunk, resident),
        jax.ShapeDtypeStruct((arriving // 2, LANES), bf16),
        [SMEM] + [VMEM] * (1 + QUAD),
        flops,
        2 * (arriving * share + QUAD * columns * share),
    )(parts, arrived, *down_weights)
    sums = neighbours([partial] * QUAD, devices)
    leaving = call(
        functools.partial(up_kernel, chunk, resident),
        jax.ShapeDtypeStruct((arriving, share), bf16),
        [SMEM] + [VMEM] * (1 + 2 * QUAD),
        flops,
        2 * (2 * arriving * share + QUAD * columns * share),
    )(parts, arrived, *sums, *up_weights)
    returned = exchange(leaving.reshape(devices, cap, share))
    return call(
        functools.partial(mix_kernel, whole, cap),
        jax.ShapeDtypeStruct((total, width), bf16),
        [VMEM, VMEM, VMEM],
        2 * arriving * total * share,
        2 * (2 * total * width + arriving * share),
    )(target.reshape(total, 1), tokens, returned)


def rows_to_quads(
    tokens, request_block_adapter, request_block_rows, adapter_down_weight, adapter_up_weight
):
    blocks, rows, width = tokens.shape
    devices = lax.axis_size("adapter")
    resident = adapter_up_weight.shape[0]
    total = blocks * rows
    i32 = jnp.int32

    quad = request_block_adapter // (resident * QUAD)
    label = request_block_adapter - quad * (resident * QUAD) + 1
    serial = jnp.arange(blocks, dtype=i32)
    same = quad[:, None] == quad[None, :]
    used = request_block_rows
    ahead = jnp.where(same & (serial[None, :] < serial[:, None]), used[None, :], 0)
    within = jnp.where(same, used[None, :], 0)
    most = lax.pmax(jnp.max(jnp.sum(within, axis=1)), ("groups", "adapter"))
    row = jnp.arange(rows, dtype=i32)
    place = jnp.where(
        row[None, :] < used[:, None], jnp.sum(ahead, axis=1)[:, None] + row[None, :], -1
    ).reshape(total)

    def by_row(value):
        return jnp.broadcast_to(value[:, None], (blocks, rows)).reshape(total)

    flat = tokens.reshape(total, width)
    normed = call(
        normalise_kernel, jax.ShapeDtypeStruct(flat.shape, jnp.bfloat16), [VMEM], 0, 4 * flat.size
    )(flat)
    me = lax.axis_index("adapter").astype(i32)
    parts = jnp.bitwise_xor(me % QUAD, jnp.arange(QUAD, dtype=i32))
    caps = [total * 5 // 16, total * 6 // 16, total * 7 // 16, total]
    index = sum((most > cap).astype(i32) for cap in caps[:-1])
    mixed = lax.switch(
        index,
        [functools.partial(quad_branch, cap) for cap in caps],
        flat,
        normed,
        by_row(quad),
        place,
        by_row(label).astype(jnp.float32),
        parts,
        adapter_down_weight,
        adapter_up_weight,
    )
    return mixed.reshape(tokens.shape)


def solution(mesh):
    placed = (
        P(("groups", "adapter"), None, None),
        P(("groups", "adapter")),
        P(("groups", "adapter")),
        P("adapter", None, None),
        P("adapter", None, None),
    )

    def per_device(tokens, request_block_adapter, request_block_rows, down_weight, up_weight):
        blocks, rows, width = tokens.shape
        devices = mesh.shape["adapter"]
        slots = max(1, 4 * blocks // devices)
        quads = devices % QUAD == 0 and slots * QUAD >= blocks
        quads = quads and width % (QUAD * LANES) == LANES and up_weight.shape[1] == HALF
        plan = rows_to_quads if quads else rows_to_holders
        return plan(tokens, request_block_adapter, request_block_rows, down_weight, up_weight)

    return jax.shard_map(
        per_device,
        mesh=mesh,
        in_specs=placed,
        out_specs=P(("groups", "adapter"), None, None),
        check_vma=False,
    )
```

```python
import functools
import math

import jax
import jax.numpy as jnp
from jax import lax
from jax.experimental import pallas as pl
from jax.experimental.pallas import tpu as pltpu
from jax.sharding import PartitionSpec as P

LANES = 128
HALF = 64
QUAD = 4
CHUNK = 512
VMEM = pl.BlockSpec(memory_space=pltpu.VMEM)
SMEM = pl.BlockSpec(memory_space=pltpu.SMEM)


def normalise(tokens):
    values = tokens.astype(jnp.float32)
    mean_sq = jnp.mean(values * values, axis=-1, keepdims=True)
    return (values, (values * lax.rsqrt(mean_sq + 1e-06)).astype(jnp.bfloat16))


def resident_update(hidden_state, block_labels, adapter_down_weight, adapter_up_weight):
    feature_width = hidden_state.shape[-1]
    leading = hidden_state.shape[:-1]
    resident_rows, unused_value, inner_rank = adapter_down_weight.shape
    flattened_tokens = hidden_state.reshape(-1, feature_width)
    down_matrix = jnp.einsum(
        "tq,iqg->tig", flattened_tokens, adapter_down_weight, preferred_element_type=jnp.float32
    )
    down_matrix = down_matrix.astype(jnp.bfloat16).reshape(
        flattened_tokens.shape[0], resident_rows * inner_rank
    )
    column_owner = jnp.arange(resident_rows * inner_rank, dtype=jnp.int32) // inner_rank
    picked = block_labels.reshape(-1, 1) == column_owner[None, :]
    down_matrix = jnp.where(picked, down_matrix, jnp.zeros_like(down_matrix))
    lowrank_update = jnp.dot(
        down_matrix,
        adapter_up_weight.reshape(resident_rows * inner_rank, feature_width),
        preferred_element_type=jnp.float32,
    )
    return lowrank_update.astype(jnp.bfloat16).reshape(leading + (feature_width,))


def rows_to_holders(
    tokens, request_block_adapter, request_block_rows, adapter_down_weight, adapter_up_weight
):
    blocks, rows, feature_width = tokens.shape
    devices = lax.axis_size("adapter")
    resident_rows = adapter_down_weight.shape[0]
    slots = max(1, 4 * blocks // devices)
    values, normed = normalise(tokens)
    owner = request_block_adapter // resident_rows
    within = request_block_adapter - owner * resident_rows
    serial = jnp.arange(blocks, dtype=jnp.int32)
    earlier = (owner[:, None] == owner[None, :]) & (serial[None, :] < serial[:, None])
    position = owner * slots + jnp.sum(earlier, axis=1)
    outgoing = (
        jnp.zeros((devices * slots, rows, feature_width), jnp.bfloat16).at[position].set(normed)
    )
    outgoing = outgoing.reshape(devices, slots, rows, feature_width)
    block_labels = jnp.full((devices * slots,), -1, jnp.int32).at[position].set(within)
    block_labels = jnp.broadcast_to(block_labels[:, None], (devices * slots, rows)).reshape(
        devices, slots, rows
    )
    arriving_rows, row_markers = (
        lax.all_to_all(outgoing, "adapter", split_axis=0, concat_axis=0, tiled=True),
        lax.all_to_all(block_labels, "adapter", split_axis=0, concat_axis=0, tiled=True),
    )
    lowrank_update = resident_update(
        arriving_rows, row_markers, adapter_down_weight, adapter_up_weight
    )
    returned = lax.all_to_all(lowrank_update, "adapter", split_axis=0, concat_axis=0, tiled=True)
    mine = returned.reshape(devices * slots, rows, feature_width)[position]
    live = jnp.arange(rows, dtype=jnp.int32)[None, :] < request_block_rows[:, None]
    mixed = values + jnp.where(live[:, :, None], mine.astype(jnp.float32), jnp.float32(0.0))
    return mixed.astype(jnp.bfloat16)


def lanes_of(rows):
    return lax.broadcasted_iota(jnp.int32, (rows, LANES), 1)


def weight_kernel(whole, part_ref, group_ref, weight_ref, *out_refs):
    quarter = LANES // QUAD
    inside = lanes_of(weight_ref.shape[0]) < quarter
    for k, out_ref in enumerate(out_refs):
        j = part_ref[k]
        count = out_ref.shape[0]
        start = 0 if k < 2 else pl.multiple_of(group_ref[0] * count, count)
        rows = pl.ds(start, count)
        out_ref[:, 0:whole] = weight_ref[rows, pl.ds(pl.multiple_of(j * whole, LANES), whole)]
        last = weight_ref[rows, QUAD * whole :].astype(jnp.float32)
        turned = pltpu.roll(last, lax.rem(LANES - quarter * j, LANES), 1)
        out_ref[:, whole:] = jnp.where(inside[0:count], turned, 0.0).astype(jnp.bfloat16)


def pack_rows(whole, cap, base, most, target_ref, label_ref, rows_ref, out_ref):
    total = rows_ref.shape[0]
    quads = out_ref.shape[0] // QUAD
    quarter = LANES // QUAD
    lane = lanes_of(total)
    last = rows_ref[:, QUAD * whole :].astype(jnp.float32)
    label = jnp.where(lane == quarter, label_ref[...], 0.0)
    ends = []
    for j in range(QUAD):
        turned = pltpu.roll(last, (LANES - quarter * j) % LANES, 1) if j else last
        ends.append(jnp.where(lane < quarter, turned, label).astype(jnp.bfloat16))
    note = jnp.where(lanes_of(cap) == quarter + 1, most, 0.0)
    for q in range(quads):
        place = lax.broadcasted_iota(jnp.int32, (cap, total), 0) + (q * total + base)
        chosen = jnp.where(target_ref[...] == place, 1.0, 0.0).astype(jnp.bfloat16)
        for j in range(QUAD):
            columns = slice(j * whole, (j + 1) * whole)
            out_ref[q * QUAD + j, :, 0:whole] = jnp.dot(
                chosen, rows_ref[:, columns], preferred_element_type=jnp.float32
            ).astype(jnp.bfloat16)
            end = jnp.dot(chosen, ends[j], preferred_element_type=jnp.float32)
            out_ref[q * QUAD + j, :, whole:] = (end + note).astype(jnp.bfloat16)


def first_pack_kernel(
    whole, cap, most_ref, target_ref, label_ref, tokens_ref, normed_ref, out_ref
):
    values = tokens_ref[...].astype(jnp.float32)
    mean_sq = jnp.mean(values * values, axis=-1, keepdims=True)
    normed_ref[...] = (values * lax.rsqrt(mean_sq + 1e-06)).astype(jnp.bfloat16)
    most = most_ref[0].astype(jnp.float32)
    pack_rows(whole, cap, 0, most, target_ref, label_ref, normed_ref, out_ref)


def next_pack_kernel(whole, cap, base, target_ref, label_ref, normed_ref, out_ref):
    pack_rows(whole, cap, base, 0.0, target_ref, label_ref, normed_ref, out_ref)


def label_of(last_tile):
    rows = last_tile.shape[0]
    quarter = LANES // QUAD
    label = last_tile[:, quarter : quarter + 1].astype(jnp.float32) - 1.0
    return label - jnp.where(lanes_of(rows) < HALF, 0.0, 1.0)


def down_kernel(chunk, first_ref, rows_ref, *refs):
    weight_refs, out_ref = refs[:-1], refs[-1]
    width = rows_ref.shape[1]
    dims = (((1,), (1,)), ((), ()))
    low = lanes_of(chunk // 2) < HALF

    def one(c, carry):
        at = pl.ds(pl.multiple_of(c * chunk, chunk), chunk)
        label = label_of(rows_ref[at, width - LANES :])
        picked = jnp.zeros((chunk, LANES), jnp.float32)
        for k, weight_ref in enumerate(weight_refs):
            product = lax.dot_general(
                rows_ref[at, :], weight_ref[...], dims, preferred_element_type=jnp.float32
            )
            first = first_ref[k].astype(jnp.float32)
            for t in range(weight_ref.shape[0] // LANES):
                columns = slice(t * LANES, (t + 1) * LANES)
                picked = jnp.where(label == first + 2.0 * t, product[:, columns], picked)
        picked = picked + pltpu.roll(picked, HALF, 1)
        half = pl.ds(pl.multiple_of(c * (chunk // 2), chunk // 2), chunk // 2)
        out_ref[half, :] = jnp.where(
            low, picked[0 : chunk // 2], picked[chunk // 2 : chunk]
        ).astype(jnp.bfloat16)
        return carry

    lax.fori_loop(0, rows_ref.shape[0] // chunk, one, 0)


def up_kernel(chunk, first_ref, ends_ref, *refs):
    sum_refs, weight_refs, out_ref = refs[:QUAD], refs[QUAD:-1], refs[-1]
    width = ends_ref.shape[1]
    low = lanes_of(chunk // 2) < HALF

    def one(c, carry):
        at = pl.ds(pl.multiple_of(c * chunk, chunk), chunk)
        half = pl.ds(pl.multiple_of(c * (chunk // 2), chunk // 2), chunk // 2)
        label = label_of(ends_ref[at, width - LANES :])
        down = sum_refs[0][half, :].astype(jnp.float32)
        for ref in sum_refs[1:]:
            down = down + ref[half, :].astype(jnp.float32)
        down = down.astype(jnp.bfloat16).astype(jnp.float32)
        turned = pltpu.roll(down, HALF, 1)
        twice = jnp.concatenate(
            [jnp.where(low, down, turned), jnp.where(low, turned, down)], axis=0
        )
        delta = jnp.zeros((chunk, out_ref.shape[1]), jnp.float32)
        for k, weight_ref in enumerate(weight_refs):
            first = first_ref[k].astype(jnp.float32)
            placed = [
                jnp.where(label == first + 2.0 * t, twice, 0.0)
                for t in range(weight_ref.shape[0] // LANES)
            ]
            placed = jnp.concatenate(placed, axis=1).astype(jnp.bfloat16)
            delta = delta + jnp.dot(placed, weight_ref[...], preferred_element_type=jnp.float32)
        out_ref[at, :] = delta.astype(jnp.bfloat16)
        return carry

    lax.fori_loop(0, ends_ref.shape[0] // chunk, one, 0)


def mix_kernel(whole, bases, target_ref, tokens_ref, *refs):
    returned_refs, out_ref = refs[:-1], refs[-1]
    total = tokens_ref.shape[0]
    quads = returned_refs[0].shape[0] // QUAD
    quarter = LANES // QUAD
    lane = lanes_of(total)
    chosen = []
    for base, ref in zip(bases, returned_refs):
        cap = ref.shape[1]
        spot = lax.broadcasted_iota(jnp.int32, (total, quads * cap), 1)
        place = spot // cap * total + spot % cap + base
        chosen.append(jnp.where(target_ref[...] == place, 1.0, 0.0).astype(jnp.bfloat16))
    end = jnp.zeros((total, LANES), jnp.float32)
    for j in range(QUAD):
        delta = jnp.zeros((total, whole + LANES), jnp.float32)
        for choice, ref in zip(chosen, returned_refs):
            share = jnp.concatenate([ref[q * QUAD + j] for q in range(quads)], axis=0)
            delta = delta + jnp.dot(choice, share, preferred_element_type=jnp.float32)
        columns = slice(j * whole, (j + 1) * whole)
        out_ref[:, columns] = (
            tokens_ref[:, columns].astype(jnp.float32) + delta[:, 0:whole]
        ).astype(jnp.bfloat16)
        last = delta[:, whole:]
        turned = pltpu.roll(last, quarter * j, 1) if j else last
        end = jnp.where((lane >= quarter * j) & (lane < quarter * (j + 1)), turned, end)
    out_ref[:, QUAD * whole :] = (
        tokens_ref[:, QUAD * whole :].astype(jnp.float32) + end
    ).astype(jnp.bfloat16)


def call(kernel, out_shape, in_specs, flops, moved):
    many = isinstance(out_shape, list)
    return pl.pallas_call(
        kernel,
        out_shape=out_shape,
        in_specs=in_specs,
        out_specs=[VMEM] * len(out_shape) if many else VMEM,
        compiler_params=pltpu.CompilerParams(vmem_limit_bytes=48 * 2**20),
        cost_estimate=pl.CostEstimate(flops=flops, bytes_accessed=moved, transcendentals=0),
    )


def exchange(value):
    return lax.all_to_all(value, "adapter", split_axis=0, concat_axis=0, tiled=True)


def towards(value, k, devices):
    return lax.ppermute(value, "adapter", [(i, i ^ k) for i in range(devices)])


def swapped(value):
    return lax.ppermute(value, "groups", [(0, 1), (1, 0)])


def down_call(first, arrived, weights):
    arriving, share = arrived.shape
    columns = sum(weight.shape[0] for weight in weights)
    chunk = math.gcd(arriving, CHUNK)
    return call(
        functools.partial(down_kernel, chunk),
        jax.ShapeDtypeStruct((arriving // 2, LANES), jnp.bfloat16),
        [SMEM] + [VMEM] * (1 + len(weights)),
        2 * arriving * columns * share,
        2 * (arriving + columns) * share,
    )(first, arrived, *weights)


def up_call(first, arrived, partial, weights, devices):
    sums = [partial] + [towards(partial, k, devices) for k in range(1, QUAD)]
    arriving, share = arrived.shape
    columns = sum(weight.shape[0] for weight in weights)
    chunk = math.gcd(arriving, CHUNK)
    leaving = call(
        functools.partial(up_kernel, chunk),
        jax.ShapeDtypeStruct((arriving, share), jnp.bfloat16),
        [SMEM] + [VMEM] * (1 + QUAD + len(weights)),
        2 * arriving * columns * share,
        2 * (2 * arriving + columns) * share,
    )(first, arrived, *sums, *weights)
    return leaving.reshape(devices, arriving // devices, share)


def second_piece(
    cap,
    base,
    tokens,
    normed,
    target,
    label,
    first,
    arrived,
    partial,
    down_weights,
    up_near,
    up_far,
):
    total, width = tokens.shape
    devices = lax.axis_size("adapter")
    whole = width // LANES // QUAD * LANES
    share = whole + LANES
    outgoing = call(
        functools.partial(next_pack_kernel, whole, cap, base),
        jax.ShapeDtypeStruct((devices, cap, share), jnp.bfloat16),
        [VMEM, VMEM, VMEM],
        2 * devices * cap * total * share,
        2 * (total * width + devices * cap * share),
    )(target.reshape(1, total), label, normed)
    later = exchange(outgoing).reshape(devices * cap, share)
    up_weights = [*up_near, *up_far, *[swapped(value) for value in up_far]]
    returned = exchange(up_call(first, arrived, partial, up_weights, devices))
    later_partial = down_call(first, later, down_weights)
    later_returned = exchange(up_call(first, later, later_partial, up_weights, devices))
    return call(
        functools.partial(mix_kernel, whole, (0, base)),
        jax.ShapeDtypeStruct((total, width), jnp.bfloat16),
        [VMEM] * 4,
        2 * devices * (cap + base) * total * share,
        2 * (2 * total * width + devices * (cap + base) * share),
    )(target.reshape(total, 1), tokens, returned, later_returned)


def rows_to_quads(
    tokens, request_block_adapter, request_block_rows, adapter_down_weight, adapter_up_weight
):
    blocks, rows, width = tokens.shape
    devices = lax.axis_size("adapter")
    resident, rank, unused_width = adapter_up_weight.shape
    total = blocks * rows
    columns = resident * rank
    whole = width // LANES // QUAD * LANES
    share = whole + LANES
    bf16, i32 = jnp.bfloat16, jnp.int32

    quad = request_block_adapter // (resident * QUAD)
    label = request_block_adapter - quad * (resident * QUAD) + 1
    serial = jnp.arange(blocks, dtype=i32)
    same = quad[:, None] == quad[None, :]
    used = request_block_rows
    ahead = jnp.where(same & (serial[None, :] < serial[:, None]), used[None, :], 0)
    most = jnp.max(jnp.sum(jnp.where(same, used[None, :], 0), axis=1))
    row = jnp.arange(rows, dtype=i32)
    start = quad * total + jnp.sum(ahead, axis=1)
    target = jnp.where(row[None, :] < used[:, None], start[:, None] + row[None, :], -1)
    target = target.reshape(total).astype(i32)
    label = jnp.broadcast_to(label[:, None], (blocks, rows)).reshape(total, 1).astype(jnp.float32)

    me = lax.axis_index("adapter").astype(i32)
    group = lax.axis_index("groups").astype(i32)
    parts = jnp.bitwise_xor(me % QUAD, jnp.arange(QUAD, dtype=i32))
    own_half, twin_half = group * (resident // 2), (1 - group) * (resident // 2)
    first = jnp.concatenate(
        [parts * resident + jnp.stack([0 * group, 0 * group, own_half, own_half])]
        + [parts[2:] * resident + twin_half]
    ).astype(i32)

    cap = total // QUAD
    flat = tokens.reshape(total, width)
    normed, outgoing = call(
        functools.partial(first_pack_kernel, whole, cap),
        [
            jax.ShapeDtypeStruct((total, width), bf16),
            jax.ShapeDtypeStruct((devices, cap, share), bf16),
        ],
        [SMEM, VMEM, VMEM, VMEM],
        2 * devices * cap * total * share,
        2 * (2 * total * width + devices * cap * share),
    )(most.reshape(1), target.reshape(1, total), label, flat)
    arrived = exchange(outgoing)

    def dealt(weight):
        counts = [columns, columns, columns // 2, columns // 2]
        values = call(
            functools.partial(weight_kernel, whole),
            [jax.ShapeDtypeStruct((count, share), bf16) for count in counts],
            [SMEM, SMEM, VMEM],
            0,
            4 * columns * width,
        )(parts, group.reshape(1), weight)
        near = [values[0], towards(values[1], 1, devices)]
        return near, [towards(values[k], k, devices) for k in range(2, QUAD)]

    down_near, down_far = dealt(adapter_down_weight.transpose(0, 2, 1).reshape(columns, width))
    up_near, up_far = dealt(adapter_up_weight.reshape(columns, width))
    down_weights = [*down_near, *down_far, *[swapped(value) for value in down_far]]

    most = jnp.max(arrived[:, 0, whole + LANES // QUAD + 1].astype(jnp.float32)).reshape(1, 1)
    most = jnp.maximum(most, swapped(most))[0, 0].astype(i32)
    caps = [total // 16, total // 8, total * 3 // 16, total - cap]
    index = sum((most > cap + more).astype(i32) for more in caps[:-1])
    arrived = arrived.reshape(devices * cap, share)
    partial = down_call(first, arrived, down_weights)
    mixed = lax.switch(
        index,
        [functools.partial(second_piece, more, cap) for more in caps],
        flat,
        normed,
        target,
        label,
        first,
        arrived,
        partial,
        down_weights,
        up_near,
        up_far,
    )
    return mixed.reshape(tokens.shape)


def solution(mesh):
    placed = (
        P(("groups", "adapter"), None, None),
        P(("groups", "adapter")),
        P(("groups", "adapter")),
        P("adapter", None, None),
        P("adapter", None, None),
    )

    def per_device(tokens, request_block_adapter, request_block_rows, down_weight, up_weight):
        blocks, rows, width = tokens.shape
        devices = mesh.shape["adapter"]
        slots = max(1, 4 * blocks // devices)
        quads = devices % QUAD == 0 and slots * QUAD >= blocks
        quads = quads and width % (QUAD * LANES) == LANES and up_weight.shape[1] == HALF
        plan = rows_to_quads if quads else rows_to_holders
        return plan(tokens, request_block_adapter, request_block_rows, down_weight, up_weight)

    return jax.shard_map(
        per_device,
        mesh=mesh,
        in_specs=placed,
        out_specs=P(("groups", "adapter"), None, None),
        check_vma=False,
    )
```

```python
import functools
import math

import jax
import jax.numpy as jnp
from jax import lax
from jax.experimental import pallas as pl
from jax.experimental.pallas import tpu as pltpu
from jax.sharding import PartitionSpec as P

LANES = 128
HALF = 64
QUAD = 4
CHUNK = 512
VMEM = pl.BlockSpec(memory_space=pltpu.VMEM)
SMEM = pl.BlockSpec(memory_space=pltpu.SMEM)


def normalise(tokens):
    values = tokens.astype(jnp.float32)
    mean_sq = jnp.mean(values * values, axis=-1, keepdims=True)
    return (values, (values * lax.rsqrt(mean_sq + 1e-06)).astype(jnp.bfloat16))


def resident_update(hidden_state, block_labels, adapter_down_weight, adapter_up_weight):
    feature_width = hidden_state.shape[-1]
    leading = hidden_state.shape[:-1]
    resident_rows, unused_value, inner_rank = adapter_down_weight.shape
    flattened_tokens = hidden_state.reshape(-1, feature_width)
    down_matrix = jnp.einsum(
        "tq,iqg->tig", flattened_tokens, adapter_down_weight, preferred_element_type=jnp.float32
    )
    down_matrix = down_matrix.astype(jnp.bfloat16).reshape(
        flattened_tokens.shape[0], resident_rows * inner_rank
    )
    column_owner = jnp.arange(resident_rows * inner_rank, dtype=jnp.int32) // inner_rank
    picked = block_labels.reshape(-1, 1) == column_owner[None, :]
    down_matrix = jnp.where(picked, down_matrix, jnp.zeros_like(down_matrix))
    lowrank_update = jnp.dot(
        down_matrix,
        adapter_up_weight.reshape(resident_rows * inner_rank, feature_width),
        preferred_element_type=jnp.float32,
    )
    return lowrank_update.astype(jnp.bfloat16).reshape(leading + (feature_width,))


def rows_to_holders(
    tokens, request_block_adapter, request_block_rows, adapter_down_weight, adapter_up_weight
):
    blocks, rows, feature_width = tokens.shape
    devices = lax.axis_size("adapter")
    resident_rows = adapter_down_weight.shape[0]
    slots = max(1, 4 * blocks // devices)
    values, normed = normalise(tokens)
    owner = request_block_adapter // resident_rows
    within = request_block_adapter - owner * resident_rows
    serial = jnp.arange(blocks, dtype=jnp.int32)
    earlier = (owner[:, None] == owner[None, :]) & (serial[None, :] < serial[:, None])
    position = owner * slots + jnp.sum(earlier, axis=1)
    outgoing = (
        jnp.zeros((devices * slots, rows, feature_width), jnp.bfloat16).at[position].set(normed)
    )
    outgoing = outgoing.reshape(devices, slots, rows, feature_width)
    block_labels = jnp.full((devices * slots,), -1, jnp.int32).at[position].set(within)
    block_labels = jnp.broadcast_to(block_labels[:, None], (devices * slots, rows)).reshape(
        devices, slots, rows
    )
    arriving_rows, row_markers = (
        lax.all_to_all(outgoing, "adapter", split_axis=0, concat_axis=0, tiled=True),
        lax.all_to_all(block_labels, "adapter", split_axis=0, concat_axis=0, tiled=True),
    )
    lowrank_update = resident_update(
        arriving_rows, row_markers, adapter_down_weight, adapter_up_weight
    )
    returned = lax.all_to_all(lowrank_update, "adapter", split_axis=0, concat_axis=0, tiled=True)
    mine = returned.reshape(devices * slots, rows, feature_width)[position]
    live = jnp.arange(rows, dtype=jnp.int32)[None, :] < request_block_rows[:, None]
    mixed = values + jnp.where(live[:, :, None], mine.astype(jnp.float32), jnp.float32(0.0))
    return mixed.astype(jnp.bfloat16)


def lanes_of(rows):
    return lax.broadcasted_iota(jnp.int32, (rows, LANES), 1)


def weight_kernel(whole, part_ref, group_ref, weight_ref, *out_refs):
    quarter = LANES // QUAD
    inside = lanes_of(weight_ref.shape[0]) < quarter
    for k, out_ref in enumerate(out_refs):
        j = part_ref[k]
        count = out_ref.shape[0]
        start = 0 if k < 2 else pl.multiple_of(group_ref[0] * count, count)
        rows = pl.ds(start, count)
        out_ref[:, 0:whole] = weight_ref[rows, pl.ds(pl.multiple_of(j * whole, LANES), whole)]
        last = weight_ref[rows, QUAD * whole :].astype(jnp.float32)
        turned = pltpu.roll(last, lax.rem(LANES - quarter * j, LANES), 1)
        out_ref[:, whole:] = jnp.where(inside[0:count], turned, 0.0).astype(jnp.bfloat16)


def pack_rows(whole, cap, base, most, target_ref, label_ref, rows_ref, out_ref):
    total = rows_ref.shape[0]
    quads = out_ref.shape[0] // QUAD
    quarter = LANES // QUAD
    lane = lanes_of(total)
    last = rows_ref[:, QUAD * whole :].astype(jnp.float32)
    label = jnp.where(lane == quarter, label_ref[...], 0.0)
    ends = []
    for j in range(QUAD):
        turned = pltpu.roll(last, (LANES - quarter * j) % LANES, 1) if j else last
        ends.append(jnp.where(lane < quarter, turned, label).astype(jnp.bfloat16))
    note = jnp.where(lanes_of(cap) == quarter + 1, most, 0.0)
    for q in range(quads):
        place = lax.broadcasted_iota(jnp.int32, (cap, total), 0) + (q * total + base)
        chosen = jnp.where(target_ref[...] == place, 1.0, 0.0).astype(jnp.bfloat16)
        for j in range(QUAD):
            columns = slice(j * whole, (j + 1) * whole)
            out_ref[q * QUAD + j, :, 0:whole] = jnp.dot(
                chosen, rows_ref[:, columns], preferred_element_type=jnp.float32
            ).astype(jnp.bfloat16)
            end = jnp.dot(chosen, ends[j], preferred_element_type=jnp.float32)
            out_ref[q * QUAD + j, :, whole:] = (end + note).astype(jnp.bfloat16)


def first_pack_kernel(
    whole, cap, most_ref, target_ref, label_ref, tokens_ref, normed_ref, out_ref
):
    values = tokens_ref[...].astype(jnp.float32)
    mean_sq = jnp.mean(values * values, axis=-1, keepdims=True)
    normed_ref[...] = (values * lax.rsqrt(mean_sq + 1e-06)).astype(jnp.bfloat16)
    most = most_ref[0].astype(jnp.float32)
    pack_rows(whole, cap, 0, most, target_ref, label_ref, normed_ref, out_ref)


def next_pack_kernel(whole, cap, base, target_ref, label_ref, normed_ref, out_ref):
    pack_rows(whole, cap, base, 0.0, target_ref, label_ref, normed_ref, out_ref)


def label_of(last_tile):
    rows = last_tile.shape[0]
    quarter = LANES // QUAD
    label = last_tile[:, quarter : quarter + 1].astype(jnp.float32) - 1.0
    return label - jnp.where(lanes_of(rows) < HALF, 0.0, 1.0)


def down_kernel(chunk, first_ref, rows_ref, *refs):
    weight_refs, out_ref = refs[:-1], refs[-1]
    width = rows_ref.shape[1]
    dims = (((1,), (1,)), ((), ()))
    low = lanes_of(chunk // 2) < HALF

    def one(c, carry):
        at = pl.ds(pl.multiple_of(c * chunk, chunk), chunk)
        label = label_of(rows_ref[at, width - LANES :])
        picked = jnp.zeros((chunk, LANES), jnp.float32)
        for k, weight_ref in enumerate(weight_refs):
            product = lax.dot_general(
                rows_ref[at, :], weight_ref[...], dims, preferred_element_type=jnp.float32
            )
            first = first_ref[k].astype(jnp.float32)
            for t in range(weight_ref.shape[0] // LANES):
                columns = slice(t * LANES, (t + 1) * LANES)
                picked = jnp.where(label == first + 2.0 * t, product[:, columns], picked)
        picked = picked + pltpu.roll(picked, HALF, 1)
        half = pl.ds(pl.multiple_of(c * (chunk // 2), chunk // 2), chunk // 2)
        out_ref[half, :] = jnp.where(
            low, picked[0 : chunk // 2], picked[chunk // 2 : chunk]
        ).astype(jnp.bfloat16)
        return carry

    lax.fori_loop(0, rows_ref.shape[0] // chunk, one, 0)


def up_kernel(chunk, first_ref, ends_ref, *refs):
    sum_refs, weight_refs, out_ref = refs[:QUAD], refs[QUAD:-1], refs[-1]
    width = ends_ref.shape[1]
    low = lanes_of(chunk // 2) < HALF

    def one(c, carry):
        at = pl.ds(pl.multiple_of(c * chunk, chunk), chunk)
        half = pl.ds(pl.multiple_of(c * (chunk // 2), chunk // 2), chunk // 2)
        label = label_of(ends_ref[at, width - LANES :])
        down = sum_refs[0][half, :].astype(jnp.float32)
        for ref in sum_refs[1:]:
            down = down + ref[half, :].astype(jnp.float32)
        down = down.astype(jnp.bfloat16).astype(jnp.float32)
        turned = pltpu.roll(down, HALF, 1)
        twice = jnp.concatenate(
            [jnp.where(low, down, turned), jnp.where(low, turned, down)], axis=0
        )
        delta = jnp.zeros((chunk, out_ref.shape[1]), jnp.float32)
        for k, weight_ref in enumerate(weight_refs):
            first = first_ref[k].astype(jnp.float32)
            placed = [
                jnp.where(label == first + 2.0 * t, twice, 0.0)
                for t in range(weight_ref.shape[0] // LANES)
            ]
            placed = jnp.concatenate(placed, axis=1).astype(jnp.bfloat16)
            delta = delta + jnp.dot(placed, weight_ref[...], preferred_element_type=jnp.float32)
        out_ref[at, :] = delta.astype(jnp.bfloat16)
        return carry

    lax.fori_loop(0, ends_ref.shape[0] // chunk, one, 0)


def mix_kernel(whole, bases, target_ref, tokens_ref, *refs):
    returned_refs, out_ref = refs[:-1], refs[-1]
    total = tokens_ref.shape[0]
    quads = returned_refs[0].shape[0] // QUAD
    quarter = LANES // QUAD
    lane = lanes_of(total)
    chosen = []
    for base, ref in zip(bases, returned_refs):
        cap = ref.shape[1]
        spot = lax.broadcasted_iota(jnp.int32, (total, quads * cap), 1)
        place = spot // cap * total + spot % cap + base
        chosen.append(jnp.where(target_ref[...] == place, 1.0, 0.0).astype(jnp.bfloat16))
    end = jnp.zeros((total, LANES), jnp.float32)
    for j in range(QUAD):
        delta = jnp.zeros((total, whole + LANES), jnp.float32)
        for choice, ref in zip(chosen, returned_refs):
            share = jnp.concatenate([ref[q * QUAD + j] for q in range(quads)], axis=0)
            delta = delta + jnp.dot(choice, share, preferred_element_type=jnp.float32)
        columns = slice(j * whole, (j + 1) * whole)
        out_ref[:, columns] = (
            tokens_ref[:, columns].astype(jnp.float32) + delta[:, 0:whole]
        ).astype(jnp.bfloat16)
        last = delta[:, whole:]
        turned = pltpu.roll(last, quarter * j, 1) if j else last
        end = jnp.where((lane >= quarter * j) & (lane < quarter * (j + 1)), turned, end)
    out_ref[:, QUAD * whole :] = (
        tokens_ref[:, QUAD * whole :].astype(jnp.float32) + end
    ).astype(jnp.bfloat16)


def call(kernel, out_shape, in_specs, flops, moved, after=()):
    many = isinstance(out_shape, list)
    skipped = len(after)
    body = (lambda *refs: kernel(*refs[skipped:])) if skipped else kernel
    run = pl.pallas_call(
        body,
        out_shape=out_shape,
        in_specs=[pl.BlockSpec(memory_space=pl.ANY)] * skipped + in_specs,
        out_specs=[VMEM] * len(out_shape) if many else VMEM,
        compiler_params=pltpu.CompilerParams(vmem_limit_bytes=48 * 2**20),
        cost_estimate=pl.CostEstimate(flops=flops, bytes_accessed=moved, transcendentals=0),
    )
    return functools.partial(run, *after)


def exchange(value):
    return lax.all_to_all(value, "adapter", split_axis=0, concat_axis=0, tiled=True)


def towards(value, k, devices):
    return lax.ppermute(value, "adapter", [(i, i ^ k) for i in range(devices)])


def swapped(value):
    return lax.ppermute(value, "groups", [(0, 1), (1, 0)])


def down_call(first, arrived, weights, after):
    arriving, share = arrived.shape
    columns = sum(weight.shape[0] for weight in weights)
    chunk = math.gcd(arriving, CHUNK)
    return call(
        functools.partial(down_kernel, chunk),
        jax.ShapeDtypeStruct((arriving // 2, LANES), jnp.bfloat16),
        [SMEM] + [VMEM] * (1 + len(weights)),
        2 * arriving * columns * share,
        2 * (arriving + columns) * share,
        after,
    )(first, arrived, *weights)


def up_call(first, arrived, partial, weights, devices):
    sums = [partial] + [towards(partial, k, devices) for k in range(1, QUAD)]
    arriving, share = arrived.shape
    columns = sum(weight.shape[0] for weight in weights)
    chunk = math.gcd(arriving, CHUNK)
    leaving = call(
        functools.partial(up_kernel, chunk),
        jax.ShapeDtypeStruct((arriving, share), jnp.bfloat16),
        [SMEM] + [VMEM] * (1 + QUAD + len(weights)),
        2 * arriving * columns * share,
        2 * (2 * arriving + columns) * share,
    )(first, arrived, *sums, *weights)
    return leaving.reshape(devices, arriving // devices, share)


def second_piece(
    cap,
    base,
    tokens,
    normed,
    target,
    label,
    first,
    arrived,
    down_weights,
    up_near,
    up_far,
):
    total, width = tokens.shape
    devices = lax.axis_size("adapter")
    whole = width // LANES // QUAD * LANES
    share = whole + LANES
    outgoing = call(
        functools.partial(next_pack_kernel, whole, cap, base),
        jax.ShapeDtypeStruct((devices, cap, share), jnp.bfloat16),
        [VMEM, VMEM, VMEM],
        2 * devices * cap * total * share,
        2 * (total * width + devices * cap * share),
    )(target.reshape(1, total), label, normed)
    later = exchange(outgoing).reshape(devices * cap, share)
    up_weights = [*up_near, *up_far, *[swapped(value) for value in up_far]]
    partial = down_call(first, arrived, down_weights, [outgoing])
    leaving = up_call(first, arrived, partial, up_weights, devices)
    returned = exchange(leaving)
    later_partial = down_call(first, later, down_weights, [leaving])
    later_returned = exchange(up_call(first, later, later_partial, up_weights, devices))
    return call(
        functools.partial(mix_kernel, whole, (0, base)),
        jax.ShapeDtypeStruct((total, width), jnp.bfloat16),
        [VMEM] * 4,
        2 * devices * (cap + base) * total * share,
        2 * (2 * total * width + devices * (cap + base) * share),
    )(target.reshape(total, 1), tokens, returned, later_returned)


def rows_to_quads(
    tokens, request_block_adapter, request_block_rows, adapter_down_weight, adapter_up_weight
):
    blocks, rows, width = tokens.shape
    devices = lax.axis_size("adapter")
    resident, rank, unused_width = adapter_up_weight.shape
    total = blocks * rows
    columns = resident * rank
    whole = width // LANES // QUAD * LANES
    share = whole + LANES
    bf16, i32 = jnp.bfloat16, jnp.int32

    quad = request_block_adapter // (resident * QUAD)
    label = request_block_adapter - quad * (resident * QUAD) + 1
    serial = jnp.arange(blocks, dtype=i32)
    same = quad[:, None] == quad[None, :]
    used = request_block_rows
    ahead = jnp.where(same & (serial[None, :] < serial[:, None]), used[None, :], 0)
    most = jnp.max(jnp.sum(jnp.where(same, used[None, :], 0), axis=1))
    row = jnp.arange(rows, dtype=i32)
    start = quad * total + jnp.sum(ahead, axis=1)
    target = jnp.where(row[None, :] < used[:, None], start[:, None] + row[None, :], -1)
    target = target.reshape(total).astype(i32)
    label = jnp.broadcast_to(label[:, None], (blocks, rows)).reshape(total, 1).astype(jnp.float32)

    me = lax.axis_index("adapter").astype(i32)
    group = lax.axis_index("groups").astype(i32)
    parts = jnp.bitwise_xor(me % QUAD, jnp.arange(QUAD, dtype=i32))
    own_half, twin_half = group * (resident // 2), (1 - group) * (resident // 2)
    first = jnp.concatenate(
        [parts * resident + jnp.stack([0 * group, 0 * group, own_half, own_half])]
        + [parts[2:] * resident + twin_half]
    ).astype(i32)

    def dealt(weight, after=()):
        counts = [columns, columns, columns // 2, columns // 2]
        values = call(
            functools.partial(weight_kernel, whole),
            [jax.ShapeDtypeStruct((count, share), bf16) for count in counts],
            [SMEM, SMEM, VMEM],
            0,
            4 * columns * width,
            after,
        )(parts, group.reshape(1), weight)
        near = [values[0], towards(values[1], 1, devices)]
        return near, [towards(values[k], k, devices) for k in range(2, QUAD)]

    down_near, down_far = dealt(adapter_down_weight.transpose(0, 2, 1).reshape(columns, width))
    up_near, up_far = dealt(adapter_up_weight.reshape(columns, width), down_far)
    down_weights = [*down_near, *down_far, *[swapped(value) for value in down_far]]

    cap = total // QUAD
    flat = tokens.reshape(total, width)
    normed, outgoing = call(
        functools.partial(first_pack_kernel, whole, cap),
        [
            jax.ShapeDtypeStruct((total, width), bf16),
            jax.ShapeDtypeStruct((devices, cap, share), bf16),
        ],
        [SMEM, VMEM, VMEM, VMEM],
        2 * devices * cap * total * share,
        2 * (2 * total * width + devices * cap * share),
        down_near[:1],
    )(most.reshape(1), target.reshape(1, total), label, flat)
    arrived = exchange(outgoing)

    most = jnp.max(arrived[:, 0, whole + LANES // QUAD + 1].astype(jnp.float32)).reshape(1, 1)
    most = jnp.maximum(most, swapped(most))[0, 0].astype(i32)
    caps = [total // 16, total // 8, total * 3 // 16, total - cap]
    index = sum((most > cap + more).astype(i32) for more in caps[:-1])
    arrived = arrived.reshape(devices * cap, share)
    mixed = lax.switch(
        index,
        [functools.partial(second_piece, more, cap) for more in caps],
        flat,
        normed,
        target,
        label,
        first,
        arrived,
        down_weights,
        up_near,
        up_far,
    )
    return mixed.reshape(tokens.shape)


def solution(mesh):
    placed = (
        P(("groups", "adapter"), None, None),
        P(("groups", "adapter")),
        P(("groups", "adapter")),
        P("adapter", None, None),
        P("adapter", None, None),
    )

    def per_device(tokens, request_block_adapter, request_block_rows, down_weight, up_weight):
        blocks, rows, width = tokens.shape
        devices = mesh.shape["adapter"]
        slots = max(1, 4 * blocks // devices)
        quads = devices % QUAD == 0 and slots * QUAD >= blocks
        quads = quads and width % (QUAD * LANES) == LANES and up_weight.shape[1] == HALF
        plan = rows_to_quads if quads else rows_to_holders
        return plan(tokens, request_block_adapter, request_block_rows, down_weight, up_weight)

    return jax.shard_map(
        per_device,
        mesh=mesh,
        in_specs=placed,
        out_specs=P(("groups", "adapter"), None, None),
        check_vma=False,
    )
```

```python
import functools
import math

import jax
import jax.numpy as jnp
from jax import lax
from jax.experimental import pallas as pl
from jax.experimental.pallas import tpu as pltpu
from jax.sharding import PartitionSpec as P

LANES = 128
HALF = 64
QUAD = 4
CHUNK = 512
VMEM = pl.BlockSpec(memory_space=pltpu.VMEM)
SMEM = pl.BlockSpec(memory_space=pltpu.SMEM)


def normalise(tokens):
    values = tokens.astype(jnp.float32)
    mean_sq = jnp.mean(values * values, axis=-1, keepdims=True)
    return (values, (values * lax.rsqrt(mean_sq + 1e-06)).astype(jnp.bfloat16))


def resident_update(hidden_state, block_labels, adapter_down_weight, adapter_up_weight):
    feature_width = hidden_state.shape[-1]
    leading = hidden_state.shape[:-1]
    resident_rows, unused_value, inner_rank = adapter_down_weight.shape
    flattened_tokens = hidden_state.reshape(-1, feature_width)
    down_matrix = jnp.einsum(
        "tq,iqg->tig", flattened_tokens, adapter_down_weight, preferred_element_type=jnp.float32
    )
    down_matrix = down_matrix.astype(jnp.bfloat16).reshape(
        flattened_tokens.shape[0], resident_rows * inner_rank
    )
    column_owner = jnp.arange(resident_rows * inner_rank, dtype=jnp.int32) // inner_rank
    picked = block_labels.reshape(-1, 1) == column_owner[None, :]
    down_matrix = jnp.where(picked, down_matrix, jnp.zeros_like(down_matrix))
    lowrank_update = jnp.dot(
        down_matrix,
        adapter_up_weight.reshape(resident_rows * inner_rank, feature_width),
        preferred_element_type=jnp.float32,
    )
    return lowrank_update.astype(jnp.bfloat16).reshape(leading + (feature_width,))


def rows_to_holders(
    tokens, request_block_adapter, request_block_rows, adapter_down_weight, adapter_up_weight
):
    blocks, rows, feature_width = tokens.shape
    devices = lax.axis_size("adapter")
    resident_rows = adapter_down_weight.shape[0]
    slots = max(1, 4 * blocks // devices)
    values, normed = normalise(tokens)
    owner = request_block_adapter // resident_rows
    within = request_block_adapter - owner * resident_rows
    serial = jnp.arange(blocks, dtype=jnp.int32)
    earlier = (owner[:, None] == owner[None, :]) & (serial[None, :] < serial[:, None])
    position = owner * slots + jnp.sum(earlier, axis=1)
    outgoing = (
        jnp.zeros((devices * slots, rows, feature_width), jnp.bfloat16).at[position].set(normed)
    )
    outgoing = outgoing.reshape(devices, slots, rows, feature_width)
    block_labels = jnp.full((devices * slots,), -1, jnp.int32).at[position].set(within)
    block_labels = jnp.broadcast_to(block_labels[:, None], (devices * slots, rows)).reshape(
        devices, slots, rows
    )
    arriving_rows, row_markers = (
        lax.all_to_all(outgoing, "adapter", split_axis=0, concat_axis=0, tiled=True),
        lax.all_to_all(block_labels, "adapter", split_axis=0, concat_axis=0, tiled=True),
    )
    lowrank_update = resident_update(
        arriving_rows, row_markers, adapter_down_weight, adapter_up_weight
    )
    returned = lax.all_to_all(lowrank_update, "adapter", split_axis=0, concat_axis=0, tiled=True)
    mine = returned.reshape(devices * slots, rows, feature_width)[position]
    live = jnp.arange(rows, dtype=jnp.int32)[None, :] < request_block_rows[:, None]
    mixed = values + jnp.where(live[:, :, None], mine.astype(jnp.float32), jnp.float32(0.0))
    return mixed.astype(jnp.bfloat16)


def lanes_of(rows):
    return lax.broadcasted_iota(jnp.int32, (rows, LANES), 1)


def weight_kernel(whole, part_ref, group_ref, weight_ref, *out_refs):
    quarter = LANES // QUAD
    inside = lanes_of(weight_ref.shape[0]) < quarter
    for k, out_ref in enumerate(out_refs):
        j = part_ref[k]
        count = out_ref.shape[0]
        start = 0 if k < 2 else pl.multiple_of(group_ref[0] * count, count)
        rows = pl.ds(start, count)
        out_ref[:, 0:whole] = weight_ref[rows, pl.ds(pl.multiple_of(j * whole, LANES), whole)]
        last = weight_ref[rows, QUAD * whole :].astype(jnp.float32)
        turned = pltpu.roll(last, lax.rem(LANES - quarter * j, LANES), 1)
        out_ref[:, whole:] = jnp.where(inside[0:count], turned, 0.0).astype(jnp.bfloat16)


def pack_rows(whole, cap, base, most, target_ref, label_ref, rows_ref, out_ref):
    total = rows_ref.shape[0]
    quads = out_ref.shape[0] // QUAD
    quarter = LANES // QUAD
    lane = lanes_of(total)
    last = rows_ref[:, QUAD * whole :].astype(jnp.float32)
    label = jnp.where(lane == quarter, label_ref[...], 0.0)
    ends = []
    for j in range(QUAD):
        turned = pltpu.roll(last, (LANES - quarter * j) % LANES, 1) if j else last
        ends.append(jnp.where(lane < quarter, turned, label).astype(jnp.bfloat16))
    note = jnp.where(lanes_of(cap) == quarter + 1, most, 0.0)
    for q in range(quads):
        place = lax.broadcasted_iota(jnp.int32, (cap, total), 0) + (q * total + base)
        chosen = jnp.where(target_ref[...] == place, 1.0, 0.0).astype(jnp.bfloat16)
        for j in range(QUAD):
            columns = slice(j * whole, (j + 1) * whole)
            out_ref[q * QUAD + j, :, 0:whole] = jnp.dot(
                chosen, rows_ref[:, columns], preferred_element_type=jnp.float32
            ).astype(jnp.bfloat16)
            end = jnp.dot(chosen, ends[j], preferred_element_type=jnp.float32)
            out_ref[q * QUAD + j, :, whole:] = (end + note).astype(jnp.bfloat16)


def first_pack_kernel(
    whole, cap, most_ref, target_ref, label_ref, tokens_ref, normed_ref, out_ref
):
    values = tokens_ref[...].astype(jnp.float32)
    mean_sq = jnp.mean(values * values, axis=-1, keepdims=True)
    normed_ref[...] = (values * lax.rsqrt(mean_sq + 1e-06)).astype(jnp.bfloat16)
    most = most_ref[0].astype(jnp.float32)
    pack_rows(whole, cap, 0, most, target_ref, label_ref, normed_ref, out_ref)


def next_pack_kernel(whole, cap, base, target_ref, label_ref, normed_ref, out_ref):
    pack_rows(whole, cap, base, 0.0, target_ref, label_ref, normed_ref, out_ref)


def label_of(last_tile):
    rows = last_tile.shape[0]
    quarter = LANES // QUAD
    label = last_tile[:, quarter : quarter + 1].astype(jnp.float32) - 1.0
    return label - jnp.where(lanes_of(rows) < HALF, 0.0, 1.0)


def down_kernel(chunk, first_ref, rows_ref, *refs):
    weight_refs, out_ref = refs[:-1], refs[-1]
    width = rows_ref.shape[1]
    dims = (((1,), (1,)), ((), ()))
    low = lanes_of(chunk // 2) < HALF

    def one(c, carry):
        at = pl.ds(pl.multiple_of(c * chunk, chunk), chunk)
        label = label_of(rows_ref[at, width - LANES :])
        picked = jnp.zeros((chunk, LANES), jnp.float32)
        for k, weight_ref in enumerate(weight_refs):
            product = lax.dot_general(
                rows_ref[at, :], weight_ref[...], dims, preferred_element_type=jnp.float32
            )
            first = first_ref[k].astype(jnp.float32)
            for t in range(weight_ref.shape[0] // LANES):
                columns = slice(t * LANES, (t + 1) * LANES)
                picked = jnp.where(label == first + 2.0 * t, product[:, columns], picked)
        picked = picked + pltpu.roll(picked, HALF, 1)
        half = pl.ds(pl.multiple_of(c * (chunk // 2), chunk // 2), chunk // 2)
        out_ref[half, :] = jnp.where(
            low, picked[0 : chunk // 2], picked[chunk // 2 : chunk]
        ).astype(jnp.bfloat16)
        return carry

    lax.fori_loop(0, rows_ref.shape[0] // chunk, one, 0)


def up_kernel(chunk, first_ref, ends_ref, *refs):
    sum_refs, weight_refs, out_ref = refs[:QUAD], refs[QUAD:-1], refs[-1]
    width = ends_ref.shape[1]
    low = lanes_of(chunk // 2) < HALF

    def one(c, carry):
        at = pl.ds(pl.multiple_of(c * chunk, chunk), chunk)
        half = pl.ds(pl.multiple_of(c * (chunk // 2), chunk // 2), chunk // 2)
        label = label_of(ends_ref[at, width - LANES :])
        down = sum_refs[0][half, :].astype(jnp.float32)
        for ref in sum_refs[1:]:
            down = down + ref[half, :].astype(jnp.float32)
        down = down.astype(jnp.bfloat16).astype(jnp.float32)
        turned = pltpu.roll(down, HALF, 1)
        twice = jnp.concatenate(
            [jnp.where(low, down, turned), jnp.where(low, turned, down)], axis=0
        )
        delta = jnp.zeros((chunk, out_ref.shape[1]), jnp.float32)
        for k, weight_ref in enumerate(weight_refs):
            first = first_ref[k].astype(jnp.float32)
            placed = [
                jnp.where(label == first + 2.0 * t, twice, 0.0)
                for t in range(weight_ref.shape[0] // LANES)
            ]
            placed = jnp.concatenate(placed, axis=1).astype(jnp.bfloat16)
            delta = delta + jnp.dot(placed, weight_ref[...], preferred_element_type=jnp.float32)
        out_ref[at, :] = delta.astype(jnp.bfloat16)
        return carry

    lax.fori_loop(0, ends_ref.shape[0] // chunk, one, 0)


def mix_kernel(whole, bases, target_ref, tokens_ref, *refs):
    returned_refs, out_ref = refs[:-1], refs[-1]
    total = tokens_ref.shape[0]
    quads = returned_refs[0].shape[0] // QUAD
    quarter = LANES // QUAD
    lane = lanes_of(total)
    chosen = []
    for base, ref in zip(bases, returned_refs):
        cap = ref.shape[1]
        spot = lax.broadcasted_iota(jnp.int32, (total, quads * cap), 1)
        place = spot // cap * total + spot % cap + base
        chosen.append(jnp.where(target_ref[...] == place, 1.0, 0.0).astype(jnp.bfloat16))
    end = jnp.zeros((total, LANES), jnp.float32)
    for j in range(QUAD):
        delta = jnp.zeros((total, whole + LANES), jnp.float32)
        for choice, ref in zip(chosen, returned_refs):
            share = jnp.concatenate([ref[q * QUAD + j] for q in range(quads)], axis=0)
            delta = delta + jnp.dot(choice, share, preferred_element_type=jnp.float32)
        columns = slice(j * whole, (j + 1) * whole)
        out_ref[:, columns] = (
            tokens_ref[:, columns].astype(jnp.float32) + delta[:, 0:whole]
        ).astype(jnp.bfloat16)
        last = delta[:, whole:]
        turned = pltpu.roll(last, quarter * j, 1) if j else last
        end = jnp.where((lane >= quarter * j) & (lane < quarter * (j + 1)), turned, end)
    out_ref[:, QUAD * whole :] = (
        tokens_ref[:, QUAD * whole :].astype(jnp.float32) + end
    ).astype(jnp.bfloat16)


def call(kernel, out_shape, in_specs, flops, moved, after=()):
    many = isinstance(out_shape, list)
    skipped = len(after)
    body = (lambda *refs: kernel(*refs[skipped:])) if skipped else kernel
    run = pl.pallas_call(
        body,
        out_shape=out_shape,
        in_specs=[pl.BlockSpec(memory_space=pl.ANY)] * skipped + in_specs,
        out_specs=[VMEM] * len(out_shape) if many else VMEM,
        compiler_params=pltpu.CompilerParams(vmem_limit_bytes=48 * 2**20),
        cost_estimate=pl.CostEstimate(flops=flops, bytes_accessed=moved, transcendentals=0),
    )
    return functools.partial(run, *after)


def exchange(value):
    return lax.all_to_all(value, "adapter", split_axis=0, concat_axis=0, tiled=True)


def towards(value, k, devices):
    return lax.ppermute(value, "adapter", [(i, i ^ k) for i in range(devices)])


def swapped(value):
    return lax.ppermute(value, "groups", [(0, 1), (1, 0)])


def down_call(first, arrived, weights, after):
    arriving, share = arrived.shape
    columns = sum(weight.shape[0] for weight in weights)
    chunk = math.gcd(arriving, CHUNK)
    return call(
        functools.partial(down_kernel, chunk),
        jax.ShapeDtypeStruct((arriving // 2, LANES), jnp.bfloat16),
        [SMEM] + [VMEM] * (1 + len(weights)),
        2 * arriving * columns * share,
        2 * (arriving + columns) * share,
        after,
    )(first, arrived, *weights)


def up_call(first, arrived, partial, weights, devices):
    sums = [partial] + [towards(partial, k, devices) for k in range(1, QUAD)]
    arriving, share = arrived.shape
    columns = sum(weight.shape[0] for weight in weights)
    chunk = math.gcd(arriving, CHUNK)
    leaving = call(
        functools.partial(up_kernel, chunk),
        jax.ShapeDtypeStruct((arriving, share), jnp.bfloat16),
        [SMEM] + [VMEM] * (1 + QUAD + len(weights)),
        2 * arriving * columns * share,
        2 * (2 * arriving + columns) * share,
    )(first, arrived, *sums, *weights)
    return leaving.reshape(devices, arriving // devices, share)


def second_piece(
    cap,
    base,
    tokens,
    normed,
    target,
    label,
    first,
    arrived,
    partial,
    down_weights,
    up_near,
    up_far,
):
    total, width = tokens.shape
    devices = lax.axis_size("adapter")
    whole = width // LANES // QUAD * LANES
    share = whole + LANES
    outgoing = call(
        functools.partial(next_pack_kernel, whole, cap, base),
        jax.ShapeDtypeStruct((devices, cap, share), jnp.bfloat16),
        [VMEM, VMEM, VMEM],
        2 * devices * cap * total * share,
        2 * (total * width + devices * cap * share),
    )(target.reshape(1, total), label, normed)
    later = exchange(outgoing).reshape(devices * cap, share)
    up_weights = [*up_near, *up_far, *[swapped(value) for value in up_far]]
    leaving = up_call(first, arrived, partial, up_weights, devices)
    returned = exchange(leaving)
    later_partial = down_call(first, later, down_weights, [leaving])
    later_leaving = up_call(first, later, later_partial, up_weights, devices)
    later_leaving = later_leaving.at[0, 0, share - HALF :].set(returned[0, 0, share - HALF :])
    later_returned = exchange(later_leaving)
    return call(
        functools.partial(mix_kernel, whole, (0, base)),
        jax.ShapeDtypeStruct((total, width), jnp.bfloat16),
        [VMEM] * 4,
        2 * devices * (cap + base) * total * share,
        2 * (2 * total * width + devices * (cap + base) * share),
    )(target.reshape(total, 1), tokens, returned, later_returned)


def rows_to_quads(
    tokens, request_block_adapter, request_block_rows, adapter_down_weight, adapter_up_weight
):
    blocks, rows, width = tokens.shape
    devices = lax.axis_size("adapter")
    resident, rank, unused_width = adapter_up_weight.shape
    total = blocks * rows
    columns = resident * rank
    whole = width // LANES // QUAD * LANES
    share = whole + LANES
    bf16, i32 = jnp.bfloat16, jnp.int32

    quad = request_block_adapter // (resident * QUAD)
    label = request_block_adapter - quad * (resident * QUAD) + 1
    serial = jnp.arange(blocks, dtype=i32)
    same = quad[:, None] == quad[None, :]
    used = request_block_rows
    ahead = jnp.where(same & (serial[None, :] < serial[:, None]), used[None, :], 0)
    most = jnp.max(jnp.sum(jnp.where(same, used[None, :], 0), axis=1))
    row = jnp.arange(rows, dtype=i32)
    start = quad * total + jnp.sum(ahead, axis=1)
    target = jnp.where(row[None, :] < used[:, None], start[:, None] + row[None, :], -1)
    target = target.reshape(total).astype(i32)
    label = jnp.broadcast_to(label[:, None], (blocks, rows)).reshape(total, 1).astype(jnp.float32)

    me = lax.axis_index("adapter").astype(i32)
    group = lax.axis_index("groups").astype(i32)
    parts = jnp.bitwise_xor(me % QUAD, jnp.arange(QUAD, dtype=i32))
    own_half, twin_half = group * (resident // 2), (1 - group) * (resident // 2)
    first = jnp.concatenate(
        [parts * resident + jnp.stack([0 * group, 0 * group, own_half, own_half])]
        + [parts[2:] * resident + twin_half]
    ).astype(i32)

    def dealt(weight, after=()):
        counts = [columns, columns, columns // 2, columns // 2]
        values = call(
            functools.partial(weight_kernel, whole),
            [jax.ShapeDtypeStruct((count, share), bf16) for count in counts],
            [SMEM, SMEM, VMEM],
            0,
            4 * columns * width,
            after,
        )(parts, group.reshape(1), weight)
        near = [values[0], towards(values[1], 1, devices)]
        return near, [towards(values[k], k, devices) for k in range(2, QUAD)]

    down_near, down_far = dealt(adapter_down_weight.transpose(0, 2, 1).reshape(columns, width))
    up_near, up_far = dealt(adapter_up_weight.reshape(columns, width), down_far)
    down_weights = [*down_near, *down_far, *[swapped(value) for value in down_far]]

    cap = total // QUAD
    flat = tokens.reshape(total, width)
    normed, outgoing = call(
        functools.partial(first_pack_kernel, whole, cap),
        [
            jax.ShapeDtypeStruct((total, width), bf16),
            jax.ShapeDtypeStruct((devices, cap, share), bf16),
        ],
        [SMEM, VMEM, VMEM, VMEM],
        2 * devices * cap * total * share,
        2 * (2 * total * width + devices * cap * share),
        down_far[:1],
    )(most.reshape(1), target.reshape(1, total), label, flat)
    arrived = exchange(outgoing)

    most = jnp.max(arrived[:, 0, whole + LANES // QUAD + 1].astype(jnp.float32)).reshape(1, 1)
    most = jnp.maximum(most, swapped(most))[0, 0].astype(i32)
    caps = [total // 16, total // 8, total * 3 // 16, total - cap]
    index = sum((most > cap + more).astype(i32) for more in caps[:-1])
    arrived = arrived.reshape(devices * cap, share)
    partial = down_call(first, arrived, down_weights, [])
    mixed = lax.switch(
        index,
        [functools.partial(second_piece, more, cap) for more in caps],
        flat,
        normed,
        target,
        label,
        first,
        arrived,
        partial,
        down_weights,
        up_near,
        up_far,
    )
    return mixed.reshape(tokens.shape)


def solution(mesh):
    placed = (
        P(("groups", "adapter"), None, None),
        P(("groups", "adapter")),
        P(("groups", "adapter")),
        P("adapter", None, None),
        P("adapter", None, None),
    )

    def per_device(tokens, request_block_adapter, request_block_rows, down_weight, up_weight):
        blocks, rows, width = tokens.shape
        devices = mesh.shape["adapter"]
        slots = max(1, 4 * blocks // devices)
        quads = devices % QUAD == 0 and slots * QUAD >= blocks
        quads = quads and width % (QUAD * LANES) == LANES and up_weight.shape[1] == HALF
        plan = rows_to_quads if quads else rows_to_holders
        return plan(tokens, request_block_adapter, request_block_rows, down_weight, up_weight)

    return jax.shard_map(
        per_device,
        mesh=mesh,
        in_specs=placed,
        out_specs=P(("groups", "adapter"), None, None),
        check_vma=False,
    )
```

```python
import functools
import math

import jax
import jax.numpy as jnp
from jax import lax
from jax.experimental import pallas as pl
from jax.experimental.pallas import tpu as pltpu
from jax.sharding import PartitionSpec as P

LANES = 128
HALF = 64
QUAD = 4
CHUNK = 512
VMEM = pl.BlockSpec(memory_space=pltpu.VMEM)
SMEM = pl.BlockSpec(memory_space=pltpu.SMEM)


def normalise(tokens):
    values = tokens.astype(jnp.float32)
    mean_sq = jnp.mean(values * values, axis=-1, keepdims=True)
    return (values, (values * lax.rsqrt(mean_sq + 1e-06)).astype(jnp.bfloat16))


def resident_update(hidden_state, block_labels, adapter_down_weight, adapter_up_weight):
    feature_width = hidden_state.shape[-1]
    leading = hidden_state.shape[:-1]
    resident_rows, unused_value, inner_rank = adapter_down_weight.shape
    flattened_tokens = hidden_state.reshape(-1, feature_width)
    down_matrix = jnp.einsum(
        "tq,iqg->tig", flattened_tokens, adapter_down_weight, preferred_element_type=jnp.float32
    )
    down_matrix = down_matrix.astype(jnp.bfloat16).reshape(
        flattened_tokens.shape[0], resident_rows * inner_rank
    )
    column_owner = jnp.arange(resident_rows * inner_rank, dtype=jnp.int32) // inner_rank
    picked = block_labels.reshape(-1, 1) == column_owner[None, :]
    down_matrix = jnp.where(picked, down_matrix, jnp.zeros_like(down_matrix))
    lowrank_update = jnp.dot(
        down_matrix,
        adapter_up_weight.reshape(resident_rows * inner_rank, feature_width),
        preferred_element_type=jnp.float32,
    )
    return lowrank_update.astype(jnp.bfloat16).reshape(leading + (feature_width,))


def rows_to_holders(
    tokens, request_block_adapter, request_block_rows, adapter_down_weight, adapter_up_weight
):
    blocks, rows, feature_width = tokens.shape
    devices = lax.axis_size("adapter")
    resident_rows = adapter_down_weight.shape[0]
    slots = max(1, 4 * blocks // devices)
    values, normed = normalise(tokens)
    owner = request_block_adapter // resident_rows
    within = request_block_adapter - owner * resident_rows
    serial = jnp.arange(blocks, dtype=jnp.int32)
    earlier = (owner[:, None] == owner[None, :]) & (serial[None, :] < serial[:, None])
    position = owner * slots + jnp.sum(earlier, axis=1)
    outgoing = (
        jnp.zeros((devices * slots, rows, feature_width), jnp.bfloat16).at[position].set(normed)
    )
    outgoing = outgoing.reshape(devices, slots, rows, feature_width)
    block_labels = jnp.full((devices * slots,), -1, jnp.int32).at[position].set(within)
    block_labels = jnp.broadcast_to(block_labels[:, None], (devices * slots, rows)).reshape(
        devices, slots, rows
    )
    arriving_rows, row_markers = (
        lax.all_to_all(outgoing, "adapter", split_axis=0, concat_axis=0, tiled=True),
        lax.all_to_all(block_labels, "adapter", split_axis=0, concat_axis=0, tiled=True),
    )
    lowrank_update = resident_update(
        arriving_rows, row_markers, adapter_down_weight, adapter_up_weight
    )
    returned = lax.all_to_all(lowrank_update, "adapter", split_axis=0, concat_axis=0, tiled=True)
    mine = returned.reshape(devices * slots, rows, feature_width)[position]
    live = jnp.arange(rows, dtype=jnp.int32)[None, :] < request_block_rows[:, None]
    mixed = values + jnp.where(live[:, :, None], mine.astype(jnp.float32), jnp.float32(0.0))
    return mixed.astype(jnp.bfloat16)


def lanes_of(rows):
    return lax.broadcasted_iota(jnp.int32, (rows, LANES), 1)


def weight_kernel(whole, part_ref, group_ref, weight_ref, *out_refs):
    quarter = LANES // QUAD
    inside = lanes_of(weight_ref.shape[0]) < quarter
    for k, out_ref in enumerate(out_refs):
        j = part_ref[k]
        count = out_ref.shape[0]
        start = 0 if k < 2 else pl.multiple_of(group_ref[0] * count, count)
        rows = pl.ds(start, count)
        out_ref[:, 0:whole] = weight_ref[rows, pl.ds(pl.multiple_of(j * whole, LANES), whole)]
        last = weight_ref[rows, QUAD * whole :].astype(jnp.float32)
        turned = pltpu.roll(last, lax.rem(LANES - quarter * j, LANES), 1)
        out_ref[:, whole:] = jnp.where(inside[0:count], turned, 0.0).astype(jnp.bfloat16)


def pack_rows(whole, cap, base, most, target_ref, label_ref, rows_ref, out_ref):
    total = rows_ref.shape[0]
    quads = out_ref.shape[0] // QUAD
    quarter = LANES // QUAD
    lane = lanes_of(total)
    last = rows_ref[:, QUAD * whole :].astype(jnp.float32)
    label = jnp.where(lane == quarter, label_ref[...], 0.0)
    ends = []
    for j in range(QUAD):
        turned = pltpu.roll(last, (LANES - quarter * j) % LANES, 1) if j else last
        ends.append(jnp.where(lane < quarter, turned, label).astype(jnp.bfloat16))
    note = jnp.where(lanes_of(cap) == quarter + 1, most, 0.0)
    for q in range(quads):
        place = lax.broadcasted_iota(jnp.int32, (cap, total), 0) + (q * total + base)
        chosen = jnp.where(target_ref[...] == place, 1.0, 0.0).astype(jnp.bfloat16)
        for j in range(QUAD):
            columns = slice(j * whole, (j + 1) * whole)
            out_ref[q * QUAD + j, :, 0:whole] = jnp.dot(
                chosen, rows_ref[:, columns], preferred_element_type=jnp.float32
            ).astype(jnp.bfloat16)
            end = jnp.dot(chosen, ends[j], preferred_element_type=jnp.float32)
            out_ref[q * QUAD + j, :, whole:] = (end + note).astype(jnp.bfloat16)


def first_pack_kernel(
    whole, cap, most_ref, target_ref, label_ref, tokens_ref, normed_ref, out_ref
):
    values = tokens_ref[...].astype(jnp.float32)
    mean_sq = jnp.mean(values * values, axis=-1, keepdims=True)
    normed_ref[...] = (values * lax.rsqrt(mean_sq + 1e-06)).astype(jnp.bfloat16)
    most = most_ref[0].astype(jnp.float32)
    pack_rows(whole, cap, 0, most, target_ref, label_ref, normed_ref, out_ref)


def next_pack_kernel(whole, cap, base, target_ref, label_ref, normed_ref, out_ref):
    pack_rows(whole, cap, base, 0.0, target_ref, label_ref, normed_ref, out_ref)


def label_of(last_tile):
    rows = last_tile.shape[0]
    quarter = LANES // QUAD
    label = last_tile[:, quarter : quarter + 1].astype(jnp.float32) - 1.0
    return label - jnp.where(lanes_of(rows) < HALF, 0.0, 1.0)


def down_kernel(chunk, first_ref, rows_ref, *refs):
    weight_refs, out_ref = refs[:-1], refs[-1]
    width = rows_ref.shape[1]
    dims = (((1,), (1,)), ((), ()))
    low = lanes_of(chunk // 2) < HALF

    def one(c, carry):
        at = pl.ds(pl.multiple_of(c * chunk, chunk), chunk)
        label = label_of(rows_ref[at, width - LANES :])
        picked = jnp.zeros((chunk, LANES), jnp.float32)
        for k, weight_ref in enumerate(weight_refs):
            product = lax.dot_general(
                rows_ref[at, :], weight_ref[...], dims, preferred_element_type=jnp.float32
            )
            first = first_ref[k].astype(jnp.float32)
            for t in range(weight_ref.shape[0] // LANES):
                columns = slice(t * LANES, (t + 1) * LANES)
                picked = jnp.where(label == first + 2.0 * t, product[:, columns], picked)
        picked = picked + pltpu.roll(picked, HALF, 1)
        half = pl.ds(pl.multiple_of(c * (chunk // 2), chunk // 2), chunk // 2)
        out_ref[half, :] = jnp.where(
            low, picked[0 : chunk // 2], picked[chunk // 2 : chunk]
        ).astype(jnp.bfloat16)
        return carry

    lax.fori_loop(0, rows_ref.shape[0] // chunk, one, 0)


def up_kernel(chunk, first_ref, ends_ref, *refs):
    sum_refs, weight_refs, out_ref = refs[:QUAD], refs[QUAD:-1], refs[-1]
    width = ends_ref.shape[1]
    low = lanes_of(chunk // 2) < HALF

    def one(c, carry):
        at = pl.ds(pl.multiple_of(c * chunk, chunk), chunk)
        half = pl.ds(pl.multiple_of(c * (chunk // 2), chunk // 2), chunk // 2)
        label = label_of(ends_ref[at, width - LANES :])
        down = sum_refs[0][half, :].astype(jnp.float32)
        for ref in sum_refs[1:]:
            down = down + ref[half, :].astype(jnp.float32)
        down = down.astype(jnp.bfloat16).astype(jnp.float32)
        turned = pltpu.roll(down, HALF, 1)
        twice = jnp.concatenate(
            [jnp.where(low, down, turned), jnp.where(low, turned, down)], axis=0
        )
        delta = jnp.zeros((chunk, out_ref.shape[1]), jnp.float32)
        for k, weight_ref in enumerate(weight_refs):
            first = first_ref[k].astype(jnp.float32)
            placed = [
                jnp.where(label == first + 2.0 * t, twice, 0.0)
                for t in range(weight_ref.shape[0] // LANES)
            ]
            placed = jnp.concatenate(placed, axis=1).astype(jnp.bfloat16)
            delta = delta + jnp.dot(placed, weight_ref[...], preferred_element_type=jnp.float32)
        out_ref[at, :] = delta.astype(jnp.bfloat16)
        return carry

    lax.fori_loop(0, ends_ref.shape[0] // chunk, one, 0)


def mix_kernel(whole, bases, target_ref, tokens_ref, *refs):
    returned_refs, out_ref = refs[:-1], refs[-1]
    total = tokens_ref.shape[0]
    quads = returned_refs[0].shape[0] // QUAD
    quarter = LANES // QUAD
    lane = lanes_of(total)
    chosen = []
    for base, ref in zip(bases, returned_refs):
        cap = ref.shape[1]
        spot = lax.broadcasted_iota(jnp.int32, (total, quads * cap), 1)
        place = spot // cap * total + spot % cap + base
        chosen.append(jnp.where(target_ref[...] == place, 1.0, 0.0).astype(jnp.bfloat16))
    end = jnp.zeros((total, LANES), jnp.float32)
    for j in range(QUAD):
        delta = jnp.zeros((total, whole + LANES), jnp.float32)
        for choice, ref in zip(chosen, returned_refs):
            share = jnp.concatenate([ref[q * QUAD + j] for q in range(quads)], axis=0)
            delta = delta + jnp.dot(choice, share, preferred_element_type=jnp.float32)
        columns = slice(j * whole, (j + 1) * whole)
        out_ref[:, columns] = (
            tokens_ref[:, columns].astype(jnp.float32) + delta[:, 0:whole]
        ).astype(jnp.bfloat16)
        last = delta[:, whole:]
        turned = pltpu.roll(last, quarter * j, 1) if j else last
        end = jnp.where((lane >= quarter * j) & (lane < quarter * (j + 1)), turned, end)
    out_ref[:, QUAD * whole :] = (
        tokens_ref[:, QUAD * whole :].astype(jnp.float32) + end
    ).astype(jnp.bfloat16)


def call(kernel, out_shape, in_specs, flops, moved, after=()):
    many = isinstance(out_shape, list)
    skipped = len(after)
    body = (lambda *refs: kernel(*refs[skipped:])) if skipped else kernel
    run = pl.pallas_call(
        body,
        out_shape=out_shape,
        in_specs=[pl.BlockSpec(memory_space=pl.ANY)] * skipped + in_specs,
        out_specs=[VMEM] * len(out_shape) if many else VMEM,
        compiler_params=pltpu.CompilerParams(vmem_limit_bytes=48 * 2**20),
        cost_estimate=pl.CostEstimate(flops=flops, bytes_accessed=moved, transcendentals=0),
    )
    return functools.partial(run, *after)


def exchange(value):
    return lax.all_to_all(value, "adapter", split_axis=0, concat_axis=0, tiled=True)


def towards(value, k, devices):
    return lax.ppermute(value, "adapter", [(i, i ^ k) for i in range(devices)])


def swapped(value):
    return lax.ppermute(value, "groups", [(0, 1), (1, 0)])


def behind(value, earlier):
    lane = value.shape[2] - 1
    return value.at[0, 0, lane].set(earlier[0, 0, lane])


def down_call(first, arrived, weights, after):
    arriving, share = arrived.shape
    columns = sum(weight.shape[0] for weight in weights)
    chunk = math.gcd(arriving, CHUNK)
    return call(
        functools.partial(down_kernel, chunk),
        jax.ShapeDtypeStruct((arriving // 2, LANES), jnp.bfloat16),
        [SMEM] + [VMEM] * (1 + len(weights)),
        2 * arriving * columns * share,
        2 * (arriving + columns) * share,
        after,
    )(first, arrived, *weights)


def up_call(first, arrived, partial, weights, devices):
    sums = [partial] + [towards(partial, k, devices) for k in range(1, QUAD)]
    arriving, share = arrived.shape
    columns = sum(weight.shape[0] for weight in weights)
    chunk = math.gcd(arriving, CHUNK)
    leaving = call(
        functools.partial(up_kernel, chunk),
        jax.ShapeDtypeStruct((arriving, share), jnp.bfloat16),
        [SMEM] + [VMEM] * (1 + QUAD + len(weights)),
        2 * arriving * columns * share,
        2 * (2 * arriving + columns) * share,
    )(first, arrived, *sums, *weights)
    return leaving.reshape(devices, arriving // devices, share)


def rows_to_quads(
    tokens, request_block_adapter, request_block_rows, adapter_down_weight, adapter_up_weight
):
    blocks, rows, width = tokens.shape
    devices = lax.axis_size("adapter")
    resident, rank, unused_width = adapter_up_weight.shape
    total = blocks * rows
    columns = resident * rank
    whole = width // LANES // QUAD * LANES
    share = whole + LANES
    bf16, i32 = jnp.bfloat16, jnp.int32

    quad = request_block_adapter // (resident * QUAD)
    label = request_block_adapter - quad * (resident * QUAD) + 1
    serial = jnp.arange(blocks, dtype=i32)
    same = quad[:, None] == quad[None, :]
    used = request_block_rows
    ahead = jnp.where(same & (serial[None, :] < serial[:, None]), used[None, :], 0)
    most = jnp.max(jnp.sum(jnp.where(same, used[None, :], 0), axis=1))
    row = jnp.arange(rows, dtype=i32)
    start = quad * total + jnp.sum(ahead, axis=1)
    target = jnp.where(row[None, :] < used[:, None], start[:, None] + row[None, :], -1)
    target = target.reshape(total).astype(i32)
    label = jnp.broadcast_to(label[:, None], (blocks, rows)).reshape(total, 1).astype(jnp.float32)

    me = lax.axis_index("adapter").astype(i32)
    group = lax.axis_index("groups").astype(i32)
    parts = jnp.bitwise_xor(me % QUAD, jnp.arange(QUAD, dtype=i32))
    own_half, twin_half = group * (resident // 2), (1 - group) * (resident // 2)
    first = jnp.concatenate(
        [parts * resident + jnp.stack([0 * group, 0 * group, own_half, own_half])]
        + [parts[2:] * resident + twin_half]
    ).astype(i32)

    def dealt(weight, after=()):
        counts = [columns, columns, columns // 2, columns // 2]
        values = call(
            functools.partial(weight_kernel, whole),
            [jax.ShapeDtypeStruct((count, share), bf16) for count in counts],
            [SMEM, SMEM, VMEM],
            0,
            4 * columns * width,
            after,
        )(parts, group.reshape(1), weight)
        near = [values[0], towards(values[1], 1, devices)]
        return near, [towards(values[k], k, devices) for k in range(2, QUAD)]

    down_near, down_far = dealt(adapter_down_weight.transpose(0, 2, 1).reshape(columns, width))
    up_near, up_far = dealt(adapter_up_weight.reshape(columns, width), down_far)
    down_weights = [*down_near, *down_far, *[swapped(value) for value in down_far]]

    cap = total // QUAD
    flat = tokens.reshape(total, width)
    normed, outgoing = call(
        functools.partial(first_pack_kernel, whole, cap),
        [
            jax.ShapeDtypeStruct((total, width), bf16),
            jax.ShapeDtypeStruct((devices, cap, share), bf16),
        ],
        [SMEM, VMEM, VMEM, VMEM],
        2 * devices * cap * total * share,
        2 * (2 * total * width + devices * cap * share),
        down_near[:1],
    )(most.reshape(1), target.reshape(1, total), label, flat)
    arrived = exchange(outgoing)

    most = jnp.max(arrived[:, 0, whole + LANES // QUAD + 1].astype(jnp.float32)).reshape(1, 1)
    most = jnp.maximum(most, swapped(most))[0, 0].astype(i32)
    later_cap = total * 3 // 16
    later_outgoing = call(
        functools.partial(next_pack_kernel, whole, later_cap, cap),
        jax.ShapeDtypeStruct((devices, later_cap, share), bf16),
        [VMEM, VMEM, VMEM],
        2 * devices * later_cap * total * share,
        2 * (total * width + devices * later_cap * share),
    )(target.reshape(1, total), label, normed)
    later_arrived = exchange(behind(later_outgoing, arrived))

    arrived = arrived.reshape(devices * cap, share)
    later_arrived = later_arrived.reshape(devices * later_cap, share)
    up_weights = [*up_near, *up_far, *[swapped(value) for value in up_far]]
    partial = down_call(first, arrived, down_weights, [])
    leaving = up_call(first, arrived, partial, up_weights, devices)
    returned = exchange(leaving)
    later_partial = down_call(first, later_arrived, down_weights, [leaving])
    later_leaving = up_call(first, later_arrived, later_partial, up_weights, devices)
    later_returned = exchange(behind(later_leaving, returned))

    def mix(tokens, target, returned, later_returned, *unused_values):
        mixed = call(
            functools.partial(mix_kernel, whole, (0, cap)),
            jax.ShapeDtypeStruct((total, width), bf16),
            [VMEM] * 4,
            2 * devices * (cap + later_cap) * total * share,
            2 * (2 * total * width + devices * (cap + later_cap) * share),
        )(target.reshape(total, 1), tokens.reshape(total, width), returned, later_returned)
        return mixed.reshape(tokens.shape)

    def start_again(tokens, target, returned, later_returned, *rest):
        return rows_to_holders(tokens, *rest)

    return lax.cond(
        most > cap + later_cap,
        start_again,
        mix,
        tokens,
        target,
        returned,
        later_returned,
        request_block_adapter,
        request_block_rows,
        adapter_down_weight,
        adapter_up_weight,
    )


def solution(mesh):
    placed = (
        P(("groups", "adapter"), None, None),
        P(("groups", "adapter")),
        P(("groups", "adapter")),
        P("adapter", None, None),
        P("adapter", None, None),
    )

    def per_device(tokens, request_block_adapter, request_block_rows, down_weight, up_weight):
        blocks, rows, width = tokens.shape
        devices = mesh.shape["adapter"]
        slots = max(1, 4 * blocks // devices)
        quads = devices % QUAD == 0 and slots * QUAD >= blocks
        quads = quads and width % (QUAD * LANES) == LANES and up_weight.shape[1] == HALF
        plan = rows_to_quads if quads else rows_to_holders
        return plan(tokens, request_block_adapter, request_block_rows, down_weight, up_weight)

    return jax.shard_map(
        per_device,
        mesh=mesh,
        in_specs=placed,
        out_specs=P(("groups", "adapter"), None, None),
        check_vma=False,
    )
```

```python
import functools
import math

import jax
import jax.numpy as jnp
from jax import lax
from jax.experimental import pallas as pl
from jax.experimental.pallas import tpu as pltpu
from jax.sharding import PartitionSpec as P

LANES = 128
HALF = 64
QUAD = 4
CHUNK = 512
VMEM = pl.BlockSpec(memory_space=pltpu.VMEM)
SMEM = pl.BlockSpec(memory_space=pltpu.SMEM)


def normalise(tokens):
    values = tokens.astype(jnp.float32)
    mean_sq = jnp.mean(values * values, axis=-1, keepdims=True)
    return (values, (values * lax.rsqrt(mean_sq + 1e-06)).astype(jnp.bfloat16))


def resident_update(hidden_state, block_labels, adapter_down_weight, adapter_up_weight):
    feature_width = hidden_state.shape[-1]
    leading = hidden_state.shape[:-1]
    resident_rows, unused_value, inner_rank = adapter_down_weight.shape
    flattened_tokens = hidden_state.reshape(-1, feature_width)
    down_matrix = jnp.einsum(
        "tq,iqg->tig", flattened_tokens, adapter_down_weight, preferred_element_type=jnp.float32
    )
    down_matrix = down_matrix.astype(jnp.bfloat16).reshape(
        flattened_tokens.shape[0], resident_rows * inner_rank
    )
    column_owner = jnp.arange(resident_rows * inner_rank, dtype=jnp.int32) // inner_rank
    picked = block_labels.reshape(-1, 1) == column_owner[None, :]
    down_matrix = jnp.where(picked, down_matrix, jnp.zeros_like(down_matrix))
    lowrank_update = jnp.dot(
        down_matrix,
        adapter_up_weight.reshape(resident_rows * inner_rank, feature_width),
        preferred_element_type=jnp.float32,
    )
    return lowrank_update.astype(jnp.bfloat16).reshape(leading + (feature_width,))


def rows_to_holders(
    tokens, request_block_adapter, request_block_rows, adapter_down_weight, adapter_up_weight
):
    blocks, rows, feature_width = tokens.shape
    devices = lax.axis_size("adapter")
    resident_rows = adapter_down_weight.shape[0]
    slots = max(1, 4 * blocks // devices)
    values, normed = normalise(tokens)
    owner = request_block_adapter // resident_rows
    within = request_block_adapter - owner * resident_rows
    serial = jnp.arange(blocks, dtype=jnp.int32)
    earlier = (owner[:, None] == owner[None, :]) & (serial[None, :] < serial[:, None])
    position = owner * slots + jnp.sum(earlier, axis=1)
    outgoing = (
        jnp.zeros((devices * slots, rows, feature_width), jnp.bfloat16).at[position].set(normed)
    )
    outgoing = outgoing.reshape(devices, slots, rows, feature_width)
    block_labels = jnp.full((devices * slots,), -1, jnp.int32).at[position].set(within)
    block_labels = jnp.broadcast_to(block_labels[:, None], (devices * slots, rows)).reshape(
        devices, slots, rows
    )
    arriving_rows, row_markers = (
        lax.all_to_all(outgoing, "adapter", split_axis=0, concat_axis=0, tiled=True),
        lax.all_to_all(block_labels, "adapter", split_axis=0, concat_axis=0, tiled=True),
    )
    lowrank_update = resident_update(
        arriving_rows, row_markers, adapter_down_weight, adapter_up_weight
    )
    returned = lax.all_to_all(lowrank_update, "adapter", split_axis=0, concat_axis=0, tiled=True)
    mine = returned.reshape(devices * slots, rows, feature_width)[position]
    live = jnp.arange(rows, dtype=jnp.int32)[None, :] < request_block_rows[:, None]
    mixed = values + jnp.where(live[:, :, None], mine.astype(jnp.float32), jnp.float32(0.0))
    return mixed.astype(jnp.bfloat16)


def lanes_of(rows):
    return lax.broadcasted_iota(jnp.int32, (rows, LANES), 1)


def weight_kernel(whole, part_ref, group_ref, weight_ref, *out_refs):
    quarter = LANES // QUAD
    inside = lanes_of(weight_ref.shape[0]) < quarter
    for k, out_ref in enumerate(out_refs):
        j = part_ref[k]
        count = out_ref.shape[0]
        start = 0 if k < 2 else pl.multiple_of(group_ref[0] * count, count)
        rows = pl.ds(start, count)
        out_ref[:, 0:whole] = weight_ref[rows, pl.ds(pl.multiple_of(j * whole, LANES), whole)]
        last = weight_ref[rows, QUAD * whole :].astype(jnp.float32)
        turned = pltpu.roll(last, lax.rem(LANES - quarter * j, LANES), 1)
        out_ref[:, whole:] = jnp.where(inside[0:count], turned, 0.0).astype(jnp.bfloat16)


def pack_rows(whole, cap, base, most, target_ref, label_ref, rows_ref, out_ref):
    total = rows_ref.shape[0]
    quads = out_ref.shape[0] // QUAD
    quarter = LANES // QUAD
    lane = lanes_of(total)
    last = rows_ref[:, QUAD * whole :].astype(jnp.float32)
    label = jnp.where(lane == quarter, label_ref[...], 0.0)
    ends = []
    for j in range(QUAD):
        turned = pltpu.roll(last, (LANES - quarter * j) % LANES, 1) if j else last
        ends.append(jnp.where(lane < quarter, turned, label).astype(jnp.bfloat16))
    note = jnp.where(lanes_of(cap) == quarter + 1, most, 0.0)
    for q in range(quads):
        place = lax.broadcasted_iota(jnp.int32, (cap, total), 0) + (q * total + base)
        chosen = jnp.where(target_ref[...] == place, 1.0, 0.0).astype(jnp.bfloat16)
        for j in range(QUAD):
            columns = slice(j * whole, (j + 1) * whole)
            out_ref[q * QUAD + j, :, 0:whole] = jnp.dot(
                chosen, rows_ref[:, columns], preferred_element_type=jnp.float32
            ).astype(jnp.bfloat16)
            end = jnp.dot(chosen, ends[j], preferred_element_type=jnp.float32)
            out_ref[q * QUAD + j, :, whole:] = (end + note).astype(jnp.bfloat16)


def first_pack_kernel(
    whole, cap, most_ref, target_ref, label_ref, tokens_ref, normed_ref, out_ref
):
    values = tokens_ref[...].astype(jnp.float32)
    mean_sq = jnp.mean(values * values, axis=-1, keepdims=True)
    normed_ref[...] = (values * lax.rsqrt(mean_sq + 1e-06)).astype(jnp.bfloat16)
    most = most_ref[0].astype(jnp.float32)
    pack_rows(whole, cap, 0, most, target_ref, label_ref, normed_ref, out_ref)


def next_pack_kernel(whole, cap, base, target_ref, label_ref, normed_ref, out_ref):
    pack_rows(whole, cap, base, 0.0, target_ref, label_ref, normed_ref, out_ref)


def label_of(last_tile):
    rows = last_tile.shape[0]
    quarter = LANES // QUAD
    label = last_tile[:, quarter : quarter + 1].astype(jnp.float32) - 1.0
    return label - jnp.where(lanes_of(rows) < HALF, 0.0, 1.0)


def down_kernel(chunk, first_ref, rows_ref, *refs):
    weight_refs, out_ref = refs[:-1], refs[-1]
    width = rows_ref.shape[1]
    dims = (((1,), (1,)), ((), ()))
    low = lanes_of(chunk // 2) < HALF

    def one(c, carry):
        at = pl.ds(pl.multiple_of(c * chunk, chunk), chunk)
        label = label_of(rows_ref[at, width - LANES :])
        picked = jnp.zeros((chunk, LANES), jnp.float32)
        for k, weight_ref in enumerate(weight_refs):
            product = lax.dot_general(
                rows_ref[at, :], weight_ref[...], dims, preferred_element_type=jnp.float32
            )
            first = first_ref[k].astype(jnp.float32)
            for t in range(weight_ref.shape[0] // LANES):
                columns = slice(t * LANES, (t + 1) * LANES)
                picked = jnp.where(label == first + 2.0 * t, product[:, columns], picked)
        picked = picked + pltpu.roll(picked, HALF, 1)
        half = pl.ds(pl.multiple_of(c * (chunk // 2), chunk // 2), chunk // 2)
        out_ref[half, :] = jnp.where(
            low, picked[0 : chunk // 2], picked[chunk // 2 : chunk]
        ).astype(jnp.bfloat16)
        return carry

    lax.fori_loop(0, rows_ref.shape[0] // chunk, one, 0)


def up_kernel(chunk, first_ref, ends_ref, *refs):
    sum_refs, weight_refs, out_ref = refs[:QUAD], refs[QUAD:-1], refs[-1]
    width = ends_ref.shape[1]
    low = lanes_of(chunk // 2) < HALF

    def one(c, carry):
        at = pl.ds(pl.multiple_of(c * chunk, chunk), chunk)
        half = pl.ds(pl.multiple_of(c * (chunk // 2), chunk // 2), chunk // 2)
        label = label_of(ends_ref[at, width - LANES :])
        down = sum_refs[0][half, :].astype(jnp.float32)
        for ref in sum_refs[1:]:
            down = down + ref[half, :].astype(jnp.float32)
        down = down.astype(jnp.bfloat16).astype(jnp.float32)
        turned = pltpu.roll(down, HALF, 1)
        twice = jnp.concatenate(
            [jnp.where(low, down, turned), jnp.where(low, turned, down)], axis=0
        )
        delta = jnp.zeros((chunk, out_ref.shape[1]), jnp.float32)
        for k, weight_ref in enumerate(weight_refs):
            first = first_ref[k].astype(jnp.float32)
            placed = [
                jnp.where(label == first + 2.0 * t, twice, 0.0)
                for t in range(weight_ref.shape[0] // LANES)
            ]
            placed = jnp.concatenate(placed, axis=1).astype(jnp.bfloat16)
            delta = delta + jnp.dot(placed, weight_ref[...], preferred_element_type=jnp.float32)
        out_ref[at, :] = delta.astype(jnp.bfloat16)
        return carry

    lax.fori_loop(0, ends_ref.shape[0] // chunk, one, 0)


def last_up_kernel(chunk, blocks_of, first_ref, ends_ref, earlier_ref, *refs):
    out_ref, delta_ref = refs[-2:]
    up_kernel(chunk, first_ref, ends_ref, *refs[:-2], delta_ref)
    devices, earlier, later = blocks_of
    kept = out_ref.shape[1] - earlier

    def one(s, carry):
        out_ref[s, 0:earlier, :] = earlier_ref[s]
        start = pl.multiple_of(s * later, later)
        out_ref[s, earlier:, :] = delta_ref[pl.ds(start, kept), :]
        return carry

    lax.fori_loop(0, devices, one, 0)


def mix_kernel(whole, target_ref, tokens_ref, returned_ref, out_ref):
    total = tokens_ref.shape[0]
    quads, cap = returned_ref.shape[0] // QUAD, returned_ref.shape[1]
    quarter = LANES // QUAD
    lane = lanes_of(total)
    spot = lax.broadcasted_iota(jnp.int32, (total, quads * cap), 1)
    place = spot // cap * total + spot % cap
    chosen = jnp.where(target_ref[...] == place, 1.0, 0.0).astype(jnp.bfloat16)
    end = jnp.zeros((total, LANES), jnp.float32)
    for j in range(QUAD):
        share = jnp.concatenate([returned_ref[q * QUAD + j] for q in range(quads)], axis=0)
        delta = jnp.dot(chosen, share, preferred_element_type=jnp.float32)
        columns = slice(j * whole, (j + 1) * whole)
        out_ref[:, columns] = (
            tokens_ref[:, columns].astype(jnp.float32) + delta[:, 0:whole]
        ).astype(jnp.bfloat16)
        last = delta[:, whole:]
        turned = pltpu.roll(last, quarter * j, 1) if j else last
        end = jnp.where((lane >= quarter * j) & (lane < quarter * (j + 1)), turned, end)
    out_ref[:, QUAD * whole :] = (
        tokens_ref[:, QUAD * whole :].astype(jnp.float32) + end
    ).astype(jnp.bfloat16)


def call(kernel, out_shape, in_specs, flops, moved, after=(), scratch=()):
    many = isinstance(out_shape, list)
    skipped = len(after)
    body = (lambda *refs: kernel(*refs[skipped:])) if skipped else kernel
    run = pl.pallas_call(
        body,
        out_shape=out_shape,
        in_specs=[pl.BlockSpec(memory_space=pl.ANY)] * skipped + in_specs,
        out_specs=[VMEM] * len(out_shape) if many else VMEM,
        scratch_shapes=scratch,
        compiler_params=pltpu.CompilerParams(vmem_limit_bytes=48 * 2**20),
        cost_estimate=pl.CostEstimate(flops=flops, bytes_accessed=moved, transcendentals=0),
    )
    return functools.partial(run, *after)


def exchange(value):
    return lax.all_to_all(value, "adapter", split_axis=0, concat_axis=0, tiled=True)


def towards(value, k, devices):
    return lax.ppermute(value, "adapter", [(i, i ^ k) for i in range(devices)])


def swapped(value):
    return lax.ppermute(value, "groups", [(0, 1), (1, 0)])


def behind(value, *earlier):
    lane = value.shape[2] - 1
    marks = sum(array.reshape(-1, array.shape[-1])[0, lane].astype(jnp.float32) for array in earlier)
    return value.at[0, 0, lane].set(marks.astype(value.dtype))


def down_call(first, arrived, weights, after):
    arriving, share = arrived.shape
    columns = sum(weight.shape[0] for weight in weights)
    chunk = math.gcd(arriving, CHUNK)
    return call(
        functools.partial(down_kernel, chunk),
        jax.ShapeDtypeStruct((arriving // 2, LANES), jnp.bfloat16),
        [SMEM] + [VMEM] * (1 + len(weights)),
        2 * arriving * columns * share,
        2 * (arriving + columns) * share,
        after,
    )(first, arrived, *weights)


def quad_sums(partial, devices):
    return [partial] + [towards(partial, k, devices) for k in range(1, QUAD)]


def up_call(first, arrived, sums, weights, devices):
    arriving, share = arrived.shape
    columns = sum(weight.shape[0] for weight in weights)
    chunk = math.gcd(arriving, CHUNK)
    leaving = call(
        functools.partial(up_kernel, chunk),
        jax.ShapeDtypeStruct((arriving, share), jnp.bfloat16),
        [SMEM] + [VMEM] * (1 + QUAD + len(weights)),
        2 * arriving * columns * share,
        2 * (2 * arriving + columns) * share,
    )(first, arrived, *sums, *weights)
    return leaving.reshape(devices, arriving // devices, share)


def back_and_mix(
    kept, tokens, target, first, later_arrived, leaving, later_sums, up_weights, *unused_values
):
    blocks, rows, width = tokens.shape
    total = blocks * rows
    devices, cap, share = leaving.shape
    whole = share - LANES
    arriving = later_arrived.shape[0]
    columns = sum(weight.shape[0] for weight in up_weights)
    everything = call(
        functools.partial(
            last_up_kernel, math.gcd(arriving, CHUNK), (devices, cap, arriving // devices)
        ),
        jax.ShapeDtypeStruct((devices, kept, share), jnp.bfloat16),
        [SMEM] + [VMEM] * (2 + QUAD + len(up_weights)),
        2 * arriving * columns * share,
        2 * (2 * devices * kept + columns) * share,
        (),
        [pltpu.VMEM((arriving, share), jnp.bfloat16)],
    )(first, later_arrived, leaving, *later_sums, *up_weights)
    mixed = call(
        functools.partial(mix_kernel, whole),
        jax.ShapeDtypeStruct((total, width), jnp.bfloat16),
        [VMEM] * 3,
        2 * devices * kept * total * share,
        2 * (2 * total * width + devices * kept * share),
    )(target.reshape(total, 1), tokens.reshape(total, width), exchange(everything))
    return mixed.reshape(tokens.shape)


def start_again(
    tokens, target, first, later_arrived, leaving, later_sums, up_weights, *arguments
):
    return rows_to_holders(tokens, *arguments)


def rows_to_quads(
    tokens, request_block_adapter, request_block_rows, adapter_down_weight, adapter_up_weight
):
    blocks, rows, width = tokens.shape
    devices = lax.axis_size("adapter")
    resident, rank, unused_width = adapter_up_weight.shape
    total = blocks * rows
    columns = resident * rank
    whole = width // LANES // QUAD * LANES
    share = whole + LANES
    bf16, i32 = jnp.bfloat16, jnp.int32

    quad = request_block_adapter // (resident * QUAD)
    label = request_block_adapter - quad * (resident * QUAD) + 1
    serial = jnp.arange(blocks, dtype=i32)
    same = quad[:, None] == quad[None, :]
    used = request_block_rows
    ahead = jnp.where(same & (serial[None, :] < serial[:, None]), used[None, :], 0)
    most = jnp.max(jnp.sum(jnp.where(same, used[None, :], 0), axis=1))
    row = jnp.arange(rows, dtype=i32)
    start = quad * total + jnp.sum(ahead, axis=1)
    target = jnp.where(row[None, :] < used[:, None], start[:, None] + row[None, :], -1)
    target = target.reshape(total).astype(i32)
    label = jnp.broadcast_to(label[:, None], (blocks, rows)).reshape(total, 1).astype(jnp.float32)

    me = lax.axis_index("adapter").astype(i32)
    group = lax.axis_index("groups").astype(i32)
    parts = jnp.bitwise_xor(me % QUAD, jnp.arange(QUAD, dtype=i32))
    own_half, twin_half = group * (resident // 2), (1 - group) * (resident // 2)
    first = jnp.concatenate(
        [parts * resident + jnp.stack([0 * group, 0 * group, own_half, own_half])]
        + [parts[2:] * resident + twin_half]
    ).astype(i32)

    def dealt(weight, after=()):
        counts = [columns, columns, columns // 2, columns // 2]
        values = call(
            functools.partial(weight_kernel, whole),
            [jax.ShapeDtypeStruct((count, share), bf16) for count in counts],
            [SMEM, SMEM, VMEM],
            0,
            4 * columns * width,
            after,
        )(parts, group.reshape(1), weight)
        near = [values[0], towards(values[1], 1, devices)]
        return near, [towards(values[k], k, devices) for k in range(2, QUAD)]

    down_near, down_far = dealt(adapter_down_weight.transpose(0, 2, 1).reshape(columns, width))
    up_near, up_far = dealt(adapter_up_weight.reshape(columns, width), down_far)
    down_weights = [*down_near, *down_far, *[swapped(value) for value in down_far]]

    cap = total // QUAD
    flat = tokens.reshape(total, width)
    normed, outgoing = call(
        functools.partial(first_pack_kernel, whole, cap),
        [
            jax.ShapeDtypeStruct((total, width), bf16),
            jax.ShapeDtypeStruct((devices, cap, share), bf16),
        ],
        [SMEM, VMEM, VMEM, VMEM],
        2 * devices * cap * total * share,
        2 * (2 * total * width + devices * cap * share),
        down_near[:1],
    )(most.reshape(1), target.reshape(1, total), label, flat)
    arrived = exchange(outgoing)

    most = jnp.max(arrived[:, 0, whole + LANES // QUAD + 1].astype(jnp.float32)).reshape(1, 1)
    most = jnp.maximum(most, swapped(most))[0, 0].astype(i32)
    later_cap = total * 3 // 16
    later_outgoing = call(
        functools.partial(next_pack_kernel, whole, later_cap, cap),
        jax.ShapeDtypeStruct((devices, later_cap, share), bf16),
        [VMEM, VMEM, VMEM],
        2 * devices * later_cap * total * share,
        2 * (total * width + devices * later_cap * share),
    )(target.reshape(1, total), label, normed)
    later_arrived = exchange(behind(later_outgoing, arrived, *down_far))

    arrived = arrived.reshape(devices * cap, share)
    later_arrived = later_arrived.reshape(devices * later_cap, share)
    up_weights = [*up_near, *up_far, *[swapped(value) for value in up_far]]
    partial = down_call(first, arrived, down_weights, [])
    leaving = up_call(first, arrived, quad_sums(partial, devices), up_weights, devices)
    later_partial = down_call(first, later_arrived, down_weights, [])
    later_sums = quad_sums(later_partial, devices)
    caps = [total * 5 // 16, total * 6 // 16, total * 7 // 16]
    return lax.switch(
        sum((most > more).astype(i32) for more in caps),
        [functools.partial(back_and_mix, more) for more in caps] + [start_again],
        tokens,
        target,
        first,
        later_arrived,
        leaving,
        later_sums,
        up_weights,
        request_block_adapter,
        request_block_rows,
        adapter_down_weight,
        adapter_up_weight,
    )


def solution(mesh):
    placed = (
        P(("groups", "adapter"), None, None),
        P(("groups", "adapter")),
        P(("groups", "adapter")),
        P("adapter", None, None),
        P("adapter", None, None),
    )

    def per_device(tokens, request_block_adapter, request_block_rows, down_weight, up_weight):
        blocks, rows, width = tokens.shape
        devices = mesh.shape["adapter"]
        slots = max(1, 4 * blocks // devices)
        quads = devices % QUAD == 0 and slots * QUAD >= blocks
        quads = quads and width % (QUAD * LANES) == LANES and up_weight.shape[1] == HALF
        plan = rows_to_quads if quads else rows_to_holders
        return plan(tokens, request_block_adapter, request_block_rows, down_weight, up_weight)

    return jax.shard_map(
        per_device,
        mesh=mesh,
        in_specs=placed,
        out_specs=P(("groups", "adapter"), None, None),
        check_vma=False,
    )
```

```python
import functools
import math

import jax
import jax.numpy as jnp
from jax import lax
from jax.experimental import pallas as pl
from jax.experimental.pallas import tpu as pltpu
from jax.sharding import PartitionSpec as P

LANES = 128
HALF = 64
QUAD = 4
CHUNK = 512
VMEM = pl.BlockSpec(memory_space=pltpu.VMEM)
SMEM = pl.BlockSpec(memory_space=pltpu.SMEM)


def normalise(tokens):
    values = tokens.astype(jnp.float32)
    mean_sq = jnp.mean(values * values, axis=-1, keepdims=True)
    return (values, (values * lax.rsqrt(mean_sq + 1e-06)).astype(jnp.bfloat16))


def resident_update(hidden_state, block_labels, adapter_down_weight, adapter_up_weight):
    feature_width = hidden_state.shape[-1]
    leading = hidden_state.shape[:-1]
    resident_rows, unused_value, inner_rank = adapter_down_weight.shape
    flattened_tokens = hidden_state.reshape(-1, feature_width)
    down_matrix = jnp.einsum(
        "tq,iqg->tig", flattened_tokens, adapter_down_weight, preferred_element_type=jnp.float32
    )
    down_matrix = down_matrix.astype(jnp.bfloat16).reshape(
        flattened_tokens.shape[0], resident_rows * inner_rank
    )
    column_owner = jnp.arange(resident_rows * inner_rank, dtype=jnp.int32) // inner_rank
    picked = block_labels.reshape(-1, 1) == column_owner[None, :]
    down_matrix = jnp.where(picked, down_matrix, jnp.zeros_like(down_matrix))
    lowrank_update = jnp.dot(
        down_matrix,
        adapter_up_weight.reshape(resident_rows * inner_rank, feature_width),
        preferred_element_type=jnp.float32,
    )
    return lowrank_update.astype(jnp.bfloat16).reshape(leading + (feature_width,))


def rows_to_holders(
    tokens, request_block_adapter, request_block_rows, adapter_down_weight, adapter_up_weight
):
    blocks, rows, feature_width = tokens.shape
    devices = lax.axis_size("adapter")
    resident_rows = adapter_down_weight.shape[0]
    slots = max(1, 4 * blocks // devices)
    values, normed = normalise(tokens)
    owner = request_block_adapter // resident_rows
    within = request_block_adapter - owner * resident_rows
    serial = jnp.arange(blocks, dtype=jnp.int32)
    earlier = (owner[:, None] == owner[None, :]) & (serial[None, :] < serial[:, None])
    position = owner * slots + jnp.sum(earlier, axis=1)
    outgoing = (
        jnp.zeros((devices * slots, rows, feature_width), jnp.bfloat16).at[position].set(normed)
    )
    outgoing = outgoing.reshape(devices, slots, rows, feature_width)
    block_labels = jnp.full((devices * slots,), -1, jnp.int32).at[position].set(within)
    block_labels = jnp.broadcast_to(block_labels[:, None], (devices * slots, rows)).reshape(
        devices, slots, rows
    )
    arriving_rows, row_markers = (
        lax.all_to_all(outgoing, "adapter", split_axis=0, concat_axis=0, tiled=True),
        lax.all_to_all(block_labels, "adapter", split_axis=0, concat_axis=0, tiled=True),
    )
    lowrank_update = resident_update(
        arriving_rows, row_markers, adapter_down_weight, adapter_up_weight
    )
    returned = lax.all_to_all(lowrank_update, "adapter", split_axis=0, concat_axis=0, tiled=True)
    mine = returned.reshape(devices * slots, rows, feature_width)[position]
    live = jnp.arange(rows, dtype=jnp.int32)[None, :] < request_block_rows[:, None]
    mixed = values + jnp.where(live[:, :, None], mine.astype(jnp.float32), jnp.float32(0.0))
    return mixed.astype(jnp.bfloat16)


def lanes_of(rows):
    return lax.broadcasted_iota(jnp.int32, (rows, LANES), 1)


def weight_kernel(whole, part_ref, group_ref, weight_ref, *out_refs):
    quarter = LANES // QUAD
    inside = lanes_of(weight_ref.shape[0]) < quarter
    for k, out_ref in enumerate(out_refs):
        j = part_ref[k]
        count = out_ref.shape[0]
        start = 0 if k < 2 else pl.multiple_of(group_ref[0] * count, count)
        rows = pl.ds(start, count)
        out_ref[:, 0:whole] = weight_ref[rows, pl.ds(pl.multiple_of(j * whole, LANES), whole)]
        last = weight_ref[rows, QUAD * whole :].astype(jnp.float32)
        turned = pltpu.roll(last, lax.rem(LANES - quarter * j, LANES), 1)
        out_ref[:, whole:] = jnp.where(inside[0:count], turned, 0.0).astype(jnp.bfloat16)


def pack_rows(whole, cap, base, most, target_ref, label_ref, rows_ref, out_ref):
    total = rows_ref.shape[0]
    quads = out_ref.shape[0] // QUAD
    quarter = LANES // QUAD
    lane = lanes_of(total)
    last = rows_ref[:, QUAD * whole :].astype(jnp.float32)
    label = jnp.where(lane == quarter, label_ref[...], 0.0)
    ends = []
    for j in range(QUAD):
        turned = pltpu.roll(last, (LANES - quarter * j) % LANES, 1) if j else last
        ends.append(jnp.where(lane < quarter, turned, label).astype(jnp.bfloat16))
    note = jnp.where(lanes_of(cap) == quarter + 1, most, 0.0)
    for q in range(quads):
        place = lax.broadcasted_iota(jnp.int32, (cap, total), 0) + (q * total + base)
        chosen = jnp.where(target_ref[...] == place, 1.0, 0.0).astype(jnp.bfloat16)
        for j in range(QUAD):
            columns = slice(j * whole, (j + 1) * whole)
            out_ref[q * QUAD + j, :, 0:whole] = jnp.dot(
                chosen, rows_ref[:, columns], preferred_element_type=jnp.float32
            ).astype(jnp.bfloat16)
            end = jnp.dot(chosen, ends[j], preferred_element_type=jnp.float32)
            out_ref[q * QUAD + j, :, whole:] = (end + note).astype(jnp.bfloat16)


def first_pack_kernel(
    whole, cap, most_ref, target_ref, label_ref, tokens_ref, normed_ref, out_ref
):
    values = tokens_ref[...].astype(jnp.float32)
    mean_sq = jnp.mean(values * values, axis=-1, keepdims=True)
    normed_ref[...] = (values * lax.rsqrt(mean_sq + 1e-06)).astype(jnp.bfloat16)
    most = most_ref[0].astype(jnp.float32)
    pack_rows(whole, cap, 0, most, target_ref, label_ref, normed_ref, out_ref)


def next_pack_kernel(whole, cap, base, target_ref, label_ref, normed_ref, out_ref):
    pack_rows(whole, cap, base, 0.0, target_ref, label_ref, normed_ref, out_ref)


def label_of(last_tile):
    rows = last_tile.shape[0]
    quarter = LANES // QUAD
    label = last_tile[:, quarter : quarter + 1].astype(jnp.float32) - 1.0
    return label - jnp.where(lanes_of(rows) < HALF, 0.0, 1.0)


def down_kernel(chunk, first_ref, rows_ref, *refs):
    weight_refs, out_ref = refs[:-1], refs[-1]
    width = rows_ref.shape[1]
    dims = (((1,), (1,)), ((), ()))
    low = lanes_of(chunk // 2) < HALF

    def one(c, carry):
        at = pl.ds(pl.multiple_of(c * chunk, chunk), chunk)
        label = label_of(rows_ref[at, width - LANES :])
        picked = jnp.zeros((chunk, LANES), jnp.float32)
        for k, weight_ref in enumerate(weight_refs):
            product = lax.dot_general(
                rows_ref[at, :], weight_ref[...], dims, preferred_element_type=jnp.float32
            )
            first = first_ref[k].astype(jnp.float32)
            for t in range(weight_ref.shape[0] // LANES):
                columns = slice(t * LANES, (t + 1) * LANES)
                picked = jnp.where(label == first + 2.0 * t, product[:, columns], picked)
        picked = picked + pltpu.roll(picked, HALF, 1)
        half = pl.ds(pl.multiple_of(c * (chunk // 2), chunk // 2), chunk // 2)
        out_ref[half, :] = jnp.where(
            low, picked[0 : chunk // 2], picked[chunk // 2 : chunk]
        ).astype(jnp.bfloat16)
        return carry

    lax.fori_loop(0, rows_ref.shape[0] // chunk, one, 0)


def up_kernel(chunk, first_ref, ends_ref, *refs):
    sum_refs, weight_refs, out_ref = refs[:QUAD], refs[QUAD:-1], refs[-1]
    width = ends_ref.shape[1]
    low = lanes_of(chunk // 2) < HALF

    def one(c, carry):
        at = pl.ds(pl.multiple_of(c * chunk, chunk), chunk)
        half = pl.ds(pl.multiple_of(c * (chunk // 2), chunk // 2), chunk // 2)
        label = label_of(ends_ref[at, width - LANES :])
        down = sum_refs[0][half, :].astype(jnp.float32)
        for ref in sum_refs[1:]:
            down = down + ref[half, :].astype(jnp.float32)
        down = down.astype(jnp.bfloat16).astype(jnp.float32)
        turned = pltpu.roll(down, HALF, 1)
        twice = jnp.concatenate(
            [jnp.where(low, down, turned), jnp.where(low, turned, down)], axis=0
        )
        delta = jnp.zeros((chunk, out_ref.shape[1]), jnp.float32)
        for k, weight_ref in enumerate(weight_refs):
            first = first_ref[k].astype(jnp.float32)
            placed = [
                jnp.where(label == first + 2.0 * t, twice, 0.0)
                for t in range(weight_ref.shape[0] // LANES)
            ]
            placed = jnp.concatenate(placed, axis=1).astype(jnp.bfloat16)
            delta = delta + jnp.dot(placed, weight_ref[...], preferred_element_type=jnp.float32)
        out_ref[at, :] = delta.astype(jnp.bfloat16)
        return carry

    lax.fori_loop(0, ends_ref.shape[0] // chunk, one, 0)


def last_up_kernel(chunk, blocks_of, first_ref, ends_ref, earlier_ref, *refs):
    out_ref, delta_ref = refs[-2:]
    up_kernel(chunk, first_ref, ends_ref, *refs[:-2], delta_ref)
    devices, earlier, later = blocks_of
    kept = out_ref.shape[1] - earlier

    def one(s, carry):
        out_ref[s, 0:earlier, :] = earlier_ref[s]
        start = pl.multiple_of(s * later, later)
        out_ref[s, earlier:, :] = delta_ref[pl.ds(start, kept), :]
        return carry

    lax.fori_loop(0, devices, one, 0)


def mix_kernel(whole, target_ref, tokens_ref, returned_ref, out_ref):
    total = tokens_ref.shape[0]
    quads, cap = returned_ref.shape[0] // QUAD, returned_ref.shape[1]
    quarter = LANES // QUAD
    lane = lanes_of(total)
    spot = lax.broadcasted_iota(jnp.int32, (total, quads * cap), 1)
    place = spot // cap * total + spot % cap
    chosen = jnp.where(target_ref[...] == place, 1.0, 0.0).astype(jnp.bfloat16)
    end = jnp.zeros((total, LANES), jnp.float32)
    for j in range(QUAD):
        share = jnp.concatenate([returned_ref[q * QUAD + j] for q in range(quads)], axis=0)
        delta = jnp.dot(chosen, share, preferred_element_type=jnp.float32)
        columns = slice(j * whole, (j + 1) * whole)
        out_ref[:, columns] = (
            tokens_ref[:, columns].astype(jnp.float32) + delta[:, 0:whole]
        ).astype(jnp.bfloat16)
        last = delta[:, whole:]
        turned = pltpu.roll(last, quarter * j, 1) if j else last
        end = jnp.where((lane >= quarter * j) & (lane < quarter * (j + 1)), turned, end)
    out_ref[:, QUAD * whole :] = (
        tokens_ref[:, QUAD * whole :].astype(jnp.float32) + end
    ).astype(jnp.bfloat16)


def call(kernel, out_shape, in_specs, flops, moved, after=(), scratch=()):
    many = isinstance(out_shape, list)
    skipped = len(after)
    body = (lambda *refs: kernel(*refs[skipped:])) if skipped else kernel
    run = pl.pallas_call(
        body,
        out_shape=out_shape,
        in_specs=[pl.BlockSpec(memory_space=pl.ANY)] * skipped + in_specs,
        out_specs=[VMEM] * len(out_shape) if many else VMEM,
        scratch_shapes=scratch,
        compiler_params=pltpu.CompilerParams(vmem_limit_bytes=48 * 2**20),
        cost_estimate=pl.CostEstimate(flops=flops, bytes_accessed=moved, transcendentals=0),
    )
    return functools.partial(run, *after)


def exchange(value):
    return lax.all_to_all(value, "adapter", split_axis=0, concat_axis=0, tiled=True)


def towards(value, k, devices):
    return lax.ppermute(value, "adapter", [(i, i ^ k) for i in range(devices)])


def swapped(value):
    return lax.ppermute(value, "groups", [(0, 1), (1, 0)])


def down_call(first, arrived, weights, after):
    arriving, share = arrived.shape
    columns = sum(weight.shape[0] for weight in weights)
    chunk = math.gcd(arriving, CHUNK)
    return call(
        functools.partial(down_kernel, chunk),
        jax.ShapeDtypeStruct((arriving // 2, LANES), jnp.bfloat16),
        [SMEM] + [VMEM] * (1 + len(weights)),
        2 * arriving * columns * share,
        2 * (arriving + columns) * share,
        after,
    )(first, arrived, *weights)


def quad_sums(partial, devices):
    return [partial] + [towards(partial, k, devices) for k in range(1, QUAD)]


def up_call(first, arrived, sums, weights, devices):
    arriving, share = arrived.shape
    columns = sum(weight.shape[0] for weight in weights)
    chunk = math.gcd(arriving, CHUNK)
    leaving = call(
        functools.partial(up_kernel, chunk),
        jax.ShapeDtypeStruct((arriving, share), jnp.bfloat16),
        [SMEM] + [VMEM] * (1 + QUAD + len(weights)),
        2 * arriving * columns * share,
        2 * (2 * arriving + columns) * share,
    )(first, arrived, *sums, *weights)
    return leaving.reshape(devices, arriving // devices, share)


def back_and_mix(
    kept, tokens, target, first, later_arrived, leaving, later_sums, up_weights, *unused_values
):
    blocks, rows, width = tokens.shape
    total = blocks * rows
    devices, cap, share = leaving.shape
    whole = share - LANES
    arriving = later_arrived.shape[0]
    columns = sum(weight.shape[0] for weight in up_weights)
    everything = call(
        functools.partial(
            last_up_kernel, math.gcd(arriving, CHUNK), (devices, cap, arriving // devices)
        ),
        jax.ShapeDtypeStruct((devices, kept, share), jnp.bfloat16),
        [SMEM] + [VMEM] * (2 + QUAD + len(up_weights)),
        2 * arriving * columns * share,
        2 * (2 * devices * kept + columns) * share,
        (),
        [pltpu.VMEM((arriving, share), jnp.bfloat16)],
    )(first, later_arrived, leaving, *later_sums, *up_weights)
    mixed = call(
        functools.partial(mix_kernel, whole),
        jax.ShapeDtypeStruct((total, width), jnp.bfloat16),
        [VMEM] * 3,
        2 * devices * kept * total * share,
        2 * (2 * total * width + devices * kept * share),
    )(target.reshape(total, 1), tokens.reshape(total, width), exchange(everything))
    return mixed.reshape(tokens.shape)


def start_again(
    tokens, target, first, later_arrived, leaving, later_sums, up_weights, *arguments
):
    return rows_to_holders(tokens, *arguments)


def rows_to_quads(
    tokens, request_block_adapter, request_block_rows, adapter_down_weight, adapter_up_weight
):
    blocks, rows, width = tokens.shape
    devices = lax.axis_size("adapter")
    resident, rank, unused_width = adapter_up_weight.shape
    total = blocks * rows
    columns = resident * rank
    whole = width // LANES // QUAD * LANES
    share = whole + LANES
    bf16, i32 = jnp.bfloat16, jnp.int32

    quad = request_block_adapter // (resident * QUAD)
    label = request_block_adapter - quad * (resident * QUAD) + 1
    serial = jnp.arange(blocks, dtype=i32)
    same = quad[:, None] == quad[None, :]
    used = request_block_rows
    ahead = jnp.where(same & (serial[None, :] < serial[:, None]), used[None, :], 0)
    most = jnp.max(jnp.sum(jnp.where(same, used[None, :], 0), axis=1))
    row = jnp.arange(rows, dtype=i32)
    start = quad * total + jnp.sum(ahead, axis=1)
    target = jnp.where(row[None, :] < used[:, None], start[:, None] + row[None, :], -1)
    target = target.reshape(total).astype(i32)
    label = jnp.broadcast_to(label[:, None], (blocks, rows)).reshape(total, 1).astype(jnp.float32)

    me = lax.axis_index("adapter").astype(i32)
    group = lax.axis_index("groups").astype(i32)
    parts = jnp.bitwise_xor(me % QUAD, jnp.arange(QUAD, dtype=i32))
    own_half, twin_half = group * (resident // 2), (1 - group) * (resident // 2)
    first = jnp.concatenate(
        [parts * resident + jnp.stack([0 * group, 0 * group, own_half, own_half])]
        + [parts[2:] * resident + twin_half]
    ).astype(i32)

    def dealt(weight, after=()):
        counts = [columns, columns, columns // 2, columns // 2]
        values = call(
            functools.partial(weight_kernel, whole),
            [jax.ShapeDtypeStruct((count, share), bf16) for count in counts],
            [SMEM, SMEM, VMEM],
            0,
            4 * columns * width,
            after,
        )(parts, group.reshape(1), weight)
        near = [values[0], towards(values[1], 1, devices)]
        return near, [towards(values[k], k, devices) for k in range(2, QUAD)]

    down_near, down_far = dealt(adapter_down_weight.transpose(0, 2, 1).reshape(columns, width))
    up_near, up_far = dealt(adapter_up_weight.reshape(columns, width), down_far[:1])
    down_weights = [*down_near, *down_far, *[swapped(value) for value in down_far]]

    cap = total // QUAD
    flat = tokens.reshape(total, width)
    normed, outgoing = call(
        functools.partial(first_pack_kernel, whole, cap),
        [
            jax.ShapeDtypeStruct((total, width), bf16),
            jax.ShapeDtypeStruct((devices, cap, share), bf16),
        ],
        [SMEM, VMEM, VMEM, VMEM],
        2 * devices * cap * total * share,
        2 * (2 * total * width + devices * cap * share),
        down_near[:1],
    )(most.reshape(1), target.reshape(1, total), label, flat)
    arrived = exchange(outgoing)

    most = jnp.max(arrived[:, 0, whole + LANES // QUAD + 1].astype(jnp.float32)).reshape(1, 1)
    most = jnp.maximum(most, swapped(most))[0, 0].astype(i32)
    later_cap = total * 3 // 16
    later_outgoing = call(
        functools.partial(next_pack_kernel, whole, later_cap, cap),
        jax.ShapeDtypeStruct((devices, later_cap, share), bf16),
        [VMEM, VMEM, VMEM],
        2 * devices * later_cap * total * share,
        2 * (total * width + devices * later_cap * share),
        [arrived, up_near[0]],
    )(target.reshape(1, total), label, normed)
    later_arrived = exchange(later_outgoing)

    arrived = arrived.reshape(devices * cap, share)
    later_arrived = later_arrived.reshape(devices * later_cap, share)
    up_weights = [*up_near, *up_far, *[swapped(value) for value in up_far]]
    partial = down_call(first, arrived, down_weights, [])
    leaving = up_call(first, arrived, quad_sums(partial, devices), up_weights, devices)
    later_partial = down_call(first, later_arrived, down_weights, [])
    later_sums = quad_sums(later_partial, devices)
    caps = [total * 5 // 16, total * 6 // 16, total * 7 // 16]
    return lax.switch(
        sum((most > more).astype(i32) for more in caps),
        [functools.partial(back_and_mix, more) for more in caps] + [start_again],
        tokens,
        target,
        first,
        later_arrived,
        leaving,
        later_sums,
        up_weights,
        request_block_adapter,
        request_block_rows,
        adapter_down_weight,
        adapter_up_weight,
    )


def solution(mesh):
    placed = (
        P(("groups", "adapter"), None, None),
        P(("groups", "adapter")),
        P(("groups", "adapter")),
        P("adapter", None, None),
        P("adapter", None, None),
    )

    def per_device(tokens, request_block_adapter, request_block_rows, down_weight, up_weight):
        blocks, rows, width = tokens.shape
        devices = mesh.shape["adapter"]
        slots = max(1, 4 * blocks // devices)
        quads = devices % QUAD == 0 and slots * QUAD >= blocks
        quads = quads and width % (QUAD * LANES) == LANES and up_weight.shape[1] == HALF
        plan = rows_to_quads if quads else rows_to_holders
        return plan(tokens, request_block_adapter, request_block_rows, down_weight, up_weight)

    return jax.shard_map(
        per_device,
        mesh=mesh,
        in_specs=placed,
        out_specs=P(("groups", "adapter"), None, None),
        check_vma=False,
    )
```

```python
import functools

import jax
import jax.numpy as jnp
from jax import lax
from jax.experimental import pallas as pl
from jax.experimental.pallas import tpu as pltpu
from jax.sharding import PartitionSpec as P

LANES = 128
HALF = 64
QUAD = 4
VMEM = pl.BlockSpec(memory_space=pltpu.VMEM)
SMEM = pl.BlockSpec(memory_space=pltpu.SMEM)


def normalise(tokens):
    values = tokens.astype(jnp.float32)
    mean_sq = jnp.mean(values * values, axis=-1, keepdims=True)
    return (values, (values * lax.rsqrt(mean_sq + 1e-06)).astype(jnp.bfloat16))


def resident_update(hidden_state, block_labels, adapter_down_weight, adapter_up_weight):
    feature_width = hidden_state.shape[-1]
    leading = hidden_state.shape[:-1]
    resident_rows, unused_value, inner_rank = adapter_down_weight.shape
    flattened_tokens = hidden_state.reshape(-1, feature_width)
    down_matrix = jnp.einsum(
        "tq,iqg->tig", flattened_tokens, adapter_down_weight, preferred_element_type=jnp.float32
    )
    down_matrix = down_matrix.astype(jnp.bfloat16).reshape(
        flattened_tokens.shape[0], resident_rows * inner_rank
    )
    column_owner = jnp.arange(resident_rows * inner_rank, dtype=jnp.int32) // inner_rank
    picked = block_labels.reshape(-1, 1) == column_owner[None, :]
    down_matrix = jnp.where(picked, down_matrix, jnp.zeros_like(down_matrix))
    lowrank_update = jnp.dot(
        down_matrix,
        adapter_up_weight.reshape(resident_rows * inner_rank, feature_width),
        preferred_element_type=jnp.float32,
    )
    return lowrank_update.astype(jnp.bfloat16).reshape(leading + (feature_width,))


def rows_to_holders(
    tokens, request_block_adapter, request_block_rows, adapter_down_weight, adapter_up_weight
):
    blocks, rows, feature_width = tokens.shape
    devices = lax.axis_size("adapter")
    resident_rows = adapter_down_weight.shape[0]
    slots = max(1, 4 * blocks // devices)
    values, normed = normalise(tokens)
    owner = request_block_adapter // resident_rows
    within = request_block_adapter - owner * resident_rows
    serial = jnp.arange(blocks, dtype=jnp.int32)
    earlier = (owner[:, None] == owner[None, :]) & (serial[None, :] < serial[:, None])
    position = owner * slots + jnp.sum(earlier, axis=1)
    outgoing = (
        jnp.zeros((devices * slots, rows, feature_width), jnp.bfloat16).at[position].set(normed)
    )
    outgoing = outgoing.reshape(devices, slots, rows, feature_width)
    block_labels = jnp.full((devices * slots,), -1, jnp.int32).at[position].set(within)
    block_labels = jnp.broadcast_to(block_labels[:, None], (devices * slots, rows)).reshape(
        devices, slots, rows
    )
    arriving_rows, row_markers = (
        lax.all_to_all(outgoing, "adapter", split_axis=0, concat_axis=0, tiled=True),
        lax.all_to_all(block_labels, "adapter", split_axis=0, concat_axis=0, tiled=True),
    )
    lowrank_update = resident_update(
        arriving_rows, row_markers, adapter_down_weight, adapter_up_weight
    )
    returned = lax.all_to_all(lowrank_update, "adapter", split_axis=0, concat_axis=0, tiled=True)
    mine = returned.reshape(devices * slots, rows, feature_width)[position]
    live = jnp.arange(rows, dtype=jnp.int32)[None, :] < request_block_rows[:, None]
    mixed = values + jnp.where(live[:, :, None], mine.astype(jnp.float32), jnp.float32(0.0))
    return mixed.astype(jnp.bfloat16)


def lanes_of(rows):
    return lax.broadcasted_iota(jnp.int32, (rows, LANES), 1)


def weight_kernel(whole, part_ref, group_ref, weight_ref, *out_refs):
    quarter = LANES // QUAD
    inside = lanes_of(weight_ref.shape[0]) < quarter
    for k, out_ref in enumerate(out_refs):
        j = part_ref[k]
        count = out_ref.shape[0]
        start = 0 if k < 2 else pl.multiple_of(group_ref[0] * count, count)
        rows = pl.ds(start, count)
        out_ref[:, 0:whole] = weight_ref[rows, pl.ds(pl.multiple_of(j * whole, LANES), whole)]
        last = weight_ref[rows, QUAD * whole :].astype(jnp.float32)
        turned = pltpu.roll(last, lax.rem(LANES - quarter * j, LANES), 1)
        out_ref[:, whole:] = jnp.where(inside[0:count], turned, 0.0).astype(jnp.bfloat16)


def pack_kernel(whole, most_ref, target_ref, label_ref, tokens_ref, out_ref, normed_ref):
    values = tokens_ref[...].astype(jnp.float32)
    mean_sq = jnp.mean(values * values, axis=-1, keepdims=True)
    normed_ref[...] = (values * lax.rsqrt(mean_sq + 1e-06)).astype(jnp.bfloat16)
    total = tokens_ref.shape[0]
    quads, cap = out_ref.shape[0] // QUAD, out_ref.shape[1]
    quarter = LANES // QUAD
    lane = lanes_of(total)
    last = normed_ref[:, QUAD * whole :].astype(jnp.float32)
    label = jnp.where(lane == quarter, label_ref[...], 0.0)
    ends = []
    for j in range(QUAD):
        turned = pltpu.roll(last, (LANES - quarter * j) % LANES, 1) if j else last
        ends.append(jnp.where(lane < quarter, turned, label).astype(jnp.bfloat16))
    most = most_ref[0].astype(jnp.float32)
    note = jnp.where(lanes_of(cap) == quarter + 1, most, 0.0)
    for q in range(quads):
        place = lax.broadcasted_iota(jnp.int32, (cap, total), 0) + q * total
        chosen = jnp.where(target_ref[...] == place, 1.0, 0.0).astype(jnp.bfloat16)
        for j in range(QUAD):
            columns = slice(j * whole, (j + 1) * whole)
            out_ref[q * QUAD + j, :, 0:whole] = jnp.dot(
                chosen, normed_ref[:, columns], preferred_element_type=jnp.float32
            ).astype(jnp.bfloat16)
            end = jnp.dot(chosen, ends[j], preferred_element_type=jnp.float32)
            out_ref[q * QUAD + j, :, whole:] = (end + note).astype(jnp.bfloat16)


def label_of(last_tile):
    rows = last_tile.shape[0]
    quarter = LANES // QUAD
    label = last_tile[:, quarter : quarter + 1].astype(jnp.float32) - 1.0
    return label - jnp.where(lanes_of(rows) < HALF, 0.0, 1.0)


def down_kernel(first_ref, rows_ref, *refs):
    weight_refs, out_ref = refs[:-1], refs[-1]
    senders, cap, width = rows_ref.shape
    dims = (((1,), (1,)), ((), ()))
    low = lanes_of(2 * cap) < HALF

    def one(c, carry):
        rows = jnp.concatenate([rows_ref[4 * c + i] for i in range(4)], axis=0)
        label = label_of(rows[:, width - LANES :])
        picked = jnp.zeros((4 * cap, LANES), jnp.float32)
        for k, weight_ref in enumerate(weight_refs):
            product = lax.dot_general(
                rows, weight_ref[...], dims, preferred_element_type=jnp.float32
            )
            first = first_ref[k].astype(jnp.float32)
            for t in range(weight_ref.shape[0] // LANES):
                columns = slice(t * LANES, (t + 1) * LANES)
                picked = jnp.where(label == first + 2.0 * t, product[:, columns], picked)
        picked = picked + pltpu.roll(picked, HALF, 1)
        out_ref[c] = jnp.where(low, picked[0 : 2 * cap], picked[2 * cap :]).astype(jnp.bfloat16)
        return carry

    lax.fori_loop(0, senders // 4, one, 0)


def up_kernel(first_ref, rows_ref, *refs):
    sum_refs, weight_refs, out_ref = refs[:QUAD], refs[QUAD:-1], refs[-1]
    senders, cap, width = rows_ref.shape
    kept = out_ref.shape[1]
    low = lanes_of(2 * cap) < HALF

    def one(c, carry):
        down = sum_refs[0][c].astype(jnp.float32)
        for ref in sum_refs[1:]:
            down = down + ref[c].astype(jnp.float32)
        down = down.astype(jnp.bfloat16).astype(jnp.float32)
        turned = pltpu.roll(down, HALF, 1)
        pairs = [jnp.where(low, down, turned), jnp.where(low, turned, down)]
        twice = jnp.concatenate(
            [pairs[i // 2][i % 2 * cap : i % 2 * cap + kept] for i in range(4)], axis=0
        )
        ends = [rows_ref[4 * c + i, 0:kept, width - LANES :] for i in range(4)]
        label = label_of(jnp.concatenate(ends, axis=0))
        delta = jnp.zeros((4 * kept, width), jnp.float32)
        for k, weight_ref in enumerate(weight_refs):
            first = first_ref[k].astype(jnp.float32)
            placed = [
                jnp.where(label == first + 2.0 * t, twice, 0.0)
                for t in range(weight_ref.shape[0] // LANES)
            ]
            placed = jnp.concatenate(placed, axis=1).astype(jnp.bfloat16)
            delta = delta + jnp.dot(placed, weight_ref[...], preferred_element_type=jnp.float32)
        for i in range(4):
            out_ref[4 * c + i] = delta[i * kept : (i + 1) * kept].astype(jnp.bfloat16)
        return carry

    lax.fori_loop(0, senders // 4, one, 0)


def mix_kernel(whole, target_ref, tokens_ref, returned_ref, out_ref):
    total = tokens_ref.shape[0]
    quads, cap = returned_ref.shape[0] // QUAD, returned_ref.shape[1]
    quarter = LANES // QUAD
    lane = lanes_of(total)
    spot = lax.broadcasted_iota(jnp.int32, (total, quads * cap), 1)
    place = spot // cap * total + spot % cap
    chosen = jnp.where(target_ref[...] == place, 1.0, 0.0).astype(jnp.bfloat16)
    end = jnp.zeros((total, LANES), jnp.float32)
    for j in range(QUAD):
        share = jnp.concatenate([returned_ref[q * QUAD + j] for q in range(quads)], axis=0)
        delta = jnp.dot(chosen, share, preferred_element_type=jnp.float32)
        columns = slice(j * whole, (j + 1) * whole)
        out_ref[:, columns] = (
            tokens_ref[:, columns].astype(jnp.float32) + delta[:, 0:whole]
        ).astype(jnp.bfloat16)
        last = delta[:, whole:]
        turned = pltpu.roll(last, quarter * j, 1) if j else last
        end = jnp.where((lane >= quarter * j) & (lane < quarter * (j + 1)), turned, end)
    out_ref[:, QUAD * whole :] = (
        tokens_ref[:, QUAD * whole :].astype(jnp.float32) + end
    ).astype(jnp.bfloat16)


def call(kernel, out_shape, in_specs, flops, moved, after=(), scratch=()):
    many = isinstance(out_shape, list)
    skipped = len(after)
    body = (lambda *refs: kernel(*refs[skipped:])) if skipped else kernel
    run = pl.pallas_call(
        body,
        out_shape=out_shape,
        in_specs=[pl.BlockSpec(memory_space=pl.ANY)] * skipped + in_specs,
        out_specs=[VMEM] * len(out_shape) if many else VMEM,
        scratch_shapes=scratch,
        compiler_params=pltpu.CompilerParams(vmem_limit_bytes=48 * 2**20),
        cost_estimate=pl.CostEstimate(flops=flops, bytes_accessed=moved, transcendentals=0),
    )
    return functools.partial(run, *after)


def exchange(value):
    return lax.all_to_all(value, "adapter", split_axis=0, concat_axis=0, tiled=True)


def towards(value, k, devices):
    return lax.ppermute(value, "adapter", [(i, i ^ k) for i in range(devices)])


def swapped(value):
    return lax.ppermute(value, "groups", [(0, 1), (1, 0)])


def back_and_mix(
    kept, tokens, target, first, arrived, sums, up_weights, *unused_values
):
    blocks, rows, width = tokens.shape
    total = blocks * rows
    devices, cap, share = arrived.shape
    columns = sum(weight.shape[0] for weight in up_weights)
    leaving = call(
        up_kernel,
        jax.ShapeDtypeStruct((devices, kept, share), jnp.bfloat16),
        [SMEM] + [VMEM] * (1 + QUAD + len(up_weights)),
        2 * devices * kept * columns * share,
        2 * (2 * devices * kept + columns) * share,
    )(first, arrived, *sums, *up_weights)
    mixed = call(
        functools.partial(mix_kernel, share - LANES),
        jax.ShapeDtypeStruct((total, width), jnp.bfloat16),
        [VMEM] * 3,
        2 * devices * kept * total * share,
        2 * (2 * total * width + devices * kept * share),
    )(target.reshape(total, 1), tokens.reshape(total, width), exchange(leaving))
    return mixed.reshape(tokens.shape)


def start_again(tokens, target, first, arrived, sums, up_weights, *arguments):
    return rows_to_holders(tokens, *arguments)


def rows_to_quads(
    tokens, request_block_adapter, request_block_rows, adapter_down_weight, adapter_up_weight
):
    blocks, rows, width = tokens.shape
    devices = lax.axis_size("adapter")
    resident, rank, unused_width = adapter_up_weight.shape
    total = blocks * rows
    columns = resident * rank
    whole = width // LANES // QUAD * LANES
    share = whole + LANES
    bf16, i32 = jnp.bfloat16, jnp.int32

    quad = request_block_adapter // (resident * QUAD)
    label = request_block_adapter - quad * (resident * QUAD) + 1
    serial = jnp.arange(blocks, dtype=i32)
    same = quad[:, None] == quad[None, :]
    used = request_block_rows
    ahead = jnp.where(same & (serial[None, :] < serial[:, None]), used[None, :], 0)
    most = jnp.max(jnp.sum(jnp.where(same, used[None, :], 0), axis=1))
    row = jnp.arange(rows, dtype=i32)
    start = quad * total + jnp.sum(ahead, axis=1)
    target = jnp.where(row[None, :] < used[:, None], start[:, None] + row[None, :], -1)
    target = target.reshape(total).astype(i32)
    label = jnp.broadcast_to(label[:, None], (blocks, rows)).reshape(total, 1).astype(jnp.float32)

    me = lax.axis_index("adapter").astype(i32)
    group = lax.axis_index("groups").astype(i32)
    parts = jnp.bitwise_xor(me % QUAD, jnp.arange(QUAD, dtype=i32))
    own_half, twin_half = group * (resident // 2), (1 - group) * (resident // 2)
    first = jnp.concatenate(
        [parts * resident + jnp.stack([0 * group, 0 * group, own_half, own_half])]
        + [parts[2:] * resident + twin_half]
    ).astype(i32)

    def dealt(weight):
        counts = [columns, columns, columns // 2, columns // 2]
        values = call(
            functools.partial(weight_kernel, whole),
            [jax.ShapeDtypeStruct((count, share), bf16) for count in counts],
            [SMEM, SMEM, VMEM],
            0,
            4 * columns * width,
        )(parts, group.reshape(1), weight)
        near = [values[0], towards(values[1], 1, devices)]
        return near, [towards(values[k], k, devices) for k in range(2, QUAD)]

    down_near, down_far = dealt(adapter_down_weight.transpose(0, 2, 1).reshape(columns, width))
    up_near, up_far = dealt(adapter_up_weight.reshape(columns, width))
    down_weights = [*down_near, *down_far, *[swapped(value) for value in down_far]]
    up_weights = [*up_near, *up_far, *[swapped(value) for value in up_far]]

    caps = [total * 5 // 16, total * 6 // 16, total * 7 // 16]
    cap = caps[-1]
    arrived = exchange(
        call(
            functools.partial(pack_kernel, whole),
            jax.ShapeDtypeStruct((devices, cap, share), bf16),
            [SMEM, VMEM, VMEM, VMEM],
            2 * devices * cap * total * share,
            2 * (total * width + devices * cap * share),
            scratch=[pltpu.VMEM((total, width), bf16)],
        )(most.reshape(1), target.reshape(1, total), label, tokens.reshape(total, width))
    )

    most = jnp.max(arrived[:, 0, whole + LANES // QUAD + 1].astype(jnp.float32)).reshape(1, 1)
    most = jnp.maximum(most, swapped(most))[0, 0].astype(i32)
    partial = call(
        down_kernel,
        jax.ShapeDtypeStruct((devices // 4, 2 * cap, LANES), bf16),
        [SMEM] + [VMEM] * (1 + len(down_weights)),
        2 * devices * cap * 4 * columns * share,
        2 * (devices * cap + 4 * columns) * share,
        up_weights,
    )(first, arrived, *down_weights)
    sums = [partial] + [towards(partial, k, devices) for k in range(1, QUAD)]
    return lax.switch(
        sum((most > more).astype(i32) for more in caps),
        [functools.partial(back_and_mix, more) for more in caps] + [start_again],
        tokens,
        target,
        first,
        arrived,
        sums,
        up_weights,
        request_block_adapter,
        request_block_rows,
        adapter_down_weight,
        adapter_up_weight,
    )


def solution(mesh):
    placed = (
        P(("groups", "adapter"), None, None),
        P(("groups", "adapter")),
        P(("groups", "adapter")),
        P("adapter", None, None),
        P("adapter", None, None),
    )

    def per_device(tokens, request_block_adapter, request_block_rows, down_weight, up_weight):
        blocks, rows, width = tokens.shape
        devices = mesh.shape["adapter"]
        slots = max(1, 4 * blocks // devices)
        quads = devices % QUAD == 0 and slots * QUAD >= blocks
        quads = quads and width % (QUAD * LANES) == LANES and up_weight.shape[1] == HALF
        plan = rows_to_quads if quads else rows_to_holders
        return plan(tokens, request_block_adapter, request_block_rows, down_weight, up_weight)

    return jax.shard_map(
        per_device,
        mesh=mesh,
        in_specs=placed,
        out_specs=P(("groups", "adapter"), None, None),
        check_vma=False,
    )
```

```python
import functools

import jax
import jax.numpy as jnp
from jax import lax
from jax.experimental import pallas as pl
from jax.experimental.pallas import tpu as pltpu
from jax.sharding import PartitionSpec as P

LANES = 128
HALF = 64
QUAD = 4
VMEM = pl.BlockSpec(memory_space=pltpu.VMEM)
SMEM = pl.BlockSpec(memory_space=pltpu.SMEM)


def normalise(tokens):
    values = tokens.astype(jnp.float32)
    mean_sq = jnp.mean(values * values, axis=-1, keepdims=True)
    return (values, (values * lax.rsqrt(mean_sq + 1e-06)).astype(jnp.bfloat16))


def resident_update(hidden_state, block_labels, adapter_down_weight, adapter_up_weight):
    feature_width = hidden_state.shape[-1]
    leading = hidden_state.shape[:-1]
    resident_rows, unused_value, inner_rank = adapter_down_weight.shape
    flattened_tokens = hidden_state.reshape(-1, feature_width)
    down_matrix = jnp.einsum(
        "tq,iqg->tig", flattened_tokens, adapter_down_weight, preferred_element_type=jnp.float32
    )
    down_matrix = down_matrix.astype(jnp.bfloat16).reshape(
        flattened_tokens.shape[0], resident_rows * inner_rank
    )
    column_owner = jnp.arange(resident_rows * inner_rank, dtype=jnp.int32) // inner_rank
    picked = block_labels.reshape(-1, 1) == column_owner[None, :]
    down_matrix = jnp.where(picked, down_matrix, jnp.zeros_like(down_matrix))
    lowrank_update = jnp.dot(
        down_matrix,
        adapter_up_weight.reshape(resident_rows * inner_rank, feature_width),
        preferred_element_type=jnp.float32,
    )
    return lowrank_update.astype(jnp.bfloat16).reshape(leading + (feature_width,))


def rows_to_holders(
    tokens, request_block_adapter, request_block_rows, adapter_down_weight, adapter_up_weight
):
    blocks, rows, feature_width = tokens.shape
    devices = lax.axis_size("adapter")
    resident_rows = adapter_down_weight.shape[0]
    slots = max(1, 4 * blocks // devices)
    values, normed = normalise(tokens)
    owner = request_block_adapter // resident_rows
    within = request_block_adapter - owner * resident_rows
    serial = jnp.arange(blocks, dtype=jnp.int32)
    earlier = (owner[:, None] == owner[None, :]) & (serial[None, :] < serial[:, None])
    position = owner * slots + jnp.sum(earlier, axis=1)
    outgoing = (
        jnp.zeros((devices * slots, rows, feature_width), jnp.bfloat16).at[position].set(normed)
    )
    outgoing = outgoing.reshape(devices, slots, rows, feature_width)
    block_labels = jnp.full((devices * slots,), -1, jnp.int32).at[position].set(within)
    block_labels = jnp.broadcast_to(block_labels[:, None], (devices * slots, rows)).reshape(
        devices, slots, rows
    )
    arriving_rows, row_markers = (
        lax.all_to_all(outgoing, "adapter", split_axis=0, concat_axis=0, tiled=True),
        lax.all_to_all(block_labels, "adapter", split_axis=0, concat_axis=0, tiled=True),
    )
    lowrank_update = resident_update(
        arriving_rows, row_markers, adapter_down_weight, adapter_up_weight
    )
    returned = lax.all_to_all(lowrank_update, "adapter", split_axis=0, concat_axis=0, tiled=True)
    mine = returned.reshape(devices * slots, rows, feature_width)[position]
    live = jnp.arange(rows, dtype=jnp.int32)[None, :] < request_block_rows[:, None]
    mixed = values + jnp.where(live[:, :, None], mine.astype(jnp.float32), jnp.float32(0.0))
    return mixed.astype(jnp.bfloat16)


def lanes_of(rows):
    return lax.broadcasted_iota(jnp.int32, (rows, LANES), 1)


def weight_kernel(whole, which, part_ref, group_ref, weight_ref, *out_refs):
    quarter = LANES // QUAD
    inside = lanes_of(weight_ref.shape[0]) < quarter
    for k, out_ref in zip(which, out_refs):
        j = part_ref[k]
        count = out_ref.shape[0]
        start = 0 if k < 2 else pl.multiple_of(group_ref[0] * count, count)
        rows = pl.ds(start, count)
        out_ref[:, 0:whole] = weight_ref[rows, pl.ds(pl.multiple_of(j * whole, LANES), whole)]
        last = weight_ref[rows, QUAD * whole :].astype(jnp.float32)
        turned = pltpu.roll(last, lax.rem(LANES - quarter * j, LANES), 1)
        out_ref[:, whole:] = jnp.where(inside[0:count], turned, 0.0).astype(jnp.bfloat16)


def pack_kernel(whole, most_ref, target_ref, label_ref, tokens_ref, out_ref, normed_ref):
    values = tokens_ref[...].astype(jnp.float32)
    mean_sq = jnp.mean(values * values, axis=-1, keepdims=True)
    normed_ref[...] = (values * lax.rsqrt(mean_sq + 1e-06)).astype(jnp.bfloat16)
    total = tokens_ref.shape[0]
    quads, cap = out_ref.shape[0] // QUAD, out_ref.shape[1]
    quarter = LANES // QUAD
    lane = lanes_of(total)
    last = normed_ref[:, QUAD * whole :].astype(jnp.float32)
    label = jnp.where(lane == quarter, label_ref[...], 0.0)
    ends = []
    for j in range(QUAD):
        turned = pltpu.roll(last, (LANES - quarter * j) % LANES, 1) if j else last
        ends.append(jnp.where(lane < quarter, turned, label).astype(jnp.bfloat16))
    most = most_ref[0].astype(jnp.float32)
    note = jnp.where(lanes_of(cap) == quarter + 1, most, 0.0)
    for q in range(quads):
        place = lax.broadcasted_iota(jnp.int32, (cap, total), 0) + q * total
        chosen = jnp.where(target_ref[...] == place, 1.0, 0.0).astype(jnp.bfloat16)
        for j in range(QUAD):
            columns = slice(j * whole, (j + 1) * whole)
            out_ref[q * QUAD + j, :, 0:whole] = jnp.dot(
                chosen, normed_ref[:, columns], preferred_element_type=jnp.float32
            ).astype(jnp.bfloat16)
            end = jnp.dot(chosen, ends[j], preferred_element_type=jnp.float32)
            out_ref[q * QUAD + j, :, whole:] = (end + note).astype(jnp.bfloat16)


def label_of(last_tile):
    rows = last_tile.shape[0]
    quarter = LANES // QUAD
    label = last_tile[:, quarter : quarter + 1].astype(jnp.float32) - 1.0
    return label - jnp.where(lanes_of(rows) < HALF, 0.0, 1.0)


def down_kernel(first_ref, rows_ref, *refs):
    weight_refs, out_ref = refs[:-1], refs[-1]
    senders, cap, width = rows_ref.shape
    dims = (((1,), (1,)), ((), ()))
    low = lanes_of(2 * cap) < HALF

    def one(c, carry):
        rows = jnp.concatenate([rows_ref[4 * c + i] for i in range(4)], axis=0)
        label = label_of(rows[:, width - LANES :])
        picked = jnp.zeros((4 * cap, LANES), jnp.float32)
        for k, weight_ref in enumerate(weight_refs):
            product = lax.dot_general(
                rows, weight_ref[...], dims, preferred_element_type=jnp.float32
            )
            first = first_ref[k].astype(jnp.float32)
            for t in range(weight_ref.shape[0] // LANES):
                columns = slice(t * LANES, (t + 1) * LANES)
                picked = jnp.where(label == first + 2.0 * t, product[:, columns], picked)
        picked = picked + pltpu.roll(picked, HALF, 1)
        out_ref[c] = jnp.where(low, picked[0 : 2 * cap], picked[2 * cap :]).astype(jnp.bfloat16)
        return carry

    lax.fori_loop(0, senders // 4, one, 0)


def up_kernel(first_ref, rows_ref, *refs):
    sum_refs, weight_refs, out_ref = refs[:QUAD], refs[QUAD:-1], refs[-1]
    senders, cap, width = rows_ref.shape
    kept = out_ref.shape[1]
    low = lanes_of(2 * cap) < HALF

    def one(c, carry):
        down = sum_refs[0][c].astype(jnp.float32)
        for ref in sum_refs[1:]:
            down = down + ref[c].astype(jnp.float32)
        down = down.astype(jnp.bfloat16).astype(jnp.float32)
        turned = pltpu.roll(down, HALF, 1)
        pairs = [jnp.where(low, down, turned), jnp.where(low, turned, down)]
        twice = jnp.concatenate(
            [pairs[i // 2][i % 2 * cap : i % 2 * cap + kept] for i in range(4)], axis=0
        )
        ends = [rows_ref[4 * c + i, 0:kept, width - LANES :] for i in range(4)]
        label = label_of(jnp.concatenate(ends, axis=0))
        delta = jnp.zeros((4 * kept, width), jnp.float32)
        for k, weight_ref in enumerate(weight_refs):
            first = first_ref[k].astype(jnp.float32)
            placed = [
                jnp.where(label == first + 2.0 * t, twice, 0.0)
                for t in range(weight_ref.shape[0] // LANES)
            ]
            placed = jnp.concatenate(placed, axis=1).astype(jnp.bfloat16)
            delta = delta + jnp.dot(placed, weight_ref[...], preferred_element_type=jnp.float32)
        for i in range(4):
            out_ref[4 * c + i] = delta[i * kept : (i + 1) * kept].astype(jnp.bfloat16)
        return carry

    lax.fori_loop(0, senders // 4, one, 0)


def mix_kernel(whole, target_ref, tokens_ref, returned_ref, out_ref):
    total = tokens_ref.shape[0]
    quads, cap = returned_ref.shape[0] // QUAD, returned_ref.shape[1]
    quarter = LANES // QUAD
    lane = lanes_of(total)
    spot = lax.broadcasted_iota(jnp.int32, (total, quads * cap), 1)
    place = spot // cap * total + spot % cap
    chosen = jnp.where(target_ref[...] == place, 1.0, 0.0).astype(jnp.bfloat16)
    end = jnp.zeros((total, LANES), jnp.float32)
    for j in range(QUAD):
        share = jnp.concatenate([returned_ref[q * QUAD + j] for q in range(quads)], axis=0)
        delta = jnp.dot(chosen, share, preferred_element_type=jnp.float32)
        columns = slice(j * whole, (j + 1) * whole)
        out_ref[:, columns] = (
            tokens_ref[:, columns].astype(jnp.float32) + delta[:, 0:whole]
        ).astype(jnp.bfloat16)
        last = delta[:, whole:]
        turned = pltpu.roll(last, quarter * j, 1) if j else last
        end = jnp.where((lane >= quarter * j) & (lane < quarter * (j + 1)), turned, end)
    out_ref[:, QUAD * whole :] = (
        tokens_ref[:, QUAD * whole :].astype(jnp.float32) + end
    ).astype(jnp.bfloat16)


def call(kernel, out_shape, in_specs, flops, moved, after=(), scratch=()):
    many = isinstance(out_shape, list)
    skipped = len(after)
    body = (lambda *refs: kernel(*refs[skipped:])) if skipped else kernel
    run = pl.pallas_call(
        body,
        out_shape=out_shape,
        in_specs=[pl.BlockSpec(memory_space=pl.ANY)] * skipped + in_specs,
        out_specs=[VMEM] * len(out_shape) if many else VMEM,
        scratch_shapes=scratch,
        compiler_params=pltpu.CompilerParams(vmem_limit_bytes=48 * 2**20),
        cost_estimate=pl.CostEstimate(flops=flops, bytes_accessed=moved, transcendentals=0),
    )
    return functools.partial(run, *after)


def exchange(value):
    return lax.all_to_all(value, "adapter", split_axis=0, concat_axis=0, tiled=True)


def towards(value, k, devices):
    return lax.ppermute(value, "adapter", [(i, i ^ k) for i in range(devices)])


def swapped(value):
    return lax.ppermute(value, "groups", [(0, 1), (1, 0)])


def back_and_mix(
    kept, tokens, target, first, arrived, sums, up_weights, *unused_values
):
    blocks, rows, width = tokens.shape
    total = blocks * rows
    devices, cap, share = arrived.shape
    columns = sum(weight.shape[0] for weight in up_weights)
    leaving = call(
        up_kernel,
        jax.ShapeDtypeStruct((devices, kept, share), jnp.bfloat16),
        [SMEM] + [VMEM] * (1 + QUAD + len(up_weights)),
        2 * devices * kept * columns * share,
        2 * (2 * devices * kept + columns) * share,
    )(first, arrived, *sums, *up_weights)
    mixed = call(
        functools.partial(mix_kernel, share - LANES),
        jax.ShapeDtypeStruct((total, width), jnp.bfloat16),
        [VMEM] * 3,
        2 * devices * kept * total * share,
        2 * (2 * total * width + devices * kept * share),
    )(target.reshape(total, 1), tokens.reshape(total, width), exchange(leaving))
    return mixed.reshape(tokens.shape)


def start_again(tokens, target, first, arrived, sums, up_weights, *arguments):
    return rows_to_holders(tokens, *arguments)


def rows_to_quads(
    tokens, request_block_adapter, request_block_rows, adapter_down_weight, adapter_up_weight
):
    blocks, rows, width = tokens.shape
    devices = lax.axis_size("adapter")
    resident, rank, unused_width = adapter_up_weight.shape
    total = blocks * rows
    columns = resident * rank
    whole = width // LANES // QUAD * LANES
    share = whole + LANES
    bf16, i32 = jnp.bfloat16, jnp.int32

    quad = request_block_adapter // (resident * QUAD)
    label = request_block_adapter - quad * (resident * QUAD) + 1
    serial = jnp.arange(blocks, dtype=i32)
    same = quad[:, None] == quad[None, :]
    used = request_block_rows
    ahead = jnp.where(same & (serial[None, :] < serial[:, None]), used[None, :], 0)
    most = jnp.max(jnp.sum(jnp.where(same, used[None, :], 0), axis=1))
    row = jnp.arange(rows, dtype=i32)
    start = quad * total + jnp.sum(ahead, axis=1)
    target = jnp.where(row[None, :] < used[:, None], start[:, None] + row[None, :], -1)
    target = target.reshape(total).astype(i32)
    label = jnp.broadcast_to(label[:, None], (blocks, rows)).reshape(total, 1).astype(jnp.float32)

    me = lax.axis_index("adapter").astype(i32)
    group = lax.axis_index("groups").astype(i32)
    parts = jnp.bitwise_xor(me % QUAD, jnp.arange(QUAD, dtype=i32))
    own_half, twin_half = group * (resident // 2), (1 - group) * (resident // 2)
    first = jnp.concatenate(
        [parts * resident + jnp.stack([0 * group, 0 * group, own_half, own_half])]
        + [parts[2:] * resident + twin_half]
    ).astype(i32)

    def shares(weight, which, after):
        values = call(
            functools.partial(weight_kernel, whole, which),
            [
                jax.ShapeDtypeStruct((columns if k < 2 else columns // 2, share), bf16)
                for k in which
            ],
            [SMEM, SMEM, VMEM],
            0,
            len(which) * columns * width,
            after,
        )(parts, group.reshape(1), weight)
        return [towards(value, k, devices) if k else value for k, value in zip(which, values)]

    weight = adapter_down_weight.transpose(0, 2, 1).reshape(columns, width)
    down_weights = shares(weight, [0, 1, 2, 3], [])
    down_weights.append(swapped(down_weights[2]))
    weight = adapter_up_weight.reshape(columns, width)
    up_weights = shares(weight, [0, 1, 2], down_weights[2:3])
    up_weights += shares(weight, [3], down_weights[3:5])
    down_weights.append(swapped(down_weights[3]))
    up_weights.append(swapped(up_weights[2]))
    up_weights.append(swapped(up_weights[3]))
    caps = [total * 5 // 16, total * 6 // 16, total * 7 // 16]
    cap = caps[-1]
    arrived = exchange(
        call(
            functools.partial(pack_kernel, whole),
            jax.ShapeDtypeStruct((devices, cap, share), bf16),
            [SMEM, VMEM, VMEM, VMEM],
            2 * devices * cap * total * share,
            2 * (total * width + devices * cap * share),
            scratch=[pltpu.VMEM((total, width), bf16)],
        )(most.reshape(1), target.reshape(1, total), label, tokens.reshape(total, width))
    )

    most = jnp.max(arrived[:, 0, whole + LANES // QUAD + 1].astype(jnp.float32)).reshape(1, 1)
    others_most = swapped(most)
    most = jnp.maximum(most, others_most)[0, 0].astype(i32)
    partial = call(
        down_kernel,
        jax.ShapeDtypeStruct((devices // 4, 2 * cap, LANES), bf16),
        [SMEM] + [VMEM] * (1 + len(down_weights)),
        2 * devices * cap * 4 * columns * share,
        2 * (devices * cap + 4 * columns) * share,
        [up_weights[4], others_most],
    )(first, arrived, *down_weights)
    sums = [partial] + [towards(partial, k, devices) for k in range(1, QUAD)]
    return lax.switch(
        sum((most > more).astype(i32) for more in caps),
        [functools.partial(back_and_mix, more) for more in caps] + [start_again],
        tokens,
        target,
        first,
        arrived,
        sums,
        up_weights,
        request_block_adapter,
        request_block_rows,
        adapter_down_weight,
        adapter_up_weight,
    )


def solution(mesh):
    placed = (
        P(("groups", "adapter"), None, None),
        P(("groups", "adapter")),
        P(("groups", "adapter")),
        P("adapter", None, None),
        P("adapter", None, None),
    )

    def per_device(tokens, request_block_adapter, request_block_rows, down_weight, up_weight):
        blocks, rows, width = tokens.shape
        devices = mesh.shape["adapter"]
        slots = max(1, 4 * blocks // devices)
        quads = devices % QUAD == 0 and slots * QUAD >= blocks
        quads = quads and width % (QUAD * LANES) == LANES and up_weight.shape[1] == HALF
        plan = rows_to_quads if quads else rows_to_holders
        return plan(tokens, request_block_adapter, request_block_rows, down_weight, up_weight)

    return jax.shard_map(
        per_device,
        mesh=mesh,
        in_specs=placed,
        out_specs=P(("groups", "adapter"), None, None),
        check_vma=False,
    )
```

```python
import functools

import jax
import jax.numpy as jnp
from jax import lax
from jax.experimental import pallas as pl
from jax.experimental.pallas import tpu as pltpu
from jax.sharding import PartitionSpec as P

LANES = 128
HALF = 64
QUAD = 4
QUARTER = 32
STEP = 16
NOTE = 96
VMEM = pl.BlockSpec(memory_space=pltpu.VMEM)
SMEM = pl.BlockSpec(memory_space=pltpu.SMEM)


def normalise(tokens):
    values = tokens.astype(jnp.float32)
    mean_sq = jnp.mean(values * values, axis=-1, keepdims=True)
    return (values, (values * lax.rsqrt(mean_sq + 1e-06)).astype(jnp.bfloat16))


def resident_update(hidden_state, block_labels, adapter_down_weight, adapter_up_weight):
    feature_width = hidden_state.shape[-1]
    leading = hidden_state.shape[:-1]
    resident_rows, unused_value, inner_rank = adapter_down_weight.shape
    flattened_tokens = hidden_state.reshape(-1, feature_width)
    down_matrix = jnp.einsum(
        "tq,iqg->tig", flattened_tokens, adapter_down_weight, preferred_element_type=jnp.float32
    )
    down_matrix = down_matrix.astype(jnp.bfloat16).reshape(
        flattened_tokens.shape[0], resident_rows * inner_rank
    )
    column_owner = jnp.arange(resident_rows * inner_rank, dtype=jnp.int32) // inner_rank
    picked = block_labels.reshape(-1, 1) == column_owner[None, :]
    down_matrix = jnp.where(picked, down_matrix, jnp.zeros_like(down_matrix))
    lowrank_update = jnp.dot(
        down_matrix,
        adapter_up_weight.reshape(resident_rows * inner_rank, feature_width),
        preferred_element_type=jnp.float32,
    )
    return lowrank_update.astype(jnp.bfloat16).reshape(leading + (feature_width,))


def rows_to_holders(
    tokens, request_block_adapter, request_block_rows, adapter_down_weight, adapter_up_weight
):
    blocks, rows, feature_width = tokens.shape
    devices = lax.axis_size("adapter")
    resident_rows = adapter_down_weight.shape[0]
    slots = max(1, 4 * blocks // devices)
    values, normed = normalise(tokens)
    owner = request_block_adapter // resident_rows
    within = request_block_adapter - owner * resident_rows
    serial = jnp.arange(blocks, dtype=jnp.int32)
    earlier = (owner[:, None] == owner[None, :]) & (serial[None, :] < serial[:, None])
    position = owner * slots + jnp.sum(earlier, axis=1)
    outgoing = (
        jnp.zeros((devices * slots, rows, feature_width), jnp.bfloat16).at[position].set(normed)
    )
    outgoing = outgoing.reshape(devices, slots, rows, feature_width)
    block_labels = jnp.full((devices * slots,), -1, jnp.int32).at[position].set(within)
    block_labels = jnp.broadcast_to(block_labels[:, None], (devices * slots, rows)).reshape(
        devices, slots, rows
    )
    arriving_rows, row_markers = (
        lax.all_to_all(outgoing, "adapter", split_axis=0, concat_axis=0, tiled=True),
        lax.all_to_all(block_labels, "adapter", split_axis=0, concat_axis=0, tiled=True),
    )
    lowrank_update = resident_update(
        arriving_rows, row_markers, adapter_down_weight, adapter_up_weight
    )
    returned = lax.all_to_all(lowrank_update, "adapter", split_axis=0, concat_axis=0, tiled=True)
    mine = returned.reshape(devices * slots, rows, feature_width)[position]
    live = jnp.arange(rows, dtype=jnp.int32)[None, :] < request_block_rows[:, None]
    mixed = values + jnp.where(live[:, :, None], mine.astype(jnp.float32), jnp.float32(0.0))
    return mixed.astype(jnp.bfloat16)


def lanes_of(rows):
    return lax.broadcasted_iota(jnp.int32, (rows, LANES), 1)


def weight_kernel(whole, which, part_ref, group_ref, weight_ref, *out_refs):
    tiles = whole // LANES
    for k, out_ref in zip(which, out_refs):
        j = part_ref[k]
        if k < 2:
            last = weight_ref[:, QUAD * whole :].astype(jnp.float32)
            turned = pltpu.roll(last, lax.rem(LANES - QUARTER * j, LANES), 1)
            inside = lanes_of(last.shape[0]) < QUARTER
            out_ref[:, 0:whole] = weight_ref[:, pl.ds(pl.multiple_of(j * whole, LANES), whole)]
            out_ref[:, whole:] = jnp.where(inside, turned, 0.0).astype(jnp.bfloat16)
            continue
        count = weight_ref.shape[0] // 2
        start = pl.multiple_of(group_ref[0] * count, count)
        for t in range(tiles):
            column = pl.multiple_of(j * whole + t * LANES, LANES)
            out_ref[t * count : (t + 1) * count, :] = weight_ref[
                pl.ds(start, count), pl.ds(column, LANES)
            ]
        last = weight_ref[pl.ds(start, count), QUAD * whole :].astype(jnp.float32)
        size = count // QUAD
        owner = lanes_of(size) // QUARTER
        merged = jnp.zeros((size, LANES), jnp.float32)
        for m in range(QUAD):
            shift = lax.rem(LANES + QUARTER * (m - j), LANES)
            turned = pltpu.roll(last[m * size : (m + 1) * size], shift, 1)
            merged = jnp.where(owner == m, turned, merged)
        out_ref[tiles * count :, :] = merged.astype(jnp.bfloat16)


def open_far(far_refs, opened_ref):
    count, width = opened_ref.shape[1:]
    tiles, size = width // LANES - 1, count // QUAD
    inside = lanes_of(size) < QUARTER
    for i, ref in enumerate(far_refs):
        for t in range(tiles):
            opened_ref[i, :, t * LANES : (t + 1) * LANES] = ref[t * count : (t + 1) * count, :]
        packed = ref[tiles * count :, :].astype(jnp.float32)
        for m in range(QUAD):
            turned = pltpu.roll(packed, (LANES - QUARTER * m) % LANES, 1) if m else packed
            opened_ref[i, m * size : (m + 1) * size, tiles * LANES :] = jnp.where(
                inside, turned, 0.0
            ).astype(jnp.bfloat16)


def pack_kernel(whole, cap, most_ref, target_ref, label_ref, tokens_ref, out_ref, normed_ref):
    values = tokens_ref[...].astype(jnp.float32)
    mean_sq = jnp.mean(values * values, axis=-1, keepdims=True)
    normed_ref[...] = (values * lax.rsqrt(mean_sq + 1e-06)).astype(jnp.bfloat16)
    total = tokens_ref.shape[0]
    quads, tiles = out_ref.shape[0] // QUAD, whole // LANES
    lane = lanes_of(total)
    last = normed_ref[:, QUAD * whole :].astype(jnp.float32)
    label = jnp.where(lane == QUARTER, label_ref[...], 0.0)
    ends = []
    for j in range(QUAD):
        turned = pltpu.roll(last, (LANES - QUARTER * j) % LANES, 1) if j else last
        ends.append(jnp.where(lane < QUARTER, turned, label).astype(jnp.bfloat16))
    most = most_ref[0].astype(jnp.float32)
    group_lane = lanes_of(QUARTER) // QUARTER
    step_lane = lanes_of(STEP)
    for q in range(quads):
        place = lax.broadcasted_iota(jnp.int32, (cap, total), 0) + q * total
        chosen = jnp.where(target_ref[...] == place, 1.0, 0.0).astype(jnp.bfloat16)
        for j in range(QUAD):
            share = jnp.dot(
                chosen,
                normed_ref[:, j * whole : (j + 1) * whole],
                preferred_element_type=jnp.float32,
            ).astype(jnp.bfloat16)
            for t in range(tiles):
                out_ref[q * QUAD + j, t * cap : (t + 1) * cap, :] = share[
                    :, t * LANES : (t + 1) * LANES
                ]
            end = jnp.dot(chosen, ends[j], preferred_element_type=jnp.float32)
            if j == 0:
                notes = jnp.where(step_lane == NOTE + cap // STEP, most, 0.0)
                for a in range(cap // STEP):
                    turned = pltpu.roll(end[a * STEP : (a + 1) * STEP], NOTE + a - QUARTER, 1)
                    notes = jnp.where(step_lane == NOTE + a, turned, notes)
            padded = jnp.concatenate(
                [end, jnp.zeros((QUAD * QUARTER - cap, LANES), jnp.float32)], axis=0
            )
            merged = padded[0:QUARTER]
            for m in range(1, QUAD):
                turned = pltpu.roll(padded[m * QUARTER : (m + 1) * QUARTER], m * QUARTER, 1)
                merged = jnp.where(group_lane == m, turned, merged)
            out_ref[q * QUAD + j, tiles * cap : tiles * cap + STEP, :] = merged[0:STEP].astype(
                jnp.bfloat16
            )
            out_ref[q * QUAD + j, tiles * cap + STEP :, :] = jnp.where(
                step_lane >= NOTE, notes, merged[STEP:]
            ).astype(jnp.bfloat16)


def step_labels(cap, tiles, a, rows_ref):
    columns = []
    for s in range(rows_ref.shape[0]):
        notes = rows_ref[s, tiles * cap + STEP :, :].astype(jnp.float32)
        turned = pltpu.roll(notes, lax.rem(2 * LANES - NOTE - a, LANES), 1)
        columns.append(jnp.broadcast_to(turned[:, 0:1], (STEP, LANES)))
    label = jnp.concatenate(columns, axis=0) - 1.0
    return label, label - jnp.where(lanes_of(label.shape[0]) < HALF, 0.0, 1.0)


def weight_blocks(near_refs, opened_ref):
    return [ref[...] for ref in near_refs] + [opened_ref[i] for i in range(opened_ref.shape[0])]


def down_kernel(first_ref, rows_ref, *refs):
    near_refs, far_refs, (out_ref, opened_ref, batch_ref) = refs[:2], refs[2:6], refs[6:]
    senders, width = rows_ref.shape[0], batch_ref.shape[1]
    tiles = width // LANES - 1
    cap = out_ref.shape[0] * STEP
    dims = (((1,), (1,)), ((), ()))
    half = senders * STEP // 2
    low = lanes_of(half) < HALF
    open_far(far_refs, opened_ref)

    def one(a, carry):
        label, lowered = step_labels(cap, tiles, a, rows_ref)
        used = jnp.max(label) >= 0.0
        out_ref[a] = jnp.zeros((half, LANES), jnp.bfloat16)

        @pl.when(used)
        def _():
            shift = lax.rem(LANES - QUARTER * (a // 2), LANES)
            spot = pl.multiple_of(tiles * cap + lax.rem(a, 2) * STEP, STEP)
            for s in range(senders):
                rows = slice(s * STEP, (s + 1) * STEP)
                for t in range(tiles):
                    at = pl.multiple_of(t * cap + a * STEP, STEP)
                    batch_ref[rows, t * LANES : (t + 1) * LANES] = rows_ref[s, pl.ds(at, STEP), :]
                end = rows_ref[s, pl.ds(spot, STEP), :].astype(jnp.float32)
                batch_ref[rows, tiles * LANES :] = pltpu.roll(end, shift, 1).astype(jnp.bfloat16)
            picked = jnp.zeros((senders * STEP, LANES), jnp.float32)
            for k, weight in enumerate(weight_blocks(near_refs, opened_ref)):
                product = lax.dot_general(
                    batch_ref[...], weight, dims, preferred_element_type=jnp.float32
                )
                first = first_ref[k].astype(jnp.float32)
                for t in range(weight.shape[0] // LANES):
                    columns = slice(t * LANES, (t + 1) * LANES)
                    picked = jnp.where(lowered == first + 2.0 * t, product[:, columns], picked)
            both = picked + pltpu.roll(picked, HALF, 1)
            out_ref[a] = jnp.where(low, both[0:half], both[half:]).astype(jnp.bfloat16)

        return carry

    lax.fori_loop(0, cap // STEP, one, 0)


def up_kernel(first_ref, rows_ref, *refs):
    sum_refs, near_refs, far_refs = refs[:QUAD], refs[QUAD : QUAD + 2], refs[QUAD + 2 : QUAD + 6]
    out_ref, opened_ref, ends_ref = refs[QUAD + 6 :]
    senders, width = rows_ref.shape[0], opened_ref.shape[2]
    tiles = width // LANES - 1
    cap = sum_refs[0].shape[0] * STEP
    kept = (out_ref.shape[1] - QUARTER) // tiles
    half = senders * STEP // 2
    low = lanes_of(half) < HALF
    group_lane = lanes_of(STEP) // QUARTER
    open_far(far_refs, opened_ref)
    ends_ref[...] = jnp.zeros(ends_ref.shape, jnp.float32)

    def one(a, carry):
        label, lowered = step_labels(cap, tiles, a, rows_ref)
        used = jnp.max(label) >= 0.0

        def leave(value):
            spot = pl.multiple_of(lax.rem(a, 2) * STEP, STEP)
            for s in range(senders):
                rows = slice(s * STEP, (s + 1) * STEP)
                for t in range(tiles):
                    at = pl.multiple_of(t * kept + a * STEP, STEP)
                    out_ref[s, pl.ds(at, STEP), :] = value[
                        rows, t * LANES : (t + 1) * LANES
                    ].astype(jnp.bfloat16)
                turned = pltpu.roll(value[rows, tiles * LANES :], QUARTER * (a // 2), 1)
                ends_ref[s, pl.ds(spot, STEP), :] = jnp.where(
                    group_lane == a // 2, turned, ends_ref[s, pl.ds(spot, STEP), :]
                )

        @pl.when(used)
        def _():
            down = sum_refs[0][a].astype(jnp.float32)
            for ref in sum_refs[1:]:
                down = down + ref[a].astype(jnp.float32)
            down = down.astype(jnp.bfloat16).astype(jnp.float32)
            turned = pltpu.roll(down, HALF, 1)
            twice = jnp.concatenate(
                [jnp.where(low, down, turned), jnp.where(low, turned, down)], axis=0
            )
            delta = jnp.zeros((senders * STEP, width), jnp.float32)
            for k, weight in enumerate(weight_blocks(near_refs, opened_ref)):
                first = first_ref[k].astype(jnp.float32)
                placed = [
                    jnp.where(lowered == first + 2.0 * t, twice, 0.0)
                    for t in range(weight.shape[0] // LANES)
                ]
                placed = jnp.concatenate(placed, axis=1).astype(jnp.bfloat16)
                delta = delta + jnp.dot(placed, weight, preferred_element_type=jnp.float32)
            leave(delta)

        @pl.when(jnp.logical_not(used))
        def _():
            leave(jnp.zeros((senders * STEP, width), jnp.float32))

        return carry

    lax.fori_loop(0, kept // STEP, one, 0)
    for s in range(senders):
        out_ref[s, tiles * kept :, :] = ends_ref[s].astype(jnp.bfloat16)


def mix_kernel(whole, target_ref, tokens_ref, returned_ref, out_ref):
    total = tokens_ref.shape[0]
    tiles = whole // LANES
    quads, kept = returned_ref.shape[0] // QUAD, (returned_ref.shape[1] - QUARTER) // tiles
    lane = lanes_of(total)
    spot = lax.broadcasted_iota(jnp.int32, (total, quads * kept), 1)
    place = spot // kept * total + spot % kept
    chosen = jnp.where(target_ref[...] == place, 1.0, 0.0).astype(jnp.bfloat16)
    end = jnp.zeros((total, LANES), jnp.float32)
    for j in range(QUAD):
        shares = []
        for q in range(quads):
            d = q * QUAD + j
            parts = [returned_ref[d, t * kept : (t + 1) * kept, :] for t in range(tiles)]
            packed = returned_ref[d, tiles * kept :, :].astype(jnp.float32)
            groups = [packed]
            for m in range(1, QUAD):
                groups.append(pltpu.roll(packed, LANES - QUARTER * m, 1))
            parts.append(jnp.concatenate(groups, axis=0)[0:kept].astype(jnp.bfloat16))
            shares.append(jnp.concatenate(parts, axis=1))
        share = jnp.concatenate(shares, axis=0)
        delta = jnp.dot(chosen, share, preferred_element_type=jnp.float32)
        columns = slice(j * whole, (j + 1) * whole)
        out_ref[:, columns] = (
            tokens_ref[:, columns].astype(jnp.float32) + delta[:, 0:whole]
        ).astype(jnp.bfloat16)
        last = delta[:, whole:]
        turned = pltpu.roll(last, QUARTER * j, 1) if j else last
        end = jnp.where((lane >= QUARTER * j) & (lane < QUARTER * (j + 1)), turned, end)
    out_ref[:, QUAD * whole :] = (
        tokens_ref[:, QUAD * whole :].astype(jnp.float32) + end
    ).astype(jnp.bfloat16)


def call(kernel, out_shape, in_specs, flops, moved, after=(), scratch=()):
    many = isinstance(out_shape, list)
    skipped = len(after)
    body = (lambda *refs: kernel(*refs[skipped:])) if skipped else kernel
    run = pl.pallas_call(
        body,
        out_shape=out_shape,
        in_specs=[pl.BlockSpec(memory_space=pl.ANY)] * skipped + in_specs,
        out_specs=[VMEM] * len(out_shape) if many else VMEM,
        scratch_shapes=scratch,
        compiler_params=pltpu.CompilerParams(vmem_limit_bytes=48 * 2**20),
        cost_estimate=pl.CostEstimate(flops=flops, bytes_accessed=moved, transcendentals=0),
    )
    return functools.partial(run, *after)


def exchange(value):
    return lax.all_to_all(value, "adapter", split_axis=0, concat_axis=0, tiled=True)


def towards(value, k, devices):
    return lax.ppermute(value, "adapter", [(i, i ^ k) for i in range(devices)])


def swapped(value):
    return lax.ppermute(value, "groups", [(0, 1), (1, 0)])


def back_and_mix(kept, tokens, target, first, arrived, sums, up_weights, *unused_values):
    blocks, rows, width = tokens.shape
    total = blocks * rows
    devices = arrived.shape[0]
    columns, share = up_weights[0].shape
    whole = share - LANES
    leaving = call(
        up_kernel,
        jax.ShapeDtypeStruct((devices, whole // LANES * kept + QUARTER, LANES), jnp.bfloat16),
        [SMEM] + [VMEM] * (1 + QUAD + len(up_weights)),
        2 * devices * kept * QUAD * columns * share,
        2 * (2 * devices * kept + QUAD * columns) * share,
        scratch=[
            pltpu.VMEM((4, columns // 2, share), jnp.bfloat16),
            pltpu.VMEM((devices, QUARTER, LANES), jnp.float32),
        ],
    )(first, arrived, *sums, *up_weights)
    mixed = call(
        functools.partial(mix_kernel, whole),
        jax.ShapeDtypeStruct((total, width), jnp.bfloat16),
        [VMEM] * 3,
        2 * devices * kept * total * share,
        2 * (2 * total * width + devices * kept * share),
    )(target.reshape(total, 1), tokens.reshape(total, width), exchange(leaving))
    return mixed.reshape(tokens.shape)


def start_again(tokens, target, first, arrived, sums, up_weights, *arguments):
    return rows_to_holders(tokens, *arguments)


def rows_to_quads(
    tokens, request_block_adapter, request_block_rows, adapter_down_weight, adapter_up_weight
):
    blocks, rows, width = tokens.shape
    devices = lax.axis_size("adapter")
    resident, rank, unused_width = adapter_up_weight.shape
    total = blocks * rows
    columns = resident * rank
    whole = width // LANES // QUAD * LANES
    share = whole + LANES
    bf16, i32 = jnp.bfloat16, jnp.int32

    quad = request_block_adapter // (resident * QUAD)
    label = request_block_adapter - quad * (resident * QUAD) + 1
    serial = jnp.arange(blocks, dtype=i32)
    same = quad[:, None] == quad[None, :]
    used = request_block_rows
    ahead = jnp.where(same & (serial[None, :] < serial[:, None]), used[None, :], 0)
    most = jnp.max(jnp.sum(jnp.where(same, used[None, :], 0), axis=1)).astype(jnp.float32)
    most = jnp.maximum(most, swapped(most.reshape(1, 1))[0, 0]).astype(i32)
    row = jnp.arange(rows, dtype=i32)
    start = quad * total + jnp.sum(ahead, axis=1)
    target = jnp.where(row[None, :] < used[:, None], start[:, None] + row[None, :], -1)
    target = target.reshape(total).astype(i32)
    label = jnp.broadcast_to(label[:, None], (blocks, rows)).reshape(total, 1).astype(jnp.float32)

    me = lax.axis_index("adapter").astype(i32)
    group = lax.axis_index("groups").astype(i32)
    parts = jnp.bitwise_xor(me % QUAD, jnp.arange(QUAD, dtype=i32))
    own_half, twin_half = group * (resident // 2), (1 - group) * (resident // 2)
    first = jnp.concatenate(
        [parts * resident + jnp.stack([0 * group, 0 * group, own_half, own_half])]
        + [parts[2:] * resident + twin_half]
    ).astype(i32)

    tiles = whole // LANES

    def shares(weight, which, after):
        far = (columns // 2 * tiles + columns // 2 // QUAD, LANES)
        values = call(
            functools.partial(weight_kernel, whole, which),
            [jax.ShapeDtypeStruct((columns, share) if k < 2 else far, bf16) for k in which],
            [SMEM, SMEM, VMEM],
            0,
            len(which) * columns * width,
            after,
        )(parts, group.reshape(1), weight)
        return [towards(value, k, devices) if k else value for k, value in zip(which, values)]

    weight = adapter_down_weight.transpose(0, 2, 1).reshape(columns, width)
    down_weights = shares(weight, [0, 1, 2, 3], [])
    down_weights.append(swapped(down_weights[2]))
    weight = adapter_up_weight.reshape(columns, width)
    up_weights = shares(weight, [0, 1, 2], down_weights[2:3])
    up_weights += shares(weight, [3], down_weights[3:5])
    down_weights.append(swapped(down_weights[3]))
    up_weights.append(swapped(up_weights[2]))
    up_weights.append(swapped(up_weights[3]))

    caps = [total * 5 // 16, total * 6 // 16, total * 7 // 16]
    cap = caps[-1]
    arrived = exchange(
        call(
            functools.partial(pack_kernel, whole, cap),
            jax.ShapeDtypeStruct((devices, tiles * cap + QUARTER, LANES), bf16),
            [SMEM, VMEM, VMEM, VMEM],
            2 * devices * cap * total * share,
            2 * (total * width + devices * cap * share),
            scratch=[pltpu.VMEM((total, width), bf16)],
        )(most.reshape(1), target.reshape(1, total), label, tokens.reshape(total, width))
    )

    counts = arrived[:, tiles * cap + STEP, NOTE + cap // STEP].astype(jnp.float32)
    most = jnp.max(counts).astype(i32)
    partial = call(
        down_kernel,
        jax.ShapeDtypeStruct((cap // STEP, devices * STEP // 2, LANES), bf16),
        [SMEM] + [VMEM] * (1 + len(down_weights)),
        2 * devices * cap * QUAD * columns * share,
        2 * (devices * cap + QUAD * columns) * share,
        up_weights[4:5],
        [
            pltpu.VMEM((4, columns // 2, share), bf16),
            pltpu.VMEM((devices * STEP, share), bf16),
        ],
    )(first, arrived, *down_weights)
    sums = [partial] + [towards(partial, k, devices) for k in range(1, QUAD)]
    return lax.switch(
        sum((most > more).astype(i32) for more in caps),
        [functools.partial(back_and_mix, more) for more in caps] + [start_again],
        tokens,
        target,
        first,
        arrived,
        sums,
        up_weights,
        request_block_adapter,
        request_block_rows,
        adapter_down_weight,
        adapter_up_weight,
    )


def solution(mesh):
    placed = (
        P(("groups", "adapter"), None, None),
        P(("groups", "adapter")),
        P(("groups", "adapter")),
        P("adapter", None, None),
        P("adapter", None, None),
    )

    def per_device(tokens, request_block_adapter, request_block_rows, down_weight, up_weight):
        blocks, rows, width = tokens.shape
        devices = mesh.shape["adapter"]
        slots = max(1, 4 * blocks // devices)
        quads = devices % QUAD == 0 and slots * QUAD >= blocks
        quads = quads and width % (QUAD * LANES) == LANES and up_weight.shape[1] == HALF
        quads = quads and blocks * rows * 7 // 16 == 7 * STEP and mesh.shape["groups"] == 2
        plan = rows_to_quads if quads else rows_to_holders
        return plan(tokens, request_block_adapter, request_block_rows, down_weight, up_weight)

    return jax.shard_map(
        per_device,
        mesh=mesh,
        in_specs=placed,
        out_specs=P(("groups", "adapter"), None, None),
        check_vma=False,
    )
```

```python
import functools

import jax
import jax.numpy as jnp
from jax import lax
from jax.experimental import pallas as pl
from jax.experimental.pallas import tpu as pltpu
from jax.sharding import PartitionSpec as P

LANES = 128
HALF = 64
QUAD = 4
QUARTER = 32
STEP = 16
NOTE = 96
VMEM = pl.BlockSpec(memory_space=pltpu.VMEM)
SMEM = pl.BlockSpec(memory_space=pltpu.SMEM)


def normalise(tokens):
    values = tokens.astype(jnp.float32)
    mean_sq = jnp.mean(values * values, axis=-1, keepdims=True)
    return (values, (values * lax.rsqrt(mean_sq + 1e-06)).astype(jnp.bfloat16))


def resident_update(hidden_state, block_labels, adapter_down_weight, adapter_up_weight):
    feature_width = hidden_state.shape[-1]
    leading = hidden_state.shape[:-1]
    resident_rows, unused_value, inner_rank = adapter_down_weight.shape
    flattened_tokens = hidden_state.reshape(-1, feature_width)
    down_matrix = jnp.einsum(
        "tq,iqg->tig", flattened_tokens, adapter_down_weight, preferred_element_type=jnp.float32
    )
    down_matrix = down_matrix.astype(jnp.bfloat16).reshape(
        flattened_tokens.shape[0], resident_rows * inner_rank
    )
    column_owner = jnp.arange(resident_rows * inner_rank, dtype=jnp.int32) // inner_rank
    picked = block_labels.reshape(-1, 1) == column_owner[None, :]
    down_matrix = jnp.where(picked, down_matrix, jnp.zeros_like(down_matrix))
    lowrank_update = jnp.dot(
        down_matrix,
        adapter_up_weight.reshape(resident_rows * inner_rank, feature_width),
        preferred_element_type=jnp.float32,
    )
    return lowrank_update.astype(jnp.bfloat16).reshape(leading + (feature_width,))


def rows_to_holders(
    tokens, request_block_adapter, request_block_rows, adapter_down_weight, adapter_up_weight
):
    blocks, rows, feature_width = tokens.shape
    devices = lax.axis_size("adapter")
    resident_rows = adapter_down_weight.shape[0]
    slots = max(1, 4 * blocks // devices)
    values, normed = normalise(tokens)
    owner = request_block_adapter // resident_rows
    within = request_block_adapter - owner * resident_rows
    serial = jnp.arange(blocks, dtype=jnp.int32)
    earlier = (owner[:, None] == owner[None, :]) & (serial[None, :] < serial[:, None])
    position = owner * slots + jnp.sum(earlier, axis=1)
    outgoing = (
        jnp.zeros((devices * slots, rows, feature_width), jnp.bfloat16).at[position].set(normed)
    )
    outgoing = outgoing.reshape(devices, slots, rows, feature_width)
    block_labels = jnp.full((devices * slots,), -1, jnp.int32).at[position].set(within)
    block_labels = jnp.broadcast_to(block_labels[:, None], (devices * slots, rows)).reshape(
        devices, slots, rows
    )
    arriving_rows, row_markers = (
        lax.all_to_all(outgoing, "adapter", split_axis=0, concat_axis=0, tiled=True),
        lax.all_to_all(block_labels, "adapter", split_axis=0, concat_axis=0, tiled=True),
    )
    lowrank_update = resident_update(
        arriving_rows, row_markers, adapter_down_weight, adapter_up_weight
    )
    returned = lax.all_to_all(lowrank_update, "adapter", split_axis=0, concat_axis=0, tiled=True)
    mine = returned.reshape(devices * slots, rows, feature_width)[position]
    live = jnp.arange(rows, dtype=jnp.int32)[None, :] < request_block_rows[:, None]
    mixed = values + jnp.where(live[:, :, None], mine.astype(jnp.float32), jnp.float32(0.0))
    return mixed.astype(jnp.bfloat16)


def lanes_of(rows):
    return lax.broadcasted_iota(jnp.int32, (rows, LANES), 1)


def weight_kernel(whole, which, part_ref, group_ref, weight_ref, *out_refs):
    tiles = whole // LANES
    for k, out_ref in zip(which, out_refs):
        j = part_ref[k]
        if k < 2:
            last = weight_ref[:, QUAD * whole :].astype(jnp.float32)
            turned = pltpu.roll(last, lax.rem(LANES - QUARTER * j, LANES), 1)
            inside = lanes_of(last.shape[0]) < QUARTER
            out_ref[:, 0:whole] = weight_ref[:, pl.ds(pl.multiple_of(j * whole, LANES), whole)]
            out_ref[:, whole:] = jnp.where(inside, turned, 0.0).astype(jnp.bfloat16)
            continue
        count = weight_ref.shape[0] // 2
        start = pl.multiple_of(group_ref[0] * count, count)
        for t in range(tiles):
            column = pl.multiple_of(j * whole + t * LANES, LANES)
            out_ref[t * count : (t + 1) * count, :] = weight_ref[
                pl.ds(start, count), pl.ds(column, LANES)
            ]
        last = weight_ref[pl.ds(start, count), QUAD * whole :].astype(jnp.float32)
        size = count // QUAD
        owner = lanes_of(size) // QUARTER
        merged = jnp.zeros((size, LANES), jnp.float32)
        for m in range(QUAD):
            shift = lax.rem(LANES + QUARTER * (m - j), LANES)
            turned = pltpu.roll(last[m * size : (m + 1) * size], shift, 1)
            merged = jnp.where(owner == m, turned, merged)
        out_ref[tiles * count :, :] = merged.astype(jnp.bfloat16)


def open_far(far_refs, opened_ref):
    count, width = opened_ref.shape[1] // 2, opened_ref.shape[2]
    tiles, size = width // LANES - 1, count // QUAD
    inside = lanes_of(size) < QUARTER
    for i, ref in enumerate(far_refs):
        holder, base = i % 2, i // 2 * count
        for t in range(tiles):
            opened_ref[holder, base : base + count, t * LANES : (t + 1) * LANES] = ref[
                t * count : (t + 1) * count, :
            ]
        packed = ref[tiles * count :, :].astype(jnp.float32)
        for m in range(QUAD):
            turned = pltpu.roll(packed, (LANES - QUARTER * m) % LANES, 1) if m else packed
            opened_ref[holder, base + m * size : base + (m + 1) * size, tiles * LANES :] = (
                jnp.where(inside, turned, 0.0).astype(jnp.bfloat16)
            )


def pack_kernel(whole, cap, most_ref, target_ref, label_ref, tokens_ref, out_ref, normed_ref):
    values = tokens_ref[...].astype(jnp.float32)
    mean_sq = jnp.mean(values * values, axis=-1, keepdims=True)
    normed_ref[...] = (values * lax.rsqrt(mean_sq + 1e-06)).astype(jnp.bfloat16)
    total = tokens_ref.shape[0]
    quads, tiles = out_ref.shape[0] // QUAD, whole // LANES
    lane = lanes_of(total)
    last = normed_ref[:, QUAD * whole :].astype(jnp.float32)
    label = jnp.where(lane == QUARTER, label_ref[...], 0.0)
    ends = []
    for j in range(QUAD):
        turned = pltpu.roll(last, (LANES - QUARTER * j) % LANES, 1) if j else last
        ends.append(jnp.where(lane < QUARTER, turned, label).astype(jnp.bfloat16))
    most = most_ref[0].astype(jnp.float32)
    group_lane = lanes_of(QUARTER) // QUARTER
    step_lane = lanes_of(STEP)
    for q in range(quads):
        place = lax.broadcasted_iota(jnp.int32, (cap, total), 0) + q * total
        chosen = jnp.where(target_ref[...] == place, 1.0, 0.0).astype(jnp.bfloat16)
        for j in range(QUAD):
            share = jnp.dot(
                chosen,
                normed_ref[:, j * whole : (j + 1) * whole],
                preferred_element_type=jnp.float32,
            ).astype(jnp.bfloat16)
            for t in range(tiles):
                out_ref[q * QUAD + j, t * cap : (t + 1) * cap, :] = share[
                    :, t * LANES : (t + 1) * LANES
                ]
            end = jnp.dot(chosen, ends[j], preferred_element_type=jnp.float32)
            if j == 0:
                notes = jnp.where(step_lane == NOTE + cap // STEP, most, 0.0)
                for a in range(cap // STEP):
                    turned = pltpu.roll(end[a * STEP : (a + 1) * STEP], NOTE + a - QUARTER, 1)
                    notes = jnp.where(step_lane == NOTE + a, turned, notes)
            padded = jnp.concatenate(
                [end, jnp.zeros((QUAD * QUARTER - cap, LANES), jnp.float32)], axis=0
            )
            merged = padded[0:QUARTER]
            for m in range(1, QUAD):
                turned = pltpu.roll(padded[m * QUARTER : (m + 1) * QUARTER], m * QUARTER, 1)
                merged = jnp.where(group_lane == m, turned, merged)
            out_ref[q * QUAD + j, tiles * cap : tiles * cap + STEP, :] = merged[0:STEP].astype(
                jnp.bfloat16
            )
            out_ref[q * QUAD + j, tiles * cap + STEP :, :] = jnp.where(
                step_lane >= NOTE, notes, merged[STEP:]
            ).astype(jnp.bfloat16)


def step_labels(cap, tiles, a, rows_ref):
    columns = []
    for s in range(rows_ref.shape[0]):
        notes = rows_ref[s, tiles * cap + STEP :, :].astype(jnp.float32)
        turned = pltpu.roll(notes, lax.rem(2 * LANES - NOTE - a, LANES), 1)
        columns.append(jnp.broadcast_to(turned[:, 0:1], (STEP, LANES)))
    label = jnp.concatenate(columns, axis=0) - 1.0
    return label, label - jnp.where(lanes_of(label.shape[0]) < HALF, 0.0, 1.0)


def for_holders(first_ref, near_refs, opened_ref, label, step):
    tiles = opened_ref.shape[1] // LANES
    resident = 2 * tiles
    for h in range(QUAD):
        base = first_ref[h].astype(jnp.float32)
        met = (label >= base) & (label < base + resident)
        firsts = [base + 2.0 * t for t in range(tiles)]
        if h >= 2:
            firsts = [
                base + first_ref[QUAD + i].astype(jnp.float32) + 2.0 * t
                for i in range(2)
                for t in range(tiles // 2)
            ]

        @pl.when(jnp.max(jnp.where(met, 1.0, 0.0)) > 0.0)
        def _(h=h, firsts=firsts):
            step(near_refs[h][...] if h < 2 else opened_ref[h - 2], firsts)


def down_kernel(first_ref, rows_ref, *refs):
    near_refs, far_refs = refs[:2], refs[2:6]
    out_ref, opened_ref, batch_ref, picked_ref = refs[6:]
    senders, width = rows_ref.shape[0], batch_ref.shape[1]
    tiles = width // LANES - 1
    cap = out_ref.shape[0] * STEP
    dims = (((1,), (1,)), ((), ()))
    half = senders * STEP // 2
    low = lanes_of(half) < HALF
    open_far(far_refs, opened_ref)

    def one(a, carry):
        label, lowered = step_labels(cap, tiles, a, rows_ref)
        used = jnp.max(label) >= 0.0
        out_ref[a] = jnp.zeros((half, LANES), jnp.bfloat16)

        @pl.when(used)
        def _():
            shift = lax.rem(LANES - QUARTER * (a // 2), LANES)
            spot = pl.multiple_of(tiles * cap + lax.rem(a, 2) * STEP, STEP)
            for s in range(senders):
                rows = slice(s * STEP, (s + 1) * STEP)
                for t in range(tiles):
                    at = pl.multiple_of(t * cap + a * STEP, STEP)
                    batch_ref[rows, t * LANES : (t + 1) * LANES] = rows_ref[s, pl.ds(at, STEP), :]
                end = rows_ref[s, pl.ds(spot, STEP), :].astype(jnp.float32)
                batch_ref[rows, tiles * LANES :] = pltpu.roll(end, shift, 1).astype(jnp.bfloat16)
            picked_ref[...] = jnp.zeros(picked_ref.shape, jnp.float32)

            def step(weight, firsts):
                product = lax.dot_general(
                    batch_ref[...], weight, dims, preferred_element_type=jnp.float32
                )
                picked = picked_ref[...]
                for t, first in enumerate(firsts):
                    columns = slice(t * LANES, (t + 1) * LANES)
                    picked = jnp.where(lowered == first, product[:, columns], picked)
                picked_ref[...] = picked

            for_holders(first_ref, near_refs, opened_ref, label, step)
            picked = picked_ref[...]
            both = picked + pltpu.roll(picked, HALF, 1)
            out_ref[a] = jnp.where(low, both[0:half], both[half:]).astype(jnp.bfloat16)

        return carry

    lax.fori_loop(0, cap // STEP, one, 0)


def up_kernel(first_ref, rows_ref, *refs):
    sum_refs, near_refs, far_refs = refs[:QUAD], refs[QUAD : QUAD + 2], refs[QUAD + 2 : QUAD + 6]
    out_ref, opened_ref, delta_ref, ends_ref = refs[QUAD + 6 :]
    senders, width = rows_ref.shape[0], opened_ref.shape[2]
    tiles = width // LANES - 1
    cap = sum_refs[0].shape[0] * STEP
    kept = (out_ref.shape[1] - QUARTER) // tiles
    half = senders * STEP // 2
    low = lanes_of(half) < HALF
    group_lane = lanes_of(STEP) // QUARTER
    open_far(far_refs, opened_ref)
    ends_ref[...] = jnp.zeros(ends_ref.shape, jnp.float32)

    def one(a, carry):
        label, lowered = step_labels(cap, tiles, a, rows_ref)
        delta_ref[...] = jnp.zeros(delta_ref.shape, jnp.float32)

        @pl.when(jnp.max(label) >= 0.0)
        def _():
            down = sum_refs[0][a].astype(jnp.float32)
            for ref in sum_refs[1:]:
                down = down + ref[a].astype(jnp.float32)
            down = down.astype(jnp.bfloat16).astype(jnp.float32)
            turned = pltpu.roll(down, HALF, 1)
            twice = jnp.concatenate(
                [jnp.where(low, down, turned), jnp.where(low, turned, down)], axis=0
            )

            def step(weight, firsts):
                placed = [jnp.where(lowered == first, twice, 0.0) for first in firsts]
                placed = jnp.concatenate(placed, axis=1).astype(jnp.bfloat16)
                delta_ref[...] += jnp.dot(placed, weight, preferred_element_type=jnp.float32)

            for_holders(first_ref, near_refs, opened_ref, label, step)

        spot = pl.multiple_of(lax.rem(a, 2) * STEP, STEP)
        for s in range(senders):
            rows = slice(s * STEP, (s + 1) * STEP)
            for t in range(tiles):
                at = pl.multiple_of(t * kept + a * STEP, STEP)
                out_ref[s, pl.ds(at, STEP), :] = delta_ref[
                    rows, t * LANES : (t + 1) * LANES
                ].astype(jnp.bfloat16)
            turned = pltpu.roll(delta_ref[rows, tiles * LANES :], QUARTER * (a // 2), 1)
            ends_ref[s, pl.ds(spot, STEP), :] = jnp.where(
                group_lane == a // 2, turned, ends_ref[s, pl.ds(spot, STEP), :]
            )
        return carry

    lax.fori_loop(0, kept // STEP, one, 0)
    for s in range(senders):
        out_ref[s, tiles * kept :, :] = ends_ref[s].astype(jnp.bfloat16)


def mix_kernel(whole, target_ref, tokens_ref, returned_ref, out_ref):
    total = tokens_ref.shape[0]
    tiles = whole // LANES
    quads, kept = returned_ref.shape[0] // QUAD, (returned_ref.shape[1] - QUARTER) // tiles
    lane = lanes_of(total)
    spot = lax.broadcasted_iota(jnp.int32, (total, quads * kept), 1)
    place = spot // kept * total + spot % kept
    chosen = jnp.where(target_ref[...] == place, 1.0, 0.0).astype(jnp.bfloat16)
    end = jnp.zeros((total, LANES), jnp.float32)
    for j in range(QUAD):
        shares = []
        for q in range(quads):
            d = q * QUAD + j
            parts = [returned_ref[d, t * kept : (t + 1) * kept, :] for t in range(tiles)]
            packed = returned_ref[d, tiles * kept :, :].astype(jnp.float32)
            groups = [packed]
            for m in range(1, QUAD):
                groups.append(pltpu.roll(packed, LANES - QUARTER * m, 1))
            parts.append(jnp.concatenate(groups, axis=0)[0:kept].astype(jnp.bfloat16))
            shares.append(jnp.concatenate(parts, axis=1))
        share = jnp.concatenate(shares, axis=0)
        delta = jnp.dot(chosen, share, preferred_element_type=jnp.float32)
        columns = slice(j * whole, (j + 1) * whole)
        out_ref[:, columns] = (
            tokens_ref[:, columns].astype(jnp.float32) + delta[:, 0:whole]
        ).astype(jnp.bfloat16)
        last = delta[:, whole:]
        turned = pltpu.roll(last, QUARTER * j, 1) if j else last
        end = jnp.where((lane >= QUARTER * j) & (lane < QUARTER * (j + 1)), turned, end)
    out_ref[:, QUAD * whole :] = (
        tokens_ref[:, QUAD * whole :].astype(jnp.float32) + end
    ).astype(jnp.bfloat16)


def call(kernel, out_shape, in_specs, flops, moved, after=(), scratch=()):
    many = isinstance(out_shape, list)
    skipped = len(after)
    body = (lambda *refs: kernel(*refs[skipped:])) if skipped else kernel
    run = pl.pallas_call(
        body,
        out_shape=out_shape,
        in_specs=[pl.BlockSpec(memory_space=pl.ANY)] * skipped + in_specs,
        out_specs=[VMEM] * len(out_shape) if many else VMEM,
        scratch_shapes=scratch,
        compiler_params=pltpu.CompilerParams(vmem_limit_bytes=48 * 2**20),
        cost_estimate=pl.CostEstimate(flops=flops, bytes_accessed=moved, transcendentals=0),
    )
    return functools.partial(run, *after)


def exchange(value):
    return lax.all_to_all(value, "adapter", split_axis=0, concat_axis=0, tiled=True)


def towards(value, k, devices):
    return lax.ppermute(value, "adapter", [(i, i ^ k) for i in range(devices)])


def swapped(value):
    return lax.ppermute(value, "groups", [(0, 1), (1, 0)])


def back_and_mix(kept, tokens, target, first, arrived, sums, up_weights, *unused_values):
    blocks, rows, width = tokens.shape
    total = blocks * rows
    devices = arrived.shape[0]
    columns, share = up_weights[0].shape
    whole = share - LANES
    leaving = call(
        up_kernel,
        jax.ShapeDtypeStruct((devices, whole // LANES * kept + QUARTER, LANES), jnp.bfloat16),
        [SMEM] + [VMEM] * (1 + QUAD + len(up_weights)),
        2 * devices * kept * QUAD * columns * share,
        2 * (2 * devices * kept + QUAD * columns) * share,
        scratch=[
            pltpu.VMEM((2, columns, share), jnp.bfloat16),
            pltpu.VMEM((devices * STEP, share), jnp.float32),
            pltpu.VMEM((devices, QUARTER, LANES), jnp.float32),
        ],
    )(first, arrived, *sums, *up_weights)
    mixed = call(
        functools.partial(mix_kernel, whole),
        jax.ShapeDtypeStruct((total, width), jnp.bfloat16),
        [VMEM] * 3,
        2 * devices * kept * total * share,
        2 * (2 * total * width + devices * kept * share),
    )(target.reshape(total, 1), tokens.reshape(total, width), exchange(leaving))
    return mixed.reshape(tokens.shape)


def start_again(tokens, target, first, arrived, sums, up_weights, *arguments):
    return rows_to_holders(tokens, *arguments)


def rows_to_quads(
    tokens, request_block_adapter, request_block_rows, adapter_down_weight, adapter_up_weight
):
    blocks, rows, width = tokens.shape
    devices = lax.axis_size("adapter")
    resident, rank, unused_width = adapter_up_weight.shape
    total = blocks * rows
    columns = resident * rank
    whole = width // LANES // QUAD * LANES
    share = whole + LANES
    bf16, i32 = jnp.bfloat16, jnp.int32

    quad = request_block_adapter // (resident * QUAD)
    label = request_block_adapter - quad * (resident * QUAD) + 1
    order = request_block_adapter * blocks + jnp.arange(blocks, dtype=i32)
    same = quad[:, None] == quad[None, :]
    used = request_block_rows
    ahead = jnp.where(same & (order[None, :] < order[:, None]), used[None, :], 0)
    most = jnp.max(jnp.sum(jnp.where(same, used[None, :], 0), axis=1))
    row = jnp.arange(rows, dtype=i32)
    start = quad * total + jnp.sum(ahead, axis=1)
    target = jnp.where(row[None, :] < used[:, None], start[:, None] + row[None, :], -1)
    target = target.reshape(total).astype(i32)
    label = jnp.broadcast_to(label[:, None], (blocks, rows)).reshape(total, 1).astype(jnp.float32)

    me = lax.axis_index("adapter").astype(i32)
    group = lax.axis_index("groups").astype(i32)
    parts = jnp.bitwise_xor(me % QUAD, jnp.arange(QUAD, dtype=i32))
    halves = jnp.stack([group, 1 - group]) * (resident // 2)
    first = jnp.concatenate([parts * resident, halves]).astype(i32)
    tiles = whole // LANES

    def shares(weight, which, after):
        far = (columns // 2 * tiles + columns // 2 // QUAD, LANES)
        values = call(
            functools.partial(weight_kernel, whole, which),
            [jax.ShapeDtypeStruct((columns, share) if k < 2 else far, bf16) for k in which],
            [SMEM, SMEM, VMEM],
            0,
            len(which) * columns * width,
            after,
        )(parts, group.reshape(1), weight)
        return [towards(value, k, devices) if k else value for k, value in zip(which, values)]

    weight = adapter_down_weight.transpose(0, 2, 1).reshape(columns, width)
    down_weights = shares(weight, [0, 1, 2, 3], [])
    down_weights.append(swapped(down_weights[2]))
    weight = adapter_up_weight.reshape(columns, width)
    up_weights = shares(weight, [0, 1, 2], down_weights[2:3])
    up_weights += shares(weight, [3], down_weights[3:5])
    down_weights.append(swapped(down_weights[3]))
    up_weights.append(swapped(up_weights[2]))
    up_weights.append(swapped(up_weights[3]))

    caps = [total * 5 // 16, total * 6 // 16, total * 7 // 16]
    cap = caps[-1]
    arrived = exchange(
        call(
            functools.partial(pack_kernel, whole, cap),
            jax.ShapeDtypeStruct((devices, tiles * cap + QUARTER, LANES), bf16),
            [SMEM, VMEM, VMEM, VMEM],
            2 * devices * cap * total * share,
            2 * (total * width + devices * cap * share),
            scratch=[pltpu.VMEM((total, width), bf16)],
        )(most.reshape(1), target.reshape(1, total), label, tokens.reshape(total, width))
    )

    counts = arrived[:, tiles * cap + STEP, NOTE + cap // STEP].astype(jnp.float32)
    most = jnp.max(counts).reshape(1, 1)
    most = jnp.maximum(most, swapped(most))[0, 0].astype(i32)
    partial = call(
        down_kernel,
        jax.ShapeDtypeStruct((cap // STEP, devices * STEP // 2, LANES), bf16),
        [SMEM] + [VMEM] * (1 + len(down_weights)),
        2 * devices * cap * QUAD * columns * share,
        2 * (devices * cap + QUAD * columns) * share,
        up_weights[4:5],
        [
            pltpu.VMEM((2, columns, share), bf16),
            pltpu.VMEM((devices * STEP, share), bf16),
            pltpu.VMEM((devices * STEP, LANES), jnp.float32),
        ],
    )(first, arrived, *down_weights)
    sums = [partial] + [towards(partial, k, devices) for k in range(1, QUAD)]
    return lax.switch(
        sum((most > more).astype(i32) for more in caps),
        [functools.partial(back_and_mix, more) for more in caps] + [start_again],
        tokens,
        target,
        first,
        arrived,
        sums,
        up_weights,
        request_block_adapter,
        request_block_rows,
        adapter_down_weight,
        adapter_up_weight,
    )


def solution(mesh):
    placed = (
        P(("groups", "adapter"), None, None),
        P(("groups", "adapter")),
        P(("groups", "adapter")),
        P("adapter", None, None),
        P("adapter", None, None),
    )

    def per_device(tokens, request_block_adapter, request_block_rows, down_weight, up_weight):
        blocks, rows, width = tokens.shape
        devices = mesh.shape["adapter"]
        slots = max(1, 4 * blocks // devices)
        quads = devices % QUAD == 0 and slots * QUAD >= blocks
        quads = quads and width % (QUAD * LANES) == LANES and up_weight.shape[1] == HALF
        quads = quads and blocks * rows * 7 // 16 == 7 * STEP and mesh.shape["groups"] == 2
        plan = rows_to_quads if quads else rows_to_holders
        return plan(tokens, request_block_adapter, request_block_rows, down_weight, up_weight)

    return jax.shard_map(
        per_device,
        mesh=mesh,
        in_specs=placed,
        out_specs=P(("groups", "adapter"), None, None),
        check_vma=False,
    )
```

```python
import functools

import jax
import jax.numpy as jnp
from jax import lax
from jax.experimental import pallas as pl
from jax.experimental.pallas import tpu as pltpu
from jax.sharding import PartitionSpec as P

LANES = 128
HALF = 64
QUAD = 4
QUARTER = 32
STEP = 16
NOTE = 96
VMEM = pl.BlockSpec(memory_space=pltpu.VMEM)
SMEM = pl.BlockSpec(memory_space=pltpu.SMEM)


def normalise(tokens):
    values = tokens.astype(jnp.float32)
    mean_sq = jnp.mean(values * values, axis=-1, keepdims=True)
    return (values, (values * lax.rsqrt(mean_sq + 1e-06)).astype(jnp.bfloat16))


def resident_update(hidden_state, block_labels, adapter_down_weight, adapter_up_weight):
    feature_width = hidden_state.shape[-1]
    leading = hidden_state.shape[:-1]
    resident_rows, unused_value, inner_rank = adapter_down_weight.shape
    flattened_tokens = hidden_state.reshape(-1, feature_width)
    down_matrix = jnp.einsum(
        "tq,iqg->tig", flattened_tokens, adapter_down_weight, preferred_element_type=jnp.float32
    )
    down_matrix = down_matrix.astype(jnp.bfloat16).reshape(
        flattened_tokens.shape[0], resident_rows * inner_rank
    )
    column_owner = jnp.arange(resident_rows * inner_rank, dtype=jnp.int32) // inner_rank
    picked = block_labels.reshape(-1, 1) == column_owner[None, :]
    down_matrix = jnp.where(picked, down_matrix, jnp.zeros_like(down_matrix))
    lowrank_update = jnp.dot(
        down_matrix,
        adapter_up_weight.reshape(resident_rows * inner_rank, feature_width),
        preferred_element_type=jnp.float32,
    )
    return lowrank_update.astype(jnp.bfloat16).reshape(leading + (feature_width,))


def rows_to_holders(
    tokens, request_block_adapter, request_block_rows, adapter_down_weight, adapter_up_weight
):
    blocks, rows, feature_width = tokens.shape
    devices = lax.axis_size("adapter")
    resident_rows = adapter_down_weight.shape[0]
    slots = max(1, 4 * blocks // devices)
    values, normed = normalise(tokens)
    owner = request_block_adapter // resident_rows
    within = request_block_adapter - owner * resident_rows
    serial = jnp.arange(blocks, dtype=jnp.int32)
    earlier = (owner[:, None] == owner[None, :]) & (serial[None, :] < serial[:, None])
    position = owner * slots + jnp.sum(earlier, axis=1)
    outgoing = (
        jnp.zeros((devices * slots, rows, feature_width), jnp.bfloat16).at[position].set(normed)
    )
    outgoing = outgoing.reshape(devices, slots, rows, feature_width)
    block_labels = jnp.full((devices * slots,), -1, jnp.int32).at[position].set(within)
    block_labels = jnp.broadcast_to(block_labels[:, None], (devices * slots, rows)).reshape(
        devices, slots, rows
    )
    arriving_rows, row_markers = (
        lax.all_to_all(outgoing, "adapter", split_axis=0, concat_axis=0, tiled=True),
        lax.all_to_all(block_labels, "adapter", split_axis=0, concat_axis=0, tiled=True),
    )
    lowrank_update = resident_update(
        arriving_rows, row_markers, adapter_down_weight, adapter_up_weight
    )
    returned = lax.all_to_all(lowrank_update, "adapter", split_axis=0, concat_axis=0, tiled=True)
    mine = returned.reshape(devices * slots, rows, feature_width)[position]
    live = jnp.arange(rows, dtype=jnp.int32)[None, :] < request_block_rows[:, None]
    mixed = values + jnp.where(live[:, :, None], mine.astype(jnp.float32), jnp.float32(0.0))
    return mixed.astype(jnp.bfloat16)


def lanes_of(rows):
    return lax.broadcasted_iota(jnp.int32, (rows, LANES), 1)


def weight_kernel(whole, which, part_ref, group_ref, weight_ref, *out_refs):
    tiles = whole // LANES
    for k, out_ref in zip(which, out_refs):
        j = part_ref[k]
        if k < 2:
            last = weight_ref[:, QUAD * whole :].astype(jnp.float32)
            turned = pltpu.roll(last, lax.rem(LANES - QUARTER * j, LANES), 1)
            inside = lanes_of(last.shape[0]) < QUARTER
            out_ref[:, 0:whole] = weight_ref[:, pl.ds(pl.multiple_of(j * whole, LANES), whole)]
            out_ref[:, whole:] = jnp.where(inside, turned, 0.0).astype(jnp.bfloat16)
            continue
        count = weight_ref.shape[0] // 2
        start = pl.multiple_of(group_ref[0] * count, count)
        for t in range(tiles):
            column = pl.multiple_of(j * whole + t * LANES, LANES)
            out_ref[t * count : (t + 1) * count, :] = weight_ref[
                pl.ds(start, count), pl.ds(column, LANES)
            ]
        last = weight_ref[pl.ds(start, count), QUAD * whole :].astype(jnp.float32)
        size = count // QUAD
        owner = lanes_of(size) // QUARTER
        merged = jnp.zeros((size, LANES), jnp.float32)
        for m in range(QUAD):
            shift = lax.rem(LANES + QUARTER * (m - j), LANES)
            turned = pltpu.roll(last[m * size : (m + 1) * size], shift, 1)
            merged = jnp.where(owner == m, turned, merged)
        out_ref[tiles * count :, :] = merged.astype(jnp.bfloat16)


def open_far(far_refs, opened_ref):
    count, width = opened_ref.shape[1] // 2, opened_ref.shape[2]
    tiles, size = width // LANES - 1, count // QUAD
    inside = lanes_of(size) < QUARTER
    for i, ref in enumerate(far_refs):
        holder, base = i % 2, i // 2 * count
        for t in range(tiles):
            opened_ref[holder, base : base + count, t * LANES : (t + 1) * LANES] = ref[
                t * count : (t + 1) * count, :
            ]
        packed = ref[tiles * count :, :].astype(jnp.float32)
        for m in range(QUAD):
            turned = pltpu.roll(packed, (LANES - QUARTER * m) % LANES, 1) if m else packed
            opened_ref[holder, base + m * size : base + (m + 1) * size, tiles * LANES :] = (
                jnp.where(inside, turned, 0.0).astype(jnp.bfloat16)
            )


def pack_kernel(whole, cap, most_ref, target_ref, label_ref, tokens_ref, out_ref, normed_ref):
    values = tokens_ref[...].astype(jnp.float32)
    mean_sq = jnp.mean(values * values, axis=-1, keepdims=True)
    normed_ref[...] = (values * lax.rsqrt(mean_sq + 1e-06)).astype(jnp.bfloat16)
    total = tokens_ref.shape[0]
    quads, tiles = out_ref.shape[0] // QUAD, whole // LANES
    lane = lanes_of(total)
    last = normed_ref[:, QUAD * whole :].astype(jnp.float32)
    label = jnp.where(lane == QUARTER, label_ref[...], 0.0)
    ends = []
    for j in range(QUAD):
        turned = pltpu.roll(last, (LANES - QUARTER * j) % LANES, 1) if j else last
        ends.append(jnp.where(lane < QUARTER, turned, label).astype(jnp.bfloat16))
    most = most_ref[0].astype(jnp.float32)
    group_lane = lanes_of(QUARTER) // QUARTER
    step_lane = lanes_of(STEP)
    for q in range(quads):
        place = lax.broadcasted_iota(jnp.int32, (cap, total), 0) + q * total
        chosen = jnp.where(target_ref[...] == place, 1.0, 0.0).astype(jnp.bfloat16)
        for j in range(QUAD):
            share = jnp.dot(
                chosen,
                normed_ref[:, j * whole : (j + 1) * whole],
                preferred_element_type=jnp.float32,
            ).astype(jnp.bfloat16)
            for t in range(tiles):
                out_ref[q * QUAD + j, t * cap : (t + 1) * cap, :] = share[
                    :, t * LANES : (t + 1) * LANES
                ]
            end = jnp.dot(chosen, ends[j], preferred_element_type=jnp.float32)
            if j == 0:
                notes = jnp.where(step_lane == NOTE + cap // STEP, most, 0.0)
                for a in range(cap // STEP):
                    turned = pltpu.roll(end[a * STEP : (a + 1) * STEP], NOTE + a - QUARTER, 1)
                    notes = jnp.where(step_lane == NOTE + a, turned, notes)
            padded = jnp.concatenate(
                [end, jnp.zeros((QUAD * QUARTER - cap, LANES), jnp.float32)], axis=0
            )
            merged = padded[0:QUARTER]
            for m in range(1, QUAD):
                turned = pltpu.roll(padded[m * QUARTER : (m + 1) * QUARTER], m * QUARTER, 1)
                merged = jnp.where(group_lane == m, turned, merged)
            out_ref[q * QUAD + j, tiles * cap : tiles * cap + STEP, :] = merged[0:STEP].astype(
                jnp.bfloat16
            )
            out_ref[q * QUAD + j, tiles * cap + STEP :, :] = jnp.where(
                step_lane >= NOTE, notes, merged[STEP:]
            ).astype(jnp.bfloat16)


def step_labels(cap, tiles, a, rows_ref):
    columns = []
    for s in range(rows_ref.shape[0]):
        notes = rows_ref[s, tiles * cap + STEP :, :].astype(jnp.float32)
        turned = pltpu.roll(notes, lax.rem(2 * LANES - NOTE - a, LANES), 1)
        columns.append(jnp.broadcast_to(turned[:, 0:1], (STEP, LANES)))
    label = jnp.concatenate(columns, axis=0)
    return label - jnp.where(lanes_of(label.shape[0]) < HALF, 1.0, 2.0)


def for_holders(met_ref, first_ref, near_refs, opened_ref, a, step):
    tiles = opened_ref.shape[1] // LANES
    for h in range(QUAD):
        base = first_ref[h].astype(jnp.float32)
        firsts = [base + 2.0 * t for t in range(tiles)]
        if h >= 2:
            firsts = [
                base + first_ref[QUAD + i].astype(jnp.float32) + 2.0 * t
                for i in range(2)
                for t in range(tiles // 2)
            ]

        @pl.when(met_ref[a * QUAD + h] > 0)
        def _(h=h, firsts=firsts):
            step(near_refs[h][...] if h < 2 else opened_ref[h - 2], firsts)


def any_met(met_ref, a):
    return sum(met_ref[a * QUAD + h] for h in range(QUAD)) > 0


def down_kernel(met_ref, first_ref, rows_ref, *refs):
    near_refs, far_refs = refs[:2], refs[2:6]
    out_ref, opened_ref, batch_ref, picked_ref = refs[6:]
    senders, width = rows_ref.shape[0], batch_ref.shape[1]
    tiles = width // LANES - 1
    cap = out_ref.shape[0] * STEP
    dims = (((1,), (1,)), ((), ()))
    half = senders * STEP // 2
    low = lanes_of(half) < HALF
    open_far(far_refs, opened_ref)

    def one(a, carry):
        out_ref[a] = jnp.zeros((half, LANES), jnp.bfloat16)

        @pl.when(any_met(met_ref, a))
        def _():
            lowered = step_labels(cap, tiles, a, rows_ref)
            shift = lax.rem(LANES - QUARTER * (a // 2), LANES)
            spot = pl.multiple_of(tiles * cap + lax.rem(a, 2) * STEP, STEP)
            for s in range(senders):
                rows = slice(s * STEP, (s + 1) * STEP)
                for t in range(tiles):
                    at = pl.multiple_of(t * cap + a * STEP, STEP)
                    batch_ref[rows, t * LANES : (t + 1) * LANES] = rows_ref[s, pl.ds(at, STEP), :]
                end = rows_ref[s, pl.ds(spot, STEP), :].astype(jnp.float32)
                batch_ref[rows, tiles * LANES :] = pltpu.roll(end, shift, 1).astype(jnp.bfloat16)
            picked_ref[...] = jnp.zeros(picked_ref.shape, jnp.float32)

            def step(weight, firsts):
                product = lax.dot_general(
                    batch_ref[...], weight, dims, preferred_element_type=jnp.float32
                )
                picked = picked_ref[...]
                for t, first in enumerate(firsts):
                    columns = slice(t * LANES, (t + 1) * LANES)
                    picked = jnp.where(lowered == first, product[:, columns], picked)
                picked_ref[...] = picked

            for_holders(met_ref, first_ref, near_refs, opened_ref, a, step)
            picked = picked_ref[...]
            both = picked + pltpu.roll(picked, HALF, 1)
            out_ref[a] = jnp.where(low, both[0:half], both[half:]).astype(jnp.bfloat16)

        return carry

    lax.fori_loop(0, cap // STEP, one, 0)


def up_kernel(met_ref, first_ref, rows_ref, *refs):
    sum_refs, near_refs, far_refs = refs[:QUAD], refs[QUAD : QUAD + 2], refs[QUAD + 2 : QUAD + 6]
    out_ref, opened_ref, delta_ref, ends_ref = refs[QUAD + 6 :]
    senders, width = rows_ref.shape[0], opened_ref.shape[2]
    tiles = width // LANES - 1
    cap = sum_refs[0].shape[0] * STEP
    kept = (out_ref.shape[1] - QUARTER) // tiles
    half = senders * STEP // 2
    low = lanes_of(half) < HALF
    group_lane = lanes_of(STEP) // QUARTER
    open_far(far_refs, opened_ref)
    ends_ref[...] = jnp.zeros(ends_ref.shape, jnp.float32)

    def one(a, carry):
        delta_ref[...] = jnp.zeros(delta_ref.shape, jnp.float32)

        @pl.when(any_met(met_ref, a))
        def _():
            lowered = step_labels(cap, tiles, a, rows_ref)
            down = sum_refs[0][a].astype(jnp.float32)
            for ref in sum_refs[1:]:
                down = down + ref[a].astype(jnp.float32)
            down = down.astype(jnp.bfloat16).astype(jnp.float32)
            turned = pltpu.roll(down, HALF, 1)
            twice = jnp.concatenate(
                [jnp.where(low, down, turned), jnp.where(low, turned, down)], axis=0
            )

            def step(weight, firsts):
                placed = [jnp.where(lowered == first, twice, 0.0) for first in firsts]
                placed = jnp.concatenate(placed, axis=1).astype(jnp.bfloat16)
                delta_ref[...] += jnp.dot(placed, weight, preferred_element_type=jnp.float32)

            for_holders(met_ref, first_ref, near_refs, opened_ref, a, step)

        spot = pl.multiple_of(lax.rem(a, 2) * STEP, STEP)
        for s in range(senders):
            rows = slice(s * STEP, (s + 1) * STEP)
            for t in range(tiles):
                at = pl.multiple_of(t * kept + a * STEP, STEP)
                out_ref[s, pl.ds(at, STEP), :] = delta_ref[
                    rows, t * LANES : (t + 1) * LANES
                ].astype(jnp.bfloat16)
            turned = pltpu.roll(delta_ref[rows, tiles * LANES :], QUARTER * (a // 2), 1)
            ends_ref[s, pl.ds(spot, STEP), :] = jnp.where(
                group_lane == a // 2, turned, ends_ref[s, pl.ds(spot, STEP), :]
            )
        return carry

    lax.fori_loop(0, kept // STEP, one, 0)
    for s in range(senders):
        out_ref[s, tiles * kept :, :] = ends_ref[s].astype(jnp.bfloat16)


def mix_kernel(whole, target_ref, tokens_ref, returned_ref, out_ref):
    total = tokens_ref.shape[0]
    tiles = whole // LANES
    quads, kept = returned_ref.shape[0] // QUAD, (returned_ref.shape[1] - QUARTER) // tiles
    lane = lanes_of(total)
    spot = lax.broadcasted_iota(jnp.int32, (total, quads * kept), 1)
    place = spot // kept * total + spot % kept
    chosen = jnp.where(target_ref[...] == place, 1.0, 0.0).astype(jnp.bfloat16)
    end = jnp.zeros((total, LANES), jnp.float32)
    for j in range(QUAD):
        shares = []
        for q in range(quads):
            d = q * QUAD + j
            parts = [returned_ref[d, t * kept : (t + 1) * kept, :] for t in range(tiles)]
            packed = returned_ref[d, tiles * kept :, :].astype(jnp.float32)
            groups = [packed]
            for m in range(1, QUAD):
                groups.append(pltpu.roll(packed, LANES - QUARTER * m, 1))
            parts.append(jnp.concatenate(groups, axis=0)[0:kept].astype(jnp.bfloat16))
            shares.append(jnp.concatenate(parts, axis=1))
        share = jnp.concatenate(shares, axis=0)
        delta = jnp.dot(chosen, share, preferred_element_type=jnp.float32)
        columns = slice(j * whole, (j + 1) * whole)
        out_ref[:, columns] = (
            tokens_ref[:, columns].astype(jnp.float32) + delta[:, 0:whole]
        ).astype(jnp.bfloat16)
        last = delta[:, whole:]
        turned = pltpu.roll(last, QUARTER * j, 1) if j else last
        end = jnp.where((lane >= QUARTER * j) & (lane < QUARTER * (j + 1)), turned, end)
    out_ref[:, QUAD * whole :] = (
        tokens_ref[:, QUAD * whole :].astype(jnp.float32) + end
    ).astype(jnp.bfloat16)


def call(kernel, out_shape, in_specs, flops, moved, after=(), scratch=()):
    many = isinstance(out_shape, list)
    skipped = len(after)
    body = (lambda *refs: kernel(*refs[skipped:])) if skipped else kernel
    run = pl.pallas_call(
        body,
        out_shape=out_shape,
        in_specs=[pl.BlockSpec(memory_space=pl.ANY)] * skipped + in_specs,
        out_specs=[VMEM] * len(out_shape) if many else VMEM,
        scratch_shapes=scratch,
        compiler_params=pltpu.CompilerParams(vmem_limit_bytes=48 * 2**20),
        cost_estimate=pl.CostEstimate(flops=flops, bytes_accessed=moved, transcendentals=0),
    )
    return functools.partial(run, *after)


def exchange(value):
    return lax.all_to_all(value, "adapter", split_axis=0, concat_axis=0, tiled=True)


def towards(value, k, devices):
    return lax.ppermute(value, "adapter", [(i, i ^ k) for i in range(devices)])


def swapped(value):
    return lax.ppermute(value, "groups", [(0, 1), (1, 0)])


def back_and_mix(kept, tokens, target, met, first, arrived, sums, up_weights, *unused_values):
    blocks, rows, width = tokens.shape
    total = blocks * rows
    devices = arrived.shape[0]
    columns, share = up_weights[0].shape
    whole = share - LANES
    leaving = call(
        up_kernel,
        jax.ShapeDtypeStruct((devices, whole // LANES * kept + QUARTER, LANES), jnp.bfloat16),
        [SMEM] * 2 + [VMEM] * (1 + QUAD + len(up_weights)),
        2 * devices * kept * QUAD * columns * share,
        2 * (2 * devices * kept + QUAD * columns) * share,
        scratch=[
            pltpu.VMEM((2, columns, share), jnp.bfloat16),
            pltpu.VMEM((devices * STEP, share), jnp.float32),
            pltpu.VMEM((devices, QUARTER, LANES), jnp.float32),
        ],
    )(met, first, arrived, *sums, *up_weights)
    mixed = call(
        functools.partial(mix_kernel, whole),
        jax.ShapeDtypeStruct((total, width), jnp.bfloat16),
        [VMEM] * 3,
        2 * devices * kept * total * share,
        2 * (2 * total * width + devices * kept * share),
    )(target.reshape(total, 1), tokens.reshape(total, width), exchange(leaving))
    return mixed.reshape(tokens.shape)


def start_again(tokens, target, met, first, arrived, sums, up_weights, *arguments):
    return rows_to_holders(tokens, *arguments)


def rows_to_quads(
    tokens, request_block_adapter, request_block_rows, adapter_down_weight, adapter_up_weight
):
    blocks, rows, width = tokens.shape
    devices = lax.axis_size("adapter")
    resident, rank, unused_width = adapter_up_weight.shape
    total = blocks * rows
    columns = resident * rank
    whole = width // LANES // QUAD * LANES
    share = whole + LANES
    bf16, i32 = jnp.bfloat16, jnp.int32

    quad = request_block_adapter // (resident * QUAD)
    label = request_block_adapter - quad * (resident * QUAD) + 1
    order = request_block_adapter * blocks + jnp.arange(blocks, dtype=i32)
    same = quad[:, None] == quad[None, :]
    used = request_block_rows
    ahead = jnp.where(same & (order[None, :] < order[:, None]), used[None, :], 0)
    most = jnp.max(jnp.sum(jnp.where(same, used[None, :], 0), axis=1)).astype(jnp.float32)
    most = jnp.maximum(most, swapped(most.reshape(1, 1))[0, 0]).astype(i32)
    row = jnp.arange(rows, dtype=i32)
    start = quad * total + jnp.sum(ahead, axis=1)
    target = jnp.where(row[None, :] < used[:, None], start[:, None] + row[None, :], -1)
    target = target.reshape(total).astype(i32)
    label = jnp.broadcast_to(label[:, None], (blocks, rows)).reshape(total, 1).astype(jnp.float32)

    me = lax.axis_index("adapter").astype(i32)
    group = lax.axis_index("groups").astype(i32)
    parts = jnp.bitwise_xor(me % QUAD, jnp.arange(QUAD, dtype=i32))
    halves = jnp.stack([group, 1 - group]) * (resident // 2)
    first = jnp.concatenate([parts * resident, halves]).astype(i32)
    tiles = whole // LANES

    def shares(weight, which, after):
        far = (columns // 2 * tiles + columns // 2 // QUAD, LANES)
        values = call(
            functools.partial(weight_kernel, whole, which),
            [jax.ShapeDtypeStruct((columns, share) if k < 2 else far, bf16) for k in which],
            [SMEM, SMEM, VMEM],
            0,
            len(which) * columns * width,
            after,
        )(parts, group.reshape(1), weight)
        return [towards(value, k, devices) if k else value for k, value in zip(which, values)]

    weight = adapter_down_weight.transpose(0, 2, 1).reshape(columns, width)
    down_weights = shares(weight, [0, 1, 2, 3], [])
    down_weights.append(swapped(down_weights[2]))
    weight = adapter_up_weight.reshape(columns, width)
    up_weights = shares(weight, [0, 1, 2], down_weights[2:3])
    up_weights += shares(weight, [3], down_weights[3:5])
    down_weights.append(swapped(down_weights[3]))
    up_weights.append(swapped(up_weights[2]))
    up_weights.append(swapped(up_weights[3]))

    caps = [total * 5 // 16, total * 6 // 16, total * 7 // 16]
    cap = caps[-1]
    arrived = exchange(
        call(
            functools.partial(pack_kernel, whole, cap),
            jax.ShapeDtypeStruct((devices, tiles * cap + QUARTER, LANES), bf16),
            [SMEM, VMEM, VMEM, VMEM],
            2 * devices * cap * total * share,
            2 * (total * width + devices * cap * share),
            down_weights[:1],
            [pltpu.VMEM((total, width), bf16)],
        )(most.reshape(1), target.reshape(1, total), label, tokens.reshape(total, width))
    )

    notes = arrived[:, tiles * cap + STEP :, NOTE : NOTE + cap // STEP + 1].astype(jnp.float32)
    most = jnp.max(notes[:, 0, -1]).astype(i32)
    holder = jnp.floor((notes[:, :, :-1] - 1.0) * (1.0 / resident)).astype(i32)
    met = jnp.any(holder[..., None] == parts, axis=(0, 1)).astype(i32).reshape(-1)
    partial = call(
        down_kernel,
        jax.ShapeDtypeStruct((cap // STEP, devices * STEP // 2, LANES), bf16),
        [SMEM] * 2 + [VMEM] * (1 + len(down_weights)),
        0,
        0,
        up_weights[4:5],
        [
            pltpu.VMEM((2, columns, share), bf16),
            pltpu.VMEM((devices * STEP, share), bf16),
            pltpu.VMEM((devices * STEP, LANES), jnp.float32),
        ],
    )(met, first, arrived, *down_weights)
    sums = [partial] + [towards(partial, k, devices) for k in range(1, QUAD)]
    return lax.switch(
        sum((most > more).astype(i32) for more in caps),
        [functools.partial(back_and_mix, more) for more in caps] + [start_again],
        tokens,
        target,
        met,
        first,
        arrived,
        sums,
        up_weights,
        request_block_adapter,
        request_block_rows,
        adapter_down_weight,
        adapter_up_weight,
    )


def solution(mesh):
    placed = (
        P(("groups", "adapter"), None, None),
        P(("groups", "adapter")),
        P(("groups", "adapter")),
        P("adapter", None, None),
        P("adapter", None, None),
    )

    def per_device(tokens, request_block_adapter, request_block_rows, down_weight, up_weight):
        blocks, rows, width = tokens.shape
        devices = mesh.shape["adapter"]
        slots = max(1, 4 * blocks // devices)
        quads = devices % QUAD == 0 and slots * QUAD >= blocks
        quads = quads and width % (QUAD * LANES) == LANES and up_weight.shape[1] == HALF
        quads = quads and blocks * rows * 7 // 16 == 7 * STEP and mesh.shape["groups"] == 2
        plan = rows_to_quads if quads else rows_to_holders
        return plan(tokens, request_block_adapter, request_block_rows, down_weight, up_weight)

    return jax.shard_map(
        per_device,
        mesh=mesh,
        in_specs=placed,
        out_specs=P(("groups", "adapter"), None, None),
        check_vma=False,
    )
```

```python
import functools

import jax
import jax.numpy as jnp
from jax import lax
from jax.experimental import pallas as pl
from jax.experimental.pallas import tpu as pltpu
from jax.sharding import PartitionSpec as P

LANES = 128
HALF = 64
QUAD = 4
QUARTER = 32
STEP = 16
NOTE = 96
VMEM = pl.BlockSpec(memory_space=pltpu.VMEM)
SMEM = pl.BlockSpec(memory_space=pltpu.SMEM)


def normalise(tokens):
    values = tokens.astype(jnp.float32)
    mean_sq = jnp.mean(values * values, axis=-1, keepdims=True)
    return (values, (values * lax.rsqrt(mean_sq + 1e-06)).astype(jnp.bfloat16))


def resident_update(hidden_state, block_labels, adapter_down_weight, adapter_up_weight):
    feature_width = hidden_state.shape[-1]
    leading = hidden_state.shape[:-1]
    resident_rows, unused_value, inner_rank = adapter_down_weight.shape
    flattened_tokens = hidden_state.reshape(-1, feature_width)
    down_matrix = jnp.einsum(
        "tq,iqg->tig", flattened_tokens, adapter_down_weight, preferred_element_type=jnp.float32
    )
    down_matrix = down_matrix.astype(jnp.bfloat16).reshape(
        flattened_tokens.shape[0], resident_rows * inner_rank
    )
    column_owner = jnp.arange(resident_rows * inner_rank, dtype=jnp.int32) // inner_rank
    picked = block_labels.reshape(-1, 1) == column_owner[None, :]
    down_matrix = jnp.where(picked, down_matrix, jnp.zeros_like(down_matrix))
    lowrank_update = jnp.dot(
        down_matrix,
        adapter_up_weight.reshape(resident_rows * inner_rank, feature_width),
        preferred_element_type=jnp.float32,
    )
    return lowrank_update.astype(jnp.bfloat16).reshape(leading + (feature_width,))


def rows_to_holders(
    tokens, request_block_adapter, request_block_rows, adapter_down_weight, adapter_up_weight
):
    blocks, rows, feature_width = tokens.shape
    devices = lax.axis_size("adapter")
    resident_rows = adapter_down_weight.shape[0]
    slots = max(1, 4 * blocks // devices)
    values, normed = normalise(tokens)
    owner = request_block_adapter // resident_rows
    within = request_block_adapter - owner * resident_rows
    serial = jnp.arange(blocks, dtype=jnp.int32)
    earlier = (owner[:, None] == owner[None, :]) & (serial[None, :] < serial[:, None])
    position = owner * slots + jnp.sum(earlier, axis=1)
    outgoing = (
        jnp.zeros((devices * slots, rows, feature_width), jnp.bfloat16).at[position].set(normed)
    )
    outgoing = outgoing.reshape(devices, slots, rows, feature_width)
    block_labels = jnp.full((devices * slots,), -1, jnp.int32).at[position].set(within)
    block_labels = jnp.broadcast_to(block_labels[:, None], (devices * slots, rows)).reshape(
        devices, slots, rows
    )
    arriving_rows, row_markers = (
        lax.all_to_all(outgoing, "adapter", split_axis=0, concat_axis=0, tiled=True),
        lax.all_to_all(block_labels, "adapter", split_axis=0, concat_axis=0, tiled=True),
    )
    lowrank_update = resident_update(
        arriving_rows, row_markers, adapter_down_weight, adapter_up_weight
    )
    returned = lax.all_to_all(lowrank_update, "adapter", split_axis=0, concat_axis=0, tiled=True)
    mine = returned.reshape(devices * slots, rows, feature_width)[position]
    live = jnp.arange(rows, dtype=jnp.int32)[None, :] < request_block_rows[:, None]
    mixed = values + jnp.where(live[:, :, None], mine.astype(jnp.float32), jnp.float32(0.0))
    return mixed.astype(jnp.bfloat16)


def lanes_of(rows):
    return lax.broadcasted_iota(jnp.int32, (rows, LANES), 1)


def weight_kernel(whole, which, part_ref, group_ref, weight_ref, *out_refs):
    tiles = whole // LANES
    for k, out_ref in zip(which, out_refs):
        j = part_ref[k]
        if k < 2:
            last = weight_ref[:, QUAD * whole :].astype(jnp.float32)
            turned = pltpu.roll(last, lax.rem(LANES - QUARTER * j, LANES), 1)
            inside = lanes_of(last.shape[0]) < QUARTER
            out_ref[:, 0:whole] = weight_ref[:, pl.ds(pl.multiple_of(j * whole, LANES), whole)]
            out_ref[:, whole:] = jnp.where(inside, turned, 0.0).astype(jnp.bfloat16)
            continue
        count = weight_ref.shape[0] // 2
        start = pl.multiple_of(group_ref[0] * count, count)
        for t in range(tiles):
            column = pl.multiple_of(j * whole + t * LANES, LANES)
            out_ref[t * count : (t + 1) * count, :] = weight_ref[
                pl.ds(start, count), pl.ds(column, LANES)
            ]
        last = weight_ref[pl.ds(start, count), QUAD * whole :].astype(jnp.float32)
        size = count // QUAD
        owner = lanes_of(size) // QUARTER
        merged = jnp.zeros((size, LANES), jnp.float32)
        for m in range(QUAD):
            shift = lax.rem(LANES + QUARTER * (m - j), LANES)
            turned = pltpu.roll(last[m * size : (m + 1) * size], shift, 1)
            merged = jnp.where(owner == m, turned, merged)
        out_ref[tiles * count :, :] = merged.astype(jnp.bfloat16)


def open_far(far_refs, opened_ref):
    count, width = opened_ref.shape[1] // 2, opened_ref.shape[2]
    tiles, size = width // LANES - 1, count // QUAD
    inside = lanes_of(size) < QUARTER
    for i, ref in enumerate(far_refs):
        holder, base = i % 2, i // 2 * count
        for t in range(tiles):
            opened_ref[holder, base : base + count, t * LANES : (t + 1) * LANES] = ref[
                t * count : (t + 1) * count, :
            ]
        packed = ref[tiles * count :, :].astype(jnp.float32)
        for m in range(QUAD):
            turned = pltpu.roll(packed, (LANES - QUARTER * m) % LANES, 1) if m else packed
            opened_ref[holder, base + m * size : base + (m + 1) * size, tiles * LANES :] = (
                jnp.where(inside, turned, 0.0).astype(jnp.bfloat16)
            )


def pack_kernel(whole, cap, most_ref, target_ref, label_ref, tokens_ref, out_ref, normed_ref):
    values = tokens_ref[...].astype(jnp.float32)
    mean_sq = jnp.mean(values * values, axis=-1, keepdims=True)
    normed_ref[...] = (values * lax.rsqrt(mean_sq + 1e-06)).astype(jnp.bfloat16)
    total = tokens_ref.shape[0]
    quads, tiles = out_ref.shape[0] // QUAD, whole // LANES
    lane = lanes_of(total)
    last = normed_ref[:, QUAD * whole :].astype(jnp.float32)
    label = jnp.where(lane == QUARTER, label_ref[...], 0.0)
    ends = []
    for j in range(QUAD):
        turned = pltpu.roll(last, (LANES - QUARTER * j) % LANES, 1) if j else last
        ends.append(jnp.where(lane < QUARTER, turned, label).astype(jnp.bfloat16))
    most = most_ref[0].astype(jnp.float32)
    group_lane = lanes_of(QUARTER) // QUARTER
    step_lane = lanes_of(STEP)
    for q in range(quads):
        place = lax.broadcasted_iota(jnp.int32, (cap, total), 0) + q * total
        chosen = jnp.where(target_ref[...] == place, 1.0, 0.0).astype(jnp.bfloat16)
        for j in range(QUAD):
            share = jnp.dot(
                chosen,
                normed_ref[:, j * whole : (j + 1) * whole],
                preferred_element_type=jnp.float32,
            ).astype(jnp.bfloat16)
            for t in range(tiles):
                out_ref[q * QUAD + j, t * cap : (t + 1) * cap, :] = share[
                    :, t * LANES : (t + 1) * LANES
                ]
            end = jnp.dot(chosen, ends[j], preferred_element_type=jnp.float32)
            if j == 0:
                notes = jnp.where(step_lane == NOTE + cap // STEP, most, 0.0)
                for a in range(cap // STEP):
                    turned = pltpu.roll(end[a * STEP : (a + 1) * STEP], NOTE + a - QUARTER, 1)
                    notes = jnp.where(step_lane == NOTE + a, turned, notes)
            padded = jnp.concatenate(
                [end, jnp.zeros((QUAD * QUARTER - cap, LANES), jnp.float32)], axis=0
            )
            merged = padded[0:QUARTER]
            for m in range(1, QUAD):
                turned = pltpu.roll(padded[m * QUARTER : (m + 1) * QUARTER], m * QUARTER, 1)
                merged = jnp.where(group_lane == m, turned, merged)
            out_ref[q * QUAD + j, tiles * cap : tiles * cap + STEP, :] = merged[0:STEP].astype(
                jnp.bfloat16
            )
            out_ref[q * QUAD + j, tiles * cap + STEP :, :] = jnp.where(
                step_lane >= NOTE, notes, merged[STEP:]
            ).astype(jnp.bfloat16)


def read_notes(rows_ref, cap, tiles, part_ref, resident, notes_ref, labels_ref, met_ref):
    senders = rows_ref.shape[0]
    for s in range(senders):
        notes_ref[s * STEP : (s + 1) * STEP, :] = rows_ref[s, tiles * cap + STEP :, :]
    steps = labels_ref.shape[0]
    row = lax.broadcasted_iota(jnp.int32, (steps, LANES), 0)
    wanted = jnp.where(lanes_of(steps) == NOTE + row, 1.0, 0.0).astype(jnp.bfloat16)
    labels = lax.dot_general(
        wanted, notes_ref[...], (((1,), (1,)), ((), ())), preferred_element_type=jnp.float32
    )
    labels_ref[...] = labels
    code = jnp.zeros((steps, 1), jnp.float32)
    for h in range(QUAD):
        first = part_ref[h].astype(jnp.float32) + 1.0
        met = jnp.where((labels >= first) & (labels < first + resident), 1.0, 0.0)
        code = code + (1 << h) * jnp.max(met, axis=1, keepdims=True)
    at = lax.broadcasted_iota(jnp.int32, (steps, 1), 0)
    for a in range(cap // STEP):
        met_ref[a] = jnp.max(jnp.where(at == a, code, 0.0)).astype(jnp.int32)


def for_holders(met_ref, first_ref, near_refs, opened_ref, a, step):
    pairs = opened_ref.shape[1] // LANES
    for h in range(QUAD):
        base = first_ref[h].astype(jnp.float32) + 1.0
        firsts = [base + 2.0 * t for t in range(pairs)]
        if h >= 2:
            firsts = [
                base + first_ref[QUAD + i].astype(jnp.float32) + 2.0 * t
                for i in range(2)
                for t in range(pairs // 2)
            ]

        @pl.when(lax.rem(met_ref[a] // (1 << h), 2) > 0)
        def _(h=h, firsts=firsts):
            step(near_refs[h] if h < 2 else opened_ref.at[h - 2], firsts)


def down_kernel(first_ref, rows_ref, *refs):
    near_refs, far_refs, out_ref = refs[:2], refs[2:6], refs[6]
    opened_ref, batch_ref, picked_ref, notes_ref, labels_ref, met_ref = refs[7:]
    senders, width = rows_ref.shape[0], batch_ref.shape[1]
    tiles = width // LANES - 1
    cap = out_ref.shape[0] * STEP
    rank = out_ref.shape[1]
    resident = opened_ref.shape[1] // rank
    dims = (((1,), (1,)), ((), ()))
    read_notes(rows_ref, cap, tiles, first_ref, resident, notes_ref, labels_ref, met_ref)
    open_far(far_refs, opened_ref)

    def one(a, carry):
        picked_ref[...] = jnp.zeros(picked_ref.shape, jnp.float32)

        @pl.when(met_ref[a] > 0)
        def _():
            shift = lax.rem(LANES - QUARTER * (a // 2), LANES)
            spot = pl.multiple_of(tiles * cap + lax.rem(a, 2) * STEP, STEP)
            for s in range(senders):
                rows = slice(s * STEP, (s + 1) * STEP)
                for t in range(tiles):
                    at = pl.multiple_of(t * cap + a * STEP, STEP)
                    batch_ref[rows, t * LANES : (t + 1) * LANES] = rows_ref[s, pl.ds(at, STEP), :]
                end = rows_ref[s, pl.ds(spot, STEP), :].astype(jnp.float32)
                batch_ref[rows, tiles * LANES :] = pltpu.roll(end, shift, 1).astype(jnp.bfloat16)
            label = labels_ref[pl.ds(a, 1), :]

            def step(weight_ref, firsts):
                product = lax.dot_general(
                    weight_ref[...], batch_ref[...], dims, preferred_element_type=jnp.float32
                )
                picked = picked_ref[...]
                for t, first in enumerate(firsts):
                    for i in range(2):
                        at = (2 * t + i) * rank
                        picked = jnp.where(
                            label == first + i, product[at : at + rank, :], picked
                        )
                picked_ref[...] = picked

            for_holders(met_ref, first_ref, near_refs, opened_ref, a, step)

        out_ref[a] = picked_ref[...].astype(jnp.bfloat16)
        return carry

    lax.fori_loop(0, cap // STEP, one, 0)


def up_kernel(first_ref, rows_ref, *refs):
    sum_refs, near_refs, far_refs = refs[:QUAD], refs[QUAD : QUAD + 2], refs[QUAD + 2 : QUAD + 6]
    out_ref, opened_ref, delta_ref, ends_ref, notes_ref, labels_ref, met_ref = refs[QUAD + 6 :]
    senders, width = rows_ref.shape[0], opened_ref.shape[2]
    tiles = width // LANES - 1
    cap, rank = sum_refs[0].shape[0] * STEP, sum_refs[0].shape[1]
    resident = opened_ref.shape[1] // rank
    kept = (out_ref.shape[1] - QUARTER) // tiles
    group_lane = lanes_of(STEP) // QUARTER
    read_notes(rows_ref, cap, tiles, first_ref, resident, notes_ref, labels_ref, met_ref)
    open_far(far_refs, opened_ref)
    ends_ref[...] = jnp.zeros(ends_ref.shape, jnp.float32)
    low = jnp.where(lanes_of(senders * STEP) < HALF, 0.0, 1.0)
    rank_row = lax.broadcasted_iota(jnp.int32, (rank, LANES), 0)
    twofold = jnp.where(lax.rem(lanes_of(rank), rank) == rank_row, 1.0, 0.0).astype(jnp.bfloat16)

    def one(a, carry):
        delta_ref[...] = jnp.zeros(delta_ref.shape, jnp.float32)

        @pl.when(met_ref[a] > 0)
        def _():
            note_row = lax.broadcasted_iota(jnp.int32, (LANES, LANES), 0)
            wanted = jnp.where(note_row == NOTE + a, 1.0, 0.0).astype(jnp.bfloat16)
            label = jnp.dot(notes_ref[...], wanted, preferred_element_type=jnp.float32) - low
            down = sum_refs[0][a].astype(jnp.float32)
            for ref in sum_refs[1:]:
                down = down + ref[a].astype(jnp.float32)
            twice = lax.dot_general(
                down.astype(jnp.bfloat16),
                twofold,
                (((0,), (0,)), ((), ())),
                preferred_element_type=jnp.float32,
            )

            def step(weight_ref, firsts):
                placed = [jnp.where(label == first, twice, 0.0) for first in firsts]
                placed = jnp.concatenate(placed, axis=1).astype(jnp.bfloat16)
                delta_ref[...] += jnp.dot(
                    placed, weight_ref[...], preferred_element_type=jnp.float32
                )

            for_holders(met_ref, first_ref, near_refs, opened_ref, a, step)

        spot = pl.multiple_of(lax.rem(a, 2) * STEP, STEP)
        for s in range(senders):
            rows = slice(s * STEP, (s + 1) * STEP)
            for t in range(tiles):
                at = pl.multiple_of(t * kept + a * STEP, STEP)
                out_ref[s, pl.ds(at, STEP), :] = delta_ref[
                    rows, t * LANES : (t + 1) * LANES
                ].astype(jnp.bfloat16)
            turned = pltpu.roll(delta_ref[rows, tiles * LANES :], QUARTER * (a // 2), 1)
            ends_ref[s, pl.ds(spot, STEP), :] = jnp.where(
                group_lane == a // 2, turned, ends_ref[s, pl.ds(spot, STEP), :]
            )
        return carry

    lax.fori_loop(0, kept // STEP, one, 0)
    for s in range(senders):
        out_ref[s, tiles * kept :, :] = ends_ref[s].astype(jnp.bfloat16)


def mix_kernel(whole, target_ref, tokens_ref, returned_ref, out_ref):
    total = tokens_ref.shape[0]
    tiles = whole // LANES
    quads, kept = returned_ref.shape[0] // QUAD, (returned_ref.shape[1] - QUARTER) // tiles
    lane = lanes_of(total)
    spot = lax.broadcasted_iota(jnp.int32, (total, quads * kept), 1)
    place = spot // kept * total + spot % kept
    chosen = jnp.where(target_ref[...] == place, 1.0, 0.0).astype(jnp.bfloat16)
    end = jnp.zeros((total, LANES), jnp.float32)
    for j in range(QUAD):
        shares = []
        for q in range(quads):
            d = q * QUAD + j
            parts = [returned_ref[d, t * kept : (t + 1) * kept, :] for t in range(tiles)]
            packed = returned_ref[d, tiles * kept :, :].astype(jnp.float32)
            groups = [packed]
            for m in range(1, QUAD):
                groups.append(pltpu.roll(packed, LANES - QUARTER * m, 1))
            parts.append(jnp.concatenate(groups, axis=0)[0:kept].astype(jnp.bfloat16))
            shares.append(jnp.concatenate(parts, axis=1))
        share = jnp.concatenate(shares, axis=0)
        delta = jnp.dot(chosen, share, preferred_element_type=jnp.float32)
        columns = slice(j * whole, (j + 1) * whole)
        out_ref[:, columns] = (
            tokens_ref[:, columns].astype(jnp.float32) + delta[:, 0:whole]
        ).astype(jnp.bfloat16)
        last = delta[:, whole:]
        turned = pltpu.roll(last, QUARTER * j, 1) if j else last
        end = jnp.where((lane >= QUARTER * j) & (lane < QUARTER * (j + 1)), turned, end)
    out_ref[:, QUAD * whole :] = (
        tokens_ref[:, QUAD * whole :].astype(jnp.float32) + end
    ).astype(jnp.bfloat16)


def call(kernel, out_shape, in_specs, flops, moved, after=(), scratch=()):
    many = isinstance(out_shape, list)
    skipped = len(after)
    body = (lambda *refs: kernel(*refs[skipped:])) if skipped else kernel
    run = pl.pallas_call(
        body,
        out_shape=out_shape,
        in_specs=[pl.BlockSpec(memory_space=pl.ANY)] * skipped + in_specs,
        out_specs=[VMEM] * len(out_shape) if many else VMEM,
        scratch_shapes=scratch,
        compiler_params=pltpu.CompilerParams(vmem_limit_bytes=48 * 2**20),
        cost_estimate=pl.CostEstimate(flops=flops, bytes_accessed=moved, transcendentals=0),
    )
    return functools.partial(run, *after)


def exchange(value):
    return lax.all_to_all(value, "adapter", split_axis=0, concat_axis=0, tiled=True)


def towards(value, k, devices):
    return lax.ppermute(value, "adapter", [(i, i ^ k) for i in range(devices)])


def swapped(value):
    return lax.ppermute(value, "groups", [(0, 1), (1, 0)])


def note_scratch(devices):
    return [
        pltpu.VMEM((devices * STEP, LANES), jnp.bfloat16),
        pltpu.VMEM((8, devices * STEP), jnp.float32),
        pltpu.SMEM((8,), jnp.int32),
    ]


def stand_behind(value, *earlier):
    return pl.pallas_call(
        lambda *refs: None,
        out_shape=jax.ShapeDtypeStruct(value.shape, value.dtype),
        in_specs=[pl.BlockSpec(memory_space=pl.ANY)] * (1 + len(earlier)),
        out_specs=pl.BlockSpec(memory_space=pl.ANY),
        input_output_aliases={0: 0},
    )(value, *earlier)


def back_and_mix(kept, tokens, target, first, arrived, sums, up_weights, *unused_values):
    blocks, rows, width = tokens.shape
    total = blocks * rows
    devices = arrived.shape[0]
    columns, share = up_weights[0].shape
    whole = share - LANES
    leaving = call(
        up_kernel,
        jax.ShapeDtypeStruct((devices, whole // LANES * kept + QUARTER, LANES), jnp.bfloat16),
        [SMEM] + [VMEM] * (1 + QUAD + len(up_weights)),
        2 * devices * kept * QUAD * columns * share,
        2 * (2 * devices * kept + QUAD * columns) * share,
        scratch=[
            pltpu.VMEM((2, columns, share), jnp.bfloat16),
            pltpu.VMEM((devices * STEP, share), jnp.float32),
            pltpu.VMEM((devices, QUARTER, LANES), jnp.float32),
            *note_scratch(devices),
        ],
    )(first, arrived, *sums, *up_weights)
    mixed = call(
        functools.partial(mix_kernel, whole),
        jax.ShapeDtypeStruct((total, width), jnp.bfloat16),
        [VMEM] * 3,
        2 * devices * kept * total * share,
        2 * (2 * total * width + devices * kept * share),
    )(target.reshape(total, 1), tokens.reshape(total, width), exchange(leaving))
    return mixed.reshape(tokens.shape)


def start_again(tokens, target, first, arrived, sums, up_weights, *arguments):
    return rows_to_holders(tokens, *arguments)


def rows_to_quads(
    tokens, request_block_adapter, request_block_rows, adapter_down_weight, adapter_up_weight
):
    blocks, rows, width = tokens.shape
    devices = lax.axis_size("adapter")
    resident, rank, unused_width = adapter_up_weight.shape
    total = blocks * rows
    columns = resident * rank
    whole = width // LANES // QUAD * LANES
    share = whole + LANES
    bf16, i32 = jnp.bfloat16, jnp.int32

    quad = request_block_adapter // (resident * QUAD)
    label = request_block_adapter - quad * (resident * QUAD) + 1
    order = request_block_adapter * blocks + jnp.arange(blocks, dtype=i32)
    same = quad[:, None] == quad[None, :]
    used = request_block_rows
    ahead = jnp.where(same & (order[None, :] < order[:, None]), used[None, :], 0)
    most = jnp.max(jnp.sum(jnp.where(same, used[None, :], 0), axis=1)).astype(jnp.float32)
    most = jnp.maximum(most, swapped(most.reshape(1, 1))[0, 0]).astype(i32)
    row = jnp.arange(rows, dtype=i32)
    start = quad * total + jnp.sum(ahead, axis=1)
    target = jnp.where(row[None, :] < used[:, None], start[:, None] + row[None, :], -1)
    target = target.reshape(total).astype(i32)
    label = jnp.broadcast_to(label[:, None], (blocks, rows)).reshape(total, 1).astype(jnp.float32)

    me = lax.axis_index("adapter").astype(i32)
    group = lax.axis_index("groups").astype(i32)
    parts = jnp.bitwise_xor(me % QUAD, jnp.arange(QUAD, dtype=i32))
    halves = jnp.stack([group, 1 - group]) * (resident // 2)
    first = jnp.concatenate([parts * resident, halves]).astype(i32)
    tiles = whole // LANES

    def shares(weight, which, after):
        far = (columns // 2 * tiles + columns // 2 // QUAD, LANES)
        values = call(
            functools.partial(weight_kernel, whole, which),
            [jax.ShapeDtypeStruct((columns, share) if k < 2 else far, bf16) for k in which],
            [SMEM, SMEM, VMEM],
            0,
            len(which) * columns * width,
            after,
        )(parts, group.reshape(1), weight)
        return [towards(value, k, devices) if k else value for k, value in zip(which, values)]

    weight = adapter_down_weight.transpose(0, 2, 1).reshape(columns, width)
    down_weights = shares(weight, [0, 1, 2, 3], [])
    down_weights.append(swapped(down_weights[2]))
    weight = adapter_up_weight.reshape(columns, width)
    up_weights = shares(weight, [0, 1, 2], down_weights[2:3])
    up_weights += shares(weight, [3], down_weights[3:5])
    down_weights.append(swapped(down_weights[3]))
    up_weights.append(swapped(up_weights[2]))

    caps = [total * 5 // 16, total * 6 // 16, total * 7 // 16]
    cap = caps[-1]
    arrived = exchange(
        call(
            functools.partial(pack_kernel, whole, cap),
            jax.ShapeDtypeStruct((devices, tiles * cap + QUARTER, LANES), bf16),
            [SMEM, VMEM, VMEM, VMEM],
            2 * devices * cap * total * share,
            2 * (total * width + devices * cap * share),
            down_weights[:1],
            [pltpu.VMEM((total, width), bf16)],
        )(most.reshape(1), target.reshape(1, total), label, tokens.reshape(total, width))
    )

    counts = arrived[:, tiles * cap + STEP, NOTE + cap // STEP].astype(jnp.float32)
    most = jnp.max(counts).astype(i32)
    partial = call(
        down_kernel,
        jax.ShapeDtypeStruct((cap // STEP, rank, devices * STEP), bf16),
        [SMEM] + [VMEM] * (1 + len(down_weights)),
        0,
        0,
        up_weights[2:3],
        [
            pltpu.VMEM((2, columns, share), bf16),
            pltpu.VMEM((devices * STEP, share), bf16),
            pltpu.VMEM((rank, devices * STEP), jnp.float32),
            *note_scratch(devices),
        ],
    )(first, arrived, *down_weights)
    up_weights[3] = stand_behind(up_weights[3], partial)
    up_weights.append(swapped(up_weights[3]))
    sums = [partial] + [towards(partial, k, devices) for k in range(1, QUAD)]
    return lax.switch(
        sum((most > more).astype(i32) for more in caps),
        [functools.partial(back_and_mix, more) for more in caps] + [start_again],
        tokens,
        target,
        first,
        arrived,
        sums,
        up_weights,
        request_block_adapter,
        request_block_rows,
        adapter_down_weight,
        adapter_up_weight,
    )


def solution(mesh):
    placed = (
        P(("groups", "adapter"), None, None),
        P(("groups", "adapter")),
        P(("groups", "adapter")),
        P("adapter", None, None),
        P("adapter", None, None),
    )

    def per_device(tokens, request_block_adapter, request_block_rows, down_weight, up_weight):
        blocks, rows, width = tokens.shape
        devices = mesh.shape["adapter"]
        slots = max(1, 4 * blocks // devices)
        quads = devices % QUAD == 0 and slots * QUAD >= blocks
        quads = quads and width % (QUAD * LANES) == LANES and up_weight.shape[1] == HALF
        quads = quads and blocks * rows * 7 // 16 == 7 * STEP and mesh.shape["groups"] == 2
        plan = rows_to_quads if quads else rows_to_holders
        return plan(tokens, request_block_adapter, request_block_rows, down_weight, up_weight)

    return jax.shard_map(
        per_device,
        mesh=mesh,
        in_specs=placed,
        out_specs=P(("groups", "adapter"), None, None),
        check_vma=False,
    )
```

```python
import functools

import jax
import jax.numpy as jnp
from jax import lax
from jax.experimental import pallas as pl
from jax.experimental.pallas import tpu as pltpu
from jax.sharding import PartitionSpec as P

LANES = 128
HALF = 64
QUAD = 4
QUARTER = 32
STEP = 16
NOTE = 96
VMEM = pl.BlockSpec(memory_space=pltpu.VMEM)
SMEM = pl.BlockSpec(memory_space=pltpu.SMEM)
HBM = pl.BlockSpec(memory_space=pltpu.HBM)


def normalise(tokens):
    values = tokens.astype(jnp.float32)
    mean_sq = jnp.mean(values * values, axis=-1, keepdims=True)
    return (values, (values * lax.rsqrt(mean_sq + 1e-06)).astype(jnp.bfloat16))


def resident_update(hidden_state, block_labels, adapter_down_weight, adapter_up_weight):
    feature_width = hidden_state.shape[-1]
    leading = hidden_state.shape[:-1]
    resident_rows, unused_value, inner_rank = adapter_down_weight.shape
    flattened_tokens = hidden_state.reshape(-1, feature_width)
    down_matrix = jnp.einsum(
        "tq,iqg->tig", flattened_tokens, adapter_down_weight, preferred_element_type=jnp.float32
    )
    down_matrix = down_matrix.astype(jnp.bfloat16).reshape(
        flattened_tokens.shape[0], resident_rows * inner_rank
    )
    column_owner = jnp.arange(resident_rows * inner_rank, dtype=jnp.int32) // inner_rank
    picked = block_labels.reshape(-1, 1) == column_owner[None, :]
    down_matrix = jnp.where(picked, down_matrix, jnp.zeros_like(down_matrix))
    lowrank_update = jnp.dot(
        down_matrix,
        adapter_up_weight.reshape(resident_rows * inner_rank, feature_width),
        preferred_element_type=jnp.float32,
    )
    return lowrank_update.astype(jnp.bfloat16).reshape(leading + (feature_width,))


def rows_to_holders(
    tokens, request_block_adapter, request_block_rows, adapter_down_weight, adapter_up_weight
):
    blocks, rows, feature_width = tokens.shape
    devices = lax.axis_size("adapter")
    resident_rows = adapter_down_weight.shape[0]
    slots = max(1, 4 * blocks // devices)
    values, normed = normalise(tokens)
    owner = request_block_adapter // resident_rows
    within = request_block_adapter - owner * resident_rows
    serial = jnp.arange(blocks, dtype=jnp.int32)
    earlier = (owner[:, None] == owner[None, :]) & (serial[None, :] < serial[:, None])
    position = owner * slots + jnp.sum(earlier, axis=1)
    outgoing = (
        jnp.zeros((devices * slots, rows, feature_width), jnp.bfloat16).at[position].set(normed)
    )
    outgoing = outgoing.reshape(devices, slots, rows, feature_width)
    block_labels = jnp.full((devices * slots,), -1, jnp.int32).at[position].set(within)
    block_labels = jnp.broadcast_to(block_labels[:, None], (devices * slots, rows)).reshape(
        devices, slots, rows
    )
    arriving_rows, row_markers = (
        lax.all_to_all(outgoing, "adapter", split_axis=0, concat_axis=0, tiled=True),
        lax.all_to_all(block_labels, "adapter", split_axis=0, concat_axis=0, tiled=True),
    )
    lowrank_update = resident_update(
        arriving_rows, row_markers, adapter_down_weight, adapter_up_weight
    )
    returned = lax.all_to_all(lowrank_update, "adapter", split_axis=0, concat_axis=0, tiled=True)
    mine = returned.reshape(devices * slots, rows, feature_width)[position]
    live = jnp.arange(rows, dtype=jnp.int32)[None, :] < request_block_rows[:, None]
    mixed = values + jnp.where(live[:, :, None], mine.astype(jnp.float32), jnp.float32(0.0))
    return mixed.astype(jnp.bfloat16)


def lanes_of(rows):
    return lax.broadcasted_iota(jnp.int32, (rows, LANES), 1)


def weight_kernel(whole, which, part_ref, group_ref, weight_ref, *out_refs):
    tiles = whole // LANES
    for k, out_ref in zip(which, out_refs):
        j = part_ref[k]
        if k < 2:
            last = weight_ref[:, QUAD * whole :].astype(jnp.float32)
            turned = pltpu.roll(last, lax.rem(LANES - QUARTER * j, LANES), 1)
            inside = lanes_of(last.shape[0]) < QUARTER
            out_ref[:, 0:whole] = weight_ref[:, pl.ds(pl.multiple_of(j * whole, LANES), whole)]
            out_ref[:, whole:] = jnp.where(inside, turned, 0.0).astype(jnp.bfloat16)
            continue
        count = weight_ref.shape[0] // 2
        start = pl.multiple_of(group_ref[0] * count, count)
        for t in range(tiles):
            column = pl.multiple_of(j * whole + t * LANES, LANES)
            out_ref[t * count : (t + 1) * count, :] = weight_ref[
                pl.ds(start, count), pl.ds(column, LANES)
            ]
        last = weight_ref[pl.ds(start, count), QUAD * whole :].astype(jnp.float32)
        size = count // QUAD
        owner = lanes_of(size) // QUARTER
        merged = jnp.zeros((size, LANES), jnp.float32)
        for m in range(QUAD):
            shift = lax.rem(LANES + QUARTER * (m - j), LANES)
            turned = pltpu.roll(last[m * size : (m + 1) * size], shift, 1)
            merged = jnp.where(owner == m, turned, merged)
        out_ref[tiles * count :, :] = merged.astype(jnp.bfloat16)


def open_far(far_refs, opened_ref):
    count, width = opened_ref.shape[1] // 2, opened_ref.shape[2]
    tiles, size = width // LANES - 1, count // QUAD
    inside = lanes_of(size) < QUARTER
    for i, ref in enumerate(far_refs):
        holder, base = i % 2, i // 2 * count
        for t in range(tiles):
            opened_ref[holder, base : base + count, t * LANES : (t + 1) * LANES] = ref[
                t * count : (t + 1) * count, :
            ]
        packed = ref[tiles * count :, :].astype(jnp.float32)
        for m in range(QUAD):
            turned = pltpu.roll(packed, (LANES - QUARTER * m) % LANES, 1) if m else packed
            opened_ref[holder, base + m * size : base + (m + 1) * size, tiles * LANES :] = (
                jnp.where(inside, turned, 0.0).astype(jnp.bfloat16)
            )


def pack_kernel(whole, cap, most_ref, target_ref, label_ref, tokens_ref, out_ref, normed_ref):
    values = tokens_ref[...].astype(jnp.float32)
    mean_sq = jnp.mean(values * values, axis=-1, keepdims=True)
    normed_ref[...] = (values * lax.rsqrt(mean_sq + 1e-06)).astype(jnp.bfloat16)
    total = tokens_ref.shape[0]
    quads, tiles = out_ref.shape[0] // QUAD, whole // LANES
    lane = lanes_of(total)
    last = normed_ref[:, QUAD * whole :].astype(jnp.float32)
    label = jnp.where(lane == QUARTER, label_ref[...], 0.0)
    ends = []
    for j in range(QUAD):
        turned = pltpu.roll(last, (LANES - QUARTER * j) % LANES, 1) if j else last
        ends.append(jnp.where(lane < QUARTER, turned, label).astype(jnp.bfloat16))
    most = most_ref[0].astype(jnp.float32)
    group_lane = lanes_of(QUARTER) // QUARTER
    step_lane = lanes_of(STEP)
    for q in range(quads):
        place = lax.broadcasted_iota(jnp.int32, (cap, total), 0) + q * total
        chosen = jnp.where(target_ref[...] == place, 1.0, 0.0).astype(jnp.bfloat16)
        for j in range(QUAD):
            share = jnp.dot(
                chosen,
                normed_ref[:, j * whole : (j + 1) * whole],
                preferred_element_type=jnp.float32,
            ).astype(jnp.bfloat16)
            for t in range(tiles):
                out_ref[q * QUAD + j, t * cap : (t + 1) * cap, :] = share[
                    :, t * LANES : (t + 1) * LANES
                ]
            end = jnp.dot(chosen, ends[j], preferred_element_type=jnp.float32)
            if j == 0:
                notes = jnp.where(step_lane == NOTE + cap // STEP, most, 0.0)
                for a in range(cap // STEP):
                    turned = pltpu.roll(end[a * STEP : (a + 1) * STEP], NOTE + a - QUARTER, 1)
                    notes = jnp.where(step_lane == NOTE + a, turned, notes)
            padded = jnp.concatenate(
                [end, jnp.zeros((QUAD * QUARTER - cap, LANES), jnp.float32)], axis=0
            )
            merged = padded[0:QUARTER]
            for m in range(1, QUAD):
                turned = pltpu.roll(padded[m * QUARTER : (m + 1) * QUARTER], m * QUARTER, 1)
                merged = jnp.where(group_lane == m, turned, merged)
            out_ref[q * QUAD + j, tiles * cap : tiles * cap + STEP, :] = merged[0:STEP].astype(
                jnp.bfloat16
            )
            out_ref[q * QUAD + j, tiles * cap + STEP :, :] = jnp.where(
                step_lane >= NOTE, notes, merged[STEP:]
            ).astype(jnp.bfloat16)


def read_notes(rows_ref, cap, tiles, part_ref, resident, notes_ref, labels_ref, met_ref):
    senders = rows_ref.shape[0]
    for s in range(senders):
        notes_ref[s * STEP : (s + 1) * STEP, :] = rows_ref[s, tiles * cap + STEP :, :]
    steps = labels_ref.shape[0]
    row = lax.broadcasted_iota(jnp.int32, (steps, LANES), 0)
    wanted = jnp.where(lanes_of(steps) == NOTE + row, 1.0, 0.0).astype(jnp.bfloat16)
    labels = lax.dot_general(
        wanted, notes_ref[...], (((1,), (1,)), ((), ())), preferred_element_type=jnp.float32
    )
    labels_ref[...] = labels
    code = jnp.zeros((steps, 1), jnp.float32)
    for h in range(QUAD):
        first = part_ref[h].astype(jnp.float32) + 1.0
        met = jnp.where((labels >= first) & (labels < first + resident), 1.0, 0.0)
        code = code + (1 << h) * jnp.max(met, axis=1, keepdims=True)
    at = lax.broadcasted_iota(jnp.int32, (steps, 1), 0)
    for a in range(cap // STEP):
        met_ref[a] = jnp.max(jnp.where(at == a, code, 0.0)).astype(jnp.int32)


def for_holders(met_ref, first_ref, near_refs, opened_ref, a, step):
    pairs = opened_ref.shape[1] // LANES
    for h in range(QUAD):
        base = first_ref[h].astype(jnp.float32) + 1.0
        firsts = [base + 2.0 * t for t in range(pairs)]
        if h >= 2:
            firsts = [
                base + first_ref[QUAD + i].astype(jnp.float32) + 2.0 * t
                for i in range(2)
                for t in range(pairs // 2)
            ]

        @pl.when(lax.rem(met_ref[a] // (1 << h), 2) > 0)
        def _(h=h, firsts=firsts):
            step(near_refs[h] if h < 2 else opened_ref.at[h - 2], firsts)


def down_kernel(first_ref, rows_ref, *refs):
    near_refs, far_refs, out_ref = refs[:2], refs[2:6], refs[6]
    opened_ref, batch_ref, picked_ref, notes_ref, labels_ref, met_ref = refs[7:]
    senders, width = rows_ref.shape[0], batch_ref.shape[1]
    tiles = width // LANES - 1
    cap = out_ref.shape[0] * STEP
    rank = out_ref.shape[1]
    resident = opened_ref.shape[1] // rank
    dims = (((1,), (1,)), ((), ()))
    read_notes(rows_ref, cap, tiles, first_ref, resident, notes_ref, labels_ref, met_ref)
    open_far(far_refs, opened_ref)

    def one(a, carry):
        picked_ref[...] = jnp.zeros(picked_ref.shape, jnp.float32)

        @pl.when(met_ref[a] > 0)
        def _():
            shift = lax.rem(LANES - QUARTER * (a // 2), LANES)
            spot = pl.multiple_of(tiles * cap + lax.rem(a, 2) * STEP, STEP)
            for s in range(senders):
                rows = slice(s * STEP, (s + 1) * STEP)
                for t in range(tiles):
                    at = pl.multiple_of(t * cap + a * STEP, STEP)
                    batch_ref[rows, t * LANES : (t + 1) * LANES] = rows_ref[s, pl.ds(at, STEP), :]
                end = rows_ref[s, pl.ds(spot, STEP), :].astype(jnp.float32)
                batch_ref[rows, tiles * LANES :] = pltpu.roll(end, shift, 1).astype(jnp.bfloat16)
            label = labels_ref[pl.ds(a, 1), :]

            def step(weight_ref, firsts):
                product = lax.dot_general(
                    weight_ref[...], batch_ref[...], dims, preferred_element_type=jnp.float32
                )
                picked = picked_ref[...]
                for t, first in enumerate(firsts):
                    for i in range(2):
                        at = (2 * t + i) * rank
                        picked = jnp.where(
                            label == first + i, product[at : at + rank, :], picked
                        )
                picked_ref[...] = picked

            for_holders(met_ref, first_ref, near_refs, opened_ref, a, step)

        out_ref[a] = picked_ref[...]
        return carry

    lax.fori_loop(0, cap // STEP, one, 0)


def pair_kernel(own_ref, other_ref, out_ref):
    out_ref[...] = (own_ref[...] + other_ref[...]).astype(jnp.bfloat16)


def up_kernel(first_ref, rows_ref, *refs):
    sum_refs, near_refs, far_refs, result_ref = refs[:2], refs[2:4], refs[4:8], refs[8]
    out_ref, sem, opened_ref, delta_ref, ends_ref, notes_ref, labels_ref, met_ref = refs[9:]
    senders, width = rows_ref.shape[0], opened_ref.shape[2]
    tiles = width // LANES - 1
    cap, rank = sum_refs[0].shape[0] * STEP, sum_refs[0].shape[1]
    resident = opened_ref.shape[1] // rank
    kept = (out_ref.shape[1] - QUARTER) // tiles
    group_lane = lanes_of(STEP) // QUARTER
    read_notes(rows_ref, cap, tiles, first_ref, resident, notes_ref, labels_ref, met_ref)
    open_far(far_refs, opened_ref)
    ends_ref[...] = jnp.zeros(ends_ref.shape, jnp.float32)
    low = jnp.where(lanes_of(senders * STEP) < HALF, 0.0, 1.0)
    rank_row = lax.broadcasted_iota(jnp.int32, (rank, LANES), 0)
    twofold = jnp.where(lax.rem(lanes_of(rank), rank) == rank_row, 1.0, 0.0).astype(jnp.bfloat16)

    def one(a, carry):
        delta_ref[...] = jnp.zeros(delta_ref.shape, jnp.float32)

        @pl.when(met_ref[a] > 0)
        def _():
            note_row = lax.broadcasted_iota(jnp.int32, (LANES, LANES), 0)
            wanted = jnp.where(note_row == NOTE + a, 1.0, 0.0).astype(jnp.bfloat16)
            label = jnp.dot(notes_ref[...], wanted, preferred_element_type=jnp.float32) - low
            down = sum_refs[0][a].astype(jnp.float32)
            for ref in sum_refs[1:]:
                down = down + ref[a].astype(jnp.float32)
            twice = lax.dot_general(
                down.astype(jnp.bfloat16),
                twofold,
                (((0,), (0,)), ((), ())),
                preferred_element_type=jnp.float32,
            )

            def step(weight_ref, firsts):
                placed = [jnp.where(label == first, twice, 0.0) for first in firsts]
                placed = jnp.concatenate(placed, axis=1).astype(jnp.bfloat16)
                delta_ref[...] += jnp.dot(
                    placed, weight_ref[...], preferred_element_type=jnp.float32
                )

            for_holders(met_ref, first_ref, near_refs, opened_ref, a, step)

        spot = pl.multiple_of(lax.rem(a, 2) * STEP, STEP)
        for s in range(senders):
            rows = slice(s * STEP, (s + 1) * STEP)
            for t in range(tiles):
                at = pl.multiple_of(t * kept + a * STEP, STEP)
                out_ref[s, pl.ds(at, STEP), :] = delta_ref[
                    rows, t * LANES : (t + 1) * LANES
                ].astype(jnp.bfloat16)
            turned = pltpu.roll(delta_ref[rows, tiles * LANES :], QUARTER * (a // 2), 1)
            ends_ref[s, pl.ds(spot, STEP), :] = jnp.where(
                group_lane == a // 2, turned, ends_ref[s, pl.ds(spot, STEP), :]
            )
        return carry

    lax.fori_loop(0, kept // STEP, one, 0)
    for s in range(senders):
        out_ref[s, tiles * kept :, :] = ends_ref[s].astype(jnp.bfloat16)
    copy = pltpu.make_async_copy(out_ref, result_ref, sem)
    copy.start()
    copy.wait()


def mix_kernel(whole, target_ref, tokens_ref, returned_ref, result_ref, out_ref, sems):
    total = tokens_ref.shape[0]
    tiles = whole // LANES
    quads, kept = returned_ref.shape[0] // QUAD, (returned_ref.shape[1] - QUARTER) // tiles
    lane = lanes_of(total)
    spot = lax.broadcasted_iota(jnp.int32, (total, quads * kept), 1)
    place = spot // kept * total + spot % kept
    chosen = jnp.where(target_ref[...] == place, 1.0, 0.0).astype(jnp.bfloat16)
    end = jnp.zeros((total, LANES), jnp.float32)
    copies = []
    for j in range(QUAD):
        shares = []
        for q in range(quads):
            d = q * QUAD + j
            parts = [returned_ref[d, t * kept : (t + 1) * kept, :] for t in range(tiles)]
            packed = returned_ref[d, tiles * kept :, :].astype(jnp.float32)
            groups = [packed]
            for m in range(1, QUAD):
                groups.append(pltpu.roll(packed, LANES - QUARTER * m, 1))
            parts.append(jnp.concatenate(groups, axis=0)[0:kept].astype(jnp.bfloat16))
            shares.append(jnp.concatenate(parts, axis=1))
        share = jnp.concatenate(shares, axis=0)
        delta = jnp.dot(chosen, share, preferred_element_type=jnp.float32)
        columns = pl.ds(j * whole, whole)
        out_ref[:, columns] = (
            tokens_ref[:, columns].astype(jnp.float32) + delta[:, 0:whole]
        ).astype(jnp.bfloat16)
        copies.append(
            pltpu.make_async_copy(out_ref.at[:, columns], result_ref.at[:, columns], sems.at[j])
        )
        copies[-1].start()
        last = delta[:, whole:]
        turned = pltpu.roll(last, QUARTER * j, 1) if j else last
        end = jnp.where((lane >= QUARTER * j) & (lane < QUARTER * (j + 1)), turned, end)
    columns = pl.ds(QUAD * whole, LANES)
    out_ref[:, columns] = (tokens_ref[:, columns].astype(jnp.float32) + end).astype(jnp.bfloat16)
    copies.append(
        pltpu.make_async_copy(out_ref.at[:, columns], result_ref.at[:, columns], sems.at[QUAD])
    )
    copies[-1].start()
    for copy in copies:
        copy.wait()


def call(kernel, out_shape, in_specs, flops, moved, after=(), scratch=(), out_spec=VMEM):
    many = isinstance(out_shape, list)
    skipped = len(after)
    body = (lambda *refs: kernel(*refs[skipped:])) if skipped else kernel
    run = pl.pallas_call(
        body,
        out_shape=out_shape,
        in_specs=[pl.BlockSpec(memory_space=pl.ANY)] * skipped + in_specs,
        out_specs=[VMEM] * len(out_shape) if many else out_spec,
        scratch_shapes=scratch,
        compiler_params=pltpu.CompilerParams(vmem_limit_bytes=48 * 2**20),
        cost_estimate=pl.CostEstimate(flops=flops, bytes_accessed=moved, transcendentals=0),
    )
    return functools.partial(run, *after)


def exchange(value):
    return lax.all_to_all(value, "adapter", split_axis=0, concat_axis=0, tiled=True)


def towards(value, k, devices):
    return lax.ppermute(value, "adapter", [(i, i ^ k) for i in range(devices)])


def swapped(value):
    return lax.ppermute(value, "groups", [(0, 1), (1, 0)])


def note_scratch(devices):
    return [
        pltpu.VMEM((devices * STEP, LANES), jnp.bfloat16),
        pltpu.VMEM((8, devices * STEP), jnp.float32),
        pltpu.SMEM((8,), jnp.int32),
    ]


def stand_behind(value, *earlier):
    return pl.pallas_call(
        lambda *refs: None,
        out_shape=jax.ShapeDtypeStruct(value.shape, value.dtype),
        in_specs=[pl.BlockSpec(memory_space=pl.ANY)] * (1 + len(earlier)),
        out_specs=pl.BlockSpec(memory_space=pl.ANY),
        input_output_aliases={0: 0},
    )(value, *earlier)


def back_and_mix(kept, tokens, target, first, arrived, sums, up_weights, *unused_values):
    blocks, rows, width = tokens.shape
    total = blocks * rows
    devices = arrived.shape[0]
    columns, share = up_weights[0].shape
    whole = share - LANES
    shape = (devices, whole // LANES * kept + QUARTER, LANES)
    leaving = call(
        up_kernel,
        jax.ShapeDtypeStruct(shape, jnp.bfloat16),
        [SMEM] + [VMEM] * (3 + len(up_weights)),
        2 * devices * kept * QUAD * columns * share,
        2 * (2 * devices * kept + QUAD * columns) * share,
        scratch=[
            pltpu.VMEM(shape, jnp.bfloat16),
            pltpu.SemaphoreType.DMA,
            pltpu.VMEM((2, columns, share), jnp.bfloat16),
            pltpu.VMEM((devices * STEP, share), jnp.float32),
            pltpu.VMEM((devices, QUARTER, LANES), jnp.float32),
            *note_scratch(devices),
        ],
        out_spec=HBM,
    )(first, arrived, *sums, *up_weights)
    mixed = call(
        functools.partial(mix_kernel, whole),
        jax.ShapeDtypeStruct((total, width), jnp.bfloat16),
        [VMEM] * 3,
        2 * devices * kept * total * share,
        2 * (2 * total * width + devices * kept * share),
        scratch=[pltpu.VMEM((total, width), jnp.bfloat16), pltpu.SemaphoreType.DMA((QUAD + 1,))],
        out_spec=HBM,
    )(target.reshape(total, 1), tokens.reshape(total, width), exchange(leaving))
    return mixed.reshape(tokens.shape)


def start_again(tokens, target, first, arrived, sums, up_weights, *arguments):
    return rows_to_holders(tokens, *arguments)


def rows_to_quads(
    tokens, request_block_adapter, request_block_rows, adapter_down_weight, adapter_up_weight
):
    blocks, rows, width = tokens.shape
    devices = lax.axis_size("adapter")
    resident, rank, unused_width = adapter_up_weight.shape
    total = blocks * rows
    columns = resident * rank
    whole = width // LANES // QUAD * LANES
    share = whole + LANES
    bf16, i32 = jnp.bfloat16, jnp.int32

    quad = request_block_adapter // (resident * QUAD)
    label = request_block_adapter - quad * (resident * QUAD) + 1
    order = request_block_adapter * blocks + jnp.arange(blocks, dtype=i32)
    same = quad[:, None] == quad[None, :]
    used = request_block_rows
    ahead = jnp.where(same & (order[None, :] < order[:, None]), used[None, :], 0)
    most = jnp.max(jnp.sum(jnp.where(same, used[None, :], 0), axis=1))
    row = jnp.arange(rows, dtype=i32)
    start = quad * total + jnp.sum(ahead, axis=1)
    target = jnp.where(row[None, :] < used[:, None], start[:, None] + row[None, :], -1)
    target = target.reshape(total).astype(i32)
    label = jnp.broadcast_to(label[:, None], (blocks, rows)).reshape(total, 1).astype(jnp.float32)

    me = lax.axis_index("adapter").astype(i32)
    group = lax.axis_index("groups").astype(i32)
    parts = jnp.bitwise_xor(me % QUAD, jnp.arange(QUAD, dtype=i32))
    halves = jnp.stack([group, 1 - group]) * (resident // 2)
    first = jnp.concatenate([parts * resident, halves]).astype(i32)
    tiles = whole // LANES

    def shares(weight, which, after):
        far = (columns // 2 * tiles + columns // 2 // QUAD, LANES)
        values = call(
            functools.partial(weight_kernel, whole, which),
            [jax.ShapeDtypeStruct((columns, share) if k < 2 else far, bf16) for k in which],
            [SMEM, SMEM, VMEM],
            0,
            len(which) * columns * width,
            after,
        )(parts, group.reshape(1), weight)
        return [towards(value, k, devices) if k else value for k, value in zip(which, values)]

    weight = adapter_down_weight.transpose(0, 2, 1).reshape(columns, width)
    down_weights = shares(weight, [0, 1, 2, 3], [])
    down_weights.append(swapped(down_weights[2]))
    weight = adapter_up_weight.reshape(columns, width)
    up_weights = shares(weight, [0, 1, 2], down_weights[2:3])
    up_weights += shares(weight, [3], down_weights[3:5])
    down_weights.append(swapped(down_weights[3]))
    up_weights.append(swapped(up_weights[2]))

    caps = [total * 5 // 16, total * 6 // 16, total * 7 // 16]
    cap = caps[-1]
    arrived = exchange(
        call(
            functools.partial(pack_kernel, whole, cap),
            jax.ShapeDtypeStruct((devices, tiles * cap + QUARTER, LANES), bf16),
            [SMEM, VMEM, VMEM, VMEM],
            2 * devices * cap * total * share,
            2 * (total * width + devices * cap * share),
            (),
            [pltpu.VMEM((total, width), bf16)],
        )(most.reshape(1), target.reshape(1, total), label, tokens.reshape(total, width))
    )

    partial = call(
        down_kernel,
        jax.ShapeDtypeStruct((cap // STEP, rank, devices * STEP), jnp.float32),
        [SMEM] + [VMEM] * (1 + len(down_weights)),
        0,
        0,
        up_weights[2:3],
        [
            pltpu.VMEM((2, columns, share), bf16),
            pltpu.VMEM((devices * STEP, share), bf16),
            pltpu.VMEM((rank, devices * STEP), jnp.float32),
            *note_scratch(devices),
        ],
    )(first, arrived, *down_weights)
    up_weights[3] = stand_behind(up_weights[3], partial)
    up_weights.append(swapped(up_weights[3]))
    pair = call(
        pair_kernel, jax.ShapeDtypeStruct(partial.shape, bf16), [VMEM, VMEM], 0, 0
    )(partial, towards(partial, 1, devices))
    sums = [pair, towards(pair, 2, devices)]
    counts = arrived[:, tiles * cap + STEP, NOTE + cap // STEP].astype(jnp.float32)
    most = stand_behind(jnp.max(counts).reshape(1, 1), partial)
    most = jnp.maximum(most, swapped(most))[0, 0].astype(i32)
    return lax.switch(
        sum((most > more).astype(i32) for more in caps),
        [functools.partial(back_and_mix, more) for more in caps] + [start_again],
        tokens,
        target,
        first,
        arrived,
        sums,
        up_weights,
        request_block_adapter,
        request_block_rows,
        adapter_down_weight,
        adapter_up_weight,
    )


def solution(mesh):
    placed = (
        P(("groups", "adapter"), None, None),
        P(("groups", "adapter")),
        P(("groups", "adapter")),
        P("adapter", None, None),
        P("adapter", None, None),
    )

    def per_device(tokens, request_block_adapter, request_block_rows, down_weight, up_weight):
        blocks, rows, width = tokens.shape
        devices = mesh.shape["adapter"]
        slots = max(1, 4 * blocks // devices)
        quads = devices % QUAD == 0 and slots * QUAD >= blocks
        quads = quads and width % (QUAD * LANES) == LANES and up_weight.shape[1] == HALF
        quads = quads and blocks * rows * 7 // 16 == 7 * STEP and mesh.shape["groups"] == 2
        plan = rows_to_quads if quads else rows_to_holders
        return plan(tokens, request_block_adapter, request_block_rows, down_weight, up_weight)

    return jax.shard_map(
        per_device,
        mesh=mesh,
        in_specs=placed,
        out_specs=P(("groups", "adapter"), None, None),
        check_vma=False,
    )
```

```python
import functools

import jax
import jax.numpy as jnp
from jax import lax
from jax.experimental import pallas as pl
from jax.experimental.pallas import tpu as pltpu
from jax.sharding import PartitionSpec as P

LANES = 128
HALF = 64
QUAD = 4
QUARTER = 32
STEP = 16
NOTE = 96
SLOW = 10**8
VMEM = pl.BlockSpec(memory_space=pltpu.VMEM)
SMEM = pl.BlockSpec(memory_space=pltpu.SMEM)


def normalise(tokens):
    values = tokens.astype(jnp.float32)
    mean_sq = jnp.mean(values * values, axis=-1, keepdims=True)
    return (values, (values * lax.rsqrt(mean_sq + 1e-06)).astype(jnp.bfloat16))


def resident_update(hidden_state, block_labels, adapter_down_weight, adapter_up_weight):
    feature_width = hidden_state.shape[-1]
    leading = hidden_state.shape[:-1]
    resident_rows, unused_value, inner_rank = adapter_down_weight.shape
    flattened_tokens = hidden_state.reshape(-1, feature_width)
    down_matrix = jnp.einsum(
        "tq,iqg->tig", flattened_tokens, adapter_down_weight, preferred_element_type=jnp.float32
    )
    down_matrix = down_matrix.astype(jnp.bfloat16).reshape(
        flattened_tokens.shape[0], resident_rows * inner_rank
    )
    column_owner = jnp.arange(resident_rows * inner_rank, dtype=jnp.int32) // inner_rank
    picked = block_labels.reshape(-1, 1) == column_owner[None, :]
    down_matrix = jnp.where(picked, down_matrix, jnp.zeros_like(down_matrix))
    lowrank_update = jnp.dot(
        down_matrix,
        adapter_up_weight.reshape(resident_rows * inner_rank, feature_width),
        preferred_element_type=jnp.float32,
    )
    return lowrank_update.astype(jnp.bfloat16).reshape(leading + (feature_width,))


def rows_to_holders(
    tokens, request_block_adapter, request_block_rows, adapter_down_weight, adapter_up_weight
):
    blocks, rows, feature_width = tokens.shape
    devices = lax.axis_size("adapter")
    resident_rows = adapter_down_weight.shape[0]
    slots = max(1, 4 * blocks // devices)
    values, normed = normalise(tokens)
    owner = request_block_adapter // resident_rows
    within = request_block_adapter - owner * resident_rows
    serial = jnp.arange(blocks, dtype=jnp.int32)
    earlier = (owner[:, None] == owner[None, :]) & (serial[None, :] < serial[:, None])
    position = owner * slots + jnp.sum(earlier, axis=1)
    outgoing = (
        jnp.zeros((devices * slots, rows, feature_width), jnp.bfloat16).at[position].set(normed)
    )
    outgoing = outgoing.reshape(devices, slots, rows, feature_width)
    block_labels = jnp.full((devices * slots,), -1, jnp.int32).at[position].set(within)
    block_labels = jnp.broadcast_to(block_labels[:, None], (devices * slots, rows)).reshape(
        devices, slots, rows
    )
    arriving_rows, row_markers = (
        lax.all_to_all(outgoing, "adapter", split_axis=0, concat_axis=0, tiled=True),
        lax.all_to_all(block_labels, "adapter", split_axis=0, concat_axis=0, tiled=True),
    )
    lowrank_update = resident_update(
        arriving_rows, row_markers, adapter_down_weight, adapter_up_weight
    )
    returned = lax.all_to_all(lowrank_update, "adapter", split_axis=0, concat_axis=0, tiled=True)
    mine = returned.reshape(devices * slots, rows, feature_width)[position]
    live = jnp.arange(rows, dtype=jnp.int32)[None, :] < request_block_rows[:, None]
    mixed = values + jnp.where(live[:, :, None], mine.astype(jnp.float32), jnp.float32(0.0))
    return mixed.astype(jnp.bfloat16)


def lanes_of(rows):
    return lax.broadcasted_iota(jnp.int32, (rows, LANES), 1)


def weight_kernel(whole, which, part_ref, group_ref, weight_ref, *out_refs):
    tiles = whole // LANES
    for k, out_ref in zip(which, out_refs):
        j = part_ref[k]
        if k < 2:
            last = weight_ref[:, QUAD * whole :].astype(jnp.float32)
            turned = pltpu.roll(last, lax.rem(LANES - QUARTER * j, LANES), 1)
            inside = lanes_of(last.shape[0]) < QUARTER
            out_ref[:, 0:whole] = weight_ref[:, pl.ds(pl.multiple_of(j * whole, LANES), whole)]
            out_ref[:, whole:] = jnp.where(inside, turned, 0.0).astype(jnp.bfloat16)
            continue
        count = weight_ref.shape[0] // 2
        start = pl.multiple_of(group_ref[0] * count, count)
        for t in range(tiles):
            column = pl.multiple_of(j * whole + t * LANES, LANES)
            out_ref[t * count : (t + 1) * count, :] = weight_ref[
                pl.ds(start, count), pl.ds(column, LANES)
            ]
        last = weight_ref[pl.ds(start, count), QUAD * whole :].astype(jnp.float32)
        size = count // QUAD
        owner = lanes_of(size) // QUARTER
        merged = jnp.zeros((size, LANES), jnp.float32)
        for m in range(QUAD):
            shift = lax.rem(LANES + QUARTER * (m - j), LANES)
            turned = pltpu.roll(last[m * size : (m + 1) * size], shift, 1)
            merged = jnp.where(owner == m, turned, merged)
        out_ref[tiles * count : tiles * count + size, :] = merged.astype(jnp.bfloat16)
        out_ref[tiles * count + size :, :] = jnp.zeros((STEP, LANES), jnp.bfloat16)


def open_kernel(own_ref, twin_ref, out_ref):
    count, width = out_ref.shape[0] // 2, out_ref.shape[1]
    tiles, size = width // LANES - 1, count // QUAD
    inside = lanes_of(size) < QUARTER
    for i, ref in enumerate((own_ref, twin_ref)):
        base = i * count
        for t in range(tiles):
            out_ref[base : base + count, t * LANES : (t + 1) * LANES] = ref[
                t * count : (t + 1) * count, :
            ]
        packed = ref[tiles * count : tiles * count + size, :].astype(jnp.float32)
        for m in range(QUAD):
            turned = pltpu.roll(packed, (LANES - QUARTER * m) % LANES, 1) if m else packed
            out_ref[base + m * size : base + (m + 1) * size, tiles * LANES :] = jnp.where(
                inside, turned, 0.0
            ).astype(jnp.bfloat16)


def pack_kernel(whole, cap, most_ref, target_ref, label_ref, tokens_ref, out_ref, normed_ref):
    values = tokens_ref[...].astype(jnp.float32)
    mean_sq = jnp.mean(values * values, axis=-1, keepdims=True)
    normed_ref[...] = (values * lax.rsqrt(mean_sq + 1e-06)).astype(jnp.bfloat16)
    total = tokens_ref.shape[0]
    quads, tiles = out_ref.shape[0] // QUAD, whole // LANES
    lane = lanes_of(total)
    last = normed_ref[:, QUAD * whole :].astype(jnp.float32)
    label = jnp.where(lane == QUARTER, label_ref[...], 0.0)
    ends = []
    for j in range(QUAD):
        turned = pltpu.roll(last, (LANES - QUARTER * j) % LANES, 1) if j else last
        ends.append(jnp.where(lane < QUARTER, turned, label).astype(jnp.bfloat16))
    most = most_ref[0].astype(jnp.float32)
    group_lane = lanes_of(QUARTER) // QUARTER
    step_lane = lanes_of(STEP)
    for q in range(quads):
        place = lax.broadcasted_iota(jnp.int32, (cap, total), 0) + q * total
        chosen = jnp.where(target_ref[...] == place, 1.0, 0.0).astype(jnp.bfloat16)
        for j in range(QUAD):
            share = jnp.dot(
                chosen,
                normed_ref[:, j * whole : (j + 1) * whole],
                preferred_element_type=jnp.float32,
            ).astype(jnp.bfloat16)
            for t in range(tiles):
                out_ref[q * QUAD + j, t * cap : (t + 1) * cap, :] = share[
                    :, t * LANES : (t + 1) * LANES
                ]
            end = jnp.dot(chosen, ends[j], preferred_element_type=jnp.float32)
            if j == 0:
                notes = jnp.where(step_lane == NOTE + cap // STEP, most, 0.0)
                for a in range(cap // STEP):
                    turned = pltpu.roll(end[a * STEP : (a + 1) * STEP], NOTE + a - QUARTER, 1)
                    notes = jnp.where(step_lane == NOTE + a, turned, notes)
            padded = jnp.concatenate(
                [end, jnp.zeros((QUAD * QUARTER - cap, LANES), jnp.float32)], axis=0
            )
            merged = padded[0:QUARTER]
            for m in range(1, QUAD):
                turned = pltpu.roll(padded[m * QUARTER : (m + 1) * QUARTER], m * QUARTER, 1)
                merged = jnp.where(group_lane == m, turned, merged)
            out_ref[q * QUAD + j, tiles * cap : tiles * cap + STEP, :] = merged[0:STEP].astype(
                jnp.bfloat16
            )
            out_ref[q * QUAD + j, tiles * cap + STEP :, :] = jnp.where(
                step_lane >= NOTE, notes, merged[STEP:]
            ).astype(jnp.bfloat16)


def read_notes(rows_ref, cap, tiles, part_ref, resident, notes_ref, labels_ref, met_ref):
    senders = rows_ref.shape[0]
    for s in range(senders):
        notes_ref[s * STEP : (s + 1) * STEP, :] = rows_ref[s, tiles * cap + STEP :, :]
    steps = labels_ref.shape[0]
    row = lax.broadcasted_iota(jnp.int32, (steps, LANES), 0)
    wanted = jnp.where(lanes_of(steps) == NOTE + row, 1.0, 0.0).astype(jnp.bfloat16)
    labels = lax.dot_general(
        wanted, notes_ref[...], (((1,), (1,)), ((), ())), preferred_element_type=jnp.float32
    )
    labels_ref[...] = labels
    code = jnp.zeros((steps, 1), jnp.float32)
    for h in range(QUAD):
        first = part_ref[h].astype(jnp.float32) + 1.0
        met = jnp.where((labels >= first) & (labels < first + resident), 1.0, 0.0)
        code = code + (1 << h) * jnp.max(met, axis=1, keepdims=True)
    at = lax.broadcasted_iota(jnp.int32, (steps, 1), 0)
    for a in range(cap // STEP):
        met_ref[a] = jnp.max(jnp.where(at == a, code, 0.0)).astype(jnp.int32)


def for_holders(met_ref, first_ref, weight_refs, a, step):
    pairs = weight_refs[0].shape[0] // LANES
    for h in range(QUAD):
        base = first_ref[h].astype(jnp.float32) + 1.0
        firsts = [base + 2.0 * t for t in range(pairs)]
        if h >= 2:
            firsts = [
                base + first_ref[QUAD + i].astype(jnp.float32) + 2.0 * t
                for i in range(2)
                for t in range(pairs // 2)
            ]

        @pl.when(lax.rem(met_ref[a] // (1 << h), 2) > 0)
        def _(h=h, firsts=firsts):
            step(weight_refs[h], firsts)


def down_kernel(first_ref, rows_ref, *refs):
    weight_refs, out_ref, count_ref = refs[:QUAD], refs[QUAD], refs[QUAD + 1]
    batch_ref, picked_ref, notes_ref, labels_ref, met_ref = refs[QUAD + 2 :]
    senders, width = rows_ref.shape[0], batch_ref.shape[1]
    tiles = width // LANES - 1
    cap = out_ref.shape[0] * STEP
    rank = out_ref.shape[1]
    resident = weight_refs[0].shape[0] // rank
    dims = (((1,), (1,)), ((), ()))
    read_notes(rows_ref, cap, tiles, first_ref, resident, notes_ref, labels_ref, met_ref)
    notes = notes_ref[...].astype(jnp.float32)
    is_count = lanes_of(senders * STEP) == NOTE + cap // STEP
    count = jnp.max(jnp.where(is_count, notes, 0.0), axis=(0, 1), keepdims=True)
    count_ref[...] = jnp.broadcast_to(count, count_ref.shape).astype(jnp.bfloat16)

    def one(a, carry):
        picked_ref[...] = jnp.zeros(picked_ref.shape, jnp.float32)

        @pl.when(met_ref[a] > 0)
        def _():
            shift = lax.rem(LANES - QUARTER * (a // 2), LANES)
            spot = pl.multiple_of(tiles * cap + lax.rem(a, 2) * STEP, STEP)
            for s in range(senders):
                rows = slice(s * STEP, (s + 1) * STEP)
                for t in range(tiles):
                    at = pl.multiple_of(t * cap + a * STEP, STEP)
                    batch_ref[rows, t * LANES : (t + 1) * LANES] = rows_ref[s, pl.ds(at, STEP), :]
                end = rows_ref[s, pl.ds(spot, STEP), :].astype(jnp.float32)
                batch_ref[rows, tiles * LANES :] = pltpu.roll(end, shift, 1).astype(jnp.bfloat16)
            label = labels_ref[pl.ds(a, 1), :]

            def step(weight_ref, firsts):
                product = lax.dot_general(
                    weight_ref[...], batch_ref[...], dims, preferred_element_type=jnp.float32
                )
                picked = picked_ref[...]
                for t, first in enumerate(firsts):
                    for i in range(2):
                        at = (2 * t + i) * rank
                        picked = jnp.where(
                            label == first + i, product[at : at + rank, :], picked
                        )
                picked_ref[...] = picked

            for_holders(met_ref, first_ref, weight_refs, a, step)

        out_ref[a] = picked_ref[...]
        return carry

    lax.fori_loop(0, cap // STEP, one, 0)


def pair_kernel(own_ref, other_ref, out_ref):
    out_ref[...] = (own_ref[...] + other_ref[...]).astype(jnp.bfloat16)


def up_kernel(first_ref, rows_ref, *refs):
    sum_refs, weight_refs, out_ref = refs[:2], refs[2 : 2 + QUAD], refs[2 + QUAD]
    delta_ref, ends_ref, notes_ref, labels_ref, met_ref = refs[3 + QUAD :]
    senders, width = rows_ref.shape[0], delta_ref.shape[1]
    tiles = width // LANES - 1
    cap, rank = sum_refs[0].shape[0] * STEP, sum_refs[0].shape[1]
    resident = weight_refs[0].shape[0] // rank
    kept = (out_ref.shape[1] - QUARTER) // tiles
    group_lane = lanes_of(STEP) // QUARTER
    read_notes(rows_ref, cap, tiles, first_ref, resident, notes_ref, labels_ref, met_ref)
    ends_ref[...] = jnp.zeros(ends_ref.shape, jnp.float32)
    low = jnp.where(lanes_of(senders * STEP) < HALF, 0.0, 1.0)
    rank_row = lax.broadcasted_iota(jnp.int32, (rank, LANES), 0)
    twofold = jnp.where(lax.rem(lanes_of(rank), rank) == rank_row, 1.0, 0.0).astype(jnp.bfloat16)

    def one(a, carry):
        delta_ref[...] = jnp.zeros(delta_ref.shape, jnp.float32)

        @pl.when(met_ref[a] > 0)
        def _():
            note_row = lax.broadcasted_iota(jnp.int32, (LANES, LANES), 0)
            wanted = jnp.where(note_row == NOTE + a, 1.0, 0.0).astype(jnp.bfloat16)
            label = jnp.dot(notes_ref[...], wanted, preferred_element_type=jnp.float32) - low
            down = sum_refs[0][a].astype(jnp.float32)
            for ref in sum_refs[1:]:
                down = down + ref[a].astype(jnp.float32)
            twice = lax.dot_general(
                down.astype(jnp.bfloat16),
                twofold,
                (((0,), (0,)), ((), ())),
                preferred_element_type=jnp.float32,
            )

            def step(weight_ref, firsts):
                placed = [jnp.where(label == first, twice, 0.0) for first in firsts]
                placed = jnp.concatenate(placed, axis=1).astype(jnp.bfloat16)
                delta_ref[...] += jnp.dot(
                    placed, weight_ref[...], preferred_element_type=jnp.float32
                )

            for_holders(met_ref, first_ref, weight_refs, a, step)

        spot = pl.multiple_of(lax.rem(a, 2) * STEP, STEP)
        for s in range(senders):
            rows = slice(s * STEP, (s + 1) * STEP)
            for t in range(tiles):
                at = pl.multiple_of(t * kept + a * STEP, STEP)
                out_ref[s, pl.ds(at, STEP), :] = delta_ref[
                    rows, t * LANES : (t + 1) * LANES
                ].astype(jnp.bfloat16)
            turned = pltpu.roll(delta_ref[rows, tiles * LANES :], QUARTER * (a // 2), 1)
            ends_ref[s, pl.ds(spot, STEP), :] = jnp.where(
                group_lane == a // 2, turned, ends_ref[s, pl.ds(spot, STEP), :]
            )
        return carry

    lax.fori_loop(0, kept // STEP, one, 0)
    for s in range(senders):
        out_ref[s, tiles * kept :, :] = ends_ref[s].astype(jnp.bfloat16)


def mix_kernel(whole, target_ref, tokens_ref, returned_ref, out_ref):
    total = tokens_ref.shape[0]
    tiles = whole // LANES
    quads, kept = returned_ref.shape[0] // QUAD, (returned_ref.shape[1] - QUARTER) // tiles
    lane = lanes_of(total)
    spot = lax.broadcasted_iota(jnp.int32, (total, quads * kept), 1)
    place = spot // kept * total + spot % kept
    chosen = jnp.where(target_ref[...] == place, 1.0, 0.0).astype(jnp.bfloat16)
    end = jnp.zeros((total, LANES), jnp.float32)
    for j in range(QUAD):
        shares = []
        for q in range(quads):
            d = q * QUAD + j
            parts = [returned_ref[d, t * kept : (t + 1) * kept, :] for t in range(tiles)]
            packed = returned_ref[d, tiles * kept :, :].astype(jnp.float32)
            groups = [packed]
            for m in range(1, QUAD):
                groups.append(pltpu.roll(packed, LANES - QUARTER * m, 1))
            parts.append(jnp.concatenate(groups, axis=0)[0:kept].astype(jnp.bfloat16))
            shares.append(jnp.concatenate(parts, axis=1))
        share = jnp.concatenate(shares, axis=0)
        delta = jnp.dot(chosen, share, preferred_element_type=jnp.float32)
        columns = pl.ds(j * whole, whole)
        out_ref[:, columns] = (
            tokens_ref[:, columns].astype(jnp.float32) + delta[:, 0:whole]
        ).astype(jnp.bfloat16)
        last = delta[:, whole:]
        turned = pltpu.roll(last, QUARTER * j, 1) if j else last
        end = jnp.where((lane >= QUARTER * j) & (lane < QUARTER * (j + 1)), turned, end)
    columns = pl.ds(QUAD * whole, LANES)
    out_ref[:, columns] = (tokens_ref[:, columns].astype(jnp.float32) + end).astype(jnp.bfloat16)


def call(kernel, out_shape, in_specs, flops, moved, after=(), scratch=()):
    many = isinstance(out_shape, list)
    skipped = len(after)
    body = (lambda *refs: kernel(*refs[skipped:])) if skipped else kernel
    run = pl.pallas_call(
        body,
        out_shape=out_shape,
        in_specs=[pl.BlockSpec(memory_space=pl.ANY)] * skipped + in_specs,
        out_specs=[VMEM] * len(out_shape) if many else VMEM,
        scratch_shapes=scratch,
        compiler_params=pltpu.CompilerParams(vmem_limit_bytes=48 * 2**20),
        cost_estimate=pl.CostEstimate(flops=flops, bytes_accessed=moved, transcendentals=0),
    )
    return functools.partial(run, *after)


def exchange(value):
    return lax.all_to_all(value, "adapter", split_axis=0, concat_axis=0, tiled=True)


def towards(value, k, devices):
    return lax.ppermute(value, "adapter", [(i, i ^ k) for i in range(devices)])


def swapped(value):
    return lax.ppermute(value, "groups", [(0, 1), (1, 0)])


def note_scratch(devices):
    return [
        pltpu.VMEM((devices * STEP, LANES), jnp.bfloat16),
        pltpu.VMEM((8, devices * STEP), jnp.float32),
        pltpu.SMEM((8,), jnp.int32),
    ]


def note_kernel(note_ref, value_ref, out_ref, sem):
    rows = note_ref.shape[0]
    last = out_ref.at[pl.ds(out_ref.shape[0] - rows, rows)]
    copy = pltpu.make_async_copy(note_ref, last, sem)
    copy.start()
    copy.wait()


def with_note(value, note):
    return pl.pallas_call(
        note_kernel,
        out_shape=jax.ShapeDtypeStruct(value.shape, value.dtype),
        in_specs=[VMEM, pl.BlockSpec(memory_space=pl.ANY)],
        out_specs=pl.BlockSpec(memory_space=pl.ANY),
        scratch_shapes=[pltpu.SemaphoreType.DMA],
        input_output_aliases={1: 0},
    )(note, value)


def back_and_mix(kept, tokens, target, first, arrived, sums, up_weights, *unused_values):
    blocks, rows, width = tokens.shape
    total = blocks * rows
    devices = arrived.shape[0]
    columns, share = up_weights[0].shape
    whole = share - LANES
    shape = (devices, whole // LANES * kept + QUARTER, LANES)
    leaving = call(
        up_kernel,
        jax.ShapeDtypeStruct(shape, jnp.bfloat16),
        [SMEM] + [VMEM] * (3 + len(up_weights)),
        2 * devices * kept * QUAD * columns * share,
        2 * (2 * devices * kept + QUAD * columns) * share,
        scratch=[
            pltpu.VMEM((devices * STEP, share), jnp.float32),
            pltpu.VMEM((devices, QUARTER, LANES), jnp.float32),
            *note_scratch(devices),
        ],
    )(first, arrived, *sums, *up_weights)
    mixed = call(
        functools.partial(mix_kernel, whole),
        jax.ShapeDtypeStruct((total, width), jnp.bfloat16),
        [VMEM] * 3,
        2 * devices * kept * total * share,
        2 * (2 * total * width + devices * kept * share),
    )(target.reshape(total, 1), tokens.reshape(total, width), exchange(leaving))
    return mixed.reshape(tokens.shape)


def start_again(tokens, target, first, arrived, sums, up_weights, *arguments):
    return rows_to_holders(tokens, *arguments)


def rows_to_quads(
    tokens, request_block_adapter, request_block_rows, adapter_down_weight, adapter_up_weight
):
    blocks, rows, width = tokens.shape
    devices = lax.axis_size("adapter")
    resident, rank, unused_width = adapter_up_weight.shape
    total = blocks * rows
    columns = resident * rank
    whole = width // LANES // QUAD * LANES
    share = whole + LANES
    bf16, i32 = jnp.bfloat16, jnp.int32

    quad = request_block_adapter // (resident * QUAD)
    label = request_block_adapter - quad * (resident * QUAD) + 1
    order = request_block_adapter * blocks + jnp.arange(blocks, dtype=i32)
    same = quad[:, None] == quad[None, :]
    used = request_block_rows
    ahead = jnp.where(same & (order[None, :] < order[:, None]), used[None, :], 0)
    most = jnp.max(jnp.sum(jnp.where(same, used[None, :], 0), axis=1))
    row = jnp.arange(rows, dtype=i32)
    start = quad * total + jnp.sum(ahead, axis=1)
    target = jnp.where(row[None, :] < used[:, None], start[:, None] + row[None, :], -1)
    target = target.reshape(total).astype(i32)
    label = jnp.broadcast_to(label[:, None], (blocks, rows)).reshape(total, 1).astype(jnp.float32)

    me = lax.axis_index("adapter").astype(i32)
    group = lax.axis_index("groups").astype(i32)
    parts = jnp.bitwise_xor(me % QUAD, jnp.arange(QUAD, dtype=i32))
    halves = jnp.stack([group, 1 - group]) * (resident // 2)
    first = jnp.concatenate([parts * resident, halves]).astype(i32)
    tiles = whole // LANES

    def shares(weight, which, after):
        far = (columns // 2 * tiles + columns // 2 // QUAD + STEP, LANES)
        values = call(
            functools.partial(weight_kernel, whole, which),
            [jax.ShapeDtypeStruct((columns, share) if k < 2 else far, bf16) for k in which],
            [SMEM, SMEM, VMEM],
            0,
            len(which) * columns * width,
            after,
        )(parts, group.reshape(1), weight)
        return [towards(value, k, devices) if k else value for k, value in zip(which, values)]

    def opened(own, twin, moved):
        return call(
            open_kernel, jax.ShapeDtypeStruct((columns, share), bf16), [VMEM, VMEM], 0, moved
        )(own, twin)

    weight = adapter_down_weight.transpose(0, 2, 1).reshape(columns, width)
    *down_weights, far_2, far_3 = shares(weight, [0, 1, 2, 3], [])
    twin_2 = swapped(far_2)
    weight = adapter_up_weight.reshape(columns, width)
    *up_weights, up_far_2 = shares(weight, [0, 1, 2], [far_2])
    up_far_3 = shares(weight, [3], [far_3, twin_2])[0]
    down_weights += [opened(far_2, twin_2, 0), opened(far_3, swapped(far_3), 0)]

    caps = [total * 5 // 16, total * 6 // 16, total * 7 // 16]
    cap = caps[-1]
    arrived = exchange(
        call(
            functools.partial(pack_kernel, whole, cap),
            jax.ShapeDtypeStruct((devices, tiles * cap + QUARTER, LANES), bf16),
            [SMEM, VMEM, VMEM, VMEM],
            2 * devices * cap * total * share,
            2 * (total * width + devices * cap * share),
            (),
            [pltpu.VMEM((total, width), bf16)],
        )(most.reshape(1), target.reshape(1, total), label, tokens.reshape(total, width))
    )

    partial, count = call(
        down_kernel,
        [
            jax.ShapeDtypeStruct((cap // STEP, rank, devices * STEP), jnp.float32),
            jax.ShapeDtypeStruct((STEP, LANES), bf16),
        ],
        [SMEM] + [VMEM] * (1 + len(down_weights)),
        0,
        0,
        [up_far_2],
        [
            pltpu.VMEM((devices * STEP, share), bf16),
            pltpu.VMEM((rank, devices * STEP), jnp.float32),
            *note_scratch(devices),
        ],
    )(first, arrived, *down_weights)
    up_far_3 = with_note(up_far_3, count)
    up_twin_3 = swapped(up_far_3)
    up_weights.append(opened(up_far_2, swapped(up_far_2), SLOW))
    up_weights.append(opened(up_far_3, up_twin_3, SLOW))
    pair = call(
        pair_kernel, jax.ShapeDtypeStruct(partial.shape, bf16), [VMEM, VMEM], 0, 0
    )(partial, towards(partial, 1, devices))
    sums = [pair, towards(pair, 2, devices)]
    most = jnp.maximum(count[0, 0], up_twin_3[-1, 0]).astype(jnp.float32)
    return lax.switch(
        sum((most > more).astype(i32) for more in caps),
        [functools.partial(back_and_mix, more) for more in caps] + [start_again],
        tokens,
        target,
        first,
        arrived,
        sums,
        up_weights,
        request_block_adapter,
        request_block_rows,
        adapter_down_weight,
        adapter_up_weight,
    )


def solution(mesh):
    placed = (
        P(("groups", "adapter"), None, None),
        P(("groups", "adapter")),
        P(("groups", "adapter")),
        P("adapter", None, None),
        P("adapter", None, None),
    )

    def per_device(tokens, request_block_adapter, request_block_rows, down_weight, up_weight):
        blocks, rows, width = tokens.shape
        devices = mesh.shape["adapter"]
        slots = max(1, 4 * blocks // devices)
        quads = devices % QUAD == 0 and slots * QUAD >= blocks
        quads = quads and width % (QUAD * LANES) == LANES and up_weight.shape[1] == HALF
        quads = quads and blocks * rows * 7 // 16 == 7 * STEP and mesh.shape["groups"] == 2
        plan = rows_to_quads if quads else rows_to_holders
        return plan(tokens, request_block_adapter, request_block_rows, down_weight, up_weight)

    return jax.shard_map(
        per_device,
        mesh=mesh,
        in_specs=placed,
        out_specs=P(("groups", "adapter"), None, None),
        check_vma=False,
    )
```

```python
import functools

import jax
import jax.numpy as jnp
from jax import lax
from jax.experimental import pallas as pl
from jax.experimental.pallas import tpu as pltpu
from jax.sharding import PartitionSpec as P

LANES = 128
HALF = 64
QUAD = 4
QUARTER = 32
STEP = 16
NOTE = 96
VMEM = pl.BlockSpec(memory_space=pltpu.VMEM)
SMEM = pl.BlockSpec(memory_space=pltpu.SMEM)


def normalise(tokens):
    values = tokens.astype(jnp.float32)
    mean_sq = jnp.mean(values * values, axis=-1, keepdims=True)
    return (values, (values * lax.rsqrt(mean_sq + 1e-06)).astype(jnp.bfloat16))


def resident_update(hidden_state, block_labels, adapter_down_weight, adapter_up_weight):
    feature_width = hidden_state.shape[-1]
    leading = hidden_state.shape[:-1]
    resident_rows, unused_value, inner_rank = adapter_down_weight.shape
    flattened_tokens = hidden_state.reshape(-1, feature_width)
    down_matrix = jnp.einsum(
        "tq,iqg->tig", flattened_tokens, adapter_down_weight, preferred_element_type=jnp.float32
    )
    down_matrix = down_matrix.astype(jnp.bfloat16).reshape(
        flattened_tokens.shape[0], resident_rows * inner_rank
    )
    column_owner = jnp.arange(resident_rows * inner_rank, dtype=jnp.int32) // inner_rank
    picked = block_labels.reshape(-1, 1) == column_owner[None, :]
    down_matrix = jnp.where(picked, down_matrix, jnp.zeros_like(down_matrix))
    lowrank_update = jnp.dot(
        down_matrix,
        adapter_up_weight.reshape(resident_rows * inner_rank, feature_width),
        preferred_element_type=jnp.float32,
    )
    return lowrank_update.astype(jnp.bfloat16).reshape(leading + (feature_width,))


def rows_to_holders(
    tokens, request_block_adapter, request_block_rows, adapter_down_weight, adapter_up_weight
):
    blocks, rows, feature_width = tokens.shape
    devices = lax.axis_size("adapter")
    resident_rows = adapter_down_weight.shape[0]
    slots = max(1, 4 * blocks // devices)
    values, normed = normalise(tokens)
    owner = request_block_adapter // resident_rows
    within = request_block_adapter - owner * resident_rows
    serial = jnp.arange(blocks, dtype=jnp.int32)
    earlier = (owner[:, None] == owner[None, :]) & (serial[None, :] < serial[:, None])
    position = owner * slots + jnp.sum(earlier, axis=1)
    outgoing = (
        jnp.zeros((devices * slots, rows, feature_width), jnp.bfloat16).at[position].set(normed)
    )
    outgoing = outgoing.reshape(devices, slots, rows, feature_width)
    block_labels = jnp.full((devices * slots,), -1, jnp.int32).at[position].set(within)
    block_labels = jnp.broadcast_to(block_labels[:, None], (devices * slots, rows)).reshape(
        devices, slots, rows
    )
    arriving_rows, row_markers = (
        lax.all_to_all(outgoing, "adapter", split_axis=0, concat_axis=0, tiled=True),
        lax.all_to_all(block_labels, "adapter", split_axis=0, concat_axis=0, tiled=True),
    )
    lowrank_update = resident_update(
        arriving_rows, row_markers, adapter_down_weight, adapter_up_weight
    )
    returned = lax.all_to_all(lowrank_update, "adapter", split_axis=0, concat_axis=0, tiled=True)
    mine = returned.reshape(devices * slots, rows, feature_width)[position]
    live = jnp.arange(rows, dtype=jnp.int32)[None, :] < request_block_rows[:, None]
    mixed = values + jnp.where(live[:, :, None], mine.astype(jnp.float32), jnp.float32(0.0))
    return mixed.astype(jnp.bfloat16)


def lanes_of(rows):
    return lax.broadcasted_iota(jnp.int32, (rows, LANES), 1)


def weight_kernel(whole, which, part_ref, group_ref, weight_ref, *out_refs):
    tiles = whole // LANES
    for k, out_ref in zip(which, out_refs):
        j = part_ref[k]
        if k < 2:
            last = weight_ref[:, QUAD * whole :].astype(jnp.float32)
            turned = pltpu.roll(last, lax.rem(LANES - QUARTER * j, LANES), 1)
            inside = lanes_of(last.shape[0]) < QUARTER
            out_ref[:, 0:whole] = weight_ref[:, pl.ds(pl.multiple_of(j * whole, LANES), whole)]
            out_ref[:, whole:] = jnp.where(inside, turned, 0.0).astype(jnp.bfloat16)
            continue
        count = weight_ref.shape[0] // 2
        start = pl.multiple_of(group_ref[0] * count, count)
        for t in range(tiles):
            column = pl.multiple_of(j * whole + t * LANES, LANES)
            out_ref[t * count : (t + 1) * count, :] = weight_ref[
                pl.ds(start, count), pl.ds(column, LANES)
            ]
        last = weight_ref[pl.ds(start, count), QUAD * whole :].astype(jnp.float32)
        size = count // QUAD
        owner = lanes_of(size) // QUARTER
        merged = jnp.zeros((size, LANES), jnp.float32)
        for m in range(QUAD):
            shift = lax.rem(LANES + QUARTER * (m - j), LANES)
            turned = pltpu.roll(last[m * size : (m + 1) * size], shift, 1)
            merged = jnp.where(owner == m, turned, merged)
        out_ref[tiles * count : tiles * count + size, :] = merged.astype(jnp.bfloat16)
        out_ref[tiles * count + size :, :] = jnp.zeros((STEP, LANES), jnp.bfloat16)


def open_far(far_refs, opened_ref):
    count, width = opened_ref.shape[1] // 2, opened_ref.shape[2]
    tiles, size = width // LANES - 1, count // QUAD
    inside = lanes_of(size) < QUARTER
    for i, ref in enumerate(far_refs):
        holder, base = i % 2, i // 2 * count
        for t in range(tiles):
            opened_ref[holder, base : base + count, t * LANES : (t + 1) * LANES] = ref[
                t * count : (t + 1) * count, :
            ]
        packed = ref[tiles * count : tiles * count + size, :].astype(jnp.float32)
        for m in range(QUAD):
            turned = pltpu.roll(packed, (LANES - QUARTER * m) % LANES, 1) if m else packed
            opened_ref[holder, base + m * size : base + (m + 1) * size, tiles * LANES :] = (
                jnp.where(inside, turned, 0.0).astype(jnp.bfloat16)
            )


def pack_kernel(whole, cap, most_ref, target_ref, label_ref, tokens_ref, out_ref, normed_ref):
    values = tokens_ref[...].astype(jnp.float32)
    mean_sq = jnp.mean(values * values, axis=-1, keepdims=True)
    normed_ref[...] = (values * lax.rsqrt(mean_sq + 1e-06)).astype(jnp.bfloat16)
    total = tokens_ref.shape[0]
    quads, tiles = out_ref.shape[0] // QUAD, whole // LANES
    lane = lanes_of(total)
    last = normed_ref[:, QUAD * whole :].astype(jnp.float32)
    label = jnp.where(lane == QUARTER, label_ref[...], 0.0)
    ends = []
    for j in range(QUAD):
        turned = pltpu.roll(last, (LANES - QUARTER * j) % LANES, 1) if j else last
        ends.append(jnp.where(lane < QUARTER, turned, label).astype(jnp.bfloat16))
    most = most_ref[0].astype(jnp.float32)
    group_lane = lanes_of(QUARTER) // QUARTER
    step_lane = lanes_of(STEP)
    for q in range(quads):
        place = lax.broadcasted_iota(jnp.int32, (cap, total), 0) + q * total
        chosen = jnp.where(target_ref[...] == place, 1.0, 0.0).astype(jnp.bfloat16)
        for j in range(QUAD):
            share = jnp.dot(
                chosen,
                normed_ref[:, j * whole : (j + 1) * whole],
                preferred_element_type=jnp.float32,
            ).astype(jnp.bfloat16)
            for t in range(tiles):
                out_ref[q * QUAD + j, t * cap : (t + 1) * cap, :] = share[
                    :, t * LANES : (t + 1) * LANES
                ]
            end = jnp.dot(chosen, ends[j], preferred_element_type=jnp.float32)
            if j == 0:
                notes = jnp.where(step_lane == NOTE + cap // STEP, most, 0.0)
                for a in range(cap // STEP):
                    turned = pltpu.roll(end[a * STEP : (a + 1) * STEP], NOTE + a - QUARTER, 1)
                    notes = jnp.where(step_lane == NOTE + a, turned, notes)
            padded = jnp.concatenate(
                [end, jnp.zeros((QUAD * QUARTER - cap, LANES), jnp.float32)], axis=0
            )
            merged = padded[0:QUARTER]
            for m in range(1, QUAD):
                turned = pltpu.roll(padded[m * QUARTER : (m + 1) * QUARTER], m * QUARTER, 1)
                merged = jnp.where(group_lane == m, turned, merged)
            out_ref[q * QUAD + j, tiles * cap : tiles * cap + STEP, :] = merged[0:STEP].astype(
                jnp.bfloat16
            )
            out_ref[q * QUAD + j, tiles * cap + STEP :, :] = jnp.where(
                step_lane >= NOTE, notes, merged[STEP:]
            ).astype(jnp.bfloat16)


def read_notes(rows_ref, cap, tiles, part_ref, resident, notes_ref, labels_ref, met_ref):
    senders = rows_ref.shape[0]
    for s in range(senders):
        notes_ref[s * STEP : (s + 1) * STEP, :] = rows_ref[s, tiles * cap + STEP :, :]
    steps = labels_ref.shape[0]
    row = lax.broadcasted_iota(jnp.int32, (steps, LANES), 0)
    wanted = jnp.where(lanes_of(steps) == NOTE + row, 1.0, 0.0).astype(jnp.bfloat16)
    labels = lax.dot_general(
        wanted, notes_ref[...], (((1,), (1,)), ((), ())), preferred_element_type=jnp.float32
    )
    labels_ref[...] = labels
    code = jnp.zeros((steps, 1), jnp.float32)
    for h in range(QUAD):
        first = part_ref[h].astype(jnp.float32) + 1.0
        met = jnp.where((labels >= first) & (labels < first + resident), 1.0, 0.0)
        code = code + (1 << h) * jnp.max(met, axis=1, keepdims=True)
    at = lax.broadcasted_iota(jnp.int32, (steps, 1), 0)
    for a in range(cap // STEP):
        met_ref[a] = jnp.max(jnp.where(at == a, code, 0.0)).astype(jnp.int32)


def for_holders(met_ref, first_ref, near_refs, opened_ref, a, step):
    pairs = opened_ref.shape[1] // LANES
    for h in range(QUAD):
        base = first_ref[h].astype(jnp.float32) + 1.0
        firsts = [base + 2.0 * t for t in range(pairs)]
        if h >= 2:
            firsts = [
                base + first_ref[QUAD + i].astype(jnp.float32) + 2.0 * t
                for i in range(2)
                for t in range(pairs // 2)
            ]

        @pl.when(lax.rem(met_ref[a] // (1 << h), 2) > 0)
        def _(h=h, firsts=firsts):
            step(near_refs[h] if h < 2 else opened_ref.at[h - 2], firsts)


def down_kernel(first_ref, rows_ref, *refs):
    near_refs, far_refs, out_ref, count_ref = refs[:2], refs[2:6], refs[6], refs[7]
    opened_ref, batch_ref, picked_ref, notes_ref, labels_ref, met_ref = refs[8:]
    senders, width = rows_ref.shape[0], batch_ref.shape[1]
    tiles = width // LANES - 1
    cap = out_ref.shape[0] * STEP
    rank = out_ref.shape[1]
    resident = opened_ref.shape[1] // rank
    dims = (((1,), (1,)), ((), ()))
    read_notes(rows_ref, cap, tiles, first_ref, resident, notes_ref, labels_ref, met_ref)
    notes = notes_ref[...].astype(jnp.float32)
    is_count = lanes_of(senders * STEP) == NOTE + cap // STEP
    count = jnp.max(jnp.where(is_count, notes, 0.0), axis=(0, 1), keepdims=True)
    count_ref[...] = jnp.broadcast_to(count, count_ref.shape).astype(jnp.bfloat16)
    open_far(far_refs, opened_ref)

    def one(a, carry):
        picked_ref[...] = jnp.zeros(picked_ref.shape, jnp.float32)

        @pl.when(met_ref[a] > 0)
        def _():
            shift = lax.rem(LANES - QUARTER * (a // 2), LANES)
            spot = pl.multiple_of(tiles * cap + lax.rem(a, 2) * STEP, STEP)
            for s in range(senders):
                rows = slice(s * STEP, (s + 1) * STEP)
                for t in range(tiles):
                    at = pl.multiple_of(t * cap + a * STEP, STEP)
                    batch_ref[rows, t * LANES : (t + 1) * LANES] = rows_ref[s, pl.ds(at, STEP), :]
                end = rows_ref[s, pl.ds(spot, STEP), :].astype(jnp.float32)
                batch_ref[rows, tiles * LANES :] = pltpu.roll(end, shift, 1).astype(jnp.bfloat16)
            label = labels_ref[pl.ds(a, 1), :]

            def step(weight_ref, firsts):
                product = lax.dot_general(
                    weight_ref[...], batch_ref[...], dims, preferred_element_type=jnp.float32
                )
                picked = picked_ref[...]
                for t, first in enumerate(firsts):
                    for i in range(2):
                        at = (2 * t + i) * rank
                        picked = jnp.where(
                            label == first + i, product[at : at + rank, :], picked
                        )
                picked_ref[...] = picked

            for_holders(met_ref, first_ref, near_refs, opened_ref, a, step)

        out_ref[a] = picked_ref[...]
        return carry

    lax.fori_loop(0, cap // STEP, one, 0)


def pair_kernel(own_ref, other_ref, out_ref):
    out_ref[...] = (own_ref[...] + other_ref[...]).astype(jnp.bfloat16)


def up_kernel(first_ref, rows_ref, *refs):
    sum_refs, near_refs, far_refs, out_ref = refs[:2], refs[2:4], refs[4:8], refs[8]
    opened_ref, delta_ref, ends_ref, notes_ref, labels_ref, met_ref = refs[9:]
    senders, width = rows_ref.shape[0], opened_ref.shape[2]
    tiles = width // LANES - 1
    cap, rank = sum_refs[0].shape[0] * STEP, sum_refs[0].shape[1]
    resident = opened_ref.shape[1] // rank
    kept = (out_ref.shape[1] - QUARTER) // tiles
    group_lane = lanes_of(STEP) // QUARTER
    read_notes(rows_ref, cap, tiles, first_ref, resident, notes_ref, labels_ref, met_ref)
    open_far(far_refs, opened_ref)
    ends_ref[...] = jnp.zeros(ends_ref.shape, jnp.float32)
    low = jnp.where(lanes_of(senders * STEP) < HALF, 0.0, 1.0)
    rank_row = lax.broadcasted_iota(jnp.int32, (rank, LANES), 0)
    twofold = jnp.where(lax.rem(lanes_of(rank), rank) == rank_row, 1.0, 0.0).astype(jnp.bfloat16)

    def one(a, carry):
        delta_ref[...] = jnp.zeros(delta_ref.shape, jnp.float32)

        @pl.when(met_ref[a] > 0)
        def _():
            note_row = lax.broadcasted_iota(jnp.int32, (LANES, LANES), 0)
            wanted = jnp.where(note_row == NOTE + a, 1.0, 0.0).astype(jnp.bfloat16)
            label = jnp.dot(notes_ref[...], wanted, preferred_element_type=jnp.float32) - low
            down = sum_refs[0][a].astype(jnp.float32)
            for ref in sum_refs[1:]:
                down = down + ref[a].astype(jnp.float32)
            twice = lax.dot_general(
                down.astype(jnp.bfloat16),
                twofold,
                (((0,), (0,)), ((), ())),
                preferred_element_type=jnp.float32,
            )

            def step(weight_ref, firsts):
                placed = [jnp.where(label == first, twice, 0.0) for first in firsts]
                placed = jnp.concatenate(placed, axis=1).astype(jnp.bfloat16)
                delta_ref[...] += jnp.dot(
                    placed, weight_ref[...], preferred_element_type=jnp.float32
                )

            for_holders(met_ref, first_ref, near_refs, opened_ref, a, step)

        spot = pl.multiple_of(lax.rem(a, 2) * STEP, STEP)
        for s in range(senders):
            rows = slice(s * STEP, (s + 1) * STEP)
            for t in range(tiles):
                at = pl.multiple_of(t * kept + a * STEP, STEP)
                out_ref[s, pl.ds(at, STEP), :] = delta_ref[
                    rows, t * LANES : (t + 1) * LANES
                ].astype(jnp.bfloat16)
            turned = pltpu.roll(delta_ref[rows, tiles * LANES :], QUARTER * (a // 2), 1)
            ends_ref[s, pl.ds(spot, STEP), :] = jnp.where(
                group_lane == a // 2, turned, ends_ref[s, pl.ds(spot, STEP), :]
            )
        return carry

    lax.fori_loop(0, kept // STEP, one, 0)
    for s in range(senders):
        out_ref[s, tiles * kept :, :] = ends_ref[s].astype(jnp.bfloat16)


def mix_kernel(whole, target_ref, tokens_ref, returned_ref, out_ref):
    total = tokens_ref.shape[0]
    tiles = whole // LANES
    quads, kept = returned_ref.shape[0] // QUAD, (returned_ref.shape[1] - QUARTER) // tiles
    lane = lanes_of(total)
    spot = lax.broadcasted_iota(jnp.int32, (total, quads * kept), 1)
    place = spot // kept * total + spot % kept
    chosen = jnp.where(target_ref[...] == place, 1.0, 0.0).astype(jnp.bfloat16)
    end = jnp.zeros((total, LANES), jnp.float32)
    for j in range(QUAD):
        shares = []
        for q in range(quads):
            d = q * QUAD + j
            parts = [returned_ref[d, t * kept : (t + 1) * kept, :] for t in range(tiles)]
            packed = returned_ref[d, tiles * kept :, :].astype(jnp.float32)
            groups = [packed]
            for m in range(1, QUAD):
                groups.append(pltpu.roll(packed, LANES - QUARTER * m, 1))
            parts.append(jnp.concatenate(groups, axis=0)[0:kept].astype(jnp.bfloat16))
            shares.append(jnp.concatenate(parts, axis=1))
        share = jnp.concatenate(shares, axis=0)
        delta = jnp.dot(chosen, share, preferred_element_type=jnp.float32)
        columns = pl.ds(j * whole, whole)
        out_ref[:, columns] = (
            tokens_ref[:, columns].astype(jnp.float32) + delta[:, 0:whole]
        ).astype(jnp.bfloat16)
        last = delta[:, whole:]
        turned = pltpu.roll(last, QUARTER * j, 1) if j else last
        end = jnp.where((lane >= QUARTER * j) & (lane < QUARTER * (j + 1)), turned, end)
    columns = pl.ds(QUAD * whole, LANES)
    out_ref[:, columns] = (tokens_ref[:, columns].astype(jnp.float32) + end).astype(jnp.bfloat16)


def call(kernel, out_shape, in_specs, flops, moved, after=(), scratch=()):
    many = isinstance(out_shape, list)
    skipped = len(after)
    body = (lambda *refs: kernel(*refs[skipped:])) if skipped else kernel
    run = pl.pallas_call(
        body,
        out_shape=out_shape,
        in_specs=[pl.BlockSpec(memory_space=pl.ANY)] * skipped + in_specs,
        out_specs=[VMEM] * len(out_shape) if many else VMEM,
        scratch_shapes=scratch,
        compiler_params=pltpu.CompilerParams(vmem_limit_bytes=48 * 2**20),
        cost_estimate=pl.CostEstimate(flops=flops, bytes_accessed=moved, transcendentals=0),
    )
    return functools.partial(run, *after)


def exchange(value):
    return lax.all_to_all(value, "adapter", split_axis=0, concat_axis=0, tiled=True)


def towards(value, k, devices):
    return lax.ppermute(value, "adapter", [(i, i ^ k) for i in range(devices)])


def swapped(value):
    return lax.ppermute(value, "groups", [(0, 1), (1, 0)])


def note_scratch(devices):
    return [
        pltpu.VMEM((devices * STEP, LANES), jnp.bfloat16),
        pltpu.VMEM((8, devices * STEP), jnp.float32),
        pltpu.SMEM((8,), jnp.int32),
    ]


def note_kernel(note_ref, value_ref, out_ref, sem):
    rows = note_ref.shape[0]
    last = out_ref.at[pl.ds(out_ref.shape[0] - rows, rows)]
    copy = pltpu.make_async_copy(note_ref, last, sem)
    copy.start()
    copy.wait()


def with_note(value, note):
    return pl.pallas_call(
        note_kernel,
        out_shape=jax.ShapeDtypeStruct(value.shape, value.dtype),
        in_specs=[VMEM, pl.BlockSpec(memory_space=pl.ANY)],
        out_specs=pl.BlockSpec(memory_space=pl.ANY),
        scratch_shapes=[pltpu.SemaphoreType.DMA],
        input_output_aliases={1: 0},
    )(note, value)


def stand_behind(value, *earlier):
    return pl.pallas_call(
        lambda *refs: None,
        out_shape=jax.ShapeDtypeStruct(value.shape, value.dtype),
        in_specs=[pl.BlockSpec(memory_space=pl.ANY)] * (1 + len(earlier)),
        out_specs=pl.BlockSpec(memory_space=pl.ANY),
        input_output_aliases={0: 0},
    )(value, *earlier)


def back_and_mix(kept, tokens, target, first, arrived, sums, up_weights, *unused_values):
    blocks, rows, width = tokens.shape
    total = blocks * rows
    devices = arrived.shape[0]
    columns, share = up_weights[0].shape
    whole = share - LANES
    shape = (devices, whole // LANES * kept + QUARTER, LANES)
    leaving = call(
        up_kernel,
        jax.ShapeDtypeStruct(shape, jnp.bfloat16),
        [SMEM] + [VMEM] * (3 + len(up_weights)),
        2 * devices * kept * QUAD * columns * share,
        2 * (2 * devices * kept + QUAD * columns) * share,
        scratch=[
            pltpu.VMEM((2, columns, share), jnp.bfloat16),
            pltpu.VMEM((devices * STEP, share), jnp.float32),
            pltpu.VMEM((devices, QUARTER, LANES), jnp.float32),
            *note_scratch(devices),
        ],
    )(first, arrived, *sums, *up_weights)
    mixed = call(
        functools.partial(mix_kernel, whole),
        jax.ShapeDtypeStruct((total, width), jnp.bfloat16),
        [VMEM] * 3,
        2 * devices * kept * total * share,
        2 * (2 * total * width + devices * kept * share),
    )(target.reshape(total, 1), tokens.reshape(total, width), exchange(leaving))
    return mixed.reshape(tokens.shape)


def start_again(tokens, target, first, arrived, sums, up_weights, *arguments):
    return rows_to_holders(tokens, *arguments)


def rows_to_quads(
    tokens, request_block_adapter, request_block_rows, adapter_down_weight, adapter_up_weight
):
    blocks, rows, width = tokens.shape
    devices = lax.axis_size("adapter")
    resident, rank, unused_width = adapter_up_weight.shape
    total = blocks * rows
    columns = resident * rank
    whole = width // LANES // QUAD * LANES
    share = whole + LANES
    bf16, i32 = jnp.bfloat16, jnp.int32

    quad = request_block_adapter // (resident * QUAD)
    label = request_block_adapter - quad * (resident * QUAD) + 1
    order = request_block_adapter * blocks + jnp.arange(blocks, dtype=i32)
    same = quad[:, None] == quad[None, :]
    used = request_block_rows
    ahead = jnp.where(same & (order[None, :] < order[:, None]), used[None, :], 0)
    most = jnp.max(jnp.sum(jnp.where(same, used[None, :], 0), axis=1))
    row = jnp.arange(rows, dtype=i32)
    start = quad * total + jnp.sum(ahead, axis=1)
    target = jnp.where(row[None, :] < used[:, None], start[:, None] + row[None, :], -1)
    target = target.reshape(total).astype(i32)
    label = jnp.broadcast_to(label[:, None], (blocks, rows)).reshape(total, 1).astype(jnp.float32)

    me = lax.axis_index("adapter").astype(i32)
    group = lax.axis_index("groups").astype(i32)
    parts = jnp.bitwise_xor(me % QUAD, jnp.arange(QUAD, dtype=i32))
    halves = jnp.stack([group, 1 - group]) * (resident // 2)
    first = jnp.concatenate([parts * resident, halves]).astype(i32)
    tiles = whole // LANES

    def shares(weight, which, after):
        far = (columns // 2 * tiles + columns // 2 // QUAD + STEP, LANES)
        values = call(
            functools.partial(weight_kernel, whole, which),
            [jax.ShapeDtypeStruct((columns, share) if k < 2 else far, bf16) for k in which],
            [SMEM, SMEM, VMEM],
            0,
            len(which) * columns * width,
            after,
        )(parts, group.reshape(1), weight)
        return [towards(value, k, devices) if k else value for k, value in zip(which, values)]

    weight = adapter_down_weight.transpose(0, 2, 1).reshape(columns, width)
    down_weights = shares(weight, [0, 1, 2, 3], [])
    down_weights.append(swapped(down_weights[2]))
    weight = adapter_up_weight.reshape(columns, width)
    up_weights = shares(weight, [0, 1, 2], down_weights[2:3])
    up_weights += shares(weight, [3], down_weights[3:5])
    down_weights.append(swapped(down_weights[3]))

    caps = [total * 5 // 16, total * 6 // 16, total * 7 // 16]
    cap = caps[-1]
    arrived = exchange(
        call(
            functools.partial(pack_kernel, whole, cap),
            jax.ShapeDtypeStruct((devices, tiles * cap + QUARTER, LANES), bf16),
            [SMEM, VMEM, VMEM, VMEM],
            2 * devices * cap * total * share,
            2 * (total * width + devices * cap * share),
            (),
            [pltpu.VMEM((total, width), bf16)],
        )(most.reshape(1), target.reshape(1, total), label, tokens.reshape(total, width))
    )

    partial, count = call(
        down_kernel,
        [
            jax.ShapeDtypeStruct((cap // STEP, rank, devices * STEP), jnp.float32),
            jax.ShapeDtypeStruct((STEP, LANES), bf16),
        ],
        [SMEM] + [VMEM] * (1 + len(down_weights)),
        0,
        0,
        up_weights[2:3],
        [
            pltpu.VMEM((2, columns, share), bf16),
            pltpu.VMEM((devices * STEP, share), bf16),
            pltpu.VMEM((rank, devices * STEP), jnp.float32),
            *note_scratch(devices),
        ],
    )(first, arrived, *down_weights)
    up_weights[2] = with_note(up_weights[2], count)
    up_weights.append(swapped(up_weights[2]))
    up_weights[3] = stand_behind(up_weights[3], count)
    up_weights.append(swapped(up_weights[3]))
    pair = call(
        pair_kernel, jax.ShapeDtypeStruct(partial.shape, bf16), [VMEM, VMEM], 0, 0
    )(partial, towards(partial, 1, devices))
    sums = [pair, towards(pair, 2, devices)]
    most = jnp.maximum(count[0, 0], up_weights[4][-1, 0]).astype(jnp.float32)
    return lax.switch(
        sum((most > more).astype(i32) for more in caps),
        [functools.partial(back_and_mix, more) for more in caps] + [start_again],
        tokens,
        target,
        first,
        arrived,
        sums,
        up_weights,
        request_block_adapter,
        request_block_rows,
        adapter_down_weight,
        adapter_up_weight,
    )


def solution(mesh):
    placed = (
        P(("groups", "adapter"), None, None),
        P(("groups", "adapter")),
        P(("groups", "adapter")),
        P("adapter", None, None),
        P("adapter", None, None),
    )

    def per_device(tokens, request_block_adapter, request_block_rows, down_weight, up_weight):
        blocks, rows, width = tokens.shape
        devices = mesh.shape["adapter"]
        slots = max(1, 4 * blocks // devices)
        quads = devices % QUAD == 0 and slots * QUAD >= blocks
        quads = quads and width % (QUAD * LANES) == LANES and up_weight.shape[1] == HALF
        quads = quads and blocks * rows * 7 // 16 == 7 * STEP and mesh.shape["groups"] == 2
        plan = rows_to_quads if quads else rows_to_holders
        return plan(tokens, request_block_adapter, request_block_rows, down_weight, up_weight)

    return jax.shard_map(
        per_device,
        mesh=mesh,
        in_specs=placed,
        out_specs=P(("groups", "adapter"), None, None),
        check_vma=False,
    )
```

```python
import functools

import jax
import jax.numpy as jnp
from jax import lax
from jax.experimental import pallas as pl
from jax.experimental.pallas import tpu as pltpu
from jax.sharding import PartitionSpec as P

LANES = 128
HALF = 64
QUAD = 4
QUARTER = 32
STEP = 16
NOTE = 96
VMEM = pl.BlockSpec(memory_space=pltpu.VMEM)
SMEM = pl.BlockSpec(memory_space=pltpu.SMEM)


def normalise(tokens):
    values = tokens.astype(jnp.float32)
    mean_sq = jnp.mean(values * values, axis=-1, keepdims=True)
    return (values, (values * lax.rsqrt(mean_sq + 1e-06)).astype(jnp.bfloat16))


def resident_update(hidden_state, block_labels, adapter_down_weight, adapter_up_weight):
    feature_width = hidden_state.shape[-1]
    leading = hidden_state.shape[:-1]
    resident_rows, unused_value, inner_rank = adapter_down_weight.shape
    flattened_tokens = hidden_state.reshape(-1, feature_width)
    down_matrix = jnp.einsum(
        "tq,iqg->tig", flattened_tokens, adapter_down_weight, preferred_element_type=jnp.float32
    )
    down_matrix = down_matrix.astype(jnp.bfloat16).reshape(
        flattened_tokens.shape[0], resident_rows * inner_rank
    )
    column_owner = jnp.arange(resident_rows * inner_rank, dtype=jnp.int32) // inner_rank
    picked = block_labels.reshape(-1, 1) == column_owner[None, :]
    down_matrix = jnp.where(picked, down_matrix, jnp.zeros_like(down_matrix))
    lowrank_update = jnp.dot(
        down_matrix,
        adapter_up_weight.reshape(resident_rows * inner_rank, feature_width),
        preferred_element_type=jnp.float32,
    )
    return lowrank_update.astype(jnp.bfloat16).reshape(leading + (feature_width,))


def rows_to_holders(
    tokens, request_block_adapter, request_block_rows, adapter_down_weight, adapter_up_weight
):
    blocks, rows, feature_width = tokens.shape
    devices = lax.axis_size("adapter")
    resident_rows = adapter_down_weight.shape[0]
    slots = max(1, 4 * blocks // devices)
    values, normed = normalise(tokens)
    owner = request_block_adapter // resident_rows
    within = request_block_adapter - owner * resident_rows
    serial = jnp.arange(blocks, dtype=jnp.int32)
    earlier = (owner[:, None] == owner[None, :]) & (serial[None, :] < serial[:, None])
    position = owner * slots + jnp.sum(earlier, axis=1)
    outgoing = (
        jnp.zeros((devices * slots, rows, feature_width), jnp.bfloat16).at[position].set(normed)
    )
    outgoing = outgoing.reshape(devices, slots, rows, feature_width)
    block_labels = jnp.full((devices * slots,), -1, jnp.int32).at[position].set(within)
    block_labels = jnp.broadcast_to(block_labels[:, None], (devices * slots, rows)).reshape(
        devices, slots, rows
    )
    arriving_rows, row_markers = (
        lax.all_to_all(outgoing, "adapter", split_axis=0, concat_axis=0, tiled=True),
        lax.all_to_all(block_labels, "adapter", split_axis=0, concat_axis=0, tiled=True),
    )
    lowrank_update = resident_update(
        arriving_rows, row_markers, adapter_down_weight, adapter_up_weight
    )
    returned = lax.all_to_all(lowrank_update, "adapter", split_axis=0, concat_axis=0, tiled=True)
    mine = returned.reshape(devices * slots, rows, feature_width)[position]
    live = jnp.arange(rows, dtype=jnp.int32)[None, :] < request_block_rows[:, None]
    mixed = values + jnp.where(live[:, :, None], mine.astype(jnp.float32), jnp.float32(0.0))
    return mixed.astype(jnp.bfloat16)


def lanes_of(rows):
    return lax.broadcasted_iota(jnp.int32, (rows, LANES), 1)


def weight_kernel(whole, which, halved, part_ref, group_ref, weight_ref, *out_refs):
    tiles = whole // LANES
    for k, out_ref in zip(which, out_refs):
        j = part_ref[k]
        if k < 2:
            last = weight_ref[:, QUAD * whole :].astype(jnp.float32)
            turned = pltpu.roll(last, lax.rem(LANES - QUARTER * j, LANES), 1)
            inside = lanes_of(last.shape[0]) < QUARTER
            out_ref[:, 0:whole] = weight_ref[:, pl.ds(pl.multiple_of(j * whole, LANES), whole)]
            out_ref[:, whole:] = jnp.where(inside, turned, 0.0).astype(jnp.bfloat16)
            continue
        count = weight_ref.shape[0] // 2 if halved else weight_ref.shape[0]
        start = pl.multiple_of(group_ref[0] * count, count) if halved else 0
        for t in range(tiles):
            column = pl.multiple_of(j * whole + t * LANES, LANES)
            out_ref[t * count : (t + 1) * count, :] = weight_ref[
                pl.ds(start, count), pl.ds(column, LANES)
            ]
        last = weight_ref[pl.ds(start, count), QUAD * whole :].astype(jnp.float32)
        size = count // QUAD
        owner = lanes_of(size) // QUARTER
        merged = jnp.zeros((size, LANES), jnp.float32)
        for m in range(QUAD):
            shift = lax.rem(LANES + QUARTER * (m - j), LANES)
            turned = pltpu.roll(last[m * size : (m + 1) * size], shift, 1)
            merged = jnp.where(owner == m, turned, merged)
        out_ref[tiles * count :, :] = merged.astype(jnp.bfloat16)


def open_far(far_refs, opened_ref):
    count, width = 2 * opened_ref.shape[1] // len(far_refs), opened_ref.shape[2]
    tiles, size = width // LANES - 1, count // QUAD
    inside = lanes_of(size) < QUARTER
    for i, ref in enumerate(far_refs):
        holder, base = i % 2, i // 2 * count
        for t in range(tiles):
            opened_ref[holder, base : base + count, t * LANES : (t + 1) * LANES] = ref[
                t * count : (t + 1) * count, :
            ]
        packed = ref[tiles * count :, :].astype(jnp.float32)
        for m in range(QUAD):
            turned = pltpu.roll(packed, (LANES - QUARTER * m) % LANES, 1) if m else packed
            opened_ref[holder, base + m * size : base + (m + 1) * size, tiles * LANES :] = (
                jnp.where(inside, turned, 0.0).astype(jnp.bfloat16)
            )


def pack_kernel(whole, cap, most_ref, target_ref, label_ref, tokens_ref, out_ref, normed_ref):
    values = tokens_ref[...].astype(jnp.float32)
    mean_sq = jnp.mean(values * values, axis=-1, keepdims=True)
    normed_ref[...] = (values * lax.rsqrt(mean_sq + 1e-06)).astype(jnp.bfloat16)
    total = tokens_ref.shape[0]
    quads, tiles = out_ref.shape[0] // QUAD, whole // LANES
    lane = lanes_of(total)
    last = normed_ref[:, QUAD * whole :].astype(jnp.float32)
    label = jnp.where(lane == QUARTER, label_ref[...], 0.0)
    ends = []
    for j in range(QUAD):
        turned = pltpu.roll(last, (LANES - QUARTER * j) % LANES, 1) if j else last
        ends.append(jnp.where(lane < QUARTER, turned, label).astype(jnp.bfloat16))
    most = most_ref[0].astype(jnp.float32)
    group_lane = lanes_of(QUARTER) // QUARTER
    step_lane = lanes_of(STEP)
    for q in range(quads):
        place = lax.broadcasted_iota(jnp.int32, (cap, total), 0) + q * total
        chosen = jnp.where(target_ref[...] == place, 1.0, 0.0).astype(jnp.bfloat16)
        for j in range(QUAD):
            share = jnp.dot(
                chosen,
                normed_ref[:, j * whole : (j + 1) * whole],
                preferred_element_type=jnp.float32,
            ).astype(jnp.bfloat16)
            for t in range(tiles):
                out_ref[q * QUAD + j, t * cap : (t + 1) * cap, :] = share[
                    :, t * LANES : (t + 1) * LANES
                ]
            end = jnp.dot(chosen, ends[j], preferred_element_type=jnp.float32)
            if j == 0:
                notes = jnp.where(step_lane == NOTE + cap // STEP, most, 0.0)
                for a in range(cap // STEP):
                    turned = pltpu.roll(end[a * STEP : (a + 1) * STEP], NOTE + a - QUARTER, 1)
                    notes = jnp.where(step_lane == NOTE + a, turned, notes)
            padded = jnp.concatenate(
                [end, jnp.zeros((QUAD * QUARTER - cap, LANES), jnp.float32)], axis=0
            )
            merged = padded[0:QUARTER]
            for m in range(1, QUAD):
                turned = pltpu.roll(padded[m * QUARTER : (m + 1) * QUARTER], m * QUARTER, 1)
                merged = jnp.where(group_lane == m, turned, merged)
            out_ref[q * QUAD + j, tiles * cap : tiles * cap + STEP, :] = merged[0:STEP].astype(
                jnp.bfloat16
            )
            out_ref[q * QUAD + j, tiles * cap + STEP :, :] = jnp.where(
                step_lane >= NOTE, notes, merged[STEP:]
            ).astype(jnp.bfloat16)


def read_notes(rows_ref, cap, tiles, part_ref, resident, notes_ref, labels_ref, met_ref):
    senders = rows_ref.shape[0]
    for s in range(senders):
        notes_ref[s * STEP : (s + 1) * STEP, :] = rows_ref[s, tiles * cap + STEP :, :]
    steps = labels_ref.shape[0]
    row = lax.broadcasted_iota(jnp.int32, (steps, LANES), 0)
    wanted = jnp.where(lanes_of(steps) == NOTE + row, 1.0, 0.0).astype(jnp.bfloat16)
    labels = lax.dot_general(
        wanted, notes_ref[...], (((1,), (1,)), ((), ())), preferred_element_type=jnp.float32
    )
    labels_ref[...] = labels
    code = jnp.zeros((steps, 1), jnp.float32)
    for h in range(QUAD):
        first = part_ref[h].astype(jnp.float32) + 1.0
        met = jnp.where((labels >= first) & (labels < first + resident), 1.0, 0.0)
        code = code + (1 << h) * jnp.max(met, axis=1, keepdims=True)
    at = lax.broadcasted_iota(jnp.int32, (steps, 1), 0)
    for a in range(cap // STEP):
        met_ref[a] = jnp.max(jnp.where(at == a, code, 0.0)).astype(jnp.int32)


def for_holders(met_ref, first_ref, near_refs, opened_ref, halved, a, step):
    pairs = opened_ref.shape[1] // LANES
    for h in range(QUAD):
        base = first_ref[h].astype(jnp.float32) + 1.0
        firsts = [base + 2.0 * t for t in range(pairs)]
        if h >= 2 and halved:
            firsts = [
                base + first_ref[QUAD + i].astype(jnp.float32) + 2.0 * t
                for i in range(2)
                for t in range(pairs // 2)
            ]

        @pl.when(lax.rem(met_ref[a] // (1 << h), 2) > 0)
        def _(h=h, firsts=firsts):
            step(near_refs[h] if h < 2 else opened_ref.at[h - 2], firsts)


def down_kernel(first_ref, rows_ref, *refs):
    near_refs, far_refs, out_ref, count_ref = refs[:2], refs[2:6], refs[6], refs[7]
    opened_ref, batch_ref, picked_ref, notes_ref, labels_ref, met_ref = refs[8:]
    senders, width = rows_ref.shape[0], batch_ref.shape[1]
    tiles = width // LANES - 1
    cap = out_ref.shape[0] * STEP
    rank = out_ref.shape[1]
    resident = opened_ref.shape[1] // rank
    dims = (((1,), (1,)), ((), ()))
    read_notes(rows_ref, cap, tiles, first_ref, resident, notes_ref, labels_ref, met_ref)
    notes = notes_ref[...].astype(jnp.float32)
    is_count = lanes_of(senders * STEP) == NOTE + cap // STEP
    count = jnp.max(jnp.where(is_count, notes, 0.0), axis=(0, 1), keepdims=True)
    count_ref[...] = jnp.broadcast_to(count, count_ref.shape).astype(jnp.bfloat16)
    open_far(far_refs, opened_ref)

    def one(a, carry):
        picked_ref[...] = jnp.zeros(picked_ref.shape, jnp.float32)

        @pl.when(met_ref[a] > 0)
        def _():
            shift = lax.rem(LANES - QUARTER * (a // 2), LANES)
            spot = pl.multiple_of(tiles * cap + lax.rem(a, 2) * STEP, STEP)
            for s in range(senders):
                rows = slice(s * STEP, (s + 1) * STEP)
                for t in range(tiles):
                    at = pl.multiple_of(t * cap + a * STEP, STEP)
                    batch_ref[rows, t * LANES : (t + 1) * LANES] = rows_ref[s, pl.ds(at, STEP), :]
                end = rows_ref[s, pl.ds(spot, STEP), :].astype(jnp.float32)
                batch_ref[rows, tiles * LANES :] = pltpu.roll(end, shift, 1).astype(jnp.bfloat16)
            label = labels_ref[pl.ds(a, 1), :]

            def step(weight_ref, firsts):
                product = lax.dot_general(
                    weight_ref[...], batch_ref[...], dims, preferred_element_type=jnp.float32
                )
                picked = picked_ref[...]
                for t, first in enumerate(firsts):
                    for i in range(2):
                        at = (2 * t + i) * rank
                        picked = jnp.where(
                            label == first + i, product[at : at + rank, :], picked
                        )
                picked_ref[...] = picked

            for_holders(met_ref, first_ref, near_refs, opened_ref, True, a, step)

        out_ref[a] = picked_ref[...]
        return carry

    lax.fori_loop(0, cap // STEP, one, 0)


def pair_kernel(own_ref, other_ref, out_ref):
    out_ref[...] = (own_ref[...] + other_ref[...]).astype(jnp.bfloat16)


def up_kernel(first_ref, rows_ref, *refs):
    sum_refs, near_refs, far_refs, out_ref = refs[:2], refs[2:4], refs[4:6], refs[6]
    opened_ref, delta_ref, ends_ref, notes_ref, labels_ref, met_ref = refs[7:]
    senders, width = rows_ref.shape[0], opened_ref.shape[2]
    tiles = width // LANES - 1
    cap, rank = sum_refs[0].shape[0] * STEP, sum_refs[0].shape[1]
    resident = opened_ref.shape[1] // rank
    kept = (out_ref.shape[1] - QUARTER) // tiles
    group_lane = lanes_of(STEP) // QUARTER
    read_notes(rows_ref, cap, tiles, first_ref, resident, notes_ref, labels_ref, met_ref)
    open_far(far_refs, opened_ref)
    ends_ref[...] = jnp.zeros(ends_ref.shape, jnp.float32)
    low = jnp.where(lanes_of(senders * STEP) < HALF, 0.0, 1.0)
    rank_row = lax.broadcasted_iota(jnp.int32, (rank, LANES), 0)
    twofold = jnp.where(lax.rem(lanes_of(rank), rank) == rank_row, 1.0, 0.0).astype(jnp.bfloat16)

    def one(a, carry):
        delta_ref[...] = jnp.zeros(delta_ref.shape, jnp.float32)

        @pl.when(met_ref[a] > 0)
        def _():
            note_row = lax.broadcasted_iota(jnp.int32, (LANES, LANES), 0)
            wanted = jnp.where(note_row == NOTE + a, 1.0, 0.0).astype(jnp.bfloat16)
            label = jnp.dot(notes_ref[...], wanted, preferred_element_type=jnp.float32) - low
            down = sum_refs[0][a].astype(jnp.float32)
            for ref in sum_refs[1:]:
                down = down + ref[a].astype(jnp.float32)
            twice = lax.dot_general(
                down.astype(jnp.bfloat16),
                twofold,
                (((0,), (0,)), ((), ())),
                preferred_element_type=jnp.float32,
            )

            def step(weight_ref, firsts):
                placed = [jnp.where(label == first, twice, 0.0) for first in firsts]
                placed = jnp.concatenate(placed, axis=1).astype(jnp.bfloat16)
                delta_ref[...] += jnp.dot(
                    placed, weight_ref[...], preferred_element_type=jnp.float32
                )

            for_holders(met_ref, first_ref, near_refs, opened_ref, False, a, step)

        spot = pl.multiple_of(lax.rem(a, 2) * STEP, STEP)
        for s in range(senders):
            rows = slice(s * STEP, (s + 1) * STEP)
            for t in range(tiles):
                at = pl.multiple_of(t * kept + a * STEP, STEP)
                out_ref[s, pl.ds(at, STEP), :] = delta_ref[
                    rows, t * LANES : (t + 1) * LANES
                ].astype(jnp.bfloat16)
            turned = pltpu.roll(delta_ref[rows, tiles * LANES :], QUARTER * (a // 2), 1)
            ends_ref[s, pl.ds(spot, STEP), :] = jnp.where(
                group_lane == a // 2, turned, ends_ref[s, pl.ds(spot, STEP), :]
            )
        return carry

    lax.fori_loop(0, kept // STEP, one, 0)
    for s in range(senders):
        out_ref[s, tiles * kept :, :] = ends_ref[s].astype(jnp.bfloat16)


def mix_kernel(whole, target_ref, tokens_ref, returned_ref, out_ref):
    total = tokens_ref.shape[0]
    tiles = whole // LANES
    quads, kept = returned_ref.shape[0] // QUAD, (returned_ref.shape[1] - QUARTER) // tiles
    lane = lanes_of(total)
    spot = lax.broadcasted_iota(jnp.int32, (total, quads * kept), 1)
    place = spot // kept * total + spot % kept
    chosen = jnp.where(target_ref[...] == place, 1.0, 0.0).astype(jnp.bfloat16)
    end = jnp.zeros((total, LANES), jnp.float32)
    for j in range(QUAD):
        shares = []
        for q in range(quads):
            d = q * QUAD + j
            parts = [returned_ref[d, t * kept : (t + 1) * kept, :] for t in range(tiles)]
            packed = returned_ref[d, tiles * kept :, :].astype(jnp.float32)
            groups = [packed]
            for m in range(1, QUAD):
                groups.append(pltpu.roll(packed, LANES - QUARTER * m, 1))
            parts.append(jnp.concatenate(groups, axis=0)[0:kept].astype(jnp.bfloat16))
            shares.append(jnp.concatenate(parts, axis=1))
        share = jnp.concatenate(shares, axis=0)
        delta = jnp.dot(chosen, share, preferred_element_type=jnp.float32)
        columns = pl.ds(j * whole, whole)
        out_ref[:, columns] = (
            tokens_ref[:, columns].astype(jnp.float32) + delta[:, 0:whole]
        ).astype(jnp.bfloat16)
        last = delta[:, whole:]
        turned = pltpu.roll(last, QUARTER * j, 1) if j else last
        end = jnp.where((lane >= QUARTER * j) & (lane < QUARTER * (j + 1)), turned, end)
    columns = pl.ds(QUAD * whole, LANES)
    out_ref[:, columns] = (tokens_ref[:, columns].astype(jnp.float32) + end).astype(jnp.bfloat16)


def call(kernel, out_shape, in_specs, flops, moved, after=(), scratch=()):
    many = isinstance(out_shape, list)
    skipped = len(after)
    body = (lambda *refs: kernel(*refs[skipped:])) if skipped else kernel
    run = pl.pallas_call(
        body,
        out_shape=out_shape,
        in_specs=[pl.BlockSpec(memory_space=pl.ANY)] * skipped + in_specs,
        out_specs=[VMEM] * len(out_shape) if many else VMEM,
        scratch_shapes=scratch,
        compiler_params=pltpu.CompilerParams(vmem_limit_bytes=48 * 2**20),
        cost_estimate=pl.CostEstimate(flops=flops, bytes_accessed=moved, transcendentals=0),
    )
    return functools.partial(run, *after)


def exchange(value):
    return lax.all_to_all(value, "adapter", split_axis=0, concat_axis=0, tiled=True)


def towards(value, k, devices):
    return lax.ppermute(value, "adapter", [(i, i ^ k) for i in range(devices)])


def swapped(value):
    return lax.ppermute(value, "groups", [(0, 1), (1, 0)])


def note_scratch(devices):
    return [
        pltpu.VMEM((devices * STEP, LANES), jnp.bfloat16),
        pltpu.VMEM((8, devices * STEP), jnp.float32),
        pltpu.SMEM((8,), jnp.int32),
    ]


def back_and_mix(kept, tokens, target, first, arrived, sums, up_weights, *unused_values):
    blocks, rows, width = tokens.shape
    total = blocks * rows
    devices = arrived.shape[0]
    columns, share = up_weights[0].shape
    whole = share - LANES
    shape = (devices, whole // LANES * kept + QUARTER, LANES)
    leaving = call(
        up_kernel,
        jax.ShapeDtypeStruct(shape, jnp.bfloat16),
        [SMEM] + [VMEM] * (3 + len(up_weights)),
        2 * devices * kept * QUAD * columns * share,
        2 * (2 * devices * kept + QUAD * columns) * share,
        scratch=[
            pltpu.VMEM((2, columns, share), jnp.bfloat16),
            pltpu.VMEM((devices * STEP, share), jnp.float32),
            pltpu.VMEM((devices, QUARTER, LANES), jnp.float32),
            *note_scratch(devices),
        ],
    )(first, arrived, *sums, *up_weights)
    mixed = call(
        functools.partial(mix_kernel, whole),
        jax.ShapeDtypeStruct((total, width), jnp.bfloat16),
        [VMEM] * 3,
        2 * devices * kept * total * share,
        2 * (2 * total * width + devices * kept * share),
    )(target.reshape(total, 1), tokens.reshape(total, width), exchange(leaving))
    return mixed.reshape(tokens.shape)


def start_again(tokens, target, first, arrived, sums, up_weights, *arguments):
    return rows_to_holders(tokens, *arguments)


def rows_to_quads(
    tokens, request_block_adapter, request_block_rows, adapter_down_weight, adapter_up_weight
):
    blocks, rows, width = tokens.shape
    devices = lax.axis_size("adapter")
    resident, rank, unused_width = adapter_up_weight.shape
    total = blocks * rows
    columns = resident * rank
    whole = width // LANES // QUAD * LANES
    share = whole + LANES
    bf16, i32 = jnp.bfloat16, jnp.int32

    quad = request_block_adapter // (resident * QUAD)
    label = request_block_adapter - quad * (resident * QUAD) + 1
    order = request_block_adapter * blocks + jnp.arange(blocks, dtype=i32)
    same = quad[:, None] == quad[None, :]
    used = request_block_rows
    ahead = jnp.where(same & (order[None, :] < order[:, None]), used[None, :], 0)
    most = jnp.max(jnp.sum(jnp.where(same, used[None, :], 0), axis=1))
    row = jnp.arange(rows, dtype=i32)
    start = quad * total + jnp.sum(ahead, axis=1)
    target = jnp.where(row[None, :] < used[:, None], start[:, None] + row[None, :], -1)
    target = target.reshape(total).astype(i32)
    label = jnp.broadcast_to(label[:, None], (blocks, rows)).reshape(total, 1).astype(jnp.float32)

    me = lax.axis_index("adapter").astype(i32)
    group = lax.axis_index("groups").astype(i32)
    parts = jnp.bitwise_xor(me % QUAD, jnp.arange(QUAD, dtype=i32))
    halves = jnp.stack([group, 1 - group]) * (resident // 2)
    first = jnp.concatenate([parts * resident, halves]).astype(i32)
    tiles = whole // LANES

    def shares(weight, which, halved, after):
        count = columns // 2 if halved else columns
        far = (count * tiles + count // QUAD, LANES)
        values = call(
            functools.partial(weight_kernel, whole, which, halved),
            [jax.ShapeDtypeStruct((columns, share) if k < 2 else far, bf16) for k in which],
            [SMEM, SMEM, VMEM],
            0,
            len(which) * columns * width,
            after,
        )(parts, group.reshape(1), weight)
        return [towards(value, k, devices) if k else value for k, value in zip(which, values)]

    weight = adapter_down_weight.transpose(0, 2, 1).reshape(columns, width)
    down_weights = shares(weight, [0, 1, 2, 3], True, [])
    down_weights.append(swapped(down_weights[2]))
    weight = adapter_up_weight.reshape(columns, width)
    up_weights = shares(weight, [0, 1, 2], False, down_weights[2:3])
    up_weights += shares(weight, [3], False, down_weights[3:5])
    down_weights.append(swapped(down_weights[3]))

    caps = [total * 5 // 16, total * 6 // 16, total * 7 // 16]
    cap = caps[-1]
    arrived = exchange(
        call(
            functools.partial(pack_kernel, whole, cap),
            jax.ShapeDtypeStruct((devices, tiles * cap + QUARTER, LANES), bf16),
            [SMEM, VMEM, VMEM, VMEM],
            2 * devices * cap * total * share,
            2 * (total * width + devices * cap * share),
            (),
            [pltpu.VMEM((total, width), bf16)],
        )(most.reshape(1), target.reshape(1, total), label, tokens.reshape(total, width))
    )

    partial, count = call(
        down_kernel,
        [
            jax.ShapeDtypeStruct((cap // STEP, rank, devices * STEP), jnp.float32),
            jax.ShapeDtypeStruct((STEP, LANES), bf16),
        ],
        [SMEM] + [VMEM] * (1 + len(down_weights)),
        0,
        0,
        up_weights[:1],
        [
            pltpu.VMEM((2, columns, share), bf16),
            pltpu.VMEM((devices * STEP, share), bf16),
            pltpu.VMEM((rank, devices * STEP), jnp.float32),
            *note_scratch(devices),
        ],
    )(first, arrived, *down_weights)
    pair = call(
        pair_kernel, jax.ShapeDtypeStruct(partial.shape, bf16), [VMEM, VMEM], 0, 0
    )(partial, towards(partial, 1, devices))
    sums = [pair, towards(pair, 2, devices)]
    count = count[0:1, 0:1]
    most = jnp.maximum(count, swapped(count))[0, 0].astype(jnp.float32)
    return lax.switch(
        sum((most > more).astype(i32) for more in caps),
        [functools.partial(back_and_mix, more) for more in caps] + [start_again],
        tokens,
        target,
        first,
        arrived,
        sums,
        up_weights,
        request_block_adapter,
        request_block_rows,
        adapter_down_weight,
        adapter_up_weight,
    )


def solution(mesh):
    placed = (
        P(("groups", "adapter"), None, None),
        P(("groups", "adapter")),
        P(("groups", "adapter")),
        P("adapter", None, None),
        P("adapter", None, None),
    )

    def per_device(tokens, request_block_adapter, request_block_rows, down_weight, up_weight):
        blocks, rows, width = tokens.shape
        devices = mesh.shape["adapter"]
        slots = max(1, 4 * blocks // devices)
        quads = devices % QUAD == 0 and slots * QUAD >= blocks
        quads = quads and width % (QUAD * LANES) == LANES and up_weight.shape[1] == HALF
        quads = quads and blocks * rows * 7 // 16 == 7 * STEP and mesh.shape["groups"] == 2
        plan = rows_to_quads if quads else rows_to_holders
        return plan(tokens, request_block_adapter, request_block_rows, down_weight, up_weight)

    return jax.shard_map(
        per_device,
        mesh=mesh,
        in_specs=placed,
        out_specs=P(("groups", "adapter"), None, None),
        check_vma=False,
    )
```

```python
import functools

import jax
import jax.numpy as jnp
from jax import lax
from jax.experimental import pallas as pl
from jax.experimental.pallas import tpu as pltpu
from jax.sharding import PartitionSpec as P

LANES = 128
HALF = 64
QUAD = 4
QUARTER = 32
STEP = 16
NOTE = 96
VMEM = pl.BlockSpec(memory_space=pltpu.VMEM)
SMEM = pl.BlockSpec(memory_space=pltpu.SMEM)


def normalise(tokens):
    values = tokens.astype(jnp.float32)
    mean_sq = jnp.mean(values * values, axis=-1, keepdims=True)
    return (values, (values * lax.rsqrt(mean_sq + 1e-06)).astype(jnp.bfloat16))


def resident_update(hidden_state, block_labels, adapter_down_weight, adapter_up_weight):
    feature_width = hidden_state.shape[-1]
    leading = hidden_state.shape[:-1]
    resident_rows, unused_value, inner_rank = adapter_down_weight.shape
    flattened_tokens = hidden_state.reshape(-1, feature_width)
    down_matrix = jnp.einsum(
        "tq,iqg->tig", flattened_tokens, adapter_down_weight, preferred_element_type=jnp.float32
    )
    down_matrix = down_matrix.astype(jnp.bfloat16).reshape(
        flattened_tokens.shape[0], resident_rows * inner_rank
    )
    column_owner = jnp.arange(resident_rows * inner_rank, dtype=jnp.int32) // inner_rank
    picked = block_labels.reshape(-1, 1) == column_owner[None, :]
    down_matrix = jnp.where(picked, down_matrix, jnp.zeros_like(down_matrix))
    lowrank_update = jnp.dot(
        down_matrix,
        adapter_up_weight.reshape(resident_rows * inner_rank, feature_width),
        preferred_element_type=jnp.float32,
    )
    return lowrank_update.astype(jnp.bfloat16).reshape(leading + (feature_width,))


def rows_to_holders(
    tokens, request_block_adapter, request_block_rows, adapter_down_weight, adapter_up_weight
):
    blocks, rows, feature_width = tokens.shape
    devices = lax.axis_size("adapter")
    resident_rows = adapter_down_weight.shape[0]
    slots = max(1, 4 * blocks // devices)
    values, normed = normalise(tokens)
    owner = request_block_adapter // resident_rows
    within = request_block_adapter - owner * resident_rows
    serial = jnp.arange(blocks, dtype=jnp.int32)
    earlier = (owner[:, None] == owner[None, :]) & (serial[None, :] < serial[:, None])
    position = owner * slots + jnp.sum(earlier, axis=1)
    outgoing = (
        jnp.zeros((devices * slots, rows, feature_width), jnp.bfloat16).at[position].set(normed)
    )
    outgoing = outgoing.reshape(devices, slots, rows, feature_width)
    block_labels = jnp.full((devices * slots,), -1, jnp.int32).at[position].set(within)
    block_labels = jnp.broadcast_to(block_labels[:, None], (devices * slots, rows)).reshape(
        devices, slots, rows
    )
    arriving_rows, row_markers = (
        lax.all_to_all(outgoing, "adapter", split_axis=0, concat_axis=0, tiled=True),
        lax.all_to_all(block_labels, "adapter", split_axis=0, concat_axis=0, tiled=True),
    )
    lowrank_update = resident_update(
        arriving_rows, row_markers, adapter_down_weight, adapter_up_weight
    )
    returned = lax.all_to_all(lowrank_update, "adapter", split_axis=0, concat_axis=0, tiled=True)
    mine = returned.reshape(devices * slots, rows, feature_width)[position]
    live = jnp.arange(rows, dtype=jnp.int32)[None, :] < request_block_rows[:, None]
    mixed = values + jnp.where(live[:, :, None], mine.astype(jnp.float32), jnp.float32(0.0))
    return mixed.astype(jnp.bfloat16)


def lanes_of(rows):
    return lax.broadcasted_iota(jnp.int32, (rows, LANES), 1)


def weight_kernel(whole, which, halved, part_ref, group_ref, weight_ref, *out_refs):
    tiles = whole // LANES
    for k, out_ref in zip(which, out_refs):
        j = part_ref[k]
        if k < 2:
            last = weight_ref[:, QUAD * whole :].astype(jnp.float32)
            turned = pltpu.roll(last, lax.rem(LANES - QUARTER * j, LANES), 1)
            inside = lanes_of(last.shape[0]) < QUARTER
            out_ref[:, 0:whole] = weight_ref[:, pl.ds(pl.multiple_of(j * whole, LANES), whole)]
            out_ref[:, whole:] = jnp.where(inside, turned, 0.0).astype(jnp.bfloat16)
            continue
        count = weight_ref.shape[0] // 2 if halved else weight_ref.shape[0]
        start = pl.multiple_of(group_ref[0] * count, count) if halved else 0
        for t in range(tiles):
            column = pl.multiple_of(j * whole + t * LANES, LANES)
            out_ref[t * count : (t + 1) * count, :] = weight_ref[
                pl.ds(start, count), pl.ds(column, LANES)
            ]
        last = weight_ref[pl.ds(start, count), QUAD * whole :].astype(jnp.float32)
        size = count // QUAD
        owner = lanes_of(size) // QUARTER
        merged = jnp.zeros((size, LANES), jnp.float32)
        for m in range(QUAD):
            shift = lax.rem(LANES + QUARTER * (m - j), LANES)
            turned = pltpu.roll(last[m * size : (m + 1) * size], shift, 1)
            merged = jnp.where(owner == m, turned, merged)
        out_ref[tiles * count :, :] = merged.astype(jnp.bfloat16)


def open_far(far_refs, opened_ref):
    count, width = 2 * opened_ref.shape[1] // len(far_refs), opened_ref.shape[2]
    tiles, size = width // LANES - 1, count // QUAD
    inside = lanes_of(size) < QUARTER
    for i, ref in enumerate(far_refs):
        holder, base = i % 2, i // 2 * count
        for t in range(tiles):
            opened_ref[holder, base : base + count, t * LANES : (t + 1) * LANES] = ref[
                t * count : (t + 1) * count, :
            ]
        packed = ref[tiles * count :, :].astype(jnp.float32)
        for m in range(QUAD):
            turned = pltpu.roll(packed, (LANES - QUARTER * m) % LANES, 1) if m else packed
            opened_ref[holder, base + m * size : base + (m + 1) * size, tiles * LANES :] = (
                jnp.where(inside, turned, 0.0).astype(jnp.bfloat16)
            )


def pack_kernel(whole, cap, most_ref, target_ref, label_ref, tokens_ref, out_ref, normed_ref):
    values = tokens_ref[...].astype(jnp.float32)
    mean_sq = jnp.mean(values * values, axis=-1, keepdims=True)
    normed_ref[...] = (values * lax.rsqrt(mean_sq + 1e-06)).astype(jnp.bfloat16)
    total = tokens_ref.shape[0]
    quads, tiles = out_ref.shape[0] // QUAD, whole // LANES
    lane = lanes_of(total)
    last = normed_ref[:, QUAD * whole :].astype(jnp.float32)
    label = jnp.where(lane == QUARTER, label_ref[...], 0.0)
    ends = []
    for j in range(QUAD):
        turned = pltpu.roll(last, (LANES - QUARTER * j) % LANES, 1) if j else last
        ends.append(jnp.where(lane < QUARTER, turned, label).astype(jnp.bfloat16))
    most = most_ref[0].astype(jnp.float32)
    group_lane = lanes_of(QUARTER) // QUARTER
    step_lane = lanes_of(STEP)
    for q in range(quads):
        place = lax.broadcasted_iota(jnp.int32, (cap, total), 0) + q * total
        chosen = jnp.where(target_ref[...] == place, 1.0, 0.0).astype(jnp.bfloat16)
        for j in range(QUAD):
            share = jnp.dot(
                chosen,
                normed_ref[:, j * whole : (j + 1) * whole],
                preferred_element_type=jnp.float32,
            ).astype(jnp.bfloat16)
            for t in range(tiles):
                out_ref[q * QUAD + j, t * cap : (t + 1) * cap, :] = share[
                    :, t * LANES : (t + 1) * LANES
                ]
            end = jnp.dot(chosen, ends[j], preferred_element_type=jnp.float32)
            if j == 0:
                notes = jnp.where(step_lane == NOTE + cap // STEP, most, 0.0)
                for a in range(cap // STEP):
                    turned = pltpu.roll(end[a * STEP : (a + 1) * STEP], NOTE + a - QUARTER, 1)
                    notes = jnp.where(step_lane == NOTE + a, turned, notes)
            padded = jnp.concatenate(
                [end, jnp.zeros((QUAD * QUARTER - cap, LANES), jnp.float32)], axis=0
            )
            merged = padded[0:QUARTER]
            for m in range(1, QUAD):
                turned = pltpu.roll(padded[m * QUARTER : (m + 1) * QUARTER], m * QUARTER, 1)
                merged = jnp.where(group_lane == m, turned, merged)
            out_ref[q * QUAD + j, tiles * cap : tiles * cap + STEP, :] = merged[0:STEP].astype(
                jnp.bfloat16
            )
            out_ref[q * QUAD + j, tiles * cap + STEP :, :] = jnp.where(
                step_lane >= NOTE, notes, merged[STEP:]
            ).astype(jnp.bfloat16)


def read_notes(rows_ref, cap, tiles, part_ref, resident, notes_ref, labels_ref, met_ref):
    senders = rows_ref.shape[0]
    for s in range(senders):
        notes_ref[s * STEP : (s + 1) * STEP, :] = rows_ref[s, tiles * cap + STEP :, :]
    steps = labels_ref.shape[0]
    row = lax.broadcasted_iota(jnp.int32, (steps, LANES), 0)
    wanted = jnp.where(lanes_of(steps) == NOTE + row, 1.0, 0.0).astype(jnp.bfloat16)
    labels = lax.dot_general(
        wanted, notes_ref[...], (((1,), (1,)), ((), ())), preferred_element_type=jnp.float32
    )
    labels_ref[...] = labels
    code = jnp.zeros((steps, 1), jnp.float32)
    for h in range(QUAD):
        first = part_ref[h].astype(jnp.float32) + 1.0
        met = jnp.where((labels >= first) & (labels < first + resident), 1.0, 0.0)
        code = code + (1 << h) * jnp.max(met, axis=1, keepdims=True)
    at = lax.broadcasted_iota(jnp.int32, (steps, 1), 0)
    for a in range(cap // STEP):
        met_ref[a] = jnp.max(jnp.where(at == a, code, 0.0)).astype(jnp.int32)


def for_holders(met_ref, first_ref, near_refs, opened_ref, halved, a, step):
    pairs = opened_ref.shape[1] // LANES
    for h in range(QUAD):
        base = first_ref[h].astype(jnp.float32) + 1.0
        firsts = [base + 2.0 * t for t in range(pairs)]
        if h >= 2 and halved:
            firsts = [
                base + first_ref[QUAD + i].astype(jnp.float32) + 2.0 * t
                for i in range(2)
                for t in range(pairs // 2)
            ]

        @pl.when(lax.rem(met_ref[a] // (1 << h), 2) > 0)
        def _(h=h, firsts=firsts):
            step(near_refs[h] if h < 2 else opened_ref.at[h - 2], firsts)


def down_kernel(first_ref, rows_ref, *refs):
    near_refs, far_refs, out_ref, count_ref = refs[:2], refs[2:6], refs[6], refs[7]
    opened_ref, batch_ref, picked_ref, notes_ref, labels_ref, met_ref = refs[8:]
    senders, width = rows_ref.shape[0], batch_ref.shape[1]
    tiles = width // LANES - 1
    cap = out_ref.shape[0] * STEP
    rank = out_ref.shape[1]
    resident = opened_ref.shape[1] // rank
    dims = (((1,), (1,)), ((), ()))
    read_notes(rows_ref, cap, tiles, first_ref, resident, notes_ref, labels_ref, met_ref)
    notes = notes_ref[...].astype(jnp.float32)
    is_count = lanes_of(senders * STEP) == NOTE + cap // STEP
    count = jnp.max(jnp.where(is_count, notes, 0.0), axis=(0, 1), keepdims=True)
    count_ref[...] = jnp.broadcast_to(count, count_ref.shape).astype(jnp.bfloat16)
    open_far(far_refs, opened_ref)

    def one(a, carry):
        picked_ref[...] = jnp.zeros(picked_ref.shape, jnp.float32)

        @pl.when(met_ref[a] > 0)
        def _():
            shift = lax.rem(LANES - QUARTER * (a // 2), LANES)
            spot = pl.multiple_of(tiles * cap + lax.rem(a, 2) * STEP, STEP)
            for s in range(senders):
                rows = slice(s * STEP, (s + 1) * STEP)
                for t in range(tiles):
                    at = pl.multiple_of(t * cap + a * STEP, STEP)
                    batch_ref[rows, t * LANES : (t + 1) * LANES] = rows_ref[s, pl.ds(at, STEP), :]
                end = rows_ref[s, pl.ds(spot, STEP), :].astype(jnp.float32)
                batch_ref[rows, tiles * LANES :] = pltpu.roll(end, shift, 1).astype(jnp.bfloat16)
            label = labels_ref[pl.ds(a, 1), :]

            def step(weight_ref, firsts):
                product = lax.dot_general(
                    weight_ref[...], batch_ref[...], dims, preferred_element_type=jnp.float32
                )
                picked = picked_ref[...]
                for t, first in enumerate(firsts):
                    for i in range(2):
                        at = (2 * t + i) * rank
                        picked = jnp.where(
                            label == first + i, product[at : at + rank, :], picked
                        )
                picked_ref[...] = picked

            for_holders(met_ref, first_ref, near_refs, opened_ref, True, a, step)

        out_ref[a] = picked_ref[...]
        return carry

    lax.fori_loop(0, cap // STEP, one, 0)


def pair_kernel(own_ref, other_ref, out_ref):
    out_ref[...] = (own_ref[...] + other_ref[...]).astype(jnp.bfloat16)


def up_kernel(first_ref, rows_ref, *refs):
    sum_refs, near_refs, far_refs, out_ref = refs[:2], refs[2:4], refs[4:6], refs[6]
    opened_ref, delta_ref, ends_ref, notes_ref, labels_ref, met_ref = refs[7:]
    senders, width = rows_ref.shape[0], opened_ref.shape[2]
    tiles = width // LANES - 1
    cap, rank = sum_refs[0].shape[0] * STEP, sum_refs[0].shape[1]
    resident = opened_ref.shape[1] // rank
    kept = (out_ref.shape[1] - QUARTER) // tiles
    group_lane = lanes_of(STEP) // QUARTER
    read_notes(rows_ref, cap, tiles, first_ref, resident, notes_ref, labels_ref, met_ref)
    open_far(far_refs, opened_ref)
    ends_ref[...] = jnp.zeros(ends_ref.shape, jnp.float32)
    low = jnp.where(lanes_of(senders * STEP) < HALF, 0.0, 1.0)
    rank_row = lax.broadcasted_iota(jnp.int32, (rank, LANES), 0)
    twofold = jnp.where(lax.rem(lanes_of(rank), rank) == rank_row, 1.0, 0.0).astype(jnp.bfloat16)

    def one(a, carry):
        delta_ref[...] = jnp.zeros(delta_ref.shape, jnp.float32)

        @pl.when(met_ref[a] > 0)
        def _():
            note_row = lax.broadcasted_iota(jnp.int32, (LANES, LANES), 0)
            wanted = jnp.where(note_row == NOTE + a, 1.0, 0.0).astype(jnp.bfloat16)
            label = jnp.dot(notes_ref[...], wanted, preferred_element_type=jnp.float32) - low
            down = sum_refs[0][a].astype(jnp.float32)
            for ref in sum_refs[1:]:
                down = down + ref[a].astype(jnp.float32)
            twice = lax.dot_general(
                down.astype(jnp.bfloat16),
                twofold,
                (((0,), (0,)), ((), ())),
                preferred_element_type=jnp.float32,
            )

            def step(weight_ref, firsts):
                placed = [jnp.where(label == first, twice, 0.0) for first in firsts]
                placed = jnp.concatenate(placed, axis=1).astype(jnp.bfloat16)
                delta_ref[...] += jnp.dot(
                    placed, weight_ref[...], preferred_element_type=jnp.float32
                )

            for_holders(met_ref, first_ref, near_refs, opened_ref, False, a, step)

        spot = pl.multiple_of(lax.rem(a, 2) * STEP, STEP)
        for s in range(senders):
            rows = slice(s * STEP, (s + 1) * STEP)
            for t in range(tiles):
                at = pl.multiple_of(t * kept + a * STEP, STEP)
                out_ref[s, pl.ds(at, STEP), :] = delta_ref[
                    rows, t * LANES : (t + 1) * LANES
                ].astype(jnp.bfloat16)
            turned = pltpu.roll(delta_ref[rows, tiles * LANES :], QUARTER * (a // 2), 1)
            ends_ref[s, pl.ds(spot, STEP), :] = jnp.where(
                group_lane == a // 2, turned, ends_ref[s, pl.ds(spot, STEP), :]
            )
        return carry

    lax.fori_loop(0, kept // STEP, one, 0)
    for s in range(senders):
        out_ref[s, tiles * kept :, :] = ends_ref[s].astype(jnp.bfloat16)


def mix_kernel(whole, target_ref, tokens_ref, returned_ref, out_ref):
    total = tokens_ref.shape[0]
    tiles = whole // LANES
    quads, kept = returned_ref.shape[0] // QUAD, (returned_ref.shape[1] - QUARTER) // tiles
    lane = lanes_of(total)
    spot = lax.broadcasted_iota(jnp.int32, (total, quads * kept), 1)
    place = spot // kept * total + spot % kept
    chosen = jnp.where(target_ref[...] == place, 1.0, 0.0).astype(jnp.bfloat16)
    end = jnp.zeros((total, LANES), jnp.float32)
    for j in range(QUAD):
        shares = []
        for q in range(quads):
            d = q * QUAD + j
            parts = [returned_ref[d, t * kept : (t + 1) * kept, :] for t in range(tiles)]
            packed = returned_ref[d, tiles * kept :, :].astype(jnp.float32)
            groups = [packed]
            for m in range(1, QUAD):
                groups.append(pltpu.roll(packed, LANES - QUARTER * m, 1))
            parts.append(jnp.concatenate(groups, axis=0)[0:kept].astype(jnp.bfloat16))
            shares.append(jnp.concatenate(parts, axis=1))
        share = jnp.concatenate(shares, axis=0)
        delta = jnp.dot(chosen, share, preferred_element_type=jnp.float32)
        columns = pl.ds(j * whole, whole)
        out_ref[:, columns] = (
            tokens_ref[:, columns].astype(jnp.float32) + delta[:, 0:whole]
        ).astype(jnp.bfloat16)
        last = delta[:, whole:]
        turned = pltpu.roll(last, QUARTER * j, 1) if j else last
        end = jnp.where((lane >= QUARTER * j) & (lane < QUARTER * (j + 1)), turned, end)
    columns = pl.ds(QUAD * whole, LANES)
    out_ref[:, columns] = (tokens_ref[:, columns].astype(jnp.float32) + end).astype(jnp.bfloat16)


def call(kernel, out_shape, in_specs, flops, moved, after=(), scratch=()):
    many = isinstance(out_shape, list)
    skipped = len(after)
    body = (lambda *refs: kernel(*refs[skipped:])) if skipped else kernel
    run = pl.pallas_call(
        body,
        out_shape=out_shape,
        in_specs=[pl.BlockSpec(memory_space=pl.ANY)] * skipped + in_specs,
        out_specs=[VMEM] * len(out_shape) if many else VMEM,
        scratch_shapes=scratch,
        compiler_params=pltpu.CompilerParams(vmem_limit_bytes=48 * 2**20),
        cost_estimate=pl.CostEstimate(flops=flops, bytes_accessed=moved, transcendentals=0),
    )
    return functools.partial(run, *after)


def exchange(value):
    return lax.all_to_all(value, "adapter", split_axis=0, concat_axis=0, tiled=True)


def towards(value, k, devices):
    return lax.ppermute(value, "adapter", [(i, i ^ k) for i in range(devices)])


def swapped(value):
    return lax.ppermute(value, "groups", [(0, 1), (1, 0)])


def stand_behind(value, *earlier):
    return pl.pallas_call(
        lambda *refs: None,
        out_shape=jax.ShapeDtypeStruct(value.shape, value.dtype),
        in_specs=[pl.BlockSpec(memory_space=pl.ANY)] * (1 + len(earlier)),
        out_specs=pl.BlockSpec(memory_space=pl.ANY),
        input_output_aliases={0: 0},
    )(value, *earlier)


def note_scratch(devices):
    return [
        pltpu.VMEM((devices * STEP, LANES), jnp.bfloat16),
        pltpu.VMEM((8, devices * STEP), jnp.float32),
        pltpu.SMEM((8,), jnp.int32),
    ]


def back_and_mix(kept, tokens, target, first, arrived, sums, up_weights, *unused_values):
    blocks, rows, width = tokens.shape
    total = blocks * rows
    devices = arrived.shape[0]
    columns, share = up_weights[0].shape
    whole = share - LANES
    shape = (devices, whole // LANES * kept + QUARTER, LANES)
    leaving = call(
        up_kernel,
        jax.ShapeDtypeStruct(shape, jnp.bfloat16),
        [SMEM] + [VMEM] * (3 + len(up_weights)),
        2 * devices * kept * QUAD * columns * share,
        2 * (2 * devices * kept + QUAD * columns) * share,
        scratch=[
            pltpu.VMEM((2, columns, share), jnp.bfloat16),
            pltpu.VMEM((devices * STEP, share), jnp.float32),
            pltpu.VMEM((devices, QUARTER, LANES), jnp.float32),
            *note_scratch(devices),
        ],
    )(first, arrived, *sums, *up_weights)
    mixed = call(
        functools.partial(mix_kernel, whole),
        jax.ShapeDtypeStruct((total, width), jnp.bfloat16),
        [VMEM] * 3,
        2 * devices * kept * total * share,
        2 * (2 * total * width + devices * kept * share),
    )(target.reshape(total, 1), tokens.reshape(total, width), exchange(leaving))
    return mixed.reshape(tokens.shape)


def start_again(tokens, target, first, arrived, sums, up_weights, *arguments):
    return rows_to_holders(tokens, *arguments)


def rows_to_quads(
    tokens, request_block_adapter, request_block_rows, adapter_down_weight, adapter_up_weight
):
    blocks, rows, width = tokens.shape
    devices = lax.axis_size("adapter")
    resident, rank, unused_width = adapter_up_weight.shape
    total = blocks * rows
    columns = resident * rank
    whole = width // LANES // QUAD * LANES
    share = whole + LANES
    bf16, i32 = jnp.bfloat16, jnp.int32

    quad = request_block_adapter // (resident * QUAD)
    label = request_block_adapter - quad * (resident * QUAD) + 1
    order = request_block_adapter * blocks + jnp.arange(blocks, dtype=i32)
    same = quad[:, None] == quad[None, :]
    used = request_block_rows
    ahead = jnp.where(same & (order[None, :] < order[:, None]), used[None, :], 0)
    most = jnp.max(jnp.sum(jnp.where(same, used[None, :], 0), axis=1))
    row = jnp.arange(rows, dtype=i32)
    start = quad * total + jnp.sum(ahead, axis=1)
    target = jnp.where(row[None, :] < used[:, None], start[:, None] + row[None, :], -1)
    target = target.reshape(total).astype(i32)
    label = jnp.broadcast_to(label[:, None], (blocks, rows)).reshape(total, 1).astype(jnp.float32)

    me = lax.axis_index("adapter").astype(i32)
    group = lax.axis_index("groups").astype(i32)
    parts = jnp.bitwise_xor(me % QUAD, jnp.arange(QUAD, dtype=i32))
    halves = jnp.stack([group, 1 - group]) * (resident // 2)
    first = jnp.concatenate([parts * resident, halves]).astype(i32)
    tiles = whole // LANES

    def shares(weight, which, halved, after):
        count = columns // 2 if halved else columns
        far = (count * tiles + count // QUAD, LANES)
        values = call(
            functools.partial(weight_kernel, whole, which, halved),
            [jax.ShapeDtypeStruct((columns, share) if k < 2 else far, bf16) for k in which],
            [SMEM, SMEM, VMEM],
            0,
            len(which) * columns * width,
            after,
        )(parts, group.reshape(1), weight)
        return [towards(value, k, devices) if k else value for k, value in zip(which, values)]

    weight = adapter_down_weight.transpose(0, 2, 1).reshape(columns, width)
    down_weights = shares(weight, [0, 1, 2, 3], True, [])
    weight = adapter_up_weight.reshape(columns, width)
    up_weights = shares(weight, [0, 1, 2, 3], False, down_weights[:1])
    down_weights[2] = stand_behind(down_weights[2], up_weights[0])
    down_weights += [swapped(down_weights[2]), swapped(down_weights[3])]

    caps = [total * 5 // 16, total * 6 // 16, total * 7 // 16]
    cap = caps[-1]
    arrived = exchange(
        call(
            functools.partial(pack_kernel, whole, cap),
            jax.ShapeDtypeStruct((devices, tiles * cap + QUARTER, LANES), bf16),
            [SMEM, VMEM, VMEM, VMEM],
            2 * devices * cap * total * share,
            2 * (total * width + devices * cap * share),
            (),
            [pltpu.VMEM((total, width), bf16)],
        )(most.reshape(1), target.reshape(1, total), label, tokens.reshape(total, width))
    )

    partial, count = call(
        down_kernel,
        [
            jax.ShapeDtypeStruct((cap // STEP, rank, devices * STEP), jnp.float32),
            jax.ShapeDtypeStruct((STEP, LANES), bf16),
        ],
        [SMEM] + [VMEM] * (1 + len(down_weights)),
        0,
        0,
        up_weights[:1],
        [
            pltpu.VMEM((2, columns, share), bf16),
            pltpu.VMEM((devices * STEP, share), bf16),
            pltpu.VMEM((rank, devices * STEP), jnp.float32),
            *note_scratch(devices),
        ],
    )(first, arrived, *down_weights)
    pair = call(
        pair_kernel, jax.ShapeDtypeStruct(partial.shape, bf16), [VMEM, VMEM], 0, 0
    )(partial, towards(partial, 1, devices))
    sums = [pair, towards(pair, 2, devices)]
    count = count[0:1, 0:1]
    most = jnp.maximum(count, swapped(count))[0, 0].astype(jnp.float32)
    return lax.switch(
        sum((most > more).astype(i32) for more in caps),
        [functools.partial(back_and_mix, more) for more in caps] + [start_again],
        tokens,
        target,
        first,
        arrived,
        sums,
        up_weights,
        request_block_adapter,
        request_block_rows,
        adapter_down_weight,
        adapter_up_weight,
    )


def solution(mesh):
    placed = (
        P(("groups", "adapter"), None, None),
        P(("groups", "adapter")),
        P(("groups", "adapter")),
        P("adapter", None, None),
        P("adapter", None, None),
    )

    def per_device(tokens, request_block_adapter, request_block_rows, down_weight, up_weight):
        blocks, rows, width = tokens.shape
        devices = mesh.shape["adapter"]
        slots = max(1, 4 * blocks // devices)
        quads = devices % QUAD == 0 and slots * QUAD >= blocks
        quads = quads and width % (QUAD * LANES) == LANES and up_weight.shape[1] == HALF
        quads = quads and blocks * rows * 7 // 16 == 7 * STEP and mesh.shape["groups"] == 2
        plan = rows_to_quads if quads else rows_to_holders
        return plan(tokens, request_block_adapter, request_block_rows, down_weight, up_weight)

    return jax.shard_map(
        per_device,
        mesh=mesh,
        in_specs=placed,
        out_specs=P(("groups", "adapter"), None, None),
        check_vma=False,
    )
```

```python
import functools

import jax
import jax.numpy as jnp
from jax import lax
from jax.experimental import pallas as pl
from jax.experimental.pallas import tpu as pltpu
from jax.sharding import PartitionSpec as P

LANES = 128
HALF = 64
QUAD = 4
QUARTER = 32
STEP = 16
NOTE = 96
DOWN_HALVED = (2, 3)
UP_HALVED = (2,)
VMEM = pl.BlockSpec(memory_space=pltpu.VMEM)
SMEM = pl.BlockSpec(memory_space=pltpu.SMEM)


def normalise(tokens):
    values = tokens.astype(jnp.float32)
    mean_sq = jnp.mean(values * values, axis=-1, keepdims=True)
    return (values, (values * lax.rsqrt(mean_sq + 1e-06)).astype(jnp.bfloat16))


def resident_update(hidden_state, block_labels, adapter_down_weight, adapter_up_weight):
    feature_width = hidden_state.shape[-1]
    leading = hidden_state.shape[:-1]
    resident_rows, unused_value, inner_rank = adapter_down_weight.shape
    flattened_tokens = hidden_state.reshape(-1, feature_width)
    down_matrix = jnp.einsum(
        "tq,iqg->tig", flattened_tokens, adapter_down_weight, preferred_element_type=jnp.float32
    )
    down_matrix = down_matrix.astype(jnp.bfloat16).reshape(
        flattened_tokens.shape[0], resident_rows * inner_rank
    )
    column_owner = jnp.arange(resident_rows * inner_rank, dtype=jnp.int32) // inner_rank
    picked = block_labels.reshape(-1, 1) == column_owner[None, :]
    down_matrix = jnp.where(picked, down_matrix, jnp.zeros_like(down_matrix))
    lowrank_update = jnp.dot(
        down_matrix,
        adapter_up_weight.reshape(resident_rows * inner_rank, feature_width),
        preferred_element_type=jnp.float32,
    )
    return lowrank_update.astype(jnp.bfloat16).reshape(leading + (feature_width,))


def rows_to_holders(
    tokens, request_block_adapter, request_block_rows, adapter_down_weight, adapter_up_weight
):
    blocks, rows, feature_width = tokens.shape
    devices = lax.axis_size("adapter")
    resident_rows = adapter_down_weight.shape[0]
    slots = max(1, 4 * blocks // devices)
    values, normed = normalise(tokens)
    owner = request_block_adapter // resident_rows
    within = request_block_adapter - owner * resident_rows
    serial = jnp.arange(blocks, dtype=jnp.int32)
    earlier = (owner[:, None] == owner[None, :]) & (serial[None, :] < serial[:, None])
    position = owner * slots + jnp.sum(earlier, axis=1)
    outgoing = (
        jnp.zeros((devices * slots, rows, feature_width), jnp.bfloat16).at[position].set(normed)
    )
    outgoing = outgoing.reshape(devices, slots, rows, feature_width)
    block_labels = jnp.full((devices * slots,), -1, jnp.int32).at[position].set(within)
    block_labels = jnp.broadcast_to(block_labels[:, None], (devices * slots, rows)).reshape(
        devices, slots, rows
    )
    arriving_rows, row_markers = (
        lax.all_to_all(outgoing, "adapter", split_axis=0, concat_axis=0, tiled=True),
        lax.all_to_all(block_labels, "adapter", split_axis=0, concat_axis=0, tiled=True),
    )
    lowrank_update = resident_update(
        arriving_rows, row_markers, adapter_down_weight, adapter_up_weight
    )
    returned = lax.all_to_all(lowrank_update, "adapter", split_axis=0, concat_axis=0, tiled=True)
    mine = returned.reshape(devices * slots, rows, feature_width)[position]
    live = jnp.arange(rows, dtype=jnp.int32)[None, :] < request_block_rows[:, None]
    mixed = values + jnp.where(live[:, :, None], mine.astype(jnp.float32), jnp.float32(0.0))
    return mixed.astype(jnp.bfloat16)


def lanes_of(rows):
    return lax.broadcasted_iota(jnp.int32, (rows, LANES), 1)


def weight_kernel(whole, which, halved, part_ref, group_ref, weight_ref, *out_refs):
    tiles = whole // LANES
    for k, out_ref in zip(which, out_refs):
        j = part_ref[k]
        if k < 2:
            last = weight_ref[:, QUAD * whole :].astype(jnp.float32)
            turned = pltpu.roll(last, lax.rem(LANES - QUARTER * j, LANES), 1)
            inside = lanes_of(last.shape[0]) < QUARTER
            out_ref[:, 0:whole] = weight_ref[:, pl.ds(pl.multiple_of(j * whole, LANES), whole)]
            out_ref[:, whole:] = jnp.where(inside, turned, 0.0).astype(jnp.bfloat16)
            continue
        count = weight_ref.shape[0] // 2 if k in halved else weight_ref.shape[0]
        start = pl.multiple_of(group_ref[0] * count, count) if k in halved else 0
        for t in range(tiles):
            column = pl.multiple_of(j * whole + t * LANES, LANES)
            out_ref[t * count : (t + 1) * count, :] = weight_ref[
                pl.ds(start, count), pl.ds(column, LANES)
            ]
        last = weight_ref[pl.ds(start, count), QUAD * whole :].astype(jnp.float32)
        size = count // QUAD
        owner = lanes_of(size) // QUARTER
        merged = jnp.zeros((size, LANES), jnp.float32)
        for m in range(QUAD):
            shift = lax.rem(LANES + QUARTER * (m - j), LANES)
            turned = pltpu.roll(last[m * size : (m + 1) * size], shift, 1)
            merged = jnp.where(owner == m, turned, merged)
        out_ref[tiles * count :, :] = merged.astype(jnp.bfloat16)


def open_far(far_refs, halved, opened_ref):
    width = opened_ref.shape[2]
    tiles = width // LANES - 1
    places = [(k - 2, 0) for k in (2, 3)] + [(k - 2, 1) for k in halved]
    for ref, (holder, part) in zip(far_refs, places):
        count = opened_ref.shape[1] // 2 if holder + 2 in halved else opened_ref.shape[1]
        base, size = part * count, count // QUAD
        inside = lanes_of(size) < QUARTER
        for t in range(tiles):
            opened_ref[holder, base : base + count, t * LANES : (t + 1) * LANES] = ref[
                t * count : (t + 1) * count, :
            ]
        packed = ref[tiles * count :, :].astype(jnp.float32)
        for m in range(QUAD):
            turned = pltpu.roll(packed, (LANES - QUARTER * m) % LANES, 1) if m else packed
            opened_ref[holder, base + m * size : base + (m + 1) * size, tiles * LANES :] = (
                jnp.where(inside, turned, 0.0).astype(jnp.bfloat16)
            )


def pack_kernel(whole, cap, most_ref, target_ref, label_ref, tokens_ref, out_ref, normed_ref):
    values = tokens_ref[...].astype(jnp.float32)
    mean_sq = jnp.mean(values * values, axis=-1, keepdims=True)
    normed_ref[...] = (values * lax.rsqrt(mean_sq + 1e-06)).astype(jnp.bfloat16)
    total = tokens_ref.shape[0]
    quads, tiles = out_ref.shape[0] // QUAD, whole // LANES
    lane = lanes_of(total)
    last = normed_ref[:, QUAD * whole :].astype(jnp.float32)
    label = jnp.where(lane == QUARTER, label_ref[...], 0.0)
    ends = []
    for j in range(QUAD):
        turned = pltpu.roll(last, (LANES - QUARTER * j) % LANES, 1) if j else last
        ends.append(jnp.where(lane < QUARTER, turned, label).astype(jnp.bfloat16))
    most = most_ref[0].astype(jnp.float32)
    group_lane = lanes_of(QUARTER) // QUARTER
    step_lane = lanes_of(STEP)
    for q in range(quads):
        place = lax.broadcasted_iota(jnp.int32, (cap, total), 0) + q * total
        chosen = jnp.where(target_ref[...] == place, 1.0, 0.0).astype(jnp.bfloat16)
        for j in range(QUAD):
            share = jnp.dot(
                chosen,
                normed_ref[:, j * whole : (j + 1) * whole],
                preferred_element_type=jnp.float32,
            ).astype(jnp.bfloat16)
            for t in range(tiles):
                out_ref[q * QUAD + j, t * cap : (t + 1) * cap, :] = share[
                    :, t * LANES : (t + 1) * LANES
                ]
            end = jnp.dot(chosen, ends[j], preferred_element_type=jnp.float32)
            if j == 0:
                notes = jnp.where(step_lane == NOTE + cap // STEP, most, 0.0)
                for a in range(cap // STEP):
                    turned = pltpu.roll(end[a * STEP : (a + 1) * STEP], NOTE + a - QUARTER, 1)
                    notes = jnp.where(step_lane == NOTE + a, turned, notes)
            padded = jnp.concatenate(
                [end, jnp.zeros((QUAD * QUARTER - cap, LANES), jnp.float32)], axis=0
            )
            merged = padded[0:QUARTER]
            for m in range(1, QUAD):
                turned = pltpu.roll(padded[m * QUARTER : (m + 1) * QUARTER], m * QUARTER, 1)
                merged = jnp.where(group_lane == m, turned, merged)
            out_ref[q * QUAD + j, tiles * cap : tiles * cap + STEP, :] = merged[0:STEP].astype(
                jnp.bfloat16
            )
            out_ref[q * QUAD + j, tiles * cap + STEP :, :] = jnp.where(
                step_lane >= NOTE, notes, merged[STEP:]
            ).astype(jnp.bfloat16)


def read_notes(rows_ref, cap, tiles, part_ref, resident, notes_ref, labels_ref, met_ref):
    senders = rows_ref.shape[0]
    for s in range(senders):
        notes_ref[s * STEP : (s + 1) * STEP, :] = rows_ref[s, tiles * cap + STEP :, :]
    steps = labels_ref.shape[0]
    row = lax.broadcasted_iota(jnp.int32, (steps, LANES), 0)
    wanted = jnp.where(lanes_of(steps) == NOTE + row, 1.0, 0.0).astype(jnp.bfloat16)
    labels = lax.dot_general(
        wanted, notes_ref[...], (((1,), (1,)), ((), ())), preferred_element_type=jnp.float32
    )
    labels_ref[...] = labels
    code = jnp.zeros((steps, 1), jnp.float32)
    for h in range(QUAD):
        first = part_ref[h].astype(jnp.float32) + 1.0
        met = jnp.where((labels >= first) & (labels < first + resident), 1.0, 0.0)
        code = code + (1 << h) * jnp.max(met, axis=1, keepdims=True)
    at = lax.broadcasted_iota(jnp.int32, (steps, 1), 0)
    for a in range(cap // STEP):
        met_ref[a] = jnp.max(jnp.where(at == a, code, 0.0)).astype(jnp.int32)


def for_holders(met_ref, first_ref, near_refs, opened_ref, halved, a, step):
    pairs = opened_ref.shape[1] // LANES
    for h in range(QUAD):
        base = first_ref[h].astype(jnp.float32) + 1.0
        firsts = [base + 2.0 * t for t in range(pairs)]
        if h in halved:
            firsts = [
                base + first_ref[QUAD + i].astype(jnp.float32) + 2.0 * t
                for i in range(2)
                for t in range(pairs // 2)
            ]

        @pl.when(lax.rem(met_ref[a] // (1 << h), 2) > 0)
        def _(h=h, firsts=firsts):
            step(near_refs[h] if h < 2 else opened_ref.at[h - 2], firsts)


def down_kernel(first_ref, rows_ref, *refs):
    near_refs, far_refs, out_ref, count_ref = refs[:2], refs[2:6], refs[6], refs[7]
    opened_ref, batch_ref, picked_ref, notes_ref, labels_ref, met_ref = refs[8:]
    senders, width = rows_ref.shape[0], batch_ref.shape[1]
    tiles = width // LANES - 1
    cap = out_ref.shape[0] * STEP
    rank = out_ref.shape[1]
    resident = opened_ref.shape[1] // rank
    dims = (((1,), (1,)), ((), ()))
    read_notes(rows_ref, cap, tiles, first_ref, resident, notes_ref, labels_ref, met_ref)
    notes = notes_ref[...].astype(jnp.float32)
    is_count = lanes_of(senders * STEP) == NOTE + cap // STEP
    count = jnp.max(jnp.where(is_count, notes, 0.0), axis=(0, 1), keepdims=True)
    count_ref[...] = jnp.broadcast_to(count, count_ref.shape).astype(jnp.bfloat16)
    open_far(far_refs, DOWN_HALVED, opened_ref)

    def one(a, carry):
        picked_ref[...] = jnp.zeros(picked_ref.shape, jnp.float32)

        @pl.when(met_ref[a] > 0)
        def _():
            shift = lax.rem(LANES - QUARTER * (a // 2), LANES)
            spot = pl.multiple_of(tiles * cap + lax.rem(a, 2) * STEP, STEP)
            for s in range(senders):
                rows = slice(s * STEP, (s + 1) * STEP)
                for t in range(tiles):
                    at = pl.multiple_of(t * cap + a * STEP, STEP)
                    batch_ref[rows, t * LANES : (t + 1) * LANES] = rows_ref[s, pl.ds(at, STEP), :]
                end = rows_ref[s, pl.ds(spot, STEP), :].astype(jnp.float32)
                batch_ref[rows, tiles * LANES :] = pltpu.roll(end, shift, 1).astype(jnp.bfloat16)
            label = labels_ref[pl.ds(a, 1), :]

            def step(weight_ref, firsts):
                product = lax.dot_general(
                    weight_ref[...], batch_ref[...], dims, preferred_element_type=jnp.float32
                )
                picked = picked_ref[...]
                for t, first in enumerate(firsts):
                    for i in range(2):
                        at = (2 * t + i) * rank
                        picked = jnp.where(
                            label == first + i, product[at : at + rank, :], picked
                        )
                picked_ref[...] = picked

            for_holders(met_ref, first_ref, near_refs, opened_ref, DOWN_HALVED, a, step)

        out_ref[a] = picked_ref[...]
        return carry

    lax.fori_loop(0, cap // STEP, one, 0)


def pair_kernel(own_ref, other_ref, out_ref):
    out_ref[...] = (own_ref[...] + other_ref[...]).astype(jnp.bfloat16)


def up_kernel(first_ref, rows_ref, *refs):
    sum_refs, near_refs, far_refs, out_ref = refs[:2], refs[2:4], refs[4:7], refs[7]
    opened_ref, delta_ref, ends_ref, notes_ref, labels_ref, met_ref = refs[8:]
    senders, width = rows_ref.shape[0], opened_ref.shape[2]
    tiles = width // LANES - 1
    cap, rank = sum_refs[0].shape[0] * STEP, sum_refs[0].shape[1]
    resident = opened_ref.shape[1] // rank
    kept = (out_ref.shape[1] - QUARTER) // tiles
    group_lane = lanes_of(STEP) // QUARTER
    read_notes(rows_ref, cap, tiles, first_ref, resident, notes_ref, labels_ref, met_ref)
    open_far(far_refs, UP_HALVED, opened_ref)
    ends_ref[...] = jnp.zeros(ends_ref.shape, jnp.float32)
    low = jnp.where(lanes_of(senders * STEP) < HALF, 0.0, 1.0)
    rank_row = lax.broadcasted_iota(jnp.int32, (rank, LANES), 0)
    twofold = jnp.where(lax.rem(lanes_of(rank), rank) == rank_row, 1.0, 0.0).astype(jnp.bfloat16)

    def one(a, carry):
        delta_ref[...] = jnp.zeros(delta_ref.shape, jnp.float32)

        @pl.when(met_ref[a] > 0)
        def _():
            note_row = lax.broadcasted_iota(jnp.int32, (LANES, LANES), 0)
            wanted = jnp.where(note_row == NOTE + a, 1.0, 0.0).astype(jnp.bfloat16)
            label = jnp.dot(notes_ref[...], wanted, preferred_element_type=jnp.float32) - low
            down = sum_refs[0][a].astype(jnp.float32)
            for ref in sum_refs[1:]:
                down = down + ref[a].astype(jnp.float32)
            twice = lax.dot_general(
                down.astype(jnp.bfloat16),
                twofold,
                (((0,), (0,)), ((), ())),
                preferred_element_type=jnp.float32,
            )

            def step(weight_ref, firsts):
                placed = [jnp.where(label == first, twice, 0.0) for first in firsts]
                placed = jnp.concatenate(placed, axis=1).astype(jnp.bfloat16)
                delta_ref[...] += jnp.dot(
                    placed, weight_ref[...], preferred_element_type=jnp.float32
                )

            for_holders(met_ref, first_ref, near_refs, opened_ref, UP_HALVED, a, step)

        spot = pl.multiple_of(lax.rem(a, 2) * STEP, STEP)
        for s in range(senders):
            rows = slice(s * STEP, (s + 1) * STEP)
            for t in range(tiles):
                at = pl.multiple_of(t * kept + a * STEP, STEP)
                out_ref[s, pl.ds(at, STEP), :] = delta_ref[
                    rows, t * LANES : (t + 1) * LANES
                ].astype(jnp.bfloat16)
            turned = pltpu.roll(delta_ref[rows, tiles * LANES :], QUARTER * (a // 2), 1)
            ends_ref[s, pl.ds(spot, STEP), :] = jnp.where(
                group_lane == a // 2, turned, ends_ref[s, pl.ds(spot, STEP), :]
            )
        return carry

    lax.fori_loop(0, kept // STEP, one, 0)
    for s in range(senders):
        out_ref[s, tiles * kept :, :] = ends_ref[s].astype(jnp.bfloat16)


def mix_kernel(whole, target_ref, tokens_ref, returned_ref, out_ref):
    total = tokens_ref.shape[0]
    tiles = whole // LANES
    quads, kept = returned_ref.shape[0] // QUAD, (returned_ref.shape[1] - QUARTER) // tiles
    lane = lanes_of(total)
    spot = lax.broadcasted_iota(jnp.int32, (total, quads * kept), 1)
    place = spot // kept * total + spot % kept
    chosen = jnp.where(target_ref[...] == place, 1.0, 0.0).astype(jnp.bfloat16)
    end = jnp.zeros((total, LANES), jnp.float32)
    for j in range(QUAD):
        shares = []
        for q in range(quads):
            d = q * QUAD + j
            parts = [returned_ref[d, t * kept : (t + 1) * kept, :] for t in range(tiles)]
            packed = returned_ref[d, tiles * kept :, :].astype(jnp.float32)
            groups = [packed]
            for m in range(1, QUAD):
                groups.append(pltpu.roll(packed, LANES - QUARTER * m, 1))
            parts.append(jnp.concatenate(groups, axis=0)[0:kept].astype(jnp.bfloat16))
            shares.append(jnp.concatenate(parts, axis=1))
        share = jnp.concatenate(shares, axis=0)
        delta = jnp.dot(chosen, share, preferred_element_type=jnp.float32)
        columns = pl.ds(j * whole, whole)
        out_ref[:, columns] = (
            tokens_ref[:, columns].astype(jnp.float32) + delta[:, 0:whole]
        ).astype(jnp.bfloat16)
        last = delta[:, whole:]
        turned = pltpu.roll(last, QUARTER * j, 1) if j else last
        end = jnp.where((lane >= QUARTER * j) & (lane < QUARTER * (j + 1)), turned, end)
    columns = pl.ds(QUAD * whole, LANES)
    out_ref[:, columns] = (tokens_ref[:, columns].astype(jnp.float32) + end).astype(jnp.bfloat16)


def call(kernel, out_shape, in_specs, flops, moved, after=(), scratch=()):
    many = isinstance(out_shape, list)
    skipped = len(after)
    body = (lambda *refs: kernel(*refs[skipped:])) if skipped else kernel
    run = pl.pallas_call(
        body,
        out_shape=out_shape,
        in_specs=[pl.BlockSpec(memory_space=pl.ANY)] * skipped + in_specs,
        out_specs=[VMEM] * len(out_shape) if many else VMEM,
        scratch_shapes=scratch,
        compiler_params=pltpu.CompilerParams(vmem_limit_bytes=48 * 2**20),
        cost_estimate=pl.CostEstimate(flops=flops, bytes_accessed=moved, transcendentals=0),
    )
    return functools.partial(run, *after)


def exchange(value):
    return lax.all_to_all(value, "adapter", split_axis=0, concat_axis=0, tiled=True)


def towards(value, k, devices):
    return lax.ppermute(value, "adapter", [(i, i ^ k) for i in range(devices)])


def swapped(value):
    return lax.ppermute(value, "groups", [(0, 1), (1, 0)])


def stand_behind(value, *earlier):
    return pl.pallas_call(
        lambda *refs: None,
        out_shape=jax.ShapeDtypeStruct(value.shape, value.dtype),
        in_specs=[pl.BlockSpec(memory_space=pl.ANY)] * (1 + len(earlier)),
        out_specs=pl.BlockSpec(memory_space=pl.ANY),
        input_output_aliases={0: 0},
    )(value, *earlier)


def note_scratch(devices):
    return [
        pltpu.VMEM((devices * STEP, LANES), jnp.bfloat16),
        pltpu.VMEM((8, devices * STEP), jnp.float32),
        pltpu.SMEM((8,), jnp.int32),
    ]


def back_and_mix(kept, tokens, target, first, arrived, sums, up_weights, *unused_values):
    blocks, rows, width = tokens.shape
    total = blocks * rows
    devices = arrived.shape[0]
    columns, share = up_weights[0].shape
    whole = share - LANES
    shape = (devices, whole // LANES * kept + QUARTER, LANES)
    leaving = call(
        up_kernel,
        jax.ShapeDtypeStruct(shape, jnp.bfloat16),
        [SMEM] + [VMEM] * (3 + len(up_weights)),
        2 * devices * kept * QUAD * columns * share,
        2 * (2 * devices * kept + QUAD * columns) * share,
        scratch=[
            pltpu.VMEM((2, columns, share), jnp.bfloat16),
            pltpu.VMEM((devices * STEP, share), jnp.float32),
            pltpu.VMEM((devices, QUARTER, LANES), jnp.float32),
            *note_scratch(devices),
        ],
    )(first, arrived, *sums, *up_weights)
    mixed = call(
        functools.partial(mix_kernel, whole),
        jax.ShapeDtypeStruct((total, width), jnp.bfloat16),
        [VMEM] * 3,
        2 * devices * kept * total * share,
        2 * (2 * total * width + devices * kept * share),
    )(target.reshape(total, 1), tokens.reshape(total, width), exchange(leaving))
    return mixed.reshape(tokens.shape)


def start_again(tokens, target, first, arrived, sums, up_weights, *arguments):
    return rows_to_holders(tokens, *arguments)


def rows_to_quads(
    tokens, request_block_adapter, request_block_rows, adapter_down_weight, adapter_up_weight
):
    blocks, rows, width = tokens.shape
    devices = lax.axis_size("adapter")
    resident, rank, unused_width = adapter_up_weight.shape
    total = blocks * rows
    columns = resident * rank
    whole = width // LANES // QUAD * LANES
    share = whole + LANES
    bf16, i32 = jnp.bfloat16, jnp.int32

    quad = request_block_adapter // (resident * QUAD)
    label = request_block_adapter - quad * (resident * QUAD) + 1
    order = request_block_adapter * blocks + jnp.arange(blocks, dtype=i32)
    same = quad[:, None] == quad[None, :]
    used = request_block_rows
    ahead = jnp.where(same & (order[None, :] < order[:, None]), used[None, :], 0)
    most = jnp.max(jnp.sum(jnp.where(same, used[None, :], 0), axis=1))
    row = jnp.arange(rows, dtype=i32)
    start = quad * total + jnp.sum(ahead, axis=1)
    target = jnp.where(row[None, :] < used[:, None], start[:, None] + row[None, :], -1)
    target = target.reshape(total).astype(i32)
    label = jnp.broadcast_to(label[:, None], (blocks, rows)).reshape(total, 1).astype(jnp.float32)

    me = lax.axis_index("adapter").astype(i32)
    group = lax.axis_index("groups").astype(i32)
    parts = jnp.bitwise_xor(me % QUAD, jnp.arange(QUAD, dtype=i32))
    halves = jnp.stack([group, 1 - group]) * (resident // 2)
    first = jnp.concatenate([parts * resident, halves]).astype(i32)
    tiles = whole // LANES

    def shares(weight, halved, after):
        shapes = []
        for k in range(QUAD):
            count = columns // 2 if k in halved else columns
            far = (count * tiles + count // QUAD, LANES)
            shapes.append(jax.ShapeDtypeStruct((columns, share) if k < 2 else far, bf16))
        values = call(
            functools.partial(weight_kernel, whole, range(QUAD), halved),
            shapes,
            [SMEM, SMEM, VMEM],
            0,
            QUAD * columns * width,
            after,
        )(parts, group.reshape(1), weight)
        return [values[0]] + [towards(values[k], k, devices) for k in range(1, QUAD)]

    weight = adapter_down_weight.transpose(0, 2, 1).reshape(columns, width)
    down_weights = shares(weight, DOWN_HALVED, [])
    weight = adapter_up_weight.reshape(columns, width)
    up_weights = shares(weight, UP_HALVED, down_weights[:1])
    down_weights[2] = stand_behind(down_weights[2], up_weights[0])
    down_weights += [swapped(down_weights[k]) for k in DOWN_HALVED]
    up_weights += [swapped(up_weights[k]) for k in UP_HALVED]

    caps = [total * 5 // 16, total * 6 // 16, total * 7 // 16]
    cap = caps[-1]
    arrived = exchange(
        call(
            functools.partial(pack_kernel, whole, cap),
            jax.ShapeDtypeStruct((devices, tiles * cap + QUARTER, LANES), bf16),
            [SMEM, VMEM, VMEM, VMEM],
            2 * devices * cap * total * share,
            2 * (total * width + devices * cap * share),
            (),
            [pltpu.VMEM((total, width), bf16)],
        )(most.reshape(1), target.reshape(1, total), label, tokens.reshape(total, width))
    )

    partial, count = call(
        down_kernel,
        [
            jax.ShapeDtypeStruct((cap // STEP, rank, devices * STEP), jnp.float32),
            jax.ShapeDtypeStruct((STEP, LANES), bf16),
        ],
        [SMEM] + [VMEM] * (1 + len(down_weights)),
        0,
        0,
        up_weights[2:3],
        [
            pltpu.VMEM((2, columns, share), bf16),
            pltpu.VMEM((devices * STEP, share), bf16),
            pltpu.VMEM((rank, devices * STEP), jnp.float32),
            *note_scratch(devices),
        ],
    )(first, arrived, *down_weights)
    pair = call(
        pair_kernel, jax.ShapeDtypeStruct(partial.shape, bf16), [VMEM, VMEM], 0, 0
    )(partial, towards(partial, 1, devices))
    sums = [pair, towards(pair, 2, devices)]
    count = count[0:1, 0:1]
    most = jnp.maximum(count, swapped(count))[0, 0].astype(jnp.float32)
    return lax.switch(
        sum((most > more).astype(i32) for more in caps),
        [functools.partial(back_and_mix, more) for more in caps] + [start_again],
        tokens,
        target,
        first,
        arrived,
        sums,
        up_weights,
        request_block_adapter,
        request_block_rows,
        adapter_down_weight,
        adapter_up_weight,
    )


def solution(mesh):
    placed = (
        P(("groups", "adapter"), None, None),
        P(("groups", "adapter")),
        P(("groups", "adapter")),
        P("adapter", None, None),
        P("adapter", None, None),
    )

    def per_device(tokens, request_block_adapter, request_block_rows, down_weight, up_weight):
        blocks, rows, width = tokens.shape
        devices = mesh.shape["adapter"]
        slots = max(1, 4 * blocks // devices)
        quads = devices % QUAD == 0 and slots * QUAD >= blocks
        quads = quads and width % (QUAD * LANES) == LANES and up_weight.shape[1] == HALF
        quads = quads and blocks * rows * 7 // 16 == 7 * STEP and mesh.shape["groups"] == 2
        plan = rows_to_quads if quads else rows_to_holders
        return plan(tokens, request_block_adapter, request_block_rows, down_weight, up_weight)

    return jax.shard_map(
        per_device,
        mesh=mesh,
        in_specs=placed,
        out_specs=P(("groups", "adapter"), None, None),
        check_vma=False,
    )
```

```python
import functools

import jax
import jax.numpy as jnp
from jax import lax
from jax.experimental import pallas as pl
from jax.experimental.pallas import tpu as pltpu
from jax.sharding import PartitionSpec as P

LANES = 128
HALF = 64
QUAD = 4
QUARTER = 32
STEP = 16
NOTE = 96
DOWN_HALVED = (2, 3)
UP_HALVED = (2,)
VMEM = pl.BlockSpec(memory_space=pltpu.VMEM)
SMEM = pl.BlockSpec(memory_space=pltpu.SMEM)


def normalise(tokens):
    values = tokens.astype(jnp.float32)
    mean_sq = jnp.mean(values * values, axis=-1, keepdims=True)
    return (values, (values * lax.rsqrt(mean_sq + 1e-06)).astype(jnp.bfloat16))


def resident_update(hidden_state, block_labels, adapter_down_weight, adapter_up_weight):
    feature_width = hidden_state.shape[-1]
    leading = hidden_state.shape[:-1]
    resident_rows, unused_value, inner_rank = adapter_down_weight.shape
    flattened_tokens = hidden_state.reshape(-1, feature_width)
    down_matrix = jnp.einsum(
        "tq,iqg->tig", flattened_tokens, adapter_down_weight, preferred_element_type=jnp.float32
    )
    down_matrix = down_matrix.astype(jnp.bfloat16).reshape(
        flattened_tokens.shape[0], resident_rows * inner_rank
    )
    column_owner = jnp.arange(resident_rows * inner_rank, dtype=jnp.int32) // inner_rank
    picked = block_labels.reshape(-1, 1) == column_owner[None, :]
    down_matrix = jnp.where(picked, down_matrix, jnp.zeros_like(down_matrix))
    lowrank_update = jnp.dot(
        down_matrix,
        adapter_up_weight.reshape(resident_rows * inner_rank, feature_width),
        preferred_element_type=jnp.float32,
    )
    return lowrank_update.astype(jnp.bfloat16).reshape(leading + (feature_width,))


def rows_to_holders(
    tokens, request_block_adapter, request_block_rows, adapter_down_weight, adapter_up_weight
):
    blocks, rows, feature_width = tokens.shape
    devices = lax.axis_size("adapter")
    resident_rows = adapter_down_weight.shape[0]
    slots = max(1, 4 * blocks // devices)
    values, normed = normalise(tokens)
    owner = request_block_adapter // resident_rows
    within = request_block_adapter - owner * resident_rows
    serial = jnp.arange(blocks, dtype=jnp.int32)
    earlier = (owner[:, None] == owner[None, :]) & (serial[None, :] < serial[:, None])
    position = owner * slots + jnp.sum(earlier, axis=1)
    outgoing = (
        jnp.zeros((devices * slots, rows, feature_width), jnp.bfloat16).at[position].set(normed)
    )
    outgoing = outgoing.reshape(devices, slots, rows, feature_width)
    block_labels = jnp.full((devices * slots,), -1, jnp.int32).at[position].set(within)
    block_labels = jnp.broadcast_to(block_labels[:, None], (devices * slots, rows)).reshape(
        devices, slots, rows
    )
    arriving_rows, row_markers = (
        lax.all_to_all(outgoing, "adapter", split_axis=0, concat_axis=0, tiled=True),
        lax.all_to_all(block_labels, "adapter", split_axis=0, concat_axis=0, tiled=True),
    )
    lowrank_update = resident_update(
        arriving_rows, row_markers, adapter_down_weight, adapter_up_weight
    )
    returned = lax.all_to_all(lowrank_update, "adapter", split_axis=0, concat_axis=0, tiled=True)
    mine = returned.reshape(devices * slots, rows, feature_width)[position]
    live = jnp.arange(rows, dtype=jnp.int32)[None, :] < request_block_rows[:, None]
    mixed = values + jnp.where(live[:, :, None], mine.astype(jnp.float32), jnp.float32(0.0))
    return mixed.astype(jnp.bfloat16)


def lanes_of(rows):
    return lax.broadcasted_iota(jnp.int32, (rows, LANES), 1)


def weight_kernel(whole, which, halved, part_ref, group_ref, weight_ref, *out_refs):
    tiles = whole // LANES
    for k, out_ref in zip(which, out_refs):
        j = part_ref[k]
        if k < 2:
            last = weight_ref[:, QUAD * whole :].astype(jnp.float32)
            turned = pltpu.roll(last, lax.rem(LANES - QUARTER * j, LANES), 1)
            inside = lanes_of(last.shape[0]) < QUARTER
            out_ref[:, 0:whole] = weight_ref[:, pl.ds(pl.multiple_of(j * whole, LANES), whole)]
            out_ref[:, whole:] = jnp.where(inside, turned, 0.0).astype(jnp.bfloat16)
            continue
        count = weight_ref.shape[0] // 2 if k in halved else weight_ref.shape[0]
        start = pl.multiple_of(group_ref[0] * count, count) if k in halved else 0
        for t in range(tiles):
            column = pl.multiple_of(j * whole + t * LANES, LANES)
            out_ref[t * count : (t + 1) * count, :] = weight_ref[
                pl.ds(start, count), pl.ds(column, LANES)
            ]
        last = weight_ref[pl.ds(start, count), QUAD * whole :].astype(jnp.float32)
        size = count // QUAD
        owner = lanes_of(size) // QUARTER
        merged = jnp.zeros((size, LANES), jnp.float32)
        for m in range(QUAD):
            shift = lax.rem(LANES + QUARTER * (m - j), LANES)
            turned = pltpu.roll(last[m * size : (m + 1) * size], shift, 1)
            merged = jnp.where(owner == m, turned, merged)
        out_ref[tiles * count :, :] = merged.astype(jnp.bfloat16)


def open_far(far_refs, halved, opened_ref):
    width = opened_ref.shape[2]
    tiles = width // LANES - 1
    places = [(k - 2, 0) for k in (2, 3)] + [(k - 2, 1) for k in halved]
    for ref, (holder, part) in zip(far_refs, places):
        count = opened_ref.shape[1] // 2 if holder + 2 in halved else opened_ref.shape[1]
        base, size = part * count, count // QUAD
        inside = lanes_of(size) < QUARTER
        for t in range(tiles):
            opened_ref[holder, base : base + count, t * LANES : (t + 1) * LANES] = ref[
                t * count : (t + 1) * count, :
            ]
        packed = ref[tiles * count :, :].astype(jnp.float32)
        for m in range(QUAD):
            turned = pltpu.roll(packed, (LANES - QUARTER * m) % LANES, 1) if m else packed
            opened_ref[holder, base + m * size : base + (m + 1) * size, tiles * LANES :] = (
                jnp.where(inside, turned, 0.0).astype(jnp.bfloat16)
            )


def pack_kernel(whole, cap, base, most_ref, target_ref, label_ref, tokens_ref, out_ref, normed_ref):
    values = tokens_ref[...].astype(jnp.float32)
    mean_sq = jnp.mean(values * values, axis=-1, keepdims=True)
    normed_ref[...] = (values * lax.rsqrt(mean_sq + 1e-06)).astype(jnp.bfloat16)
    total = tokens_ref.shape[0]
    quads, tiles = out_ref.shape[0] // QUAD, whole // LANES
    lane = lanes_of(total)
    last = normed_ref[:, QUAD * whole :].astype(jnp.float32)
    label = jnp.where(lane == QUARTER, label_ref[...], 0.0)
    ends = []
    for j in range(QUAD):
        turned = pltpu.roll(last, (LANES - QUARTER * j) % LANES, 1) if j else last
        ends.append(jnp.where(lane < QUARTER, turned, label).astype(jnp.bfloat16))
    most = most_ref[0].astype(jnp.float32)
    group_lane = lanes_of(QUARTER) // QUARTER
    step_lane = lanes_of(STEP)
    for q in range(quads):
        place = lax.broadcasted_iota(jnp.int32, (cap, total), 0) + (q * total + base)
        chosen = jnp.where(target_ref[...] == place, 1.0, 0.0).astype(jnp.bfloat16)
        for j in range(QUAD):
            share = jnp.dot(
                chosen,
                normed_ref[:, j * whole : (j + 1) * whole],
                preferred_element_type=jnp.float32,
            ).astype(jnp.bfloat16)
            for t in range(tiles):
                out_ref[q * QUAD + j, t * cap : (t + 1) * cap, :] = share[
                    :, t * LANES : (t + 1) * LANES
                ]
            end = jnp.dot(chosen, ends[j], preferred_element_type=jnp.float32)
            if j == 0:
                notes = jnp.where(step_lane == NOTE + cap // STEP, most, 0.0)
                for a in range(cap // STEP):
                    turned = pltpu.roll(end[a * STEP : (a + 1) * STEP], NOTE + a - QUARTER, 1)
                    notes = jnp.where(step_lane == NOTE + a, turned, notes)
            padded = jnp.concatenate(
                [end, jnp.zeros((QUAD * QUARTER - cap, LANES), jnp.float32)], axis=0
            )
            merged = padded[0:QUARTER]
            for m in range(1, QUAD):
                turned = pltpu.roll(padded[m * QUARTER : (m + 1) * QUARTER], m * QUARTER, 1)
                merged = jnp.where(group_lane == m, turned, merged)
            out_ref[q * QUAD + j, tiles * cap : tiles * cap + STEP, :] = merged[0:STEP].astype(
                jnp.bfloat16
            )
            out_ref[q * QUAD + j, tiles * cap + STEP :, :] = jnp.where(
                step_lane >= NOTE, notes, merged[STEP:]
            ).astype(jnp.bfloat16)


def read_notes(rows_ref, cap, tiles, part_ref, resident, notes_ref, labels_ref, met_ref):
    senders = rows_ref.shape[0]
    for s in range(senders):
        notes_ref[s * STEP : (s + 1) * STEP, :] = rows_ref[s, tiles * cap + STEP :, :]
    steps = labels_ref.shape[0]
    row = lax.broadcasted_iota(jnp.int32, (steps, LANES), 0)
    wanted = jnp.where(lanes_of(steps) == NOTE + row, 1.0, 0.0).astype(jnp.bfloat16)
    labels = lax.dot_general(
        wanted, notes_ref[...], (((1,), (1,)), ((), ())), preferred_element_type=jnp.float32
    )
    labels_ref[...] = labels
    code = jnp.zeros((steps, 1), jnp.float32)
    for h in range(QUAD):
        first = part_ref[h].astype(jnp.float32) + 1.0
        met = jnp.where((labels >= first) & (labels < first + resident), 1.0, 0.0)
        code = code + (1 << h) * jnp.max(met, axis=1, keepdims=True)
    at = lax.broadcasted_iota(jnp.int32, (steps, 1), 0)
    for a in range(cap // STEP):
        met_ref[a] = jnp.max(jnp.where(at == a, code, 0.0)).astype(jnp.int32)


def for_holders(met_ref, first_ref, near_refs, opened_ref, halved, a, step):
    pairs = opened_ref.shape[1] // LANES
    for h in range(QUAD):
        base = first_ref[h].astype(jnp.float32) + 1.0
        firsts = [base + 2.0 * t for t in range(pairs)]
        if h in halved:
            firsts = [
                base + first_ref[QUAD + i].astype(jnp.float32) + 2.0 * t
                for i in range(2)
                for t in range(pairs // 2)
            ]

        @pl.when(lax.rem(met_ref[a] // (1 << h), 2) > 0)
        def _(h=h, firsts=firsts):
            step(near_refs[h] if h < 2 else opened_ref.at[h - 2], firsts)


def down_kernel(first_ref, rows_ref, *refs):
    near_refs, far_refs, out_ref, count_ref = refs[:2], refs[2:6], refs[6], refs[7]
    opened_ref, batch_ref, picked_ref, notes_ref, labels_ref, met_ref = refs[8:]
    senders, width = rows_ref.shape[0], batch_ref.shape[1]
    tiles = width // LANES - 1
    cap = out_ref.shape[0] * STEP
    rank = out_ref.shape[1]
    resident = opened_ref.shape[1] // rank
    dims = (((1,), (1,)), ((), ()))
    read_notes(rows_ref, cap, tiles, first_ref, resident, notes_ref, labels_ref, met_ref)
    notes = notes_ref[...].astype(jnp.float32)
    is_count = lanes_of(senders * STEP) == NOTE + cap // STEP
    count = jnp.max(jnp.where(is_count, notes, 0.0), axis=(0, 1), keepdims=True)
    count_ref[...] = jnp.broadcast_to(count, count_ref.shape).astype(jnp.bfloat16)
    open_far(far_refs, DOWN_HALVED, opened_ref)

    def one(a, carry):
        picked_ref[...] = jnp.zeros(picked_ref.shape, jnp.float32)

        @pl.when(met_ref[a] > 0)
        def _():
            shift = lax.rem(LANES - QUARTER * (a // 2), LANES)
            spot = pl.multiple_of(tiles * cap + lax.rem(a, 2) * STEP, STEP)
            for s in range(senders):
                rows = slice(s * STEP, (s + 1) * STEP)
                for t in range(tiles):
                    at = pl.multiple_of(t * cap + a * STEP, STEP)
                    batch_ref[rows, t * LANES : (t + 1) * LANES] = rows_ref[s, pl.ds(at, STEP), :]
                end = rows_ref[s, pl.ds(spot, STEP), :].astype(jnp.float32)
                batch_ref[rows, tiles * LANES :] = pltpu.roll(end, shift, 1).astype(jnp.bfloat16)
            label = labels_ref[pl.ds(a, 1), :]

            def step(weight_ref, firsts):
                product = lax.dot_general(
                    weight_ref[...], batch_ref[...], dims, preferred_element_type=jnp.float32
                )
                picked = picked_ref[...]
                for t, first in enumerate(firsts):
                    for i in range(2):
                        at = (2 * t + i) * rank
                        picked = jnp.where(
                            label == first + i, product[at : at + rank, :], picked
                        )
                picked_ref[...] = picked

            for_holders(met_ref, first_ref, near_refs, opened_ref, DOWN_HALVED, a, step)

        out_ref[a] = picked_ref[...]
        return carry

    lax.fori_loop(0, cap // STEP, one, 0)


def pair_kernel(own_ref, other_ref, out_ref):
    out_ref[...] = (own_ref[...] + other_ref[...]).astype(jnp.bfloat16)


def up_kernel(first_ref, rows_ref, *refs):
    sum_refs, near_refs, far_refs, out_ref = refs[:2], refs[2:4], refs[4:7], refs[7]
    opened_ref, delta_ref, ends_ref, notes_ref, labels_ref, met_ref = refs[8:]
    senders, width = rows_ref.shape[0], opened_ref.shape[2]
    tiles = width // LANES - 1
    cap, rank = sum_refs[0].shape[0] * STEP, sum_refs[0].shape[1]
    resident = opened_ref.shape[1] // rank
    kept = (out_ref.shape[1] - QUARTER) // tiles
    group_lane = lanes_of(STEP) // QUARTER
    read_notes(rows_ref, cap, tiles, first_ref, resident, notes_ref, labels_ref, met_ref)
    open_far(far_refs, UP_HALVED, opened_ref)
    ends_ref[...] = jnp.zeros(ends_ref.shape, jnp.float32)
    low = jnp.where(lanes_of(senders * STEP) < HALF, 0.0, 1.0)
    rank_row = lax.broadcasted_iota(jnp.int32, (rank, LANES), 0)
    twofold = jnp.where(lax.rem(lanes_of(rank), rank) == rank_row, 1.0, 0.0).astype(jnp.bfloat16)

    def one(a, carry):
        delta_ref[...] = jnp.zeros(delta_ref.shape, jnp.float32)

        @pl.when(met_ref[a] > 0)
        def _():
            note_row = lax.broadcasted_iota(jnp.int32, (LANES, LANES), 0)
            wanted = jnp.where(note_row == NOTE + a, 1.0, 0.0).astype(jnp.bfloat16)
            label = jnp.dot(notes_ref[...], wanted, preferred_element_type=jnp.float32) - low
            down = sum_refs[0][a].astype(jnp.float32)
            for ref in sum_refs[1:]:
                down = down + ref[a].astype(jnp.float32)
            twice = lax.dot_general(
                down.astype(jnp.bfloat16),
                twofold,
                (((0,), (0,)), ((), ())),
                preferred_element_type=jnp.float32,
            )

            def step(weight_ref, firsts):
                placed = [jnp.where(label == first, twice, 0.0) for first in firsts]
                placed = jnp.concatenate(placed, axis=1).astype(jnp.bfloat16)
                delta_ref[...] += jnp.dot(
                    placed, weight_ref[...], preferred_element_type=jnp.float32
                )

            for_holders(met_ref, first_ref, near_refs, opened_ref, UP_HALVED, a, step)

        spot = pl.multiple_of(lax.rem(a, 2) * STEP, STEP)
        for s in range(senders):
            rows = slice(s * STEP, (s + 1) * STEP)
            for t in range(tiles):
                at = pl.multiple_of(t * kept + a * STEP, STEP)
                out_ref[s, pl.ds(at, STEP), :] = delta_ref[
                    rows, t * LANES : (t + 1) * LANES
                ].astype(jnp.bfloat16)
            turned = pltpu.roll(delta_ref[rows, tiles * LANES :], QUARTER * (a // 2), 1)
            ends_ref[s, pl.ds(spot, STEP), :] = jnp.where(
                group_lane == a // 2, turned, ends_ref[s, pl.ds(spot, STEP), :]
            )
        return carry

    lax.fori_loop(0, kept // STEP, one, 0)
    for s in range(senders):
        out_ref[s, tiles * kept :, :] = ends_ref[s].astype(jnp.bfloat16)


def mix_kernel(whole, bases, target_ref, tokens_ref, *refs):
    returned_refs, out_ref = refs[:-1], refs[-1]
    total = tokens_ref.shape[0]
    tiles, quads = whole // LANES, returned_refs[0].shape[0] // QUAD
    lane = lanes_of(total)
    chosen = []
    for base, ref in zip(bases, returned_refs):
        kept = (ref.shape[1] - QUARTER) // tiles
        spot = lax.broadcasted_iota(jnp.int32, (total, quads * kept), 1)
        place = spot // kept * total + spot % kept + base
        chosen.append(jnp.where(target_ref[...] == place, 1.0, 0.0).astype(jnp.bfloat16))
    end = jnp.zeros((total, LANES), jnp.float32)
    for j in range(QUAD):
        delta = 0.0
        for choice, ref in zip(chosen, returned_refs):
            kept = choice.shape[1] // quads
            shares = []
            for q in range(quads):
                d = q * QUAD + j
                parts = [ref[d, t * kept : (t + 1) * kept, :] for t in range(tiles)]
                packed = ref[d, tiles * kept :, :].astype(jnp.float32)
                groups = [packed]
                for m in range(1, QUAD):
                    groups.append(pltpu.roll(packed, LANES - QUARTER * m, 1))
                parts.append(jnp.concatenate(groups, axis=0)[0:kept].astype(jnp.bfloat16))
                shares.append(jnp.concatenate(parts, axis=1))
            share = jnp.concatenate(shares, axis=0)
            delta = delta + jnp.dot(choice, share, preferred_element_type=jnp.float32)
        columns = slice(j * whole, (j + 1) * whole)
        out_ref[:, columns] = (
            tokens_ref[:, columns].astype(jnp.float32) + delta[:, 0:whole]
        ).astype(jnp.bfloat16)
        last = delta[:, whole:]
        turned = pltpu.roll(last, QUARTER * j, 1) if j else last
        end = jnp.where((lane >= QUARTER * j) & (lane < QUARTER * (j + 1)), turned, end)
    out_ref[:, QUAD * whole :] = (
        tokens_ref[:, QUAD * whole :].astype(jnp.float32) + end
    ).astype(jnp.bfloat16)


def call(kernel, out_shape, in_specs, flops, moved, after=(), scratch=()):
    many = isinstance(out_shape, list)
    skipped = len(after)
    body = (lambda *refs: kernel(*refs[skipped:])) if skipped else kernel
    run = pl.pallas_call(
        body,
        out_shape=out_shape,
        in_specs=[pl.BlockSpec(memory_space=pl.ANY)] * skipped + in_specs,
        out_specs=[VMEM] * len(out_shape) if many else VMEM,
        scratch_shapes=scratch,
        compiler_params=pltpu.CompilerParams(vmem_limit_bytes=48 * 2**20),
        cost_estimate=pl.CostEstimate(flops=flops, bytes_accessed=moved, transcendentals=0),
    )
    return functools.partial(run, *after)


def exchange(value):
    return lax.all_to_all(value, "adapter", split_axis=0, concat_axis=0, tiled=True)


def towards(value, k, devices):
    return lax.ppermute(value, "adapter", [(i, i ^ k) for i in range(devices)])


def swapped(value):
    return lax.ppermute(value, "groups", [(0, 1), (1, 0)])


def stand_behind(value, *earlier):
    return pl.pallas_call(
        lambda *refs: None,
        out_shape=jax.ShapeDtypeStruct(value.shape, value.dtype),
        in_specs=[pl.BlockSpec(memory_space=pl.ANY)] * (1 + len(earlier)),
        out_specs=pl.BlockSpec(memory_space=pl.ANY),
        input_output_aliases={0: 0},
    )(value, *earlier)


def note_scratch(devices):
    return [
        pltpu.VMEM((devices * STEP, LANES), jnp.bfloat16),
        pltpu.VMEM((8, devices * STEP), jnp.float32),
        pltpu.SMEM((8,), jnp.int32),
    ]


def pack_call(cap, base, whole, devices, most, target, label, tokens):
    blocks, rows, width = tokens.shape
    total = blocks * rows
    return call(
        functools.partial(pack_kernel, whole, cap, base),
        jax.ShapeDtypeStruct((devices, whole // LANES * cap + QUARTER, LANES), jnp.bfloat16),
        [SMEM, VMEM, VMEM, VMEM],
        2 * devices * cap * total * whole,
        2 * (total * width + devices * cap * whole),
        scratch=[pltpu.VMEM((total, width), jnp.bfloat16)],
    )(most, target.reshape(1, total), label, tokens.reshape(total, width))


def down_call(cap, first, arrived, down_weights, after):
    devices = arrived.shape[0]
    columns, share = down_weights[0].shape
    return call(
        down_kernel,
        [
            jax.ShapeDtypeStruct((cap // STEP, HALF, devices * STEP), jnp.float32),
            jax.ShapeDtypeStruct((STEP, LANES), jnp.bfloat16),
        ],
        [SMEM] + [VMEM] * (1 + len(down_weights)),
        0,
        0,
        after,
        [
            pltpu.VMEM((2, columns, share), jnp.bfloat16),
            pltpu.VMEM((devices * STEP, share), jnp.bfloat16),
            pltpu.VMEM((HALF, devices * STEP), jnp.float32),
            *note_scratch(devices),
        ],
    )(first, arrived, *down_weights)


def quad_sums(partial, devices):
    pair = call(
        pair_kernel, jax.ShapeDtypeStruct(partial.shape, jnp.bfloat16), [VMEM, VMEM], 0, 0
    )(partial, towards(partial, 1, devices))
    return [pair, towards(pair, 2, devices)]


def up_call(kept, first, arrived, sums, up_weights):
    devices = arrived.shape[0]
    columns, share = up_weights[0].shape
    shape = (devices, (share // LANES - 1) * kept + QUARTER, LANES)
    return call(
        up_kernel,
        jax.ShapeDtypeStruct(shape, jnp.bfloat16),
        [SMEM] + [VMEM] * (3 + len(up_weights)),
        2 * devices * kept * QUAD * columns * share,
        2 * (2 * devices * kept + QUAD * columns) * share,
        scratch=[
            pltpu.VMEM((2, columns, share), jnp.bfloat16),
            pltpu.VMEM((devices * STEP, share), jnp.float32),
            pltpu.VMEM((devices, QUARTER, LANES), jnp.float32),
            *note_scratch(devices),
        ],
    )(first, arrived, *sums, *up_weights)


def back_and_mix(
    kept, more, tokens, target, label, first, arrived, sums, down_weights, up_weights, *unused
):
    blocks, rows, width = tokens.shape
    total = blocks * rows
    devices = arrived.shape[0]
    whole = up_weights[0].shape[1] - LANES
    pieces = [exchange(up_call(kept, first, arrived, sums, up_weights))]
    if more:
        no_count = jnp.zeros((1,), jnp.int32)
        outgoing = pack_call(more, kept, whole, devices, no_count, target, label, tokens)
        arrived = exchange(outgoing)
        partial = down_call(more, first, arrived, down_weights, [])[0]
        sums = quad_sums(partial, devices)
        pieces.append(exchange(up_call(more, first, arrived, sums, up_weights)))
    mixed = call(
        functools.partial(mix_kernel, whole, (0, kept)[: len(pieces)]),
        jax.ShapeDtypeStruct((total, width), jnp.bfloat16),
        [VMEM] * (2 + len(pieces)),
        2 * devices * (kept + more) * total * whole,
        2 * (2 * total * width + devices * (kept + more) * whole),
    )(target.reshape(total, 1), tokens.reshape(total, width), *pieces)
    return mixed.reshape(tokens.shape)


def start_again(
    tokens, target, label, first, arrived, sums, down_weights, up_weights, *arguments
):
    return rows_to_holders(tokens, *arguments)


def rows_to_quads(
    tokens, request_block_adapter, request_block_rows, adapter_down_weight, adapter_up_weight
):
    blocks, rows, width = tokens.shape
    devices = lax.axis_size("adapter")
    resident, rank, unused_width = adapter_up_weight.shape
    total = blocks * rows
    columns = resident * rank
    whole = width // LANES // QUAD * LANES
    share = whole + LANES
    bf16, i32 = jnp.bfloat16, jnp.int32

    quad = request_block_adapter // (resident * QUAD)
    label = request_block_adapter - quad * (resident * QUAD) + 1
    order = request_block_adapter * blocks + jnp.arange(blocks, dtype=i32)
    same = quad[:, None] == quad[None, :]
    used = request_block_rows
    ahead = jnp.where(same & (order[None, :] < order[:, None]), used[None, :], 0)
    most = jnp.max(jnp.sum(jnp.where(same, used[None, :], 0), axis=1))
    row = jnp.arange(rows, dtype=i32)
    start = quad * total + jnp.sum(ahead, axis=1)
    target = jnp.where(row[None, :] < used[:, None], start[:, None] + row[None, :], -1)
    target = target.reshape(total).astype(i32)
    label = jnp.broadcast_to(label[:, None], (blocks, rows)).reshape(total, 1).astype(jnp.float32)

    me = lax.axis_index("adapter").astype(i32)
    group = lax.axis_index("groups").astype(i32)
    parts = jnp.bitwise_xor(me % QUAD, jnp.arange(QUAD, dtype=i32))
    halves = jnp.stack([group, 1 - group]) * (resident // 2)
    first = jnp.concatenate([parts * resident, halves]).astype(i32)
    tiles = whole // LANES

    def shares(weight, halved, after):
        shapes = []
        for k in range(QUAD):
            count = columns // 2 if k in halved else columns
            far = (count * tiles + count // QUAD, LANES)
            shapes.append(jax.ShapeDtypeStruct((columns, share) if k < 2 else far, bf16))
        values = call(
            functools.partial(weight_kernel, whole, range(QUAD), halved),
            shapes,
            [SMEM, SMEM, VMEM],
            0,
            QUAD * columns * width,
            after,
        )(parts, group.reshape(1), weight)
        return [values[0]] + [towards(values[k], k, devices) for k in range(1, QUAD)]

    weight = adapter_down_weight.transpose(0, 2, 1).reshape(columns, width)
    down_weights = shares(weight, DOWN_HALVED, [])
    weight = adapter_up_weight.reshape(columns, width)
    up_weights = shares(weight, UP_HALVED, down_weights[:1])
    down_weights[2] = stand_behind(down_weights[2], up_weights[0])
    down_weights += [swapped(down_weights[k]) for k in DOWN_HALVED]
    up_weights += [swapped(up_weights[k]) for k in UP_HALVED]

    caps = [total * 5 // 16, total * 6 // 16, total * 7 // 16]
    cap = caps[-1]
    arrived = exchange(
        pack_call(cap, 0, whole, devices, most.reshape(1), target, label, tokens)
    )
    partial, count = down_call(cap, first, arrived, down_weights, up_weights[2:3])
    sums = quad_sums(partial, devices)
    count = count[0:1, 0:1]
    most = jnp.maximum(count, swapped(count))[0, 0].astype(jnp.float32)
    branches = [functools.partial(back_and_mix, kept, 0) for kept in caps]
    branches += [functools.partial(back_and_mix, cap, STEP), start_again]
    return lax.switch(
        sum((most > limit).astype(i32) for limit in [*caps, cap + STEP]),
        branches,
        tokens,
        target,
        label,
        first,
        arrived,
        sums,
        down_weights,
        up_weights,
        request_block_adapter,
        request_block_rows,
        adapter_down_weight,
        adapter_up_weight,
    )


def solution(mesh):
    placed = (
        P(("groups", "adapter"), None, None),
        P(("groups", "adapter")),
        P(("groups", "adapter")),
        P("adapter", None, None),
        P("adapter", None, None),
    )

    def per_device(tokens, request_block_adapter, request_block_rows, down_weight, up_weight):
        blocks, rows, width = tokens.shape
        devices = mesh.shape["adapter"]
        slots = max(1, 4 * blocks // devices)
        quads = devices % QUAD == 0 and slots * QUAD >= blocks
        quads = quads and width % (QUAD * LANES) == LANES and up_weight.shape[1] == HALF
        quads = quads and blocks * rows * 7 // 16 == 7 * STEP and mesh.shape["groups"] == 2
        plan = rows_to_quads if quads else rows_to_holders
        return plan(tokens, request_block_adapter, request_block_rows, down_weight, up_weight)

    return jax.shard_map(
        per_device,
        mesh=mesh,
        in_specs=placed,
        out_specs=P(("groups", "adapter"), None, None),
        check_vma=False,
    )
```

```python
import functools

import jax
import jax.numpy as jnp
from jax import lax
from jax.experimental import pallas as pl
from jax.experimental.pallas import tpu as pltpu
from jax.sharding import PartitionSpec as P

LANES = 128
HALF = 64
QUAD = 4
QUARTER = 32
STEP = 16
NOTE = 96
DOWN_HALVED = (2, 3)
UP_HALVED = (2,)
VMEM = pl.BlockSpec(memory_space=pltpu.VMEM)
SMEM = pl.BlockSpec(memory_space=pltpu.SMEM)


def normalise(tokens):
    values = tokens.astype(jnp.float32)
    mean_sq = jnp.mean(values * values, axis=-1, keepdims=True)
    return (values, (values * lax.rsqrt(mean_sq + 1e-06)).astype(jnp.bfloat16))


def resident_update(hidden_state, block_labels, adapter_down_weight, adapter_up_weight):
    feature_width = hidden_state.shape[-1]
    leading = hidden_state.shape[:-1]
    resident_rows, unused_value, inner_rank = adapter_down_weight.shape
    flattened_tokens = hidden_state.reshape(-1, feature_width)
    down_matrix = jnp.einsum(
        "tq,iqg->tig", flattened_tokens, adapter_down_weight, preferred_element_type=jnp.float32
    )
    down_matrix = down_matrix.astype(jnp.bfloat16).reshape(
        flattened_tokens.shape[0], resident_rows * inner_rank
    )
    column_owner = jnp.arange(resident_rows * inner_rank, dtype=jnp.int32) // inner_rank
    picked = block_labels.reshape(-1, 1) == column_owner[None, :]
    down_matrix = jnp.where(picked, down_matrix, jnp.zeros_like(down_matrix))
    lowrank_update = jnp.dot(
        down_matrix,
        adapter_up_weight.reshape(resident_rows * inner_rank, feature_width),
        preferred_element_type=jnp.float32,
    )
    return lowrank_update.astype(jnp.bfloat16).reshape(leading + (feature_width,))


def rows_to_holders(
    tokens, request_block_adapter, request_block_rows, adapter_down_weight, adapter_up_weight
):
    blocks, rows, feature_width = tokens.shape
    devices = lax.axis_size("adapter")
    resident_rows = adapter_down_weight.shape[0]
    slots = max(1, 4 * blocks // devices)
    values, normed = normalise(tokens)
    owner = request_block_adapter // resident_rows
    within = request_block_adapter - owner * resident_rows
    serial = jnp.arange(blocks, dtype=jnp.int32)
    earlier = (owner[:, None] == owner[None, :]) & (serial[None, :] < serial[:, None])
    position = owner * slots + jnp.sum(earlier, axis=1)
    outgoing = (
        jnp.zeros((devices * slots, rows, feature_width), jnp.bfloat16).at[position].set(normed)
    )
    outgoing = outgoing.reshape(devices, slots, rows, feature_width)
    block_labels = jnp.full((devices * slots,), -1, jnp.int32).at[position].set(within)
    block_labels = jnp.broadcast_to(block_labels[:, None], (devices * slots, rows)).reshape(
        devices, slots, rows
    )
    arriving_rows, row_markers = (
        lax.all_to_all(outgoing, "adapter", split_axis=0, concat_axis=0, tiled=True),
        lax.all_to_all(block_labels, "adapter", split_axis=0, concat_axis=0, tiled=True),
    )
    lowrank_update = resident_update(
        arriving_rows, row_markers, adapter_down_weight, adapter_up_weight
    )
    returned = lax.all_to_all(lowrank_update, "adapter", split_axis=0, concat_axis=0, tiled=True)
    mine = returned.reshape(devices * slots, rows, feature_width)[position]
    live = jnp.arange(rows, dtype=jnp.int32)[None, :] < request_block_rows[:, None]
    mixed = values + jnp.where(live[:, :, None], mine.astype(jnp.float32), jnp.float32(0.0))
    return mixed.astype(jnp.bfloat16)


def lanes_of(rows):
    return lax.broadcasted_iota(jnp.int32, (rows, LANES), 1)


def weight_kernel(whole, which, halved, part_ref, group_ref, weight_ref, *out_refs):
    tiles = whole // LANES
    for k, out_ref in zip(which, out_refs):
        j = part_ref[k]
        if k < 2:
            last = weight_ref[:, QUAD * whole :].astype(jnp.float32)
            turned = pltpu.roll(last, lax.rem(LANES - QUARTER * j, LANES), 1)
            inside = lanes_of(last.shape[0]) < QUARTER
            out_ref[:, 0:whole] = weight_ref[:, pl.ds(pl.multiple_of(j * whole, LANES), whole)]
            out_ref[:, whole:] = jnp.where(inside, turned, 0.0).astype(jnp.bfloat16)
            continue
        count = weight_ref.shape[0] // 2 if k in halved else weight_ref.shape[0]
        start = pl.multiple_of(group_ref[0] * count, count) if k in halved else 0
        for t in range(tiles):
            column = pl.multiple_of(j * whole + t * LANES, LANES)
            out_ref[t * count : (t + 1) * count, :] = weight_ref[
                pl.ds(start, count), pl.ds(column, LANES)
            ]
        last = weight_ref[pl.ds(start, count), QUAD * whole :].astype(jnp.float32)
        size = count // QUAD
        owner = lanes_of(size) // QUARTER
        merged = jnp.zeros((size, LANES), jnp.float32)
        for m in range(QUAD):
            shift = lax.rem(LANES + QUARTER * (m - j), LANES)
            turned = pltpu.roll(last[m * size : (m + 1) * size], shift, 1)
            merged = jnp.where(owner == m, turned, merged)
        out_ref[tiles * count :, :] = merged.astype(jnp.bfloat16)


def open_far(far_refs, halved, opened_ref):
    width = opened_ref.shape[2]
    tiles = width // LANES - 1
    places = [(k - 2, 0) for k in (2, 3)] + [(k - 2, 1) for k in halved]
    for ref, (holder, part) in zip(far_refs, places):
        count = opened_ref.shape[1] // 2 if holder + 2 in halved else opened_ref.shape[1]
        base, size = part * count, count // QUAD
        inside = lanes_of(size) < QUARTER
        for t in range(tiles):
            opened_ref[holder, base : base + count, t * LANES : (t + 1) * LANES] = ref[
                t * count : (t + 1) * count, :
            ]
        packed = ref[tiles * count :, :].astype(jnp.float32)
        for m in range(QUAD):
            turned = pltpu.roll(packed, (LANES - QUARTER * m) % LANES, 1) if m else packed
            opened_ref[holder, base + m * size : base + (m + 1) * size, tiles * LANES :] = (
                jnp.where(inside, turned, 0.0).astype(jnp.bfloat16)
            )


def lay_out(resident, adapter_ref, used_ref, most_ref, target_ref, label_ref):
    blocks, total = adapter_ref.shape[1], target_ref.shape[1]
    rows = total // blocks
    adapter, used = adapter_ref[...], used_ref[...]
    down = lax.broadcasted_iota(jnp.int32, (blocks, blocks), 0)
    across = lax.broadcasted_iota(jnp.int32, (blocks, blocks), 1)

    def turned(value):
        return jnp.sum(jnp.where(down == across, value, 0), axis=1, keepdims=True)

    span = resident * QUAD
    quad = jnp.floor((adapter.astype(jnp.float32) + 0.5) * (1.0 / span)).astype(jnp.int32)
    order = adapter * blocks + lax.broadcasted_iota(jnp.int32, (1, blocks), 1)
    quad_down, order_down, used_down = turned(quad), turned(order), turned(used)
    same = quad_down == quad
    ahead = jnp.sum(jnp.where(same & (order < order_down), used, 0), axis=1, keepdims=True)
    within = jnp.sum(jnp.where(same, used, 0), axis=1, keepdims=True)
    most_ref[...] = jnp.broadcast_to(jnp.max(within, axis=0, keepdims=True), most_ref.shape)
    start = quad_down * total + ahead

    block = lax.broadcasted_iota(jnp.int32, (blocks, total), 0)
    row = lax.broadcasted_iota(jnp.int32, (blocks, total), 1) - block * rows
    place = jnp.where((row >= 0) & (row < used_down), start + row + 1, 0)
    target_ref[...] = jnp.sum(place, axis=0, keepdims=True) - 1
    block = lax.broadcasted_iota(jnp.int32, (total, blocks), 1)
    row = lax.broadcasted_iota(jnp.int32, (total, blocks), 0) - block * rows
    label = jnp.where((row >= 0) & (row < rows), adapter - quad * span + 1, 0)
    label_ref[...] = jnp.sum(label.astype(jnp.float32), axis=1, keepdims=True)


def first_pack_kernel(
    whole, cap, resident, adapter_ref, used_ref, tokens_ref, out_ref, target_ref, label_ref, *refs
):
    normed_ref, most_ref = refs
    lay_out(resident, adapter_ref, used_ref, most_ref, target_ref, label_ref)
    pack_kernel(
        whole, cap, 0, most_ref, target_ref, label_ref, tokens_ref, out_ref, normed_ref
    )


def pack_kernel(
    whole, cap, base, most_ref, target_ref, label_ref, tokens_ref, out_ref, normed_ref
):
    values = tokens_ref[...].astype(jnp.float32)
    mean_sq = jnp.mean(values * values, axis=-1, keepdims=True)
    normed_ref[...] = (values * lax.rsqrt(mean_sq + 1e-06)).astype(jnp.bfloat16)
    total = tokens_ref.shape[0]
    quads, tiles = out_ref.shape[0] // QUAD, whole // LANES
    lane = lanes_of(total)
    last = normed_ref[:, QUAD * whole :].astype(jnp.float32)
    label = jnp.where(lane == QUARTER, label_ref[...], 0.0)
    ends = []
    for j in range(QUAD):
        turned = pltpu.roll(last, (LANES - QUARTER * j) % LANES, 1) if j else last
        ends.append(jnp.where(lane < QUARTER, turned, label).astype(jnp.bfloat16))
    most = most_ref[0:1, 0:1].astype(jnp.float32)
    group_lane = lanes_of(QUARTER) // QUARTER
    step_lane = lanes_of(STEP)
    chosen = []
    for q in range(quads):
        place = lax.broadcasted_iota(jnp.int32, (cap, total), 0) + (q * total + base)
        chosen.append(jnp.where(target_ref[...] == place, 1.0, 0.0).astype(jnp.bfloat16))
    chosen = jnp.concatenate(chosen, axis=0)
    notes = [jnp.where(step_lane == NOTE + cap // STEP, most, 0.0)] * quads
    for j in range(QUAD):
        for t in range(tiles):
            column = j * whole + t * LANES
            if t % 2 == 0:
                count = min(2, tiles - t) * LANES
                share = jnp.dot(
                    chosen,
                    normed_ref[:, column : column + count],
                    preferred_element_type=jnp.float32,
                ).astype(jnp.bfloat16)
            for q in range(quads):
                out_ref[q * QUAD + j, t * cap : (t + 1) * cap, :] = share[
                    q * cap : (q + 1) * cap, t % 2 * LANES : (t % 2 + 1) * LANES
                ]
        end_rows = jnp.dot(chosen, ends[j], preferred_element_type=jnp.float32)
        for q in range(quads):
            end = end_rows[q * cap : (q + 1) * cap]
            if j == 0:
                for a in range(cap // STEP):
                    turned = pltpu.roll(end[a * STEP : (a + 1) * STEP], NOTE + a - QUARTER, 1)
                    notes[q] = jnp.where(step_lane == NOTE + a, turned, notes[q])
            padded = jnp.concatenate(
                [end, jnp.zeros((QUAD * QUARTER - cap, LANES), jnp.float32)], axis=0
            )
            merged = padded[0:QUARTER]
            for m in range(1, QUAD):
                turned = pltpu.roll(padded[m * QUARTER : (m + 1) * QUARTER], m * QUARTER, 1)
                merged = jnp.where(group_lane == m, turned, merged)
            out_ref[q * QUAD + j, tiles * cap : tiles * cap + STEP, :] = merged[0:STEP].astype(
                jnp.bfloat16
            )
            out_ref[q * QUAD + j, tiles * cap + STEP :, :] = jnp.where(
                step_lane >= NOTE, notes[q], merged[STEP:]
            ).astype(jnp.bfloat16)


def read_notes(rows_ref, cap, tiles, part_ref, resident, notes_ref, labels_ref, met_ref):
    senders = rows_ref.shape[0]
    for s in range(senders):
        notes_ref[s * STEP : (s + 1) * STEP, :] = rows_ref[s, tiles * cap + STEP :, :]
    steps = labels_ref.shape[0]
    row = lax.broadcasted_iota(jnp.int32, (steps, LANES), 0)
    wanted = jnp.where(lanes_of(steps) == NOTE + row, 1.0, 0.0).astype(jnp.bfloat16)
    labels = lax.dot_general(
        wanted, notes_ref[...], (((1,), (1,)), ((), ())), preferred_element_type=jnp.float32
    )
    labels_ref[...] = labels
    code = jnp.zeros((steps, 1), jnp.float32)
    for h in range(QUAD):
        first = part_ref[h].astype(jnp.float32) + 1.0
        met = jnp.where((labels >= first) & (labels < first + resident), 1.0, 0.0)
        code = code + (1 << h) * jnp.max(met, axis=1, keepdims=True)
    at = lax.broadcasted_iota(jnp.int32, (steps, 1), 0)
    for a in range(cap // STEP):
        met_ref[a] = jnp.max(jnp.where(at == a, code, 0.0)).astype(jnp.int32)


def for_holders(met_ref, first_ref, near_refs, opened_ref, halved, a, step):
    pairs = opened_ref.shape[1] // LANES
    for h in range(QUAD):
        base = first_ref[h].astype(jnp.float32) + 1.0
        firsts = [base + 2.0 * t for t in range(pairs)]
        if h in halved:
            firsts = [
                base + first_ref[QUAD + i].astype(jnp.float32) + 2.0 * t
                for i in range(2)
                for t in range(pairs // 2)
            ]

        @pl.when(lax.rem(met_ref[a] // (1 << h), 2) > 0)
        def _(h=h, firsts=firsts):
            step(near_refs[h] if h < 2 else opened_ref.at[h - 2], firsts)


def down_kernel(first_ref, rows_ref, *refs):
    near_refs, far_refs, out_ref, count_ref = refs[:2], refs[2:6], refs[6], refs[7]
    opened_ref, batch_ref, picked_ref, notes_ref, labels_ref, met_ref = refs[8:]
    senders, width = rows_ref.shape[0], batch_ref.shape[1]
    tiles = width // LANES - 1
    cap = out_ref.shape[0] * STEP
    rank = out_ref.shape[1]
    resident = opened_ref.shape[1] // rank
    dims = (((1,), (1,)), ((), ()))
    read_notes(rows_ref, cap, tiles, first_ref, resident, notes_ref, labels_ref, met_ref)
    notes = notes_ref[...].astype(jnp.float32)
    is_count = lanes_of(senders * STEP) == NOTE + cap // STEP
    count = jnp.max(jnp.where(is_count, notes, 0.0), axis=(0, 1), keepdims=True)
    count_ref[...] = jnp.broadcast_to(count, count_ref.shape).astype(jnp.bfloat16)
    open_far(far_refs, DOWN_HALVED, opened_ref)

    def one(a, carry):
        picked_ref[...] = jnp.zeros(picked_ref.shape, jnp.float32)

        @pl.when(met_ref[a] > 0)
        def _():
            shift = lax.rem(LANES - QUARTER * (a // 2), LANES)
            spot = pl.multiple_of(tiles * cap + lax.rem(a, 2) * STEP, STEP)
            for s in range(senders):
                rows = slice(s * STEP, (s + 1) * STEP)
                for t in range(tiles):
                    at = pl.multiple_of(t * cap + a * STEP, STEP)
                    batch_ref[rows, t * LANES : (t + 1) * LANES] = rows_ref[s, pl.ds(at, STEP), :]
                end = rows_ref[s, pl.ds(spot, STEP), :].astype(jnp.float32)
                batch_ref[rows, tiles * LANES :] = pltpu.roll(end, shift, 1).astype(jnp.bfloat16)
            label = labels_ref[pl.ds(a, 1), :]

            def step(weight_ref, firsts):
                product = lax.dot_general(
                    weight_ref[...], batch_ref[...], dims, preferred_element_type=jnp.float32
                )
                picked = picked_ref[...]
                for t, first in enumerate(firsts):
                    for i in range(2):
                        at = (2 * t + i) * rank
                        picked = jnp.where(
                            label == first + i, product[at : at + rank, :], picked
                        )
                picked_ref[...] = picked

            for_holders(met_ref, first_ref, near_refs, opened_ref, DOWN_HALVED, a, step)

        out_ref[a] = picked_ref[...]
        return carry

    lax.fori_loop(0, cap // STEP, one, 0)


def pair_kernel(own_ref, other_ref, out_ref):
    out_ref[...] = (own_ref[...] + other_ref[...]).astype(jnp.bfloat16)


def up_kernel(first_ref, rows_ref, *refs):
    sum_refs, near_refs, far_refs, out_ref = refs[:2], refs[2:4], refs[4:7], refs[7]
    opened_ref, delta_ref, ends_ref, label_ref, twice_ref = refs[8:13]
    notes_ref, labels_ref, met_ref = refs[13:]
    senders, width = rows_ref.shape[0], opened_ref.shape[2]
    tiles = width // LANES - 1
    cap, rank = sum_refs[0].shape[0] * STEP, sum_refs[0].shape[1]
    resident = opened_ref.shape[1] // rank
    kept = (out_ref.shape[1] - QUARTER) // tiles
    group_lane = lanes_of(STEP) // QUARTER
    read_notes(rows_ref, cap, tiles, first_ref, resident, notes_ref, labels_ref, met_ref)
    open_far(far_refs, UP_HALVED, opened_ref)
    ends_ref[...] = jnp.zeros(ends_ref.shape, jnp.float32)
    low = jnp.where(lanes_of(senders * STEP) < HALF, 0.0, 1.0)
    rank_row = lax.broadcasted_iota(jnp.int32, (rank, LANES), 0)
    twofold = jnp.where(lax.rem(lanes_of(rank), rank) == rank_row, 1.0, 0.0).astype(jnp.bfloat16)

    note_row = lax.broadcasted_iota(jnp.int32, (LANES, LANES), 0)
    for a in range(kept // STEP):
        wanted = jnp.where(note_row == NOTE + a, 1.0, 0.0).astype(jnp.bfloat16)
        label_ref[a] = jnp.dot(notes_ref[...], wanted, preferred_element_type=jnp.float32) - low
        down = sum_refs[0][a].astype(jnp.float32) + sum_refs[1][a].astype(jnp.float32)
        twice_ref[a] = lax.dot_general(
            down.astype(jnp.bfloat16),
            twofold,
            (((0,), (0,)), ((), ())),
            preferred_element_type=jnp.float32,
        )

    def one(a, carry):
        delta_ref[...] = jnp.zeros(delta_ref.shape, jnp.float32)

        @pl.when(met_ref[a] > 0)
        def _():
            label, twice = label_ref[a], twice_ref[a]

            def step(weight_ref, firsts):
                placed = [jnp.where(label == first, twice, 0.0) for first in firsts]
                placed = jnp.concatenate(placed, axis=1).astype(jnp.bfloat16)
                delta_ref[...] += jnp.dot(
                    placed, weight_ref[...], preferred_element_type=jnp.float32
                )

            for_holders(met_ref, first_ref, near_refs, opened_ref, UP_HALVED, a, step)

        spot = pl.multiple_of(lax.rem(a, 2) * STEP, STEP)
        for s in range(senders):
            rows = slice(s * STEP, (s + 1) * STEP)
            for t in range(tiles):
                at = pl.multiple_of(t * kept + a * STEP, STEP)
                out_ref[s, pl.ds(at, STEP), :] = delta_ref[
                    rows, t * LANES : (t + 1) * LANES
                ].astype(jnp.bfloat16)
            turned = pltpu.roll(delta_ref[rows, tiles * LANES :], QUARTER * (a // 2), 1)
            ends_ref[s, pl.ds(spot, STEP), :] = jnp.where(
                group_lane == a // 2, turned, ends_ref[s, pl.ds(spot, STEP), :]
            )
        return carry

    lax.fori_loop(0, kept // STEP, one, 0)
    for s in range(senders):
        out_ref[s, tiles * kept :, :] = ends_ref[s].astype(jnp.bfloat16)


def mix_kernel(whole, bases, target_ref, tokens_ref, *refs):
    returned_refs, out_ref = refs[:-1], refs[-1]
    total = tokens_ref.shape[0]
    tiles, quads = whole // LANES, returned_refs[0].shape[0] // QUAD
    lane = lanes_of(total)
    chosen = []
    for base, ref in zip(bases, returned_refs):
        kept = (ref.shape[1] - QUARTER) // tiles
        spot = lax.broadcasted_iota(jnp.int32, (total, quads * kept), 1)
        place = spot // kept * total + spot % kept + base
        chosen.append(jnp.where(target_ref[...] == place, 1.0, 0.0).astype(jnp.bfloat16))
    end = jnp.zeros((total, LANES), jnp.float32)
    for j in range(QUAD):
        delta = 0.0
        for choice, ref in zip(chosen, returned_refs):
            kept = choice.shape[1] // quads
            shares = []
            for q in range(quads):
                d = q * QUAD + j
                parts = [ref[d, t * kept : (t + 1) * kept, :] for t in range(tiles)]
                packed = ref[d, tiles * kept :, :].astype(jnp.float32)
                groups = [packed]
                for m in range(1, QUAD):
                    groups.append(pltpu.roll(packed, LANES - QUARTER * m, 1))
                parts.append(jnp.concatenate(groups, axis=0)[0:kept].astype(jnp.bfloat16))
                shares.append(jnp.concatenate(parts, axis=1))
            share = jnp.concatenate(shares, axis=0)
            delta = delta + jnp.dot(choice, share, preferred_element_type=jnp.float32)
        columns = slice(j * whole, (j + 1) * whole)
        out_ref[:, columns] = (
            tokens_ref[:, columns].astype(jnp.float32) + delta[:, 0:whole]
        ).astype(jnp.bfloat16)
        last = delta[:, whole:]
        turned = pltpu.roll(last, QUARTER * j, 1) if j else last
        end = jnp.where((lane >= QUARTER * j) & (lane < QUARTER * (j + 1)), turned, end)
    out_ref[:, QUAD * whole :] = (
        tokens_ref[:, QUAD * whole :].astype(jnp.float32) + end
    ).astype(jnp.bfloat16)


def call(kernel, out_shape, in_specs, flops, moved, after=(), scratch=()):
    many = isinstance(out_shape, list)
    skipped = len(after)
    body = (lambda *refs: kernel(*refs[skipped:])) if skipped else kernel
    run = pl.pallas_call(
        body,
        out_shape=out_shape,
        in_specs=[pl.BlockSpec(memory_space=pl.ANY)] * skipped + in_specs,
        out_specs=[VMEM] * len(out_shape) if many else VMEM,
        scratch_shapes=scratch,
        compiler_params=pltpu.CompilerParams(vmem_limit_bytes=48 * 2**20),
        cost_estimate=pl.CostEstimate(flops=flops, bytes_accessed=moved, transcendentals=0),
    )
    return functools.partial(run, *after)


def exchange(value):
    return lax.all_to_all(value, "adapter", split_axis=0, concat_axis=0, tiled=True)


def towards(value, k, devices):
    return lax.ppermute(value, "adapter", [(i, i ^ k) for i in range(devices)])


def swapped(value):
    return lax.ppermute(value, "groups", [(0, 1), (1, 0)])


def stand_behind(value, *earlier):
    return pl.pallas_call(
        lambda *refs: None,
        out_shape=jax.ShapeDtypeStruct(value.shape, value.dtype),
        in_specs=[pl.BlockSpec(memory_space=pl.ANY)] * (1 + len(earlier)),
        out_specs=pl.BlockSpec(memory_space=pl.ANY),
        input_output_aliases={0: 0},
    )(value, *earlier)


def note_scratch(devices):
    return [
        pltpu.VMEM((devices * STEP, LANES), jnp.bfloat16),
        pltpu.VMEM((8, devices * STEP), jnp.float32),
        pltpu.SMEM((8,), jnp.int32),
    ]


def first_pack_call(cap, whole, devices, resident, adapter, used, tokens):
    blocks, rows, width = tokens.shape
    total = blocks * rows
    return call(
        functools.partial(first_pack_kernel, whole, cap, resident),
        [
            jax.ShapeDtypeStruct((devices, whole // LANES * cap + QUARTER, LANES), jnp.bfloat16),
            jax.ShapeDtypeStruct((1, total), jnp.int32),
            jax.ShapeDtypeStruct((total, 1), jnp.float32),
        ],
        [VMEM, VMEM, VMEM],
        2 * devices * cap * total * whole,
        2 * (total * width + devices * cap * whole),
        scratch=[pltpu.VMEM((total, width), jnp.bfloat16), pltpu.VMEM((8, LANES), jnp.int32)],
    )(adapter.reshape(1, blocks), used.reshape(1, blocks), tokens.reshape(total, width))


def pack_call(cap, base, whole, devices, target, label, tokens):
    blocks, rows, width = tokens.shape
    total = blocks * rows
    return call(
        functools.partial(pack_kernel, whole, cap, base),
        jax.ShapeDtypeStruct((devices, whole // LANES * cap + QUARTER, LANES), jnp.bfloat16),
        [VMEM, VMEM, VMEM, VMEM],
        2 * devices * cap * total * whole,
        2 * (total * width + devices * cap * whole),
        scratch=[pltpu.VMEM((total, width), jnp.bfloat16)],
    )(jnp.zeros((8, LANES), jnp.int32), target, label, tokens.reshape(total, width))


def down_call(cap, first, arrived, down_weights, after):
    devices = arrived.shape[0]
    columns, share = down_weights[0].shape
    return call(
        down_kernel,
        [
            jax.ShapeDtypeStruct((cap // STEP, HALF, devices * STEP), jnp.float32),
            jax.ShapeDtypeStruct((STEP, LANES), jnp.bfloat16),
        ],
        [SMEM] + [VMEM] * (1 + len(down_weights)),
        0,
        0,
        after,
        [
            pltpu.VMEM((2, columns, share), jnp.bfloat16),
            pltpu.VMEM((devices * STEP, share), jnp.bfloat16),
            pltpu.VMEM((HALF, devices * STEP), jnp.float32),
            *note_scratch(devices),
        ],
    )(first, arrived, *down_weights)


def quad_sums(partial, devices):
    pair = call(
        pair_kernel, jax.ShapeDtypeStruct(partial.shape, jnp.bfloat16), [VMEM, VMEM], 0, 0
    )(partial, towards(partial, 1, devices))
    return [pair, towards(pair, 2, devices)]


def up_call(kept, first, arrived, sums, up_weights):
    devices = arrived.shape[0]
    columns, share = up_weights[0].shape
    shape = (devices, (share // LANES - 1) * kept + QUARTER, LANES)
    return call(
        up_kernel,
        jax.ShapeDtypeStruct(shape, jnp.bfloat16),
        [SMEM] + [VMEM] * (3 + len(up_weights)),
        2 * devices * kept * QUAD * columns * share,
        2 * (2 * devices * kept + QUAD * columns) * share,
        scratch=[
            pltpu.VMEM((2, columns, share), jnp.bfloat16),
            pltpu.VMEM((devices * STEP, share), jnp.float32),
            pltpu.VMEM((devices, QUARTER, LANES), jnp.float32),
            *[pltpu.VMEM((kept // STEP, devices * STEP, LANES), jnp.float32)] * 2,
            *note_scratch(devices),
        ],
    )(first, arrived, *sums, *up_weights)


def back_and_mix(
    kept, more, tokens, target, label, first, arrived, sums, down_weights, up_weights, *unused
):
    blocks, rows, width = tokens.shape
    total = blocks * rows
    devices = arrived.shape[0]
    whole = up_weights[0].shape[1] - LANES
    pieces = [exchange(up_call(kept, first, arrived, sums, up_weights))]
    if more:
        outgoing = pack_call(more, kept, whole, devices, target, label, tokens)
        arrived = exchange(outgoing)
        partial = down_call(more, first, arrived, down_weights, [])[0]
        sums = quad_sums(partial, devices)
        pieces.append(exchange(up_call(more, first, arrived, sums, up_weights)))
    mixed = call(
        functools.partial(mix_kernel, whole, (0, kept)[: len(pieces)]),
        jax.ShapeDtypeStruct((total, width), jnp.bfloat16),
        [VMEM] * (2 + len(pieces)),
        2 * devices * (kept + more) * total * whole,
        2 * (2 * total * width + devices * (kept + more) * whole),
    )(target.reshape(total, 1), tokens.reshape(total, width), *pieces)
    return mixed.reshape(tokens.shape)


def start_again(
    tokens, target, label, first, arrived, sums, down_weights, up_weights, *arguments
):
    return rows_to_holders(tokens, *arguments)


def rows_to_quads(
    tokens, request_block_adapter, request_block_rows, adapter_down_weight, adapter_up_weight
):
    blocks, rows, width = tokens.shape
    devices = lax.axis_size("adapter")
    resident, rank, unused_width = adapter_up_weight.shape
    total = blocks * rows
    columns = resident * rank
    whole = width // LANES // QUAD * LANES
    share = whole + LANES
    bf16, i32 = jnp.bfloat16, jnp.int32

    me = lax.axis_index("adapter").astype(i32)
    group = lax.axis_index("groups").astype(i32)
    parts = jnp.bitwise_xor(me % QUAD, jnp.arange(QUAD, dtype=i32))
    halves = jnp.stack([group, 1 - group]) * (resident // 2)
    first = jnp.concatenate([parts * resident, halves]).astype(i32)
    tiles = whole // LANES

    def shares(weight, halved, after):
        shapes = []
        for k in range(QUAD):
            count = columns // 2 if k in halved else columns
            far = (count * tiles + count // QUAD, LANES)
            shapes.append(jax.ShapeDtypeStruct((columns, share) if k < 2 else far, bf16))
        values = call(
            functools.partial(weight_kernel, whole, range(QUAD), halved),
            shapes,
            [SMEM, SMEM, VMEM],
            0,
            QUAD * columns * width,
            after,
        )(parts, group.reshape(1), weight)
        return [values[0]] + [towards(values[k], k, devices) for k in range(1, QUAD)]

    weight = adapter_down_weight.transpose(0, 2, 1).reshape(columns, width)
    down_weights = shares(weight, DOWN_HALVED, [])
    weight = adapter_up_weight.reshape(columns, width)
    up_weights = shares(weight, UP_HALVED, down_weights[:1])
    down_weights[2] = stand_behind(down_weights[2], up_weights[0])
    down_weights += [swapped(down_weights[k]) for k in DOWN_HALVED]
    up_weights += [swapped(up_weights[k]) for k in UP_HALVED]

    caps = [total * 5 // 16, total * 6 // 16, total * 7 // 16]
    cap = caps[-1]
    outgoing, target, label = first_pack_call(
        cap, whole, devices, resident, request_block_adapter, request_block_rows, tokens
    )
    arrived = exchange(outgoing)
    partial, count = down_call(cap, first, arrived, down_weights, up_weights[2:3])
    sums = quad_sums(partial, devices)
    count = count[0:1, 0:1]
    most = jnp.maximum(count, swapped(count))[0, 0].astype(jnp.float32)
    branches = [functools.partial(back_and_mix, kept, 0) for kept in caps]
    branches += [functools.partial(back_and_mix, cap, STEP), start_again]
    return lax.switch(
        sum((most > limit).astype(i32) for limit in [*caps, cap + STEP]),
        branches,
        tokens,
        target,
        label,
        first,
        arrived,
        sums,
        down_weights,
        up_weights,
        request_block_adapter,
        request_block_rows,
        adapter_down_weight,
        adapter_up_weight,
    )


def solution(mesh):
    placed = (
        P(("groups", "adapter"), None, None),
        P(("groups", "adapter")),
        P(("groups", "adapter")),
        P("adapter", None, None),
        P("adapter", None, None),
    )

    def per_device(tokens, request_block_adapter, request_block_rows, down_weight, up_weight):
        blocks, rows, width = tokens.shape
        devices = mesh.shape["adapter"]
        slots = max(1, 4 * blocks // devices)
        quads = devices % QUAD == 0 and slots * QUAD >= blocks
        quads = quads and width % (QUAD * LANES) == LANES and up_weight.shape[1] == HALF
        quads = quads and blocks * rows * 7 // 16 == 7 * STEP and mesh.shape["groups"] == 2
        plan = rows_to_quads if quads else rows_to_holders
        return plan(tokens, request_block_adapter, request_block_rows, down_weight, up_weight)

    return jax.shard_map(
        per_device,
        mesh=mesh,
        in_specs=placed,
        out_specs=P(("groups", "adapter"), None, None),
        check_vma=False,
    )
```

```python
import functools

import jax
import jax.numpy as jnp
from jax import lax
from jax.experimental import pallas as pl
from jax.experimental.pallas import tpu as pltpu
from jax.sharding import PartitionSpec as P

LANES = 128
HALF = 64
QUAD = 4
QUARTER = 32
STEP = 16
NOTE = 96
DOWN_HALVED = (2, 3)
UP_HALVED = (2,)
VMEM = pl.BlockSpec(memory_space=pltpu.VMEM)
SMEM = pl.BlockSpec(memory_space=pltpu.SMEM)


def normalise(tokens):
    values = tokens.astype(jnp.float32)
    mean_sq = jnp.mean(values * values, axis=-1, keepdims=True)
    return (values, (values * lax.rsqrt(mean_sq + 1e-06)).astype(jnp.bfloat16))


def resident_update(hidden_state, block_labels, adapter_down_weight, adapter_up_weight):
    feature_width = hidden_state.shape[-1]
    leading = hidden_state.shape[:-1]
    resident_rows, unused_value, inner_rank = adapter_down_weight.shape
    flattened_tokens = hidden_state.reshape(-1, feature_width)
    down_matrix = jnp.einsum(
        "tq,iqg->tig", flattened_tokens, adapter_down_weight, preferred_element_type=jnp.float32
    )
    down_matrix = down_matrix.astype(jnp.bfloat16).reshape(
        flattened_tokens.shape[0], resident_rows * inner_rank
    )
    column_owner = jnp.arange(resident_rows * inner_rank, dtype=jnp.int32) // inner_rank
    picked = block_labels.reshape(-1, 1) == column_owner[None, :]
    down_matrix = jnp.where(picked, down_matrix, jnp.zeros_like(down_matrix))
    lowrank_update = jnp.dot(
        down_matrix,
        adapter_up_weight.reshape(resident_rows * inner_rank, feature_width),
        preferred_element_type=jnp.float32,
    )
    return lowrank_update.astype(jnp.bfloat16).reshape(leading + (feature_width,))


def rows_to_holders(
    tokens, request_block_adapter, request_block_rows, adapter_down_weight, adapter_up_weight
):
    blocks, rows, feature_width = tokens.shape
    devices = lax.axis_size("adapter")
    resident_rows = adapter_down_weight.shape[0]
    slots = max(1, 4 * blocks // devices)
    values, normed = normalise(tokens)
    owner = request_block_adapter // resident_rows
    within = request_block_adapter - owner * resident_rows
    serial = jnp.arange(blocks, dtype=jnp.int32)
    earlier = (owner[:, None] == owner[None, :]) & (serial[None, :] < serial[:, None])
    position = owner * slots + jnp.sum(earlier, axis=1)
    outgoing = (
        jnp.zeros((devices * slots, rows, feature_width), jnp.bfloat16).at[position].set(normed)
    )
    outgoing = outgoing.reshape(devices, slots, rows, feature_width)
    block_labels = jnp.full((devices * slots,), -1, jnp.int32).at[position].set(within)
    block_labels = jnp.broadcast_to(block_labels[:, None], (devices * slots, rows)).reshape(
        devices, slots, rows
    )
    arriving_rows, row_markers = (
        lax.all_to_all(outgoing, "adapter", split_axis=0, concat_axis=0, tiled=True),
        lax.all_to_all(block_labels, "adapter", split_axis=0, concat_axis=0, tiled=True),
    )
    lowrank_update = resident_update(
        arriving_rows, row_markers, adapter_down_weight, adapter_up_weight
    )
    returned = lax.all_to_all(lowrank_update, "adapter", split_axis=0, concat_axis=0, tiled=True)
    mine = returned.reshape(devices * slots, rows, feature_width)[position]
    live = jnp.arange(rows, dtype=jnp.int32)[None, :] < request_block_rows[:, None]
    mixed = values + jnp.where(live[:, :, None], mine.astype(jnp.float32), jnp.float32(0.0))
    return mixed.astype(jnp.bfloat16)


def lanes_of(rows):
    return lax.broadcasted_iota(jnp.int32, (rows, LANES), 1)


def weight_kernel(whole, which, halved, part_ref, group_ref, weight_ref, *out_refs):
    tiles = whole // LANES
    for k, out_ref in zip(which, out_refs):
        j = part_ref[k]
        if k < 2:
            last = weight_ref[:, QUAD * whole :].astype(jnp.float32)
            turned = pltpu.roll(last, lax.rem(LANES - QUARTER * j, LANES), 1)
            inside = lanes_of(last.shape[0]) < QUARTER
            out_ref[:, 0:whole] = weight_ref[:, pl.ds(pl.multiple_of(j * whole, LANES), whole)]
            out_ref[:, whole:] = jnp.where(inside, turned, 0.0).astype(jnp.bfloat16)
            continue
        count = weight_ref.shape[0] // 2 if k in halved else weight_ref.shape[0]
        start = pl.multiple_of(group_ref[0] * count, count) if k in halved else 0
        for t in range(tiles):
            column = pl.multiple_of(j * whole + t * LANES, LANES)
            out_ref[t * count : (t + 1) * count, :] = weight_ref[
                pl.ds(start, count), pl.ds(column, LANES)
            ]
        last = weight_ref[pl.ds(start, count), QUAD * whole :].astype(jnp.float32)
        size = count // QUAD
        owner = lanes_of(size) // QUARTER
        merged = jnp.zeros((size, LANES), jnp.float32)
        for m in range(QUAD):
            shift = lax.rem(LANES + QUARTER * (m - j), LANES)
            turned = pltpu.roll(last[m * size : (m + 1) * size], shift, 1)
            merged = jnp.where(owner == m, turned, merged)
        out_ref[tiles * count :, :] = merged.astype(jnp.bfloat16)


def open_far(far_refs, halved, opened_ref):
    width = opened_ref.shape[2]
    tiles = width // LANES - 1
    places = [(k - 2, 0) for k in (2, 3)] + [(k - 2, 1) for k in halved]
    for ref, (holder, part) in zip(far_refs, places):
        count = opened_ref.shape[1] // 2 if holder + 2 in halved else opened_ref.shape[1]
        base, size = part * count, count // QUAD
        inside = lanes_of(size) < QUARTER
        for t in range(tiles):
            opened_ref[holder, base : base + count, t * LANES : (t + 1) * LANES] = ref[
                t * count : (t + 1) * count, :
            ]
        packed = ref[tiles * count :, :].astype(jnp.float32)
        for m in range(QUAD):
            turned = pltpu.roll(packed, (LANES - QUARTER * m) % LANES, 1) if m else packed
            opened_ref[holder, base + m * size : base + (m + 1) * size, tiles * LANES :] = (
                jnp.where(inside, turned, 0.0).astype(jnp.bfloat16)
            )


def lay_out(resident, adapter_ref, used_ref, most_ref, target_ref, label_ref):
    blocks, total = adapter_ref.shape[1], target_ref.shape[1]
    rows = total // blocks
    adapter, used = adapter_ref[...], used_ref[...]
    down = lax.broadcasted_iota(jnp.int32, (blocks, blocks), 0)
    across = lax.broadcasted_iota(jnp.int32, (blocks, blocks), 1)

    def turned(value):
        return jnp.sum(jnp.where(down == across, value, 0), axis=1, keepdims=True)

    span = resident * QUAD
    quad = jnp.floor((adapter.astype(jnp.float32) + 0.5) * (1.0 / span)).astype(jnp.int32)
    order = adapter * blocks + lax.broadcasted_iota(jnp.int32, (1, blocks), 1)
    quad_down, order_down, used_down = turned(quad), turned(order), turned(used)
    same = quad_down == quad
    ahead = jnp.sum(jnp.where(same & (order < order_down), used, 0), axis=1, keepdims=True)
    within = jnp.sum(jnp.where(same, used, 0), axis=1, keepdims=True)
    most_ref[...] = jnp.broadcast_to(jnp.max(within, axis=0, keepdims=True), most_ref.shape)
    start = quad_down * total + ahead

    block = lax.broadcasted_iota(jnp.int32, (blocks, total), 0)
    row = lax.broadcasted_iota(jnp.int32, (blocks, total), 1) - block * rows
    place = jnp.where((row >= 0) & (row < used_down), start + row + 1, 0)
    target_ref[...] = jnp.sum(place, axis=0, keepdims=True) - 1
    block = lax.broadcasted_iota(jnp.int32, (total, blocks), 1)
    row = lax.broadcasted_iota(jnp.int32, (total, blocks), 0) - block * rows
    label = jnp.where((row >= 0) & (row < rows), adapter - quad * span + 1, 0)
    label_ref[...] = jnp.sum(label.astype(jnp.float32), axis=1, keepdims=True)


def first_pack_kernel(
    whole, cap, resident, adapter_ref, used_ref, tokens_ref, out_ref, target_ref, label_ref, *refs
):
    normed_ref, most_ref = refs
    lay_out(resident, adapter_ref, used_ref, most_ref, target_ref, label_ref)
    pack_kernel(
        whole, cap, 0, most_ref, target_ref, label_ref, tokens_ref, out_ref, normed_ref
    )


def pack_kernel(
    whole, cap, base, most_ref, target_ref, label_ref, tokens_ref, out_ref, normed_ref
):
    values = tokens_ref[...].astype(jnp.float32)
    mean_sq = jnp.mean(values * values, axis=-1, keepdims=True)
    normed_ref[...] = (values * lax.rsqrt(mean_sq + 1e-06)).astype(jnp.bfloat16)
    total = tokens_ref.shape[0]
    quads, tiles = out_ref.shape[0] // QUAD, whole // LANES
    lane = lanes_of(total)
    last = normed_ref[:, QUAD * whole :].astype(jnp.float32)
    label = jnp.where(lane == QUARTER, label_ref[...], 0.0)
    ends = []
    for j in range(QUAD):
        turned = pltpu.roll(last, (LANES - QUARTER * j) % LANES, 1) if j else last
        ends.append(jnp.where(lane < QUARTER, turned, label).astype(jnp.bfloat16))
    most = most_ref[0:1, 0:1].astype(jnp.float32)
    group_lane = lanes_of(QUARTER) // QUARTER
    step_lane = lanes_of(STEP)
    chosen = []
    for q in range(quads):
        place = lax.broadcasted_iota(jnp.int32, (cap, total), 0) + (q * total + base)
        chosen.append(jnp.where(target_ref[...] == place, 1.0, 0.0).astype(jnp.bfloat16))
    chosen = jnp.concatenate(chosen, axis=0)
    notes = [jnp.where(step_lane == NOTE + cap // STEP, most, 0.0)] * quads
    for j in range(QUAD):
        for t in range(tiles):
            column = j * whole + t * LANES
            if t % 2 == 0:
                count = min(2, tiles - t) * LANES
                share = jnp.dot(
                    chosen,
                    normed_ref[:, column : column + count],
                    preferred_element_type=jnp.float32,
                ).astype(jnp.bfloat16)
            for q in range(quads):
                out_ref[q * QUAD + j, t * cap : (t + 1) * cap, :] = share[
                    q * cap : (q + 1) * cap, t % 2 * LANES : (t % 2 + 1) * LANES
                ]
        end_rows = jnp.dot(chosen, ends[j], preferred_element_type=jnp.float32)
        for q in range(quads):
            end = end_rows[q * cap : (q + 1) * cap]
            if j == 0:
                for a in range(cap // STEP):
                    turned = pltpu.roll(end[a * STEP : (a + 1) * STEP], NOTE + a - QUARTER, 1)
                    notes[q] = jnp.where(step_lane == NOTE + a, turned, notes[q])
            padded = jnp.concatenate(
                [end, jnp.zeros((QUAD * QUARTER - cap, LANES), jnp.float32)], axis=0
            )
            merged = padded[0:QUARTER]
            for m in range(1, QUAD):
                turned = pltpu.roll(padded[m * QUARTER : (m + 1) * QUARTER], m * QUARTER, 1)
                merged = jnp.where(group_lane == m, turned, merged)
            out_ref[q * QUAD + j, tiles * cap : tiles * cap + STEP, :] = merged[0:STEP].astype(
                jnp.bfloat16
            )
            out_ref[q * QUAD + j, tiles * cap + STEP :, :] = jnp.where(
                step_lane >= NOTE, notes[q], merged[STEP:]
            ).astype(jnp.bfloat16)


def read_notes(rows_ref, cap, tiles, part_ref, resident, notes_ref, labels_ref, met_ref):
    senders = rows_ref.shape[0]
    for s in range(senders):
        notes_ref[s * STEP : (s + 1) * STEP, :] = rows_ref[s, tiles * cap + STEP :, :]
    steps = labels_ref.shape[0]
    row = lax.broadcasted_iota(jnp.int32, (steps, LANES), 0)
    wanted = jnp.where(lanes_of(steps) == NOTE + row, 1.0, 0.0).astype(jnp.bfloat16)
    labels = lax.dot_general(
        wanted, notes_ref[...], (((1,), (1,)), ((), ())), preferred_element_type=jnp.float32
    )
    labels_ref[...] = labels
    code = jnp.zeros((steps, 1), jnp.float32)
    for h in range(QUAD):
        first = part_ref[h].astype(jnp.float32) + 1.0
        met = jnp.where((labels >= first) & (labels < first + resident), 1.0, 0.0)
        code = code + (1 << h) * jnp.max(met, axis=1, keepdims=True)
    at = lax.broadcasted_iota(jnp.int32, (steps, 1), 0)
    for a in range(cap // STEP):
        met_ref[a] = jnp.max(jnp.where(at == a, code, 0.0)).astype(jnp.int32)


def for_holders(met_ref, first_ref, near_refs, opened_ref, halved, a, step):
    pairs = opened_ref.shape[1] // LANES
    for h in range(QUAD):
        base = first_ref[h].astype(jnp.float32) + 1.0
        firsts = [base + 2.0 * t for t in range(pairs)]
        if h in halved:
            firsts = [
                base + first_ref[QUAD + i].astype(jnp.float32) + 2.0 * t
                for i in range(2)
                for t in range(pairs // 2)
            ]

        @pl.when(lax.rem(met_ref[a] // (1 << h), 2) > 0)
        def _(h=h, firsts=firsts):
            step(near_refs[h] if h < 2 else opened_ref.at[h - 2], firsts)


def down_kernel(first_ref, rows_ref, *refs):
    near_refs, far_refs, out_ref, count_ref = refs[:2], refs[2:6], refs[6], refs[7]
    notes_ref, met_ref, opened_ref, batch_ref, picked_ref, labels_ref = refs[8:]
    senders, width = rows_ref.shape[0], batch_ref.shape[1]
    tiles = width // LANES - 1
    cap = out_ref.shape[0] * STEP
    rank = out_ref.shape[1]
    resident = opened_ref.shape[1] // rank
    dims = (((1,), (1,)), ((), ()))
    read_notes(rows_ref, cap, tiles, first_ref, resident, notes_ref, labels_ref, met_ref)
    notes = notes_ref[...].astype(jnp.float32)
    is_count = lanes_of(senders * STEP) == NOTE + cap // STEP
    count = jnp.max(jnp.where(is_count, notes, 0.0), axis=(0, 1), keepdims=True)
    count_ref[...] = jnp.broadcast_to(count, count_ref.shape).astype(jnp.bfloat16)
    open_far(far_refs, DOWN_HALVED, opened_ref)

    def one(a, carry):
        picked_ref[...] = jnp.zeros(picked_ref.shape, jnp.float32)

        @pl.when(met_ref[a] > 0)
        def _():
            shift = lax.rem(LANES - QUARTER * (a // 2), LANES)
            spot = pl.multiple_of(tiles * cap + lax.rem(a, 2) * STEP, STEP)
            for s in range(senders):
                rows = slice(s * STEP, (s + 1) * STEP)
                for t in range(tiles):
                    at = pl.multiple_of(t * cap + a * STEP, STEP)
                    batch_ref[rows, t * LANES : (t + 1) * LANES] = rows_ref[s, pl.ds(at, STEP), :]
                end = rows_ref[s, pl.ds(spot, STEP), :].astype(jnp.float32)
                batch_ref[rows, tiles * LANES :] = pltpu.roll(end, shift, 1).astype(jnp.bfloat16)
            label = labels_ref[pl.ds(a, 1), :]

            def step(weight_ref, firsts):
                product = lax.dot_general(
                    weight_ref[...], batch_ref[...], dims, preferred_element_type=jnp.float32
                )
                picked = picked_ref[...]
                for t, first in enumerate(firsts):
                    for i in range(2):
                        at = (2 * t + i) * rank
                        picked = jnp.where(
                            label == first + i, product[at : at + rank, :], picked
                        )
                picked_ref[...] = picked

            for_holders(met_ref, first_ref, near_refs, opened_ref, DOWN_HALVED, a, step)

        out_ref[a] = picked_ref[...]
        return carry

    lax.fori_loop(0, cap // STEP, one, 0)


def pair_kernel(own_ref, other_ref, out_ref):
    out_ref[...] = (own_ref[...] + other_ref[...]).astype(jnp.bfloat16)


def up_kernel(first_ref, met_ref, notes_ref, *refs):
    sum_refs, near_refs, far_refs, out_ref = refs[:2], refs[2:4], refs[4:7], refs[7]
    opened_ref, delta_ref, ends_ref, label_ref, twice_ref = refs[8:]
    senders, width = out_ref.shape[0], opened_ref.shape[2]
    tiles = width // LANES - 1
    rank = sum_refs[0].shape[1]
    kept = (out_ref.shape[1] - QUARTER) // tiles
    group_lane = lanes_of(STEP) // QUARTER
    open_far(far_refs, UP_HALVED, opened_ref)
    ends_ref[...] = jnp.zeros(ends_ref.shape, jnp.float32)
    low = jnp.where(lanes_of(senders * STEP) < HALF, 0.0, 1.0)
    rank_row = lax.broadcasted_iota(jnp.int32, (rank, LANES), 0)
    twofold = jnp.where(lax.rem(lanes_of(rank), rank) == rank_row, 1.0, 0.0).astype(jnp.bfloat16)

    note_row = lax.broadcasted_iota(jnp.int32, (LANES, LANES), 0)
    for a in range(kept // STEP):
        wanted = jnp.where(note_row == NOTE + a, 1.0, 0.0).astype(jnp.bfloat16)
        label_ref[a] = jnp.dot(notes_ref[...], wanted, preferred_element_type=jnp.float32) - low
        down = sum_refs[0][a].astype(jnp.float32) + sum_refs[1][a].astype(jnp.float32)
        twice_ref[a] = lax.dot_general(
            down.astype(jnp.bfloat16),
            twofold,
            (((0,), (0,)), ((), ())),
            preferred_element_type=jnp.float32,
        )

    def one(a, carry):
        delta_ref[...] = jnp.zeros(delta_ref.shape, jnp.float32)

        @pl.when(met_ref[a] > 0)
        def _():
            label, twice = label_ref[a], twice_ref[a]

            def step(weight_ref, firsts):
                placed = [jnp.where(label == first, twice, 0.0) for first in firsts]
                placed = jnp.concatenate(placed, axis=1).astype(jnp.bfloat16)
                delta_ref[...] += jnp.dot(
                    placed, weight_ref[...], preferred_element_type=jnp.float32
                )

            for_holders(met_ref, first_ref, near_refs, opened_ref, UP_HALVED, a, step)

        spot = pl.multiple_of(lax.rem(a, 2) * STEP, STEP)
        for s in range(senders):
            rows = slice(s * STEP, (s + 1) * STEP)
            for t in range(tiles):
                at = pl.multiple_of(t * kept + a * STEP, STEP)
                out_ref[s, pl.ds(at, STEP), :] = delta_ref[
                    rows, t * LANES : (t + 1) * LANES
                ].astype(jnp.bfloat16)
            turned = pltpu.roll(delta_ref[rows, tiles * LANES :], QUARTER * (a // 2), 1)
            ends_ref[s, pl.ds(spot, STEP), :] = jnp.where(
                group_lane == a // 2, turned, ends_ref[s, pl.ds(spot, STEP), :]
            )
        return carry

    lax.fori_loop(0, kept // STEP, one, 0)
    for s in range(senders):
        out_ref[s, tiles * kept :, :] = ends_ref[s].astype(jnp.bfloat16)


def mix_kernel(whole, bases, target_ref, tokens_ref, *refs):
    returned_refs, out_ref = refs[:-1], refs[-1]
    total = tokens_ref.shape[0]
    tiles, quads = whole // LANES, returned_refs[0].shape[0] // QUAD
    lane = lanes_of(total)
    chosen = []
    for base, ref in zip(bases, returned_refs):
        kept = (ref.shape[1] - QUARTER) // tiles
        spot = lax.broadcasted_iota(jnp.int32, (total, quads * kept), 1)
        place = spot // kept * total + spot % kept + base
        chosen.append(jnp.where(target_ref[...] == place, 1.0, 0.0).astype(jnp.bfloat16))
    end = jnp.zeros((total, LANES), jnp.float32)
    for j in range(QUAD):
        delta = 0.0
        for choice, ref in zip(chosen, returned_refs):
            kept = choice.shape[1] // quads
            shares = []
            for q in range(quads):
                d = q * QUAD + j
                parts = [ref[d, t * kept : (t + 1) * kept, :] for t in range(tiles)]
                packed = ref[d, tiles * kept :, :].astype(jnp.float32)
                groups = [packed]
                for m in range(1, QUAD):
                    groups.append(pltpu.roll(packed, LANES - QUARTER * m, 1))
                parts.append(jnp.concatenate(groups, axis=0)[0:kept].astype(jnp.bfloat16))
                shares.append(jnp.concatenate(parts, axis=1))
            share = jnp.concatenate(shares, axis=0)
            delta = delta + jnp.dot(choice, share, preferred_element_type=jnp.float32)
        columns = slice(j * whole, (j + 1) * whole)
        out_ref[:, columns] = (
            tokens_ref[:, columns].astype(jnp.float32) + delta[:, 0:whole]
        ).astype(jnp.bfloat16)
        last = delta[:, whole:]
        turned = pltpu.roll(last, QUARTER * j, 1) if j else last
        end = jnp.where((lane >= QUARTER * j) & (lane < QUARTER * (j + 1)), turned, end)
    out_ref[:, QUAD * whole :] = (
        tokens_ref[:, QUAD * whole :].astype(jnp.float32) + end
    ).astype(jnp.bfloat16)


def call(kernel, out_shape, in_specs, flops, moved, after=(), scratch=(), out_specs=None):
    many = isinstance(out_shape, list)
    skipped = len(after)
    body = (lambda *refs: kernel(*refs[skipped:])) if skipped else kernel
    run = pl.pallas_call(
        body,
        out_shape=out_shape,
        in_specs=[pl.BlockSpec(memory_space=pl.ANY)] * skipped + in_specs,
        out_specs=out_specs or ([VMEM] * len(out_shape) if many else VMEM),
        scratch_shapes=scratch,
        compiler_params=pltpu.CompilerParams(vmem_limit_bytes=48 * 2**20),
        cost_estimate=pl.CostEstimate(flops=flops, bytes_accessed=moved, transcendentals=0),
    )
    return functools.partial(run, *after)


def exchange(value):
    return lax.all_to_all(value, "adapter", split_axis=0, concat_axis=0, tiled=True)


def towards(value, k, devices):
    return lax.ppermute(value, "adapter", [(i, i ^ k) for i in range(devices)])


def swapped(value):
    return lax.ppermute(value, "groups", [(0, 1), (1, 0)])


def stand_behind(value, *earlier):
    return pl.pallas_call(
        lambda *refs: None,
        out_shape=jax.ShapeDtypeStruct(value.shape, value.dtype),
        in_specs=[pl.BlockSpec(memory_space=pl.ANY)] * (1 + len(earlier)),
        out_specs=pl.BlockSpec(memory_space=pl.ANY),
        input_output_aliases={0: 0},
    )(value, *earlier)


def first_pack_call(cap, whole, devices, resident, adapter, used, tokens):
    blocks, rows, width = tokens.shape
    total = blocks * rows
    return call(
        functools.partial(first_pack_kernel, whole, cap, resident),
        [
            jax.ShapeDtypeStruct((devices, whole // LANES * cap + QUARTER, LANES), jnp.bfloat16),
            jax.ShapeDtypeStruct((1, total), jnp.int32),
            jax.ShapeDtypeStruct((total, 1), jnp.float32),
        ],
        [VMEM, VMEM, VMEM],
        2 * devices * cap * total * whole,
        2 * (total * width + devices * cap * whole),
        scratch=[pltpu.VMEM((total, width), jnp.bfloat16), pltpu.VMEM((8, LANES), jnp.int32)],
    )(adapter.reshape(1, blocks), used.reshape(1, blocks), tokens.reshape(total, width))


def pack_call(cap, base, whole, devices, target, label, tokens):
    blocks, rows, width = tokens.shape
    total = blocks * rows
    return call(
        functools.partial(pack_kernel, whole, cap, base),
        jax.ShapeDtypeStruct((devices, whole // LANES * cap + QUARTER, LANES), jnp.bfloat16),
        [VMEM, VMEM, VMEM, VMEM],
        2 * devices * cap * total * whole,
        2 * (total * width + devices * cap * whole),
        scratch=[pltpu.VMEM((total, width), jnp.bfloat16)],
    )(jnp.zeros((8, LANES), jnp.int32), target, label, tokens.reshape(total, width))


def down_call(cap, first, arrived, down_weights, after):
    devices = arrived.shape[0]
    columns, share = down_weights[0].shape
    return call(
        down_kernel,
        [
            jax.ShapeDtypeStruct((cap // STEP, HALF, devices * STEP), jnp.float32),
            jax.ShapeDtypeStruct((STEP, LANES), jnp.bfloat16),
            jax.ShapeDtypeStruct((devices * STEP, LANES), jnp.bfloat16),
            jax.ShapeDtypeStruct((8,), jnp.int32),
        ],
        [SMEM] + [VMEM] * (1 + len(down_weights)),
        0,
        0,
        after,
        [
            pltpu.VMEM((2, columns, share), jnp.bfloat16),
            pltpu.VMEM((devices * STEP, share), jnp.bfloat16),
            pltpu.VMEM((HALF, devices * STEP), jnp.float32),
            pltpu.VMEM((8, devices * STEP), jnp.float32),
        ],
        [VMEM, VMEM, VMEM, SMEM],
    )(first, arrived, *down_weights)


def quad_sums(partial, devices):
    pair = call(
        pair_kernel, jax.ShapeDtypeStruct(partial.shape, jnp.bfloat16), [VMEM, VMEM], 0, 0
    )(partial, towards(partial, 1, devices))
    return [pair, towards(pair, 2, devices)]


def up_call(kept, first, met, notes, sums, up_weights):
    devices = notes.shape[0] // STEP
    columns, share = up_weights[0].shape
    shape = (devices, (share // LANES - 1) * kept + QUARTER, LANES)
    return call(
        up_kernel,
        jax.ShapeDtypeStruct(shape, jnp.bfloat16),
        [SMEM, SMEM] + [VMEM] * (3 + len(up_weights)),
        2 * devices * kept * QUAD * columns * share,
        2 * (2 * devices * kept + QUAD * columns) * share,
        scratch=[
            pltpu.VMEM((2, columns, share), jnp.bfloat16),
            pltpu.VMEM((devices * STEP, share), jnp.float32),
            pltpu.VMEM((devices, QUARTER, LANES), jnp.float32),
            *[pltpu.VMEM((kept // STEP, devices * STEP, LANES), jnp.float32)] * 2,
        ],
    )(first, met, notes, *sums, *up_weights)


def back_and_mix(
    kept, more, tokens, target, label, first, met, notes, sums, down_weights, up_weights, *unused
):
    blocks, rows, width = tokens.shape
    total = blocks * rows
    devices = notes.shape[0] // STEP
    whole = up_weights[0].shape[1] - LANES
    pieces = [exchange(up_call(kept, first, met, notes, sums, up_weights))]
    if more:
        outgoing = pack_call(more, kept, whole, devices, target, label, tokens)
        arrived = exchange(outgoing)
        partial, unused_count, notes, met = down_call(more, first, arrived, down_weights, [])
        sums = quad_sums(partial, devices)
        pieces.append(exchange(up_call(more, first, met, notes, sums, up_weights)))
    mixed = call(
        functools.partial(mix_kernel, whole, (0, kept)[: len(pieces)]),
        jax.ShapeDtypeStruct((total, width), jnp.bfloat16),
        [VMEM] * (2 + len(pieces)),
        2 * devices * (kept + more) * total * whole,
        2 * (2 * total * width + devices * (kept + more) * whole),
    )(target.reshape(total, 1), tokens.reshape(total, width), *pieces)
    return mixed.reshape(tokens.shape)


def start_again(
    tokens, target, label, first, met, notes, sums, down_weights, up_weights, *arguments
):
    return rows_to_holders(tokens, *arguments)


def rows_to_quads(
    tokens, request_block_adapter, request_block_rows, adapter_down_weight, adapter_up_weight
):
    blocks, rows, width = tokens.shape
    devices = lax.axis_size("adapter")
    resident, rank, unused_width = adapter_up_weight.shape
    total = blocks * rows
    columns = resident * rank
    whole = width // LANES // QUAD * LANES
    share = whole + LANES
    bf16, i32 = jnp.bfloat16, jnp.int32

    me = lax.axis_index("adapter").astype(i32)
    group = lax.axis_index("groups").astype(i32)
    parts = jnp.bitwise_xor(me % QUAD, jnp.arange(QUAD, dtype=i32))
    halves = jnp.stack([group, 1 - group]) * (resident // 2)
    first = jnp.concatenate([parts * resident, halves]).astype(i32)
    tiles = whole // LANES

    def shares(weight, halved, after):
        shapes = []
        for k in range(QUAD):
            count = columns // 2 if k in halved else columns
            far = (count * tiles + count // QUAD, LANES)
            shapes.append(jax.ShapeDtypeStruct((columns, share) if k < 2 else far, bf16))
        values = call(
            functools.partial(weight_kernel, whole, range(QUAD), halved),
            shapes,
            [SMEM, SMEM, VMEM],
            0,
            QUAD * columns * width,
            after,
        )(parts, group.reshape(1), weight)
        return [values[0]] + [towards(values[k], k, devices) for k in range(1, QUAD)]

    weight = adapter_down_weight.transpose(0, 2, 1).reshape(columns, width)
    down_weights = shares(weight, DOWN_HALVED, [])
    weight = adapter_up_weight.reshape(columns, width)
    up_weights = shares(weight, UP_HALVED, down_weights[:1])
    down_weights[2] = stand_behind(down_weights[2], up_weights[0])
    down_weights += [swapped(down_weights[k]) for k in DOWN_HALVED]
    up_weights += [swapped(up_weights[k]) for k in UP_HALVED]

    caps = [total * 5 // 16, total * 6 // 16, total * 7 // 16]
    cap = caps[-1]
    outgoing, target, label = first_pack_call(
        cap, whole, devices, resident, request_block_adapter, request_block_rows, tokens
    )
    arrived = exchange(outgoing)
    partial, count, notes, met = down_call(cap, first, arrived, down_weights, up_weights[2:3])
    sums = quad_sums(partial, devices)
    count = count[0:1, 0:1]
    most = jnp.maximum(count, swapped(count))[0, 0].astype(jnp.float32)
    branches = [functools.partial(back_and_mix, kept, 0) for kept in caps]
    branches += [functools.partial(back_and_mix, cap, STEP), start_again]
    return lax.switch(
        sum((most > limit).astype(i32) for limit in [*caps, cap + STEP]),
        branches,
        tokens,
        target,
        label,
        first,
        met,
        notes,
        sums,
        down_weights,
        up_weights,
        request_block_adapter,
        request_block_rows,
        adapter_down_weight,
        adapter_up_weight,
    )


def solution(mesh):
    placed = (
        P(("groups", "adapter"), None, None),
        P(("groups", "adapter")),
        P(("groups", "adapter")),
        P("adapter", None, None),
        P("adapter", None, None),
    )

    def per_device(tokens, request_block_adapter, request_block_rows, down_weight, up_weight):
        blocks, rows, width = tokens.shape
        devices = mesh.shape["adapter"]
        slots = max(1, 4 * blocks // devices)
        quads = devices % QUAD == 0 and slots * QUAD >= blocks
        quads = quads and width % (QUAD * LANES) == LANES and up_weight.shape[1] == HALF
        quads = quads and blocks * rows * 7 // 16 == 7 * STEP and mesh.shape["groups"] == 2
        plan = rows_to_quads if quads else rows_to_holders
        return plan(tokens, request_block_adapter, request_block_rows, down_weight, up_weight)

    return jax.shard_map(
        per_device,
        mesh=mesh,
        in_specs=placed,
        out_specs=P(("groups", "adapter"), None, None),
        check_vma=False,
    )
```

```python
import functools

import jax
import jax.numpy as jnp
from jax import lax
from jax.experimental import pallas as pl
from jax.experimental.pallas import tpu as pltpu
from jax.sharding import PartitionSpec as P

LANES = 128
HALF = 64
QUAD = 4
QUARTER = 32
STEP = 16
NOTE = 96
DOWN_HALVED = (2, 3)
UP_HALVED = (2,)
VMEM = pl.BlockSpec(memory_space=pltpu.VMEM)
SMEM = pl.BlockSpec(memory_space=pltpu.SMEM)


def normalise(tokens):
    values = tokens.astype(jnp.float32)
    mean_sq = jnp.mean(values * values, axis=-1, keepdims=True)
    return (values, (values * lax.rsqrt(mean_sq + 1e-06)).astype(jnp.bfloat16))


def resident_update(hidden_state, block_labels, adapter_down_weight, adapter_up_weight):
    feature_width = hidden_state.shape[-1]
    leading = hidden_state.shape[:-1]
    resident_rows, unused_value, inner_rank = adapter_down_weight.shape
    flattened_tokens = hidden_state.reshape(-1, feature_width)
    down_matrix = jnp.einsum(
        "tq,iqg->tig", flattened_tokens, adapter_down_weight, preferred_element_type=jnp.float32
    )
    down_matrix = down_matrix.astype(jnp.bfloat16).reshape(
        flattened_tokens.shape[0], resident_rows * inner_rank
    )
    column_owner = jnp.arange(resident_rows * inner_rank, dtype=jnp.int32) // inner_rank
    picked = block_labels.reshape(-1, 1) == column_owner[None, :]
    down_matrix = jnp.where(picked, down_matrix, jnp.zeros_like(down_matrix))
    lowrank_update = jnp.dot(
        down_matrix,
        adapter_up_weight.reshape(resident_rows * inner_rank, feature_width),
        preferred_element_type=jnp.float32,
    )
    return lowrank_update.astype(jnp.bfloat16).reshape(leading + (feature_width,))


def rows_to_holders(
    tokens, request_block_adapter, request_block_rows, adapter_down_weight, adapter_up_weight
):
    blocks, rows, feature_width = tokens.shape
    devices = lax.axis_size("adapter")
    resident_rows = adapter_down_weight.shape[0]
    slots = max(1, 4 * blocks // devices)
    values, normed = normalise(tokens)
    owner = request_block_adapter // resident_rows
    within = request_block_adapter - owner * resident_rows
    serial = jnp.arange(blocks, dtype=jnp.int32)
    earlier = (owner[:, None] == owner[None, :]) & (serial[None, :] < serial[:, None])
    position = owner * slots + jnp.sum(earlier, axis=1)
    outgoing = (
        jnp.zeros((devices * slots, rows, feature_width), jnp.bfloat16).at[position].set(normed)
    )
    outgoing = outgoing.reshape(devices, slots, rows, feature_width)
    block_labels = jnp.full((devices * slots,), -1, jnp.int32).at[position].set(within)
    block_labels = jnp.broadcast_to(block_labels[:, None], (devices * slots, rows)).reshape(
        devices, slots, rows
    )
    arriving_rows, row_markers = (
        lax.all_to_all(outgoing, "adapter", split_axis=0, concat_axis=0, tiled=True),
        lax.all_to_all(block_labels, "adapter", split_axis=0, concat_axis=0, tiled=True),
    )
    lowrank_update = resident_update(
        arriving_rows, row_markers, adapter_down_weight, adapter_up_weight
    )
    returned = lax.all_to_all(lowrank_update, "adapter", split_axis=0, concat_axis=0, tiled=True)
    mine = returned.reshape(devices * slots, rows, feature_width)[position]
    live = jnp.arange(rows, dtype=jnp.int32)[None, :] < request_block_rows[:, None]
    mixed = values + jnp.where(live[:, :, None], mine.astype(jnp.float32), jnp.float32(0.0))
    return mixed.astype(jnp.bfloat16)


def lanes_of(rows):
    return lax.broadcasted_iota(jnp.int32, (rows, LANES), 1)


def weight_kernel(whole, which, halved, part_ref, group_ref, weight_ref, *out_refs):
    tiles = whole // LANES
    for k, out_ref in zip(which, out_refs):
        j = part_ref[k]
        if k < 2:
            last = weight_ref[:, QUAD * whole :].astype(jnp.float32)
            turned = pltpu.roll(last, lax.rem(LANES - QUARTER * j, LANES), 1)
            inside = lanes_of(last.shape[0]) < QUARTER
            out_ref[:, 0:whole] = weight_ref[:, pl.ds(pl.multiple_of(j * whole, LANES), whole)]
            out_ref[:, whole:] = jnp.where(inside, turned, 0.0).astype(jnp.bfloat16)
            continue
        count = weight_ref.shape[0] // 2 if k in halved else weight_ref.shape[0]
        start = pl.multiple_of(group_ref[0] * count, count) if k in halved else 0
        for t in range(tiles):
            column = pl.multiple_of(j * whole + t * LANES, LANES)
            out_ref[t * count : (t + 1) * count, :] = weight_ref[
                pl.ds(start, count), pl.ds(column, LANES)
            ]
        last = weight_ref[pl.ds(start, count), QUAD * whole :].astype(jnp.float32)
        size = count // QUAD
        owner = lanes_of(size) // QUARTER
        merged = jnp.zeros((size, LANES), jnp.float32)
        for m in range(QUAD):
            shift = lax.rem(LANES + QUARTER * (m - j), LANES)
            turned = pltpu.roll(last[m * size : (m + 1) * size], shift, 1)
            merged = jnp.where(owner == m, turned, merged)
        out_ref[tiles * count :, :] = merged.astype(jnp.bfloat16)


def open_far(far_refs, halved, opened_ref):
    width = opened_ref.shape[2]
    tiles = width // LANES - 1
    places = [(k - 2, 0) for k in (2, 3)] + [(k - 2, 1) for k in halved]
    for ref, (holder, part) in zip(far_refs, places):
        count = opened_ref.shape[1] // 2 if holder + 2 in halved else opened_ref.shape[1]
        base, size = part * count, count // QUAD
        inside = lanes_of(size) < QUARTER
        for t in range(tiles):
            opened_ref[holder, base : base + count, t * LANES : (t + 1) * LANES] = ref[
                t * count : (t + 1) * count, :
            ]
        packed = ref[tiles * count :, :].astype(jnp.float32)
        for m in range(QUAD):
            turned = pltpu.roll(packed, (LANES - QUARTER * m) % LANES, 1) if m else packed
            opened_ref[holder, base + m * size : base + (m + 1) * size, tiles * LANES :] = (
                jnp.where(inside, turned, 0.0).astype(jnp.bfloat16)
            )


def lay_out(resident, adapter_ref, used_ref, most_ref, target_ref, label_ref):
    blocks, total = adapter_ref.shape[1], target_ref.shape[1]
    rows = total // blocks
    adapter, used = adapter_ref[...], used_ref[...]
    down = lax.broadcasted_iota(jnp.int32, (blocks, blocks), 0)
    across = lax.broadcasted_iota(jnp.int32, (blocks, blocks), 1)

    def turned(value):
        return jnp.sum(jnp.where(down == across, value, 0), axis=1, keepdims=True)

    span = resident * QUAD
    quad = jnp.floor((adapter.astype(jnp.float32) + 0.5) * (1.0 / span)).astype(jnp.int32)
    order = adapter * blocks + lax.broadcasted_iota(jnp.int32, (1, blocks), 1)
    quad_down, order_down, used_down = turned(quad), turned(order), turned(used)
    same = quad_down == quad
    ahead = jnp.sum(jnp.where(same & (order < order_down), used, 0), axis=1, keepdims=True)
    within = jnp.sum(jnp.where(same, used, 0), axis=1, keepdims=True)
    most_ref[...] = jnp.broadcast_to(jnp.max(within, axis=0, keepdims=True), most_ref.shape)
    start = quad_down * total + ahead

    block = lax.broadcasted_iota(jnp.int32, (blocks, total), 0)
    row = lax.broadcasted_iota(jnp.int32, (blocks, total), 1) - block * rows
    place = jnp.where((row >= 0) & (row < used_down), start + row + 1, 0)
    target_ref[...] = jnp.sum(place, axis=0, keepdims=True) - 1
    block = lax.broadcasted_iota(jnp.int32, (total, blocks), 1)
    row = lax.broadcasted_iota(jnp.int32, (total, blocks), 0) - block * rows
    label = jnp.where((row >= 0) & (row < rows), adapter - quad * span + 1, 0)
    label_ref[...] = jnp.sum(label.astype(jnp.float32), axis=1, keepdims=True)


def first_pack_kernel(
    whole, cap, resident, adapter_ref, used_ref, tokens_ref, out_ref, target_ref, label_ref, *refs
):
    normed_ref, most_ref = refs
    lay_out(resident, adapter_ref, used_ref, most_ref, target_ref, label_ref)
    pack_kernel(
        whole, cap, 0, most_ref, target_ref, label_ref, tokens_ref, out_ref, normed_ref
    )


def pack_kernel(
    whole, cap, base, most_ref, target_ref, label_ref, tokens_ref, out_ref, normed_ref
):
    values = tokens_ref[...].astype(jnp.float32)
    mean_sq = jnp.mean(values * values, axis=-1, keepdims=True)
    normed_ref[...] = (values * lax.rsqrt(mean_sq + 1e-06)).astype(jnp.bfloat16)
    total = tokens_ref.shape[0]
    quads, tiles = out_ref.shape[0] // QUAD, whole // LANES
    lane = lanes_of(total)
    last = normed_ref[:, QUAD * whole :].astype(jnp.float32)
    label = jnp.where(lane == QUARTER, label_ref[...], 0.0)
    ends = []
    for j in range(QUAD):
        turned = pltpu.roll(last, (LANES - QUARTER * j) % LANES, 1) if j else last
        ends.append(jnp.where(lane < QUARTER, turned, label).astype(jnp.bfloat16))
    most = most_ref[0:1, 0:1].astype(jnp.float32)
    group_lane = lanes_of(QUARTER) // QUARTER
    step_lane = lanes_of(STEP)
    chosen = []
    for q in range(quads):
        place = lax.broadcasted_iota(jnp.int32, (cap, total), 0) + (q * total + base)
        chosen.append(jnp.where(target_ref[...] == place, 1.0, 0.0).astype(jnp.bfloat16))
    chosen = jnp.concatenate(chosen, axis=0)
    notes = [jnp.where(step_lane == NOTE + cap // STEP, most, 0.0)] * quads
    for j in range(QUAD):
        for t in range(tiles):
            column = j * whole + t * LANES
            if t % 2 == 0:
                count = min(2, tiles - t) * LANES
                share = jnp.dot(
                    chosen,
                    normed_ref[:, column : column + count],
                    preferred_element_type=jnp.float32,
                ).astype(jnp.bfloat16)
            for q in range(quads):
                out_ref[q * QUAD + j, t * cap : (t + 1) * cap, :] = share[
                    q * cap : (q + 1) * cap, t % 2 * LANES : (t % 2 + 1) * LANES
                ]
        end_rows = jnp.dot(chosen, ends[j], preferred_element_type=jnp.float32)
        for q in range(quads):
            end = end_rows[q * cap : (q + 1) * cap]
            if j == 0:
                for a in range(cap // STEP):
                    turned = pltpu.roll(end[a * STEP : (a + 1) * STEP], NOTE + a - QUARTER, 1)
                    notes[q] = jnp.where(step_lane == NOTE + a, turned, notes[q])
            padded = jnp.concatenate(
                [end, jnp.zeros((QUAD * QUARTER - cap, LANES), jnp.float32)], axis=0
            )
            merged = padded[0:QUARTER]
            for m in range(1, QUAD):
                turned = pltpu.roll(padded[m * QUARTER : (m + 1) * QUARTER], m * QUARTER, 1)
                merged = jnp.where(group_lane == m, turned, merged)
            out_ref[q * QUAD + j, tiles * cap : tiles * cap + STEP, :] = merged[0:STEP].astype(
                jnp.bfloat16
            )
            out_ref[q * QUAD + j, tiles * cap + STEP :, :] = jnp.where(
                step_lane >= NOTE, notes[q], merged[STEP:]
            ).astype(jnp.bfloat16)


def read_notes(rows_ref, cap, tiles, part_ref, resident, notes_ref, labels_ref, met_ref):
    senders = rows_ref.shape[0]
    for s in range(senders):
        notes_ref[s * STEP : (s + 1) * STEP, :] = rows_ref[s, tiles * cap + STEP :, :]
    steps = labels_ref.shape[0]
    row = lax.broadcasted_iota(jnp.int32, (steps, LANES), 0)
    wanted = jnp.where(lanes_of(steps) == NOTE + row, 1.0, 0.0).astype(jnp.bfloat16)
    labels = lax.dot_general(
        wanted, notes_ref[...], (((1,), (1,)), ((), ())), preferred_element_type=jnp.float32
    )
    labels_ref[...] = labels
    code = jnp.zeros((steps, 1), jnp.float32)
    for h in range(QUAD):
        first = part_ref[h].astype(jnp.float32) + 1.0
        met = jnp.where((labels >= first) & (labels < first + resident), 1.0, 0.0)
        code = code + (1 << h) * jnp.max(met, axis=1, keepdims=True)
    at = lax.broadcasted_iota(jnp.int32, (steps, 1), 0)
    for a in range(cap // STEP):
        met_ref[a] = jnp.max(jnp.where(at == a, code, 0.0)).astype(jnp.int32)


def for_holders(met_ref, first_ref, near_refs, opened_ref, halved, a, step):
    pairs = opened_ref.shape[1] // LANES
    for h in range(QUAD):
        base = first_ref[h].astype(jnp.float32) + 1.0
        firsts = [base + 2.0 * t for t in range(pairs)]
        if h in halved:
            firsts = [
                base + first_ref[QUAD + i].astype(jnp.float32) + 2.0 * t
                for i in range(2)
                for t in range(pairs // 2)
            ]

        @pl.when(lax.rem(met_ref[a] // (1 << h), 2) > 0)
        def _(h=h, firsts=firsts):
            step(near_refs[h] if h < 2 else opened_ref.at[h - 2], firsts)


def down_kernel(first_ref, rows_ref, *refs):
    near_refs, far_refs, out_ref, count_ref = refs[:2], refs[2:6], refs[6], refs[7]
    notes_ref, met_ref, opened_ref, batch_ref, picked_ref, labels_ref = refs[8:]
    senders, width = rows_ref.shape[0], batch_ref.shape[1]
    tiles = width // LANES - 1
    cap = out_ref.shape[0] * STEP
    rank = out_ref.shape[1]
    resident = opened_ref.shape[1] // rank
    dims = (((1,), (1,)), ((), ()))
    read_notes(rows_ref, cap, tiles, first_ref, resident, notes_ref, labels_ref, met_ref)
    notes = notes_ref[...].astype(jnp.float32)
    is_count = lanes_of(senders * STEP) == NOTE + cap // STEP
    count = jnp.max(jnp.where(is_count, notes, 0.0), axis=(0, 1), keepdims=True)
    count_ref[...] = jnp.broadcast_to(count, count_ref.shape).astype(jnp.bfloat16)
    open_far(far_refs, DOWN_HALVED, opened_ref)

    def one(a, carry):
        picked_ref[...] = jnp.zeros(picked_ref.shape, jnp.float32)

        @pl.when(met_ref[a] > 0)
        def _():
            shift = lax.rem(LANES - QUARTER * (a // 2), LANES)
            spot = pl.multiple_of(tiles * cap + lax.rem(a, 2) * STEP, STEP)
            for s in range(senders):
                rows = slice(s * STEP, (s + 1) * STEP)
                for t in range(tiles):
                    at = pl.multiple_of(t * cap + a * STEP, STEP)
                    batch_ref[rows, t * LANES : (t + 1) * LANES] = rows_ref[s, pl.ds(at, STEP), :]
                end = rows_ref[s, pl.ds(spot, STEP), :].astype(jnp.float32)
                batch_ref[rows, tiles * LANES :] = pltpu.roll(end, shift, 1).astype(jnp.bfloat16)
            label = labels_ref[pl.ds(a, 1), :]

            def step(weight_ref, firsts):
                product = lax.dot_general(
                    weight_ref[...], batch_ref[...], dims, preferred_element_type=jnp.float32
                )
                picked = picked_ref[...]
                for t, first in enumerate(firsts):
                    for i in range(2):
                        at = (2 * t + i) * rank
                        picked = jnp.where(
                            label == first + i, product[at : at + rank, :], picked
                        )
                picked_ref[...] = picked

            for_holders(met_ref, first_ref, near_refs, opened_ref, DOWN_HALVED, a, step)

        out_ref[a] = picked_ref[...]
        return carry

    lax.fori_loop(0, cap // STEP, one, 0)


def pair_kernel(own_ref, other_ref, out_ref):
    out_ref[...] = (own_ref[...] + other_ref[...]).astype(jnp.bfloat16)


def up_kernel(first_ref, met_ref, notes_ref, *refs):
    sum_refs, near_refs, far_refs, out_ref = refs[:2], refs[2:4], refs[4:7], refs[7]
    opened_ref, delta_ref, ends_ref, label_ref, twice_ref = refs[8:]
    senders, width = out_ref.shape[0], opened_ref.shape[2]
    tiles = width // LANES - 1
    rank = sum_refs[0].shape[1]
    kept = (out_ref.shape[1] - QUARTER) // tiles
    full = kept // STEP * STEP
    group_lane = lanes_of(STEP) // QUARTER
    open_far(far_refs, UP_HALVED, opened_ref)
    ends_ref[...] = jnp.zeros(ends_ref.shape, jnp.float32)
    low = jnp.where(lanes_of(senders * STEP) < HALF, 0.0, 1.0)
    rank_row = lax.broadcasted_iota(jnp.int32, (rank, LANES), 0)
    twofold = jnp.where(lax.rem(lanes_of(rank), rank) == rank_row, 1.0, 0.0).astype(jnp.bfloat16)

    note_row = lax.broadcasted_iota(jnp.int32, (LANES, LANES), 0)
    for a in range(label_ref.shape[0]):
        wanted = jnp.where(note_row == NOTE + a, 1.0, 0.0).astype(jnp.bfloat16)
        label_ref[a] = jnp.dot(notes_ref[...], wanted, preferred_element_type=jnp.float32) - low
        down = sum_refs[0][a].astype(jnp.float32) + sum_refs[1][a].astype(jnp.float32)
        twice_ref[a] = lax.dot_general(
            down.astype(jnp.bfloat16),
            twofold,
            (((0,), (0,)), ((), ())),
            preferred_element_type=jnp.float32,
        )

    def one(a):
        delta_ref[...] = jnp.zeros(delta_ref.shape, jnp.float32)

        @pl.when(met_ref[a] > 0)
        def _():
            label, twice = label_ref[a], twice_ref[a]

            def step(weight_ref, firsts):
                placed = [jnp.where(label == first, twice, 0.0) for first in firsts]
                placed = jnp.concatenate(placed, axis=1).astype(jnp.bfloat16)
                delta_ref[...] += jnp.dot(
                    placed, weight_ref[...], preferred_element_type=jnp.float32
                )

            for_holders(met_ref, first_ref, near_refs, opened_ref, UP_HALVED, a, step)

        spot = pl.multiple_of(lax.rem(a, 2) * STEP, STEP)
        for s in range(senders):
            rows = slice(s * STEP, (s + 1) * STEP)
            turned = pltpu.roll(delta_ref[rows, tiles * LANES :], QUARTER * (a // 2), 1)
            ends_ref[s, pl.ds(spot, STEP), :] = jnp.where(
                group_lane == a // 2, turned, ends_ref[s, pl.ds(spot, STEP), :]
            )

    def whole_step(a, carry):
        one(a)
        for s in range(senders):
            rows = slice(s * STEP, (s + 1) * STEP)
            for t in range(tiles):
                at = pl.multiple_of(t * full + a * STEP, STEP)
                out_ref[s, pl.ds(at, STEP), :] = delta_ref[
                    rows, t * LANES : (t + 1) * LANES
                ].astype(jnp.bfloat16)
        return carry

    lax.fori_loop(0, full // STEP, whole_step, 0)
    if kept > full:
        one(jnp.int32(full // STEP))
        for s in range(senders):
            rows = slice(s * STEP, s * STEP + STEP // 2)
            for t in range(0, tiles, 2):
                both = [
                    delta_ref[rows, (t + i) * LANES : (t + i + 1) * LANES] for i in range(2)
                ]
                at = tiles * full + t * (STEP // 2)
                out_ref[s, at : at + STEP, :] = jnp.concatenate(both, axis=0).astype(jnp.bfloat16)
    for s in range(senders):
        out_ref[s, tiles * kept :, :] = ends_ref[s].astype(jnp.bfloat16)


def mix_kernel(whole, bases, target_ref, tokens_ref, *refs):
    returned_refs, out_ref = refs[:-1], refs[-1]
    total = tokens_ref.shape[0]
    tiles, quads = whole // LANES, returned_refs[0].shape[0] // QUAD
    lane = lanes_of(total)
    chosen = []
    for base, ref in zip(bases, returned_refs):
        kept = (ref.shape[1] - QUARTER) // tiles
        full = kept // STEP * STEP
        spot = lax.broadcasted_iota(jnp.int32, (total, quads * kept), 1)
        place = spot // full * total + spot % full
        if kept > full:
            later = spot - quads * full
            half_place = later // (STEP // 2) * total + later % (STEP // 2) + full
            place = jnp.where(later >= 0, half_place, place)
        place = place + base
        chosen.append(jnp.where(target_ref[...] == place, 1.0, 0.0).astype(jnp.bfloat16))
    end = jnp.zeros((total, LANES), jnp.float32)
    for j in range(QUAD):
        delta = 0.0
        for choice, ref in zip(chosen, returned_refs):
            kept = choice.shape[1] // quads
            full = kept // STEP * STEP
            shares, halves = [], []
            for q in range(quads):
                d = q * QUAD + j
                parts = [ref[d, t * full : (t + 1) * full, :] for t in range(tiles)]
                packed = ref[d, tiles * kept :, :].astype(jnp.float32)
                groups = [packed]
                for m in range(1, QUAD):
                    groups.append(pltpu.roll(packed, LANES - QUARTER * m, 1))
                ends = jnp.concatenate(groups, axis=0)
                parts.append(ends[0:full].astype(jnp.bfloat16))
                shares.append(jnp.concatenate(parts, axis=1))
                if kept > full:
                    pairs = ref[d, tiles * full : tiles * kept, :].astype(jnp.float32)
                    parts = [pairs[t * (STEP // 2) : (t + 1) * (STEP // 2)] for t in range(tiles)]
                    halves.append(jnp.concatenate([*parts, ends[full:kept]], axis=1))
            if halves:
                shares.append(jnp.concatenate(halves, axis=0).astype(jnp.bfloat16))
            share = jnp.concatenate(shares, axis=0)
            delta = delta + jnp.dot(choice, share, preferred_element_type=jnp.float32)
        columns = slice(j * whole, (j + 1) * whole)
        out_ref[:, columns] = (
            tokens_ref[:, columns].astype(jnp.float32) + delta[:, 0:whole]
        ).astype(jnp.bfloat16)
        last = delta[:, whole:]
        turned = pltpu.roll(last, QUARTER * j, 1) if j else last
        end = jnp.where((lane >= QUARTER * j) & (lane < QUARTER * (j + 1)), turned, end)
    out_ref[:, QUAD * whole :] = (
        tokens_ref[:, QUAD * whole :].astype(jnp.float32) + end
    ).astype(jnp.bfloat16)


def call(kernel, out_shape, in_specs, flops, moved, after=(), scratch=(), out_specs=None):
    many = isinstance(out_shape, list)
    skipped = len(after)
    body = (lambda *refs: kernel(*refs[skipped:])) if skipped else kernel
    run = pl.pallas_call(
        body,
        out_shape=out_shape,
        in_specs=[pl.BlockSpec(memory_space=pl.ANY)] * skipped + in_specs,
        out_specs=out_specs or ([VMEM] * len(out_shape) if many else VMEM),
        scratch_shapes=scratch,
        compiler_params=pltpu.CompilerParams(vmem_limit_bytes=48 * 2**20),
        cost_estimate=pl.CostEstimate(flops=flops, bytes_accessed=moved, transcendentals=0),
    )
    return functools.partial(run, *after)


def exchange(value):
    return lax.all_to_all(value, "adapter", split_axis=0, concat_axis=0, tiled=True)


def towards(value, k, devices):
    return lax.ppermute(value, "adapter", [(i, i ^ k) for i in range(devices)])


def swapped(value):
    return lax.ppermute(value, "groups", [(0, 1), (1, 0)])


def stand_behind(value, *earlier):
    return pl.pallas_call(
        lambda *refs: None,
        out_shape=jax.ShapeDtypeStruct(value.shape, value.dtype),
        in_specs=[pl.BlockSpec(memory_space=pl.ANY)] * (1 + len(earlier)),
        out_specs=pl.BlockSpec(memory_space=pl.ANY),
        input_output_aliases={0: 0},
    )(value, *earlier)


def first_pack_call(cap, whole, devices, resident, adapter, used, tokens):
    blocks, rows, width = tokens.shape
    total = blocks * rows
    return call(
        functools.partial(first_pack_kernel, whole, cap, resident),
        [
            jax.ShapeDtypeStruct((devices, whole // LANES * cap + QUARTER, LANES), jnp.bfloat16),
            jax.ShapeDtypeStruct((1, total), jnp.int32),
            jax.ShapeDtypeStruct((total, 1), jnp.float32),
        ],
        [VMEM, VMEM, VMEM],
        2 * devices * cap * total * whole,
        2 * (total * width + devices * cap * whole),
        scratch=[pltpu.VMEM((total, width), jnp.bfloat16), pltpu.VMEM((8, LANES), jnp.int32)],
    )(adapter.reshape(1, blocks), used.reshape(1, blocks), tokens.reshape(total, width))


def pack_call(cap, base, whole, devices, target, label, tokens):
    blocks, rows, width = tokens.shape
    total = blocks * rows
    return call(
        functools.partial(pack_kernel, whole, cap, base),
        jax.ShapeDtypeStruct((devices, whole // LANES * cap + QUARTER, LANES), jnp.bfloat16),
        [VMEM, VMEM, VMEM, VMEM],
        2 * devices * cap * total * whole,
        2 * (total * width + devices * cap * whole),
        scratch=[pltpu.VMEM((total, width), jnp.bfloat16)],
    )(jnp.zeros((8, LANES), jnp.int32), target, label, tokens.reshape(total, width))


def down_call(cap, first, arrived, down_weights, after):
    devices = arrived.shape[0]
    columns, share = down_weights[0].shape
    return call(
        down_kernel,
        [
            jax.ShapeDtypeStruct((cap // STEP, HALF, devices * STEP), jnp.float32),
            jax.ShapeDtypeStruct((STEP, LANES), jnp.bfloat16),
            jax.ShapeDtypeStruct((devices * STEP, LANES), jnp.bfloat16),
            jax.ShapeDtypeStruct((8,), jnp.int32),
        ],
        [SMEM] + [VMEM] * (1 + len(down_weights)),
        0,
        0,
        after,
        [
            pltpu.VMEM((2, columns, share), jnp.bfloat16),
            pltpu.VMEM((devices * STEP, share), jnp.bfloat16),
            pltpu.VMEM((HALF, devices * STEP), jnp.float32),
            pltpu.VMEM((8, devices * STEP), jnp.float32),
        ],
        [VMEM, VMEM, VMEM, SMEM],
    )(first, arrived, *down_weights)


def quad_sums(partial, devices):
    pair = call(
        pair_kernel, jax.ShapeDtypeStruct(partial.shape, jnp.bfloat16), [VMEM, VMEM], 0, 0
    )(partial, towards(partial, 1, devices))
    return [pair, towards(pair, 2, devices)]


def up_call(kept, first, met, notes, sums, up_weights):
    devices = notes.shape[0] // STEP
    columns, share = up_weights[0].shape
    shape = (devices, (share // LANES - 1) * kept + QUARTER, LANES)
    return call(
        up_kernel,
        jax.ShapeDtypeStruct(shape, jnp.bfloat16),
        [SMEM, SMEM] + [VMEM] * (3 + len(up_weights)),
        2 * devices * kept * QUAD * columns * share,
        2 * (2 * devices * kept + QUAD * columns) * share,
        scratch=[
            pltpu.VMEM((2, columns, share), jnp.bfloat16),
            pltpu.VMEM((devices * STEP, share), jnp.float32),
            pltpu.VMEM((devices, QUARTER, LANES), jnp.float32),
            *[pltpu.VMEM((-(-kept // STEP), devices * STEP, LANES), jnp.float32)] * 2,
        ],
    )(first, met, notes, *sums, *up_weights)


def back_and_mix(
    kept, more, tokens, target, label, first, met, notes, sums, down_weights, up_weights, *unused
):
    blocks, rows, width = tokens.shape
    total = blocks * rows
    devices = notes.shape[0] // STEP
    whole = up_weights[0].shape[1] - LANES
    pieces = [exchange(up_call(kept, first, met, notes, sums, up_weights))]
    if more:
        outgoing = pack_call(more, kept, whole, devices, target, label, tokens)
        arrived = exchange(outgoing)
        partial, unused_count, notes, met = down_call(more, first, arrived, down_weights, [])
        sums = quad_sums(partial, devices)
        pieces.append(exchange(up_call(more, first, met, notes, sums, up_weights)))
    mixed = call(
        functools.partial(mix_kernel, whole, (0, kept)[: len(pieces)]),
        jax.ShapeDtypeStruct((total, width), jnp.bfloat16),
        [VMEM] * (2 + len(pieces)),
        2 * devices * (kept + more) * total * whole,
        2 * (2 * total * width + devices * (kept + more) * whole),
    )(target.reshape(total, 1), tokens.reshape(total, width), *pieces)
    return mixed.reshape(tokens.shape)


def start_again(
    tokens, target, label, first, met, notes, sums, down_weights, up_weights, *arguments
):
    return rows_to_holders(tokens, *arguments)


def rows_to_quads(
    tokens, request_block_adapter, request_block_rows, adapter_down_weight, adapter_up_weight
):
    blocks, rows, width = tokens.shape
    devices = lax.axis_size("adapter")
    resident, rank, unused_width = adapter_up_weight.shape
    total = blocks * rows
    columns = resident * rank
    whole = width // LANES // QUAD * LANES
    share = whole + LANES
    bf16, i32 = jnp.bfloat16, jnp.int32

    me = lax.axis_index("adapter").astype(i32)
    group = lax.axis_index("groups").astype(i32)
    parts = jnp.bitwise_xor(me % QUAD, jnp.arange(QUAD, dtype=i32))
    halves = jnp.stack([group, 1 - group]) * (resident // 2)
    first = jnp.concatenate([parts * resident, halves]).astype(i32)
    tiles = whole // LANES

    def shares(weight, halved, after):
        shapes = []
        for k in range(QUAD):
            count = columns // 2 if k in halved else columns
            far = (count * tiles + count // QUAD, LANES)
            shapes.append(jax.ShapeDtypeStruct((columns, share) if k < 2 else far, bf16))
        values = call(
            functools.partial(weight_kernel, whole, range(QUAD), halved),
            shapes,
            [SMEM, SMEM, VMEM],
            0,
            QUAD * columns * width,
            after,
        )(parts, group.reshape(1), weight)
        return [values[0]] + [towards(values[k], k, devices) for k in range(1, QUAD)]

    weight = adapter_down_weight.transpose(0, 2, 1).reshape(columns, width)
    down_weights = shares(weight, DOWN_HALVED, [])
    weight = adapter_up_weight.reshape(columns, width)
    up_weights = shares(weight, UP_HALVED, down_weights[:1])
    down_weights[2] = stand_behind(down_weights[2], up_weights[0])
    down_weights += [swapped(down_weights[k]) for k in DOWN_HALVED]
    up_weights += [swapped(up_weights[k]) for k in UP_HALVED]

    caps = [total * parts_of // 32 for parts_of in range(9, 15)]
    cap = caps[-1]
    outgoing, target, label = first_pack_call(
        cap, whole, devices, resident, request_block_adapter, request_block_rows, tokens
    )
    arrived = exchange(outgoing)
    partial, count, notes, met = down_call(cap, first, arrived, down_weights, up_weights[2:3])
    sums = quad_sums(partial, devices)
    count = count[0:1, 0:1]
    most = jnp.maximum(count, swapped(count))[0, 0].astype(jnp.float32)
    branches = [functools.partial(back_and_mix, kept, 0) for kept in caps]
    branches += [functools.partial(back_and_mix, cap, STEP), start_again]
    return lax.switch(
        sum((most > limit).astype(i32) for limit in [*caps, cap + STEP]),
        branches,
        tokens,
        target,
        label,
        first,
        met,
        notes,
        sums,
        down_weights,
        up_weights,
        request_block_adapter,
        request_block_rows,
        adapter_down_weight,
        adapter_up_weight,
    )


def solution(mesh):
    placed = (
        P(("groups", "adapter"), None, None),
        P(("groups", "adapter")),
        P(("groups", "adapter")),
        P("adapter", None, None),
        P("adapter", None, None),
    )

    def per_device(tokens, request_block_adapter, request_block_rows, down_weight, up_weight):
        blocks, rows, width = tokens.shape
        devices = mesh.shape["adapter"]
        slots = max(1, 4 * blocks // devices)
        quads = devices % QUAD == 0 and slots * QUAD >= blocks
        quads = quads and width % (QUAD * LANES) == LANES and up_weight.shape[1] == HALF
        quads = quads and blocks * rows * 7 // 16 == 7 * STEP and mesh.shape["groups"] == 2
        plan = rows_to_quads if quads else rows_to_holders
        return plan(tokens, request_block_adapter, request_block_rows, down_weight, up_weight)

    return jax.shard_map(
        per_device,
        mesh=mesh,
        in_specs=placed,
        out_specs=P(("groups", "adapter"), None, None),
        check_vma=False,
    )
```

```python
import functools

import jax
import jax.numpy as jnp
from jax import lax
from jax.experimental import pallas as pl
from jax.experimental.pallas import tpu as pltpu
from jax.sharding import PartitionSpec as P

LANES = 128
HALF = 64
QUAD = 4
QUARTER = 32
STEP = 16
NOTE = 96
VMEM = pl.BlockSpec(memory_space=pltpu.VMEM)
SMEM = pl.BlockSpec(memory_space=pltpu.SMEM)


def normalise(tokens):
    values = tokens.astype(jnp.float32)
    mean_sq = jnp.mean(values * values, axis=-1, keepdims=True)
    return (values, (values * lax.rsqrt(mean_sq + 1e-06)).astype(jnp.bfloat16))


def resident_update(hidden_state, block_labels, adapter_down_weight, adapter_up_weight):
    feature_width = hidden_state.shape[-1]
    leading = hidden_state.shape[:-1]
    resident_rows, unused_value, inner_rank = adapter_down_weight.shape
    flattened_tokens = hidden_state.reshape(-1, feature_width)
    down_matrix = jnp.einsum(
        "tq,iqg->tig", flattened_tokens, adapter_down_weight, preferred_element_type=jnp.float32
    )
    down_matrix = down_matrix.astype(jnp.bfloat16).reshape(
        flattened_tokens.shape[0], resident_rows * inner_rank
    )
    column_owner = jnp.arange(resident_rows * inner_rank, dtype=jnp.int32) // inner_rank
    picked = block_labels.reshape(-1, 1) == column_owner[None, :]
    down_matrix = jnp.where(picked, down_matrix, jnp.zeros_like(down_matrix))
    lowrank_update = jnp.dot(
        down_matrix,
        adapter_up_weight.reshape(resident_rows * inner_rank, feature_width),
        preferred_element_type=jnp.float32,
    )
    return lowrank_update.astype(jnp.bfloat16).reshape(leading + (feature_width,))


def rows_to_holders(
    tokens, request_block_adapter, request_block_rows, adapter_down_weight, adapter_up_weight
):
    blocks, rows, feature_width = tokens.shape
    devices = lax.axis_size("adapter")
    resident_rows = adapter_down_weight.shape[0]
    slots = max(1, 4 * blocks // devices)
    values, normed = normalise(tokens)
    owner = request_block_adapter // resident_rows
    within = request_block_adapter - owner * resident_rows
    serial = jnp.arange(blocks, dtype=jnp.int32)
    earlier = (owner[:, None] == owner[None, :]) & (serial[None, :] < serial[:, None])
    position = owner * slots + jnp.sum(earlier, axis=1)
    outgoing = (
        jnp.zeros((devices * slots, rows, feature_width), jnp.bfloat16).at[position].set(normed)
    )
    outgoing = outgoing.reshape(devices, slots, rows, feature_width)
    block_labels = jnp.full((devices * slots,), -1, jnp.int32).at[position].set(within)
    block_labels = jnp.broadcast_to(block_labels[:, None], (devices * slots, rows)).reshape(
        devices, slots, rows
    )
    arriving_rows, row_markers = (
        lax.all_to_all(outgoing, "adapter", split_axis=0, concat_axis=0, tiled=True),
        lax.all_to_all(block_labels, "adapter", split_axis=0, concat_axis=0, tiled=True),
    )
    lowrank_update = resident_update(
        arriving_rows, row_markers, adapter_down_weight, adapter_up_weight
    )
    returned = lax.all_to_all(lowrank_update, "adapter", split_axis=0, concat_axis=0, tiled=True)
    mine = returned.reshape(devices * slots, rows, feature_width)[position]
    live = jnp.arange(rows, dtype=jnp.int32)[None, :] < request_block_rows[:, None]
    mixed = values + jnp.where(live[:, :, None], mine.astype(jnp.float32), jnp.float32(0.0))
    return mixed.astype(jnp.bfloat16)


def lanes_of(rows):
    return lax.broadcasted_iota(jnp.int32, (rows, LANES), 1)


def weight_kernel(whole, pieces, part_ref, group_ref, weight_ref, *out_refs):
    tiles = whole // LANES
    for (k, start, count, halved), out_ref in zip(pieces, out_refs):
        j = part_ref[k]
        if k < 2:
            last = weight_ref[:, QUAD * whole :].astype(jnp.float32)
            turned = pltpu.roll(last, lax.rem(LANES - QUARTER * j, LANES), 1)
            inside = lanes_of(last.shape[0]) < QUARTER
            out_ref[:, 0:whole] = weight_ref[:, pl.ds(pl.multiple_of(j * whole, LANES), whole)]
            out_ref[:, whole:] = jnp.where(inside, turned, 0.0).astype(jnp.bfloat16)
            continue
        if halved:
            start = pl.multiple_of(group_ref[0] * (weight_ref.shape[0] // 2) + start, count)
        for t in range(tiles):
            column = pl.multiple_of(j * whole + t * LANES, LANES)
            out_ref[t * count : (t + 1) * count, :] = weight_ref[
                pl.ds(start, count), pl.ds(column, LANES)
            ]
        last = weight_ref[pl.ds(start, count), QUAD * whole :].astype(jnp.float32)
        size = count // QUAD
        owner = lanes_of(size) // QUARTER
        merged = jnp.zeros((size, LANES), jnp.float32)
        for m in range(QUAD):
            shift = lax.rem(LANES + QUARTER * (m - j), LANES)
            turned = pltpu.roll(last[m * size : (m + 1) * size], shift, 1)
            merged = jnp.where(owner == m, turned, merged)
        out_ref[tiles * count :, :] = merged.astype(jnp.bfloat16)


def open_far(far_refs, places, opened_ref):
    width = opened_ref.shape[2]
    tiles = width // LANES - 1
    for ref, (holder, base, count) in zip(far_refs, places):
        size = count // QUAD
        inside = lanes_of(size) < QUARTER
        for t in range(tiles):
            opened_ref[holder, base : base + count, t * LANES : (t + 1) * LANES] = ref[
                t * count : (t + 1) * count, :
            ]
        packed = ref[tiles * count :, :].astype(jnp.float32)
        for m in range(QUAD):
            turned = pltpu.roll(packed, (LANES - QUARTER * m) % LANES, 1) if m else packed
            opened_ref[holder, base + m * size : base + (m + 1) * size, tiles * LANES :] = (
                jnp.where(inside, turned, 0.0).astype(jnp.bfloat16)
            )


def far_places(pieces, rows):
    far = [piece for piece in pieces if piece[0] >= 2]
    own = [(k - 2, start, count) for k, start, count, halved in far]
    return own + [(k - 2, rows // 2 + start, count) for k, start, count, halved in far if halved]


def split(pieces):
    return sorted({k for k, start, count, halved in pieces if halved})


def lay_out(resident, adapter_ref, used_ref, most_ref, target_ref, label_ref):
    blocks, total = adapter_ref.shape[1], target_ref.shape[1]
    rows = total // blocks
    adapter, used = adapter_ref[...], used_ref[...]
    down = lax.broadcasted_iota(jnp.int32, (blocks, blocks), 0)
    across = lax.broadcasted_iota(jnp.int32, (blocks, blocks), 1)

    def turned(value):
        return jnp.sum(jnp.where(down == across, value, 0), axis=1, keepdims=True)

    span = resident * QUAD
    quad = jnp.floor((adapter.astype(jnp.float32) + 0.5) * (1.0 / span)).astype(jnp.int32)
    order = adapter * blocks + lax.broadcasted_iota(jnp.int32, (1, blocks), 1)
    quad_down, order_down, used_down = turned(quad), turned(order), turned(used)
    same = quad_down == quad
    ahead = jnp.sum(jnp.where(same & (order < order_down), used, 0), axis=1, keepdims=True)
    within = jnp.sum(jnp.where(same, used, 0), axis=1, keepdims=True)
    most_ref[...] = jnp.broadcast_to(jnp.max(within, axis=0, keepdims=True), most_ref.shape)
    start = quad_down * total + ahead

    block = lax.broadcasted_iota(jnp.int32, (blocks, total), 0)
    row = lax.broadcasted_iota(jnp.int32, (blocks, total), 1) - block * rows
    place = jnp.where((row >= 0) & (row < used_down), start + row + 1, 0)
    target_ref[...] = jnp.sum(place, axis=0, keepdims=True) - 1
    block = lax.broadcasted_iota(jnp.int32, (total, blocks), 1)
    row = lax.broadcasted_iota(jnp.int32, (total, blocks), 0) - block * rows
    label = jnp.where((row >= 0) & (row < rows), adapter - quad * span + 1, 0)
    label_ref[...] = jnp.sum(label.astype(jnp.float32), axis=1, keepdims=True)


def first_pack_kernel(
    whole, cap, resident, adapter_ref, used_ref, tokens_ref, out_ref, target_ref, label_ref, *refs
):
    normed_ref, most_ref = refs
    lay_out(resident, adapter_ref, used_ref, most_ref, target_ref, label_ref)
    pack_kernel(
        whole, cap, 0, most_ref, target_ref, label_ref, tokens_ref, out_ref, normed_ref
    )


def pack_kernel(
    whole, cap, base, most_ref, target_ref, label_ref, tokens_ref, out_ref, normed_ref
):
    values = tokens_ref[...].astype(jnp.float32)
    mean_sq = jnp.mean(values * values, axis=-1, keepdims=True)
    normed_ref[...] = (values * lax.rsqrt(mean_sq + 1e-06)).astype(jnp.bfloat16)
    total = tokens_ref.shape[0]
    quads, tiles = out_ref.shape[0] // QUAD, whole // LANES
    lane = lanes_of(total)
    last = normed_ref[:, QUAD * whole :].astype(jnp.float32)
    label = jnp.where(lane == QUARTER, label_ref[...], 0.0)
    ends = []
    for j in range(QUAD):
        turned = pltpu.roll(last, (LANES - QUARTER * j) % LANES, 1) if j else last
        ends.append(jnp.where(lane < QUARTER, turned, label).astype(jnp.bfloat16))
    most = most_ref[0:1, 0:1].astype(jnp.float32)
    group_lane = lanes_of(QUARTER) // QUARTER
    step_lane = lanes_of(STEP)
    chosen = []
    for q in range(quads):
        place = lax.broadcasted_iota(jnp.int32, (cap, total), 0) + (q * total + base)
        chosen.append(jnp.where(target_ref[...] == place, 1.0, 0.0).astype(jnp.bfloat16))
    chosen = jnp.concatenate(chosen, axis=0)
    notes = [jnp.where(step_lane == NOTE + cap // STEP, most, 0.0)] * quads
    for j in range(QUAD):
        for t in range(tiles):
            column = j * whole + t * LANES
            if t % 2 == 0:
                count = min(2, tiles - t) * LANES
                share = jnp.dot(
                    chosen,
                    normed_ref[:, column : column + count],
                    preferred_element_type=jnp.float32,
                ).astype(jnp.bfloat16)
            for q in range(quads):
                out_ref[q * QUAD + j, t * cap : (t + 1) * cap, :] = share[
                    q * cap : (q + 1) * cap, t % 2 * LANES : (t % 2 + 1) * LANES
                ]
        end_rows = jnp.dot(chosen, ends[j], preferred_element_type=jnp.float32)
        for q in range(quads):
            end = end_rows[q * cap : (q + 1) * cap]
            if j == 0:
                for a in range(cap // STEP):
                    turned = pltpu.roll(end[a * STEP : (a + 1) * STEP], NOTE + a - QUARTER, 1)
                    notes[q] = jnp.where(step_lane == NOTE + a, turned, notes[q])
            padded = jnp.concatenate(
                [end, jnp.zeros((QUAD * QUARTER - cap, LANES), jnp.float32)], axis=0
            )
            merged = padded[0:QUARTER]
            for m in range(1, QUAD):
                turned = pltpu.roll(padded[m * QUARTER : (m + 1) * QUARTER], m * QUARTER, 1)
                merged = jnp.where(group_lane == m, turned, merged)
            out_ref[q * QUAD + j, tiles * cap : tiles * cap + STEP, :] = merged[0:STEP].astype(
                jnp.bfloat16
            )
            out_ref[q * QUAD + j, tiles * cap + STEP :, :] = jnp.where(
                step_lane >= NOTE, notes[q], merged[STEP:]
            ).astype(jnp.bfloat16)


def read_notes(rows_ref, cap, tiles, part_ref, resident, notes_ref, labels_ref, met_ref):
    senders = rows_ref.shape[0]
    for s in range(senders):
        notes_ref[s * STEP : (s + 1) * STEP, :] = rows_ref[s, tiles * cap + STEP :, :]
    steps = labels_ref.shape[0]
    row = lax.broadcasted_iota(jnp.int32, (steps, LANES), 0)
    wanted = jnp.where(lanes_of(steps) == NOTE + row, 1.0, 0.0).astype(jnp.bfloat16)
    labels = lax.dot_general(
        wanted, notes_ref[...], (((1,), (1,)), ((), ())), preferred_element_type=jnp.float32
    )
    labels_ref[...] = labels
    code = jnp.zeros((steps, 1), jnp.float32)
    for h in range(QUAD):
        first = part_ref[h].astype(jnp.float32) + 1.0
        met = jnp.where((labels >= first) & (labels < first + resident), 1.0, 0.0)
        code = code + (1 << h) * jnp.max(met, axis=1, keepdims=True)
    at = lax.broadcasted_iota(jnp.int32, (steps, 1), 0)
    for a in range(cap // STEP):
        met_ref[a] = jnp.max(jnp.where(at == a, code, 0.0)).astype(jnp.int32)


def for_holders(met_ref, first_ref, near_refs, opened_ref, halved, a, step):
    pairs = opened_ref.shape[1] // LANES
    for h in range(QUAD):
        base = first_ref[h].astype(jnp.float32) + 1.0
        firsts = [base + 2.0 * t for t in range(pairs)]
        if h in halved:
            firsts = [
                base + first_ref[QUAD + i].astype(jnp.float32) + 2.0 * t
                for i in range(2)
                for t in range(pairs // 2)
            ]

        @pl.when(lax.rem(met_ref[a] // (1 << h), 2) > 0)
        def _(h=h, firsts=firsts):
            step(near_refs[h] if h < 2 else opened_ref.at[h - 2], firsts)


def down_kernel(pieces, first_ref, rows_ref, *refs):
    near_refs, far_refs, (out_ref, count_ref, notes_ref, met_ref) = refs[:2], refs[2:-8], refs[-8:-4]
    opened_ref, batch_ref, picked_ref, labels_ref = refs[-4:]
    senders, width = rows_ref.shape[0], batch_ref.shape[1]
    tiles = width // LANES - 1
    cap = out_ref.shape[0] * STEP
    rank = out_ref.shape[1]
    resident = opened_ref.shape[1] // rank
    dims = (((1,), (1,)), ((), ()))
    read_notes(rows_ref, cap, tiles, first_ref, resident, notes_ref, labels_ref, met_ref)
    notes = notes_ref[...].astype(jnp.float32)
    is_count = lanes_of(senders * STEP) == NOTE + cap // STEP
    count = jnp.max(jnp.where(is_count, notes, 0.0), axis=(0, 1), keepdims=True)
    count_ref[...] = jnp.broadcast_to(count, count_ref.shape).astype(jnp.bfloat16)
    open_far(far_refs, far_places(pieces, opened_ref.shape[1]), opened_ref)

    def one(a, carry):
        picked_ref[...] = jnp.zeros(picked_ref.shape, jnp.float32)

        @pl.when(met_ref[a] > 0)
        def _():
            shift = lax.rem(LANES - QUARTER * (a // 2), LANES)
            spot = pl.multiple_of(tiles * cap + lax.rem(a, 2) * STEP, STEP)
            for s in range(senders):
                rows = slice(s * STEP, (s + 1) * STEP)
                for t in range(tiles):
                    at = pl.multiple_of(t * cap + a * STEP, STEP)
                    batch_ref[rows, t * LANES : (t + 1) * LANES] = rows_ref[s, pl.ds(at, STEP), :]
                end = rows_ref[s, pl.ds(spot, STEP), :].astype(jnp.float32)
                batch_ref[rows, tiles * LANES :] = pltpu.roll(end, shift, 1).astype(jnp.bfloat16)
            label = labels_ref[pl.ds(a, 1), :]

            def step(weight_ref, firsts):
                product = lax.dot_general(
                    weight_ref[...], batch_ref[...], dims, preferred_element_type=jnp.float32
                )
                picked = picked_ref[...]
                for t, first in enumerate(firsts):
                    for i in range(2):
                        at = (2 * t + i) * rank
                        picked = jnp.where(
                            label == first + i, product[at : at + rank, :], picked
                        )
                picked_ref[...] = picked

            for_holders(met_ref, first_ref, near_refs, opened_ref, split(pieces), a, step)

        out_ref[a] = picked_ref[...]
        return carry

    lax.fori_loop(0, cap // STEP, one, 0)


def pair_kernel(own_ref, other_ref, out_ref):
    out_ref[...] = (own_ref[...] + other_ref[...]).astype(jnp.bfloat16)


def up_kernel(pieces, first_ref, met_ref, notes_ref, *refs):
    sum_refs, near_refs, far_refs, out_ref = refs[:2], refs[2:4], refs[4:-6], refs[-6]
    opened_ref, delta_ref, ends_ref, label_ref, twice_ref = refs[-5:]
    senders, width = out_ref.shape[0], opened_ref.shape[2]
    tiles = width // LANES - 1
    rank = sum_refs[0].shape[1]
    kept = (out_ref.shape[1] - QUARTER) // tiles
    group_lane = lanes_of(STEP) // QUARTER
    open_far(far_refs, far_places(pieces, opened_ref.shape[1]), opened_ref)
    ends_ref[...] = jnp.zeros(ends_ref.shape, jnp.float32)
    low = jnp.where(lanes_of(senders * STEP) < HALF, 0.0, 1.0)
    rank_row = lax.broadcasted_iota(jnp.int32, (rank, LANES), 0)
    twofold = jnp.where(lax.rem(lanes_of(rank), rank) == rank_row, 1.0, 0.0).astype(jnp.bfloat16)

    note_row = lax.broadcasted_iota(jnp.int32, (LANES, LANES), 0)
    for a in range(kept // STEP):
        wanted = jnp.where(note_row == NOTE + a, 1.0, 0.0).astype(jnp.bfloat16)
        label_ref[a] = jnp.dot(notes_ref[...], wanted, preferred_element_type=jnp.float32) - low
        down = sum_refs[0][a].astype(jnp.float32) + sum_refs[1][a].astype(jnp.float32)
        twice_ref[a] = lax.dot_general(
            down.astype(jnp.bfloat16),
            twofold,
            (((0,), (0,)), ((), ())),
            preferred_element_type=jnp.float32,
        )

    def one(a, carry):
        delta_ref[...] = jnp.zeros(delta_ref.shape, jnp.float32)

        @pl.when(met_ref[a] > 0)
        def _():
            label, twice = label_ref[a], twice_ref[a]

            def step(weight_ref, firsts):
                placed = [jnp.where(label == first, twice, 0.0) for first in firsts]
                placed = jnp.concatenate(placed, axis=1).astype(jnp.bfloat16)
                delta_ref[...] += jnp.dot(
                    placed, weight_ref[...], preferred_element_type=jnp.float32
                )

            for_holders(met_ref, first_ref, near_refs, opened_ref, split(pieces), a, step)

        spot = pl.multiple_of(lax.rem(a, 2) * STEP, STEP)
        for s in range(senders):
            rows = slice(s * STEP, (s + 1) * STEP)
            for t in range(tiles):
                at = pl.multiple_of(t * kept + a * STEP, STEP)
                out_ref[s, pl.ds(at, STEP), :] = delta_ref[
                    rows, t * LANES : (t + 1) * LANES
                ].astype(jnp.bfloat16)
            turned = pltpu.roll(delta_ref[rows, tiles * LANES :], QUARTER * (a // 2), 1)
            ends_ref[s, pl.ds(spot, STEP), :] = jnp.where(
                group_lane == a // 2, turned, ends_ref[s, pl.ds(spot, STEP), :]
            )
        return carry

    lax.fori_loop(0, kept // STEP, one, 0)
    for s in range(senders):
        out_ref[s, tiles * kept :, :] = ends_ref[s].astype(jnp.bfloat16)


def mix_kernel(whole, bases, target_ref, tokens_ref, *refs):
    returned_refs, out_ref = refs[:-1], refs[-1]
    total = tokens_ref.shape[0]
    tiles, quads = whole // LANES, returned_refs[0].shape[0] // QUAD
    lane = lanes_of(total)
    chosen = []
    for base, ref in zip(bases, returned_refs):
        kept = (ref.shape[1] - QUARTER) // tiles
        spot = lax.broadcasted_iota(jnp.int32, (total, quads * kept), 1)
        place = spot // kept * total + spot % kept + base
        chosen.append(jnp.where(target_ref[...] == place, 1.0, 0.0).astype(jnp.bfloat16))
    end = jnp.zeros((total, LANES), jnp.float32)
    for j in range(QUAD):
        delta = 0.0
        for choice, ref in zip(chosen, returned_refs):
            kept = choice.shape[1] // quads
            shares = []
            for q in range(quads):
                d = q * QUAD + j
                parts = [ref[d, t * kept : (t + 1) * kept, :] for t in range(tiles)]
                packed = ref[d, tiles * kept :, :].astype(jnp.float32)
                groups = [packed]
                for m in range(1, QUAD):
                    groups.append(pltpu.roll(packed, LANES - QUARTER * m, 1))
                parts.append(jnp.concatenate(groups, axis=0)[0:kept].astype(jnp.bfloat16))
                shares.append(jnp.concatenate(parts, axis=1))
            share = jnp.concatenate(shares, axis=0)
            delta = delta + jnp.dot(choice, share, preferred_element_type=jnp.float32)
        columns = slice(j * whole, (j + 1) * whole)
        out_ref[:, columns] = (
            tokens_ref[:, columns].astype(jnp.float32) + delta[:, 0:whole]
        ).astype(jnp.bfloat16)
        last = delta[:, whole:]
        turned = pltpu.roll(last, QUARTER * j, 1) if j else last
        end = jnp.where((lane >= QUARTER * j) & (lane < QUARTER * (j + 1)), turned, end)
    out_ref[:, QUAD * whole :] = (
        tokens_ref[:, QUAD * whole :].astype(jnp.float32) + end
    ).astype(jnp.bfloat16)


def call(kernel, out_shape, in_specs, flops, moved, after=(), scratch=(), out_specs=None):
    many = isinstance(out_shape, list)
    skipped = len(after)
    body = (lambda *refs: kernel(*refs[skipped:])) if skipped else kernel
    run = pl.pallas_call(
        body,
        out_shape=out_shape,
        in_specs=[pl.BlockSpec(memory_space=pl.ANY)] * skipped + in_specs,
        out_specs=out_specs or ([VMEM] * len(out_shape) if many else VMEM),
        scratch_shapes=scratch,
        compiler_params=pltpu.CompilerParams(vmem_limit_bytes=48 * 2**20),
        cost_estimate=pl.CostEstimate(flops=flops, bytes_accessed=moved, transcendentals=0),
    )
    return functools.partial(run, *after)


def exchange(value):
    return lax.all_to_all(value, "adapter", split_axis=0, concat_axis=0, tiled=True)


def towards(value, k, devices):
    return lax.ppermute(value, "adapter", [(i, i ^ k) for i in range(devices)])


def swapped(value):
    return lax.ppermute(value, "groups", [(0, 1), (1, 0)])


def stand_behind(value, *earlier):
    return pl.pallas_call(
        lambda *refs: None,
        out_shape=jax.ShapeDtypeStruct(value.shape, value.dtype),
        in_specs=[pl.BlockSpec(memory_space=pl.ANY)] * (1 + len(earlier)),
        out_specs=pl.BlockSpec(memory_space=pl.ANY),
        input_output_aliases={0: 0},
    )(value, *earlier)


def first_pack_call(cap, whole, devices, resident, adapter, used, tokens):
    blocks, rows, width = tokens.shape
    total = blocks * rows
    return call(
        functools.partial(first_pack_kernel, whole, cap, resident),
        [
            jax.ShapeDtypeStruct((devices, whole // LANES * cap + QUARTER, LANES), jnp.bfloat16),
            jax.ShapeDtypeStruct((1, total), jnp.int32),
            jax.ShapeDtypeStruct((total, 1), jnp.float32),
        ],
        [VMEM, VMEM, VMEM],
        2 * devices * cap * total * whole,
        2 * (total * width + devices * cap * whole),
        scratch=[pltpu.VMEM((total, width), jnp.bfloat16), pltpu.VMEM((8, LANES), jnp.int32)],
    )(adapter.reshape(1, blocks), used.reshape(1, blocks), tokens.reshape(total, width))


def pack_call(cap, base, whole, devices, target, label, tokens):
    blocks, rows, width = tokens.shape
    total = blocks * rows
    return call(
        functools.partial(pack_kernel, whole, cap, base),
        jax.ShapeDtypeStruct((devices, whole // LANES * cap + QUARTER, LANES), jnp.bfloat16),
        [VMEM, VMEM, VMEM, VMEM],
        2 * devices * cap * total * whole,
        2 * (total * width + devices * cap * whole),
        scratch=[pltpu.VMEM((total, width), jnp.bfloat16)],
    )(jnp.zeros((8, LANES), jnp.int32), target, label, tokens.reshape(total, width))


def down_pieces(rows):
    quarter, half = rows // 4, rows // 2
    return [(0, 0, rows, False), (1, 0, rows, False)] + [
        (2, 0, quarter, True),
        (2, quarter, quarter, True),
        (3, 0, half, True),
    ]


def up_pieces(rows):
    return [(0, 0, rows, False), (1, 0, rows, False)] + [
        (2, 0, rows // 2, True),
        (3, 0, rows, False),
    ]


def down_call(cap, first, arrived, down_weights, after):
    devices = arrived.shape[0]
    columns, share = down_weights[0].shape
    return call(
        functools.partial(down_kernel, down_pieces(columns)),
        [
            jax.ShapeDtypeStruct((cap // STEP, HALF, devices * STEP), jnp.float32),
            jax.ShapeDtypeStruct((STEP, LANES), jnp.bfloat16),
            jax.ShapeDtypeStruct((devices * STEP, LANES), jnp.bfloat16),
            jax.ShapeDtypeStruct((8,), jnp.int32),
        ],
        [SMEM] + [VMEM] * (1 + len(down_weights)),
        0,
        0,
        after,
        [
            pltpu.VMEM((2, columns, share), jnp.bfloat16),
            pltpu.VMEM((devices * STEP, share), jnp.bfloat16),
            pltpu.VMEM((HALF, devices * STEP), jnp.float32),
            pltpu.VMEM((8, devices * STEP), jnp.float32),
        ],
        [VMEM, VMEM, VMEM, SMEM],
    )(first, arrived, *down_weights)


def quad_sums(partial, devices):
    pair = call(
        pair_kernel, jax.ShapeDtypeStruct(partial.shape, jnp.bfloat16), [VMEM, VMEM], 0, 0
    )(partial, towards(partial, 1, devices))
    return [pair, towards(pair, 2, devices)]


def up_call(kept, first, met, notes, sums, up_weights):
    devices = notes.shape[0] // STEP
    columns, share = up_weights[0].shape
    shape = (devices, (share // LANES - 1) * kept + QUARTER, LANES)
    return call(
        functools.partial(up_kernel, up_pieces(columns)),
        jax.ShapeDtypeStruct(shape, jnp.bfloat16),
        [SMEM, SMEM] + [VMEM] * (3 + len(up_weights)),
        2 * devices * kept * QUAD * columns * share,
        2 * (2 * devices * kept + QUAD * columns) * share,
        scratch=[
            pltpu.VMEM((2, columns, share), jnp.bfloat16),
            pltpu.VMEM((devices * STEP, share), jnp.float32),
            pltpu.VMEM((devices, QUARTER, LANES), jnp.float32),
            *[pltpu.VMEM((kept // STEP, devices * STEP, LANES), jnp.float32)] * 2,
        ],
    )(first, met, notes, *sums, *up_weights)


def back_and_mix(
    kept, more, tokens, target, label, first, met, notes, sums, down_weights, up_weights, *unused
):
    blocks, rows, width = tokens.shape
    total = blocks * rows
    devices = notes.shape[0] // STEP
    whole = up_weights[0].shape[1] - LANES
    pieces = [exchange(up_call(kept, first, met, notes, sums, up_weights))]
    if more:
        outgoing = pack_call(more, kept, whole, devices, target, label, tokens)
        arrived = exchange(outgoing)
        partial, unused_count, notes, met = down_call(more, first, arrived, down_weights, [])
        sums = quad_sums(partial, devices)
        pieces.append(exchange(up_call(more, first, met, notes, sums, up_weights)))
    mixed = call(
        functools.partial(mix_kernel, whole, (0, kept)[: len(pieces)]),
        jax.ShapeDtypeStruct((total, width), jnp.bfloat16),
        [VMEM] * (2 + len(pieces)),
        2 * devices * (kept + more) * total * whole,
        2 * (2 * total * width + devices * (kept + more) * whole),
    )(target.reshape(total, 1), tokens.reshape(total, width), *pieces)
    return mixed.reshape(tokens.shape)


def start_again(
    tokens, target, label, first, met, notes, sums, down_weights, up_weights, *arguments
):
    return rows_to_holders(tokens, *arguments)


def rows_to_quads(
    tokens, request_block_adapter, request_block_rows, adapter_down_weight, adapter_up_weight
):
    blocks, rows, width = tokens.shape
    devices = lax.axis_size("adapter")
    resident, rank, unused_width = adapter_up_weight.shape
    total = blocks * rows
    columns = resident * rank
    whole = width // LANES // QUAD * LANES
    share = whole + LANES
    bf16, i32 = jnp.bfloat16, jnp.int32

    me = lax.axis_index("adapter").astype(i32)
    group = lax.axis_index("groups").astype(i32)
    parts = jnp.bitwise_xor(me % QUAD, jnp.arange(QUAD, dtype=i32))
    halves = jnp.stack([group, 1 - group]) * (resident // 2)
    first = jnp.concatenate([parts * resident, halves]).astype(i32)
    tiles = whole // LANES

    def shares(weight, pieces, after):
        shapes = []
        for k, start, count, halved in pieces:
            far = (count * tiles + count // QUAD, LANES)
            shapes.append(jax.ShapeDtypeStruct((columns, share) if k < 2 else far, bf16))
        values = call(
            functools.partial(weight_kernel, whole, pieces),
            shapes,
            [SMEM, SMEM, VMEM],
            0,
            QUAD * columns * width,
            after,
        )(parts, group.reshape(1), weight)
        return [
            towards(value, piece[0], devices) if piece[0] else value
            for piece, value in zip(pieces, values)
        ]

    pieces = down_pieces(columns)
    down_weights = shares(adapter_down_weight.transpose(0, 2, 1).reshape(columns, width), pieces, [])
    early = down_weights[2]
    pieces = up_pieces(columns)
    up_weights = shares(adapter_up_weight.reshape(columns, width), pieces, down_weights[:1])
    down_weights[3] = stand_behind(down_weights[3], up_weights[0])
    down_weights += [swapped(value) for value in down_weights[2:]]
    up_weights.append(swapped(up_weights[2]))

    caps = [total * 5 // 16, total * 6 // 16, total * 7 // 16]
    cap = caps[-1]
    outgoing, target, label = first_pack_call(
        cap, whole, devices, resident, request_block_adapter, request_block_rows, tokens
    )
    arrived = exchange(stand_behind(outgoing, early))
    partial, count, notes, met = down_call(cap, first, arrived, down_weights, up_weights[2:3])
    sums = quad_sums(partial, devices)
    count = count[0:1, 0:1]
    most = jnp.maximum(count, swapped(count))[0, 0].astype(jnp.float32)
    branches = [functools.partial(back_and_mix, kept, 0) for kept in caps]
    branches += [functools.partial(back_and_mix, cap, STEP), start_again]
    return lax.switch(
        sum((most > limit).astype(i32) for limit in [*caps, cap + STEP]),
        branches,
        tokens,
        target,
        label,
        first,
        met,
        notes,
        sums,
        down_weights,
        up_weights,
        request_block_adapter,
        request_block_rows,
        adapter_down_weight,
        adapter_up_weight,
    )


def solution(mesh):
    placed = (
        P(("groups", "adapter"), None, None),
        P(("groups", "adapter")),
        P(("groups", "adapter")),
        P("adapter", None, None),
        P("adapter", None, None),
    )

    def per_device(tokens, request_block_adapter, request_block_rows, down_weight, up_weight):
        blocks, rows, width = tokens.shape
        devices = mesh.shape["adapter"]
        slots = max(1, 4 * blocks // devices)
        quads = devices % QUAD == 0 and slots * QUAD >= blocks
        quads = quads and width % (QUAD * LANES) == LANES and up_weight.shape[1] == HALF
        quads = quads and blocks * rows * 7 // 16 == 7 * STEP and mesh.shape["groups"] == 2
        plan = rows_to_quads if quads else rows_to_holders
        return plan(tokens, request_block_adapter, request_block_rows, down_weight, up_weight)

    return jax.shard_map(
        per_device,
        mesh=mesh,
        in_specs=placed,
        out_specs=P(("groups", "adapter"), None, None),
        check_vma=False,
    )
```

```python
import functools

import jax
import jax.numpy as jnp
from jax import lax
from jax.experimental import pallas as pl
from jax.experimental.pallas import tpu as pltpu
from jax.sharding import PartitionSpec as P

LANES = 128
HALF = 64
QUAD = 4
QUARTER = 32
STEP = 16
NOTE = 96
DOWN_HALVED = (2, 3)
UP_HALVED = (2,)
VMEM = pl.BlockSpec(memory_space=pltpu.VMEM)
SMEM = pl.BlockSpec(memory_space=pltpu.SMEM)


def normalise(tokens):
    values = tokens.astype(jnp.float32)
    mean_sq = jnp.mean(values * values, axis=-1, keepdims=True)
    return (values, (values * lax.rsqrt(mean_sq + 1e-06)).astype(jnp.bfloat16))


def resident_update(hidden_state, block_labels, adapter_down_weight, adapter_up_weight):
    feature_width = hidden_state.shape[-1]
    leading = hidden_state.shape[:-1]
    resident_rows, unused_value, inner_rank = adapter_down_weight.shape
    flattened_tokens = hidden_state.reshape(-1, feature_width)
    down_matrix = jnp.einsum(
        "tq,iqg->tig", flattened_tokens, adapter_down_weight, preferred_element_type=jnp.float32
    )
    down_matrix = down_matrix.astype(jnp.bfloat16).reshape(
        flattened_tokens.shape[0], resident_rows * inner_rank
    )
    column_owner = jnp.arange(resident_rows * inner_rank, dtype=jnp.int32) // inner_rank
    picked = block_labels.reshape(-1, 1) == column_owner[None, :]
    down_matrix = jnp.where(picked, down_matrix, jnp.zeros_like(down_matrix))
    lowrank_update = jnp.dot(
        down_matrix,
        adapter_up_weight.reshape(resident_rows * inner_rank, feature_width),
        preferred_element_type=jnp.float32,
    )
    return lowrank_update.astype(jnp.bfloat16).reshape(leading + (feature_width,))


def rows_to_holders(
    tokens, request_block_adapter, request_block_rows, adapter_down_weight, adapter_up_weight
):
    blocks, rows, feature_width = tokens.shape
    devices = lax.axis_size("adapter")
    resident_rows = adapter_down_weight.shape[0]
    slots = max(1, 4 * blocks // devices)
    values, normed = normalise(tokens)
    owner = request_block_adapter // resident_rows
    within = request_block_adapter - owner * resident_rows
    serial = jnp.arange(blocks, dtype=jnp.int32)
    earlier = (owner[:, None] == owner[None, :]) & (serial[None, :] < serial[:, None])
    position = owner * slots + jnp.sum(earlier, axis=1)
    outgoing = (
        jnp.zeros((devices * slots, rows, feature_width), jnp.bfloat16).at[position].set(normed)
    )
    outgoing = outgoing.reshape(devices, slots, rows, feature_width)
    block_labels = jnp.full((devices * slots,), -1, jnp.int32).at[position].set(within)
    block_labels = jnp.broadcast_to(block_labels[:, None], (devices * slots, rows)).reshape(
        devices, slots, rows
    )
    arriving_rows, row_markers = (
        lax.all_to_all(outgoing, "adapter", split_axis=0, concat_axis=0, tiled=True),
        lax.all_to_all(block_labels, "adapter", split_axis=0, concat_axis=0, tiled=True),
    )
    lowrank_update = resident_update(
        arriving_rows, row_markers, adapter_down_weight, adapter_up_weight
    )
    returned = lax.all_to_all(lowrank_update, "adapter", split_axis=0, concat_axis=0, tiled=True)
    mine = returned.reshape(devices * slots, rows, feature_width)[position]
    live = jnp.arange(rows, dtype=jnp.int32)[None, :] < request_block_rows[:, None]
    mixed = values + jnp.where(live[:, :, None], mine.astype(jnp.float32), jnp.float32(0.0))
    return mixed.astype(jnp.bfloat16)


def lanes_of(rows):
    return lax.broadcasted_iota(jnp.int32, (rows, LANES), 1)


def weight_kernel(whole, which, halved, part_ref, group_ref, weight_ref, *out_refs):
    tiles = whole // LANES
    for k, out_ref in zip(which, out_refs):
        j = part_ref[k]
        if k < 2:
            last = weight_ref[:, QUAD * whole :].astype(jnp.float32)
            turned = pltpu.roll(last, lax.rem(LANES - QUARTER * j, LANES), 1)
            inside = lanes_of(last.shape[0]) < QUARTER
            out_ref[:, 0:whole] = weight_ref[:, pl.ds(pl.multiple_of(j * whole, LANES), whole)]
            out_ref[:, whole:] = jnp.where(inside, turned, 0.0).astype(jnp.bfloat16)
            continue
        count = weight_ref.shape[0] // 2 if k in halved else weight_ref.shape[0]
        start = pl.multiple_of(group_ref[0] * count, count) if k in halved else 0
        for t in range(tiles):
            column = pl.multiple_of(j * whole + t * LANES, LANES)
            out_ref[t * count : (t + 1) * count, :] = weight_ref[
                pl.ds(start, count), pl.ds(column, LANES)
            ]
        last = weight_ref[pl.ds(start, count), QUAD * whole :].astype(jnp.float32)
        size = count // QUAD
        owner = lanes_of(size) // QUARTER
        merged = jnp.zeros((size, LANES), jnp.float32)
        for m in range(QUAD):
            shift = lax.rem(LANES + QUARTER * (m - j), LANES)
            turned = pltpu.roll(last[m * size : (m + 1) * size], shift, 1)
            merged = jnp.where(owner == m, turned, merged)
        out_ref[tiles * count :, :] = merged.astype(jnp.bfloat16)


def open_far(far_refs, halved, opened_ref):
    width = opened_ref.shape[2]
    tiles = width // LANES - 1
    places = [(k - 2, 0) for k in (2, 3)] + [(k - 2, 1) for k in halved]
    for ref, (holder, part) in zip(far_refs, places):
        count = opened_ref.shape[1] // 2 if holder + 2 in halved else opened_ref.shape[1]
        base, size = part * count, count // QUAD
        inside = lanes_of(size) < QUARTER
        for t in range(tiles):
            opened_ref[holder, base : base + count, t * LANES : (t + 1) * LANES] = ref[
                t * count : (t + 1) * count, :
            ]
        packed = ref[tiles * count :, :].astype(jnp.float32)
        for m in range(QUAD):
            turned = pltpu.roll(packed, (LANES - QUARTER * m) % LANES, 1) if m else packed
            opened_ref[holder, base + m * size : base + (m + 1) * size, tiles * LANES :] = (
                jnp.where(inside, turned, 0.0).astype(jnp.bfloat16)
            )


def lay_out(resident, adapter_ref, used_ref, most_ref, target_ref, label_ref):
    blocks, total = adapter_ref.shape[1], target_ref.shape[1]
    rows = total // blocks
    adapter, used = adapter_ref[...], used_ref[...]
    down = lax.broadcasted_iota(jnp.int32, (blocks, blocks), 0)
    across = lax.broadcasted_iota(jnp.int32, (blocks, blocks), 1)

    def turned(value):
        return jnp.sum(jnp.where(down == across, value, 0), axis=1, keepdims=True)

    span = resident * QUAD
    quad = jnp.floor((adapter.astype(jnp.float32) + 0.5) * (1.0 / span)).astype(jnp.int32)
    order = adapter * blocks + lax.broadcasted_iota(jnp.int32, (1, blocks), 1)
    quad_down, order_down, used_down = turned(quad), turned(order), turned(used)
    same = quad_down == quad
    ahead = jnp.sum(jnp.where(same & (order < order_down), used, 0), axis=1, keepdims=True)
    within = jnp.sum(jnp.where(same, used, 0), axis=1, keepdims=True)
    most_ref[...] = jnp.broadcast_to(jnp.max(within, axis=0, keepdims=True), most_ref.shape)
    start = quad_down * total + ahead

    block = lax.broadcasted_iota(jnp.int32, (blocks, total), 0)
    row = lax.broadcasted_iota(jnp.int32, (blocks, total), 1) - block * rows
    place = jnp.where((row >= 0) & (row < used_down), start + row + 1, 0)
    target_ref[...] = jnp.sum(place, axis=0, keepdims=True) - 1
    block = lax.broadcasted_iota(jnp.int32, (total, blocks), 1)
    row = lax.broadcasted_iota(jnp.int32, (total, blocks), 0) - block * rows
    label = jnp.where((row >= 0) & (row < rows), adapter - quad * span + 1, 0)
    label_ref[...] = jnp.sum(label.astype(jnp.float32), axis=1, keepdims=True)


def first_pack_kernel(
    whole, cap, resident, adapter_ref, used_ref, tokens_ref, out_ref, target_ref, label_ref, *refs
):
    normed_ref, most_ref = refs
    lay_out(resident, adapter_ref, used_ref, most_ref, target_ref, label_ref)
    pack_kernel(
        whole, cap, 0, most_ref, target_ref, label_ref, tokens_ref, out_ref, normed_ref
    )


def pack_kernel(
    whole, cap, base, most_ref, target_ref, label_ref, tokens_ref, out_ref, normed_ref
):
    values = tokens_ref[...].astype(jnp.float32)
    mean_sq = jnp.mean(values * values, axis=-1, keepdims=True)
    normed_ref[...] = (values * lax.rsqrt(mean_sq + 1e-06)).astype(jnp.bfloat16)
    total = tokens_ref.shape[0]
    quads, tiles = out_ref.shape[0] // QUAD, whole // LANES
    lane = lanes_of(total)
    last = normed_ref[:, QUAD * whole :].astype(jnp.float32)
    label = jnp.where(lane == QUARTER, label_ref[...], 0.0)
    ends = []
    for j in range(QUAD):
        turned = pltpu.roll(last, (LANES - QUARTER * j) % LANES, 1) if j else last
        ends.append(jnp.where(lane < QUARTER, turned, label).astype(jnp.bfloat16))
    most = most_ref[0:1, 0:1].astype(jnp.float32)
    group_lane = lanes_of(QUARTER) // QUARTER
    step_lane = lanes_of(STEP)
    chosen = []
    for q in range(quads):
        place = lax.broadcasted_iota(jnp.int32, (cap, total), 0) + (q * total + base)
        chosen.append(jnp.where(target_ref[...] == place, 1.0, 0.0).astype(jnp.bfloat16))
    chosen = jnp.concatenate(chosen, axis=0)
    notes = [jnp.where(step_lane == NOTE + cap // STEP, most, 0.0)] * quads
    for j in range(QUAD):
        for t in range(tiles):
            column = j * whole + t * LANES
            if t % 2 == 0:
                count = min(2, tiles - t) * LANES
                share = jnp.dot(
                    chosen,
                    normed_ref[:, column : column + count],
                    preferred_element_type=jnp.float32,
                ).astype(jnp.bfloat16)
            for q in range(quads):
                out_ref[q * QUAD + j, t * cap : (t + 1) * cap, :] = share[
                    q * cap : (q + 1) * cap, t % 2 * LANES : (t % 2 + 1) * LANES
                ]
        end_rows = jnp.dot(chosen, ends[j], preferred_element_type=jnp.float32)
        for q in range(quads):
            end = end_rows[q * cap : (q + 1) * cap]
            if j == 0:
                for a in range(cap // STEP):
                    turned = pltpu.roll(end[a * STEP : (a + 1) * STEP], NOTE + a - QUARTER, 1)
                    notes[q] = jnp.where(step_lane == NOTE + a, turned, notes[q])
            padded = jnp.concatenate(
                [end, jnp.zeros((QUAD * QUARTER - cap, LANES), jnp.float32)], axis=0
            )
            merged = padded[0:QUARTER]
            for m in range(1, QUAD):
                turned = pltpu.roll(padded[m * QUARTER : (m + 1) * QUARTER], m * QUARTER, 1)
                merged = jnp.where(group_lane == m, turned, merged)
            out_ref[q * QUAD + j, tiles * cap : tiles * cap + STEP, :] = merged[0:STEP].astype(
                jnp.bfloat16
            )
            out_ref[q * QUAD + j, tiles * cap + STEP :, :] = jnp.where(
                step_lane >= NOTE, notes[q], merged[STEP:]
            ).astype(jnp.bfloat16)


def read_notes(rows_ref, cap, tiles, part_ref, resident, notes_ref, labels_ref, met_ref):
    senders = rows_ref.shape[0]
    for s in range(senders):
        notes_ref[s * STEP : (s + 1) * STEP, :] = rows_ref[s, tiles * cap + STEP :, :]
    steps = labels_ref.shape[0]
    row = lax.broadcasted_iota(jnp.int32, (steps, LANES), 0)
    wanted = jnp.where(lanes_of(steps) == NOTE + row, 1.0, 0.0).astype(jnp.bfloat16)
    labels = lax.dot_general(
        wanted, notes_ref[...], (((1,), (1,)), ((), ())), preferred_element_type=jnp.float32
    )
    labels_ref[...] = labels
    code = jnp.zeros((steps, 1), jnp.float32)
    for h in range(QUAD):
        first = part_ref[h].astype(jnp.float32) + 1.0
        met = jnp.where((labels >= first) & (labels < first + resident), 1.0, 0.0)
        code = code + (1 << h) * jnp.max(met, axis=1, keepdims=True)
    at = lax.broadcasted_iota(jnp.int32, (steps, 1), 0)
    for a in range(cap // STEP):
        met_ref[a] = jnp.max(jnp.where(at == a, code, 0.0)).astype(jnp.int32)


def for_holders(met_ref, first_ref, near_refs, opened_ref, halved, a, step):
    pairs = opened_ref.shape[1] // LANES
    for h in range(QUAD):
        base = first_ref[h].astype(jnp.float32) + 1.0
        firsts = [base + 2.0 * t for t in range(pairs)]
        if h in halved:
            firsts = [
                base + first_ref[QUAD + i].astype(jnp.float32) + 2.0 * t
                for i in range(2)
                for t in range(pairs // 2)
            ]

        @pl.when(lax.rem(met_ref[a] // (1 << h), 2) > 0)
        def _(h=h, firsts=firsts):
            is_first = lax.rem(met_ref[a], 1 << h) == 0
            step(near_refs[h] if h < 2 else opened_ref.at[h - 2], firsts, is_first)


def down_kernel(first_ref, rows_ref, *refs):
    near_refs, far_refs, out_ref, count_ref = refs[:2], refs[2:6], refs[6], refs[7]
    notes_ref, met_ref, opened_ref, batch_ref, picked_ref, labels_ref = refs[8:]
    senders, width = rows_ref.shape[0], batch_ref.shape[1]
    tiles = width // LANES - 1
    cap = out_ref.shape[0] * STEP
    rank = out_ref.shape[1]
    resident = opened_ref.shape[1] // rank
    dims = (((1,), (1,)), ((), ()))
    read_notes(rows_ref, cap, tiles, first_ref, resident, notes_ref, labels_ref, met_ref)
    notes = notes_ref[...].astype(jnp.float32)
    is_count = lanes_of(senders * STEP) == NOTE + cap // STEP
    count = jnp.max(jnp.where(is_count, notes, 0.0), axis=(0, 1), keepdims=True)
    count_ref[...] = jnp.broadcast_to(count, count_ref.shape).astype(jnp.bfloat16)
    open_far(far_refs, DOWN_HALVED, opened_ref)

    def one(a, carry):
        picked_ref[...] = jnp.zeros(picked_ref.shape, jnp.float32)

        @pl.when(met_ref[a] > 0)
        def _():
            shift = lax.rem(LANES - QUARTER * (a // 2), LANES)
            spot = pl.multiple_of(tiles * cap + lax.rem(a, 2) * STEP, STEP)
            for s in range(senders):
                rows = slice(s * STEP, (s + 1) * STEP)
                for t in range(tiles):
                    at = pl.multiple_of(t * cap + a * STEP, STEP)
                    batch_ref[rows, t * LANES : (t + 1) * LANES] = rows_ref[s, pl.ds(at, STEP), :]
                end = rows_ref[s, pl.ds(spot, STEP), :].astype(jnp.float32)
                batch_ref[rows, tiles * LANES :] = pltpu.roll(end, shift, 1).astype(jnp.bfloat16)
            label = labels_ref[pl.ds(a, 1), :]

            def step(weight_ref, firsts, is_first):
                product = lax.dot_general(
                    weight_ref[...], batch_ref[...], dims, preferred_element_type=jnp.float32
                )
                picked = picked_ref[...]
                for t, first in enumerate(firsts):
                    for i in range(2):
                        at = (2 * t + i) * rank
                        picked = jnp.where(
                            label == first + i, product[at : at + rank, :], picked
                        )
                picked_ref[...] = picked

            for_holders(met_ref, first_ref, near_refs, opened_ref, DOWN_HALVED, a, step)

        out_ref[a] = picked_ref[...]
        return carry

    lax.fori_loop(0, cap // STEP, one, 0)


def pair_kernel(own_ref, other_ref, out_ref):
    out_ref[...] = (own_ref[...] + other_ref[...]).astype(jnp.bfloat16)


def up_kernel(first_ref, met_ref, notes_ref, *refs):
    sum_refs, near_refs, far_refs, out_ref = refs[:2], refs[2:4], refs[4:7], refs[7]
    opened_ref, delta_ref, ends_ref, label_ref, twice_ref = refs[8:]
    senders, width = out_ref.shape[0], opened_ref.shape[2]
    tiles = width // LANES - 1
    rank = sum_refs[0].shape[1]
    kept = (out_ref.shape[1] - QUARTER) // tiles
    group_lane = lanes_of(STEP) // QUARTER
    open_far(far_refs, UP_HALVED, opened_ref)
    ends_ref[...] = jnp.zeros(ends_ref.shape, jnp.float32)
    low = jnp.where(lanes_of(senders * STEP) < HALF, 0.0, 1.0)
    rank_row = lax.broadcasted_iota(jnp.int32, (rank, LANES), 0)
    twofold = jnp.where(lax.rem(lanes_of(rank), rank) == rank_row, 1.0, 0.0).astype(jnp.bfloat16)

    note_row = lax.broadcasted_iota(jnp.int32, (LANES, LANES), 0)
    for a in range(kept // STEP):
        wanted = jnp.where(note_row == NOTE + a, 1.0, 0.0).astype(jnp.bfloat16)
        label_ref[a] = jnp.dot(notes_ref[...], wanted, preferred_element_type=jnp.float32) - low
        down = sum_refs[0][a].astype(jnp.float32) + sum_refs[1][a].astype(jnp.float32)
        twice_ref[a] = lax.dot_general(
            down.astype(jnp.bfloat16),
            twofold,
            (((0,), (0,)), ((), ())),
            preferred_element_type=jnp.float32,
        )

    def one(a, carry):
        @pl.when(met_ref[a] == 0)
        def _():
            delta_ref[...] = jnp.zeros(delta_ref.shape, jnp.float32)

        @pl.when(met_ref[a] > 0)
        def _():
            label, twice = label_ref[a], twice_ref[a]

            def step(weight_ref, firsts, is_first):
                placed = [jnp.where(label == first, twice, 0.0) for first in firsts]
                placed = jnp.concatenate(placed, axis=1).astype(jnp.bfloat16)
                before = jnp.where(is_first, 0.0, delta_ref[...])
                delta_ref[...] = before + jnp.dot(
                    placed, weight_ref[...], preferred_element_type=jnp.float32
                )

            for_holders(met_ref, first_ref, near_refs, opened_ref, UP_HALVED, a, step)

        spot = pl.multiple_of(lax.rem(a, 2) * STEP, STEP)
        for s in range(senders):
            rows = slice(s * STEP, (s + 1) * STEP)
            for t in range(tiles):
                at = pl.multiple_of(t * kept + a * STEP, STEP)
                out_ref[s, pl.ds(at, STEP), :] = delta_ref[
                    rows, t * LANES : (t + 1) * LANES
                ].astype(jnp.bfloat16)
            turned = pltpu.roll(delta_ref[rows, tiles * LANES :], QUARTER * (a // 2), 1)
            ends_ref[s, pl.ds(spot, STEP), :] = jnp.where(
                group_lane == a // 2, turned, ends_ref[s, pl.ds(spot, STEP), :]
            )
        return carry

    lax.fori_loop(0, kept // STEP, one, 0)
    for s in range(senders):
        out_ref[s, tiles * kept :, :] = ends_ref[s].astype(jnp.bfloat16)


def mix_kernel(whole, bases, target_ref, tokens_ref, *refs):
    returned_refs, out_ref = refs[:-1], refs[-1]
    total = tokens_ref.shape[0]
    tiles, quads = whole // LANES, returned_refs[0].shape[0] // QUAD
    lane = lanes_of(total)
    chosen = []
    for base, ref in zip(bases, returned_refs):
        kept = (ref.shape[1] - QUARTER) // tiles
        spot = lax.broadcasted_iota(jnp.int32, (total, quads * kept), 1)
        place = spot // kept * total + spot % kept + base
        chosen.append(jnp.where(target_ref[...] == place, 1.0, 0.0).astype(jnp.bfloat16))
    end = jnp.zeros((total, LANES), jnp.float32)
    for j in range(QUAD):
        delta = 0.0
        for choice, ref in zip(chosen, returned_refs):
            kept = choice.shape[1] // quads
            shares = []
            for q in range(quads):
                d = q * QUAD + j
                parts = [ref[d, t * kept : (t + 1) * kept, :] for t in range(tiles)]
                packed = ref[d, tiles * kept :, :].astype(jnp.float32)
                groups = [packed]
                for m in range(1, QUAD):
                    groups.append(pltpu.roll(packed, LANES - QUARTER * m, 1))
                parts.append(jnp.concatenate(groups, axis=0)[0:kept].astype(jnp.bfloat16))
                shares.append(jnp.concatenate(parts, axis=1))
            share = jnp.concatenate(shares, axis=0)
            delta = delta + jnp.dot(choice, share, preferred_element_type=jnp.float32)
        columns = slice(j * whole, (j + 1) * whole)
        out_ref[:, columns] = (
            tokens_ref[:, columns].astype(jnp.float32) + delta[:, 0:whole]
        ).astype(jnp.bfloat16)
        last = delta[:, whole:]
        turned = pltpu.roll(last, QUARTER * j, 1) if j else last
        end = jnp.where((lane >= QUARTER * j) & (lane < QUARTER * (j + 1)), turned, end)
    out_ref[:, QUAD * whole :] = (
        tokens_ref[:, QUAD * whole :].astype(jnp.float32) + end
    ).astype(jnp.bfloat16)


def call(kernel, out_shape, in_specs, flops, moved, after=(), scratch=(), out_specs=None):
    many = isinstance(out_shape, list)
    skipped = len(after)
    body = (lambda *refs: kernel(*refs[skipped:])) if skipped else kernel
    run = pl.pallas_call(
        body,
        out_shape=out_shape,
        in_specs=[pl.BlockSpec(memory_space=pl.ANY)] * skipped + in_specs,
        out_specs=out_specs or ([VMEM] * len(out_shape) if many else VMEM),
        scratch_shapes=scratch,
        compiler_params=pltpu.CompilerParams(vmem_limit_bytes=48 * 2**20),
        cost_estimate=pl.CostEstimate(flops=flops, bytes_accessed=moved, transcendentals=0),
    )
    return functools.partial(run, *after)


def exchange(value):
    return lax.all_to_all(value, "adapter", split_axis=0, concat_axis=0, tiled=True)


def towards(value, k, devices):
    return lax.ppermute(value, "adapter", [(i, i ^ k) for i in range(devices)])


def swapped(value):
    return lax.ppermute(value, "groups", [(0, 1), (1, 0)])


def stand_behind(value, *earlier):
    return pl.pallas_call(
        lambda *refs: None,
        out_shape=jax.ShapeDtypeStruct(value.shape, value.dtype),
        in_specs=[pl.BlockSpec(memory_space=pl.ANY)] * (1 + len(earlier)),
        out_specs=pl.BlockSpec(memory_space=pl.ANY),
        input_output_aliases={0: 0},
    )(value, *earlier)


def first_pack_call(cap, whole, devices, resident, adapter, used, tokens):
    blocks, rows, width = tokens.shape
    total = blocks * rows
    return call(
        functools.partial(first_pack_kernel, whole, cap, resident),
        [
            jax.ShapeDtypeStruct((devices, whole // LANES * cap + QUARTER, LANES), jnp.bfloat16),
            jax.ShapeDtypeStruct((1, total), jnp.int32),
            jax.ShapeDtypeStruct((total, 1), jnp.float32),
        ],
        [VMEM, VMEM, VMEM],
        2 * devices * cap * total * whole,
        2 * (total * width + devices * cap * whole),
        scratch=[pltpu.VMEM((total, width), jnp.bfloat16), pltpu.VMEM((8, LANES), jnp.int32)],
    )(adapter.reshape(1, blocks), used.reshape(1, blocks), tokens.reshape(total, width))


def pack_call(cap, base, whole, devices, target, label, tokens):
    blocks, rows, width = tokens.shape
    total = blocks * rows
    return call(
        functools.partial(pack_kernel, whole, cap, base),
        jax.ShapeDtypeStruct((devices, whole // LANES * cap + QUARTER, LANES), jnp.bfloat16),
        [VMEM, VMEM, VMEM, VMEM],
        2 * devices * cap * total * whole,
        2 * (total * width + devices * cap * whole),
        scratch=[pltpu.VMEM((total, width), jnp.bfloat16)],
    )(jnp.zeros((8, LANES), jnp.int32), target, label, tokens.reshape(total, width))


def down_call(cap, first, arrived, down_weights, after):
    devices = arrived.shape[0]
    columns, share = down_weights[0].shape
    return call(
        down_kernel,
        [
            jax.ShapeDtypeStruct((cap // STEP, HALF, devices * STEP), jnp.float32),
            jax.ShapeDtypeStruct((STEP, LANES), jnp.bfloat16),
            jax.ShapeDtypeStruct((devices * STEP, LANES), jnp.bfloat16),
            jax.ShapeDtypeStruct((8,), jnp.int32),
        ],
        [SMEM] + [VMEM] * (1 + len(down_weights)),
        0,
        0,
        after,
        [
            pltpu.VMEM((2, columns, share), jnp.bfloat16),
            pltpu.VMEM((devices * STEP, share), jnp.bfloat16),
            pltpu.VMEM((HALF, devices * STEP), jnp.float32),
            pltpu.VMEM((8, devices * STEP), jnp.float32),
        ],
        [VMEM, VMEM, VMEM, SMEM],
    )(first, arrived, *down_weights)


def quad_sums(partial, devices):
    pair = call(
        pair_kernel, jax.ShapeDtypeStruct(partial.shape, jnp.bfloat16), [VMEM, VMEM], 0, 0
    )(partial, towards(partial, 1, devices))
    return [pair, towards(pair, 2, devices)]


def up_call(kept, first, met, notes, sums, up_weights):
    devices = notes.shape[0] // STEP
    columns, share = up_weights[0].shape
    shape = (devices, (share // LANES - 1) * kept + QUARTER, LANES)
    return call(
        up_kernel,
        jax.ShapeDtypeStruct(shape, jnp.bfloat16),
        [SMEM, SMEM] + [VMEM] * (3 + len(up_weights)),
        2 * devices * kept * QUAD * columns * share,
        2 * (2 * devices * kept + QUAD * columns) * share,
        scratch=[
            pltpu.VMEM((2, columns, share), jnp.bfloat16),
            pltpu.VMEM((devices * STEP, share), jnp.float32),
            pltpu.VMEM((devices, QUARTER, LANES), jnp.float32),
            *[pltpu.VMEM((kept // STEP, devices * STEP, LANES), jnp.float32)] * 2,
        ],
    )(first, met, notes, *sums, *up_weights)


def back_and_mix(
    kept, more, tokens, target, label, first, met, notes, sums, down_weights, up_weights, *unused
):
    blocks, rows, width = tokens.shape
    total = blocks * rows
    devices = notes.shape[0] // STEP
    whole = up_weights[0].shape[1] - LANES
    pieces = [exchange(up_call(kept, first, met, notes, sums, up_weights))]
    if more:
        outgoing = pack_call(more, kept, whole, devices, target, label, tokens)
        arrived = exchange(outgoing)
        partial, unused_count, notes, met = down_call(more, first, arrived, down_weights, [])
        sums = quad_sums(partial, devices)
        pieces.append(exchange(up_call(more, first, met, notes, sums, up_weights)))
    mixed = call(
        functools.partial(mix_kernel, whole, (0, kept)[: len(pieces)]),
        jax.ShapeDtypeStruct((total, width), jnp.bfloat16),
        [VMEM] * (2 + len(pieces)),
        2 * devices * (kept + more) * total * whole,
        2 * (2 * total * width + devices * (kept + more) * whole),
    )(target.reshape(total, 1), tokens.reshape(total, width), *pieces)
    return mixed.reshape(tokens.shape)


def start_again(
    tokens, target, label, first, met, notes, sums, down_weights, up_weights, *arguments
):
    return rows_to_holders(tokens, *arguments)


def rows_to_quads(
    tokens, request_block_adapter, request_block_rows, adapter_down_weight, adapter_up_weight
):
    blocks, rows, width = tokens.shape
    devices = lax.axis_size("adapter")
    resident, rank, unused_width = adapter_up_weight.shape
    total = blocks * rows
    columns = resident * rank
    whole = width // LANES // QUAD * LANES
    share = whole + LANES
    bf16, i32 = jnp.bfloat16, jnp.int32

    me = lax.axis_index("adapter").astype(i32)
    group = lax.axis_index("groups").astype(i32)
    parts = jnp.bitwise_xor(me % QUAD, jnp.arange(QUAD, dtype=i32))
    halves = jnp.stack([group, 1 - group]) * (resident // 2)
    first = jnp.concatenate([parts * resident, halves]).astype(i32)
    tiles = whole // LANES

    def shares(weight, which, halved, after):
        shapes = []
        for k in which:
            count = columns // 2 if k in halved else columns
            far = (count * tiles + count // QUAD, LANES)
            shapes.append(jax.ShapeDtypeStruct((columns, share) if k < 2 else far, bf16))
        return call(
            functools.partial(weight_kernel, whole, which, halved),
            shapes,
            [SMEM, SMEM, VMEM],
            0,
            len(which) * columns * width,
            after,
        )(parts, group.reshape(1), weight)

    down_weight = adapter_down_weight.transpose(0, 2, 1).reshape(columns, width)
    up_weight = adapter_up_weight.reshape(columns, width)
    down_far = shares(down_weight, (2, 3), DOWN_HALVED, [])
    up_far = shares(up_weight, (2, 3), UP_HALVED, down_far[:1])
    down_near = shares(down_weight, (0, 1), (), up_far[:1])
    up_near = shares(up_weight, (0, 1), (), down_near[:1])
    down_weights = [down_near[0], towards(down_near[1], 1, devices)]
    down_weights += [towards(value, k, devices) for k, value in zip((2, 3), down_far)]
    up_weights = [up_near[0], towards(up_near[1], 1, devices)]
    up_weights += [towards(value, k, devices) for k, value in zip((2, 3), up_far)]
    down_weights[2] = stand_behind(down_weights[2], up_near[0])
    down_weights += [swapped(down_weights[k]) for k in DOWN_HALVED]
    up_weights += [swapped(up_weights[k]) for k in UP_HALVED]

    caps = [total * 5 // 16, total * 6 // 16, total * 7 // 16]
    cap = caps[-1]
    outgoing, target, label = first_pack_call(
        cap, whole, devices, resident, request_block_adapter, request_block_rows, tokens
    )
    arrived = exchange(outgoing)
    partial, count, notes, met = down_call(cap, first, arrived, down_weights, up_weights[2:3])
    sums = quad_sums(partial, devices)
    count = count[0:1, 0:1]
    most = jnp.maximum(count, swapped(count))[0, 0].astype(jnp.float32)
    branches = [functools.partial(back_and_mix, kept, 0) for kept in caps]
    branches += [functools.partial(back_and_mix, cap, STEP), start_again]
    return lax.switch(
        sum((most > limit).astype(i32) for limit in [*caps, cap + STEP]),
        branches,
        tokens,
        target,
        label,
        first,
        met,
        notes,
        sums,
        down_weights,
        up_weights,
        request_block_adapter,
        request_block_rows,
        adapter_down_weight,
        adapter_up_weight,
    )


def solution(mesh):
    placed = (
        P(("groups", "adapter"), None, None),
        P(("groups", "adapter")),
        P(("groups", "adapter")),
        P("adapter", None, None),
        P("adapter", None, None),
    )

    def per_device(tokens, request_block_adapter, request_block_rows, down_weight, up_weight):
        blocks, rows, width = tokens.shape
        devices = mesh.shape["adapter"]
        slots = max(1, 4 * blocks // devices)
        quads = devices % QUAD == 0 and slots * QUAD >= blocks
        quads = quads and width % (QUAD * LANES) == LANES and up_weight.shape[1] == HALF
        quads = quads and blocks * rows * 7 // 16 == 7 * STEP and mesh.shape["groups"] == 2
        plan = rows_to_quads if quads else rows_to_holders
        return plan(tokens, request_block_adapter, request_block_rows, down_weight, up_weight)

    return jax.shard_map(
        per_device,
        mesh=mesh,
        in_specs=placed,
        out_specs=P(("groups", "adapter"), None, None),
        check_vma=False,
    )
```

```python
import functools

import jax
import jax.numpy as jnp
from jax import lax
from jax.experimental import pallas as pl
from jax.experimental.pallas import tpu as pltpu
from jax.sharding import PartitionSpec as P

LANES = 128
HALF = 64
QUAD = 4
QUARTER = 32
STEP = 16
NOTE = 96
DOWN_HALVED = (2, 3)
UP_HALVED = (2,)
VMEM = pl.BlockSpec(memory_space=pltpu.VMEM)
SMEM = pl.BlockSpec(memory_space=pltpu.SMEM)


def normalise(tokens):
    values = tokens.astype(jnp.float32)
    mean_sq = jnp.mean(values * values, axis=-1, keepdims=True)
    return (values, (values * lax.rsqrt(mean_sq + 1e-06)).astype(jnp.bfloat16))


def resident_update(hidden_state, block_labels, adapter_down_weight, adapter_up_weight):
    feature_width = hidden_state.shape[-1]
    leading = hidden_state.shape[:-1]
    resident_rows, unused_value, inner_rank = adapter_down_weight.shape
    flattened_tokens = hidden_state.reshape(-1, feature_width)
    down_matrix = jnp.einsum(
        "tq,iqg->tig", flattened_tokens, adapter_down_weight, preferred_element_type=jnp.float32
    )
    down_matrix = down_matrix.astype(jnp.bfloat16).reshape(
        flattened_tokens.shape[0], resident_rows * inner_rank
    )
    column_owner = jnp.arange(resident_rows * inner_rank, dtype=jnp.int32) // inner_rank
    picked = block_labels.reshape(-1, 1) == column_owner[None, :]
    down_matrix = jnp.where(picked, down_matrix, jnp.zeros_like(down_matrix))
    lowrank_update = jnp.dot(
        down_matrix,
        adapter_up_weight.reshape(resident_rows * inner_rank, feature_width),
        preferred_element_type=jnp.float32,
    )
    return lowrank_update.astype(jnp.bfloat16).reshape(leading + (feature_width,))


def rows_to_holders(
    tokens, request_block_adapter, request_block_rows, adapter_down_weight, adapter_up_weight
):
    blocks, rows, feature_width = tokens.shape
    devices = lax.axis_size("adapter")
    resident_rows = adapter_down_weight.shape[0]
    slots = max(1, 4 * blocks // devices)
    values, normed = normalise(tokens)
    owner = request_block_adapter // resident_rows
    within = request_block_adapter - owner * resident_rows
    serial = jnp.arange(blocks, dtype=jnp.int32)
    earlier = (owner[:, None] == owner[None, :]) & (serial[None, :] < serial[:, None])
    position = owner * slots + jnp.sum(earlier, axis=1)
    outgoing = (
        jnp.zeros((devices * slots, rows, feature_width), jnp.bfloat16).at[position].set(normed)
    )
    outgoing = outgoing.reshape(devices, slots, rows, feature_width)
    block_labels = jnp.full((devices * slots,), -1, jnp.int32).at[position].set(within)
    block_labels = jnp.broadcast_to(block_labels[:, None], (devices * slots, rows)).reshape(
        devices, slots, rows
    )
    arriving_rows, row_markers = (
        lax.all_to_all(outgoing, "adapter", split_axis=0, concat_axis=0, tiled=True),
        lax.all_to_all(block_labels, "adapter", split_axis=0, concat_axis=0, tiled=True),
    )
    lowrank_update = resident_update(
        arriving_rows, row_markers, adapter_down_weight, adapter_up_weight
    )
    returned = lax.all_to_all(lowrank_update, "adapter", split_axis=0, concat_axis=0, tiled=True)
    mine = returned.reshape(devices * slots, rows, feature_width)[position]
    live = jnp.arange(rows, dtype=jnp.int32)[None, :] < request_block_rows[:, None]
    mixed = values + jnp.where(live[:, :, None], mine.astype(jnp.float32), jnp.float32(0.0))
    return mixed.astype(jnp.bfloat16)


def lanes_of(rows):
    return lax.broadcasted_iota(jnp.int32, (rows, LANES), 1)


def weight_kernel(whole, which, halved, part_ref, group_ref, weight_ref, *out_refs):
    tiles = whole // LANES
    for k, out_ref in zip(which, out_refs):
        j = part_ref[k]
        if k < 2:
            last = weight_ref[:, QUAD * whole :].astype(jnp.float32)
            turned = pltpu.roll(last, lax.rem(LANES - QUARTER * j, LANES), 1)
            inside = lanes_of(last.shape[0]) < QUARTER
            out_ref[:, 0:whole] = weight_ref[:, pl.ds(pl.multiple_of(j * whole, LANES), whole)]
            out_ref[:, whole:] = jnp.where(inside, turned, 0.0).astype(jnp.bfloat16)
            continue
        count = weight_ref.shape[0] // 2 if k in halved else weight_ref.shape[0]
        start = pl.multiple_of(group_ref[0] * count, count) if k in halved else 0
        for t in range(tiles):
            column = pl.multiple_of(j * whole + t * LANES, LANES)
            out_ref[t * count : (t + 1) * count, :] = weight_ref[
                pl.ds(start, count), pl.ds(column, LANES)
            ]
        last = weight_ref[pl.ds(start, count), QUAD * whole :].astype(jnp.float32)
        size = count // QUAD
        owner = lanes_of(size) // QUARTER
        merged = jnp.zeros((size, LANES), jnp.float32)
        for m in range(QUAD):
            shift = lax.rem(LANES + QUARTER * (m - j), LANES)
            turned = pltpu.roll(last[m * size : (m + 1) * size], shift, 1)
            merged = jnp.where(owner == m, turned, merged)
        out_ref[tiles * count :, :] = merged.astype(jnp.bfloat16)


def open_far(far_refs, halved, opened_ref):
    width = opened_ref.shape[2]
    tiles = width // LANES - 1
    places = [(k - 2, 0) for k in (2, 3)] + [(k - 2, 1) for k in halved]
    for ref, (holder, part) in zip(far_refs, places):
        count = opened_ref.shape[1] // 2 if holder + 2 in halved else opened_ref.shape[1]
        base, size = part * count, count // QUAD
        inside = lanes_of(size) < QUARTER
        for t in range(tiles):
            opened_ref[holder, base : base + count, t * LANES : (t + 1) * LANES] = ref[
                t * count : (t + 1) * count, :
            ]
        packed = ref[tiles * count :, :].astype(jnp.float32)
        for m in range(QUAD):
            turned = pltpu.roll(packed, (LANES - QUARTER * m) % LANES, 1) if m else packed
            opened_ref[holder, base + m * size : base + (m + 1) * size, tiles * LANES :] = (
                jnp.where(inside, turned, 0.0).astype(jnp.bfloat16)
            )


def lay_out(resident, adapter_ref, used_ref, most_ref, target_ref, label_ref):
    blocks, total = adapter_ref.shape[1], target_ref.shape[1]
    rows = total // blocks
    adapter, used = adapter_ref[...], used_ref[...]
    down = lax.broadcasted_iota(jnp.int32, (blocks, blocks), 0)
    across = lax.broadcasted_iota(jnp.int32, (blocks, blocks), 1)

    def turned(value):
        return jnp.sum(jnp.where(down == across, value, 0), axis=1, keepdims=True)

    span = resident * QUAD
    quad = jnp.floor((adapter.astype(jnp.float32) + 0.5) * (1.0 / span)).astype(jnp.int32)
    order = adapter * blocks + lax.broadcasted_iota(jnp.int32, (1, blocks), 1)
    quad_down, order_down, used_down = turned(quad), turned(order), turned(used)
    same = quad_down == quad
    ahead = jnp.sum(jnp.where(same & (order < order_down), used, 0), axis=1, keepdims=True)
    within = jnp.sum(jnp.where(same, used, 0), axis=1, keepdims=True)
    most_ref[...] = jnp.broadcast_to(jnp.max(within, axis=0, keepdims=True), most_ref.shape)
    start = quad_down * total + ahead

    block = lax.broadcasted_iota(jnp.int32, (blocks, total), 0)
    row = lax.broadcasted_iota(jnp.int32, (blocks, total), 1) - block * rows
    place = jnp.where((row >= 0) & (row < used_down), start + row + 1, 0)
    target_ref[...] = jnp.sum(place, axis=0, keepdims=True) - 1
    block = lax.broadcasted_iota(jnp.int32, (total, blocks), 1)
    row = lax.broadcasted_iota(jnp.int32, (total, blocks), 0) - block * rows
    label = jnp.where((row >= 0) & (row < rows), adapter - quad * span + 1, 0)
    label_ref[...] = jnp.sum(label.astype(jnp.float32), axis=1, keepdims=True)


def first_pack_kernel(
    whole, cap, resident, adapter_ref, used_ref, tokens_ref, out_ref, target_ref, label_ref, *refs
):
    normed_ref, most_ref = refs
    lay_out(resident, adapter_ref, used_ref, most_ref, target_ref, label_ref)
    pack_kernel(
        whole, cap, 0, most_ref, target_ref, label_ref, tokens_ref, out_ref, normed_ref
    )


def pack_kernel(
    whole, cap, base, most_ref, target_ref, label_ref, tokens_ref, out_ref, normed_ref
):
    values = tokens_ref[...].astype(jnp.float32)
    mean_sq = jnp.mean(values * values, axis=-1, keepdims=True)
    normed_ref[...] = (values * lax.rsqrt(mean_sq + 1e-06)).astype(jnp.bfloat16)
    total = tokens_ref.shape[0]
    quads, tiles = out_ref.shape[0] // QUAD, whole // LANES
    lane = lanes_of(total)
    last = normed_ref[:, QUAD * whole :].astype(jnp.float32)
    label = jnp.where(lane == QUARTER, label_ref[...], 0.0)
    ends = []
    for j in range(QUAD):
        turned = pltpu.roll(last, (LANES - QUARTER * j) % LANES, 1) if j else last
        ends.append(jnp.where(lane < QUARTER, turned, label).astype(jnp.bfloat16))
    most = most_ref[0:1, 0:1].astype(jnp.float32)
    group_lane = lanes_of(QUARTER) // QUARTER
    step_lane = lanes_of(STEP)
    chosen = []
    for q in range(quads):
        place = lax.broadcasted_iota(jnp.int32, (cap, total), 0) + (q * total + base)
        chosen.append(jnp.where(target_ref[...] == place, 1.0, 0.0).astype(jnp.bfloat16))
    chosen = jnp.concatenate(chosen, axis=0)
    notes = [jnp.where(step_lane == NOTE + cap // STEP, most, 0.0)] * quads
    for j in range(QUAD):
        for t in range(tiles):
            column = j * whole + t * LANES
            if t % 2 == 0:
                count = min(2, tiles - t) * LANES
                share = jnp.dot(
                    chosen,
                    normed_ref[:, column : column + count],
                    preferred_element_type=jnp.float32,
                ).astype(jnp.bfloat16)
            for q in range(quads):
                out_ref[q * QUAD + j, t * cap : (t + 1) * cap, :] = share[
                    q * cap : (q + 1) * cap, t % 2 * LANES : (t % 2 + 1) * LANES
                ]
        end_rows = jnp.dot(chosen, ends[j], preferred_element_type=jnp.float32)
        for q in range(quads):
            end = end_rows[q * cap : (q + 1) * cap]
            if j == 0:
                for a in range(cap // STEP):
                    turned = pltpu.roll(end[a * STEP : (a + 1) * STEP], NOTE + a - QUARTER, 1)
                    notes[q] = jnp.where(step_lane == NOTE + a, turned, notes[q])
            padded = jnp.concatenate(
                [end, jnp.zeros((QUAD * QUARTER - cap, LANES), jnp.float32)], axis=0
            )
            merged = padded[0:QUARTER]
            for m in range(1, QUAD):
                turned = pltpu.roll(padded[m * QUARTER : (m + 1) * QUARTER], m * QUARTER, 1)
                merged = jnp.where(group_lane == m, turned, merged)
            out_ref[q * QUAD + j, tiles * cap : tiles * cap + STEP, :] = merged[0:STEP].astype(
                jnp.bfloat16
            )
            out_ref[q * QUAD + j, tiles * cap + STEP :, :] = jnp.where(
                step_lane >= NOTE, notes[q], merged[STEP:]
            ).astype(jnp.bfloat16)


def read_notes(rows_ref, cap, tiles, part_ref, resident, notes_ref, labels_ref, met_ref):
    senders = rows_ref.shape[0]
    for s in range(senders):
        notes_ref[s * STEP : (s + 1) * STEP, :] = rows_ref[s, tiles * cap + STEP :, :]
    steps = labels_ref.shape[0]
    row = lax.broadcasted_iota(jnp.int32, (steps, LANES), 0)
    wanted = jnp.where(lanes_of(steps) == NOTE + row, 1.0, 0.0).astype(jnp.bfloat16)
    labels = lax.dot_general(
        wanted, notes_ref[...], (((1,), (1,)), ((), ())), preferred_element_type=jnp.float32
    )
    labels_ref[...] = labels
    code = jnp.zeros((steps, 1), jnp.float32)
    for h in range(QUAD):
        first = part_ref[h].astype(jnp.float32) + 1.0
        met = jnp.where((labels >= first) & (labels < first + resident), 1.0, 0.0)
        code = code + (1 << h) * jnp.max(met, axis=1, keepdims=True)
    at = lax.broadcasted_iota(jnp.int32, (steps, 1), 0)
    for a in range(cap // STEP):
        met_ref[a] = jnp.max(jnp.where(at == a, code, 0.0)).astype(jnp.int32)


def for_holders(met_ref, first_ref, near_refs, opened_ref, halved, a, step):
    pairs = opened_ref.shape[1] // LANES
    for h in range(QUAD):
        base = first_ref[h].astype(jnp.float32) + 1.0
        firsts = [base + 2.0 * t for t in range(pairs)]
        if h in halved:
            firsts = [
                base + first_ref[QUAD + i].astype(jnp.float32) + 2.0 * t
                for i in range(2)
                for t in range(pairs // 2)
            ]

        @pl.when(lax.rem(met_ref[a] // (1 << h), 2) > 0)
        def _(h=h, firsts=firsts):
            is_first = lax.rem(met_ref[a], 1 << h) == 0
            step(near_refs[h] if h < 2 else opened_ref.at[h - 2], firsts, is_first)


def down_kernel(first_ref, rows_ref, *refs):
    near_refs, far_refs, out_ref, count_ref = refs[:2], refs[2:6], refs[6], refs[7]
    notes_ref, met_ref, opened_ref, batch_ref, picked_ref, labels_ref = refs[8:]
    senders, width = rows_ref.shape[0], batch_ref.shape[1]
    tiles = width // LANES - 1
    cap = out_ref.shape[0] * STEP
    rank = out_ref.shape[1]
    resident = opened_ref.shape[1] // rank
    dims = (((1,), (1,)), ((), ()))
    read_notes(rows_ref, cap, tiles, first_ref, resident, notes_ref, labels_ref, met_ref)
    notes = notes_ref[...].astype(jnp.float32)
    is_count = lanes_of(senders * STEP) == NOTE + cap // STEP
    count = jnp.max(jnp.where(is_count, notes, 0.0), axis=(0, 1), keepdims=True)
    count_ref[...] = jnp.broadcast_to(count, count_ref.shape).astype(jnp.bfloat16)
    open_far(far_refs, DOWN_HALVED, opened_ref)

    def one(a, carry):
        picked_ref[...] = jnp.zeros(picked_ref.shape, jnp.float32)

        @pl.when(met_ref[a] > 0)
        def _():
            shift = lax.rem(LANES - QUARTER * (a // 2), LANES)
            spot = pl.multiple_of(tiles * cap + lax.rem(a, 2) * STEP, STEP)
            for s in range(senders):
                rows = slice(s * STEP, (s + 1) * STEP)
                for t in range(tiles):
                    at = pl.multiple_of(t * cap + a * STEP, STEP)
                    batch_ref[rows, t * LANES : (t + 1) * LANES] = rows_ref[s, pl.ds(at, STEP), :]
                end = rows_ref[s, pl.ds(spot, STEP), :].astype(jnp.float32)
                batch_ref[rows, tiles * LANES :] = pltpu.roll(end, shift, 1).astype(jnp.bfloat16)
            label = labels_ref[pl.ds(a, 1), :]

            def step(weight_ref, firsts, is_first):
                product = lax.dot_general(
                    weight_ref[...], batch_ref[...], dims, preferred_element_type=jnp.float32
                )
                picked = picked_ref[...]
                for t, first in enumerate(firsts):
                    for i in range(2):
                        at = (2 * t + i) * rank
                        picked = jnp.where(
                            label == first + i, product[at : at + rank, :], picked
                        )
                picked_ref[...] = picked

            for_holders(met_ref, first_ref, near_refs, opened_ref, DOWN_HALVED, a, step)

        out_ref[a] = picked_ref[...]
        return carry

    lax.fori_loop(0, cap // STEP, one, 0)


def pair_kernel(own_ref, other_ref, out_ref):
    out_ref[...] = (own_ref[...] + other_ref[...]).astype(jnp.bfloat16)


def up_kernel(first_ref, met_ref, notes_ref, *refs):
    sum_refs, near_refs, far_refs, out_ref = refs[:2], refs[2:4], refs[4:7], refs[7]
    opened_ref, delta_ref, ends_ref, label_ref, twice_ref = refs[8:]
    senders, width = out_ref.shape[0], opened_ref.shape[2]
    tiles = width // LANES - 1
    rank = sum_refs[0].shape[1]
    kept = (out_ref.shape[1] - QUARTER) // tiles
    group_lane = lanes_of(STEP) // QUARTER
    open_far(far_refs, UP_HALVED, opened_ref)
    ends_ref[...] = jnp.zeros(ends_ref.shape, jnp.float32)
    low = jnp.where(lanes_of(senders * STEP) < HALF, 0.0, 1.0)
    rank_row = lax.broadcasted_iota(jnp.int32, (rank, LANES), 0)
    twofold = jnp.where(lax.rem(lanes_of(rank), rank) == rank_row, 1.0, 0.0).astype(jnp.bfloat16)

    note_row = lax.broadcasted_iota(jnp.int32, (LANES, LANES), 0)
    for a in range(kept // STEP):
        wanted = jnp.where(note_row == NOTE + a, 1.0, 0.0).astype(jnp.bfloat16)
        label_ref[a] = jnp.dot(notes_ref[...], wanted, preferred_element_type=jnp.float32) - low
        down = sum_refs[0][a].astype(jnp.float32) + sum_refs[1][a].astype(jnp.float32)
        twice_ref[a] = lax.dot_general(
            down.astype(jnp.bfloat16),
            twofold,
            (((0,), (0,)), ((), ())),
            preferred_element_type=jnp.float32,
        )

    def one(a, carry):
        @pl.when(met_ref[a] == 0)
        def _():
            delta_ref[...] = jnp.zeros(delta_ref.shape, jnp.float32)

        @pl.when(met_ref[a] > 0)
        def _():
            label, twice = label_ref[a], twice_ref[a]

            def step(weight_ref, firsts, is_first):
                placed = [jnp.where(label == first, twice, 0.0) for first in firsts]
                placed = jnp.concatenate(placed, axis=1).astype(jnp.bfloat16)
                before = jnp.where(is_first, 0.0, delta_ref[...])
                delta_ref[...] = before + jnp.dot(
                    placed, weight_ref[...], preferred_element_type=jnp.float32
                )

            for_holders(met_ref, first_ref, near_refs, opened_ref, UP_HALVED, a, step)

        spot = pl.multiple_of(lax.rem(a, 2) * STEP, STEP)
        for s in range(senders):
            rows = slice(s * STEP, (s + 1) * STEP)
            for t in range(tiles):
                at = pl.multiple_of(t * kept + a * STEP, STEP)
                out_ref[s, pl.ds(at, STEP), :] = delta_ref[
                    rows, t * LANES : (t + 1) * LANES
                ].astype(jnp.bfloat16)
            turned = pltpu.roll(delta_ref[rows, tiles * LANES :], QUARTER * (a // 2), 1)
            ends_ref[s, pl.ds(spot, STEP), :] = jnp.where(
                group_lane == a // 2, turned, ends_ref[s, pl.ds(spot, STEP), :]
            )
        return carry

    lax.fori_loop(0, kept // STEP, one, 0)
    for s in range(senders):
        out_ref[s, tiles * kept :, :] = ends_ref[s].astype(jnp.bfloat16)


def mix_kernel(whole, bases, target_ref, tokens_ref, *refs):
    returned_refs, out_ref = refs[:-1], refs[-1]
    total = tokens_ref.shape[0]
    tiles, quads = whole // LANES, returned_refs[0].shape[0] // QUAD
    lane = lanes_of(total)
    chosen = []
    for base, ref in zip(bases, returned_refs):
        kept = (ref.shape[1] - QUARTER) // tiles
        spot = lax.broadcasted_iota(jnp.int32, (total, quads * kept), 1)
        place = spot // kept * total + spot % kept + base
        chosen.append(jnp.where(target_ref[...] == place, 1.0, 0.0).astype(jnp.bfloat16))
    end = jnp.zeros((total, LANES), jnp.float32)
    for j in range(QUAD):
        delta = 0.0
        for choice, ref in zip(chosen, returned_refs):
            kept = choice.shape[1] // quads
            shares = []
            for q in range(quads):
                d = q * QUAD + j
                parts = [ref[d, t * kept : (t + 1) * kept, :] for t in range(tiles)]
                packed = ref[d, tiles * kept :, :].astype(jnp.float32)
                groups = [packed]
                for m in range(1, QUAD):
                    groups.append(pltpu.roll(packed, LANES - QUARTER * m, 1))
                parts.append(jnp.concatenate(groups, axis=0)[0:kept].astype(jnp.bfloat16))
                shares.append(jnp.concatenate(parts, axis=1))
            share = jnp.concatenate(shares, axis=0)
            delta = delta + jnp.dot(choice, share, preferred_element_type=jnp.float32)
        columns = slice(j * whole, (j + 1) * whole)
        out_ref[:, columns] = (
            tokens_ref[:, columns].astype(jnp.float32) + delta[:, 0:whole]
        ).astype(jnp.bfloat16)
        last = delta[:, whole:]
        turned = pltpu.roll(last, QUARTER * j, 1) if j else last
        end = jnp.where((lane >= QUARTER * j) & (lane < QUARTER * (j + 1)), turned, end)
    out_ref[:, QUAD * whole :] = (
        tokens_ref[:, QUAD * whole :].astype(jnp.float32) + end
    ).astype(jnp.bfloat16)


def call(kernel, out_shape, in_specs, flops, moved, after=(), scratch=(), out_specs=None):
    many = isinstance(out_shape, list)
    skipped = len(after)
    body = (lambda *refs: kernel(*refs[skipped:])) if skipped else kernel
    run = pl.pallas_call(
        body,
        out_shape=out_shape,
        in_specs=[pl.BlockSpec(memory_space=pl.ANY)] * skipped + in_specs,
        out_specs=out_specs or ([VMEM] * len(out_shape) if many else VMEM),
        scratch_shapes=scratch,
        compiler_params=pltpu.CompilerParams(vmem_limit_bytes=28 * 2**20),
        cost_estimate=pl.CostEstimate(flops=flops, bytes_accessed=moved, transcendentals=0),
    )
    return functools.partial(run, *after)


def exchange(value):
    return lax.all_to_all(value, "adapter", split_axis=0, concat_axis=0, tiled=True)


def towards(value, k, devices):
    return lax.ppermute(value, "adapter", [(i, i ^ k) for i in range(devices)])


def swapped(value):
    return lax.ppermute(value, "groups", [(0, 1), (1, 0)])


def stand_behind(value, *earlier):
    return pl.pallas_call(
        lambda *refs: None,
        out_shape=jax.ShapeDtypeStruct(value.shape, value.dtype),
        in_specs=[pl.BlockSpec(memory_space=pl.ANY)] * (1 + len(earlier)),
        out_specs=pl.BlockSpec(memory_space=pl.ANY),
        input_output_aliases={0: 0},
    )(value, *earlier)


def first_pack_call(cap, whole, devices, resident, adapter, used, tokens):
    blocks, rows, width = tokens.shape
    total = blocks * rows
    return call(
        functools.partial(first_pack_kernel, whole, cap, resident),
        [
            jax.ShapeDtypeStruct((devices, whole // LANES * cap + QUARTER, LANES), jnp.bfloat16),
            jax.ShapeDtypeStruct((1, total), jnp.int32),
            jax.ShapeDtypeStruct((total, 1), jnp.float32),
        ],
        [VMEM, VMEM, VMEM],
        2 * devices * cap * total * whole,
        2 * (total * width + devices * cap * whole),
        scratch=[pltpu.VMEM((total, width), jnp.bfloat16), pltpu.VMEM((8, LANES), jnp.int32)],
    )(adapter.reshape(1, blocks), used.reshape(1, blocks), tokens.reshape(total, width))


def pack_call(cap, base, whole, devices, target, label, tokens):
    blocks, rows, width = tokens.shape
    total = blocks * rows
    return call(
        functools.partial(pack_kernel, whole, cap, base),
        jax.ShapeDtypeStruct((devices, whole // LANES * cap + QUARTER, LANES), jnp.bfloat16),
        [VMEM, VMEM, VMEM, VMEM],
        2 * devices * cap * total * whole,
        2 * (total * width + devices * cap * whole),
        scratch=[pltpu.VMEM((total, width), jnp.bfloat16)],
    )(jnp.zeros((8, LANES), jnp.int32), target, label, tokens.reshape(total, width))


def down_call(cap, first, arrived, down_weights, after):
    devices = arrived.shape[0]
    columns, share = down_weights[0].shape
    return call(
        down_kernel,
        [
            jax.ShapeDtypeStruct((cap // STEP, HALF, devices * STEP), jnp.float32),
            jax.ShapeDtypeStruct((STEP, LANES), jnp.bfloat16),
            jax.ShapeDtypeStruct((devices * STEP, LANES), jnp.bfloat16),
            jax.ShapeDtypeStruct((8,), jnp.int32),
        ],
        [SMEM] + [VMEM] * (1 + len(down_weights)),
        0,
        0,
        after,
        [
            pltpu.VMEM((2, columns, share), jnp.bfloat16),
            pltpu.VMEM((devices * STEP, share), jnp.bfloat16),
            pltpu.VMEM((HALF, devices * STEP), jnp.float32),
            pltpu.VMEM((8, devices * STEP), jnp.float32),
        ],
        [VMEM, VMEM, VMEM, SMEM],
    )(first, arrived, *down_weights)


def quad_sums(partial, devices):
    pair = call(
        pair_kernel, jax.ShapeDtypeStruct(partial.shape, jnp.bfloat16), [VMEM, VMEM], 0, 0
    )(partial, towards(partial, 1, devices))
    return [pair, towards(pair, 2, devices)]


def up_call(kept, first, met, notes, sums, up_weights):
    devices = notes.shape[0] // STEP
    columns, share = up_weights[0].shape
    shape = (devices, (share // LANES - 1) * kept + QUARTER, LANES)
    return call(
        up_kernel,
        jax.ShapeDtypeStruct(shape, jnp.bfloat16),
        [SMEM, SMEM] + [VMEM] * (3 + len(up_weights)),
        2 * devices * kept * QUAD * columns * share,
        2 * (2 * devices * kept + QUAD * columns) * share,
        scratch=[
            pltpu.VMEM((2, columns, share), jnp.bfloat16),
            pltpu.VMEM((devices * STEP, share), jnp.float32),
            pltpu.VMEM((devices, QUARTER, LANES), jnp.float32),
            *[pltpu.VMEM((kept // STEP, devices * STEP, LANES), jnp.float32)] * 2,
        ],
    )(first, met, notes, *sums, *up_weights)


def back_and_mix(
    kept, more, tokens, target, label, first, met, notes, sums, down_weights, up_weights, *unused
):
    blocks, rows, width = tokens.shape
    total = blocks * rows
    devices = notes.shape[0] // STEP
    whole = up_weights[0].shape[1] - LANES
    pieces = [exchange(up_call(kept, first, met, notes, sums, up_weights))]
    if more:
        outgoing = pack_call(more, kept, whole, devices, target, label, tokens)
        arrived = exchange(outgoing)
        partial, unused_count, notes, met = down_call(more, first, arrived, down_weights, [])
        sums = quad_sums(partial, devices)
        pieces.append(exchange(up_call(more, first, met, notes, sums, up_weights)))
    mixed = call(
        functools.partial(mix_kernel, whole, (0, kept)[: len(pieces)]),
        jax.ShapeDtypeStruct((total, width), jnp.bfloat16),
        [VMEM] * (2 + len(pieces)),
        2 * devices * (kept + more) * total * whole,
        2 * (2 * total * width + devices * (kept + more) * whole),
    )(target.reshape(total, 1), tokens.reshape(total, width), *pieces)
    return mixed.reshape(tokens.shape)


def start_again(
    tokens, target, label, first, met, notes, sums, down_weights, up_weights, *arguments
):
    return rows_to_holders(tokens, *arguments)


def rows_to_quads(
    tokens, request_block_adapter, request_block_rows, adapter_down_weight, adapter_up_weight
):
    blocks, rows, width = tokens.shape
    devices = lax.axis_size("adapter")
    resident, rank, unused_width = adapter_up_weight.shape
    total = blocks * rows
    columns = resident * rank
    whole = width // LANES // QUAD * LANES
    share = whole + LANES
    bf16, i32 = jnp.bfloat16, jnp.int32

    me = lax.axis_index("adapter").astype(i32)
    group = lax.axis_index("groups").astype(i32)
    parts = jnp.bitwise_xor(me % QUAD, jnp.arange(QUAD, dtype=i32))
    halves = jnp.stack([group, 1 - group]) * (resident // 2)
    first = jnp.concatenate([parts * resident, halves]).astype(i32)
    tiles = whole // LANES

    def shares(weight, which, halved, after):
        shapes = []
        for k in which:
            count = columns // 2 if k in halved else columns
            far = (count * tiles + count // QUAD, LANES)
            shapes.append(jax.ShapeDtypeStruct((columns, share) if k < 2 else far, bf16))
        return call(
            functools.partial(weight_kernel, whole, which, halved),
            shapes,
            [SMEM, SMEM, VMEM],
            0,
            len(which) * columns * width,
            after,
        )(parts, group.reshape(1), weight)

    down_weight = adapter_down_weight.transpose(0, 2, 1).reshape(columns, width)
    up_weight = adapter_up_weight.reshape(columns, width)
    down_far = shares(down_weight, (2, 3), DOWN_HALVED, [])
    up_far = shares(up_weight, (2, 3), UP_HALVED, down_far[:1])
    down_near = shares(down_weight, (0, 1), (), up_far[:1])
    up_near = shares(up_weight, (0, 1), (), down_near[:1])
    down_weights = [down_near[0], towards(down_near[1], 1, devices)]
    down_weights += [towards(value, k, devices) for k, value in zip((2, 3), down_far)]
    up_weights = [up_near[0], towards(up_near[1], 1, devices)]
    up_weights += [towards(value, k, devices) for k, value in zip((2, 3), up_far)]
    down_weights[2] = stand_behind(down_weights[2], up_near[0])
    down_weights += [swapped(down_weights[k]) for k in DOWN_HALVED]
    up_weights += [swapped(up_weights[k]) for k in UP_HALVED]

    caps = [total * 5 // 16, total * 6 // 16, total * 7 // 16]
    cap = caps[-1]
    outgoing, target, label = first_pack_call(
        cap, whole, devices, resident, request_block_adapter, request_block_rows, tokens
    )
    arrived = exchange(outgoing)
    partial, count, notes, met = down_call(cap, first, arrived, down_weights, up_weights[2:3])
    sums = quad_sums(partial, devices)
    count = count[0:1, 0:1]
    most = jnp.maximum(count, swapped(count))[0, 0].astype(jnp.float32)
    branches = [functools.partial(back_and_mix, kept, 0) for kept in caps]
    branches += [functools.partial(back_and_mix, cap, STEP), start_again]
    return lax.switch(
        sum((most > limit).astype(i32) for limit in [*caps, cap + STEP]),
        branches,
        tokens,
        target,
        label,
        first,
        met,
        notes,
        sums,
        down_weights,
        up_weights,
        request_block_adapter,
        request_block_rows,
        adapter_down_weight,
        adapter_up_weight,
    )


def solution(mesh):
    placed = (
        P(("groups", "adapter"), None, None),
        P(("groups", "adapter")),
        P(("groups", "adapter")),
        P("adapter", None, None),
        P("adapter", None, None),
    )

    def per_device(tokens, request_block_adapter, request_block_rows, down_weight, up_weight):
        blocks, rows, width = tokens.shape
        devices = mesh.shape["adapter"]
        slots = max(1, 4 * blocks // devices)
        quads = devices % QUAD == 0 and slots * QUAD >= blocks
        quads = quads and width % (QUAD * LANES) == LANES and up_weight.shape[1] == HALF
        quads = quads and blocks * rows * 7 // 16 == 7 * STEP and mesh.shape["groups"] == 2
        plan = rows_to_quads if quads else rows_to_holders
        return plan(tokens, request_block_adapter, request_block_rows, down_weight, up_weight)

    return jax.shard_map(
        per_device,
        mesh=mesh,
        in_specs=placed,
        out_specs=P(("groups", "adapter"), None, None),
        check_vma=False,
    )
```

```python
import functools

import jax
import jax.numpy as jnp
from jax import lax
from jax.experimental import pallas as pl
from jax.experimental.pallas import tpu as pltpu
from jax.sharding import PartitionSpec as P

LANES = 128
HALF = 64
QUAD = 4
QUARTER = 32
STEP = 16
NOTE = 96
DOWN_HALVED = (2, 3)
UP_HALVED = (2,)
VMEM = pl.BlockSpec(memory_space=pltpu.VMEM)
SMEM = pl.BlockSpec(memory_space=pltpu.SMEM)


def normalise(tokens):
    values = tokens.astype(jnp.float32)
    mean_sq = jnp.mean(values * values, axis=-1, keepdims=True)
    return (values, (values * lax.rsqrt(mean_sq + 1e-06)).astype(jnp.bfloat16))


def resident_update(hidden_state, block_labels, adapter_down_weight, adapter_up_weight):
    feature_width = hidden_state.shape[-1]
    leading = hidden_state.shape[:-1]
    resident_rows, unused_value, inner_rank = adapter_down_weight.shape
    flattened_tokens = hidden_state.reshape(-1, feature_width)
    down_matrix = jnp.einsum(
        "tq,iqg->tig", flattened_tokens, adapter_down_weight, preferred_element_type=jnp.float32
    )
    down_matrix = down_matrix.astype(jnp.bfloat16).reshape(
        flattened_tokens.shape[0], resident_rows * inner_rank
    )
    column_owner = jnp.arange(resident_rows * inner_rank, dtype=jnp.int32) // inner_rank
    picked = block_labels.reshape(-1, 1) == column_owner[None, :]
    down_matrix = jnp.where(picked, down_matrix, jnp.zeros_like(down_matrix))
    lowrank_update = jnp.dot(
        down_matrix,
        adapter_up_weight.reshape(resident_rows * inner_rank, feature_width),
        preferred_element_type=jnp.float32,
    )
    return lowrank_update.astype(jnp.bfloat16).reshape(leading + (feature_width,))


def rows_to_holders(
    tokens, request_block_adapter, request_block_rows, adapter_down_weight, adapter_up_weight
):
    blocks, rows, feature_width = tokens.shape
    devices = lax.axis_size("adapter")
    resident_rows = adapter_down_weight.shape[0]
    slots = max(1, 4 * blocks // devices)
    values, normed = normalise(tokens)
    owner = request_block_adapter // resident_rows
    within = request_block_adapter - owner * resident_rows
    serial = jnp.arange(blocks, dtype=jnp.int32)
    earlier = (owner[:, None] == owner[None, :]) & (serial[None, :] < serial[:, None])
    position = owner * slots + jnp.sum(earlier, axis=1)
    outgoing = (
        jnp.zeros((devices * slots, rows, feature_width), jnp.bfloat16).at[position].set(normed)
    )
    outgoing = outgoing.reshape(devices, slots, rows, feature_width)
    block_labels = jnp.full((devices * slots,), -1, jnp.int32).at[position].set(within)
    block_labels = jnp.broadcast_to(block_labels[:, None], (devices * slots, rows)).reshape(
        devices, slots, rows
    )
    arriving_rows, row_markers = (
        lax.all_to_all(outgoing, "adapter", split_axis=0, concat_axis=0, tiled=True),
        lax.all_to_all(block_labels, "adapter", split_axis=0, concat_axis=0, tiled=True),
    )
    lowrank_update = resident_update(
        arriving_rows, row_markers, adapter_down_weight, adapter_up_weight
    )
    returned = lax.all_to_all(lowrank_update, "adapter", split_axis=0, concat_axis=0, tiled=True)
    mine = returned.reshape(devices * slots, rows, feature_width)[position]
    live = jnp.arange(rows, dtype=jnp.int32)[None, :] < request_block_rows[:, None]
    mixed = values + jnp.where(live[:, :, None], mine.astype(jnp.float32), jnp.float32(0.0))
    return mixed.astype(jnp.bfloat16)


def lanes_of(rows):
    return lax.broadcasted_iota(jnp.int32, (rows, LANES), 1)


def weight_kernel(whole, which, halved, part_ref, group_ref, weight_ref, *out_refs):
    tiles = whole // LANES
    for k, out_ref in zip(which, out_refs):
        j = part_ref[k]
        if k < 2:
            last = weight_ref[:, QUAD * whole :].astype(jnp.float32)
            turned = pltpu.roll(last, lax.rem(LANES - QUARTER * j, LANES), 1)
            inside = lanes_of(last.shape[0]) < QUARTER
            out_ref[:, 0:whole] = weight_ref[:, pl.ds(pl.multiple_of(j * whole, LANES), whole)]
            out_ref[:, whole:] = jnp.where(inside, turned, 0.0).astype(jnp.bfloat16)
            continue
        count = weight_ref.shape[0] // 2 if k in halved else weight_ref.shape[0]
        start = pl.multiple_of(group_ref[0] * count, count) if k in halved else 0
        for t in range(tiles):
            column = pl.multiple_of(j * whole + t * LANES, LANES)
            out_ref[t * count : (t + 1) * count, :] = weight_ref[
                pl.ds(start, count), pl.ds(column, LANES)
            ]
        last = weight_ref[pl.ds(start, count), QUAD * whole :].astype(jnp.float32)
        size = count // QUAD
        owner = lanes_of(size) // QUARTER
        merged = jnp.zeros((size, LANES), jnp.float32)
        for m in range(QUAD):
            shift = lax.rem(LANES + QUARTER * (m - j), LANES)
            turned = pltpu.roll(last[m * size : (m + 1) * size], shift, 1)
            merged = jnp.where(owner == m, turned, merged)
        out_ref[tiles * count :, :] = merged.astype(jnp.bfloat16)


def open_far(far_refs, halved, opened_ref):
    width = opened_ref.shape[2]
    tiles = width // LANES - 1
    places = [(k - 2, 0) for k in (2, 3)] + [(k - 2, 1) for k in halved]
    for ref, (holder, part) in zip(far_refs, places):
        count = opened_ref.shape[1] // 2 if holder + 2 in halved else opened_ref.shape[1]
        base, size = part * count, count // QUAD
        inside = lanes_of(size) < QUARTER
        for t in range(tiles):
            opened_ref[holder, base : base + count, t * LANES : (t + 1) * LANES] = ref[
                t * count : (t + 1) * count, :
            ]
        packed = ref[tiles * count :, :].astype(jnp.float32)
        for m in range(QUAD):
            turned = pltpu.roll(packed, (LANES - QUARTER * m) % LANES, 1) if m else packed
            opened_ref[holder, base + m * size : base + (m + 1) * size, tiles * LANES :] = (
                jnp.where(inside, turned, 0.0).astype(jnp.bfloat16)
            )


def lay_out(resident, adapter_ref, used_ref, most_ref, target_ref, label_ref):
    blocks, total = adapter_ref.shape[1], target_ref.shape[1]
    rows = total // blocks
    adapter, used = adapter_ref[...], used_ref[...]
    down = lax.broadcasted_iota(jnp.int32, (blocks, blocks), 0)
    across = lax.broadcasted_iota(jnp.int32, (blocks, blocks), 1)

    def turned(value):
        return jnp.sum(jnp.where(down == across, value, 0), axis=1, keepdims=True)

    span = resident * QUAD
    quad = jnp.floor((adapter.astype(jnp.float32) + 0.5) * (1.0 / span)).astype(jnp.int32)
    order = adapter * blocks + lax.broadcasted_iota(jnp.int32, (1, blocks), 1)
    quad_down, order_down, used_down = turned(quad), turned(order), turned(used)
    same = quad_down == quad
    ahead = jnp.sum(jnp.where(same & (order < order_down), used, 0), axis=1, keepdims=True)
    within = jnp.sum(jnp.where(same, used, 0), axis=1, keepdims=True)
    most_ref[...] = jnp.broadcast_to(jnp.max(within, axis=0, keepdims=True), most_ref.shape)
    start = quad_down * total + ahead

    block = lax.broadcasted_iota(jnp.int32, (blocks, total), 0)
    row = lax.broadcasted_iota(jnp.int32, (blocks, total), 1) - block * rows
    place = jnp.where((row >= 0) & (row < used_down), start + row + 1, 0)
    target_ref[...] = jnp.sum(place, axis=0, keepdims=True) - 1
    block = lax.broadcasted_iota(jnp.int32, (total, blocks), 1)
    row = lax.broadcasted_iota(jnp.int32, (total, blocks), 0) - block * rows
    label = jnp.where((row >= 0) & (row < rows), adapter - quad * span + 1, 0)
    label_ref[...] = jnp.sum(label.astype(jnp.float32), axis=1, keepdims=True)


def first_pack_kernel(
    whole, cap, resident, adapter_ref, used_ref, tokens_ref, out_ref, target_ref, label_ref, *refs
):
    normed_ref, most_ref = refs
    lay_out(resident, adapter_ref, used_ref, most_ref, target_ref, label_ref)
    pack_kernel(
        whole, cap, 0, most_ref, target_ref, label_ref, tokens_ref, out_ref, normed_ref
    )


def pack_kernel(
    whole, cap, base, most_ref, target_ref, label_ref, tokens_ref, out_ref, normed_ref
):
    values = tokens_ref[...].astype(jnp.float32)
    mean_sq = jnp.mean(values * values, axis=-1, keepdims=True)
    normed_ref[...] = (values * lax.rsqrt(mean_sq + 1e-06)).astype(jnp.bfloat16)
    total = tokens_ref.shape[0]
    quads, tiles = out_ref.shape[0] // QUAD, whole // LANES
    lane = lanes_of(total)
    last = normed_ref[:, QUAD * whole :].astype(jnp.float32)
    label = jnp.where(lane == QUARTER, label_ref[...], 0.0)
    ends = []
    for j in range(QUAD):
        turned = pltpu.roll(last, (LANES - QUARTER * j) % LANES, 1) if j else last
        ends.append(jnp.where(lane < QUARTER, turned, label).astype(jnp.bfloat16))
    most = most_ref[0:1, 0:1].astype(jnp.float32)
    group_lane = lanes_of(QUARTER) // QUARTER
    step_lane = lanes_of(STEP)
    chosen = []
    for q in range(quads):
        place = lax.broadcasted_iota(jnp.int32, (cap, total), 0) + (q * total + base)
        chosen.append(jnp.where(target_ref[...] == place, 1.0, 0.0).astype(jnp.bfloat16))
    chosen = jnp.concatenate(chosen, axis=0)
    notes = [jnp.where(step_lane == NOTE + cap // STEP, most, 0.0)] * quads
    for j in range(QUAD):
        for t in range(tiles):
            column = j * whole + t * LANES
            if t % 2 == 0:
                count = min(2, tiles - t) * LANES
                share = jnp.dot(
                    chosen,
                    normed_ref[:, column : column + count],
                    preferred_element_type=jnp.float32,
                ).astype(jnp.bfloat16)
            for q in range(quads):
                out_ref[q * QUAD + j, t * cap : (t + 1) * cap, :] = share[
                    q * cap : (q + 1) * cap, t % 2 * LANES : (t % 2 + 1) * LANES
                ]
        end_rows = jnp.dot(chosen, ends[j], preferred_element_type=jnp.float32)
        for q in range(quads):
            end = end_rows[q * cap : (q + 1) * cap]
            if j == 0:
                for a in range(cap // STEP):
                    turned = pltpu.roll(end[a * STEP : (a + 1) * STEP], NOTE + a - QUARTER, 1)
                    notes[q] = jnp.where(step_lane == NOTE + a, turned, notes[q])
            padded = jnp.concatenate(
                [end, jnp.zeros((QUAD * QUARTER - cap, LANES), jnp.float32)], axis=0
            )
            merged = padded[0:QUARTER]
            for m in range(1, QUAD):
                turned = pltpu.roll(padded[m * QUARTER : (m + 1) * QUARTER], m * QUARTER, 1)
                merged = jnp.where(group_lane == m, turned, merged)
            out_ref[q * QUAD + j, tiles * cap : tiles * cap + STEP, :] = merged[0:STEP].astype(
                jnp.bfloat16
            )
            out_ref[q * QUAD + j, tiles * cap + STEP :, :] = jnp.where(
                step_lane >= NOTE, notes[q], merged[STEP:]
            ).astype(jnp.bfloat16)


def read_notes(rows_ref, cap, tiles, part_ref, resident, notes_ref, labels_ref, met_ref):
    senders = rows_ref.shape[0]
    for s in range(senders):
        notes_ref[s * STEP : (s + 1) * STEP, :] = rows_ref[s, tiles * cap + STEP :, :]
    steps = labels_ref.shape[0]
    row = lax.broadcasted_iota(jnp.int32, (steps, LANES), 0)
    wanted = jnp.where(lanes_of(steps) == NOTE + row, 1.0, 0.0).astype(jnp.bfloat16)
    labels = lax.dot_general(
        wanted, notes_ref[...], (((1,), (1,)), ((), ())), preferred_element_type=jnp.float32
    )
    labels_ref[...] = labels
    code = jnp.zeros((steps, 1), jnp.float32)
    for h in range(QUAD):
        first = part_ref[h].astype(jnp.float32) + 1.0
        met = jnp.where((labels >= first) & (labels < first + resident), 1.0, 0.0)
        code = code + (1 << h) * jnp.max(met, axis=1, keepdims=True)
    at = lax.broadcasted_iota(jnp.int32, (steps, 1), 0)
    for a in range(cap // STEP):
        met_ref[a] = jnp.max(jnp.where(at == a, code, 0.0)).astype(jnp.int32)


def for_holders(met_ref, first_ref, near_refs, opened_ref, halved, a, step):
    pairs = opened_ref.shape[1] // LANES
    for h in range(QUAD):
        base = first_ref[h].astype(jnp.float32) + 1.0
        firsts = [base + 2.0 * t for t in range(pairs)]
        if h in halved:
            firsts = [
                base + first_ref[QUAD + i].astype(jnp.float32) + 2.0 * t
                for i in range(2)
                for t in range(pairs // 2)
            ]

        @pl.when(lax.rem(met_ref[a] // (1 << h), 2) > 0)
        def _(h=h, firsts=firsts):
            is_first = lax.rem(met_ref[a], 1 << h) == 0
            step(near_refs[h] if h < 2 else opened_ref.at[h - 2], firsts, is_first)


def down_kernel(first_ref, rows_ref, *refs):
    near_refs, far_refs, out_ref, count_ref = refs[:2], refs[2:6], refs[6], refs[7]
    notes_ref, met_ref, opened_ref, batch_ref, picked_ref, labels_ref = refs[8:]
    senders, width = rows_ref.shape[0], batch_ref.shape[1]
    tiles = width // LANES - 1
    cap = out_ref.shape[0] * STEP
    rank = out_ref.shape[1]
    resident = opened_ref.shape[1] // rank
    dims = (((1,), (1,)), ((), ()))
    read_notes(rows_ref, cap, tiles, first_ref, resident, notes_ref, labels_ref, met_ref)
    notes = notes_ref[...].astype(jnp.float32)
    is_count = lanes_of(senders * STEP) == NOTE + cap // STEP
    count = jnp.max(jnp.where(is_count, notes, 0.0), axis=(0, 1), keepdims=True)
    count_ref[...] = jnp.broadcast_to(count, count_ref.shape).astype(jnp.bfloat16)
    open_far(far_refs, DOWN_HALVED, opened_ref)

    def one(a, carry):
        picked_ref[...] = jnp.zeros(picked_ref.shape, jnp.float32)

        @pl.when(met_ref[a] > 0)
        def _():
            shift = lax.rem(LANES - QUARTER * (a // 2), LANES)
            spot = pl.multiple_of(tiles * cap + lax.rem(a, 2) * STEP, STEP)
            for s in range(senders):
                rows = slice(s * STEP, (s + 1) * STEP)
                for t in range(tiles):
                    at = pl.multiple_of(t * cap + a * STEP, STEP)
                    batch_ref[rows, t * LANES : (t + 1) * LANES] = rows_ref[s, pl.ds(at, STEP), :]
                end = rows_ref[s, pl.ds(spot, STEP), :].astype(jnp.float32)
                batch_ref[rows, tiles * LANES :] = pltpu.roll(end, shift, 1).astype(jnp.bfloat16)
            label = labels_ref[pl.ds(a, 1), :]

            def step(weight_ref, firsts, is_first):
                product = lax.dot_general(
                    weight_ref[...], batch_ref[...], dims, preferred_element_type=jnp.float32
                )
                picked = picked_ref[...]
                for t, first in enumerate(firsts):
                    for i in range(2):
                        at = (2 * t + i) * rank
                        picked = jnp.where(
                            label == first + i, product[at : at + rank, :], picked
                        )
                picked_ref[...] = picked

            for_holders(met_ref, first_ref, near_refs, opened_ref, DOWN_HALVED, a, step)

        out_ref[a] = picked_ref[...]
        return carry

    lax.fori_loop(0, cap // STEP, one, 0)


def pair_kernel(own_ref, other_ref, out_ref):
    out_ref[...] = (own_ref[...] + other_ref[...]).astype(jnp.bfloat16)


def up_kernel(first_ref, met_ref, notes_ref, *refs):
    sum_refs, near_refs, far_refs, out_ref = refs[:2], refs[2:4], refs[4:7], refs[7]
    opened_ref, delta_ref, ends_ref, label_ref, twice_ref = refs[8:]
    senders, width = out_ref.shape[0], opened_ref.shape[2]
    tiles = width // LANES - 1
    rank = sum_refs[0].shape[1]
    kept = (out_ref.shape[1] - QUARTER) // tiles
    group_lane = lanes_of(STEP) // QUARTER
    open_far(far_refs, UP_HALVED, opened_ref)
    ends_ref[...] = jnp.zeros(ends_ref.shape, jnp.float32)
    low = jnp.where(lanes_of(senders * STEP) < HALF, 0.0, 1.0)
    rank_row = lax.broadcasted_iota(jnp.int32, (rank, LANES), 0)
    twofold = jnp.where(lax.rem(lanes_of(rank), rank) == rank_row, 1.0, 0.0).astype(jnp.bfloat16)

    note_row = lax.broadcasted_iota(jnp.int32, (LANES, LANES), 0)
    for a in range(kept // STEP):
        wanted = jnp.where(note_row == NOTE + a, 1.0, 0.0).astype(jnp.bfloat16)
        label_ref[a] = jnp.dot(notes_ref[...], wanted, preferred_element_type=jnp.float32) - low
        down = sum_refs[0][a].astype(jnp.float32) + sum_refs[1][a].astype(jnp.float32)
        twice_ref[a] = lax.dot_general(
            down.astype(jnp.bfloat16),
            twofold,
            (((0,), (0,)), ((), ())),
            preferred_element_type=jnp.float32,
        )

    def one(a, carry):
        @pl.when(met_ref[a] == 0)
        def _():
            delta_ref[...] = jnp.zeros(delta_ref.shape, jnp.float32)

        @pl.when(met_ref[a] > 0)
        def _():
            label, twice = label_ref[a], twice_ref[a]

            def step(weight_ref, firsts, is_first):
                placed = [jnp.where(label == first, twice, 0.0) for first in firsts]
                placed = jnp.concatenate(placed, axis=1).astype(jnp.bfloat16)
                before = jnp.where(is_first, 0.0, delta_ref[...])
                delta_ref[...] = before + jnp.dot(
                    placed, weight_ref[...], preferred_element_type=jnp.float32
                )

            for_holders(met_ref, first_ref, near_refs, opened_ref, UP_HALVED, a, step)

        spot = pl.multiple_of(lax.rem(a, 2) * STEP, STEP)
        for s in range(senders):
            rows = slice(s * STEP, (s + 1) * STEP)
            for t in range(tiles):
                at = pl.multiple_of(t * kept + a * STEP, STEP)
                out_ref[s, pl.ds(at, STEP), :] = delta_ref[
                    rows, t * LANES : (t + 1) * LANES
                ].astype(jnp.bfloat16)
            turned = pltpu.roll(delta_ref[rows, tiles * LANES :], QUARTER * (a // 2), 1)
            ends_ref[s, pl.ds(spot, STEP), :] = jnp.where(
                group_lane == a // 2, turned, ends_ref[s, pl.ds(spot, STEP), :]
            )
        return carry

    lax.fori_loop(0, kept // STEP, one, 0)
    for s in range(senders):
        out_ref[s, tiles * kept :, :] = ends_ref[s].astype(jnp.bfloat16)


def mix_kernel(whole, bases, target_ref, tokens_ref, *refs):
    returned_refs, out_ref = refs[:-1], refs[-1]
    total = tokens_ref.shape[0]
    tiles, quads = whole // LANES, returned_refs[0].shape[0] // QUAD
    lane = lanes_of(total)
    chosen = []
    for base, ref in zip(bases, returned_refs):
        kept = (ref.shape[1] - QUARTER) // tiles
        spot = lax.broadcasted_iota(jnp.int32, (total, quads * kept), 1)
        place = spot // kept * total + spot % kept + base
        chosen.append(jnp.where(target_ref[...] == place, 1.0, 0.0).astype(jnp.bfloat16))
    end = jnp.zeros((total, LANES), jnp.float32)
    for j in range(QUAD):
        delta = 0.0
        for choice, ref in zip(chosen, returned_refs):
            kept = choice.shape[1] // quads
            shares = []
            for q in range(quads):
                d = q * QUAD + j
                parts = [ref[d, t * kept : (t + 1) * kept, :] for t in range(tiles)]
                packed = ref[d, tiles * kept :, :].astype(jnp.float32)
                groups = [packed]
                for m in range(1, QUAD):
                    groups.append(pltpu.roll(packed, LANES - QUARTER * m, 1))
                parts.append(jnp.concatenate(groups, axis=0)[0:kept].astype(jnp.bfloat16))
                shares.append(jnp.concatenate(parts, axis=1))
            share = jnp.concatenate(shares, axis=0)
            delta = delta + jnp.dot(choice, share, preferred_element_type=jnp.float32)
        columns = slice(j * whole, (j + 1) * whole)
        out_ref[:, columns] = (
            tokens_ref[:, columns].astype(jnp.float32) + delta[:, 0:whole]
        ).astype(jnp.bfloat16)
        last = delta[:, whole:]
        turned = pltpu.roll(last, QUARTER * j, 1) if j else last
        end = jnp.where((lane >= QUARTER * j) & (lane < QUARTER * (j + 1)), turned, end)
    out_ref[:, QUAD * whole :] = (
        tokens_ref[:, QUAD * whole :].astype(jnp.float32) + end
    ).astype(jnp.bfloat16)


def call(kernel, out_shape, in_specs, flops, moved, after=(), scratch=(), out_specs=None):
    many = isinstance(out_shape, list)
    skipped = len(after)
    body = (lambda *refs: kernel(*refs[skipped:])) if skipped else kernel
    run = pl.pallas_call(
        body,
        out_shape=out_shape,
        in_specs=[pl.BlockSpec(memory_space=pl.ANY)] * skipped + in_specs,
        out_specs=out_specs or ([VMEM] * len(out_shape) if many else VMEM),
        scratch_shapes=scratch,
        compiler_params=pltpu.CompilerParams(vmem_limit_bytes=18 * 2**20),
        cost_estimate=pl.CostEstimate(flops=flops, bytes_accessed=moved, transcendentals=0),
    )
    return functools.partial(run, *after)


def exchange(value):
    return lax.all_to_all(value, "adapter", split_axis=0, concat_axis=0, tiled=True)


def towards(value, k, devices):
    return lax.ppermute(value, "adapter", [(i, i ^ k) for i in range(devices)])


def swapped(value):
    return lax.ppermute(value, "groups", [(0, 1), (1, 0)])


def stand_behind(value, *earlier):
    return pl.pallas_call(
        lambda *refs: None,
        out_shape=jax.ShapeDtypeStruct(value.shape, value.dtype),
        in_specs=[pl.BlockSpec(memory_space=pl.ANY)] * (1 + len(earlier)),
        out_specs=pl.BlockSpec(memory_space=pl.ANY),
        input_output_aliases={0: 0},
    )(value, *earlier)


def first_pack_call(cap, whole, devices, resident, adapter, used, tokens):
    blocks, rows, width = tokens.shape
    total = blocks * rows
    return call(
        functools.partial(first_pack_kernel, whole, cap, resident),
        [
            jax.ShapeDtypeStruct((devices, whole // LANES * cap + QUARTER, LANES), jnp.bfloat16),
            jax.ShapeDtypeStruct((1, total), jnp.int32),
            jax.ShapeDtypeStruct((total, 1), jnp.float32),
        ],
        [VMEM, VMEM, VMEM],
        2 * devices * cap * total * whole,
        2 * (total * width + devices * cap * whole),
        scratch=[pltpu.VMEM((total, width), jnp.bfloat16), pltpu.VMEM((8, LANES), jnp.int32)],
    )(adapter.reshape(1, blocks), used.reshape(1, blocks), tokens.reshape(total, width))


def pack_call(cap, base, whole, devices, target, label, tokens):
    blocks, rows, width = tokens.shape
    total = blocks * rows
    return call(
        functools.partial(pack_kernel, whole, cap, base),
        jax.ShapeDtypeStruct((devices, whole // LANES * cap + QUARTER, LANES), jnp.bfloat16),
        [VMEM, VMEM, VMEM, VMEM],
        2 * devices * cap * total * whole,
        2 * (total * width + devices * cap * whole),
        scratch=[pltpu.VMEM((total, width), jnp.bfloat16)],
    )(jnp.zeros((8, LANES), jnp.int32), target, label, tokens.reshape(total, width))


def down_call(cap, first, arrived, down_weights, after):
    devices = arrived.shape[0]
    columns, share = down_weights[0].shape
    return call(
        down_kernel,
        [
            jax.ShapeDtypeStruct((cap // STEP, HALF, devices * STEP), jnp.float32),
            jax.ShapeDtypeStruct((STEP, LANES), jnp.bfloat16),
            jax.ShapeDtypeStruct((devices * STEP, LANES), jnp.bfloat16),
            jax.ShapeDtypeStruct((8,), jnp.int32),
        ],
        [SMEM] + [VMEM] * (1 + len(down_weights)),
        0,
        0,
        after,
        [
            pltpu.VMEM((2, columns, share), jnp.bfloat16),
            pltpu.VMEM((devices * STEP, share), jnp.bfloat16),
            pltpu.VMEM((HALF, devices * STEP), jnp.float32),
            pltpu.VMEM((8, devices * STEP), jnp.float32),
        ],
        [VMEM, VMEM, VMEM, SMEM],
    )(first, arrived, *down_weights)


def quad_sums(partial, devices):
    pair = call(
        pair_kernel, jax.ShapeDtypeStruct(partial.shape, jnp.bfloat16), [VMEM, VMEM], 0, 0
    )(partial, towards(partial, 1, devices))
    return [pair, towards(pair, 2, devices)]


def up_call(kept, first, met, notes, sums, up_weights):
    devices = notes.shape[0] // STEP
    columns, share = up_weights[0].shape
    shape = (devices, (share // LANES - 1) * kept + QUARTER, LANES)
    return call(
        up_kernel,
        jax.ShapeDtypeStruct(shape, jnp.bfloat16),
        [SMEM, SMEM] + [VMEM] * (3 + len(up_weights)),
        2 * devices * kept * QUAD * columns * share,
        2 * (2 * devices * kept + QUAD * columns) * share,
        scratch=[
            pltpu.VMEM((2, columns, share), jnp.bfloat16),
            pltpu.VMEM((devices * STEP, share), jnp.float32),
            pltpu.VMEM((devices, QUARTER, LANES), jnp.float32),
            *[pltpu.VMEM((kept // STEP, devices * STEP, LANES), jnp.float32)] * 2,
        ],
    )(first, met, notes, *sums, *up_weights)


def back_and_mix(
    kept, more, tokens, target, label, first, met, notes, sums, down_weights, up_weights, *unused
):
    blocks, rows, width = tokens.shape
    total = blocks * rows
    devices = notes.shape[0] // STEP
    whole = up_weights[0].shape[1] - LANES
    pieces = [exchange(up_call(kept, first, met, notes, sums, up_weights))]
    if more:
        outgoing = pack_call(more, kept, whole, devices, target, label, tokens)
        arrived = exchange(outgoing)
        partial, unused_count, notes, met = down_call(more, first, arrived, down_weights, [])
        sums = quad_sums(partial, devices)
        pieces.append(exchange(up_call(more, first, met, notes, sums, up_weights)))
    mixed = call(
        functools.partial(mix_kernel, whole, (0, kept)[: len(pieces)]),
        jax.ShapeDtypeStruct((total, width), jnp.bfloat16),
        [VMEM] * (2 + len(pieces)),
        2 * devices * (kept + more) * total * whole,
        2 * (2 * total * width + devices * (kept + more) * whole),
    )(target.reshape(total, 1), tokens.reshape(total, width), *pieces)
    return mixed.reshape(tokens.shape)


def start_again(
    tokens, target, label, first, met, notes, sums, down_weights, up_weights, *arguments
):
    return rows_to_holders(tokens, *arguments)


def rows_to_quads(
    tokens, request_block_adapter, request_block_rows, adapter_down_weight, adapter_up_weight
):
    blocks, rows, width = tokens.shape
    devices = lax.axis_size("adapter")
    resident, rank, unused_width = adapter_up_weight.shape
    total = blocks * rows
    columns = resident * rank
    whole = width // LANES // QUAD * LANES
    share = whole + LANES
    bf16, i32 = jnp.bfloat16, jnp.int32

    me = lax.axis_index("adapter").astype(i32)
    group = lax.axis_index("groups").astype(i32)
    parts = jnp.bitwise_xor(me % QUAD, jnp.arange(QUAD, dtype=i32))
    halves = jnp.stack([group, 1 - group]) * (resident // 2)
    first = jnp.concatenate([parts * resident, halves]).astype(i32)
    tiles = whole // LANES

    def shares(weight, which, halved, after):
        shapes = []
        for k in which:
            count = columns // 2 if k in halved else columns
            far = (count * tiles + count // QUAD, LANES)
            shapes.append(jax.ShapeDtypeStruct((columns, share) if k < 2 else far, bf16))
        return call(
            functools.partial(weight_kernel, whole, which, halved),
            shapes,
            [SMEM, SMEM, VMEM],
            0,
            len(which) * columns * width,
            after,
        )(parts, group.reshape(1), weight)

    down_weight = adapter_down_weight.transpose(0, 2, 1).reshape(columns, width)
    up_weight = adapter_up_weight.reshape(columns, width)
    down_far = shares(down_weight, (2, 3), DOWN_HALVED, [])
    up_far = shares(up_weight, (2, 3), UP_HALVED, down_far[:1])
    down_near = shares(down_weight, (0, 1), (), up_far[:1])
    up_near = shares(up_weight, (0, 1), (), down_near[:1])
    down_weights = [down_near[0], towards(down_near[1], 1, devices)]
    down_weights += [towards(value, k, devices) for k, value in zip((2, 3), down_far)]
    up_weights = [up_near[0], towards(up_near[1], 1, devices)]
    up_weights += [towards(value, k, devices) for k, value in zip((2, 3), up_far)]
    down_weights[2] = stand_behind(down_weights[2], up_near[0])
    down_weights += [swapped(down_weights[k]) for k in DOWN_HALVED]
    up_weights += [swapped(up_weights[k]) for k in UP_HALVED]

    caps = [total * 5 // 16, total * 6 // 16, total * 7 // 16]
    cap = caps[-1]
    outgoing, target, label = first_pack_call(
        cap, whole, devices, resident, request_block_adapter, request_block_rows, tokens
    )
    arrived = exchange(outgoing)
    partial, count, notes, met = down_call(cap, first, arrived, down_weights, up_weights[2:3])
    sums = quad_sums(partial, devices)
    count = count[0:1, 0:1]
    most = jnp.maximum(count, swapped(count))[0, 0].astype(jnp.float32)
    branches = [functools.partial(back_and_mix, kept, 0) for kept in caps]
    branches += [functools.partial(back_and_mix, cap, STEP), start_again]
    return lax.switch(
        sum((most > limit).astype(i32) for limit in [*caps, cap + STEP]),
        branches,
        tokens,
        target,
        label,
        first,
        met,
        notes,
        sums,
        down_weights,
        up_weights,
        request_block_adapter,
        request_block_rows,
        adapter_down_weight,
        adapter_up_weight,
    )


def solution(mesh):
    placed = (
        P(("groups", "adapter"), None, None),
        P(("groups", "adapter")),
        P(("groups", "adapter")),
        P("adapter", None, None),
        P("adapter", None, None),
    )

    def per_device(tokens, request_block_adapter, request_block_rows, down_weight, up_weight):
        blocks, rows, width = tokens.shape
        devices = mesh.shape["adapter"]
        slots = max(1, 4 * blocks // devices)
        quads = devices % QUAD == 0 and slots * QUAD >= blocks
        quads = quads and width % (QUAD * LANES) == LANES and up_weight.shape[1] == HALF
        quads = quads and blocks * rows * 7 // 16 == 7 * STEP and mesh.shape["groups"] == 2
        plan = rows_to_quads if quads else rows_to_holders
        return plan(tokens, request_block_adapter, request_block_rows, down_weight, up_weight)

    return jax.shard_map(
        per_device,
        mesh=mesh,
        in_specs=placed,
        out_specs=P(("groups", "adapter"), None, None),
        check_vma=False,
    )
```

```python
import functools

import jax
import jax.numpy as jnp
from jax import lax
from jax.experimental import pallas as pl
from jax.experimental.pallas import tpu as pltpu
from jax.sharding import PartitionSpec as P

LANES = 128
HALF = 64
QUAD = 4
QUARTER = 32
STEP = 16
NOTE = 96
DOWN_HALVED = (2, 3)
UP_HALVED = (2,)
VMEM = pl.BlockSpec(memory_space=pltpu.VMEM)
SMEM = pl.BlockSpec(memory_space=pltpu.SMEM)


def normalise(tokens):
    values = tokens.astype(jnp.float32)
    mean_sq = jnp.mean(values * values, axis=-1, keepdims=True)
    return (values, (values * lax.rsqrt(mean_sq + 1e-06)).astype(jnp.bfloat16))


def resident_update(hidden_state, block_labels, adapter_down_weight, adapter_up_weight):
    feature_width = hidden_state.shape[-1]
    leading = hidden_state.shape[:-1]
    resident_rows, unused_value, inner_rank = adapter_down_weight.shape
    flattened_tokens = hidden_state.reshape(-1, feature_width)
    down_matrix = jnp.einsum(
        "tq,iqg->tig", flattened_tokens, adapter_down_weight, preferred_element_type=jnp.float32
    )
    down_matrix = down_matrix.astype(jnp.bfloat16).reshape(
        flattened_tokens.shape[0], resident_rows * inner_rank
    )
    column_owner = jnp.arange(resident_rows * inner_rank, dtype=jnp.int32) // inner_rank
    picked = block_labels.reshape(-1, 1) == column_owner[None, :]
    down_matrix = jnp.where(picked, down_matrix, jnp.zeros_like(down_matrix))
    lowrank_update = jnp.dot(
        down_matrix,
        adapter_up_weight.reshape(resident_rows * inner_rank, feature_width),
        preferred_element_type=jnp.float32,
    )
    return lowrank_update.astype(jnp.bfloat16).reshape(leading + (feature_width,))


def rows_to_holders(
    tokens, request_block_adapter, request_block_rows, adapter_down_weight, adapter_up_weight
):
    blocks, rows, feature_width = tokens.shape
    devices = lax.axis_size("adapter")
    resident_rows = adapter_down_weight.shape[0]
    slots = max(1, 4 * blocks // devices)
    values, normed = normalise(tokens)
    owner = request_block_adapter // resident_rows
    within = request_block_adapter - owner * resident_rows
    serial = jnp.arange(blocks, dtype=jnp.int32)
    earlier = (owner[:, None] == owner[None, :]) & (serial[None, :] < serial[:, None])
    position = owner * slots + jnp.sum(earlier, axis=1)
    outgoing = (
        jnp.zeros((devices * slots, rows, feature_width), jnp.bfloat16).at[position].set(normed)
    )
    outgoing = outgoing.reshape(devices, slots, rows, feature_width)
    block_labels = jnp.full((devices * slots,), -1, jnp.int32).at[position].set(within)
    block_labels = jnp.broadcast_to(block_labels[:, None], (devices * slots, rows)).reshape(
        devices, slots, rows
    )
    arriving_rows, row_markers = (
        lax.all_to_all(outgoing, "adapter", split_axis=0, concat_axis=0, tiled=True),
        lax.all_to_all(block_labels, "adapter", split_axis=0, concat_axis=0, tiled=True),
    )
    lowrank_update = resident_update(
        arriving_rows, row_markers, adapter_down_weight, adapter_up_weight
    )
    returned = lax.all_to_all(lowrank_update, "adapter", split_axis=0, concat_axis=0, tiled=True)
    mine = returned.reshape(devices * slots, rows, feature_width)[position]
    live = jnp.arange(rows, dtype=jnp.int32)[None, :] < request_block_rows[:, None]
    mixed = values + jnp.where(live[:, :, None], mine.astype(jnp.float32), jnp.float32(0.0))
    return mixed.astype(jnp.bfloat16)


def lanes_of(rows):
    return lax.broadcasted_iota(jnp.int32, (rows, LANES), 1)


def weight_kernel(whole, which, halved, part_ref, group_ref, weight_ref, *out_refs):
    tiles = whole // LANES
    for k, out_ref in zip(which, out_refs):
        j = part_ref[k]
        if k < 2:
            last = weight_ref[:, QUAD * whole :].astype(jnp.float32)
            turned = pltpu.roll(last, lax.rem(LANES - QUARTER * j, LANES), 1)
            inside = lanes_of(last.shape[0]) < QUARTER
            out_ref[:, 0:whole] = weight_ref[:, pl.ds(pl.multiple_of(j * whole, LANES), whole)]
            out_ref[:, whole:] = jnp.where(inside, turned, 0.0).astype(jnp.bfloat16)
            continue
        count = weight_ref.shape[0] // 2 if k in halved else weight_ref.shape[0]
        start = pl.multiple_of(group_ref[0] * count, count) if k in halved else 0
        for t in range(tiles):
            column = pl.multiple_of(j * whole + t * LANES, LANES)
            out_ref[t * count : (t + 1) * count, :] = weight_ref[
                pl.ds(start, count), pl.ds(column, LANES)
            ]
        last = weight_ref[pl.ds(start, count), QUAD * whole :].astype(jnp.float32)
        size = count // QUAD
        owner = lanes_of(size) // QUARTER
        merged = jnp.zeros((size, LANES), jnp.float32)
        for m in range(QUAD):
            shift = lax.rem(LANES + QUARTER * (m - j), LANES)
            turned = pltpu.roll(last[m * size : (m + 1) * size], shift, 1)
            merged = jnp.where(owner == m, turned, merged)
        out_ref[tiles * count :, :] = merged.astype(jnp.bfloat16)


def open_far(far_refs, halved, opened_ref):
    width = opened_ref.shape[2]
    tiles = width // LANES - 1
    places = [(k - 2, 0) for k in (2, 3)] + [(k - 2, 1) for k in halved]
    for ref, (holder, part) in zip(far_refs, places):
        count = opened_ref.shape[1] // 2 if holder + 2 in halved else opened_ref.shape[1]
        base, size = part * count, count // QUAD
        inside = lanes_of(size) < QUARTER
        for t in range(tiles):
            opened_ref[holder, base : base + count, t * LANES : (t + 1) * LANES] = ref[
                t * count : (t + 1) * count, :
            ]
        packed = ref[tiles * count :, :].astype(jnp.float32)
        for m in range(QUAD):
            turned = pltpu.roll(packed, (LANES - QUARTER * m) % LANES, 1) if m else packed
            opened_ref[holder, base + m * size : base + (m + 1) * size, tiles * LANES :] = (
                jnp.where(inside, turned, 0.0).astype(jnp.bfloat16)
            )


def lay_out(resident, adapter_ref, used_ref, most_ref, target_ref, label_ref):
    blocks, total = adapter_ref.shape[1], target_ref.shape[1]
    rows = total // blocks
    adapter, used = adapter_ref[...], used_ref[...]
    down = lax.broadcasted_iota(jnp.int32, (blocks, blocks), 0)
    across = lax.broadcasted_iota(jnp.int32, (blocks, blocks), 1)

    def turned(value):
        return jnp.sum(jnp.where(down == across, value, 0), axis=1, keepdims=True)

    span = resident * QUAD
    quad = jnp.floor((adapter.astype(jnp.float32) + 0.5) * (1.0 / span)).astype(jnp.int32)
    order = adapter * blocks + lax.broadcasted_iota(jnp.int32, (1, blocks), 1)
    quad_down, order_down, used_down = turned(quad), turned(order), turned(used)
    same = quad_down == quad
    ahead = jnp.sum(jnp.where(same & (order < order_down), used, 0), axis=1, keepdims=True)
    within = jnp.sum(jnp.where(same, used, 0), axis=1, keepdims=True)
    most_ref[...] = jnp.broadcast_to(jnp.max(within, axis=0, keepdims=True), most_ref.shape)
    start = quad_down * total + ahead

    block = lax.broadcasted_iota(jnp.int32, (blocks, total), 0)
    row = lax.broadcasted_iota(jnp.int32, (blocks, total), 1) - block * rows
    place = jnp.where((row >= 0) & (row < used_down), start + row + 1, 0)
    target_ref[...] = jnp.sum(place, axis=0, keepdims=True) - 1
    block = lax.broadcasted_iota(jnp.int32, (total, blocks), 1)
    row = lax.broadcasted_iota(jnp.int32, (total, blocks), 0) - block * rows
    label = jnp.where((row >= 0) & (row < rows), adapter - quad * span + 1, 0)
    label_ref[...] = jnp.sum(label.astype(jnp.float32), axis=1, keepdims=True)


def first_pack_kernel(
    whole, resident, adapter_ref, used_ref, tokens_ref, out_ref, target_ref, label_ref, *refs
):
    normed_ref, chosen_ref, notes_ref, most_ref = refs

    @pl.when(pl.program_id(0) == 0)
    def _():
        lay_out(resident, adapter_ref, used_ref, most_ref, target_ref, label_ref)

    refs = (out_ref, normed_ref, chosen_ref, notes_ref)
    pack_kernel(whole, 0, most_ref, target_ref, label_ref, tokens_ref, *refs)


def pack_kernel(
    whole, base, most_ref, target_ref, label_ref, tokens_ref, out_ref, normed_ref, *refs
):
    chosen_ref, notes_ref = refs
    total = tokens_ref.shape[0]
    quads, tiles = out_ref.shape[0], whole // LANES
    cap = chosen_ref.shape[0] // quads
    step_lane = lanes_of(STEP)
    j = pl.program_id(0)

    @pl.when(j == 0)
    def _():
        values = tokens_ref[...].astype(jnp.float32)
        mean_sq = jnp.mean(values * values, axis=-1, keepdims=True)
        normed_ref[...] = (values * lax.rsqrt(mean_sq + 1e-06)).astype(jnp.bfloat16)
        most = most_ref[0:1, 0:1].astype(jnp.float32)
        label = jnp.where(lanes_of(total) == 0, label_ref[...], 0.0).astype(jnp.bfloat16)
        for q in range(quads):
            place = lax.broadcasted_iota(jnp.int32, (cap, total), 0) + (q * total + base)
            chosen = jnp.where(target_ref[...] == place, 1.0, 0.0).astype(jnp.bfloat16)
            chosen_ref[q * cap : (q + 1) * cap, :] = chosen
            labels = jnp.dot(chosen, label, preferred_element_type=jnp.float32)
            notes = jnp.where(step_lane == NOTE + cap // STEP, most, 0.0)
            for a in range(cap // STEP):
                turned = pltpu.roll(labels[a * STEP : (a + 1) * STEP], NOTE + a, 1)
                notes = jnp.where(step_lane == NOTE + a, turned, notes)
            notes_ref[q] = notes

    group_lane = lanes_of(QUARTER) // QUARTER
    chosen = chosen_ref[...]
    for t in range(0, tiles, 2):
        column = pl.multiple_of(j * whole + t * LANES, LANES)
        share = jnp.dot(
            chosen, normed_ref[:, pl.ds(column, 2 * LANES)], preferred_element_type=jnp.float32
        ).astype(jnp.bfloat16)
        for q in range(quads):
            for i in range(2):
                out_ref[q, 0, (t + i) * cap : (t + i + 1) * cap, :] = share[
                    q * cap : (q + 1) * cap, i * LANES : (i + 1) * LANES
                ]
    last = normed_ref[:, QUAD * whole :].astype(jnp.float32)
    last = pltpu.roll(last, lax.rem(LANES - QUARTER * j, LANES), 1).astype(jnp.bfloat16)
    ends = jnp.dot(chosen, last, preferred_element_type=jnp.float32)
    for q in range(quads):
        spare = jnp.zeros((QUAD * QUARTER - cap, LANES), jnp.float32)
        padded = jnp.concatenate([ends[q * cap : (q + 1) * cap], spare], axis=0)
        merged = padded[0:QUARTER]
        for m in range(1, QUAD):
            turned = pltpu.roll(padded[m * QUARTER : (m + 1) * QUARTER], m * QUARTER, 1)
            merged = jnp.where(group_lane == m, turned, merged)
        out_ref[q, 0, tiles * cap : tiles * cap + STEP, :] = merged[0:STEP].astype(jnp.bfloat16)
        out_ref[q, 0, tiles * cap + STEP :, :] = jnp.where(
            step_lane >= NOTE, notes_ref[q], merged[STEP:]
        ).astype(jnp.bfloat16)


def read_notes(rows_ref, cap, tiles, part_ref, resident, notes_ref, labels_ref, met_ref):
    senders = rows_ref.shape[0]
    for s in range(senders):
        notes_ref[s * STEP : (s + 1) * STEP, :] = rows_ref[s, tiles * cap + STEP :, :]
    steps = labels_ref.shape[0]
    row = lax.broadcasted_iota(jnp.int32, (steps, LANES), 0)
    wanted = jnp.where(lanes_of(steps) == NOTE + row, 1.0, 0.0).astype(jnp.bfloat16)
    labels = lax.dot_general(
        wanted, notes_ref[...], (((1,), (1,)), ((), ())), preferred_element_type=jnp.float32
    )
    labels_ref[...] = labels
    code = jnp.zeros((steps, 1), jnp.float32)
    for h in range(QUAD):
        first = part_ref[h].astype(jnp.float32) + 1.0
        met = jnp.where((labels >= first) & (labels < first + resident), 1.0, 0.0)
        code = code + (1 << h) * jnp.max(met, axis=1, keepdims=True)
    at = lax.broadcasted_iota(jnp.int32, (steps, 1), 0)
    for a in range(cap // STEP):
        met_ref[a] = jnp.max(jnp.where(at == a, code, 0.0)).astype(jnp.int32)


def for_holders(met_ref, first_ref, near_refs, opened_ref, halved, a, step):
    pairs = opened_ref.shape[1] // LANES
    for h in range(QUAD):
        base = first_ref[h].astype(jnp.float32) + 1.0
        firsts = [base + 2.0 * t for t in range(pairs)]
        if h in halved:
            firsts = [
                base + first_ref[QUAD + i].astype(jnp.float32) + 2.0 * t
                for i in range(2)
                for t in range(pairs // 2)
            ]

        @pl.when(lax.rem(met_ref[a] // (1 << h), 2) > 0)
        def _(h=h, firsts=firsts):
            is_first = lax.rem(met_ref[a], 1 << h) == 0
            step(near_refs[h] if h < 2 else opened_ref.at[h - 2], firsts, is_first)


def down_kernel(first_ref, rows_ref, *refs):
    near_refs, far_refs, out_ref, count_ref = refs[:2], refs[2:6], refs[6], refs[7]
    notes_ref, met_ref, opened_ref, batch_ref, picked_ref, labels_ref = refs[8:]
    senders, width = rows_ref.shape[0], batch_ref.shape[1]
    tiles = width // LANES - 1
    cap = out_ref.shape[0] * STEP
    rank = out_ref.shape[1]
    resident = opened_ref.shape[1] // rank
    dims = (((1,), (1,)), ((), ()))
    read_notes(rows_ref, cap, tiles, first_ref, resident, notes_ref, labels_ref, met_ref)
    notes = notes_ref[...].astype(jnp.float32)
    is_count = lanes_of(senders * STEP) == NOTE + cap // STEP
    count = jnp.max(jnp.where(is_count, notes, 0.0), axis=(0, 1), keepdims=True)
    count_ref[...] = jnp.broadcast_to(count, count_ref.shape).astype(jnp.bfloat16)
    open_far(far_refs, DOWN_HALVED, opened_ref)

    def one(a, carry):
        picked_ref[...] = jnp.zeros(picked_ref.shape, jnp.float32)

        @pl.when(met_ref[a] > 0)
        def _():
            shift = lax.rem(LANES - QUARTER * (a // 2), LANES)
            spot = pl.multiple_of(tiles * cap + lax.rem(a, 2) * STEP, STEP)
            for s in range(senders):
                rows = slice(s * STEP, (s + 1) * STEP)
                for t in range(tiles):
                    at = pl.multiple_of(t * cap + a * STEP, STEP)
                    batch_ref[rows, t * LANES : (t + 1) * LANES] = rows_ref[s, pl.ds(at, STEP), :]
                end = rows_ref[s, pl.ds(spot, STEP), :].astype(jnp.float32)
                batch_ref[rows, tiles * LANES :] = pltpu.roll(end, shift, 1).astype(jnp.bfloat16)
            label = labels_ref[pl.ds(a, 1), :]

            def step(weight_ref, firsts, is_first):
                product = lax.dot_general(
                    weight_ref[...], batch_ref[...], dims, preferred_element_type=jnp.float32
                )
                picked = picked_ref[...]
                for t, first in enumerate(firsts):
                    for i in range(2):
                        at = (2 * t + i) * rank
                        picked = jnp.where(
                            label == first + i, product[at : at + rank, :], picked
                        )
                picked_ref[...] = picked

            for_holders(met_ref, first_ref, near_refs, opened_ref, DOWN_HALVED, a, step)

        out_ref[a] = picked_ref[...]
        return carry

    lax.fori_loop(0, cap // STEP, one, 0)


def pair_kernel(own_ref, other_ref, out_ref):
    out_ref[...] = (own_ref[...] + other_ref[...]).astype(jnp.bfloat16)


def up_kernel(first_ref, met_ref, notes_ref, *refs):
    sum_refs, near_refs, far_refs, out_ref = refs[:2], refs[2:4], refs[4:7], refs[7]
    opened_ref, delta_ref, ends_ref, label_ref, twice_ref = refs[8:]
    senders, width = out_ref.shape[0], opened_ref.shape[2]
    tiles = width // LANES - 1
    rank = sum_refs[0].shape[1]
    kept = (out_ref.shape[1] - QUARTER) // tiles
    group_lane = lanes_of(STEP) // QUARTER
    open_far(far_refs, UP_HALVED, opened_ref)
    ends_ref[...] = jnp.zeros(ends_ref.shape, jnp.float32)
    low = jnp.where(lanes_of(senders * STEP) < HALF, 0.0, 1.0)
    rank_row = lax.broadcasted_iota(jnp.int32, (rank, LANES), 0)
    twofold = jnp.where(lax.rem(lanes_of(rank), rank) == rank_row, 1.0, 0.0).astype(jnp.bfloat16)

    note_row = lax.broadcasted_iota(jnp.int32, (LANES, LANES), 0)
    for a in range(kept // STEP):
        wanted = jnp.where(note_row == NOTE + a, 1.0, 0.0).astype(jnp.bfloat16)
        label_ref[a] = jnp.dot(notes_ref[...], wanted, preferred_element_type=jnp.float32) - low
        down = sum_refs[0][a].astype(jnp.float32) + sum_refs[1][a].astype(jnp.float32)
        twice_ref[a] = lax.dot_general(
            down.astype(jnp.bfloat16),
            twofold,
            (((0,), (0,)), ((), ())),
            preferred_element_type=jnp.float32,
        )

    def one(a, carry):
        @pl.when(met_ref[a] == 0)
        def _():
            delta_ref[...] = jnp.zeros(delta_ref.shape, jnp.float32)

        @pl.when(met_ref[a] > 0)
        def _():
            label, twice = label_ref[a], twice_ref[a]

            def step(weight_ref, firsts, is_first):
                placed = [jnp.where(label == first, twice, 0.0) for first in firsts]
                placed = jnp.concatenate(placed, axis=1).astype(jnp.bfloat16)
                before = jnp.where(is_first, 0.0, delta_ref[...])
                delta_ref[...] = before + jnp.dot(
                    placed, weight_ref[...], preferred_element_type=jnp.float32
                )

            for_holders(met_ref, first_ref, near_refs, opened_ref, UP_HALVED, a, step)

        spot = pl.multiple_of(lax.rem(a, 2) * STEP, STEP)
        for s in range(senders):
            rows = slice(s * STEP, (s + 1) * STEP)
            for t in range(tiles):
                at = pl.multiple_of(t * kept + a * STEP, STEP)
                out_ref[s, pl.ds(at, STEP), :] = delta_ref[
                    rows, t * LANES : (t + 1) * LANES
                ].astype(jnp.bfloat16)
            turned = pltpu.roll(delta_ref[rows, tiles * LANES :], QUARTER * (a // 2), 1)
            ends_ref[s, pl.ds(spot, STEP), :] = jnp.where(
                group_lane == a // 2, turned, ends_ref[s, pl.ds(spot, STEP), :]
            )
        return carry

    lax.fori_loop(0, kept // STEP, one, 0)
    for s in range(senders):
        out_ref[s, tiles * kept :, :] = ends_ref[s].astype(jnp.bfloat16)


def mix_kernel(whole, bases, target_ref, tokens_ref, *refs):
    returned_refs, out_ref = refs[:-1], refs[-1]
    total = tokens_ref.shape[0]
    tiles, quads = whole // LANES, returned_refs[0].shape[0] // QUAD
    lane = lanes_of(total)
    chosen = []
    for base, ref in zip(bases, returned_refs):
        kept = (ref.shape[1] - QUARTER) // tiles
        spot = lax.broadcasted_iota(jnp.int32, (total, quads * kept), 1)
        place = spot // kept * total + spot % kept + base
        chosen.append(jnp.where(target_ref[...] == place, 1.0, 0.0).astype(jnp.bfloat16))
    end = jnp.zeros((total, LANES), jnp.float32)
    for j in range(QUAD):
        delta = 0.0
        for choice, ref in zip(chosen, returned_refs):
            kept = choice.shape[1] // quads
            shares = []
            for q in range(quads):
                d = q * QUAD + j
                parts = [ref[d, t * kept : (t + 1) * kept, :] for t in range(tiles)]
                packed = ref[d, tiles * kept :, :].astype(jnp.float32)
                groups = [packed]
                for m in range(1, QUAD):
                    groups.append(pltpu.roll(packed, LANES - QUARTER * m, 1))
                parts.append(jnp.concatenate(groups, axis=0)[0:kept].astype(jnp.bfloat16))
                shares.append(jnp.concatenate(parts, axis=1))
            share = jnp.concatenate(shares, axis=0)
            delta = delta + jnp.dot(choice, share, preferred_element_type=jnp.float32)
        columns = slice(j * whole, (j + 1) * whole)
        out_ref[:, columns] = (
            tokens_ref[:, columns].astype(jnp.float32) + delta[:, 0:whole]
        ).astype(jnp.bfloat16)
        last = delta[:, whole:]
        turned = pltpu.roll(last, QUARTER * j, 1) if j else last
        end = jnp.where((lane >= QUARTER * j) & (lane < QUARTER * (j + 1)), turned, end)
    out_ref[:, QUAD * whole :] = (
        tokens_ref[:, QUAD * whole :].astype(jnp.float32) + end
    ).astype(jnp.bfloat16)


def call(kernel, out_shape, in_specs, flops, moved, after=(), scratch=(), out_specs=None):
    many = isinstance(out_shape, list)
    skipped = len(after)
    body = (lambda *refs: kernel(*refs[skipped:])) if skipped else kernel
    run = pl.pallas_call(
        body,
        out_shape=out_shape,
        in_specs=[pl.BlockSpec(memory_space=pl.ANY)] * skipped + in_specs,
        out_specs=out_specs or ([VMEM] * len(out_shape) if many else VMEM),
        scratch_shapes=scratch,
        compiler_params=pltpu.CompilerParams(vmem_limit_bytes=18 * 2**20),
        cost_estimate=pl.CostEstimate(flops=flops, bytes_accessed=moved, transcendentals=0),
    )
    return functools.partial(run, *after)


def exchange(value):
    return lax.all_to_all(value, "adapter", split_axis=0, concat_axis=0, tiled=True)


def towards(value, k, devices):
    return lax.ppermute(value, "adapter", [(i, i ^ k) for i in range(devices)])


def swapped(value):
    return lax.ppermute(value, "groups", [(0, 1), (1, 0)])


def stand_behind(value, *earlier):
    return pl.pallas_call(
        lambda *refs: None,
        out_shape=jax.ShapeDtypeStruct(value.shape, value.dtype),
        in_specs=[pl.BlockSpec(memory_space=pl.ANY)] * (1 + len(earlier)),
        out_specs=pl.BlockSpec(memory_space=pl.ANY),
        input_output_aliases={0: 0},
    )(value, *earlier)


def pack_grid(kernel, cap, whole, devices, extra, scratch, *operands):
    total, width = operands[-1].shape
    quads, rows = devices // QUAD, whole // LANES * cap + QUARTER

    def all_of(shape):
        return pl.BlockSpec(shape, lambda j: (0,) * len(shape))

    shares, *rest = pl.pallas_call(
        kernel,
        grid=(QUAD,),
        out_shape=[jax.ShapeDtypeStruct((quads, QUAD, rows, LANES), jnp.bfloat16), *extra],
        in_specs=[all_of(operand.shape) for operand in operands],
        out_specs=[
            pl.BlockSpec((quads, 1, rows, LANES), lambda j: (0, j, 0, 0)),
            *[all_of(shape.shape) for shape in extra],
        ],
        scratch_shapes=[
            pltpu.VMEM((total, width), jnp.bfloat16),
            pltpu.VMEM((quads * cap, total), jnp.bfloat16),
            pltpu.VMEM((quads, STEP, LANES), jnp.float32),
            *scratch,
        ],
        compiler_params=pltpu.CompilerParams(vmem_limit_bytes=60 * 2**20),
        cost_estimate=pl.CostEstimate(
            flops=2 * devices * cap * total * whole,
            bytes_accessed=2 * (total * width + devices * cap * whole),
            transcendentals=0,
        ),
    )(*operands)
    return shares.reshape(devices, rows, LANES), *rest


def first_pack_call(cap, whole, devices, resident, adapter, used, tokens):
    blocks, rows, width = tokens.shape
    total = blocks * rows
    extra = [
        jax.ShapeDtypeStruct((1, total), jnp.int32),
        jax.ShapeDtypeStruct((total, 1), jnp.float32),
    ]
    kernel = functools.partial(first_pack_kernel, whole, resident)
    operands = adapter.reshape(1, blocks), used.reshape(1, blocks), tokens.reshape(total, width)
    scratch = [pltpu.VMEM((8, LANES), jnp.int32)]
    return pack_grid(kernel, cap, whole, devices, extra, scratch, *operands)


def pack_call(cap, base, whole, devices, target, label, tokens):
    no_count = jnp.zeros((8, LANES), jnp.int32)
    kernel = functools.partial(pack_kernel, whole, base)
    operands = no_count, target, label, tokens.reshape(-1, tokens.shape[2])
    return pack_grid(kernel, cap, whole, devices, [], [], *operands)[0]


def down_call(cap, first, arrived, down_weights, after):
    devices = arrived.shape[0]
    columns, share = down_weights[0].shape
    return call(
        down_kernel,
        [
            jax.ShapeDtypeStruct((cap // STEP, HALF, devices * STEP), jnp.float32),
            jax.ShapeDtypeStruct((STEP, LANES), jnp.bfloat16),
            jax.ShapeDtypeStruct((devices * STEP, LANES), jnp.bfloat16),
            jax.ShapeDtypeStruct((8,), jnp.int32),
        ],
        [SMEM] + [VMEM] * (1 + len(down_weights)),
        0,
        0,
        after,
        [
            pltpu.VMEM((2, columns, share), jnp.bfloat16),
            pltpu.VMEM((devices * STEP, share), jnp.bfloat16),
            pltpu.VMEM((HALF, devices * STEP), jnp.float32),
            pltpu.VMEM((8, devices * STEP), jnp.float32),
        ],
        [VMEM, VMEM, VMEM, SMEM],
    )(first, arrived, *down_weights)


def quad_sums(partial, devices):
    pair = call(
        pair_kernel, jax.ShapeDtypeStruct(partial.shape, jnp.bfloat16), [VMEM, VMEM], 0, 0
    )(partial, towards(partial, 1, devices))
    return [pair, towards(pair, 2, devices)]


def up_call(kept, first, met, notes, sums, up_weights):
    devices = notes.shape[0] // STEP
    columns, share = up_weights[0].shape
    shape = (devices, (share // LANES - 1) * kept + QUARTER, LANES)
    return call(
        up_kernel,
        jax.ShapeDtypeStruct(shape, jnp.bfloat16),
        [SMEM, SMEM] + [VMEM] * (3 + len(up_weights)),
        2 * devices * kept * QUAD * columns * share,
        2 * (2 * devices * kept + QUAD * columns) * share,
        scratch=[
            pltpu.VMEM((2, columns, share), jnp.bfloat16),
            pltpu.VMEM((devices * STEP, share), jnp.float32),
            pltpu.VMEM((devices, QUARTER, LANES), jnp.float32),
            *[pltpu.VMEM((kept // STEP, devices * STEP, LANES), jnp.float32)] * 2,
        ],
    )(first, met, notes, *sums, *up_weights)


def back_and_mix(
    kept, more, tokens, target, label, first, met, notes, sums, down_weights, up_weights, *unused
):
    blocks, rows, width = tokens.shape
    total = blocks * rows
    devices = notes.shape[0] // STEP
    whole = up_weights[0].shape[1] - LANES
    pieces = [exchange(up_call(kept, first, met, notes, sums, up_weights))]
    if more:
        outgoing = pack_call(more, kept, whole, devices, target, label, tokens)
        arrived = exchange(outgoing)
        partial, unused_count, notes, met = down_call(more, first, arrived, down_weights, [])
        sums = quad_sums(partial, devices)
        pieces.append(exchange(up_call(more, first, met, notes, sums, up_weights)))
    mixed = call(
        functools.partial(mix_kernel, whole, (0, kept)[: len(pieces)]),
        jax.ShapeDtypeStruct((total, width), jnp.bfloat16),
        [VMEM] * (2 + len(pieces)),
        2 * devices * (kept + more) * total * whole,
        2 * (2 * total * width + devices * (kept + more) * whole),
    )(target.reshape(total, 1), tokens.reshape(total, width), *pieces)
    return mixed.reshape(tokens.shape)


def start_again(
    tokens, target, label, first, met, notes, sums, down_weights, up_weights, *arguments
):
    return rows_to_holders(tokens, *arguments)


def rows_to_quads(
    tokens, request_block_adapter, request_block_rows, adapter_down_weight, adapter_up_weight
):
    blocks, rows, width = tokens.shape
    devices = lax.axis_size("adapter")
    resident, rank, unused_width = adapter_up_weight.shape
    total = blocks * rows
    columns = resident * rank
    whole = width // LANES // QUAD * LANES
    share = whole + LANES
    bf16, i32 = jnp.bfloat16, jnp.int32

    me = lax.axis_index("adapter").astype(i32)
    group = lax.axis_index("groups").astype(i32)
    parts = jnp.bitwise_xor(me % QUAD, jnp.arange(QUAD, dtype=i32))
    halves = jnp.stack([group, 1 - group]) * (resident // 2)
    first = jnp.concatenate([parts * resident, halves]).astype(i32)
    tiles = whole // LANES

    def shares(weight, which, halved, after):
        shapes = []
        for k in which:
            count = columns // 2 if k in halved else columns
            far = (count * tiles + count // QUAD, LANES)
            shapes.append(jax.ShapeDtypeStruct((columns, share) if k < 2 else far, bf16))
        return call(
            functools.partial(weight_kernel, whole, which, halved),
            shapes,
            [SMEM, SMEM, VMEM],
            0,
            len(which) * columns * width,
            after,
        )(parts, group.reshape(1), weight)

    down_weight = adapter_down_weight.transpose(0, 2, 1).reshape(columns, width)
    up_weight = adapter_up_weight.reshape(columns, width)
    down_far = shares(down_weight, (2, 3), DOWN_HALVED, [])
    up_far = shares(up_weight, (2, 3), UP_HALVED, down_far[:1])
    down_near = shares(down_weight, (0, 1), (), up_far[:1])
    up_near = shares(up_weight, (0, 1), (), down_near[:1])
    down_weights = [down_near[0], towards(down_near[1], 1, devices)]
    down_weights += [towards(value, k, devices) for k, value in zip((2, 3), down_far)]
    up_weights = [up_near[0], towards(up_near[1], 1, devices)]
    up_weights += [towards(value, k, devices) for k, value in zip((2, 3), up_far)]
    down_weights[2] = stand_behind(down_weights[2], up_near[0])
    down_weights += [swapped(down_weights[k]) for k in DOWN_HALVED]
    up_weights += [swapped(up_weights[k]) for k in UP_HALVED]

    caps = [total * 5 // 16, total * 6 // 16, total * 7 // 16]
    cap = caps[-1]
    outgoing, target, label = first_pack_call(
        cap, whole, devices, resident, request_block_adapter, request_block_rows, tokens
    )
    arrived = exchange(outgoing)
    partial, count, notes, met = down_call(cap, first, arrived, down_weights, up_weights[2:3])
    sums = quad_sums(partial, devices)
    count = count[0:1, 0:1]
    most = jnp.maximum(count, swapped(count))[0, 0].astype(jnp.float32)
    branches = [functools.partial(back_and_mix, kept, 0) for kept in caps]
    branches += [functools.partial(back_and_mix, cap, STEP), start_again]
    return lax.switch(
        sum((most > limit).astype(i32) for limit in [*caps, cap + STEP]),
        branches,
        tokens,
        target,
        label,
        first,
        met,
        notes,
        sums,
        down_weights,
        up_weights,
        request_block_adapter,
        request_block_rows,
        adapter_down_weight,
        adapter_up_weight,
    )


def solution(mesh):
    placed = (
        P(("groups", "adapter"), None, None),
        P(("groups", "adapter")),
        P(("groups", "adapter")),
        P("adapter", None, None),
        P("adapter", None, None),
    )

    def per_device(tokens, request_block_adapter, request_block_rows, down_weight, up_weight):
        blocks, rows, width = tokens.shape
        devices = mesh.shape["adapter"]
        slots = max(1, 4 * blocks // devices)
        quads = devices % QUAD == 0 and slots * QUAD >= blocks
        quads = quads and width % (QUAD * LANES) == LANES and up_weight.shape[1] == HALF
        quads = quads and blocks * rows * 7 // 16 == 7 * STEP and mesh.shape["groups"] == 2
        plan = rows_to_quads if quads else rows_to_holders
        return plan(tokens, request_block_adapter, request_block_rows, down_weight, up_weight)

    return jax.shard_map(
        per_device,
        mesh=mesh,
        in_specs=placed,
        out_specs=P(("groups", "adapter"), None, None),
        check_vma=False,
    )
```

```python
import functools

import jax
import jax.numpy as jnp
from jax import lax
from jax.experimental import pallas as pl
from jax.experimental.pallas import tpu as pltpu
from jax.sharding import PartitionSpec as P

LANES = 128
HALF = 64
QUAD = 4
QUARTER = 32
STEP = 16
NOTE = 96
DOWN_HALVED = (2, 3)
UP_HALVED = (2,)
VMEM = pl.BlockSpec(memory_space=pltpu.VMEM)
SMEM = pl.BlockSpec(memory_space=pltpu.SMEM)


def normalise(tokens):
    values = tokens.astype(jnp.float32)
    mean_sq = jnp.mean(values * values, axis=-1, keepdims=True)
    return (values, (values * lax.rsqrt(mean_sq + 1e-06)).astype(jnp.bfloat16))


def resident_update(hidden_state, block_labels, adapter_down_weight, adapter_up_weight):
    feature_width = hidden_state.shape[-1]
    leading = hidden_state.shape[:-1]
    resident_rows, unused_value, inner_rank = adapter_down_weight.shape
    flattened_tokens = hidden_state.reshape(-1, feature_width)
    down_matrix = jnp.einsum(
        "tq,iqg->tig", flattened_tokens, adapter_down_weight, preferred_element_type=jnp.float32
    )
    down_matrix = down_matrix.astype(jnp.bfloat16).reshape(
        flattened_tokens.shape[0], resident_rows * inner_rank
    )
    column_owner = jnp.arange(resident_rows * inner_rank, dtype=jnp.int32) // inner_rank
    picked = block_labels.reshape(-1, 1) == column_owner[None, :]
    down_matrix = jnp.where(picked, down_matrix, jnp.zeros_like(down_matrix))
    lowrank_update = jnp.dot(
        down_matrix,
        adapter_up_weight.reshape(resident_rows * inner_rank, feature_width),
        preferred_element_type=jnp.float32,
    )
    return lowrank_update.astype(jnp.bfloat16).reshape(leading + (feature_width,))


def rows_to_holders(
    tokens, request_block_adapter, request_block_rows, adapter_down_weight, adapter_up_weight
):
    blocks, rows, feature_width = tokens.shape
    devices = lax.axis_size("adapter")
    resident_rows = adapter_down_weight.shape[0]
    slots = max(1, 4 * blocks // devices)
    values, normed = normalise(tokens)
    owner = request_block_adapter // resident_rows
    within = request_block_adapter - owner * resident_rows
    serial = jnp.arange(blocks, dtype=jnp.int32)
    earlier = (owner[:, None] == owner[None, :]) & (serial[None, :] < serial[:, None])
    position = owner * slots + jnp.sum(earlier, axis=1)
    outgoing = (
        jnp.zeros((devices * slots, rows, feature_width), jnp.bfloat16).at[position].set(normed)
    )
    outgoing = outgoing.reshape(devices, slots, rows, feature_width)
    block_labels = jnp.full((devices * slots,), -1, jnp.int32).at[position].set(within)
    block_labels = jnp.broadcast_to(block_labels[:, None], (devices * slots, rows)).reshape(
        devices, slots, rows
    )
    arriving_rows, row_markers = (
        lax.all_to_all(outgoing, "adapter", split_axis=0, concat_axis=0, tiled=True),
        lax.all_to_all(block_labels, "adapter", split_axis=0, concat_axis=0, tiled=True),
    )
    lowrank_update = resident_update(
        arriving_rows, row_markers, adapter_down_weight, adapter_up_weight
    )
    returned = lax.all_to_all(lowrank_update, "adapter", split_axis=0, concat_axis=0, tiled=True)
    mine = returned.reshape(devices * slots, rows, feature_width)[position]
    live = jnp.arange(rows, dtype=jnp.int32)[None, :] < request_block_rows[:, None]
    mixed = values + jnp.where(live[:, :, None], mine.astype(jnp.float32), jnp.float32(0.0))
    return mixed.astype(jnp.bfloat16)


def lanes_of(rows):
    return lax.broadcasted_iota(jnp.int32, (rows, LANES), 1)


def weight_kernel(whole, which, halved, part_ref, group_ref, weight_ref, *out_refs):
    tiles = whole // LANES
    for k, out_ref in zip(which, out_refs):
        j = part_ref[k]
        if k < 2:
            last = weight_ref[:, QUAD * whole :].astype(jnp.float32)
            turned = pltpu.roll(last, lax.rem(LANES - QUARTER * j, LANES), 1)
            inside = lanes_of(last.shape[0]) < QUARTER
            out_ref[:, 0:whole] = weight_ref[:, pl.ds(pl.multiple_of(j * whole, LANES), whole)]
            out_ref[:, whole:] = jnp.where(inside, turned, 0.0).astype(jnp.bfloat16)
            continue
        count = weight_ref.shape[0] // 2 if k in halved else weight_ref.shape[0]
        start = pl.multiple_of(group_ref[0] * count, count) if k in halved else 0
        for t in range(tiles):
            column = pl.multiple_of(j * whole + t * LANES, LANES)
            out_ref[t * count : (t + 1) * count, :] = weight_ref[
                pl.ds(start, count), pl.ds(column, LANES)
            ]
        last = weight_ref[pl.ds(start, count), QUAD * whole :].astype(jnp.float32)
        size = count // QUAD
        owner = lanes_of(size) // QUARTER
        merged = jnp.zeros((size, LANES), jnp.float32)
        for m in range(QUAD):
            shift = lax.rem(LANES + QUARTER * (m - j), LANES)
            turned = pltpu.roll(last[m * size : (m + 1) * size], shift, 1)
            merged = jnp.where(owner == m, turned, merged)
        out_ref[tiles * count :, :] = merged.astype(jnp.bfloat16)


def open_far(far_refs, halved, opened_ref):
    width = opened_ref.shape[2]
    tiles = width // LANES - 1
    places = [(k - 2, 0) for k in (2, 3)] + [(k - 2, 1) for k in halved]
    for ref, (holder, part) in zip(far_refs, places):
        count = opened_ref.shape[1] // 2 if holder + 2 in halved else opened_ref.shape[1]
        base, size = part * count, count // QUAD
        inside = lanes_of(size) < QUARTER
        for t in range(tiles):
            opened_ref[holder, base : base + count, t * LANES : (t + 1) * LANES] = ref[
                t * count : (t + 1) * count, :
            ]
        packed = ref[tiles * count :, :].astype(jnp.float32)
        for m in range(QUAD):
            turned = pltpu.roll(packed, (LANES - QUARTER * m) % LANES, 1) if m else packed
            opened_ref[holder, base + m * size : base + (m + 1) * size, tiles * LANES :] = (
                jnp.where(inside, turned, 0.0).astype(jnp.bfloat16)
            )


def lay_out(resident, adapter_ref, used_ref, most_ref, target_ref, label_ref):
    blocks, total = adapter_ref.shape[1], target_ref.shape[1]
    rows = total // blocks
    adapter, used = adapter_ref[...], used_ref[...]
    down = lax.broadcasted_iota(jnp.int32, (blocks, blocks), 0)
    across = lax.broadcasted_iota(jnp.int32, (blocks, blocks), 1)

    def turned(value):
        return jnp.sum(jnp.where(down == across, value, 0), axis=1, keepdims=True)

    span = resident * QUAD
    quad = jnp.floor((adapter.astype(jnp.float32) + 0.5) * (1.0 / span)).astype(jnp.int32)
    order = adapter * blocks + lax.broadcasted_iota(jnp.int32, (1, blocks), 1)
    quad_down, order_down, used_down = turned(quad), turned(order), turned(used)
    same = quad_down == quad
    ahead = jnp.sum(jnp.where(same & (order < order_down), used, 0), axis=1, keepdims=True)
    within = jnp.sum(jnp.where(same, used, 0), axis=1, keepdims=True)
    most_ref[...] = jnp.broadcast_to(jnp.max(within, axis=0, keepdims=True), most_ref.shape)
    start = quad_down * total + ahead

    block = lax.broadcasted_iota(jnp.int32, (blocks, total), 0)
    row = lax.broadcasted_iota(jnp.int32, (blocks, total), 1) - block * rows
    place = jnp.where((row >= 0) & (row < used_down), start + row + 1, 0)
    target_ref[...] = jnp.sum(place, axis=0, keepdims=True) - 1
    block = lax.broadcasted_iota(jnp.int32, (total, blocks), 1)
    row = lax.broadcasted_iota(jnp.int32, (total, blocks), 0) - block * rows
    label = jnp.where((row >= 0) & (row < rows), adapter - quad * span + 1, 0)
    label_ref[...] = jnp.sum(label.astype(jnp.float32), axis=1, keepdims=True)


def first_pack_kernel(
    whole, cap, resident, adapter_ref, used_ref, tokens_ref, out_ref, target_ref, label_ref, *refs
):
    normed_ref, most_ref = refs
    lay_out(resident, adapter_ref, used_ref, most_ref, target_ref, label_ref)
    pack_kernel(
        whole, cap, 0, most_ref, target_ref, label_ref, tokens_ref, out_ref, normed_ref
    )


def pack_kernel(
    whole, cap, base, most_ref, target_ref, label_ref, tokens_ref, out_ref, normed_ref
):
    values = tokens_ref[...].astype(jnp.float32)
    mean_sq = jnp.mean(values * values, axis=-1, keepdims=True)
    normed_ref[...] = (values * lax.rsqrt(mean_sq + 1e-06)).astype(jnp.bfloat16)
    total = tokens_ref.shape[0]
    quads, tiles = out_ref.shape[0] // QUAD, whole // LANES
    lane = lanes_of(total)
    last = normed_ref[:, QUAD * whole :].astype(jnp.float32)
    label = jnp.where(lane == QUARTER, label_ref[...], 0.0)
    ends = []
    for j in range(QUAD):
        turned = pltpu.roll(last, (LANES - QUARTER * j) % LANES, 1) if j else last
        ends.append(jnp.where(lane < QUARTER, turned, label).astype(jnp.bfloat16))
    most = most_ref[0:1, 0:1].astype(jnp.float32)
    group_lane = lanes_of(QUARTER) // QUARTER
    step_lane = lanes_of(STEP)
    chosen = []
    for q in range(quads):
        place = lax.broadcasted_iota(jnp.int32, (cap, total), 0) + (q * total + base)
        chosen.append(jnp.where(target_ref[...] == place, 1.0, 0.0).astype(jnp.bfloat16))
    chosen = jnp.concatenate(chosen, axis=0)
    notes = [jnp.where(step_lane == NOTE + cap // STEP, most, 0.0)] * quads
    for j in range(QUAD):
        for t in range(tiles):
            column = j * whole + t * LANES
            if t % 2 == 0:
                count = min(2, tiles - t) * LANES
                share = jnp.dot(
                    chosen,
                    normed_ref[:, column : column + count],
                    preferred_element_type=jnp.float32,
                ).astype(jnp.bfloat16)
            for q in range(quads):
                out_ref[q * QUAD + j, t * cap : (t + 1) * cap, :] = share[
                    q * cap : (q + 1) * cap, t % 2 * LANES : (t % 2 + 1) * LANES
                ]
        end_rows = jnp.dot(chosen, ends[j], preferred_element_type=jnp.float32)
        for q in range(quads):
            end = end_rows[q * cap : (q + 1) * cap]
            if j == 0:
                for a in range(cap // STEP):
                    turned = pltpu.roll(end[a * STEP : (a + 1) * STEP], NOTE + a - QUARTER, 1)
                    notes[q] = jnp.where(step_lane == NOTE + a, turned, notes[q])
            padded = jnp.concatenate(
                [end, jnp.zeros((QUAD * QUARTER - cap, LANES), jnp.float32)], axis=0
            )
            merged = padded[0:QUARTER]
            for m in range(1, QUAD):
                turned = pltpu.roll(padded[m * QUARTER : (m + 1) * QUARTER], m * QUARTER, 1)
                merged = jnp.where(group_lane == m, turned, merged)
            out_ref[q * QUAD + j, tiles * cap : tiles * cap + STEP, :] = merged[0:STEP].astype(
                jnp.bfloat16
            )
            out_ref[q * QUAD + j, tiles * cap + STEP :, :] = jnp.where(
                step_lane >= NOTE, notes[q], merged[STEP:]
            ).astype(jnp.bfloat16)


def read_notes(rows_ref, cap, tiles, part_ref, resident, notes_ref, labels_ref, met_ref):
    senders = rows_ref.shape[0]
    for s in range(senders):
        notes_ref[s * STEP : (s + 1) * STEP, :] = rows_ref[s, tiles * cap + STEP :, :]
    steps = labels_ref.shape[0]
    row = lax.broadcasted_iota(jnp.int32, (steps, LANES), 0)
    wanted = jnp.where(lanes_of(steps) == NOTE + row, 1.0, 0.0).astype(jnp.bfloat16)
    labels = lax.dot_general(
        wanted, notes_ref[...], (((1,), (1,)), ((), ())), preferred_element_type=jnp.float32
    )
    labels_ref[...] = labels
    code = jnp.zeros((steps, 1), jnp.float32)
    for h in range(QUAD):
        first = part_ref[h].astype(jnp.float32) + 1.0
        met = jnp.where((labels >= first) & (labels < first + resident), 1.0, 0.0)
        code = code + (1 << h) * jnp.max(met, axis=1, keepdims=True)
    at = lax.broadcasted_iota(jnp.int32, (steps, 1), 0)
    for a in range(cap // STEP):
        met_ref[a] = jnp.max(jnp.where(at == a, code, 0.0)).astype(jnp.int32)


def for_holders(met_ref, first_ref, near_refs, opened_ref, halved, a, step):
    pairs = opened_ref.shape[1] // LANES
    for h in range(QUAD):
        base = first_ref[h].astype(jnp.float32) + 1.0
        firsts = [base + 2.0 * t for t in range(pairs)]
        if h in halved:
            firsts = [
                base + first_ref[QUAD + i].astype(jnp.float32) + 2.0 * t
                for i in range(2)
                for t in range(pairs // 2)
            ]

        @pl.when(lax.rem(met_ref[a] // (1 << h), 2) > 0)
        def _(h=h, firsts=firsts):
            is_first = lax.rem(met_ref[a], 1 << h) == 0
            step(near_refs[h] if h < 2 else opened_ref.at[h - 2], firsts, is_first)


def down_kernel(first_ref, rows_ref, *refs):
    near_refs, far_refs, out_ref, count_ref = refs[:2], refs[2:6], refs[6], refs[7]
    notes_ref, met_ref, opened_ref, batch_ref, picked_ref, labels_ref = refs[8:]
    senders, width = rows_ref.shape[0], batch_ref.shape[1]
    tiles = width // LANES - 1
    cap = out_ref.shape[0] * STEP
    rank = out_ref.shape[1]
    resident = opened_ref.shape[1] // rank
    dims = (((1,), (1,)), ((), ()))
    read_notes(rows_ref, cap, tiles, first_ref, resident, notes_ref, labels_ref, met_ref)
    notes = notes_ref[...].astype(jnp.float32)
    is_count = lanes_of(senders * STEP) == NOTE + cap // STEP
    count = jnp.max(jnp.where(is_count, notes, 0.0), axis=(0, 1), keepdims=True)
    count_ref[...] = jnp.broadcast_to(count, count_ref.shape).astype(jnp.bfloat16)
    open_far(far_refs, DOWN_HALVED, opened_ref)

    def one(a, carry):
        picked_ref[...] = jnp.zeros(picked_ref.shape, jnp.float32)

        @pl.when(met_ref[a] > 0)
        def _():
            shift = lax.rem(LANES - QUARTER * (a // 2), LANES)
            spot = pl.multiple_of(tiles * cap + lax.rem(a, 2) * STEP, STEP)
            for s in range(senders):
                rows = slice(s * STEP, (s + 1) * STEP)
                for t in range(tiles):
                    at = pl.multiple_of(t * cap + a * STEP, STEP)
                    batch_ref[rows, t * LANES : (t + 1) * LANES] = rows_ref[s, pl.ds(at, STEP), :]
                end = rows_ref[s, pl.ds(spot, STEP), :].astype(jnp.float32)
                batch_ref[rows, tiles * LANES :] = pltpu.roll(end, shift, 1).astype(jnp.bfloat16)
            label = labels_ref[pl.ds(a, 1), :]

            def step(weight_ref, firsts, is_first):
                product = lax.dot_general(
                    weight_ref[...], batch_ref[...], dims, preferred_element_type=jnp.float32
                )
                picked = picked_ref[...]
                for t, first in enumerate(firsts):
                    for i in range(2):
                        at = (2 * t + i) * rank
                        picked = jnp.where(
                            label == first + i, product[at : at + rank, :], picked
                        )
                picked_ref[...] = picked

            for_holders(met_ref, first_ref, near_refs, opened_ref, DOWN_HALVED, a, step)

        out_ref[a] = picked_ref[...]
        return carry

    lax.fori_loop(0, cap // STEP, one, 0)


def pair_kernel(own_ref, other_ref, out_ref):
    out_ref[...] = (own_ref[...] + other_ref[...]).astype(jnp.bfloat16)


def up_kernel(first_ref, met_ref, notes_ref, *refs):
    sum_refs, near_refs, far_refs, out_ref = refs[:2], refs[2:4], refs[4:7], refs[7]
    opened_ref, delta_ref, ends_ref, label_ref, twice_ref = refs[8:]
    senders, width = out_ref.shape[0], opened_ref.shape[2]
    tiles = width // LANES - 1
    rank = sum_refs[0].shape[1]
    kept = (out_ref.shape[1] - QUARTER) // tiles
    full = kept // STEP * STEP
    group_lane = lanes_of(STEP) // QUARTER
    open_far(far_refs, UP_HALVED, opened_ref)
    ends_ref[...] = jnp.zeros(ends_ref.shape, jnp.float32)
    low = jnp.where(lanes_of(senders * STEP) < HALF, 0.0, 1.0)
    rank_row = lax.broadcasted_iota(jnp.int32, (rank, LANES), 0)
    twofold = jnp.where(lax.rem(lanes_of(rank), rank) == rank_row, 1.0, 0.0).astype(jnp.bfloat16)

    note_row = lax.broadcasted_iota(jnp.int32, (LANES, LANES), 0)
    for a in range(label_ref.shape[0]):
        wanted = jnp.where(note_row == NOTE + a, 1.0, 0.0).astype(jnp.bfloat16)
        label_ref[a] = jnp.dot(notes_ref[...], wanted, preferred_element_type=jnp.float32) - low
        down = sum_refs[0][a].astype(jnp.float32) + sum_refs[1][a].astype(jnp.float32)
        twice_ref[a] = lax.dot_general(
            down.astype(jnp.bfloat16),
            twofold,
            (((0,), (0,)), ((), ())),
            preferred_element_type=jnp.float32,
        )

    def one(a, carry):
        @pl.when(met_ref[a] == 0)
        def _():
            delta_ref[...] = jnp.zeros(delta_ref.shape, jnp.float32)

        @pl.when(met_ref[a] > 0)
        def _():
            label, twice = label_ref[a], twice_ref[a]

            def step(weight_ref, firsts, is_first):
                placed = [jnp.where(label == first, twice, 0.0) for first in firsts]
                placed = jnp.concatenate(placed, axis=1).astype(jnp.bfloat16)
                before = jnp.where(is_first, 0.0, delta_ref[...])
                delta_ref[...] = before + jnp.dot(
                    placed, weight_ref[...], preferred_element_type=jnp.float32
                )

            for_holders(met_ref, first_ref, near_refs, opened_ref, UP_HALVED, a, step)

        spot = pl.multiple_of(lax.rem(a, 2) * STEP, STEP)
        for s in range(senders):
            rows = slice(s * STEP, (s + 1) * STEP)
            turned = pltpu.roll(delta_ref[rows, tiles * LANES :], QUARTER * (a // 2), 1)
            ends_ref[s, pl.ds(spot, STEP), :] = jnp.where(
                group_lane == a // 2, turned, ends_ref[s, pl.ds(spot, STEP), :]
            )

        @pl.when(a < full // STEP)
        def _():
            for s in range(senders):
                rows = slice(s * STEP, (s + 1) * STEP)
                for t in range(tiles):
                    at = pl.multiple_of(t * full + a * STEP, STEP)
                    out_ref[s, pl.ds(at, STEP), :] = delta_ref[
                        rows, t * LANES : (t + 1) * LANES
                    ].astype(jnp.bfloat16)

        return carry

    lax.fori_loop(0, label_ref.shape[0], one, 0)
    if kept > full:
        for s in range(senders):
            rows = slice(s * STEP, s * STEP + STEP // 2)
            for t in range(0, tiles, 2):
                both = [
                    delta_ref[rows, (t + i) * LANES : (t + i + 1) * LANES] for i in range(2)
                ]
                at = tiles * full + t * (STEP // 2)
                out_ref[s, at : at + STEP, :] = jnp.concatenate(both, axis=0).astype(jnp.bfloat16)
    for s in range(senders):
        out_ref[s, tiles * kept :, :] = ends_ref[s].astype(jnp.bfloat16)


def mix_kernel(whole, bases, target_ref, tokens_ref, *refs):
    returned_refs, out_ref = refs[:-1], refs[-1]
    total = tokens_ref.shape[0]
    tiles, quads = whole // LANES, returned_refs[0].shape[0] // QUAD
    lane = lanes_of(total)
    chosen = []
    for base, ref in zip(bases, returned_refs):
        kept = (ref.shape[1] - QUARTER) // tiles
        full = kept // STEP * STEP
        spot = lax.broadcasted_iota(jnp.int32, (total, quads * kept), 1)
        place = spot // full * total + spot % full
        if kept > full:
            later = spot - quads * full
            half_place = later // (STEP // 2) * total + later % (STEP // 2) + full
            place = jnp.where(later >= 0, half_place, place)
        place = place + base
        chosen.append(jnp.where(target_ref[...] == place, 1.0, 0.0).astype(jnp.bfloat16))
    end = jnp.zeros((total, LANES), jnp.float32)
    for j in range(QUAD):
        delta = 0.0
        for choice, ref in zip(chosen, returned_refs):
            kept = choice.shape[1] // quads
            full = kept // STEP * STEP
            shares, halves = [], []
            for q in range(quads):
                d = q * QUAD + j
                parts = [ref[d, t * full : (t + 1) * full, :] for t in range(tiles)]
                packed = ref[d, tiles * kept :, :].astype(jnp.float32)
                groups = [packed]
                for m in range(1, QUAD):
                    groups.append(pltpu.roll(packed, LANES - QUARTER * m, 1))
                ends = jnp.concatenate(groups, axis=0)
                parts.append(ends[0:full].astype(jnp.bfloat16))
                shares.append(jnp.concatenate(parts, axis=1))
                if kept > full:
                    pairs = ref[d, tiles * full : tiles * kept, :].astype(jnp.float32)
                    parts = [pairs[t * (STEP // 2) : (t + 1) * (STEP // 2)] for t in range(tiles)]
                    halves.append(jnp.concatenate([*parts, ends[full:kept]], axis=1))
            if halves:
                shares.append(jnp.concatenate(halves, axis=0).astype(jnp.bfloat16))
            share = jnp.concatenate(shares, axis=0)
            delta = delta + jnp.dot(choice, share, preferred_element_type=jnp.float32)
        columns = slice(j * whole, (j + 1) * whole)
        out_ref[:, columns] = (
            tokens_ref[:, columns].astype(jnp.float32) + delta[:, 0:whole]
        ).astype(jnp.bfloat16)
        last = delta[:, whole:]
        turned = pltpu.roll(last, QUARTER * j, 1) if j else last
        end = jnp.where((lane >= QUARTER * j) & (lane < QUARTER * (j + 1)), turned, end)
    out_ref[:, QUAD * whole :] = (
        tokens_ref[:, QUAD * whole :].astype(jnp.float32) + end
    ).astype(jnp.bfloat16)


def call(kernel, out_shape, in_specs, flops, moved, after=(), scratch=(), out_specs=None):
    many = isinstance(out_shape, list)
    skipped = len(after)
    body = (lambda *refs: kernel(*refs[skipped:])) if skipped else kernel
    run = pl.pallas_call(
        body,
        out_shape=out_shape,
        in_specs=[pl.BlockSpec(memory_space=pl.ANY)] * skipped + in_specs,
        out_specs=out_specs or ([VMEM] * len(out_shape) if many else VMEM),
        scratch_shapes=scratch,
        compiler_params=pltpu.CompilerParams(vmem_limit_bytes=18 * 2**20),
        cost_estimate=pl.CostEstimate(flops=flops, bytes_accessed=moved, transcendentals=0),
    )
    return functools.partial(run, *after)


def exchange(value):
    return lax.all_to_all(value, "adapter", split_axis=0, concat_axis=0, tiled=True)


def towards(value, k, devices):
    return lax.ppermute(value, "adapter", [(i, i ^ k) for i in range(devices)])


def swapped(value):
    return lax.ppermute(value, "groups", [(0, 1), (1, 0)])


def stand_behind(value, *earlier):
    return pl.pallas_call(
        lambda *refs: None,
        out_shape=jax.ShapeDtypeStruct(value.shape, value.dtype),
        in_specs=[pl.BlockSpec(memory_space=pl.ANY)] * (1 + len(earlier)),
        out_specs=pl.BlockSpec(memory_space=pl.ANY),
        input_output_aliases={0: 0},
    )(value, *earlier)


def first_pack_call(cap, whole, devices, resident, adapter, used, tokens):
    blocks, rows, width = tokens.shape
    total = blocks * rows
    return call(
        functools.partial(first_pack_kernel, whole, cap, resident),
        [
            jax.ShapeDtypeStruct((devices, whole // LANES * cap + QUARTER, LANES), jnp.bfloat16),
            jax.ShapeDtypeStruct((1, total), jnp.int32),
            jax.ShapeDtypeStruct((total, 1), jnp.float32),
        ],
        [VMEM, VMEM, VMEM],
        2 * devices * cap * total * whole,
        2 * (total * width + devices * cap * whole),
        scratch=[pltpu.VMEM((total, width), jnp.bfloat16), pltpu.VMEM((8, LANES), jnp.int32)],
    )(adapter.reshape(1, blocks), used.reshape(1, blocks), tokens.reshape(total, width))


def pack_call(cap, base, whole, devices, target, label, tokens):
    blocks, rows, width = tokens.shape
    total = blocks * rows
    return call(
        functools.partial(pack_kernel, whole, cap, base),
        jax.ShapeDtypeStruct((devices, whole // LANES * cap + QUARTER, LANES), jnp.bfloat16),
        [VMEM, VMEM, VMEM, VMEM],
        2 * devices * cap * total * whole,
        2 * (total * width + devices * cap * whole),
        scratch=[pltpu.VMEM((total, width), jnp.bfloat16)],
    )(jnp.zeros((8, LANES), jnp.int32), target, label, tokens.reshape(total, width))


def down_call(cap, first, arrived, down_weights, after):
    devices = arrived.shape[0]
    columns, share = down_weights[0].shape
    return call(
        down_kernel,
        [
            jax.ShapeDtypeStruct((cap // STEP, HALF, devices * STEP), jnp.float32),
            jax.ShapeDtypeStruct((STEP, LANES), jnp.bfloat16),
            jax.ShapeDtypeStruct((devices * STEP, LANES), jnp.bfloat16),
            jax.ShapeDtypeStruct((8,), jnp.int32),
        ],
        [SMEM] + [VMEM] * (1 + len(down_weights)),
        0,
        0,
        after,
        [
            pltpu.VMEM((2, columns, share), jnp.bfloat16),
            pltpu.VMEM((devices * STEP, share), jnp.bfloat16),
            pltpu.VMEM((HALF, devices * STEP), jnp.float32),
            pltpu.VMEM((8, devices * STEP), jnp.float32),
        ],
        [VMEM, VMEM, VMEM, SMEM],
    )(first, arrived, *down_weights)


def quad_sums(partial, devices):
    pair = call(
        pair_kernel, jax.ShapeDtypeStruct(partial.shape, jnp.bfloat16), [VMEM, VMEM], 0, 0
    )(partial, towards(partial, 1, devices))
    return [pair, towards(pair, 2, devices)]


def up_call(kept, first, met, notes, sums, up_weights):
    devices = notes.shape[0] // STEP
    columns, share = up_weights[0].shape
    shape = (devices, (share // LANES - 1) * kept + QUARTER, LANES)
    return call(
        up_kernel,
        jax.ShapeDtypeStruct(shape, jnp.bfloat16),
        [SMEM, SMEM] + [VMEM] * (3 + len(up_weights)),
        2 * devices * kept * QUAD * columns * share,
        2 * (2 * devices * kept + QUAD * columns) * share,
        scratch=[
            pltpu.VMEM((2, columns, share), jnp.bfloat16),
            pltpu.VMEM((devices * STEP, share), jnp.float32),
            pltpu.VMEM((devices, QUARTER, LANES), jnp.float32),
            *[pltpu.VMEM((-(-kept // STEP), devices * STEP, LANES), jnp.float32)] * 2,
        ],
    )(first, met, notes, *sums, *up_weights)


def back_and_mix(
    kept, more, tokens, target, label, first, met, notes, sums, down_weights, up_weights, *unused
):
    blocks, rows, width = tokens.shape
    total = blocks * rows
    devices = notes.shape[0] // STEP
    whole = up_weights[0].shape[1] - LANES
    pieces = [exchange(up_call(kept, first, met, notes, sums, up_weights))]
    if more:
        outgoing = pack_call(more, kept, whole, devices, target, label, tokens)
        arrived = exchange(outgoing)
        partial, unused_count, notes, met = down_call(more, first, arrived, down_weights, [])
        sums = quad_sums(partial, devices)
        pieces.append(exchange(up_call(more, first, met, notes, sums, up_weights)))
    mixed = call(
        functools.partial(mix_kernel, whole, (0, kept)[: len(pieces)]),
        jax.ShapeDtypeStruct((total, width), jnp.bfloat16),
        [VMEM] * (2 + len(pieces)),
        2 * devices * (kept + more) * total * whole,
        2 * (2 * total * width + devices * (kept + more) * whole),
    )(target.reshape(total, 1), tokens.reshape(total, width), *pieces)
    return mixed.reshape(tokens.shape)


def start_again(
    tokens, target, label, first, met, notes, sums, down_weights, up_weights, *arguments
):
    return rows_to_holders(tokens, *arguments)


def rows_to_quads(
    tokens, request_block_adapter, request_block_rows, adapter_down_weight, adapter_up_weight
):
    blocks, rows, width = tokens.shape
    devices = lax.axis_size("adapter")
    resident, rank, unused_width = adapter_up_weight.shape
    total = blocks * rows
    columns = resident * rank
    whole = width // LANES // QUAD * LANES
    share = whole + LANES
    bf16, i32 = jnp.bfloat16, jnp.int32

    me = lax.axis_index("adapter").astype(i32)
    group = lax.axis_index("groups").astype(i32)
    parts = jnp.bitwise_xor(me % QUAD, jnp.arange(QUAD, dtype=i32))
    halves = jnp.stack([group, 1 - group]) * (resident // 2)
    first = jnp.concatenate([parts * resident, halves]).astype(i32)
    tiles = whole // LANES

    def shares(weight, which, halved, after):
        shapes = []
        for k in which:
            count = columns // 2 if k in halved else columns
            far = (count * tiles + count // QUAD, LANES)
            shapes.append(jax.ShapeDtypeStruct((columns, share) if k < 2 else far, bf16))
        return call(
            functools.partial(weight_kernel, whole, which, halved),
            shapes,
            [SMEM, SMEM, VMEM],
            0,
            len(which) * columns * width,
            after,
        )(parts, group.reshape(1), weight)

    down_weight = adapter_down_weight.transpose(0, 2, 1).reshape(columns, width)
    up_weight = adapter_up_weight.reshape(columns, width)
    down_far = shares(down_weight, (2, 3), DOWN_HALVED, [])
    up_far = shares(up_weight, (2, 3), UP_HALVED, down_far[:1])
    down_near = shares(down_weight, (0, 1), (), up_far[:1])
    up_near = shares(up_weight, (0, 1), (), down_near[:1])
    down_weights = [down_near[0], towards(down_near[1], 1, devices)]
    down_weights += [towards(value, k, devices) for k, value in zip((2, 3), down_far)]
    up_weights = [up_near[0], towards(up_near[1], 1, devices)]
    up_weights += [towards(value, k, devices) for k, value in zip((2, 3), up_far)]
    down_weights[2] = stand_behind(down_weights[2], up_near[0])
    down_weights += [swapped(down_weights[k]) for k in DOWN_HALVED]
    up_weights += [swapped(up_weights[k]) for k in UP_HALVED]

    caps = [total * 10 // 32, total * 11 // 32, total * 12 // 32, total * 14 // 32]
    cap = caps[-1]
    outgoing, target, label = first_pack_call(
        cap, whole, devices, resident, request_block_adapter, request_block_rows, tokens
    )
    arrived = exchange(outgoing)
    partial, count, notes, met = down_call(cap, first, arrived, down_weights, up_weights[2:3])
    sums = quad_sums(partial, devices)
    count = count[0:1, 0:1]
    most = jnp.maximum(count, swapped(count))[0, 0].astype(jnp.float32)
    branches = [functools.partial(back_and_mix, kept, 0) for kept in caps]
    branches += [functools.partial(back_and_mix, cap, STEP), start_again]
    return lax.switch(
        sum((most > limit).astype(i32) for limit in [*caps, cap + STEP]),
        branches,
        tokens,
        target,
        label,
        first,
        met,
        notes,
        sums,
        down_weights,
        up_weights,
        request_block_adapter,
        request_block_rows,
        adapter_down_weight,
        adapter_up_weight,
    )


def solution(mesh):
    placed = (
        P(("groups", "adapter"), None, None),
        P(("groups", "adapter")),
        P(("groups", "adapter")),
        P("adapter", None, None),
        P("adapter", None, None),
    )

    def per_device(tokens, request_block_adapter, request_block_rows, down_weight, up_weight):
        blocks, rows, width = tokens.shape
        devices = mesh.shape["adapter"]
        slots = max(1, 4 * blocks // devices)
        quads = devices % QUAD == 0 and slots * QUAD >= blocks
        quads = quads and width % (QUAD * LANES) == LANES and up_weight.shape[1] == HALF
        quads = quads and blocks * rows * 7 // 16 == 7 * STEP and mesh.shape["groups"] == 2
        plan = rows_to_quads if quads else rows_to_holders
        return plan(tokens, request_block_adapter, request_block_rows, down_weight, up_weight)

    return jax.shard_map(
        per_device,
        mesh=mesh,
        in_specs=placed,
        out_specs=P(("groups", "adapter"), None, None),
        check_vma=False,
    )
```

```python
import functools

import jax
import jax.numpy as jnp
from jax import lax
from jax.experimental import pallas as pl
from jax.experimental.pallas import tpu as pltpu
from jax.sharding import PartitionSpec as P

LANES = 128
HALF = 64
QUAD = 4
QUARTER = 32
STEP = 16
NOTE = 96
DOWN_HALVED = (2, 3)
UP_HALVED = (2,)
VMEM = pl.BlockSpec(memory_space=pltpu.VMEM)
SMEM = pl.BlockSpec(memory_space=pltpu.SMEM)


def normalise(tokens):
    values = tokens.astype(jnp.float32)
    mean_sq = jnp.mean(values * values, axis=-1, keepdims=True)
    return (values, (values * lax.rsqrt(mean_sq + 1e-06)).astype(jnp.bfloat16))


def resident_update(hidden_state, block_labels, adapter_down_weight, adapter_up_weight):
    feature_width = hidden_state.shape[-1]
    leading = hidden_state.shape[:-1]
    resident_rows, unused_value, inner_rank = adapter_down_weight.shape
    flattened_tokens = hidden_state.reshape(-1, feature_width)
    down_matrix = jnp.einsum(
        "tq,iqg->tig", flattened_tokens, adapter_down_weight, preferred_element_type=jnp.float32
    )
    down_matrix = down_matrix.astype(jnp.bfloat16).reshape(
        flattened_tokens.shape[0], resident_rows * inner_rank
    )
    column_owner = jnp.arange(resident_rows * inner_rank, dtype=jnp.int32) // inner_rank
    picked = block_labels.reshape(-1, 1) == column_owner[None, :]
    down_matrix = jnp.where(picked, down_matrix, jnp.zeros_like(down_matrix))
    lowrank_update = jnp.dot(
        down_matrix,
        adapter_up_weight.reshape(resident_rows * inner_rank, feature_width),
        preferred_element_type=jnp.float32,
    )
    return lowrank_update.astype(jnp.bfloat16).reshape(leading + (feature_width,))


def rows_to_holders(
    tokens, request_block_adapter, request_block_rows, adapter_down_weight, adapter_up_weight
):
    blocks, rows, feature_width = tokens.shape
    devices = lax.axis_size("adapter")
    resident_rows = adapter_down_weight.shape[0]
    slots = max(1, 4 * blocks // devices)
    values, normed = normalise(tokens)
    owner = request_block_adapter // resident_rows
    within = request_block_adapter - owner * resident_rows
    serial = jnp.arange(blocks, dtype=jnp.int32)
    earlier = (owner[:, None] == owner[None, :]) & (serial[None, :] < serial[:, None])
    position = owner * slots + jnp.sum(earlier, axis=1)
    outgoing = (
        jnp.zeros((devices * slots, rows, feature_width), jnp.bfloat16).at[position].set(normed)
    )
    outgoing = outgoing.reshape(devices, slots, rows, feature_width)
    block_labels = jnp.full((devices * slots,), -1, jnp.int32).at[position].set(within)
    block_labels = jnp.broadcast_to(block_labels[:, None], (devices * slots, rows)).reshape(
        devices, slots, rows
    )
    arriving_rows, row_markers = (
        lax.all_to_all(outgoing, "adapter", split_axis=0, concat_axis=0, tiled=True),
        lax.all_to_all(block_labels, "adapter", split_axis=0, concat_axis=0, tiled=True),
    )
    lowrank_update = resident_update(
        arriving_rows, row_markers, adapter_down_weight, adapter_up_weight
    )
    returned = lax.all_to_all(lowrank_update, "adapter", split_axis=0, concat_axis=0, tiled=True)
    mine = returned.reshape(devices * slots, rows, feature_width)[position]
    live = jnp.arange(rows, dtype=jnp.int32)[None, :] < request_block_rows[:, None]
    mixed = values + jnp.where(live[:, :, None], mine.astype(jnp.float32), jnp.float32(0.0))
    return mixed.astype(jnp.bfloat16)


def lanes_of(rows):
    return lax.broadcasted_iota(jnp.int32, (rows, LANES), 1)


def weight_kernel(whole, which, halved, part_ref, group_ref, weight_ref, *out_refs):
    tiles = whole // LANES
    for k, out_ref in zip(which, out_refs):
        j = part_ref[k]
        if k < 2:
            last = weight_ref[:, QUAD * whole :].astype(jnp.float32)
            turned = pltpu.roll(last, lax.rem(LANES - QUARTER * j, LANES), 1)
            inside = lanes_of(last.shape[0]) < QUARTER
            out_ref[:, 0:whole] = weight_ref[:, pl.ds(pl.multiple_of(j * whole, LANES), whole)]
            out_ref[:, whole:] = jnp.where(inside, turned, 0.0).astype(jnp.bfloat16)
            continue
        count = weight_ref.shape[0] // 2 if k in halved else weight_ref.shape[0]
        start = pl.multiple_of(group_ref[0] * count, count) if k in halved else 0
        for t in range(tiles):
            column = pl.multiple_of(j * whole + t * LANES, LANES)
            out_ref[t * count : (t + 1) * count, :] = weight_ref[
                pl.ds(start, count), pl.ds(column, LANES)
            ]
        last = weight_ref[pl.ds(start, count), QUAD * whole :].astype(jnp.float32)
        size = count // QUAD
        owner = lanes_of(size) // QUARTER
        merged = jnp.zeros((size, LANES), jnp.float32)
        for m in range(QUAD):
            shift = lax.rem(LANES + QUARTER * (m - j), LANES)
            turned = pltpu.roll(last[m * size : (m + 1) * size], shift, 1)
            merged = jnp.where(owner == m, turned, merged)
        out_ref[tiles * count :, :] = merged.astype(jnp.bfloat16)


def open_far(far_refs, halved, opened_ref):
    width = opened_ref.shape[2]
    tiles = width // LANES - 1
    places = [(k - 2, 0) for k in (2, 3)] + [(k - 2, 1) for k in halved]
    for ref, (holder, part) in zip(far_refs, places):
        count = opened_ref.shape[1] // 2 if holder + 2 in halved else opened_ref.shape[1]
        base, size = part * count, count // QUAD
        inside = lanes_of(size) < QUARTER
        for t in range(tiles):
            opened_ref[holder, base : base + count, t * LANES : (t + 1) * LANES] = ref[
                t * count : (t + 1) * count, :
            ]
        packed = ref[tiles * count :, :].astype(jnp.float32)
        for m in range(QUAD):
            turned = pltpu.roll(packed, (LANES - QUARTER * m) % LANES, 1) if m else packed
            opened_ref[holder, base + m * size : base + (m + 1) * size, tiles * LANES :] = (
                jnp.where(inside, turned, 0.0).astype(jnp.bfloat16)
            )


def lay_out(resident, adapter_ref, used_ref, most_ref, target_ref, label_ref):
    blocks, total = adapter_ref.shape[1], target_ref.shape[1]
    rows = total // blocks
    adapter, used = adapter_ref[...], used_ref[...]
    down = lax.broadcasted_iota(jnp.int32, (blocks, blocks), 0)
    across = lax.broadcasted_iota(jnp.int32, (blocks, blocks), 1)

    def turned(value):
        return jnp.sum(jnp.where(down == across, value, 0), axis=1, keepdims=True)

    span = resident * QUAD
    quad = jnp.floor((adapter.astype(jnp.float32) + 0.5) * (1.0 / span)).astype(jnp.int32)
    order = adapter * blocks + lax.broadcasted_iota(jnp.int32, (1, blocks), 1)
    quad_down, order_down, used_down = turned(quad), turned(order), turned(used)
    same = quad_down == quad
    ahead = jnp.sum(jnp.where(same & (order < order_down), used, 0), axis=1, keepdims=True)
    within = jnp.sum(jnp.where(same, used, 0), axis=1, keepdims=True)
    most_ref[...] = jnp.broadcast_to(jnp.max(within, axis=0, keepdims=True), most_ref.shape)
    start = quad_down * total + ahead

    block = lax.broadcasted_iota(jnp.int32, (blocks, total), 0)
    row = lax.broadcasted_iota(jnp.int32, (blocks, total), 1) - block * rows
    place = jnp.where((row >= 0) & (row < used_down), start + row + 1, 0)
    target_ref[...] = jnp.sum(place, axis=0, keepdims=True) - 1
    block = lax.broadcasted_iota(jnp.int32, (total, blocks), 1)
    row = lax.broadcasted_iota(jnp.int32, (total, blocks), 0) - block * rows
    label = jnp.where((row >= 0) & (row < rows), adapter - quad * span + 1, 0)
    label_ref[...] = jnp.sum(label.astype(jnp.float32), axis=1, keepdims=True)


def first_pack_kernel(
    whole, cap, resident, adapter_ref, used_ref, tokens_ref, out_ref, target_ref, label_ref, *refs
):
    normed_ref, most_ref = refs
    lay_out(resident, adapter_ref, used_ref, most_ref, target_ref, label_ref)
    pack_kernel(
        whole, cap, 0, most_ref, target_ref, label_ref, tokens_ref, out_ref, normed_ref
    )


def pack_kernel(
    whole, cap, base, most_ref, target_ref, label_ref, tokens_ref, out_ref, normed_ref
):
    values = tokens_ref[...].astype(jnp.float32)
    mean_sq = jnp.mean(values * values, axis=-1, keepdims=True)
    normed_ref[...] = (values * lax.rsqrt(mean_sq + 1e-06)).astype(jnp.bfloat16)
    total = tokens_ref.shape[0]
    quads, tiles = out_ref.shape[0] // QUAD, whole // LANES
    lane = lanes_of(total)
    last = normed_ref[:, QUAD * whole :].astype(jnp.float32)
    label = jnp.where(lane == QUARTER, label_ref[...], 0.0)
    ends = []
    for j in range(QUAD):
        turned = pltpu.roll(last, (LANES - QUARTER * j) % LANES, 1) if j else last
        ends.append(jnp.where(lane < QUARTER, turned, label).astype(jnp.bfloat16))
    most = most_ref[0:1, 0:1].astype(jnp.float32)
    group_lane = lanes_of(QUARTER) // QUARTER
    step_lane = lanes_of(STEP)
    chosen = []
    for q in range(quads):
        place = lax.broadcasted_iota(jnp.int32, (cap, total), 0) + (q * total + base)
        chosen.append(jnp.where(target_ref[...] == place, 1.0, 0.0).astype(jnp.bfloat16))
    chosen = jnp.concatenate(chosen, axis=0)
    notes = [jnp.where(step_lane == NOTE + cap // STEP, most, 0.0)] * quads
    for j in range(QUAD):
        for t in range(tiles):
            column = j * whole + t * LANES
            if t % 2 == 0:
                count = min(2, tiles - t) * LANES
                share = jnp.dot(
                    chosen,
                    normed_ref[:, column : column + count],
                    preferred_element_type=jnp.float32,
                ).astype(jnp.bfloat16)
            for q in range(quads):
                out_ref[q * QUAD + j, t * cap : (t + 1) * cap, :] = share[
                    q * cap : (q + 1) * cap, t % 2 * LANES : (t % 2 + 1) * LANES
                ]
        end_rows = jnp.dot(chosen, ends[j], preferred_element_type=jnp.float32)
        for q in range(quads):
            end = end_rows[q * cap : (q + 1) * cap]
            if j == 0:
                for a in range(cap // STEP):
                    turned = pltpu.roll(end[a * STEP : (a + 1) * STEP], NOTE + a - QUARTER, 1)
                    notes[q] = jnp.where(step_lane == NOTE + a, turned, notes[q])
            padded = jnp.concatenate(
                [end, jnp.zeros((QUAD * QUARTER - cap, LANES), jnp.float32)], axis=0
            )
            merged = padded[0:QUARTER]
            for m in range(1, QUAD):
                turned = pltpu.roll(padded[m * QUARTER : (m + 1) * QUARTER], m * QUARTER, 1)
                merged = jnp.where(group_lane == m, turned, merged)
            out_ref[q * QUAD + j, tiles * cap : tiles * cap + STEP, :] = merged[0:STEP].astype(
                jnp.bfloat16
            )
            out_ref[q * QUAD + j, tiles * cap + STEP :, :] = jnp.where(
                step_lane >= NOTE, notes[q], merged[STEP:]
            ).astype(jnp.bfloat16)


def read_notes(rows_ref, cap, tiles, part_ref, resident, notes_ref, labels_ref, met_ref):
    senders = rows_ref.shape[0]
    for s in range(senders):
        notes_ref[s * STEP : (s + 1) * STEP, :] = rows_ref[s, tiles * cap + STEP :, :]
    steps = labels_ref.shape[0]
    row = lax.broadcasted_iota(jnp.int32, (steps, LANES), 0)
    wanted = jnp.where(lanes_of(steps) == NOTE + row, 1.0, 0.0).astype(jnp.bfloat16)
    labels = lax.dot_general(
        wanted, notes_ref[...], (((1,), (1,)), ((), ())), preferred_element_type=jnp.float32
    )
    labels_ref[...] = labels
    code = jnp.zeros((steps, 1), jnp.float32)
    for h in range(QUAD):
        first = part_ref[h].astype(jnp.float32) + 1.0
        met = jnp.where((labels >= first) & (labels < first + resident), 1.0, 0.0)
        code = code + (1 << h) * jnp.max(met, axis=1, keepdims=True)
    at = lax.broadcasted_iota(jnp.int32, (steps, 1), 0)
    for a in range(cap // STEP):
        met_ref[a] = jnp.max(jnp.where(at == a, code, 0.0)).astype(jnp.int32)


def for_holders(met_ref, first_ref, near_refs, opened_ref, halved, a, step):
    pairs = opened_ref.shape[1] // LANES
    for h in range(QUAD):
        base = first_ref[h].astype(jnp.float32) + 1.0
        firsts = [base + 2.0 * t for t in range(pairs)]
        if h in halved:
            firsts = [
                base + first_ref[QUAD + i].astype(jnp.float32) + 2.0 * t
                for i in range(2)
                for t in range(pairs // 2)
            ]

        @pl.when(lax.rem(met_ref[a] // (1 << h), 2) > 0)
        def _(h=h, firsts=firsts):
            is_first = lax.rem(met_ref[a], 1 << h) == 0
            step(near_refs[h] if h < 2 else opened_ref.at[h - 2], firsts, is_first)


def down_kernel(first_ref, rows_ref, *refs):
    near_refs, far_refs, out_ref, count_ref = refs[:2], refs[2:6], refs[6], refs[7]
    notes_ref, met_ref, opened_ref, batch_ref, picked_ref, labels_ref = refs[8:]
    senders, width = rows_ref.shape[0], batch_ref.shape[1]
    tiles = width // LANES - 1
    cap = out_ref.shape[0] * STEP
    rank = out_ref.shape[1]
    resident = opened_ref.shape[1] // rank
    dims = (((1,), (1,)), ((), ()))
    read_notes(rows_ref, cap, tiles, first_ref, resident, notes_ref, labels_ref, met_ref)
    notes = notes_ref[...].astype(jnp.float32)
    is_count = lanes_of(senders * STEP) == NOTE + cap // STEP
    count = jnp.max(jnp.where(is_count, notes, 0.0), axis=(0, 1), keepdims=True)
    count_ref[...] = jnp.broadcast_to(count, count_ref.shape).astype(jnp.bfloat16)
    open_far(far_refs, DOWN_HALVED, opened_ref)

    def one(a, carry):
        picked_ref[...] = jnp.zeros(picked_ref.shape, jnp.float32)

        @pl.when(met_ref[a] > 0)
        def _():
            shift = lax.rem(LANES - QUARTER * (a // 2), LANES)
            spot = pl.multiple_of(tiles * cap + lax.rem(a, 2) * STEP, STEP)
            for s in range(senders):
                rows = slice(s * STEP, (s + 1) * STEP)
                for t in range(tiles):
                    at = pl.multiple_of(t * cap + a * STEP, STEP)
                    batch_ref[rows, t * LANES : (t + 1) * LANES] = rows_ref[s, pl.ds(at, STEP), :]
                end = rows_ref[s, pl.ds(spot, STEP), :].astype(jnp.float32)
                batch_ref[rows, tiles * LANES :] = pltpu.roll(end, shift, 1).astype(jnp.bfloat16)
            label = labels_ref[pl.ds(a, 1), :]

            def step(weight_ref, firsts, is_first):
                product = lax.dot_general(
                    weight_ref[...], batch_ref[...], dims, preferred_element_type=jnp.float32
                )
                picked = picked_ref[...]
                for t, first in enumerate(firsts):
                    for i in range(2):
                        at = (2 * t + i) * rank
                        picked = jnp.where(
                            label == first + i, product[at : at + rank, :], picked
                        )
                picked_ref[...] = picked

            for_holders(met_ref, first_ref, near_refs, opened_ref, DOWN_HALVED, a, step)

        out_ref[a] = picked_ref[...]
        return carry

    lax.fori_loop(0, cap // STEP, one, 0)


def pair_kernel(own_ref, other_ref, out_ref):
    out_ref[...] = (own_ref[...] + other_ref[...]).astype(jnp.bfloat16)


def up_kernel(first_ref, met_ref, notes_ref, *refs):
    sum_refs, near_refs, far_refs, out_ref = refs[:2], refs[2:4], refs[4:7], refs[7]
    opened_ref, delta_ref, ends_ref, label_ref, twice_ref = refs[8:]
    senders, width = out_ref.shape[0], opened_ref.shape[2]
    tiles = width // LANES - 1
    rank = sum_refs[0].shape[1]
    kept = (out_ref.shape[1] - QUARTER) // tiles
    full = kept // STEP * STEP
    group_lane = lanes_of(STEP) // QUARTER
    open_far(far_refs, UP_HALVED, opened_ref)
    ends_ref[...] = jnp.zeros(ends_ref.shape, jnp.float32)
    low = jnp.where(lanes_of(senders * STEP) < HALF, 0.0, 1.0)
    rank_row = lax.broadcasted_iota(jnp.int32, (rank, LANES), 0)
    twofold = jnp.where(lax.rem(lanes_of(rank), rank) == rank_row, 1.0, 0.0).astype(jnp.bfloat16)

    note_row = lax.broadcasted_iota(jnp.int32, (LANES, LANES), 0)
    for a in range(label_ref.shape[0]):
        wanted = jnp.where(note_row == NOTE + a, 1.0, 0.0).astype(jnp.bfloat16)
        label_ref[a] = jnp.dot(notes_ref[...], wanted, preferred_element_type=jnp.float32) - low
        down = sum_refs[0][a].astype(jnp.float32) + sum_refs[1][a].astype(jnp.float32)
        twice_ref[a] = lax.dot_general(
            down.astype(jnp.bfloat16),
            twofold,
            (((0,), (0,)), ((), ())),
            preferred_element_type=jnp.float32,
        )

    def one(a, carry):
        @pl.when(met_ref[a] == 0)
        def _():
            delta_ref[...] = jnp.zeros(delta_ref.shape, jnp.float32)

        @pl.when(met_ref[a] > 0)
        def _():
            label, twice = label_ref[a], twice_ref[a]

            def step(weight_ref, firsts, is_first):
                placed = [jnp.where(label == first, twice, 0.0) for first in firsts]
                placed = jnp.concatenate(placed, axis=1).astype(jnp.bfloat16)
                before = jnp.where(is_first, 0.0, delta_ref[...])
                delta_ref[...] = before + jnp.dot(
                    placed, weight_ref[...], preferred_element_type=jnp.float32
                )

            for_holders(met_ref, first_ref, near_refs, opened_ref, UP_HALVED, a, step)

        spot = pl.multiple_of(lax.rem(a, 2) * STEP, STEP)
        for s in range(senders):
            rows = slice(s * STEP, (s + 1) * STEP)
            turned = pltpu.roll(delta_ref[rows, tiles * LANES :], QUARTER * (a // 2), 1)
            ends_ref[s, pl.ds(spot, STEP), :] = jnp.where(
                group_lane == a // 2, turned, ends_ref[s, pl.ds(spot, STEP), :]
            )

        @pl.when(a < full // STEP)
        def _():
            for s in range(senders):
                rows = slice(s * STEP, (s + 1) * STEP)
                for t in range(tiles):
                    at = pl.multiple_of(t * full + a * STEP, STEP)
                    out_ref[s, pl.ds(at, STEP), :] = delta_ref[
                        rows, t * LANES : (t + 1) * LANES
                    ].astype(jnp.bfloat16)

        return carry

    lax.fori_loop(0, label_ref.shape[0], one, 0)
    if kept > full:
        for s in range(senders):
            rows = slice(s * STEP, s * STEP + STEP // 2)
            for t in range(0, tiles, 2):
                both = [
                    delta_ref[rows, (t + i) * LANES : (t + i + 1) * LANES] for i in range(2)
                ]
                at = tiles * full + t * (STEP // 2)
                out_ref[s, at : at + STEP, :] = jnp.concatenate(both, axis=0).astype(jnp.bfloat16)
    for s in range(senders):
        out_ref[s, tiles * kept :, :] = ends_ref[s].astype(jnp.bfloat16)


def mix_kernel(whole, bases, target_ref, tokens_ref, *refs):
    returned_refs, out_ref = refs[:-1], refs[-1]
    total = tokens_ref.shape[0]
    tiles, quads = whole // LANES, returned_refs[0].shape[0] // QUAD
    lane = lanes_of(total)
    chosen = []
    for base, ref in zip(bases, returned_refs):
        kept = (ref.shape[1] - QUARTER) // tiles
        full = kept // STEP * STEP
        spot = lax.broadcasted_iota(jnp.int32, (total, quads * kept), 1)
        place = spot // full * total + spot % full
        if kept > full:
            later = spot - quads * full
            half_place = later // (STEP // 2) * total + later % (STEP // 2) + full
            place = jnp.where(later >= 0, half_place, place)
        place = place + base
        chosen.append(jnp.where(target_ref[...] == place, 1.0, 0.0).astype(jnp.bfloat16))

    def one(j, end):
        delta = 0.0
        for choice, ref in zip(chosen, returned_refs):
            kept = choice.shape[1] // quads
            full = kept // STEP * STEP
            shares, halves = [], []
            for q in range(quads):
                d = q * QUAD + j
                parts = [ref[d, t * full : (t + 1) * full, :] for t in range(tiles)]
                packed = ref[d, tiles * kept :, :].astype(jnp.float32)
                groups = [packed]
                for m in range(1, QUAD):
                    groups.append(pltpu.roll(packed, LANES - QUARTER * m, 1))
                ends = jnp.concatenate(groups, axis=0)
                parts.append(ends[0:full].astype(jnp.bfloat16))
                shares.append(jnp.concatenate(parts, axis=1))
                if kept > full:
                    pairs = ref[d, tiles * full : tiles * kept, :].astype(jnp.float32)
                    parts = [pairs[t * (STEP // 2) : (t + 1) * (STEP // 2)] for t in range(tiles)]
                    halves.append(jnp.concatenate([*parts, ends[full:kept]], axis=1))
            if halves:
                shares.append(jnp.concatenate(halves, axis=0).astype(jnp.bfloat16))
            share = jnp.concatenate(shares, axis=0)
            delta = delta + jnp.dot(choice, share, preferred_element_type=jnp.float32)
        columns = pl.ds(pl.multiple_of(j * whole, LANES), whole)
        out_ref[:, columns] = (
            tokens_ref[:, columns].astype(jnp.float32) + delta[:, 0:whole]
        ).astype(jnp.bfloat16)
        turned = pltpu.roll(delta[:, whole:], QUARTER * j, 1)
        return jnp.where(lane // QUARTER == j, turned, end)

    end = lax.fori_loop(0, QUAD, one, jnp.zeros((total, LANES), jnp.float32))
    out_ref[:, QUAD * whole :] = (
        tokens_ref[:, QUAD * whole :].astype(jnp.float32) + end
    ).astype(jnp.bfloat16)


def call(kernel, out_shape, in_specs, flops, moved, after=(), scratch=(), out_specs=None):
    many = isinstance(out_shape, list)
    skipped = len(after)
    body = (lambda *refs: kernel(*refs[skipped:])) if skipped else kernel
    run = pl.pallas_call(
        body,
        out_shape=out_shape,
        in_specs=[pl.BlockSpec(memory_space=pl.ANY)] * skipped + in_specs,
        out_specs=out_specs or ([VMEM] * len(out_shape) if many else VMEM),
        scratch_shapes=scratch,
        compiler_params=pltpu.CompilerParams(vmem_limit_bytes=18 * 2**20),
        cost_estimate=pl.CostEstimate(flops=flops, bytes_accessed=moved, transcendentals=0),
    )
    return functools.partial(run, *after)


def exchange(value):
    return lax.all_to_all(value, "adapter", split_axis=0, concat_axis=0, tiled=True)


def towards(value, k, devices):
    return lax.ppermute(value, "adapter", [(i, i ^ k) for i in range(devices)])


def swapped(value):
    return lax.ppermute(value, "groups", [(0, 1), (1, 0)])


def stand_behind(value, *earlier):
    return pl.pallas_call(
        lambda *refs: None,
        out_shape=jax.ShapeDtypeStruct(value.shape, value.dtype),
        in_specs=[pl.BlockSpec(memory_space=pl.ANY)] * (1 + len(earlier)),
        out_specs=pl.BlockSpec(memory_space=pl.ANY),
        input_output_aliases={0: 0},
    )(value, *earlier)


def first_pack_call(cap, whole, devices, resident, adapter, used, tokens):
    blocks, rows, width = tokens.shape
    total = blocks * rows
    return call(
        functools.partial(first_pack_kernel, whole, cap, resident),
        [
            jax.ShapeDtypeStruct((devices, whole // LANES * cap + QUARTER, LANES), jnp.bfloat16),
            jax.ShapeDtypeStruct((1, total), jnp.int32),
            jax.ShapeDtypeStruct((total, 1), jnp.float32),
        ],
        [VMEM, VMEM, VMEM],
        2 * devices * cap * total * whole,
        2 * (total * width + devices * cap * whole),
        scratch=[pltpu.VMEM((total, width), jnp.bfloat16), pltpu.VMEM((8, LANES), jnp.int32)],
    )(adapter.reshape(1, blocks), used.reshape(1, blocks), tokens.reshape(total, width))


def pack_call(cap, base, whole, devices, target, label, tokens):
    blocks, rows, width = tokens.shape
    total = blocks * rows
    return call(
        functools.partial(pack_kernel, whole, cap, base),
        jax.ShapeDtypeStruct((devices, whole // LANES * cap + QUARTER, LANES), jnp.bfloat16),
        [VMEM, VMEM, VMEM, VMEM],
        2 * devices * cap * total * whole,
        2 * (total * width + devices * cap * whole),
        scratch=[pltpu.VMEM((total, width), jnp.bfloat16)],
    )(jnp.zeros((8, LANES), jnp.int32), target, label, tokens.reshape(total, width))


def down_call(cap, first, arrived, down_weights, after):
    devices = arrived.shape[0]
    columns, share = down_weights[0].shape
    return call(
        down_kernel,
        [
            jax.ShapeDtypeStruct((cap // STEP, HALF, devices * STEP), jnp.float32),
            jax.ShapeDtypeStruct((STEP, LANES), jnp.bfloat16),
            jax.ShapeDtypeStruct((devices * STEP, LANES), jnp.bfloat16),
            jax.ShapeDtypeStruct((8,), jnp.int32),
        ],
        [SMEM] + [VMEM] * (1 + len(down_weights)),
        0,
        0,
        after,
        [
            pltpu.VMEM((2, columns, share), jnp.bfloat16),
            pltpu.VMEM((devices * STEP, share), jnp.bfloat16),
            pltpu.VMEM((HALF, devices * STEP), jnp.float32),
            pltpu.VMEM((8, devices * STEP), jnp.float32),
        ],
        [VMEM, VMEM, VMEM, SMEM],
    )(first, arrived, *down_weights)


def quad_sums(partial, devices):
    pair = call(
        pair_kernel, jax.ShapeDtypeStruct(partial.shape, jnp.bfloat16), [VMEM, VMEM], 0, 0
    )(partial, towards(partial, 1, devices))
    return [pair, towards(pair, 2, devices)]


def up_call(kept, first, met, notes, sums, up_weights):
    devices = notes.shape[0] // STEP
    columns, share = up_weights[0].shape
    shape = (devices, (share // LANES - 1) * kept + QUARTER, LANES)
    return call(
        up_kernel,
        jax.ShapeDtypeStruct(shape, jnp.bfloat16),
        [SMEM, SMEM] + [VMEM] * (3 + len(up_weights)),
        2 * devices * kept * QUAD * columns * share,
        2 * (2 * devices * kept + QUAD * columns) * share,
        scratch=[
            pltpu.VMEM((2, columns, share), jnp.bfloat16),
            pltpu.VMEM((devices * STEP, share), jnp.float32),
            pltpu.VMEM((devices, QUARTER, LANES), jnp.float32),
            *[pltpu.VMEM((-(-kept // STEP), devices * STEP, LANES), jnp.float32)] * 2,
        ],
    )(first, met, notes, *sums, *up_weights)


def back_and_mix(
    kept, more, tokens, target, label, first, met, notes, sums, down_weights, up_weights, *unused
):
    blocks, rows, width = tokens.shape
    total = blocks * rows
    devices = notes.shape[0] // STEP
    whole = up_weights[0].shape[1] - LANES
    pieces = [exchange(up_call(kept, first, met, notes, sums, up_weights))]
    if more:
        outgoing = pack_call(more, kept, whole, devices, target, label, tokens)
        arrived = exchange(outgoing)
        partial, unused_count, notes, met = down_call(more, first, arrived, down_weights, [])
        sums = quad_sums(partial, devices)
        pieces.append(exchange(up_call(more, first, met, notes, sums, up_weights)))
    mixed = call(
        functools.partial(mix_kernel, whole, (0, kept)[: len(pieces)]),
        jax.ShapeDtypeStruct((total, width), jnp.bfloat16),
        [VMEM] * (2 + len(pieces)),
        2 * devices * (kept + more) * total * whole,
        2 * (2 * total * width + devices * (kept + more) * whole),
    )(target.reshape(total, 1), tokens.reshape(total, width), *pieces)
    return mixed.reshape(tokens.shape)


def start_again(
    tokens, target, label, first, met, notes, sums, down_weights, up_weights, *arguments
):
    return rows_to_holders(tokens, *arguments)


def rows_to_quads(
    tokens, request_block_adapter, request_block_rows, adapter_down_weight, adapter_up_weight
):
    blocks, rows, width = tokens.shape
    devices = lax.axis_size("adapter")
    resident, rank, unused_width = adapter_up_weight.shape
    total = blocks * rows
    columns = resident * rank
    whole = width // LANES // QUAD * LANES
    share = whole + LANES
    bf16, i32 = jnp.bfloat16, jnp.int32

    me = lax.axis_index("adapter").astype(i32)
    group = lax.axis_index("groups").astype(i32)
    parts = jnp.bitwise_xor(me % QUAD, jnp.arange(QUAD, dtype=i32))
    halves = jnp.stack([group, 1 - group]) * (resident // 2)
    first = jnp.concatenate([parts * resident, halves]).astype(i32)
    tiles = whole // LANES

    def shares(weight, which, halved, after):
        shapes = []
        for k in which:
            count = columns // 2 if k in halved else columns
            far = (count * tiles + count // QUAD, LANES)
            shapes.append(jax.ShapeDtypeStruct((columns, share) if k < 2 else far, bf16))
        return call(
            functools.partial(weight_kernel, whole, which, halved),
            shapes,
            [SMEM, SMEM, VMEM],
            0,
            len(which) * columns * width,
            after,
        )(parts, group.reshape(1), weight)

    down_weight = adapter_down_weight.transpose(0, 2, 1).reshape(columns, width)
    up_weight = adapter_up_weight.reshape(columns, width)
    down_far = shares(down_weight, (2, 3), DOWN_HALVED, [])
    up_far = shares(up_weight, (2, 3), UP_HALVED, down_far[:1])
    down_near = shares(down_weight, (0, 1), (), up_far[:1])
    up_near = shares(up_weight, (0, 1), (), down_near[:1])
    down_weights = [down_near[0], towards(down_near[1], 1, devices)]
    down_weights += [towards(value, k, devices) for k, value in zip((2, 3), down_far)]
    up_weights = [up_near[0], towards(up_near[1], 1, devices)]
    up_weights += [towards(value, k, devices) for k, value in zip((2, 3), up_far)]
    down_weights[2] = stand_behind(down_weights[2], up_near[0])
    down_weights += [swapped(down_weights[k]) for k in DOWN_HALVED]
    up_weights += [swapped(up_weights[k]) for k in UP_HALVED]

    caps = [total * 10 // 32, total * 11 // 32, total * 12 // 32, total * 14 // 32]
    cap = caps[-1]
    outgoing, target, label = first_pack_call(
        cap, whole, devices, resident, request_block_adapter, request_block_rows, tokens
    )
    arrived = exchange(outgoing)
    partial, count, notes, met = down_call(cap, first, arrived, down_weights, up_weights[2:3])
    sums = quad_sums(partial, devices)
    count = count[0:1, 0:1]
    most = jnp.maximum(count, swapped(count))[0, 0].astype(jnp.float32)
    branches = [functools.partial(back_and_mix, kept, 0) for kept in caps]
    branches += [functools.partial(back_and_mix, cap, STEP), start_again]
    return lax.switch(
        sum((most > limit).astype(i32) for limit in [*caps, cap + STEP]),
        branches,
        tokens,
        target,
        label,
        first,
        met,
        notes,
        sums,
        down_weights,
        up_weights,
        request_block_adapter,
        request_block_rows,
        adapter_down_weight,
        adapter_up_weight,
    )


def solution(mesh):
    placed = (
        P(("groups", "adapter"), None, None),
        P(("groups", "adapter")),
        P(("groups", "adapter")),
        P("adapter", None, None),
        P("adapter", None, None),
    )

    def per_device(tokens, request_block_adapter, request_block_rows, down_weight, up_weight):
        blocks, rows, width = tokens.shape
        devices = mesh.shape["adapter"]
        slots = max(1, 4 * blocks // devices)
        quads = devices % QUAD == 0 and slots * QUAD >= blocks
        quads = quads and width % (QUAD * LANES) == LANES and up_weight.shape[1] == HALF
        quads = quads and blocks * rows * 7 // 16 == 7 * STEP and mesh.shape["groups"] == 2
        plan = rows_to_quads if quads else rows_to_holders
        return plan(tokens, request_block_adapter, request_block_rows, down_weight, up_weight)

    return jax.shard_map(
        per_device,
        mesh=mesh,
        in_specs=placed,
        out_specs=P(("groups", "adapter"), None, None),
        check_vma=False,
    )
```

```python
import functools

import jax
import jax.numpy as jnp
from jax import lax
from jax.experimental import pallas as pl
from jax.experimental.pallas import tpu as pltpu
from jax.sharding import PartitionSpec as P

LANES = 128
HALF = 64
QUAD = 4
QUARTER = 32
STEP = 16
NOTE = 96
DOWN_HALVED = (2, 3)
UP_HALVED = (2,)
VMEM = pl.BlockSpec(memory_space=pltpu.VMEM)
SMEM = pl.BlockSpec(memory_space=pltpu.SMEM)


def normalise(tokens):
    values = tokens.astype(jnp.float32)
    mean_sq = jnp.mean(values * values, axis=-1, keepdims=True)
    return (values, (values * lax.rsqrt(mean_sq + 1e-06)).astype(jnp.bfloat16))


def resident_update(hidden_state, block_labels, adapter_down_weight, adapter_up_weight):
    feature_width = hidden_state.shape[-1]
    leading = hidden_state.shape[:-1]
    resident_rows, unused_value, inner_rank = adapter_down_weight.shape
    flattened_tokens = hidden_state.reshape(-1, feature_width)
    down_matrix = jnp.einsum(
        "tq,iqg->tig", flattened_tokens, adapter_down_weight, preferred_element_type=jnp.float32
    )
    down_matrix = down_matrix.astype(jnp.bfloat16).reshape(
        flattened_tokens.shape[0], resident_rows * inner_rank
    )
    column_owner = jnp.arange(resident_rows * inner_rank, dtype=jnp.int32) // inner_rank
    picked = block_labels.reshape(-1, 1) == column_owner[None, :]
    down_matrix = jnp.where(picked, down_matrix, jnp.zeros_like(down_matrix))
    lowrank_update = jnp.dot(
        down_matrix,
        adapter_up_weight.reshape(resident_rows * inner_rank, feature_width),
        preferred_element_type=jnp.float32,
    )
    return lowrank_update.astype(jnp.bfloat16).reshape(leading + (feature_width,))


def rows_to_holders(
    tokens, request_block_adapter, request_block_rows, adapter_down_weight, adapter_up_weight
):
    blocks, rows, feature_width = tokens.shape
    devices = lax.axis_size("adapter")
    resident_rows = adapter_down_weight.shape[0]
    slots = max(1, 4 * blocks // devices)
    values, normed = normalise(tokens)
    owner = request_block_adapter // resident_rows
    within = request_block_adapter - owner * resident_rows
    serial = jnp.arange(blocks, dtype=jnp.int32)
    earlier = (owner[:, None] == owner[None, :]) & (serial[None, :] < serial[:, None])
    position = owner * slots + jnp.sum(earlier, axis=1)
    outgoing = (
        jnp.zeros((devices * slots, rows, feature_width), jnp.bfloat16).at[position].set(normed)
    )
    outgoing = outgoing.reshape(devices, slots, rows, feature_width)
    block_labels = jnp.full((devices * slots,), -1, jnp.int32).at[position].set(within)
    block_labels = jnp.broadcast_to(block_labels[:, None], (devices * slots, rows)).reshape(
        devices, slots, rows
    )
    arriving_rows, row_markers = (
        lax.all_to_all(outgoing, "adapter", split_axis=0, concat_axis=0, tiled=True),
        lax.all_to_all(block_labels, "adapter", split_axis=0, concat_axis=0, tiled=True),
    )
    lowrank_update = resident_update(
        arriving_rows, row_markers, adapter_down_weight, adapter_up_weight
    )
    returned = lax.all_to_all(lowrank_update, "adapter", split_axis=0, concat_axis=0, tiled=True)
    mine = returned.reshape(devices * slots, rows, feature_width)[position]
    live = jnp.arange(rows, dtype=jnp.int32)[None, :] < request_block_rows[:, None]
    mixed = values + jnp.where(live[:, :, None], mine.astype(jnp.float32), jnp.float32(0.0))
    return mixed.astype(jnp.bfloat16)


def lanes_of(rows):
    return lax.broadcasted_iota(jnp.int32, (rows, LANES), 1)


def weight_kernel(whole, which, halved, part_ref, group_ref, weight_ref, *out_refs):
    tiles = whole // LANES
    for k, out_ref in zip(which, out_refs):
        j = part_ref[k]
        if k < 2:
            last = weight_ref[:, QUAD * whole :].astype(jnp.float32)
            turned = pltpu.roll(last, lax.rem(LANES - QUARTER * j, LANES), 1)
            inside = lanes_of(last.shape[0]) < QUARTER
            out_ref[:, 0:whole] = weight_ref[:, pl.ds(pl.multiple_of(j * whole, LANES), whole)]
            out_ref[:, whole:] = jnp.where(inside, turned, 0.0).astype(jnp.bfloat16)
            continue
        count = weight_ref.shape[0] // 2 if k in halved else weight_ref.shape[0]
        start = pl.multiple_of(group_ref[0] * count, count) if k in halved else 0
        for t in range(tiles):
            column = pl.multiple_of(j * whole + t * LANES, LANES)
            out_ref[t * count : (t + 1) * count, :] = weight_ref[
                pl.ds(start, count), pl.ds(column, LANES)
            ]
        last = weight_ref[pl.ds(start, count), QUAD * whole :].astype(jnp.float32)
        size = count // QUAD
        owner = lanes_of(size) // QUARTER
        merged = jnp.zeros((size, LANES), jnp.float32)
        for m in range(QUAD):
            shift = lax.rem(LANES + QUARTER * (m - j), LANES)
            turned = pltpu.roll(last[m * size : (m + 1) * size], shift, 1)
            merged = jnp.where(owner == m, turned, merged)
        out_ref[tiles * count :, :] = merged.astype(jnp.bfloat16)


def open_far(far_refs, halved, opened_ref):
    width = opened_ref.shape[2]
    tiles = width // LANES - 1
    places = [(k - 2, 0) for k in (2, 3)] + [(k - 2, 1) for k in halved]
    for ref, (holder, part) in zip(far_refs, places):
        count = opened_ref.shape[1] // 2 if holder + 2 in halved else opened_ref.shape[1]
        base, size = part * count, count // QUAD
        inside = lanes_of(size) < QUARTER
        for t in range(tiles):
            opened_ref[holder, base : base + count, t * LANES : (t + 1) * LANES] = ref[
                t * count : (t + 1) * count, :
            ]
        packed = ref[tiles * count :, :].astype(jnp.float32)
        for m in range(QUAD):
            turned = pltpu.roll(packed, (LANES - QUARTER * m) % LANES, 1) if m else packed
            opened_ref[holder, base + m * size : base + (m + 1) * size, tiles * LANES :] = (
                jnp.where(inside, turned, 0.0).astype(jnp.bfloat16)
            )


def lay_out(resident, adapter_ref, used_ref, most_ref, target_ref, label_ref):
    blocks, total = adapter_ref.shape[1], target_ref.shape[1]
    rows = total // blocks
    adapter, used = adapter_ref[...], used_ref[...]
    down = lax.broadcasted_iota(jnp.int32, (blocks, blocks), 0)
    across = lax.broadcasted_iota(jnp.int32, (blocks, blocks), 1)

    def turned(value):
        return jnp.sum(jnp.where(down == across, value, 0), axis=1, keepdims=True)

    span = resident * QUAD
    quad = jnp.floor((adapter.astype(jnp.float32) + 0.5) * (1.0 / span)).astype(jnp.int32)
    order = adapter * blocks + lax.broadcasted_iota(jnp.int32, (1, blocks), 1)
    quad_down, order_down, used_down = turned(quad), turned(order), turned(used)
    same = quad_down == quad
    ahead = jnp.sum(jnp.where(same & (order < order_down), used, 0), axis=1, keepdims=True)
    within = jnp.sum(jnp.where(same, used, 0), axis=1, keepdims=True)
    most_ref[...] = jnp.broadcast_to(jnp.max(within, axis=0, keepdims=True), most_ref.shape)
    start = quad_down * total + ahead

    block = lax.broadcasted_iota(jnp.int32, (blocks, total), 0)
    row = lax.broadcasted_iota(jnp.int32, (blocks, total), 1) - block * rows
    place = jnp.where((row >= 0) & (row < used_down), start + row + 1, 0)
    target_ref[...] = jnp.sum(place, axis=0, keepdims=True) - 1
    block = lax.broadcasted_iota(jnp.int32, (total, blocks), 1)
    row = lax.broadcasted_iota(jnp.int32, (total, blocks), 0) - block * rows
    label = jnp.where((row >= 0) & (row < rows), adapter - quad * span + 1, 0)
    label_ref[...] = jnp.sum(label.astype(jnp.float32), axis=1, keepdims=True)


def first_pack_kernel(
    whole, cap, resident, adapter_ref, used_ref, tokens_ref, out_ref, target_ref, label_ref, *refs
):
    normed_ref, most_ref = refs
    lay_out(resident, adapter_ref, used_ref, most_ref, target_ref, label_ref)
    pack_kernel(
        whole, cap, 0, most_ref, target_ref, label_ref, tokens_ref, out_ref, normed_ref
    )


def pack_kernel(
    whole, cap, base, most_ref, target_ref, label_ref, tokens_ref, out_ref, normed_ref
):
    values = tokens_ref[...].astype(jnp.float32)
    mean_sq = jnp.mean(values * values, axis=-1, keepdims=True)
    normed_ref[...] = (values * lax.rsqrt(mean_sq + 1e-06)).astype(jnp.bfloat16)
    total = tokens_ref.shape[0]
    quads, tiles = out_ref.shape[0] // QUAD, whole // LANES
    lane = lanes_of(total)
    last = normed_ref[:, QUAD * whole :].astype(jnp.float32)
    label = jnp.where(lane == QUARTER, label_ref[...], 0.0)
    ends = []
    for j in range(QUAD):
        turned = pltpu.roll(last, (LANES - QUARTER * j) % LANES, 1) if j else last
        ends.append(jnp.where(lane < QUARTER, turned, label).astype(jnp.bfloat16))
    most = most_ref[0:1, 0:1].astype(jnp.float32)
    group_lane = lanes_of(QUARTER) // QUARTER
    step_lane = lanes_of(STEP)
    chosen = []
    for q in range(quads):
        place = lax.broadcasted_iota(jnp.int32, (cap, total), 0) + (q * total + base)
        chosen.append(jnp.where(target_ref[...] == place, 1.0, 0.0).astype(jnp.bfloat16))
    chosen = jnp.concatenate(chosen, axis=0)
    notes = [jnp.where(step_lane == NOTE + cap // STEP, most, 0.0)] * quads
    for j in range(QUAD):
        for t in range(tiles):
            column = j * whole + t * LANES
            if t % 2 == 0:
                count = min(2, tiles - t) * LANES
                share = jnp.dot(
                    chosen,
                    normed_ref[:, column : column + count],
                    preferred_element_type=jnp.float32,
                ).astype(jnp.bfloat16)
            for q in range(quads):
                out_ref[q * QUAD + j, t * cap : (t + 1) * cap, :] = share[
                    q * cap : (q + 1) * cap, t % 2 * LANES : (t % 2 + 1) * LANES
                ]
        end_rows = jnp.dot(chosen, ends[j], preferred_element_type=jnp.float32)
        for q in range(quads):
            end = end_rows[q * cap : (q + 1) * cap]
            if j == 0:
                for a in range(cap // STEP):
                    turned = pltpu.roll(end[a * STEP : (a + 1) * STEP], NOTE + a - QUARTER, 1)
                    notes[q] = jnp.where(step_lane == NOTE + a, turned, notes[q])
            padded = jnp.concatenate(
                [end, jnp.zeros((QUAD * QUARTER - cap, LANES), jnp.float32)], axis=0
            )
            merged = padded[0:QUARTER]
            for m in range(1, QUAD):
                turned = pltpu.roll(padded[m * QUARTER : (m + 1) * QUARTER], m * QUARTER, 1)
                merged = jnp.where(group_lane == m, turned, merged)
            out_ref[q * QUAD + j, tiles * cap : tiles * cap + STEP, :] = merged[0:STEP].astype(
                jnp.bfloat16
            )
            out_ref[q * QUAD + j, tiles * cap + STEP :, :] = jnp.where(
                step_lane >= NOTE, notes[q], merged[STEP:]
            ).astype(jnp.bfloat16)


def read_notes(rows_ref, cap, tiles, part_ref, resident, notes_ref, labels_ref, met_ref):
    senders = rows_ref.shape[0]
    for s in range(senders):
        notes_ref[s * STEP : (s + 1) * STEP, :] = rows_ref[s, tiles * cap + STEP :, :]
    steps = labels_ref.shape[0]
    row = lax.broadcasted_iota(jnp.int32, (steps, LANES), 0)
    wanted = jnp.where(lanes_of(steps) == NOTE + row, 1.0, 0.0).astype(jnp.bfloat16)
    labels = lax.dot_general(
        wanted, notes_ref[...], (((1,), (1,)), ((), ())), preferred_element_type=jnp.float32
    )
    labels_ref[...] = labels
    code = jnp.zeros((steps, 1), jnp.float32)
    for h in range(QUAD):
        first = part_ref[h].astype(jnp.float32) + 1.0
        met = jnp.where((labels >= first) & (labels < first + resident), 1.0, 0.0)
        code = code + (1 << h) * jnp.max(met, axis=1, keepdims=True)
    at = lax.broadcasted_iota(jnp.int32, (steps, 1), 0)
    for a in range(cap // STEP):
        met_ref[a] = jnp.max(jnp.where(at == a, code, 0.0)).astype(jnp.int32)


def for_holders(met_ref, first_ref, near_refs, opened_ref, halved, a, step):
    pairs = opened_ref.shape[1] // LANES
    for h in range(QUAD):
        base = first_ref[h].astype(jnp.float32) + 1.0
        firsts = [base + 2.0 * t for t in range(pairs)]
        if h in halved:
            firsts = [
                base + first_ref[QUAD + i].astype(jnp.float32) + 2.0 * t
                for i in range(2)
                for t in range(pairs // 2)
            ]

        @pl.when(lax.rem(met_ref[a] // (1 << h), 2) > 0)
        def _(h=h, firsts=firsts):
            is_first = lax.rem(met_ref[a], 1 << h) == 0
            step(near_refs[h] if h < 2 else opened_ref.at[h - 2], firsts, is_first)


def down_kernel(first_ref, rows_ref, *refs):
    near_refs, far_refs, out_ref, count_ref = refs[:2], refs[2:6], refs[6], refs[7]
    notes_ref, met_ref, opened_ref, batch_ref, picked_ref, labels_ref = refs[8:]
    senders, width = rows_ref.shape[0], batch_ref.shape[1]
    tiles = width // LANES - 1
    cap = out_ref.shape[0] * STEP
    rank = out_ref.shape[1]
    resident = opened_ref.shape[1] // rank
    dims = (((1,), (1,)), ((), ()))
    read_notes(rows_ref, cap, tiles, first_ref, resident, notes_ref, labels_ref, met_ref)
    notes = notes_ref[...].astype(jnp.float32)
    is_count = lanes_of(senders * STEP) == NOTE + cap // STEP
    count = jnp.max(jnp.where(is_count, notes, 0.0), axis=(0, 1), keepdims=True)
    count_ref[...] = jnp.broadcast_to(count, count_ref.shape).astype(jnp.bfloat16)
    open_far(far_refs, DOWN_HALVED, opened_ref)

    def one(a, carry):
        picked_ref[...] = jnp.zeros(picked_ref.shape, jnp.float32)

        @pl.when(met_ref[a] > 0)
        def _():
            shift = lax.rem(LANES - QUARTER * (a // 2), LANES)
            spot = pl.multiple_of(tiles * cap + lax.rem(a, 2) * STEP, STEP)
            for s in range(senders):
                rows = slice(s * STEP, (s + 1) * STEP)
                for t in range(tiles):
                    at = pl.multiple_of(t * cap + a * STEP, STEP)
                    batch_ref[rows, t * LANES : (t + 1) * LANES] = rows_ref[s, pl.ds(at, STEP), :]
                end = rows_ref[s, pl.ds(spot, STEP), :].astype(jnp.float32)
                batch_ref[rows, tiles * LANES :] = pltpu.roll(end, shift, 1).astype(jnp.bfloat16)
            label = labels_ref[pl.ds(a, 1), :]

            def step(weight_ref, firsts, is_first):
                product = lax.dot_general(
                    weight_ref[...], batch_ref[...], dims, preferred_element_type=jnp.float32
                )
                picked = picked_ref[...]
                for t, first in enumerate(firsts):
                    for i in range(2):
                        at = (2 * t + i) * rank
                        picked = jnp.where(
                            label == first + i, product[at : at + rank, :], picked
                        )
                picked_ref[...] = picked

            for_holders(met_ref, first_ref, near_refs, opened_ref, DOWN_HALVED, a, step)

        out_ref[a] = picked_ref[...]
        return carry

    lax.fori_loop(0, cap // STEP, one, 0)


def pair_kernel(own_ref, other_ref, out_ref):
    out_ref[...] = (own_ref[...] + other_ref[...]).astype(jnp.bfloat16)


def up_kernel(first_ref, met_ref, notes_ref, *refs):
    sum_refs, near_refs, far_refs, out_ref = refs[:2], refs[2:4], refs[4:7], refs[7]
    opened_ref, delta_ref, ends_ref, label_ref, twice_ref = refs[8:]
    senders, width = out_ref.shape[0], opened_ref.shape[2]
    tiles = width // LANES - 1
    rank = sum_refs[0].shape[1]
    kept = (out_ref.shape[1] - QUARTER) // tiles
    full = kept // STEP * STEP
    group_lane = lanes_of(STEP) // QUARTER
    open_far(far_refs, UP_HALVED, opened_ref)
    ends_ref[...] = jnp.zeros(ends_ref.shape, jnp.float32)
    low = jnp.where(lanes_of(senders * STEP) < HALF, 0.0, 1.0)
    rank_row = lax.broadcasted_iota(jnp.int32, (rank, LANES), 0)
    twofold = jnp.where(lax.rem(lanes_of(rank), rank) == rank_row, 1.0, 0.0).astype(jnp.bfloat16)

    note_row = lax.broadcasted_iota(jnp.int32, (LANES, LANES), 0)
    for a in range(label_ref.shape[0]):
        wanted = jnp.where(note_row == NOTE + a, 1.0, 0.0).astype(jnp.bfloat16)
        label_ref[a] = jnp.dot(notes_ref[...], wanted, preferred_element_type=jnp.float32) - low
        down = sum_refs[0][a].astype(jnp.float32) + sum_refs[1][a].astype(jnp.float32)
        twice_ref[a] = lax.dot_general(
            down.astype(jnp.bfloat16),
            twofold,
            (((0,), (0,)), ((), ())),
            preferred_element_type=jnp.float32,
        )

    def one(a, carry):
        @pl.when(met_ref[a] == 0)
        def _():
            delta_ref[...] = jnp.zeros(delta_ref.shape, jnp.float32)

        @pl.when(met_ref[a] > 0)
        def _():
            label, twice = label_ref[a], twice_ref[a]

            def step(weight_ref, firsts, is_first):
                placed = [jnp.where(label == first, twice, 0.0) for first in firsts]
                placed = jnp.concatenate(placed, axis=1).astype(jnp.bfloat16)
                before = jnp.where(is_first, 0.0, delta_ref[...])
                delta_ref[...] = before + jnp.dot(
                    placed, weight_ref[...], preferred_element_type=jnp.float32
                )

            for_holders(met_ref, first_ref, near_refs, opened_ref, UP_HALVED, a, step)

        spot = pl.multiple_of(lax.rem(a, 2) * STEP, STEP)
        for s in range(senders):
            rows = slice(s * STEP, (s + 1) * STEP)
            turned = pltpu.roll(delta_ref[rows, tiles * LANES :], QUARTER * (a // 2), 1)
            ends_ref[s, pl.ds(spot, STEP), :] = jnp.where(
                group_lane == a // 2, turned, ends_ref[s, pl.ds(spot, STEP), :]
            )

        @pl.when(a < full // STEP)
        def _():
            for s in range(senders):
                rows = slice(s * STEP, (s + 1) * STEP)
                for t in range(tiles):
                    at = pl.multiple_of(t * full + a * STEP, STEP)
                    out_ref[s, pl.ds(at, STEP), :] = delta_ref[
                        rows, t * LANES : (t + 1) * LANES
                    ].astype(jnp.bfloat16)

        return carry

    lax.fori_loop(0, label_ref.shape[0], one, 0)
    if kept > full:
        for s in range(senders):
            rows = slice(s * STEP, s * STEP + STEP // 2)
            for t in range(0, tiles, 2):
                both = [
                    delta_ref[rows, (t + i) * LANES : (t + i + 1) * LANES] for i in range(2)
                ]
                at = tiles * full + t * (STEP // 2)
                out_ref[s, at : at + STEP, :] = jnp.concatenate(both, axis=0).astype(jnp.bfloat16)
    for s in range(senders):
        out_ref[s, tiles * kept :, :] = ends_ref[s].astype(jnp.bfloat16)


def mix_kernel(whole, bases, target_ref, tokens_ref, *refs):
    returned_refs, out_ref = refs[:-1], refs[-1]
    total = tokens_ref.shape[0]
    tiles, quads = whole // LANES, returned_refs[0].shape[0] // QUAD
    lane = lanes_of(total)
    chosen = []
    for base, ref in zip(bases, returned_refs):
        kept = (ref.shape[1] - QUARTER) // tiles
        full = kept // STEP * STEP
        spot = lax.broadcasted_iota(jnp.int32, (total, quads * kept), 1)
        place = spot // full * total + spot % full
        if kept > full:
            later = spot - quads * full
            half_place = later // (STEP // 2) * total + later % (STEP // 2) + full
            place = jnp.where(later >= 0, half_place, place)
        place = place + base
        chosen.append(jnp.where(target_ref[...] == place, 1.0, 0.0).astype(jnp.bfloat16))

    def one(j, end):
        delta = 0.0
        for choice, ref in zip(chosen, returned_refs):
            kept = choice.shape[1] // quads
            full = kept // STEP * STEP
            shares, halves = [], []
            for q in range(quads):
                d = q * QUAD + j
                parts = [ref[d, t * full : (t + 1) * full, :] for t in range(tiles)]
                packed = ref[d, tiles * kept :, :].astype(jnp.float32)
                groups = [packed]
                for m in range(1, QUAD):
                    groups.append(pltpu.roll(packed, LANES - QUARTER * m, 1))
                ends = jnp.concatenate(groups, axis=0)
                parts.append(ends[0:full].astype(jnp.bfloat16))
                shares.append(jnp.concatenate(parts, axis=1))
                if kept > full:
                    pairs = ref[d, tiles * full : tiles * kept, :].astype(jnp.float32)
                    parts = [pairs[t * (STEP // 2) : (t + 1) * (STEP // 2)] for t in range(tiles)]
                    halves.append(jnp.concatenate([*parts, ends[full:kept]], axis=1))
            if halves:
                shares.append(jnp.concatenate(halves, axis=0).astype(jnp.bfloat16))
            share = jnp.concatenate(shares, axis=0)
            delta = delta + jnp.dot(choice, share, preferred_element_type=jnp.float32)
        columns = pl.ds(pl.multiple_of(j * whole, LANES), whole)
        out_ref[:, columns] = (
            tokens_ref[:, columns].astype(jnp.float32) + delta[:, 0:whole]
        ).astype(jnp.bfloat16)
        turned = pltpu.roll(delta[:, whole:], QUARTER * j, 1)
        return jnp.where(lane // QUARTER == j, turned, end)

    end = lax.fori_loop(0, QUAD, one, jnp.zeros((total, LANES), jnp.float32), unroll=2)
    out_ref[:, QUAD * whole :] = (
        tokens_ref[:, QUAD * whole :].astype(jnp.float32) + end
    ).astype(jnp.bfloat16)


def call(kernel, out_shape, in_specs, flops, moved, after=(), scratch=(), out_specs=None):
    many = isinstance(out_shape, list)
    skipped = len(after)
    body = (lambda *refs: kernel(*refs[skipped:])) if skipped else kernel
    run = pl.pallas_call(
        body,
        out_shape=out_shape,
        in_specs=[pl.BlockSpec(memory_space=pl.ANY)] * skipped + in_specs,
        out_specs=out_specs or ([VMEM] * len(out_shape) if many else VMEM),
        scratch_shapes=scratch,
        compiler_params=pltpu.CompilerParams(vmem_limit_bytes=18 * 2**20),
        cost_estimate=pl.CostEstimate(flops=flops, bytes_accessed=moved, transcendentals=0),
    )
    return functools.partial(run, *after)


def exchange(value):
    return lax.all_to_all(value, "adapter", split_axis=0, concat_axis=0, tiled=True)


def towards(value, k, devices):
    return lax.ppermute(value, "adapter", [(i, i ^ k) for i in range(devices)])


def swapped(value):
    return lax.ppermute(value, "groups", [(0, 1), (1, 0)])


def stand_behind(value, *earlier):
    return pl.pallas_call(
        lambda *refs: None,
        out_shape=jax.ShapeDtypeStruct(value.shape, value.dtype),
        in_specs=[pl.BlockSpec(memory_space=pl.ANY)] * (1 + len(earlier)),
        out_specs=pl.BlockSpec(memory_space=pl.ANY),
        input_output_aliases={0: 0},
    )(value, *earlier)


def first_pack_call(cap, whole, devices, resident, adapter, used, tokens):
    blocks, rows, width = tokens.shape
    total = blocks * rows
    return call(
        functools.partial(first_pack_kernel, whole, cap, resident),
        [
            jax.ShapeDtypeStruct((devices, whole // LANES * cap + QUARTER, LANES), jnp.bfloat16),
            jax.ShapeDtypeStruct((1, total), jnp.int32),
            jax.ShapeDtypeStruct((total, 1), jnp.float32),
        ],
        [VMEM, VMEM, VMEM],
        2 * devices * cap * total * whole,
        2 * (total * width + devices * cap * whole),
        scratch=[pltpu.VMEM((total, width), jnp.bfloat16), pltpu.VMEM((8, LANES), jnp.int32)],
    )(adapter.reshape(1, blocks), used.reshape(1, blocks), tokens.reshape(total, width))


def pack_call(cap, base, whole, devices, target, label, tokens):
    blocks, rows, width = tokens.shape
    total = blocks * rows
    return call(
        functools.partial(pack_kernel, whole, cap, base),
        jax.ShapeDtypeStruct((devices, whole // LANES * cap + QUARTER, LANES), jnp.bfloat16),
        [VMEM, VMEM, VMEM, VMEM],
        2 * devices * cap * total * whole,
        2 * (total * width + devices * cap * whole),
        scratch=[pltpu.VMEM((total, width), jnp.bfloat16)],
    )(jnp.zeros((8, LANES), jnp.int32), target, label, tokens.reshape(total, width))


def down_call(cap, first, arrived, down_weights, after):
    devices = arrived.shape[0]
    columns, share = down_weights[0].shape
    return call(
        down_kernel,
        [
            jax.ShapeDtypeStruct((cap // STEP, HALF, devices * STEP), jnp.float32),
            jax.ShapeDtypeStruct((STEP, LANES), jnp.bfloat16),
            jax.ShapeDtypeStruct((devices * STEP, LANES), jnp.bfloat16),
            jax.ShapeDtypeStruct((8,), jnp.int32),
        ],
        [SMEM] + [VMEM] * (1 + len(down_weights)),
        0,
        0,
        after,
        [
            pltpu.VMEM((2, columns, share), jnp.bfloat16),
            pltpu.VMEM((devices * STEP, share), jnp.bfloat16),
            pltpu.VMEM((HALF, devices * STEP), jnp.float32),
            pltpu.VMEM((8, devices * STEP), jnp.float32),
        ],
        [VMEM, VMEM, VMEM, SMEM],
    )(first, arrived, *down_weights)


def quad_sums(partial, devices):
    pair = call(
        pair_kernel, jax.ShapeDtypeStruct(partial.shape, jnp.bfloat16), [VMEM, VMEM], 0, 0
    )(partial, towards(partial, 1, devices))
    return [pair, towards(pair, 2, devices)]


def up_call(kept, first, met, notes, sums, up_weights):
    devices = notes.shape[0] // STEP
    columns, share = up_weights[0].shape
    shape = (devices, (share // LANES - 1) * kept + QUARTER, LANES)
    return call(
        up_kernel,
        jax.ShapeDtypeStruct(shape, jnp.bfloat16),
        [SMEM, SMEM] + [VMEM] * (3 + len(up_weights)),
        2 * devices * kept * QUAD * columns * share,
        2 * (2 * devices * kept + QUAD * columns) * share,
        scratch=[
            pltpu.VMEM((2, columns, share), jnp.bfloat16),
            pltpu.VMEM((devices * STEP, share), jnp.float32),
            pltpu.VMEM((devices, QUARTER, LANES), jnp.float32),
            *[pltpu.VMEM((-(-kept // STEP), devices * STEP, LANES), jnp.float32)] * 2,
        ],
    )(first, met, notes, *sums, *up_weights)


def back_and_mix(
    kept, more, tokens, target, label, first, met, notes, sums, down_weights, up_weights, *unused
):
    blocks, rows, width = tokens.shape
    total = blocks * rows
    devices = notes.shape[0] // STEP
    whole = up_weights[0].shape[1] - LANES
    pieces = [exchange(up_call(kept, first, met, notes, sums, up_weights))]
    if more:
        outgoing = pack_call(more, kept, whole, devices, target, label, tokens)
        arrived = exchange(outgoing)
        partial, unused_count, notes, met = down_call(more, first, arrived, down_weights, [])
        sums = quad_sums(partial, devices)
        pieces.append(exchange(up_call(more, first, met, notes, sums, up_weights)))
    mixed = call(
        functools.partial(mix_kernel, whole, (0, kept)[: len(pieces)]),
        jax.ShapeDtypeStruct((total, width), jnp.bfloat16),
        [VMEM] * (2 + len(pieces)),
        2 * devices * (kept + more) * total * whole,
        2 * (2 * total * width + devices * (kept + more) * whole),
    )(target.reshape(total, 1), tokens.reshape(total, width), *pieces)
    return mixed.reshape(tokens.shape)


def start_again(
    tokens, target, label, first, met, notes, sums, down_weights, up_weights, *arguments
):
    return rows_to_holders(tokens, *arguments)


def rows_to_quads(
    tokens, request_block_adapter, request_block_rows, adapter_down_weight, adapter_up_weight
):
    blocks, rows, width = tokens.shape
    devices = lax.axis_size("adapter")
    resident, rank, unused_width = adapter_up_weight.shape
    total = blocks * rows
    columns = resident * rank
    whole = width // LANES // QUAD * LANES
    share = whole + LANES
    bf16, i32 = jnp.bfloat16, jnp.int32

    me = lax.axis_index("adapter").astype(i32)
    group = lax.axis_index("groups").astype(i32)
    parts = jnp.bitwise_xor(me % QUAD, jnp.arange(QUAD, dtype=i32))
    halves = jnp.stack([group, 1 - group]) * (resident // 2)
    first = jnp.concatenate([parts * resident, halves]).astype(i32)
    tiles = whole // LANES

    def shares(weight, which, halved, after):
        shapes = []
        for k in which:
            count = columns // 2 if k in halved else columns
            far = (count * tiles + count // QUAD, LANES)
            shapes.append(jax.ShapeDtypeStruct((columns, share) if k < 2 else far, bf16))
        return call(
            functools.partial(weight_kernel, whole, which, halved),
            shapes,
            [SMEM, SMEM, VMEM],
            0,
            len(which) * columns * width,
            after,
        )(parts, group.reshape(1), weight)

    down_weight = adapter_down_weight.transpose(0, 2, 1).reshape(columns, width)
    up_weight = adapter_up_weight.reshape(columns, width)
    down_far = shares(down_weight, (2, 3), DOWN_HALVED, [])
    up_far = shares(up_weight, (2, 3), UP_HALVED, down_far[:1])
    down_near = shares(down_weight, (0, 1), (), up_far[:1])
    up_near = shares(up_weight, (0, 1), (), down_near[:1])
    down_weights = [down_near[0], towards(down_near[1], 1, devices)]
    down_weights += [towards(value, k, devices) for k, value in zip((2, 3), down_far)]
    up_weights = [up_near[0], towards(up_near[1], 1, devices)]
    up_weights += [towards(value, k, devices) for k, value in zip((2, 3), up_far)]
    down_weights[2] = stand_behind(down_weights[2], up_near[0])
    down_weights += [swapped(down_weights[k]) for k in DOWN_HALVED]
    up_weights += [swapped(up_weights[k]) for k in UP_HALVED]

    caps = [total * 10 // 32, total * 11 // 32, total * 12 // 32, total * 14 // 32]
    cap = caps[-1]
    outgoing, target, label = first_pack_call(
        cap, whole, devices, resident, request_block_adapter, request_block_rows, tokens
    )
    arrived = exchange(outgoing)
    partial, count, notes, met = down_call(cap, first, arrived, down_weights, up_weights[2:3])
    sums = quad_sums(partial, devices)
    count = count[0:1, 0:1]
    most = jnp.maximum(count, swapped(count))[0, 0].astype(jnp.float32)
    branches = [functools.partial(back_and_mix, kept, 0) for kept in caps]
    branches += [functools.partial(back_and_mix, cap, STEP), start_again]
    return lax.switch(
        sum((most > limit).astype(i32) for limit in [*caps, cap + STEP]),
        branches,
        tokens,
        target,
        label,
        first,
        met,
        notes,
        sums,
        down_weights,
        up_weights,
        request_block_adapter,
        request_block_rows,
        adapter_down_weight,
        adapter_up_weight,
    )


def solution(mesh):
    placed = (
        P(("groups", "adapter"), None, None),
        P(("groups", "adapter")),
        P(("groups", "adapter")),
        P("adapter", None, None),
        P("adapter", None, None),
    )

    def per_device(tokens, request_block_adapter, request_block_rows, down_weight, up_weight):
        blocks, rows, width = tokens.shape
        devices = mesh.shape["adapter"]
        slots = max(1, 4 * blocks // devices)
        quads = devices % QUAD == 0 and slots * QUAD >= blocks
        quads = quads and width % (QUAD * LANES) == LANES and up_weight.shape[1] == HALF
        quads = quads and blocks * rows * 7 // 16 == 7 * STEP and mesh.shape["groups"] == 2
        plan = rows_to_quads if quads else rows_to_holders
        return plan(tokens, request_block_adapter, request_block_rows, down_weight, up_weight)

    return jax.shard_map(
        per_device,
        mesh=mesh,
        in_specs=placed,
        out_specs=P(("groups", "adapter"), None, None),
        check_vma=False,
    )
```

```python
import functools

import jax
import jax.numpy as jnp
from jax import lax
from jax.experimental import pallas as pl
from jax.experimental.pallas import tpu as pltpu
from jax.sharding import PartitionSpec as P

LANES = 128
HALF = 64
QUAD = 4
QUARTER = 32
STEP = 16
NOTE = 96
DOWN_HALVED = (2, 3)
UP_HALVED = (2,)
VMEM = pl.BlockSpec(memory_space=pltpu.VMEM)
SMEM = pl.BlockSpec(memory_space=pltpu.SMEM)


def normalise(tokens):
    values = tokens.astype(jnp.float32)
    mean_sq = jnp.mean(values * values, axis=-1, keepdims=True)
    return (values, (values * lax.rsqrt(mean_sq + 1e-06)).astype(jnp.bfloat16))


def resident_update(hidden_state, block_labels, adapter_down_weight, adapter_up_weight):
    feature_width = hidden_state.shape[-1]
    leading = hidden_state.shape[:-1]
    resident_rows, unused_value, inner_rank = adapter_down_weight.shape
    flattened_tokens = hidden_state.reshape(-1, feature_width)
    down_matrix = jnp.einsum(
        "tq,iqg->tig", flattened_tokens, adapter_down_weight, preferred_element_type=jnp.float32
    )
    down_matrix = down_matrix.astype(jnp.bfloat16).reshape(
        flattened_tokens.shape[0], resident_rows * inner_rank
    )
    column_owner = jnp.arange(resident_rows * inner_rank, dtype=jnp.int32) // inner_rank
    picked = block_labels.reshape(-1, 1) == column_owner[None, :]
    down_matrix = jnp.where(picked, down_matrix, jnp.zeros_like(down_matrix))
    lowrank_update = jnp.dot(
        down_matrix,
        adapter_up_weight.reshape(resident_rows * inner_rank, feature_width),
        preferred_element_type=jnp.float32,
    )
    return lowrank_update.astype(jnp.bfloat16).reshape(leading + (feature_width,))


def rows_to_holders(
    tokens, request_block_adapter, request_block_rows, adapter_down_weight, adapter_up_weight
):
    blocks, rows, feature_width = tokens.shape
    devices = lax.axis_size("adapter")
    resident_rows = adapter_down_weight.shape[0]
    slots = max(1, 4 * blocks // devices)
    values, normed = normalise(tokens)
    owner = request_block_adapter // resident_rows
    within = request_block_adapter - owner * resident_rows
    serial = jnp.arange(blocks, dtype=jnp.int32)
    earlier = (owner[:, None] == owner[None, :]) & (serial[None, :] < serial[:, None])
    position = owner * slots + jnp.sum(earlier, axis=1)
    outgoing = (
        jnp.zeros((devices * slots, rows, feature_width), jnp.bfloat16).at[position].set(normed)
    )
    outgoing = outgoing.reshape(devices, slots, rows, feature_width)
    block_labels = jnp.full((devices * slots,), -1, jnp.int32).at[position].set(within)
    block_labels = jnp.broadcast_to(block_labels[:, None], (devices * slots, rows)).reshape(
        devices, slots, rows
    )
    arriving_rows, row_markers = (
        lax.all_to_all(outgoing, "adapter", split_axis=0, concat_axis=0, tiled=True),
        lax.all_to_all(block_labels, "adapter", split_axis=0, concat_axis=0, tiled=True),
    )
    lowrank_update = resident_update(
        arriving_rows, row_markers, adapter_down_weight, adapter_up_weight
    )
    returned = lax.all_to_all(lowrank_update, "adapter", split_axis=0, concat_axis=0, tiled=True)
    mine = returned.reshape(devices * slots, rows, feature_width)[position]
    live = jnp.arange(rows, dtype=jnp.int32)[None, :] < request_block_rows[:, None]
    mixed = values + jnp.where(live[:, :, None], mine.astype(jnp.float32), jnp.float32(0.0))
    return mixed.astype(jnp.bfloat16)


def lanes_of(rows):
    return lax.broadcasted_iota(jnp.int32, (rows, LANES), 1)


def weight_kernel(whole, which, halved, part_ref, group_ref, weight_ref, *out_refs):
    tiles = whole // LANES
    for k, out_ref in zip(which, out_refs):
        j = part_ref[k]
        if k < 2:
            last = weight_ref[:, QUAD * whole :].astype(jnp.float32)
            turned = pltpu.roll(last, lax.rem(LANES - QUARTER * j, LANES), 1)
            inside = lanes_of(last.shape[0]) < QUARTER
            out_ref[:, 0:whole] = weight_ref[:, pl.ds(pl.multiple_of(j * whole, LANES), whole)]
            out_ref[:, whole:] = jnp.where(inside, turned, 0.0).astype(jnp.bfloat16)
            continue
        count = weight_ref.shape[0] // 2 if k in halved else weight_ref.shape[0]
        start = pl.multiple_of(group_ref[0] * count, count) if k in halved else 0
        for t in range(tiles):
            column = pl.multiple_of(j * whole + t * LANES, LANES)
            out_ref[t * count : (t + 1) * count, :] = weight_ref[
                pl.ds(start, count), pl.ds(column, LANES)
            ]
        last = weight_ref[pl.ds(start, count), QUAD * whole :].astype(jnp.float32)
        size = count // QUAD
        owner = lanes_of(size) // QUARTER
        merged = jnp.zeros((size, LANES), jnp.float32)
        for m in range(QUAD):
            shift = lax.rem(LANES + QUARTER * (m - j), LANES)
            turned = pltpu.roll(last[m * size : (m + 1) * size], shift, 1)
            merged = jnp.where(owner == m, turned, merged)
        out_ref[tiles * count :, :] = merged.astype(jnp.bfloat16)


def open_far(far_refs, halved, opened_ref):
    width = opened_ref.shape[2]
    tiles = width // LANES - 1
    places = [(k - 2, 0) for k in (2, 3)] + [(k - 2, 1) for k in halved]
    for ref, (holder, part) in zip(far_refs, places):
        count = opened_ref.shape[1] // 2 if holder + 2 in halved else opened_ref.shape[1]
        base, size = part * count, count // QUAD
        inside = lanes_of(size) < QUARTER
        for t in range(tiles):
            opened_ref[holder, base : base + count, t * LANES : (t + 1) * LANES] = ref[
                t * count : (t + 1) * count, :
            ]
        packed = ref[tiles * count :, :].astype(jnp.float32)
        for m in range(QUAD):
            turned = pltpu.roll(packed, (LANES - QUARTER * m) % LANES, 1) if m else packed
            opened_ref[holder, base + m * size : base + (m + 1) * size, tiles * LANES :] = (
                jnp.where(inside, turned, 0.0).astype(jnp.bfloat16)
            )


def lay_out(resident, adapter_ref, used_ref, most_ref, target_ref, label_ref):
    blocks, total = adapter_ref.shape[1], target_ref.shape[1]
    rows = total // blocks
    adapter, used = adapter_ref[...], used_ref[...]
    down = lax.broadcasted_iota(jnp.int32, (blocks, blocks), 0)
    across = lax.broadcasted_iota(jnp.int32, (blocks, blocks), 1)

    def turned(value):
        return jnp.sum(jnp.where(down == across, value, 0), axis=1, keepdims=True)

    span = resident * QUAD
    quad = jnp.floor((adapter.astype(jnp.float32) + 0.5) * (1.0 / span)).astype(jnp.int32)
    order = adapter * blocks + lax.broadcasted_iota(jnp.int32, (1, blocks), 1)
    quad_down, order_down, used_down = turned(quad), turned(order), turned(used)
    same = quad_down == quad
    ahead = jnp.sum(jnp.where(same & (order < order_down), used, 0), axis=1, keepdims=True)
    within = jnp.sum(jnp.where(same, used, 0), axis=1, keepdims=True)
    most_ref[...] = jnp.broadcast_to(jnp.max(within, axis=0, keepdims=True), most_ref.shape)
    start = quad_down * total + ahead

    block = lax.broadcasted_iota(jnp.int32, (blocks, total), 0)
    row = lax.broadcasted_iota(jnp.int32, (blocks, total), 1) - block * rows
    place = jnp.where((row >= 0) & (row < used_down), start + row + 1, 0)
    target_ref[...] = jnp.sum(place, axis=0, keepdims=True) - 1
    block = lax.broadcasted_iota(jnp.int32, (total, blocks), 1)
    row = lax.broadcasted_iota(jnp.int32, (total, blocks), 0) - block * rows
    label = jnp.where((row >= 0) & (row < rows), adapter - quad * span + 1, 0)
    label_ref[...] = jnp.sum(label.astype(jnp.float32), axis=1, keepdims=True)


def first_pack_kernel(
    whole, cap, resident, adapter_ref, used_ref, tokens_ref, out_ref, target_ref, label_ref, *refs
):
    normed_ref, most_ref = refs
    lay_out(resident, adapter_ref, used_ref, most_ref, target_ref, label_ref)
    pack_kernel(
        whole, cap, 0, most_ref, target_ref, label_ref, tokens_ref, out_ref, normed_ref
    )


def pack_kernel(
    whole, cap, base, most_ref, target_ref, label_ref, tokens_ref, out_ref, normed_ref
):
    values = tokens_ref[...].astype(jnp.float32)
    mean_sq = jnp.mean(values * values, axis=-1, keepdims=True)
    normed_ref[...] = (values * lax.rsqrt(mean_sq + 1e-06)).astype(jnp.bfloat16)
    total = tokens_ref.shape[0]
    quads, tiles = out_ref.shape[0] // QUAD, whole // LANES
    lane = lanes_of(total)
    last = normed_ref[:, QUAD * whole :].astype(jnp.float32)
    label = jnp.where(lane == QUARTER, label_ref[...], 0.0)
    ends = []
    for j in range(QUAD):
        turned = pltpu.roll(last, (LANES - QUARTER * j) % LANES, 1) if j else last
        ends.append(jnp.where(lane < QUARTER, turned, label).astype(jnp.bfloat16))
    most = most_ref[0:1, 0:1].astype(jnp.float32)
    group_lane = lanes_of(QUARTER) // QUARTER
    step_lane = lanes_of(STEP)
    chosen = []
    for q in range(quads):
        place = lax.broadcasted_iota(jnp.int32, (cap, total), 0) + (q * total + base)
        chosen.append(jnp.where(target_ref[...] == place, 1.0, 0.0).astype(jnp.bfloat16))
    chosen = jnp.concatenate(chosen, axis=0)
    notes = [jnp.where(step_lane == NOTE + cap // STEP, most, 0.0)] * quads
    for j in range(QUAD):
        for t in range(tiles):
            column = j * whole + t * LANES
            if t % 2 == 0:
                count = min(2, tiles - t) * LANES
                share = jnp.dot(
                    chosen,
                    normed_ref[:, column : column + count],
                    preferred_element_type=jnp.float32,
                ).astype(jnp.bfloat16)
            for q in range(quads):
                out_ref[q * QUAD + j, t * cap : (t + 1) * cap, :] = share[
                    q * cap : (q + 1) * cap, t % 2 * LANES : (t % 2 + 1) * LANES
                ]
        end_rows = jnp.dot(chosen, ends[j], preferred_element_type=jnp.float32)
        for q in range(quads):
            end = end_rows[q * cap : (q + 1) * cap]
            if j == 0:
                for a in range(cap // STEP):
                    turned = pltpu.roll(end[a * STEP : (a + 1) * STEP], NOTE + a - QUARTER, 1)
                    notes[q] = jnp.where(step_lane == NOTE + a, turned, notes[q])
            padded = jnp.concatenate(
                [end, jnp.zeros((QUAD * QUARTER - cap, LANES), jnp.float32)], axis=0
            )
            merged = padded[0:QUARTER]
            for m in range(1, QUAD):
                turned = pltpu.roll(padded[m * QUARTER : (m + 1) * QUARTER], m * QUARTER, 1)
                merged = jnp.where(group_lane == m, turned, merged)
            out_ref[q * QUAD + j, tiles * cap : tiles * cap + STEP, :] = merged[0:STEP].astype(
                jnp.bfloat16
            )
            out_ref[q * QUAD + j, tiles * cap + STEP :, :] = jnp.where(
                step_lane >= NOTE, notes[q], merged[STEP:]
            ).astype(jnp.bfloat16)


def read_notes(rows_ref, cap, tiles, part_ref, resident, notes_ref, labels_ref, met_ref):
    senders = rows_ref.shape[0]
    for s in range(senders):
        notes_ref[s * STEP : (s + 1) * STEP, :] = rows_ref[s, tiles * cap + STEP :, :]
    steps = labels_ref.shape[0]
    row = lax.broadcasted_iota(jnp.int32, (steps, LANES), 0)
    wanted = jnp.where(lanes_of(steps) == NOTE + row, 1.0, 0.0).astype(jnp.bfloat16)
    labels = lax.dot_general(
        wanted, notes_ref[...], (((1,), (1,)), ((), ())), preferred_element_type=jnp.float32
    )
    labels_ref[...] = labels
    code = jnp.zeros((steps, 1), jnp.float32)
    for h in range(QUAD):
        first = part_ref[h].astype(jnp.float32) + 1.0
        met = jnp.where((labels >= first) & (labels < first + resident), 1.0, 0.0)
        code = code + (1 << h) * jnp.max(met, axis=1, keepdims=True)
    at = lax.broadcasted_iota(jnp.int32, (steps, 1), 0)
    for a in range(cap // STEP):
        met_ref[a] = jnp.max(jnp.where(at == a, code, 0.0)).astype(jnp.int32)


def for_holders(met_ref, first_ref, near_refs, opened_ref, halved, a, step):
    pairs = opened_ref.shape[1] // LANES
    for h in range(QUAD):
        base = first_ref[h].astype(jnp.float32) + 1.0
        firsts = [base + 2.0 * t for t in range(pairs)]
        if h in halved:
            firsts = [
                base + first_ref[QUAD + i].astype(jnp.float32) + 2.0 * t
                for i in range(2)
                for t in range(pairs // 2)
            ]

        @pl.when(lax.rem(met_ref[a] // (1 << h), 2) > 0)
        def _(h=h, firsts=firsts):
            is_first = lax.rem(met_ref[a], 1 << h) == 0
            step(near_refs[h] if h < 2 else opened_ref.at[h - 2], firsts, is_first)


def down_kernel(first_ref, rows_ref, *refs):
    near_refs, far_refs, out_ref, count_ref = refs[:2], refs[2:6], refs[6], refs[7]
    notes_ref, met_ref, opened_ref, batch_ref, picked_ref, labels_ref = refs[8:]
    senders, width = rows_ref.shape[0], batch_ref.shape[1]
    tiles = width // LANES - 1
    cap = out_ref.shape[0] * STEP
    rank = out_ref.shape[1]
    resident = opened_ref.shape[1] // rank
    dims = (((1,), (1,)), ((), ()))
    read_notes(rows_ref, cap, tiles, first_ref, resident, notes_ref, labels_ref, met_ref)
    notes = notes_ref[...].astype(jnp.float32)
    is_count = lanes_of(senders * STEP) == NOTE + cap // STEP
    count = jnp.max(jnp.where(is_count, notes, 0.0), axis=(0, 1), keepdims=True)
    count_ref[...] = jnp.broadcast_to(count, count_ref.shape).astype(jnp.bfloat16)
    open_far(far_refs, DOWN_HALVED, opened_ref)

    def one(a, carry):
        picked_ref[...] = jnp.zeros(picked_ref.shape, jnp.float32)

        @pl.when(met_ref[a] > 0)
        def _():
            shift = lax.rem(LANES - QUARTER * (a // 2), LANES)
            spot = pl.multiple_of(tiles * cap + lax.rem(a, 2) * STEP, STEP)
            for s in range(senders):
                rows = slice(s * STEP, (s + 1) * STEP)
                for t in range(tiles):
                    at = pl.multiple_of(t * cap + a * STEP, STEP)
                    batch_ref[rows, t * LANES : (t + 1) * LANES] = rows_ref[s, pl.ds(at, STEP), :]
                end = rows_ref[s, pl.ds(spot, STEP), :].astype(jnp.float32)
                batch_ref[rows, tiles * LANES :] = pltpu.roll(end, shift, 1).astype(jnp.bfloat16)
            label = labels_ref[pl.ds(a, 1), :]

            def step(weight_ref, firsts, is_first):
                product = lax.dot_general(
                    weight_ref[...], batch_ref[...], dims, preferred_element_type=jnp.float32
                )
                picked = picked_ref[...]
                for t, first in enumerate(firsts):
                    for i in range(2):
                        at = (2 * t + i) * rank
                        picked = jnp.where(
                            label == first + i, product[at : at + rank, :], picked
                        )
                picked_ref[...] = picked

            for_holders(met_ref, first_ref, near_refs, opened_ref, DOWN_HALVED, a, step)

        out_ref[a] = picked_ref[...]
        return carry

    lax.fori_loop(0, cap // STEP, one, 0)


def pair_kernel(own_ref, other_ref, out_ref):
    out_ref[...] = (own_ref[...] + other_ref[...]).astype(jnp.bfloat16)


def up_kernel(first_ref, met_ref, notes_ref, *refs):
    sum_refs, near_refs, far_refs, out_ref = refs[:2], refs[2:4], refs[4:7], refs[7]
    opened_ref, delta_ref, ends_ref, label_ref, twice_ref = refs[8:]
    senders, width = out_ref.shape[0], opened_ref.shape[2]
    tiles = width // LANES - 1
    rank = sum_refs[0].shape[1]
    kept = (out_ref.shape[1] - QUARTER) // tiles
    full = kept // STEP * STEP
    group_lane = lanes_of(STEP) // QUARTER
    open_far(far_refs, UP_HALVED, opened_ref)
    ends_ref[...] = jnp.zeros(ends_ref.shape, jnp.float32)
    low = jnp.where(lanes_of(senders * STEP) < HALF, 0.0, 1.0)
    rank_row = lax.broadcasted_iota(jnp.int32, (rank, LANES), 0)
    twofold = jnp.where(lax.rem(lanes_of(rank), rank) == rank_row, 1.0, 0.0).astype(jnp.bfloat16)

    note_row = lax.broadcasted_iota(jnp.int32, (LANES, LANES), 0)
    for a in range(label_ref.shape[0]):
        wanted = jnp.where(note_row == NOTE + a, 1.0, 0.0).astype(jnp.bfloat16)
        label_ref[a] = jnp.dot(notes_ref[...], wanted, preferred_element_type=jnp.float32) - low
        down = sum_refs[0][a].astype(jnp.float32) + sum_refs[1][a].astype(jnp.float32)
        twice_ref[a] = lax.dot_general(
            down.astype(jnp.bfloat16),
            twofold,
            (((0,), (0,)), ((), ())),
            preferred_element_type=jnp.float32,
        )

    def one(a, carry):
        @pl.when(met_ref[a] == 0)
        def _():
            delta_ref[...] = jnp.zeros(delta_ref.shape, jnp.float32)

        @pl.when(met_ref[a] > 0)
        def _():
            label, twice = label_ref[a], twice_ref[a]

            def step(weight_ref, firsts, is_first):
                placed = [jnp.where(label == first, twice, 0.0) for first in firsts]
                placed = jnp.concatenate(placed, axis=1).astype(jnp.bfloat16)
                before = jnp.where(is_first, 0.0, delta_ref[...])
                delta_ref[...] = before + jnp.dot(
                    placed, weight_ref[...], preferred_element_type=jnp.float32
                )

            for_holders(met_ref, first_ref, near_refs, opened_ref, UP_HALVED, a, step)

        spot = pl.multiple_of(lax.rem(a, 2) * STEP, STEP)
        for s in range(senders):
            rows = slice(s * STEP, (s + 1) * STEP)
            turned = pltpu.roll(delta_ref[rows, tiles * LANES :], QUARTER * (a // 2), 1)
            ends_ref[s, pl.ds(spot, STEP), :] = jnp.where(
                group_lane == a // 2, turned, ends_ref[s, pl.ds(spot, STEP), :]
            )

        @pl.when(a < full // STEP)
        def _():
            for s in range(senders):
                rows = slice(s * STEP, (s + 1) * STEP)
                for t in range(tiles):
                    at = pl.multiple_of(t * full + a * STEP, STEP)
                    out_ref[s, pl.ds(at, STEP), :] = delta_ref[
                        rows, t * LANES : (t + 1) * LANES
                    ].astype(jnp.bfloat16)

        return carry

    lax.fori_loop(0, label_ref.shape[0], one, 0)
    if kept > full:
        for s in range(senders):
            rows = slice(s * STEP, s * STEP + STEP // 2)
            for t in range(0, tiles, 2):
                both = [
                    delta_ref[rows, (t + i) * LANES : (t + i + 1) * LANES] for i in range(2)
                ]
                at = tiles * full + t * (STEP // 2)
                out_ref[s, at : at + STEP, :] = jnp.concatenate(both, axis=0).astype(jnp.bfloat16)
    for s in range(senders):
        out_ref[s, tiles * kept :, :] = ends_ref[s].astype(jnp.bfloat16)


def mix_kernel(whole, bases, target_ref, tokens_ref, *refs):
    returned_refs, out_ref = refs[:-1], refs[-1]
    total = tokens_ref.shape[0]
    tiles, quads = whole // LANES, returned_refs[0].shape[0] // QUAD
    lane = lanes_of(total)
    chosen = []
    for base, ref in zip(bases, returned_refs):
        kept = (ref.shape[1] - QUARTER) // tiles
        full = kept // STEP * STEP
        spot = lax.broadcasted_iota(jnp.int32, (total, quads * kept), 1)
        place = spot // full * total + spot % full
        if kept > full:
            later = spot - quads * full
            half_place = later // (STEP // 2) * total + later % (STEP // 2) + full
            place = jnp.where(later >= 0, half_place, place)
        place = place + base
        chosen.append(jnp.where(target_ref[...] == place, 1.0, 0.0).astype(jnp.bfloat16))

    def one(j, end):
        delta = 0.0
        for choice, ref in zip(chosen, returned_refs):
            kept = choice.shape[1] // quads
            full = kept // STEP * STEP
            shares, halves = [], []
            for q in range(quads):
                d = q * QUAD + j
                parts = [ref[d, t * full : (t + 1) * full, :] for t in range(tiles)]
                packed = ref[d, tiles * kept :, :].astype(jnp.float32)
                groups = [packed]
                for m in range(1, QUAD):
                    groups.append(pltpu.roll(packed, LANES - QUARTER * m, 1))
                ends = jnp.concatenate(groups, axis=0)
                parts.append(ends[0:full].astype(jnp.bfloat16))
                shares.append(jnp.concatenate(parts, axis=1))
                if kept > full:
                    pairs = ref[d, tiles * full : tiles * kept, :].astype(jnp.float32)
                    parts = [pairs[t * (STEP // 2) : (t + 1) * (STEP // 2)] for t in range(tiles)]
                    halves.append(jnp.concatenate([*parts, ends[full:kept]], axis=1))
            if halves:
                shares.append(jnp.concatenate(halves, axis=0).astype(jnp.bfloat16))
            share = jnp.concatenate(shares, axis=0)
            delta = delta + jnp.dot(choice, share, preferred_element_type=jnp.float32)
        columns = pl.ds(pl.multiple_of(j * whole, LANES), whole)
        out_ref[:, columns] = (
            tokens_ref[:, columns].astype(jnp.float32) + delta[:, 0:whole]
        ).astype(jnp.bfloat16)
        turned = pltpu.roll(delta[:, whole:], QUARTER * j, 1)
        return jnp.where(lane // QUARTER == j, turned, end)

    end = lax.fori_loop(0, QUAD, one, jnp.zeros((total, LANES), jnp.float32), unroll=2)
    out_ref[:, QUAD * whole :] = (
        tokens_ref[:, QUAD * whole :].astype(jnp.float32) + end
    ).astype(jnp.bfloat16)


def call(kernel, out_shape, in_specs, flops, moved, after=(), scratch=(), out_specs=None):
    many = isinstance(out_shape, list)
    skipped = len(after)
    body = (lambda *refs: kernel(*refs[skipped:])) if skipped else kernel
    run = pl.pallas_call(
        body,
        out_shape=out_shape,
        in_specs=[pl.BlockSpec(memory_space=pl.ANY)] * skipped + in_specs,
        out_specs=out_specs or ([VMEM] * len(out_shape) if many else VMEM),
        scratch_shapes=scratch,
        compiler_params=pltpu.CompilerParams(vmem_limit_bytes=18 * 2**20),
        cost_estimate=pl.CostEstimate(flops=flops, bytes_accessed=moved, transcendentals=0),
    )
    return functools.partial(run, *after)


def exchange(value):
    return lax.all_to_all(value, "adapter", split_axis=0, concat_axis=0, tiled=True)


def towards(value, k, devices):
    return lax.ppermute(value, "adapter", [(i, i ^ k) for i in range(devices)])


def swapped(value):
    return lax.ppermute(value, "groups", [(0, 1), (1, 0)])


def stand_behind(value, *earlier):
    return pl.pallas_call(
        lambda *refs: None,
        out_shape=jax.ShapeDtypeStruct(value.shape, value.dtype),
        in_specs=[pl.BlockSpec(memory_space=pl.ANY)] * (1 + len(earlier)),
        out_specs=pl.BlockSpec(memory_space=pl.ANY),
        input_output_aliases={0: 0},
    )(value, *earlier)


def first_pack_call(cap, whole, devices, resident, adapter, used, tokens):
    blocks, rows, width = tokens.shape
    total = blocks * rows
    return call(
        functools.partial(first_pack_kernel, whole, cap, resident),
        [
            jax.ShapeDtypeStruct((devices, whole // LANES * cap + QUARTER, LANES), jnp.bfloat16),
            jax.ShapeDtypeStruct((1, total), jnp.int32),
            jax.ShapeDtypeStruct((total, 1), jnp.float32),
        ],
        [VMEM, VMEM, VMEM],
        2 * devices * cap * total * whole,
        2 * (total * width + devices * cap * whole),
        scratch=[pltpu.VMEM((total, width), jnp.bfloat16), pltpu.VMEM((8, LANES), jnp.int32)],
    )(adapter.reshape(1, blocks), used.reshape(1, blocks), tokens.reshape(total, width))


def pack_call(cap, base, whole, devices, target, label, tokens):
    blocks, rows, width = tokens.shape
    total = blocks * rows
    return call(
        functools.partial(pack_kernel, whole, cap, base),
        jax.ShapeDtypeStruct((devices, whole // LANES * cap + QUARTER, LANES), jnp.bfloat16),
        [VMEM, VMEM, VMEM, VMEM],
        2 * devices * cap * total * whole,
        2 * (total * width + devices * cap * whole),
        scratch=[pltpu.VMEM((total, width), jnp.bfloat16)],
    )(jnp.zeros((8, LANES), jnp.int32), target, label, tokens.reshape(total, width))


def down_call(cap, first, arrived, down_weights, after):
    devices = arrived.shape[0]
    columns, share = down_weights[0].shape
    return call(
        down_kernel,
        [
            jax.ShapeDtypeStruct((cap // STEP, HALF, devices * STEP), jnp.float32),
            jax.ShapeDtypeStruct((STEP, LANES), jnp.bfloat16),
            jax.ShapeDtypeStruct((devices * STEP, LANES), jnp.bfloat16),
            jax.ShapeDtypeStruct((8,), jnp.int32),
        ],
        [SMEM] + [VMEM] * (1 + len(down_weights)),
        0,
        0,
        after,
        [
            pltpu.VMEM((2, columns, share), jnp.bfloat16),
            pltpu.VMEM((devices * STEP, share), jnp.bfloat16),
            pltpu.VMEM((HALF, devices * STEP), jnp.float32),
            pltpu.VMEM((8, devices * STEP), jnp.float32),
        ],
        [VMEM, VMEM, VMEM, SMEM],
    )(first, arrived, *down_weights)


def quad_sums(partial, devices):
    pair = call(
        pair_kernel, jax.ShapeDtypeStruct(partial.shape, jnp.bfloat16), [VMEM, VMEM], 0, 0
    )(partial, towards(partial, 1, devices))
    return [pair, towards(pair, 2, devices)]


def up_call(kept, first, met, notes, sums, up_weights):
    devices = notes.shape[0] // STEP
    columns, share = up_weights[0].shape
    shape = (devices, (share // LANES - 1) * kept + QUARTER, LANES)
    return call(
        up_kernel,
        jax.ShapeDtypeStruct(shape, jnp.bfloat16),
        [SMEM, SMEM] + [VMEM] * (3 + len(up_weights)),
        2 * devices * kept * QUAD * columns * share,
        2 * (2 * devices * kept + QUAD * columns) * share,
        scratch=[
            pltpu.VMEM((2, columns, share), jnp.bfloat16),
            pltpu.VMEM((devices * STEP, share), jnp.float32),
            pltpu.VMEM((devices, QUARTER, LANES), jnp.float32),
            *[pltpu.VMEM((-(-kept // STEP), devices * STEP, LANES), jnp.float32)] * 2,
        ],
    )(first, met, notes, *sums, *up_weights)


def back_and_mix(
    kept, more, tokens, target, label, first, met, notes, sums, down_weights, up_weights, *unused
):
    blocks, rows, width = tokens.shape
    total = blocks * rows
    devices = notes.shape[0] // STEP
    whole = up_weights[0].shape[1] - LANES
    pieces = [exchange(up_call(kept, first, met, notes, sums, up_weights))]
    if more:
        outgoing = pack_call(more, kept, whole, devices, target, label, tokens)
        arrived = exchange(outgoing)
        partial, unused_count, notes, met = down_call(more, first, arrived, down_weights, [])
        sums = quad_sums(partial, devices)
        pieces.append(exchange(up_call(more, first, met, notes, sums, up_weights)))
    mixed = call(
        functools.partial(mix_kernel, whole, (0, kept)[: len(pieces)]),
        jax.ShapeDtypeStruct((total, width), jnp.bfloat16),
        [VMEM] * (2 + len(pieces)),
        2 * devices * (kept + more) * total * whole,
        2 * (2 * total * width + devices * (kept + more) * whole),
    )(target.reshape(total, 1), tokens.reshape(total, width), *pieces)
    return mixed.reshape(tokens.shape)


def start_again(
    tokens, target, label, first, met, notes, sums, down_weights, up_weights, *arguments
):
    return rows_to_holders(tokens, *arguments)


def rows_to_quads(
    tokens, request_block_adapter, request_block_rows, adapter_down_weight, adapter_up_weight
):
    blocks, rows, width = tokens.shape
    devices = lax.axis_size("adapter")
    resident, rank, unused_width = adapter_up_weight.shape
    total = blocks * rows
    columns = resident * rank
    whole = width // LANES // QUAD * LANES
    share = whole + LANES
    bf16, i32 = jnp.bfloat16, jnp.int32

    me = lax.axis_index("adapter").astype(i32)
    group = lax.axis_index("groups").astype(i32)
    parts = jnp.bitwise_xor(me % QUAD, jnp.arange(QUAD, dtype=i32))
    halves = jnp.stack([group, 1 - group]) * (resident // 2)
    first = jnp.concatenate([parts * resident, halves]).astype(i32)
    tiles = whole // LANES

    def shares(weight, which, halved, after):
        shapes = []
        for k in which:
            count = columns // 2 if k in halved else columns
            far = (count * tiles + count // QUAD, LANES)
            shapes.append(jax.ShapeDtypeStruct((columns, share) if k < 2 else far, bf16))
        return call(
            functools.partial(weight_kernel, whole, which, halved),
            shapes,
            [SMEM, SMEM, VMEM],
            0,
            len(which) * columns * width,
            after,
        )(parts, group.reshape(1), weight)

    down_weight = adapter_down_weight.transpose(0, 2, 1).reshape(columns, width)
    up_weight = adapter_up_weight.reshape(columns, width)
    down_far = shares(down_weight, (2, 3), DOWN_HALVED, [])
    up_far = shares(up_weight, (2, 3), UP_HALVED, down_far[:1])
    down_near = shares(down_weight, (0, 1), (), up_far[:1])
    up_near = shares(up_weight, (0, 1), (), down_near[:1])
    down_weights = [down_near[0], towards(down_near[1], 1, devices)]
    down_weights += [towards(value, k, devices) for k, value in zip((2, 3), down_far)]
    up_weights = [up_near[0], towards(up_near[1], 1, devices)]
    up_weights += [towards(value, k, devices) for k, value in zip((2, 3), up_far)]
    down_weights[2] = stand_behind(down_weights[2], up_near[0])
    down_weights += [swapped(down_weights[k]) for k in DOWN_HALVED]
    up_weights += [swapped(up_weights[k]) for k in UP_HALVED]

    caps = [total * 10 // 32, total * 11 // 32, total * 12 // 32, total * 14 // 32]
    cap = caps[-1]
    outgoing, target, label = first_pack_call(
        cap, whole, devices, resident, request_block_adapter, request_block_rows, tokens
    )
    arrived = exchange(outgoing)
    partial, count, notes, met = down_call(cap, first, arrived, down_weights, up_weights[2:3])
    sums = quad_sums(partial, devices)
    count = stand_behind(count[0:1, 0:1], sums[0])
    most = jnp.maximum(count, swapped(count))[0, 0].astype(jnp.float32)
    branches = [functools.partial(back_and_mix, kept, 0) for kept in caps]
    branches += [functools.partial(back_and_mix, cap, STEP), start_again]
    return lax.switch(
        sum((most > limit).astype(i32) for limit in [*caps, cap + STEP]),
        branches,
        tokens,
        target,
        label,
        first,
        met,
        notes,
        sums,
        down_weights,
        up_weights,
        request_block_adapter,
        request_block_rows,
        adapter_down_weight,
        adapter_up_weight,
    )


def solution(mesh):
    placed = (
        P(("groups", "adapter"), None, None),
        P(("groups", "adapter")),
        P(("groups", "adapter")),
        P("adapter", None, None),
        P("adapter", None, None),
    )

    def per_device(tokens, request_block_adapter, request_block_rows, down_weight, up_weight):
        blocks, rows, width = tokens.shape
        devices = mesh.shape["adapter"]
        slots = max(1, 4 * blocks // devices)
        quads = devices % QUAD == 0 and slots * QUAD >= blocks
        quads = quads and width % (QUAD * LANES) == LANES and up_weight.shape[1] == HALF
        quads = quads and blocks * rows * 7 // 16 == 7 * STEP and mesh.shape["groups"] == 2
        plan = rows_to_quads if quads else rows_to_holders
        return plan(tokens, request_block_adapter, request_block_rows, down_weight, up_weight)

    return jax.shard_map(
        per_device,
        mesh=mesh,
        in_specs=placed,
        out_specs=P(("groups", "adapter"), None, None),
        check_vma=False,
    )
```

```python
import functools

import jax
import jax.numpy as jnp
from jax import lax
from jax.experimental import pallas as pl
from jax.experimental.pallas import tpu as pltpu
from jax.sharding import PartitionSpec as P

LANES = 128
HALF = 64
QUAD = 4
QUARTER = 32
STEP = 16
NOTE = 96
DOWN_HALVED = (2, 3)
UP_HALVED = (2,)
VMEM = pl.BlockSpec(memory_space=pltpu.VMEM)
SMEM = pl.BlockSpec(memory_space=pltpu.SMEM)


def normalise(tokens):
    values = tokens.astype(jnp.float32)
    mean_sq = jnp.mean(values * values, axis=-1, keepdims=True)
    return (values, (values * lax.rsqrt(mean_sq + 1e-06)).astype(jnp.bfloat16))


def resident_update(hidden_state, block_labels, adapter_down_weight, adapter_up_weight):
    feature_width = hidden_state.shape[-1]
    leading = hidden_state.shape[:-1]
    resident_rows, unused_value, inner_rank = adapter_down_weight.shape
    flattened_tokens = hidden_state.reshape(-1, feature_width)
    down_matrix = jnp.einsum(
        "tq,iqg->tig", flattened_tokens, adapter_down_weight, preferred_element_type=jnp.float32
    )
    down_matrix = down_matrix.astype(jnp.bfloat16).reshape(
        flattened_tokens.shape[0], resident_rows * inner_rank
    )
    column_owner = jnp.arange(resident_rows * inner_rank, dtype=jnp.int32) // inner_rank
    picked = block_labels.reshape(-1, 1) == column_owner[None, :]
    down_matrix = jnp.where(picked, down_matrix, jnp.zeros_like(down_matrix))
    lowrank_update = jnp.dot(
        down_matrix,
        adapter_up_weight.reshape(resident_rows * inner_rank, feature_width),
        preferred_element_type=jnp.float32,
    )
    return lowrank_update.astype(jnp.bfloat16).reshape(leading + (feature_width,))


def rows_to_holders(
    tokens, request_block_adapter, request_block_rows, adapter_down_weight, adapter_up_weight
):
    blocks, rows, feature_width = tokens.shape
    devices = lax.axis_size("adapter")
    resident_rows = adapter_down_weight.shape[0]
    slots = max(1, 4 * blocks // devices)
    values, normed = normalise(tokens)
    owner = request_block_adapter // resident_rows
    within = request_block_adapter - owner * resident_rows
    serial = jnp.arange(blocks, dtype=jnp.int32)
    earlier = (owner[:, None] == owner[None, :]) & (serial[None, :] < serial[:, None])
    position = owner * slots + jnp.sum(earlier, axis=1)
    outgoing = (
        jnp.zeros((devices * slots, rows, feature_width), jnp.bfloat16).at[position].set(normed)
    )
    outgoing = outgoing.reshape(devices, slots, rows, feature_width)
    block_labels = jnp.full((devices * slots,), -1, jnp.int32).at[position].set(within)
    block_labels = jnp.broadcast_to(block_labels[:, None], (devices * slots, rows)).reshape(
        devices, slots, rows
    )
    arriving_rows, row_markers = (
        lax.all_to_all(outgoing, "adapter", split_axis=0, concat_axis=0, tiled=True),
        lax.all_to_all(block_labels, "adapter", split_axis=0, concat_axis=0, tiled=True),
    )
    lowrank_update = resident_update(
        arriving_rows, row_markers, adapter_down_weight, adapter_up_weight
    )
    returned = lax.all_to_all(lowrank_update, "adapter", split_axis=0, concat_axis=0, tiled=True)
    mine = returned.reshape(devices * slots, rows, feature_width)[position]
    live = jnp.arange(rows, dtype=jnp.int32)[None, :] < request_block_rows[:, None]
    mixed = values + jnp.where(live[:, :, None], mine.astype(jnp.float32), jnp.float32(0.0))
    return mixed.astype(jnp.bfloat16)


def lanes_of(rows):
    return lax.broadcasted_iota(jnp.int32, (rows, LANES), 1)


def weight_kernel(whole, which, halved, part_ref, group_ref, weight_ref, *out_refs):
    tiles = whole // LANES
    for k, out_ref in zip(which, out_refs):
        j = part_ref[k]
        if k < 2:
            last = weight_ref[:, QUAD * whole :].astype(jnp.float32)
            turned = pltpu.roll(last, lax.rem(LANES - QUARTER * j, LANES), 1)
            inside = lanes_of(last.shape[0]) < QUARTER
            out_ref[:, 0:whole] = weight_ref[:, pl.ds(pl.multiple_of(j * whole, LANES), whole)]
            out_ref[:, whole:] = jnp.where(inside, turned, 0.0).astype(jnp.bfloat16)
            continue
        count = weight_ref.shape[0] // 2 if k in halved else weight_ref.shape[0]
        start = pl.multiple_of(group_ref[0] * count, count) if k in halved else 0
        for t in range(tiles):
            column = pl.multiple_of(j * whole + t * LANES, LANES)
            out_ref[t * count : (t + 1) * count, :] = weight_ref[
                pl.ds(start, count), pl.ds(column, LANES)
            ]
        last = weight_ref[pl.ds(start, count), QUAD * whole :].astype(jnp.float32)
        size = count // QUAD
        owner = lanes_of(size) // QUARTER
        merged = jnp.zeros((size, LANES), jnp.float32)
        for m in range(QUAD):
            shift = lax.rem(LANES + QUARTER * (m - j), LANES)
            turned = pltpu.roll(last[m * size : (m + 1) * size], shift, 1)
            merged = jnp.where(owner == m, turned, merged)
        out_ref[tiles * count :, :] = merged.astype(jnp.bfloat16)


def open_far(far_refs, halved, opened_ref):
    width = opened_ref.shape[2]
    tiles = width // LANES - 1
    places = [(k - 2, 0) for k in (2, 3)] + [(k - 2, 1) for k in halved]
    for ref, (holder, part) in zip(far_refs, places):
        count = opened_ref.shape[1] // 2 if holder + 2 in halved else opened_ref.shape[1]
        base, size = part * count, count // QUAD
        inside = lanes_of(size) < QUARTER
        for t in range(tiles):
            opened_ref[holder, base : base + count, t * LANES : (t + 1) * LANES] = ref[
                t * count : (t + 1) * count, :
            ]
        packed = ref[tiles * count :, :].astype(jnp.float32)
        for m in range(QUAD):
            turned = pltpu.roll(packed, (LANES - QUARTER * m) % LANES, 1) if m else packed
            opened_ref[holder, base + m * size : base + (m + 1) * size, tiles * LANES :] = (
                jnp.where(inside, turned, 0.0).astype(jnp.bfloat16)
            )


def lay_out(resident, adapter_ref, used_ref, most_ref, target_ref, label_ref):
    blocks, total = adapter_ref.shape[1], target_ref.shape[1]
    rows = total // blocks
    adapter, used = adapter_ref[...], used_ref[...]
    down = lax.broadcasted_iota(jnp.int32, (blocks, blocks), 0)
    across = lax.broadcasted_iota(jnp.int32, (blocks, blocks), 1)

    def turned(value):
        return jnp.sum(jnp.where(down == across, value, 0), axis=1, keepdims=True)

    span = resident * QUAD
    quad = jnp.floor((adapter.astype(jnp.float32) + 0.5) * (1.0 / span)).astype(jnp.int32)
    order = adapter * blocks + lax.broadcasted_iota(jnp.int32, (1, blocks), 1)
    quad_down, order_down, used_down = turned(quad), turned(order), turned(used)
    same = quad_down == quad
    ahead = jnp.sum(jnp.where(same & (order < order_down), used, 0), axis=1, keepdims=True)
    within = jnp.sum(jnp.where(same, used, 0), axis=1, keepdims=True)
    most_ref[...] = jnp.broadcast_to(jnp.max(within, axis=0, keepdims=True), most_ref.shape)
    start = quad_down * total + ahead

    block = lax.broadcasted_iota(jnp.int32, (blocks, total), 0)
    row = lax.broadcasted_iota(jnp.int32, (blocks, total), 1) - block * rows
    place = jnp.where((row >= 0) & (row < used_down), start + row + 1, 0)
    target_ref[...] = jnp.sum(place, axis=0, keepdims=True) - 1
    block = lax.broadcasted_iota(jnp.int32, (total, blocks), 1)
    row = lax.broadcasted_iota(jnp.int32, (total, blocks), 0) - block * rows
    label = jnp.where((row >= 0) & (row < rows), adapter - quad * span + 1, 0)
    label_ref[...] = jnp.sum(label.astype(jnp.float32), axis=1, keepdims=True)


def first_pack_kernel(
    whole, cap, resident, adapter_ref, used_ref, tokens_ref, out_ref, target_ref, label_ref, *refs
):
    normed_ref, most_ref = refs
    lay_out(resident, adapter_ref, used_ref, most_ref, target_ref, label_ref)
    pack_kernel(
        whole, cap, 0, most_ref, target_ref, label_ref, tokens_ref, out_ref, normed_ref
    )


def pack_kernel(
    whole, cap, base, most_ref, target_ref, label_ref, tokens_ref, out_ref, normed_ref
):
    values = tokens_ref[...].astype(jnp.float32)
    mean_sq = jnp.mean(values * values, axis=-1, keepdims=True)
    normed_ref[...] = (values * lax.rsqrt(mean_sq + 1e-06)).astype(jnp.bfloat16)
    total = tokens_ref.shape[0]
    quads, tiles = out_ref.shape[0] // QUAD, whole // LANES
    lane = lanes_of(total)
    last = normed_ref[:, QUAD * whole :].astype(jnp.float32)
    label = jnp.where(lane == QUARTER, label_ref[...], 0.0)
    ends = []
    for j in range(QUAD):
        turned = pltpu.roll(last, (LANES - QUARTER * j) % LANES, 1) if j else last
        ends.append(jnp.where(lane < QUARTER, turned, label).astype(jnp.bfloat16))
    most = most_ref[0:1, 0:1].astype(jnp.float32)
    group_lane = lanes_of(QUARTER) // QUARTER
    step_lane = lanes_of(STEP)
    chosen = []
    for q in range(quads):
        place = lax.broadcasted_iota(jnp.int32, (cap, total), 0) + (q * total + base)
        chosen.append(jnp.where(target_ref[...] == place, 1.0, 0.0).astype(jnp.bfloat16))
    chosen = jnp.concatenate(chosen, axis=0)
    notes = [jnp.where(step_lane == NOTE + cap // STEP, most, 0.0)] * quads
    for j in range(QUAD):
        for t in range(tiles):
            column = j * whole + t * LANES
            if t % 2 == 0:
                count = min(2, tiles - t) * LANES
                share = jnp.dot(
                    chosen,
                    normed_ref[:, column : column + count],
                    preferred_element_type=jnp.float32,
                ).astype(jnp.bfloat16)
            for q in range(quads):
                out_ref[q * QUAD + j, t * cap : (t + 1) * cap, :] = share[
                    q * cap : (q + 1) * cap, t % 2 * LANES : (t % 2 + 1) * LANES
                ]
        end_rows = jnp.dot(chosen, ends[j], preferred_element_type=jnp.float32)
        for q in range(quads):
            end = end_rows[q * cap : (q + 1) * cap]
            if j == 0:
                for a in range(cap // STEP):
                    turned = pltpu.roll(end[a * STEP : (a + 1) * STEP], NOTE + a - QUARTER, 1)
                    notes[q] = jnp.where(step_lane == NOTE + a, turned, notes[q])
            padded = jnp.concatenate(
                [end, jnp.zeros((QUAD * QUARTER - cap, LANES), jnp.float32)], axis=0
            )
            merged = padded[0:QUARTER]
            for m in range(1, QUAD):
                turned = pltpu.roll(padded[m * QUARTER : (m + 1) * QUARTER], m * QUARTER, 1)
                merged = jnp.where(group_lane == m, turned, merged)
            out_ref[q * QUAD + j, tiles * cap : tiles * cap + STEP, :] = merged[0:STEP].astype(
                jnp.bfloat16
            )
            out_ref[q * QUAD + j, tiles * cap + STEP :, :] = jnp.where(
                step_lane >= NOTE, notes[q], merged[STEP:]
            ).astype(jnp.bfloat16)


def read_notes(rows_ref, cap, tiles, part_ref, resident, notes_ref, labels_ref, met_ref):
    senders = rows_ref.shape[0]
    for s in range(senders):
        notes_ref[s * STEP : (s + 1) * STEP, :] = rows_ref[s, tiles * cap + STEP :, :]
    steps = labels_ref.shape[0]
    row = lax.broadcasted_iota(jnp.int32, (steps, LANES), 0)
    wanted = jnp.where(lanes_of(steps) == NOTE + row, 1.0, 0.0).astype(jnp.bfloat16)
    labels = lax.dot_general(
        wanted, notes_ref[...], (((1,), (1,)), ((), ())), preferred_element_type=jnp.float32
    )
    labels_ref[...] = labels
    code = jnp.zeros((steps, 1), jnp.float32)
    for h in range(QUAD):
        first = part_ref[h].astype(jnp.float32) + 1.0
        met = jnp.where((labels >= first) & (labels < first + resident), 1.0, 0.0)
        code = code + (1 << h) * jnp.max(met, axis=1, keepdims=True)
    at = lax.broadcasted_iota(jnp.int32, (steps, 1), 0)
    for a in range(cap // STEP):
        met_ref[a] = jnp.max(jnp.where(at == a, code, 0.0)).astype(jnp.int32)


def for_holders(met_ref, first_ref, near_refs, opened_ref, halved, a, step):
    pairs = opened_ref.shape[1] // LANES
    for h in range(QUAD):
        base = first_ref[h].astype(jnp.float32) + 1.0
        firsts = [base + 2.0 * t for t in range(pairs)]
        if h in halved:
            firsts = [
                base + first_ref[QUAD + i].astype(jnp.float32) + 2.0 * t
                for i in range(2)
                for t in range(pairs // 2)
            ]

        @pl.when(lax.rem(met_ref[a] // (1 << h), 2) > 0)
        def _(h=h, firsts=firsts):
            is_first = lax.rem(met_ref[a], 1 << h) == 0
            step(near_refs[h] if h < 2 else opened_ref.at[h - 2], firsts, is_first)


def down_kernel(first_ref, rows_ref, *refs):
    near_refs, far_refs, out_ref, count_ref = refs[:2], refs[2:6], refs[6], refs[7]
    notes_ref, met_ref, opened_ref, batch_ref, picked_ref, labels_ref = refs[8:]
    senders, width = rows_ref.shape[0], batch_ref.shape[1]
    tiles = width // LANES - 1
    cap = out_ref.shape[0] * STEP
    rank = out_ref.shape[1]
    resident = opened_ref.shape[1] // rank
    dims = (((1,), (1,)), ((), ()))
    read_notes(rows_ref, cap, tiles, first_ref, resident, notes_ref, labels_ref, met_ref)
    notes = notes_ref[...].astype(jnp.float32)
    is_count = lanes_of(senders * STEP) == NOTE + cap // STEP
    count = jnp.max(jnp.where(is_count, notes, 0.0), axis=(0, 1), keepdims=True)
    count_ref[...] = jnp.broadcast_to(count, count_ref.shape).astype(jnp.bfloat16)
    open_far(far_refs, DOWN_HALVED, opened_ref)

    def one(a, carry):
        picked_ref[...] = jnp.zeros(picked_ref.shape, jnp.float32)

        @pl.when(met_ref[a] > 0)
        def _():
            shift = lax.rem(LANES - QUARTER * (a // 2), LANES)
            spot = pl.multiple_of(tiles * cap + lax.rem(a, 2) * STEP, STEP)
            for s in range(senders):
                rows = slice(s * STEP, (s + 1) * STEP)
                for t in range(tiles):
                    at = pl.multiple_of(t * cap + a * STEP, STEP)
                    batch_ref[rows, t * LANES : (t + 1) * LANES] = rows_ref[s, pl.ds(at, STEP), :]
                end = rows_ref[s, pl.ds(spot, STEP), :].astype(jnp.float32)
                batch_ref[rows, tiles * LANES :] = pltpu.roll(end, shift, 1).astype(jnp.bfloat16)
            label = labels_ref[pl.ds(a, 1), :]

            def step(weight_ref, firsts, is_first):
                product = lax.dot_general(
                    weight_ref[...], batch_ref[...], dims, preferred_element_type=jnp.float32
                )
                picked = picked_ref[...]
                for t, first in enumerate(firsts):
                    for i in range(2):
                        at = (2 * t + i) * rank
                        picked = jnp.where(
                            label == first + i, product[at : at + rank, :], picked
                        )
                picked_ref[...] = picked

            for_holders(met_ref, first_ref, near_refs, opened_ref, DOWN_HALVED, a, step)

        out_ref[a] = picked_ref[...]
        return carry

    lax.fori_loop(0, cap // STEP, one, 0)


def pair_kernel(own_ref, other_ref, out_ref):
    out_ref[...] = (own_ref[...] + other_ref[...]).astype(jnp.bfloat16)


def up_kernel(first_ref, met_ref, notes_ref, *refs):
    sum_refs, near_refs, far_refs, out_ref = refs[:2], refs[2:4], refs[4:7], refs[7]
    opened_ref, delta_ref, ends_ref, label_ref, twice_ref = refs[8:]
    senders, width = out_ref.shape[0], opened_ref.shape[2]
    tiles = width // LANES - 1
    rank = sum_refs[0].shape[1]
    kept = (out_ref.shape[1] - QUARTER) // tiles
    full = kept // STEP * STEP
    group_lane = lanes_of(STEP) // QUARTER
    open_far(far_refs, UP_HALVED, opened_ref)
    ends_ref[...] = jnp.zeros(ends_ref.shape, jnp.float32)
    low = jnp.where(lanes_of(senders * STEP) < HALF, 0.0, 1.0)
    rank_row = lax.broadcasted_iota(jnp.int32, (rank, LANES), 0)
    twofold = jnp.where(lax.rem(lanes_of(rank), rank) == rank_row, 1.0, 0.0).astype(jnp.bfloat16)

    note_row = lax.broadcasted_iota(jnp.int32, (LANES, LANES), 0)
    for a in range(label_ref.shape[0]):
        wanted = jnp.where(note_row == NOTE + a, 1.0, 0.0).astype(jnp.bfloat16)
        label_ref[a] = jnp.dot(notes_ref[...], wanted, preferred_element_type=jnp.float32) - low
        down = sum_refs[0][a].astype(jnp.float32) + sum_refs[1][a].astype(jnp.float32)
        twice_ref[a] = lax.dot_general(
            down.astype(jnp.bfloat16),
            twofold,
            (((0,), (0,)), ((), ())),
            preferred_element_type=jnp.float32,
        )

    def one(a, carry):
        @pl.when(met_ref[a] == 0)
        def _():
            delta_ref[...] = jnp.zeros(delta_ref.shape, jnp.float32)

        @pl.when(met_ref[a] > 0)
        def _():
            label, twice = label_ref[a], twice_ref[a]

            def step(weight_ref, firsts, is_first):
                placed = [jnp.where(label == first, twice, 0.0) for first in firsts]
                placed = jnp.concatenate(placed, axis=1).astype(jnp.bfloat16)
                before = jnp.where(is_first, 0.0, delta_ref[...])
                delta_ref[...] = before + jnp.dot(
                    placed, weight_ref[...], preferred_element_type=jnp.float32
                )

            for_holders(met_ref, first_ref, near_refs, opened_ref, UP_HALVED, a, step)

        spot = pl.multiple_of(lax.rem(a, 2) * STEP, STEP)
        for s in range(senders):
            rows = slice(s * STEP, (s + 1) * STEP)
            turned = pltpu.roll(delta_ref[rows, tiles * LANES :], QUARTER * (a // 2), 1)
            ends_ref[s, pl.ds(spot, STEP), :] = jnp.where(
                group_lane == a // 2, turned, ends_ref[s, pl.ds(spot, STEP), :]
            )

        @pl.when(a < full // STEP)
        def _():
            for s in range(senders):
                rows = slice(s * STEP, (s + 1) * STEP)
                for t in range(tiles):
                    at = pl.multiple_of(t * full + a * STEP, STEP)
                    out_ref[s, pl.ds(at, STEP), :] = delta_ref[
                        rows, t * LANES : (t + 1) * LANES
                    ].astype(jnp.bfloat16)

        return carry

    lax.fori_loop(0, label_ref.shape[0], one, 0)
    if kept > full:
        for s in range(senders):
            rows = slice(s * STEP, s * STEP + STEP // 2)
            for t in range(0, tiles, 2):
                both = [
                    delta_ref[rows, (t + i) * LANES : (t + i + 1) * LANES] for i in range(2)
                ]
                at = tiles * full + t * (STEP // 2)
                out_ref[s, at : at + STEP, :] = jnp.concatenate(both, axis=0).astype(jnp.bfloat16)
    for s in range(senders):
        out_ref[s, tiles * kept :, :] = ends_ref[s].astype(jnp.bfloat16)


def mix_kernel(whole, bases, target_ref, tokens_ref, *refs):
    returned_refs, out_ref = refs[:-1], refs[-1]
    total = tokens_ref.shape[0]
    tiles, quads = whole // LANES, returned_refs[0].shape[0] // QUAD
    lane = lanes_of(total)
    chosen = []
    for base, ref in zip(bases, returned_refs):
        kept = (ref.shape[1] - QUARTER) // tiles
        full = kept // STEP * STEP
        spot = lax.broadcasted_iota(jnp.int32, (total, quads * kept), 1)
        place = spot // full * total + spot % full
        if kept > full:
            later = spot - quads * full
            half_place = later // (STEP // 2) * total + later % (STEP // 2) + full
            place = jnp.where(later >= 0, half_place, place)
        place = place + base
        chosen.append(jnp.where(target_ref[...] == place, 1.0, 0.0).astype(jnp.bfloat16))

    def one(j, end):
        delta = 0.0
        for choice, ref in zip(chosen, returned_refs):
            kept = choice.shape[1] // quads
            full = kept // STEP * STEP
            shares, halves = [], []
            for q in range(quads):
                d = q * QUAD + j
                parts = [ref[d, t * full : (t + 1) * full, :] for t in range(tiles)]
                packed = ref[d, tiles * kept :, :].astype(jnp.float32)
                groups = [packed]
                for m in range(1, QUAD):
                    groups.append(pltpu.roll(packed, LANES - QUARTER * m, 1))
                ends = jnp.concatenate(groups, axis=0)
                parts.append(ends[0:full].astype(jnp.bfloat16))
                shares.append(jnp.concatenate(parts, axis=1))
                if kept > full:
                    pairs = ref[d, tiles * full : tiles * kept, :].astype(jnp.float32)
                    parts = [pairs[t * (STEP // 2) : (t + 1) * (STEP // 2)] for t in range(tiles)]
                    halves.append(jnp.concatenate([*parts, ends[full:kept]], axis=1))
            if halves:
                shares.append(jnp.concatenate(halves, axis=0).astype(jnp.bfloat16))
            share = jnp.concatenate(shares, axis=0)
            delta = delta + jnp.dot(choice, share, preferred_element_type=jnp.float32)
        columns = pl.ds(pl.multiple_of(j * whole, LANES), whole)
        out_ref[:, columns] = (
            tokens_ref[:, columns].astype(jnp.float32) + delta[:, 0:whole]
        ).astype(jnp.bfloat16)
        turned = pltpu.roll(delta[:, whole:], QUARTER * j, 1)
        return jnp.where(lane // QUARTER == j, turned, end)

    end = lax.fori_loop(0, QUAD, one, jnp.zeros((total, LANES), jnp.float32), unroll=2)
    out_ref[:, QUAD * whole :] = (
        tokens_ref[:, QUAD * whole :].astype(jnp.float32) + end
    ).astype(jnp.bfloat16)


def call(kernel, out_shape, in_specs, flops, moved, after=(), scratch=(), out_specs=None):
    many = isinstance(out_shape, list)
    skipped = len(after)
    body = (lambda *refs: kernel(*refs[skipped:])) if skipped else kernel
    run = pl.pallas_call(
        body,
        out_shape=out_shape,
        in_specs=[pl.BlockSpec(memory_space=pl.ANY)] * skipped + in_specs,
        out_specs=out_specs or ([VMEM] * len(out_shape) if many else VMEM),
        scratch_shapes=scratch,
        compiler_params=pltpu.CompilerParams(vmem_limit_bytes=28 * 2**20),
        cost_estimate=pl.CostEstimate(flops=flops, bytes_accessed=moved, transcendentals=0),
    )
    return functools.partial(run, *after)


def exchange(value):
    return lax.all_to_all(value, "adapter", split_axis=0, concat_axis=0, tiled=True)


def towards(value, k, devices):
    return lax.ppermute(value, "adapter", [(i, i ^ k) for i in range(devices)])


def swapped(value):
    return lax.ppermute(value, "groups", [(0, 1), (1, 0)])


def stand_behind(value, *earlier):
    return pl.pallas_call(
        lambda *refs: None,
        out_shape=jax.ShapeDtypeStruct(value.shape, value.dtype),
        in_specs=[pl.BlockSpec(memory_space=pl.ANY)] * (1 + len(earlier)),
        out_specs=pl.BlockSpec(memory_space=pl.ANY),
        input_output_aliases={0: 0},
    )(value, *earlier)


def first_pack_call(cap, whole, devices, resident, adapter, used, tokens):
    blocks, rows, width = tokens.shape
    total = blocks * rows
    return call(
        functools.partial(first_pack_kernel, whole, cap, resident),
        [
            jax.ShapeDtypeStruct((devices, whole // LANES * cap + QUARTER, LANES), jnp.bfloat16),
            jax.ShapeDtypeStruct((1, total), jnp.int32),
            jax.ShapeDtypeStruct((total, 1), jnp.float32),
        ],
        [VMEM, VMEM, VMEM],
        2 * devices * cap * total * whole,
        2 * (total * width + devices * cap * whole),
        scratch=[pltpu.VMEM((total, width), jnp.bfloat16), pltpu.VMEM((8, LANES), jnp.int32)],
    )(adapter.reshape(1, blocks), used.reshape(1, blocks), tokens.reshape(total, width))


def pack_call(cap, base, whole, devices, target, label, tokens):
    blocks, rows, width = tokens.shape
    total = blocks * rows
    return call(
        functools.partial(pack_kernel, whole, cap, base),
        jax.ShapeDtypeStruct((devices, whole // LANES * cap + QUARTER, LANES), jnp.bfloat16),
        [VMEM, VMEM, VMEM, VMEM],
        2 * devices * cap * total * whole,
        2 * (total * width + devices * cap * whole),
        scratch=[pltpu.VMEM((total, width), jnp.bfloat16)],
    )(jnp.zeros((8, LANES), jnp.int32), target, label, tokens.reshape(total, width))


def down_call(cap, first, arrived, down_weights, after):
    devices = arrived.shape[0]
    columns, share = down_weights[0].shape
    return call(
        down_kernel,
        [
            jax.ShapeDtypeStruct((cap // STEP, HALF, devices * STEP), jnp.float32),
            jax.ShapeDtypeStruct((STEP, LANES), jnp.bfloat16),
            jax.ShapeDtypeStruct((devices * STEP, LANES), jnp.bfloat16),
            jax.ShapeDtypeStruct((8,), jnp.int32),
        ],
        [SMEM] + [VMEM] * (1 + len(down_weights)),
        0,
        0,
        after,
        [
            pltpu.VMEM((2, columns, share), jnp.bfloat16),
            pltpu.VMEM((devices * STEP, share), jnp.bfloat16),
            pltpu.VMEM((HALF, devices * STEP), jnp.float32),
            pltpu.VMEM((8, devices * STEP), jnp.float32),
        ],
        [VMEM, VMEM, VMEM, SMEM],
    )(first, arrived, *down_weights)


def quad_sums(partial, devices):
    pair = call(
        pair_kernel, jax.ShapeDtypeStruct(partial.shape, jnp.bfloat16), [VMEM, VMEM], 0, 0
    )(partial, towards(partial, 1, devices))
    return [pair, towards(pair, 2, devices)]


def up_call(kept, first, met, notes, sums, up_weights):
    devices = notes.shape[0] // STEP
    columns, share = up_weights[0].shape
    shape = (devices, (share // LANES - 1) * kept + QUARTER, LANES)
    return call(
        up_kernel,
        jax.ShapeDtypeStruct(shape, jnp.bfloat16),
        [SMEM, SMEM] + [VMEM] * (3 + len(up_weights)),
        2 * devices * kept * QUAD * columns * share,
        2 * (2 * devices * kept + QUAD * columns) * share,
        scratch=[
            pltpu.VMEM((2, columns, share), jnp.bfloat16),
            pltpu.VMEM((devices * STEP, share), jnp.float32),
            pltpu.VMEM((devices, QUARTER, LANES), jnp.float32),
            *[pltpu.VMEM((-(-kept // STEP), devices * STEP, LANES), jnp.float32)] * 2,
        ],
    )(first, met, notes, *sums, *up_weights)


def back_and_mix(
    kept, more, tokens, target, label, first, met, notes, sums, down_weights, up_weights, *unused
):
    blocks, rows, width = tokens.shape
    total = blocks * rows
    devices = notes.shape[0] // STEP
    whole = up_weights[0].shape[1] - LANES
    pieces = [exchange(up_call(kept, first, met, notes, sums, up_weights))]
    if more:
        outgoing = pack_call(more, kept, whole, devices, target, label, tokens)
        arrived = exchange(outgoing)
        partial, unused_count, notes, met = down_call(more, first, arrived, down_weights, [])
        sums = quad_sums(partial, devices)
        pieces.append(exchange(up_call(more, first, met, notes, sums, up_weights)))
    mixed = call(
        functools.partial(mix_kernel, whole, (0, kept)[: len(pieces)]),
        jax.ShapeDtypeStruct((total, width), jnp.bfloat16),
        [VMEM] * (2 + len(pieces)),
        2 * devices * (kept + more) * total * whole,
        2 * (2 * total * width + devices * (kept + more) * whole),
    )(target.reshape(total, 1), tokens.reshape(total, width), *pieces)
    return mixed.reshape(tokens.shape)


def start_again(
    tokens, target, label, first, met, notes, sums, down_weights, up_weights, *arguments
):
    return rows_to_holders(tokens, *arguments)


def rows_to_quads(
    tokens, request_block_adapter, request_block_rows, adapter_down_weight, adapter_up_weight
):
    blocks, rows, width = tokens.shape
    devices = lax.axis_size("adapter")
    resident, rank, unused_width = adapter_up_weight.shape
    total = blocks * rows
    columns = resident * rank
    whole = width // LANES // QUAD * LANES
    share = whole + LANES
    bf16, i32 = jnp.bfloat16, jnp.int32

    me = lax.axis_index("adapter").astype(i32)
    group = lax.axis_index("groups").astype(i32)
    parts = jnp.bitwise_xor(me % QUAD, jnp.arange(QUAD, dtype=i32))
    halves = jnp.stack([group, 1 - group]) * (resident // 2)
    first = jnp.concatenate([parts * resident, halves]).astype(i32)
    tiles = whole // LANES

    def shares(weight, which, halved, after):
        shapes = []
        for k in which:
            count = columns // 2 if k in halved else columns
            far = (count * tiles + count // QUAD, LANES)
            shapes.append(jax.ShapeDtypeStruct((columns, share) if k < 2 else far, bf16))
        return call(
            functools.partial(weight_kernel, whole, which, halved),
            shapes,
            [SMEM, SMEM, VMEM],
            0,
            len(which) * columns * width,
            after,
        )(parts, group.reshape(1), weight)

    down_weight = adapter_down_weight.transpose(0, 2, 1).reshape(columns, width)
    up_weight = adapter_up_weight.reshape(columns, width)
    down_far = shares(down_weight, (2, 3), DOWN_HALVED, [])
    up_far = shares(up_weight, (2, 3), UP_HALVED, down_far[:1])
    down_near = shares(down_weight, (0, 1), (), up_far[:1])
    up_near = shares(up_weight, (0, 1), (), down_near[:1])
    down_weights = [down_near[0], towards(down_near[1], 1, devices)]
    down_weights += [towards(value, k, devices) for k, value in zip((2, 3), down_far)]
    up_weights = [up_near[0], towards(up_near[1], 1, devices)]
    up_weights += [towards(value, k, devices) for k, value in zip((2, 3), up_far)]
    down_weights[2] = stand_behind(down_weights[2], up_near[0])
    down_weights += [swapped(down_weights[k]) for k in DOWN_HALVED]
    up_weights += [swapped(up_weights[k]) for k in UP_HALVED]

    caps = [total * 10 // 32, total * 11 // 32, total * 12 // 32, total * 14 // 32]
    cap = caps[-1]
    outgoing, target, label = first_pack_call(
        cap, whole, devices, resident, request_block_adapter, request_block_rows, tokens
    )
    arrived = exchange(outgoing)
    partial, count, notes, met = down_call(cap, first, arrived, down_weights, up_weights[2:3])
    sums = quad_sums(partial, devices)
    count = stand_behind(count[0:1, 0:1], sums[0])
    most = jnp.maximum(count, swapped(count))[0, 0].astype(jnp.float32)
    branches = [functools.partial(back_and_mix, kept, 0) for kept in caps]
    branches += [functools.partial(back_and_mix, cap, STEP), start_again]
    return lax.switch(
        sum((most > limit).astype(i32) for limit in [*caps, cap + STEP]),
        branches,
        tokens,
        target,
        label,
        first,
        met,
        notes,
        sums,
        down_weights,
        up_weights,
        request_block_adapter,
        request_block_rows,
        adapter_down_weight,
        adapter_up_weight,
    )


def solution(mesh):
    placed = (
        P(("groups", "adapter"), None, None),
        P(("groups", "adapter")),
        P(("groups", "adapter")),
        P("adapter", None, None),
        P("adapter", None, None),
    )

    def per_device(tokens, request_block_adapter, request_block_rows, down_weight, up_weight):
        blocks, rows, width = tokens.shape
        devices = mesh.shape["adapter"]
        slots = max(1, 4 * blocks // devices)
        quads = devices % QUAD == 0 and slots * QUAD >= blocks
        quads = quads and width % (QUAD * LANES) == LANES and up_weight.shape[1] == HALF
        quads = quads and blocks * rows * 7 // 16 == 7 * STEP and mesh.shape["groups"] == 2
        plan = rows_to_quads if quads else rows_to_holders
        return plan(tokens, request_block_adapter, request_block_rows, down_weight, up_weight)

    return jax.shard_map(
        per_device,
        mesh=mesh,
        in_specs=placed,
        out_specs=P(("groups", "adapter"), None, None),
        check_vma=False,
    )
```
